32 devices in a mesh: ctx: 8 (over y, x, core), wt: 4 (over z).
Axes of the slice: x: 2, y: 2, z: 4, core: 2. Of those that a mesh axis runs over, the one named last changes fastest.
Arguments:
- hidden: bfloat16 [4, 2048, 1536], P('wt', 'ctx'), may hold values from -6 to 6
- teacher: bfloat16 [4, 2048, 1536], P('wt', 'ctx'), may hold values from -6 to 6
- valid_mask: int32 [4, 2048], P('wt', 'ctx'), may hold values from 0 to 1, as said below
- routes: int32 [4, 2048, 6], P('wt', 'ctx'), may hold values from 0 to 15, all different within a row; in each aligned block of 256 rows (0 to 255, 256 to 511, ..., all dimensions but the last counted through in order) at most 128 rows name the same one
- route_gates: float32 [4, 2048, 6], P('wt', 'ctx'), may hold values from 0.2 to 0.8
- gain_in: bfloat16 [1536], P('wt'), may hold values from 0.25 to 1.75
- query_key_value_weight: bfloat16 [1536, 2560], P('wt'), may hold values from -0.15625 to 0.15625
- out_weight: bfloat16 [1536, 1536], P('wt'), may hold values from -2.5 to 2.5
- gain_mid: bfloat16 [1536], P('wt'), may hold values from 0.25 to 1.75
- shared_weight: bfloat16 [1536, 3072], P('wt'), may hold values from -0.15625 to 0.15625
- expert_weight: bfloat16 [16, 1536, 1536], P('wt'), may hold values from -0.21875 to 0.21875
Outputs:
- output: bfloat16 [4, 2048, 1536], P('wt', 'ctx')
- loss: float32 [], replicated
- grad_hidden: float32 [4, 2048, 1536], P('wt', 'ctx')
- grad_gain_in: float32 [1536], P('wt')
- grad_qkv: float32 [1536, 2560], P('wt')
- grad_out: float32 [1536, 1536], P('wt')
- grad_gain_mid: float32 [1536], P('wt')
- grad_shared: float32 [1536, 3072], P('wt')
- grad_experts: float32 [16, 1536, 1536], P('wt')
The draws below stay inside these ranges and needn't reach their ends.
Inputs may be any that keep to these rules, and one draw needn't show every extreme that they name: `valid_mask`: in the last row of every aligned block of 256 rows of a sequence the mask is 1. A token's 6 routes name different experts. In the rows of one device (aligned blocks of 256 rows of a sequence) no expert is named more than 128 times, a bound that some block reaches.
All inputs are finite; a program needn't handle non-finite values.
Results may differ from the reference program's by a relative error of at most 0.023.
Values may be sent and summed in bfloat16 or wider, within the bound.
No kernel may reach another device: no remote copies, remote signals or barrier semaphores. Data moves between devices by JAX's collectives and lax.ppermute only.
A program may use at most 512 MiB of HBM per device.

```python
import math
import jax
import jax.numpy as jnp
import numpy as np
from jax import lax

MODEL_DIM = 1536
QUERY_HEADS = 12
KEY_VALUE_HEADS = 4
HEAD_SIZE = 128
F = 512
SF = 1024
EXPERTS = 16
TOP = 6
TOK_DEV = 256
CAP = 128
SEQUENCE_LENGTH = 2048
SEQS = 4
TOKENS = 8192
N_CTX = 8


def draw_valid_mask(key, part):
    key = jax.random.fold_in(key, 7)
    row_index = jnp.arange(SEQS * SEQUENCE_LENGTH, dtype=jnp.int32).reshape(SEQS, SEQUENCE_LENGTH)
    block_index = row_index // TOK_DEV
    block_total = SEQS * SEQUENCE_LENGTH // TOK_DEV
    threshold = 250 + 650 * block_index // max(block_total - 1, 1)
    draws = jax.random.randint(key, (SEQS, SEQUENCE_LENGTH), 0, 1000, dtype=jnp.int32)
    last_row = row_index % TOK_DEV == TOK_DEV - 1
    return jnp.where((draws < threshold) | last_row, 1, 0).astype(jnp.int32)


def steps_of(stream_key, dims, pieces, smallest, largest):
    factor_of, own = 1.0, jax.random.fold_in(stream_key, 6)
    for axis_at, blocks in pieces:
        steps = jnp.exp(jax.random.uniform(jax.random.fold_in(own, axis_at), (blocks,), jnp.float32, smallest / len(pieces), largest / len(pieces)))
        factor_of = factor_of * jnp.repeat(steps, dims[axis_at] // blocks).reshape([-1 if axis == axis_at else 1 for axis in range(len(dims))])
    return factor_of


def assign_block(key, own, number, rows, number_of, top, most, skew):
    sequence = jax.random.permutation(key, number_of)
    heavy_load, common = shares(number_of, rows * top, most, skew, True), shares(number_of, rows * top, most, skew, False)
    places = jnp.arange(number_of)

    def named(sizes, offset_by):
        used = int((sizes > 0).sum())
        fixed = max(1, used // 4)
        passed = fixed + (places - fixed + offset_by * (used - fixed)) % max(1, number_of - fixed)
        return jnp.zeros((number_of,), jnp.int32).at[sequence[jnp.where(places < fixed, places, passed)]].set(jnp.asarray(sizes, jnp.int32))

    sizes = jnp.where(number % 4 == 0, named(heavy_load, number // 4), named(common, number - number // 4 - 1))
    mixed = jax.random.permutation(jax.random.fold_in(own, 3), number_of)
    donor, receiver = mixed[0:number_of // 2 * 2:2], mixed[1:number_of // 2 * 2:2]
    room = jnp.minimum(sizes[donor] - 1, most - sizes[receiver]) // 2
    room = jnp.where((donor == sequence[0]) | (receiver == sequence[0]) | (sizes[receiver] == 0), 0, jnp.maximum(room, 0))
    passed = jax.random.randint(jax.random.fold_in(own, 4), (number_of // 2,), 0, 1 << 20) % (room + 1)
    sizes = sizes.at[donor].add(-passed).at[receiver].add(passed)
    labels = jnp.searchsorted(jnp.cumsum(sizes), jnp.arange(rows * top), side="right").astype(jnp.int32)
    grid = labels.reshape(top, rows).T
    grid = grid[jax.random.permutation(jax.random.fold_in(own, 1), rows)]
    offset_by = jax.random.randint(jax.random.fold_in(own, 2), (rows, 1), 0, top)
    return jnp.take_along_axis(grid, (jnp.arange(top)[None, :] + offset_by) % top, axis=1)


def shares(amount, total, reach, lean, full):
    loads = [(1 << 20) // math.isqrt(rank ** lean) + 1 for rank in range(1, amount + 1)]
    largest = reach if full else min(reach, max(-(-total // amount), total * loads[0] // sum(loads)))
    least = 1 if total - largest >= amount - 1 else 0
    given, surplus = [largest] + [least] * (amount - 1), total - largest - least * (amount - 1)
    while surplus > 0:
        candidates = [i for i in range(1, amount) if given[i] < largest] or [i for i in range(1, amount) if given[i] < reach]
        pool, budget = sum([loads[i] for i in candidates]), surplus
        for i in candidates:
            extra = min(reach - given[i], max(1, budget * loads[i] // pool), surplus)
            given[i] = given[i] + extra
            surplus = surplus - extra
    return np.array(given)


def gaussian(stream_key, shape, scale, reach, pieces=(), kind=jnp.bfloat16):
    values = scale * jax.random.normal(stream_key, shape, jnp.float32)
    if pieces:
        values = values * steps_of(stream_key, shape, pieces, -0.22, 0.18)
    return jnp.clip(values, -reach, reach).astype(kind)


def setup_inputs(seed: int = 0) -> dict:
    key_list = jax.random.split(jax.random.key(seed), 12)
    hidden = gaussian(key_list[0], (SEQS, SEQUENCE_LENGTH, MODEL_DIM), 1.0, 6.0, ((0, 4), (1, 8)))
    teacher = gaussian(key_list[1], (SEQS, SEQUENCE_LENGTH, MODEL_DIM), 1.0, 6.0, ((0, 4), (1, 8)))
    valid_mask = draw_valid_mask(jax.random.fold_in(key_list[11], 71), 0)
    routes_keys = jax.random.split(jax.random.fold_in(key_list[3], 1), SEQS * SEQUENCE_LENGTH // TOK_DEV)
    routes_turns = jax.random.permutation(jax.random.fold_in(key_list[3], 3), SEQS * SEQUENCE_LENGTH // TOK_DEV)
    routes = jax.vmap(lambda own, number: assign_block(jax.random.fold_in(key_list[3], 2), own, number, TOK_DEV, EXPERTS, TOP, CAP, 2))(routes_keys, routes_turns).reshape((SEQS, SEQUENCE_LENGTH, TOP))
    route_gates = jnp.clip(0.2 + 0.6 * jax.random.uniform(key_list[4], (SEQS, SEQUENCE_LENGTH, TOP), jnp.float32) ** steps_of(key_list[4], (SEQS, SEQUENCE_LENGTH, TOP), ((0, 4), (1, 8)), -0.2, 0.2), 0.2, 0.8)
    gain_in = jnp.clip(1.0 + 0.15 * jax.random.normal(key_list[5], (MODEL_DIM,), jnp.float32), 0.25, 1.75).astype(jnp.bfloat16)
    query_key_value_weight = gaussian(key_list[6], (MODEL_DIM, (QUERY_HEADS + 2 * KEY_VALUE_HEADS) * HEAD_SIZE), MODEL_DIM ** -0.5, 0.15625, ((0, 4),))
    out_weight = gaussian(key_list[7], (QUERY_HEADS * HEAD_SIZE, MODEL_DIM), (max(1, QUERY_HEADS * HEAD_SIZE * 8 // SEQUENCE_LENGTH)) ** -0.5, 2.5, ((0, 4),))
    gain_mid = jnp.clip(1.0 + 0.15 * jax.random.normal(key_list[8], (MODEL_DIM,), jnp.float32), 0.25, 1.75).astype(jnp.bfloat16)
    shared_weight = gaussian(key_list[9], (MODEL_DIM, 3 * SF), MODEL_DIM ** -0.5, 0.15625, ((0, 4),))
    expert_weight = gaussian(key_list[10], (EXPERTS, MODEL_DIM, 3 * F), (MODEL_DIM // 2) ** -0.5, 0.21875, ((0, 4),))
    return {"hidden": hidden, "teacher": teacher, "valid_mask": valid_mask, "routes": routes, "route_gates": route_gates, "gain_in": gain_in, "query_key_value_weight": query_key_value_weight, "out_weight": out_weight, "gain_mid": gain_mid, "shared_weight": shared_weight, "expert_weight": expert_weight}


norm_eps = 1e-05
masked_score = -1e+30
exact_mode = lax.Precision.HIGHEST

@jax.custom_vjp
def low(v):
    return lax.optimization_barrier(v.astype(jnp.bfloat16)).astype(jnp.float32)

@jax.custom_vjp
def low_back(v):
    return v

def low_keep(v):
    return (low(v), None)

def low_pass(kept, grad):
    return (grad,)

def back_keep(v):
    return (v, None)

def back_low(kept, grad):
    return (low(grad),)
low.defvjp(low_keep, low_pass)
low_back.defvjp(back_keep, back_low)

def positions(row_ids):
    piece_index = row_ids // TOK_DEV
    within = row_ids % TOK_DEV
    half_rows = TOK_DEV // 2
    mirrored = jnp.where(within < half_rows, piece_index, 2 * N_CTX - 1 - piece_index)
    return (mirrored * half_rows + within % half_rows).astype(jnp.int32)

def rms_scale(values, gain_vector):
    return values * lax.rsqrt(lax.optimization_barrier(jnp.mean(values * values, axis=-1, keepdims=True)) + norm_eps) * gain_vector

def sigmoid_linear(values):
    return values * jax.nn.sigmoid(values)

def route_tables(block_routes, block_gates):
    flat_routes = block_routes.reshape(-1)
    one_hot = (flat_routes[:, None] == jnp.arange(EXPERTS, dtype=jnp.int32)[None, :]).astype(jnp.int32)
    earlier = jnp.cumsum(one_hot, axis=0) - one_hot
    slot_index = lax.optimization_barrier(jnp.sum(earlier * one_hot, axis=1)).astype(jnp.int32)
    token_index = (jnp.arange(TOK_DEV * TOP, dtype=jnp.int32) // TOP).astype(jnp.int32)
    slot_table = jnp.full((EXPERTS, CAP), TOK_DEV, jnp.int32).at[flat_routes, slot_index].set(token_index)
    slot_gate = jnp.zeros((EXPERTS, CAP), jnp.float32).at[flat_routes, slot_index].set(block_gates.reshape(-1))
    return (slot_table, slot_gate)

def expert_block(normed_block, slot_table, slot_gate, expert_weight):
    padded = jnp.concatenate([normed_block, jnp.zeros((1, MODEL_DIM), jnp.float32)], axis=0)
    rows_in = low_back(padded[slot_table])
    gate_up = low_back(jnp.einsum('ecd,edf->ecf', rows_in, expert_weight[:, :, :2 * F], precision=exact_mode))
    active = low(sigmoid_linear(gate_up[..., :F]) * gate_up[..., F:])
    result = low(low_back(jnp.einsum('ecf,edf->ecd', active, expert_weight[:, :, 2 * F:], precision=exact_mode)))
    placed = jnp.zeros((TOK_DEV + 1, MODEL_DIM), jnp.float32).at[slot_table].add(result * slot_gate[..., None])
    return placed[:TOK_DEV]

def forward(params, inputs, teacher_seq, valid_seq, table_seq, gate_seq):
    gain_in, query_key_value_weight, out_weight, gain_mid, shared_weight, expert_weight = params
    query_groups = QUERY_HEADS // KEY_VALUE_HEADS
    normed_in = low(rms_scale(inputs, gain_in))
    projected_rows = low(low_back(jnp.dot(normed_in, query_key_value_weight, precision=exact_mode)))
    query_rows = projected_rows[:, :QUERY_HEADS * HEAD_SIZE].reshape(SEQUENCE_LENGTH, KEY_VALUE_HEADS, query_groups, HEAD_SIZE)
    gathered_keys = projected_rows[:, QUERY_HEADS * HEAD_SIZE:(QUERY_HEADS + KEY_VALUE_HEADS) * HEAD_SIZE].reshape(SEQUENCE_LENGTH, KEY_VALUE_HEADS, HEAD_SIZE)
    gathered_values = projected_rows[:, (QUERY_HEADS + KEY_VALUE_HEADS) * HEAD_SIZE:].reshape(SEQUENCE_LENGTH, KEY_VALUE_HEADS, HEAD_SIZE)
    key_position = positions(jnp.arange(SEQUENCE_LENGTH, dtype=jnp.int32))
    rows_per_block = min(512, SEQUENCE_LENGTH)
    score_scale = 1.0 / math.sqrt(HEAD_SIZE)

    def apply_attention(block_args):
        query_block, query_place = block_args
        scores = low_back(jnp.einsum('qhgd,khd->qhgk', query_block, gathered_keys, precision=exact_mode) * score_scale)
        allowed = key_position[None, None, None, :] <= query_place[:, None, None, None]
        scores = jnp.where(allowed, scores, masked_score)
        highest = lax.optimization_barrier(jnp.max(scores, axis=-1, keepdims=True))
        powers = jnp.exp(scores - highest)
        probabilities = low(powers / lax.optimization_barrier(jnp.sum(powers, axis=-1, keepdims=True)))
        return jnp.einsum('qhgk,khd->qhgd', probabilities, gathered_values, precision=exact_mode)
    attention_output = lax.map(jax.checkpoint(apply_attention), (query_rows.reshape(SEQUENCE_LENGTH // rows_per_block, rows_per_block, KEY_VALUE_HEADS, query_groups, HEAD_SIZE), key_position.reshape(SEQUENCE_LENGTH // rows_per_block, rows_per_block)))
    mixed_rows = low(low_back(attention_output.reshape(SEQUENCE_LENGTH, QUERY_HEADS * HEAD_SIZE)))
    middle = inputs + low_back(jnp.dot(mixed_rows, out_weight, precision=exact_mode))
    normed_mid = low(rms_scale(middle, gain_mid))
    shared_gate_up = low_back(jnp.dot(normed_mid, shared_weight[:, :2 * SF], precision=exact_mode))
    shared_act = low(sigmoid_linear(shared_gate_up[:, :SF]) * shared_gate_up[:, SF:])
    shared_out = low_back(jnp.dot(shared_act, shared_weight[:, 2 * SF:].T, precision=exact_mode))

    def experts_on(block_args):
        normed_block, slot_table, slot_gate = block_args
        return expert_block(normed_block, slot_table, slot_gate, expert_weight)
    routed = lax.map(jax.checkpoint(experts_on), (normed_mid.reshape(N_CTX, TOK_DEV, MODEL_DIM), table_seq, gate_seq)).reshape(SEQUENCE_LENGTH, MODEL_DIM)
    final_state = middle + shared_out + routed
    deviation = final_state - teacher_seq
    return (final_state, jnp.sum(valid_seq[:, None] * deviation * deviation))

def add_tree(total_part, grad_part):
    return total_part + grad_part

def reference(hidden, teacher, valid_mask, routes, route_gates, gain_in, query_key_value_weight, out_weight, gain_mid, shared_weight, expert_weight):
    params = (gain_in.astype(jnp.float32), query_key_value_weight.astype(jnp.float32), out_weight.astype(jnp.float32), gain_mid.astype(jnp.float32), shared_weight.astype(jnp.float32), expert_weight.astype(jnp.float32))
    valid_float = valid_mask.astype(jnp.float32)
    valid_count = jnp.sum(valid_float)
    slot_tables, slot_gates = jax.vmap(jax.vmap(route_tables))(routes.reshape(SEQS, N_CTX, TOK_DEV, TOP), route_gates.reshape(SEQS, N_CTX, TOK_DEV, TOP))
    loss_scale = TOKENS * 0.5 / valid_count

    def per_sequence(totals, sequence_args):
        inputs, teacher_seq, valid_seq, table_seq, gate_seq = sequence_args

        def objective(weights, states):
            return forward(weights, states, teacher_seq, valid_seq, table_seq, gate_seq)
        (final_state, squared), pull_back = jax.vjp(objective, params, inputs)
        weight_grads, input_grad = pull_back((jnp.zeros_like(final_state), loss_scale))
        totals = jax.tree.map(add_tree, totals, weight_grads)
        return (totals, (final_state.astype(jnp.bfloat16), input_grad, squared))
    zero_grads = jax.tree.map(jnp.zeros_like, params)
    totals, (output_state, input_grads, squares) = lax.scan(per_sequence, zero_grads, (hidden.astype(jnp.float32), teacher.astype(jnp.float32), valid_float, slot_tables, slot_gates))
    loss_value = 0.5 * jnp.sum(squares) / (valid_count * MODEL_DIM)
    return (output_state, loss_value, input_grads, totals[0], totals[1], totals[2], totals[3], totals[4], totals[5])
```

```python
import math

import jax
import jax.numpy as jnp
from jax import lax
from jax.experimental import pallas as pl
from jax.experimental.pallas import tpu as pltpu
from jax.sharding import PartitionSpec as P

QUERY_HEADS = 12
KEY_VALUE_HEADS = 4
HEAD_SIZE = 128
F = 512
SF = 1024
EXPERTS = 16
TOP = 6


norm_eps = 1e-05
masked_score = -1e30


def sigmoid_linear(values):
    return values * jax.nn.sigmoid(values)


def silu_slope(values):
    sigma_value = jax.nn.sigmoid(values)
    return sigma_value * (1.0 + values * (1.0 - sigma_value))


def normalize(values):
    inverse = lax.rsqrt(jnp.mean(values * values, axis=-1, keepdims=True) + norm_eps)
    return (values * inverse, inverse)


def norm_back(grad_normed, scaled, inverse, gain_vector):
    grad_scaled = grad_normed * gain_vector
    return inverse * (grad_scaled - scaled * jnp.mean(grad_scaled * scaled, axis=-1, keepdims=True))


def positions(row_ids, token_rows, context_count):
    piece_index = row_ids // token_rows
    within = row_ids % token_rows
    half_rows = token_rows // 2
    mirrored = jnp.where(within < half_rows, piece_index, 2 * context_count - 1 - piece_index)
    return mirrored * half_rows + within % half_rows


def route_tables(local_routes, local_gates, experts, capacity):
    token_rows = local_routes.shape[0]
    flat_routes = local_routes.reshape(-1)
    one_hot = (flat_routes[:, None] == jnp.arange(experts, dtype=jnp.int32)[None, :]).astype(
        jnp.int32
    )
    earlier = jnp.cumsum(one_hot, axis=0) - one_hot
    slot_index = jnp.sum(earlier * one_hot, axis=1)
    token_index = jnp.arange(flat_routes.shape[0], dtype=jnp.int32) // local_routes.shape[1]
    slot_table = (
        jnp.full((experts, capacity), token_rows, jnp.int32)
        .at[flat_routes, slot_index]
        .set(token_index)
    )
    slot_gate = (
        jnp.zeros((experts, capacity), jnp.float32)
        .at[flat_routes, slot_index]
        .set(local_gates.reshape(-1))
    )
    return (slot_table, slot_gate)


def block_scores(query_rows, key_block, key_position, query_place, score_scale):
    scores = (
        jnp.einsum("qhgd,khd->qhgk", query_rows, key_block, preferred_element_type=jnp.float32)
        * score_scale
    )
    allowed = key_position[None, None, None, :] <= query_place[:, None, None, None]
    return jnp.where(allowed, scores, masked_score)


def attend_forward(
    query_rows, blocked_keys, blocked_values, place_blocks, query_place, score_scale
):
    head_shape = query_rows.shape[:3]

    def online_step(running, block_args):
        running_max, running_sum, accumulated = running
        key_block, value_block, key_position = block_args
        scores = block_scores(query_rows, key_block, key_position, query_place, score_scale)
        new_max = jnp.maximum(running_max, jnp.max(scores, axis=-1))
        rescale = jnp.exp(running_max - new_max)
        powers = jnp.exp(scores - new_max[..., None])
        new_sum = running_sum * rescale + jnp.sum(powers, axis=-1)
        weighted = jnp.einsum(
            "qhgk,khd->qhgd",
            powers.astype(jnp.bfloat16),
            value_block,
            preferred_element_type=jnp.float32,
        )
        return ((new_max, new_sum, accumulated * rescale[..., None] + weighted), None)

    initial = (
        jnp.full(head_shape, masked_score, jnp.float32),
        jnp.zeros(head_shape, jnp.float32),
        jnp.zeros(query_rows.shape, jnp.float32),
    )
    row_max, row_sum, accumulated = lax.scan(
        online_step, initial, (blocked_keys, blocked_values, place_blocks)
    )[0]
    log_total = row_max + jnp.log(row_sum)
    return (accumulated / row_sum[..., None], log_total)


def attend_backward(
    query_rows,
    blocked_keys,
    blocked_values,
    place_blocks,
    query_place,
    log_total,
    attention_output_gradient,
    attention_output,
    score_scale,
):
    row_delta = jnp.sum(attention_output_gradient.astype(jnp.float32) * attention_output, axis=-1)

    def block_grads(grad_queries, block_args):
        key_block, value_block, key_position = block_args
        scores = block_scores(query_rows, key_block, key_position, query_place, score_scale)
        probabilities = jnp.exp(scores - log_total[..., None])
        grad_probs = jnp.einsum(
            "qhgd,khd->qhgk",
            attention_output_gradient,
            value_block,
            preferred_element_type=jnp.float32,
        )
        grad_scores = (probabilities * (grad_probs - row_delta[..., None])).astype(jnp.bfloat16)
        grad_queries = grad_queries + jnp.einsum(
            "qhgk,khd->qhgd", grad_scores, key_block, preferred_element_type=jnp.float32
        )
        grad_keys = (
            jnp.einsum(
                "qhgk,qhgd->khd", grad_scores, query_rows, preferred_element_type=jnp.float32
            )
            * score_scale
        )
        grad_values = jnp.einsum(
            "qhgk,qhgd->khd",
            probabilities.astype(jnp.bfloat16),
            attention_output_gradient,
            preferred_element_type=jnp.float32,
        )
        return (grad_queries, (grad_keys, grad_values))

    grad_queries, (grad_keys, grad_values) = lax.scan(
        block_grads,
        jnp.zeros(query_rows.shape, jnp.float32),
        (blocked_keys, blocked_values, place_blocks),
    )
    return (grad_queries * score_scale, grad_keys, grad_values)


def gate_up_grads(grad_act, gate_up, hidden_units):
    gate_part = gate_up[..., :hidden_units]
    up_part = gate_up[..., hidden_units:]
    return jnp.concatenate(
        [grad_act * up_part * silu_slope(gate_part), grad_act * sigmoid_linear(gate_part)], axis=-1
    ).astype(jnp.bfloat16)


def on_device(
    hidden,
    teacher,
    valid_mask,
    routes,
    route_gates,
    gain_in,
    query_key_value_weight,
    out_weight,
    gain_mid,
    shared_weight,
    expert_weight,
):
    token_rows = hidden.shape[1]
    model_width = hidden.shape[2]
    context_count = lax.axis_size("ctx")
    shard_count = lax.axis_size("wt")
    seq_rows = token_rows * context_count
    all_tokens = seq_rows * shard_count
    query_groups = QUERY_HEADS // KEY_VALUE_HEADS
    query_total_width = QUERY_HEADS * HEAD_SIZE
    key_value_width = KEY_VALUE_HEADS * HEAD_SIZE
    score_scale = 1.0 / math.sqrt(HEAD_SIZE)
    key_row_count = min(512, seq_rows)
    number_of_blocks = seq_rows // key_row_count
    capacity = token_rows * TOP // 12
    local_experts = expert_weight.shape[0]
    contract_last = (((1,), (1,)), ((), ()))
    contract_first = (((0,), (0,)), ((), ()))
    full_gain_in, full_qkv, full_out, full_gain_mid, full_shared = (
        lax.all_gather(gain_in, "wt", axis=0, tiled=True),
        lax.all_gather(query_key_value_weight, "wt", axis=0, tiled=True),
        lax.all_gather(out_weight, "wt", axis=0, tiled=True),
        lax.all_gather(gain_mid, "wt", axis=0, tiled=True),
        lax.all_gather(shared_weight, "wt", axis=0, tiled=True),
    )
    gain_in_float = full_gain_in.astype(jnp.float32)
    gain_mid_float = full_gain_mid.astype(jnp.float32)
    inputs = hidden[0].astype(jnp.float32)
    scaled_in, inverse_in = normalize(inputs)
    normed_in = (scaled_in * gain_in_float).astype(jnp.bfloat16)
    projected_rows = jnp.dot(normed_in, full_qkv, preferred_element_type=jnp.float32).astype(
        jnp.bfloat16
    )
    query_rows = projected_rows[:, :query_total_width].reshape(
        token_rows, KEY_VALUE_HEADS, query_groups, HEAD_SIZE
    )
    context_local = projected_rows[:, query_total_width:]
    context_gathered = lax.all_gather(context_local, "ctx", axis=0, tiled=True)
    context_index = lax.axis_index("ctx")
    query_place = positions(
        context_index * token_rows + jnp.arange(token_rows, dtype=jnp.int32),
        token_rows,
        context_count,
    )
    place_blocks = positions(
        jnp.arange(seq_rows, dtype=jnp.int32), token_rows, context_count
    ).reshape(number_of_blocks, key_row_count)
    blocked_keys = context_gathered[:, :key_value_width].reshape(
        number_of_blocks, key_row_count, KEY_VALUE_HEADS, HEAD_SIZE
    )
    blocked_values = context_gathered[:, key_value_width:].reshape(
        number_of_blocks, key_row_count, KEY_VALUE_HEADS, HEAD_SIZE
    )
    attention_output, log_total = attend_forward(
        query_rows, blocked_keys, blocked_values, place_blocks, query_place, score_scale
    )
    mixed_rows = attention_output.reshape(token_rows, query_total_width).astype(jnp.bfloat16)
    middle = inputs + jnp.dot(mixed_rows, full_out, preferred_element_type=jnp.float32)
    scaled_mid, inverse_mid = normalize(middle)
    normed_mid = (scaled_mid * gain_mid_float).astype(jnp.bfloat16)
    shared_gate_up = jnp.dot(
        normed_mid, full_shared[:, : 2 * SF], preferred_element_type=jnp.float32
    )
    shared_act = (sigmoid_linear(shared_gate_up[:, :SF]) * shared_gate_up[:, SF:]).astype(
        jnp.bfloat16
    )
    shared_out = lax.dot_general(
        shared_act, full_shared[:, 2 * SF :], contract_last, preferred_element_type=jnp.float32
    )
    slot_table, slot_gate = route_tables(routes[0], route_gates[0], EXPERTS, capacity)
    padded_rows = jnp.concatenate([normed_mid, jnp.zeros((1, model_width), jnp.bfloat16)], axis=0)
    expert_rows = jnp.take(padded_rows, slot_table, axis=0)
    arrived = lax.all_to_all(expert_rows, "wt", split_axis=0, concat_axis=0, tiled=True)
    slot_count = arrived.shape[1]
    grouped = arrived.reshape(shard_count, local_experts, slot_count, model_width)
    owner_gate_up = jnp.einsum(
        "wesd,edf->wesf", grouped, expert_weight[:, :, : 2 * F], preferred_element_type=jnp.float32
    )
    owner_act = (sigmoid_linear(owner_gate_up[..., :F]) * owner_gate_up[..., F:]).astype(
        jnp.bfloat16
    )
    owner_out = jnp.einsum(
        "wesf,edf->wesd",
        owner_act,
        expert_weight[:, :, 2 * F :],
        preferred_element_type=jnp.float32,
    ).astype(jnp.bfloat16)
    returned = lax.all_to_all(
        owner_out.reshape(shard_count * local_experts, slot_count, model_width),
        "wt",
        split_axis=0,
        concat_axis=0,
        tiled=True,
    )
    expert_out, owner_rows, owner_gate_up, owner_act = (
        returned,
        arrived,
        owner_gate_up.reshape(shard_count * local_experts, slot_count, 2 * F),
        owner_act.reshape(shard_count * local_experts, slot_count, F),
    )
    routed = (
        jnp.zeros((token_rows + 1, model_width), jnp.float32)
        .at[slot_table]
        .add(expert_out.astype(jnp.float32) * slot_gate[..., None])[:token_rows]
    )
    final_state = middle + shared_out + routed
    valid_float = valid_mask[0].astype(jnp.float32)
    deviation = final_state - teacher[0].astype(jnp.float32)
    squared_local = jnp.sum(valid_float[:, None] * deviation * deviation)
    count_local = jnp.sum(valid_float)
    squared_total, valid_count = lax.psum((squared_local, count_local), ("ctx", "wt"))
    loss_value = 0.5 * squared_total / (valid_count * model_width)
    grad_final = all_tokens / valid_count * valid_float[:, None] * deviation
    grad_shared_out = grad_final.astype(jnp.bfloat16)
    grad_shared_act = jnp.dot(
        grad_shared_out, full_shared[:, 2 * SF :], preferred_element_type=jnp.float32
    )
    grad_shared_down = lax.dot_general(
        grad_shared_out, shared_act, contract_first, preferred_element_type=jnp.float32
    )
    grad_shared_gate_up = gate_up_grads(grad_shared_act, shared_gate_up, SF)
    grad_normed_mid = lax.dot_general(
        grad_shared_gate_up,
        full_shared[:, : 2 * SF],
        contract_last,
        preferred_element_type=jnp.float32,
    )
    grad_shared_front = lax.dot_general(
        normed_mid, grad_shared_gate_up, contract_first, preferred_element_type=jnp.float32
    )
    grad_shared_full = jnp.concatenate([grad_shared_front, grad_shared_down], axis=1)
    padded_grads = jnp.concatenate([grad_final, jnp.zeros((1, model_width), jnp.float32)], axis=0)
    grad_expert_out = (jnp.take(padded_grads, slot_table, axis=0) * slot_gate[..., None]).astype(
        jnp.bfloat16
    )
    grad_arrived = lax.all_to_all(grad_expert_out, "wt", split_axis=0, concat_axis=0, tiled=True)
    grad_grouped = grad_arrived.reshape(shard_count, local_experts, capacity, model_width)
    owner_gate_up_grouped = owner_gate_up.reshape(shard_count, local_experts, capacity, 2 * F)
    owner_act_grouped = owner_act.reshape(shard_count, local_experts, capacity, F)
    owner_rows_grouped = owner_rows.reshape(shard_count, local_experts, capacity, model_width)
    grad_owner_act = jnp.einsum(
        "wecd,edf->wecf",
        grad_grouped,
        expert_weight[:, :, 2 * F :],
        preferred_element_type=jnp.float32,
    )
    grad_owner_gate_up = gate_up_grads(grad_owner_act, owner_gate_up_grouped, F)
    grad_owner_rows = jnp.einsum(
        "wecf,edf->wecd",
        grad_owner_gate_up,
        expert_weight[:, :, : 2 * F],
        preferred_element_type=jnp.float32,
    ).astype(jnp.bfloat16)
    front = jnp.einsum(
        "wecd,wecf->edf", owner_rows_grouped, grad_owner_gate_up, preferred_element_type=jnp.float32
    )
    back = jnp.einsum(
        "wecd,wecf->edf", grad_grouped, owner_act_grouped, preferred_element_type=jnp.float32
    )
    expert_grad = jnp.concatenate([front, back], axis=2)
    grad_rows = lax.all_to_all(
        grad_owner_rows.reshape(shard_count * local_experts, capacity, model_width),
        "wt",
        split_axis=0,
        concat_axis=0,
        tiled=True,
    )
    grad_normed_mid = (
        grad_normed_mid
        + jnp.zeros((token_rows + 1, model_width), jnp.float32)
        .at[slot_table]
        .add(grad_rows.astype(jnp.float32))[:token_rows]
    )
    grad_gain_mid_local = jnp.sum(grad_normed_mid * scaled_mid, axis=0)
    grad_middle = grad_final + norm_back(grad_normed_mid, scaled_mid, inverse_mid, gain_mid_float)
    grad_branch = grad_middle.astype(jnp.bfloat16)
    mixed_gradient = lax.dot_general(
        grad_branch, full_out, contract_last, preferred_element_type=jnp.float32
    ).astype(jnp.bfloat16)
    grad_out_local = lax.dot_general(
        mixed_rows, grad_branch, contract_first, preferred_element_type=jnp.float32
    )
    context_recomputed = lax.all_gather(context_local, "ctx", axis=0, tiled=True)
    backward_keys = context_recomputed[:, :key_value_width].reshape(
        number_of_blocks, key_row_count, KEY_VALUE_HEADS, HEAD_SIZE
    )
    backward_values = context_recomputed[:, key_value_width:].reshape(
        number_of_blocks, key_row_count, KEY_VALUE_HEADS, HEAD_SIZE
    )
    attention_output_gradient = mixed_gradient.reshape(
        token_rows, KEY_VALUE_HEADS, query_groups, HEAD_SIZE
    )
    grad_queries, grad_keys, grad_values = attend_backward(
        query_rows,
        backward_keys,
        backward_values,
        place_blocks,
        query_place,
        log_total,
        attention_output_gradient,
        attention_output,
        score_scale,
    )
    grad_context_all = jnp.concatenate(
        [
            grad_keys.reshape(seq_rows, key_value_width),
            grad_values.reshape(seq_rows, key_value_width),
        ],
        axis=1,
    )
    grad_context = lax.psum_scatter(
        grad_context_all.astype(jnp.bfloat16), "ctx", scatter_dimension=0, tiled=True
    ).astype(jnp.float32)
    grad_projected = jnp.concatenate(
        [grad_queries.reshape(token_rows, query_total_width), grad_context], axis=1
    ).astype(jnp.bfloat16)
    grad_normed_in = lax.dot_general(
        grad_projected, full_qkv, contract_last, preferred_element_type=jnp.float32
    )
    grad_qkv_local = lax.dot_general(
        normed_in, grad_projected, contract_first, preferred_element_type=jnp.float32
    )
    grad_gain_in_local = jnp.sum(grad_normed_in * scaled_in, axis=0)
    grad_inputs = grad_middle + norm_back(grad_normed_in, scaled_in, inverse_in, gain_in_float)
    weight_sums = (
        lax.psum_scatter(
            grad_gain_in_local.astype(jnp.bfloat16), "wt", scatter_dimension=0, tiled=True
        ).astype(jnp.float32),
        lax.psum_scatter(
            grad_qkv_local.astype(jnp.bfloat16), "wt", scatter_dimension=0, tiled=True
        ).astype(jnp.float32),
        lax.psum_scatter(
            grad_out_local.astype(jnp.bfloat16), "wt", scatter_dimension=0, tiled=True
        ).astype(jnp.float32),
        lax.psum_scatter(
            grad_gain_mid_local.astype(jnp.bfloat16), "wt", scatter_dimension=0, tiled=True
        ).astype(jnp.float32),
        lax.psum_scatter(
            grad_shared_full.astype(jnp.bfloat16), "wt", scatter_dimension=0, tiled=True
        ).astype(jnp.float32),
    )
    summed = (
        lax.psum(weight_sums[0].astype(jnp.bfloat16), "ctx").astype(jnp.float32),
        lax.psum(weight_sums[1].astype(jnp.bfloat16), "ctx").astype(jnp.float32),
        lax.psum(weight_sums[2].astype(jnp.bfloat16), "ctx").astype(jnp.float32),
        lax.psum(weight_sums[3].astype(jnp.bfloat16), "ctx").astype(jnp.float32),
        lax.psum(weight_sums[4].astype(jnp.bfloat16), "ctx").astype(jnp.float32),
        lax.psum(expert_grad.astype(jnp.bfloat16), "ctx").astype(jnp.float32),
    )
    return (
        final_state.astype(jnp.bfloat16)[None],
        loss_value,
        grad_inputs[None],
        summed[0],
        summed[1],
        summed[2],
        summed[3],
        summed[4],
        summed[5],
    )


def flip(value, bit):
    return lax.ppermute(value, "ctx", [(index, index ^ bit) for index in range(8)])


def line_swap(value, offset):
    return lax.ppermute(value, "wt", [(index, index ^ offset) for index in range(4)])


def line_middle(value):
    return lax.ppermute(value, "wt", [(1, 2), (2, 1)])


def line_outward(value):
    return lax.ppermute(value, "wt", [(1, 0), (2, 3)])


def line_inward(value):
    return lax.ppermute(value, "wt", [(0, 1), (3, 2)])


def line_gather(value, at_end):
    near = line_swap(value, 1)
    middle = line_middle(value)
    middle_far = line_middle(near)
    outward = line_outward(middle)
    outward_far = line_outward(middle_far)
    return [
        value,
        near,
        jnp.where(at_end, outward, middle_far),
        jnp.where(at_end, outward_far, middle),
    ]


def line_reduce(parts):
    far = line_inward(parts[3])
    carried = parts[2] + far
    inward = line_inward(carried)
    crossed = line_middle(carried)
    near = line_swap(parts[1] + crossed, 1)
    middle = line_middle(parts[3] + inward)
    return (
        parts[0].astype(jnp.float32) + near.astype(jnp.float32) + middle.astype(jnp.float32)
    )


def chips_gather(value):
    half = value.shape[0] // 2
    along_x = flip(value, 2)
    along_y = flip(value, 4)
    corner = jnp.concatenate([flip(along_x[:half], 4), flip(along_y[half:], 2)], axis=0)
    return [value, along_x, along_y, corner]


def plane_gather(value):
    chips = jnp.stack(chips_gather(value))
    return jnp.stack([chips, flip(chips, 1)], axis=1).reshape((8,) + value.shape)


def pick(blocks, index):
    return lax.dynamic_index_in_dim(blocks, index, 0, keepdims=False)


def plane_reduce(blocks, context_index):
    core = context_index & 1
    x_bit = (context_index >> 1) & 1
    y_bit = context_index >> 2
    rows, columns = blocks.shape[1:]
    by_core = blocks.reshape(4, 2, rows, columns)
    keep = lax.dynamic_index_in_dim(by_core, core, 1, keepdims=False)
    give = lax.dynamic_index_in_dim(by_core, 1 - core, 1, keepdims=False)
    chip_sum = (keep + flip(give, 1)).reshape(2, 2, rows, columns)
    left = chip_sum[..., : columns // 2]
    right = chip_sum[..., columns // 2 :]
    left_x = lax.dynamic_index_in_dim(left, x_bit, 1, keepdims=False) + flip(
        lax.dynamic_index_in_dim(left, 1 - x_bit, 1, keepdims=False), 2
    )
    right_y = pick(right, y_bit) + flip(pick(right, 1 - y_bit), 4)
    left_done = pick(left_x, y_bit) + flip(pick(left_x, 1 - y_bit), 4)
    right_done = pick(right_y, x_bit) + flip(pick(right_y, 1 - x_bit), 2)
    return jnp.concatenate([left_done, right_done], axis=1)


def plane_sum_small(value):
    for bit in (1, 2, 4):
        value = value + flip(value, bit)
    return value


def gated(gate_up, units):
    gate_part = gate_up[:, :units]
    sigma = 1.0 / (1.0 + jnp.exp(-gate_part))
    return gate_part * sigma * gate_up[:, units:]


def gated_back(grad_act, gate_up, units):
    gate_part = gate_up[:, :units].astype(jnp.float32)
    up_part = gate_up[:, units:].astype(jnp.float32)
    sigma = 1.0 / (1.0 + jnp.exp(-gate_part))
    linear = gate_part * sigma
    grad_gate = grad_act * up_part * (sigma * (1.0 + gate_part * (1.0 - sigma)))
    return grad_gate, grad_act * linear, linear * up_part


def dot_plain(left, right):
    return lax.dot_general(
        left, right, (((1,), (0,)), ((), ())), preferred_element_type=jnp.float32
    )


def dot_last(left, right):
    return lax.dot_general(
        left, right, (((1,), (1,)), ((), ())), preferred_element_type=jnp.float32
    )


def dot_first(left, right):
    return lax.dot_general(
        left, right, (((0,), (0,)), ((), ())), preferred_element_type=jnp.float32
    )


def experts_forward_kernel(
    rows_ref, gates_ref, expert_ref, shared_ref, gate_up_ref, shared_gate_up_ref, out_ref, total
):
    expert = pl.program_id(0)
    rows = rows_ref[...]

    @pl.when(expert == 0)
    def _():
        units = shared_ref.shape[1] // 3
        gate_up = dot_plain(rows, shared_ref[:, : 2 * units])
        shared_gate_up_ref[...] = gate_up.astype(jnp.bfloat16)
        act = gated(gate_up, units).astype(jnp.bfloat16)
        total[...] = dot_last(act, shared_ref[:, 2 * units :])

    gate_up = dot_plain(rows, expert_ref[0, :, : 2 * F])
    gate_up_ref[0] = gate_up.astype(jnp.bfloat16)
    act = (gated(gate_up, F) * gates_ref[0]).astype(jnp.bfloat16)
    total[...] += dot_last(act, expert_ref[0, :, 2 * F :])

    @pl.when(expert == pl.num_programs(0) - 1)
    def _():
        out_ref[...] = total[...].astype(jnp.bfloat16)


def experts_forward(rows, gates, expert_weight, shared_slice):
    local_experts, width, _ = expert_weight.shape
    token_rows = rows.shape[0]
    shared_units = shared_slice.shape[1] // 3
    return pl.pallas_call(
        experts_forward_kernel,
        grid=(local_experts,),
        in_specs=[
            pl.BlockSpec((token_rows, width), lambda e: (0, 0)),
            pl.BlockSpec((1, token_rows, 1), lambda e: (e, 0, 0)),
            pl.BlockSpec((1, width, 3 * F), lambda e: (e, 0, 0)),
            pl.BlockSpec((width, 3 * shared_units), lambda e: (0, 0)),
        ],
        out_specs=[
            pl.BlockSpec((1, token_rows, 2 * F), lambda e: (e, 0, 0)),
            pl.BlockSpec((token_rows, 2 * shared_units), lambda e: (0, 0)),
            pl.BlockSpec((token_rows, width), lambda e: (0, 0)),
        ],
        out_shape=[
            jax.ShapeDtypeStruct((local_experts, token_rows, 2 * F), jnp.bfloat16),
            jax.ShapeDtypeStruct((token_rows, 2 * shared_units), jnp.bfloat16),
            jax.ShapeDtypeStruct((token_rows, width), jnp.bfloat16),
        ],
        scratch_shapes=[pltpu.VMEM((token_rows, width), jnp.float32)],
        compiler_params=pltpu.CompilerParams(vmem_limit_bytes=48 * 1024 * 1024),
        name="experts_forward",
    )(rows, gates, expert_weight, shared_slice)


def experts_backward_kernel(
    grad_ref,
    gates_ref,
    gate_up_ref,
    shared_gate_up_ref,
    expert_ref,
    shared_ref,
    grad_gate_up_ref,
    act_ref,
    shared_grad_ref,
    shared_act_ref,
    grad_rows_ref,
    total,
):
    expert = pl.program_id(0)
    grad = grad_ref[...]

    @pl.when(expert == 0)
    def _():
        units = shared_ref.shape[1] // 3
        grad_act = dot_plain(grad, shared_ref[:, 2 * units :])
        grad_gate, grad_up, act = gated_back(grad_act, shared_gate_up_ref[...], units)
        both = jnp.concatenate([grad_gate, grad_up], axis=1).astype(jnp.bfloat16)
        shared_grad_ref[...] = both
        shared_act_ref[...] = act.astype(jnp.bfloat16)
        total[...] = dot_last(both, shared_ref[:, : 2 * units])

    grad_act = dot_plain(grad, expert_ref[0, :, 2 * F :]) * gates_ref[0]
    grad_gate, grad_up, act = gated_back(grad_act, gate_up_ref[0], F)
    both = jnp.concatenate([grad_gate, grad_up], axis=1).astype(jnp.bfloat16)
    grad_gate_up_ref[0] = both
    act_ref[0] = (act * gates_ref[0]).astype(jnp.bfloat16)
    total[...] += dot_last(both, expert_ref[0, :, : 2 * F])

    @pl.when(expert == pl.num_programs(0) - 1)
    def _():
        grad_rows_ref[...] = total[...].astype(jnp.bfloat16)


def experts_backward(grad, gates, gate_up, shared_gate_up, expert_weight, shared_slice):
    local_experts, width, _ = expert_weight.shape
    token_rows = grad.shape[0]
    shared_units = shared_slice.shape[1] // 3
    return pl.pallas_call(
        experts_backward_kernel,
        grid=(local_experts,),
        in_specs=[
            pl.BlockSpec((token_rows, width), lambda e: (0, 0)),
            pl.BlockSpec((1, token_rows, 1), lambda e: (e, 0, 0)),
            pl.BlockSpec((1, token_rows, 2 * F), lambda e: (e, 0, 0)),
            pl.BlockSpec((token_rows, 2 * shared_units), lambda e: (0, 0)),
            pl.BlockSpec((1, width, 3 * F), lambda e: (e, 0, 0)),
            pl.BlockSpec((width, 3 * shared_units), lambda e: (0, 0)),
        ],
        out_specs=[
            pl.BlockSpec((1, token_rows, 2 * F), lambda e: (e, 0, 0)),
            pl.BlockSpec((1, token_rows, F), lambda e: (e, 0, 0)),
            pl.BlockSpec((token_rows, 2 * shared_units), lambda e: (0, 0)),
            pl.BlockSpec((token_rows, shared_units), lambda e: (0, 0)),
            pl.BlockSpec((token_rows, width), lambda e: (0, 0)),
        ],
        out_shape=[
            jax.ShapeDtypeStruct((local_experts, token_rows, 2 * F), jnp.bfloat16),
            jax.ShapeDtypeStruct((local_experts, token_rows, F), jnp.bfloat16),
            jax.ShapeDtypeStruct((token_rows, 2 * shared_units), jnp.bfloat16),
            jax.ShapeDtypeStruct((token_rows, shared_units), jnp.bfloat16),
            jax.ShapeDtypeStruct((token_rows, width), jnp.bfloat16),
        ],
        scratch_shapes=[pltpu.VMEM((token_rows, width), jnp.float32)],
        compiler_params=pltpu.CompilerParams(vmem_limit_bytes=48 * 1024 * 1024),
        name="experts_backward",
    )(grad, gates, gate_up, shared_gate_up, expert_weight, shared_slice)


def weight_grad_kernel(count, *refs):
    rows, grads = refs[:count], refs[count : 2 * count]
    front, acts = refs[2 * count : 3 * count], refs[3 * count : 4 * count]
    out_ref = refs[4 * count]
    split = front[0].shape[-1]
    out_ref[:, :split] = sum(
        dot_first(rows[i][...], front[i][0]) for i in range(count)
    ).astype(jnp.bfloat16)
    out_ref[:, split:] = sum(
        dot_first(grads[i][...], acts[i][0]) for i in range(count)
    ).astype(jnp.bfloat16)


def weight_grad(rows, grads, front, acts, expert):
    count = len(rows)
    token_rows, width = rows[0].shape
    tile = 256
    front_units, act_units = front[0].shape[-1], acts[0].shape[-1]
    column = pl.BlockSpec((token_rows, tile), lambda i: (0, i))
    return pl.pallas_call(
        lambda *refs: weight_grad_kernel(count, *refs),
        grid=(width // tile,),
        in_specs=[column] * (2 * count)
        + [pl.BlockSpec((1, token_rows, front_units), lambda i: (expert, 0, 0))] * count
        + [pl.BlockSpec((1, token_rows, act_units), lambda i: (expert, 0, 0))] * count,
        out_specs=pl.BlockSpec((tile, front_units + act_units), lambda i: (i, 0)),
        out_shape=jax.ShapeDtypeStruct((width, front_units + act_units), jnp.bfloat16),
        compiler_params=pltpu.CompilerParams(vmem_limit_bytes=48 * 1024 * 1024),
        name="weight_grad",
    )(*rows, *grads, *front, *acts)


def plane_places(context_index, token_rows, context_count):
    blocks = (context_index ^ jnp.arange(8, dtype=jnp.int32))[:, None]
    return positions(
        blocks * token_rows + jnp.arange(token_rows, dtype=jnp.int32)[None, :],
        token_rows,
        context_count,
    )


def attention_scores(query, keys, key_place, query_place, scale):
    scores = jnp.einsum("qhd,kd->hqk", query, keys, preferred_element_type=jnp.float32) * scale
    return jnp.where(key_place[None, None, :] <= query_place[None, :, None], scores, masked_score)


def heads_forward(query, keys, values, key_place, query_place, scale):
    scores = attention_scores(query, keys, key_place, query_place, scale)
    highest = jnp.max(scores, axis=-1, keepdims=True)
    powers = jnp.exp(scores - highest)
    total = jnp.sum(powers, axis=-1, keepdims=True)
    mixed = jnp.einsum(
        "hqk,kd->qhd", powers.astype(jnp.bfloat16), values, preferred_element_type=jnp.float32
    ) / jnp.transpose(total, (1, 0, 2))
    return mixed, (highest + jnp.log(total))[..., 0]


def heads_backward(query, keys, values, key_place, query_place, scale, log_total, mixed, grad):
    scores = attention_scores(query, keys, key_place, query_place, scale)
    probs = jnp.exp(scores - log_total[..., None])
    delta = jnp.sum(grad.astype(jnp.float32) * mixed.astype(jnp.float32), axis=-1).T
    grad_probs = jnp.einsum("qhd,kd->hqk", grad, values, preferred_element_type=jnp.float32)
    grad_scores = (probs * (grad_probs - delta[..., None])).astype(jnp.bfloat16)
    grad_query = (
        jnp.einsum("hqk,kd->qhd", grad_scores, keys, preferred_element_type=jnp.float32) * scale
    )
    grad_keys = (
        jnp.einsum("hqk,qhd->kd", grad_scores, query, preferred_element_type=jnp.float32) * scale
    )
    grad_values = jnp.einsum(
        "hqk,qhd->kd", probs.astype(jnp.bfloat16), grad, preferred_element_type=jnp.float32
    )
    return grad_query, grad_keys, grad_values


def fast_device(
    hidden,
    teacher,
    valid_mask,
    routes,
    route_gates,
    gain_in,
    query_key_value_weight,
    out_weight,
    gain_mid,
    shared_weight,
    expert_weight,
):
    token_rows, width = hidden.shape[1:]
    context_count, shard_count = 8, 4
    context_index = lax.axis_index("ctx")
    shard_index = lax.axis_index("wt")
    core = context_index & 1
    chip = context_index >> 1
    at_end = (shard_index == 0) | (shard_index == shard_count - 1)
    four = jnp.arange(4, dtype=jnp.int32)
    eight = jnp.arange(8, dtype=jnp.int32)
    group = QUERY_HEADS // KEY_VALUE_HEADS
    group_width = group * HEAD_SIZE
    query_width = QUERY_HEADS * HEAD_SIZE
    kv_width = KEY_VALUE_HEADS * HEAD_SIZE
    slice_width = group_width + 2 * HEAD_SIZE
    scale = 1.0 / math.sqrt(HEAD_SIZE)
    all_tokens = token_rows * context_count * shard_count
    shard_rows = query_key_value_weight.shape[0]
    half_rows = shard_rows // 2
    local_experts = expert_weight.shape[0]
    bf16, f32 = jnp.bfloat16, jnp.float32

    states = jnp.concatenate(chips_gather(hidden[0]), axis=0).astype(f32)

    gains = jnp.stack([gain_in, gain_mid])
    gains = jnp.stack([gains] + [line_swap(gains, i) for i in (1, 2, 3)])
    gains = jnp.take(gains, shard_index ^ four, axis=0)
    gain_in_float = gains[:, 0].reshape(width).astype(f32)
    gain_mid_float = gains[:, 1].reshape(width).astype(f32)

    def own_heads(rows):
        return jnp.concatenate(
            [
                lax.dynamic_slice_in_dim(rows, chip * group_width, group_width, 1),
                lax.dynamic_slice_in_dim(rows, query_width + chip * HEAD_SIZE, HEAD_SIZE, 1),
                lax.dynamic_slice_in_dim(
                    rows, query_width + kv_width + chip * HEAD_SIZE, HEAD_SIZE, 1
                ),
            ],
            axis=1,
        )

    def both_cores(mine, axis):
        other = flip(mine, 1)
        return jnp.where(
            core == 0, jnp.stack([mine, other], axis=axis), jnp.stack([other, mine], axis=axis)
        )

    def half_shard(rows):
        return lax.dynamic_slice_in_dim(rows, core * half_rows, half_rows, 0)

    qkv_half = jnp.stack(line_gather(own_heads(half_shard(query_key_value_weight)), at_end))
    qkv_slice = jnp.take(both_cores(qkv_half, 1), shard_index ^ four, axis=0).reshape(
        width, slice_width
    )

    scaled_in = states * lax.rsqrt(jnp.mean(states * states, axis=-1, keepdims=True) + norm_eps)
    normed_in = (scaled_in * gain_in_float).astype(bf16)
    projected = jnp.dot(normed_in, qkv_slice, preferred_element_type=f32).astype(bf16)
    key_value = projected[:, group_width:].reshape(4, token_rows, 2 * HEAD_SIZE)
    key_value = jnp.stack([key_value, flip(key_value, 1)], axis=1)
    keys = key_value[..., :HEAD_SIZE].reshape(8 * token_rows, HEAD_SIZE)
    values = key_value[..., HEAD_SIZE:].reshape(8 * token_rows, HEAD_SIZE)
    places = plane_places(context_index, token_rows, context_count)
    key_place = places.reshape(-1)
    query_place = places.reshape(4, 2, token_rows)[:, 0].reshape(-1)
    query = projected[:, :group_width].reshape(4 * token_rows, group, HEAD_SIZE)

    out_half = jnp.stack(line_gather(half_shard(out_weight), at_end))
    out_rel = jnp.take(both_cores(out_half, 1), shard_index ^ chip ^ four, axis=0).reshape(
        query_width, width
    )

    eighth = shard_rows // 8
    shared_piece = lax.dynamic_slice_in_dim(shared_weight, context_index * eighth, eighth, 0)
    shared_units = SF // shard_count
    shared_piece = shared_piece.reshape(eighth, 3, shard_count, shared_units)

    def shared_columns(index):
        return lax.dynamic_index_in_dim(shared_piece, shard_index ^ index, 2, keepdims=False)

    shared_pieces = jnp.stack(
        [shared_columns(0)] + [line_swap(shared_columns(i), i) for i in (1, 2, 3)]
    ).reshape(4 * eighth, 3 * shared_units)
    shared_all = plane_gather(shared_pieces).reshape(8, 4, eighth, 3 * shared_units)
    shared_slice = jnp.transpose(
        jnp.take(jnp.take(shared_all, context_index ^ eight, axis=0), shard_index ^ four, axis=1),
        (1, 0, 2, 3),
    ).reshape(width, 3 * shared_units)

    expert_ids = jnp.arange(EXPERTS, dtype=jnp.int32)
    gate_matrix = jnp.sum(
        jnp.where(
            routes[0][None, :, :] == expert_ids[:, None, None], route_gates[0][None, :, :], 0.0
        ),
        axis=-1,
    ).reshape(shard_count, local_experts, token_rows)
    gates = [pick(gate_matrix, shard_index)] + [
        line_swap(pick(gate_matrix, shard_index ^ i), i) for i in (1, 2, 3)
    ]
    gates = [part[..., None] for part in gates]

    valid_float = valid_mask[0].astype(f32)
    valid_count = plane_sum_small(jnp.full((8, 128), jnp.sum(valid_float), f32))
    valid_count = valid_count + line_swap(valid_count, 1)
    valid_count = (valid_count + line_swap(valid_count, 2))[0, 0]

    mixed_heads, log_total = heads_forward(query, keys, values, key_place, query_place, scale)
    mixed_heads = mixed_heads.reshape(4, token_rows, group_width).astype(bf16)
    mixed = jnp.concatenate(
        [mixed_heads[0]] + [flip(mixed_heads[r], 2 * r) for r in (1, 2, 3)], axis=1
    )
    inputs = hidden[0].astype(f32)
    middle = inputs + jnp.dot(mixed, out_rel, preferred_element_type=f32)
    scaled_mid, inverse_mid = normalize(middle)
    normed_mid = (scaled_mid * gain_mid_float).astype(bf16)

    line_rows = line_gather(normed_mid, at_end)
    forward = [
        experts_forward(line_rows[i], gates[i], expert_weight, shared_slice) for i in range(4)
    ]
    gate_ups, shared_gate_ups, partial_out = zip(*forward)
    final_state = middle + line_reduce(partial_out)

    deviation = final_state - teacher[0].astype(f32)
    squared = jnp.sum(valid_float[:, None] * deviation * deviation)
    squared = plane_sum_small(jnp.full((8, 128), squared, f32))
    squared = squared + line_swap(squared, 1)
    squared = (squared + line_swap(squared, 2))[0, 0]
    loss_value = 0.5 * squared / (valid_count * width)
    grad_final = all_tokens / valid_count * valid_float[:, None] * deviation

    line_grads = line_gather(grad_final.astype(bf16), at_end)
    backward = [
        experts_backward(
            line_grads[i], gates[i], gate_ups[i], shared_gate_ups[i], expert_weight, shared_slice
        )
        for i in range(4)
    ]
    grad_gate_ups, acts, shared_grads, shared_acts, partial_rows = zip(*backward)
    grad_normed_mid = line_reduce(partial_rows)

    grad_experts = []
    for expert in range(local_experts):
        own = weight_grad(line_rows, line_grads, grad_gate_ups, acts, expert)
        reduced = plane_reduce(own.reshape(8, width // 8, 3 * F), context_index)
        gathered = jnp.take(plane_gather(reduced), context_index ^ eight, axis=0)
        grad_experts.append(gathered.reshape(width, 3 * F).astype(f32))
    grad_experts = jnp.stack(grad_experts)

    own = weight_grad(
        line_rows, line_grads, [v[None] for v in shared_grads], [v[None] for v in shared_acts], 0
    )
    own = jnp.transpose(own.reshape(4, 8, eighth, 3 * shared_units), (1, 0, 2, 3))
    reduced = plane_reduce(own.reshape(8, 4 * eighth, 3 * shared_units), context_index)
    reduced = reduced.reshape(4, eighth, 3 * shared_units)
    reduced = jnp.stack(
        [pick(reduced, shard_index)]
        + [line_swap(pick(reduced, shard_index ^ i), i) for i in (1, 2, 3)]
    )
    gathered = jnp.take(plane_gather(reduced), context_index ^ eight, axis=0)
    gathered = jnp.take(gathered, shard_index ^ four, axis=1)
    grad_shared = jnp.transpose(
        gathered.reshape(8, 4, eighth, 3, shared_units), (0, 2, 3, 1, 4)
    ).reshape(shard_rows, 3 * SF)
    grad_shared = grad_shared.astype(f32)

    grad_gain_mid = jnp.sum(grad_normed_mid * scaled_mid, axis=0)
    grad_middle = grad_final + norm_back(grad_normed_mid, scaled_mid, inverse_mid, gain_mid_float)
    grad_branch = grad_middle.astype(bf16)
    grad_mixed = dot_last(grad_branch, out_rel).astype(bf16)
    grad_mixed = jnp.stack(
        [grad_mixed[:, :group_width]]
        + [
            flip(grad_mixed[:, r * group_width : (r + 1) * group_width], 2 * r)
            for r in (1, 2, 3)
        ]
    )

    grad_out = dot_first(mixed, grad_branch).astype(bf16).reshape(4, 2, half_rows, width)
    grad_out = lax.dynamic_index_in_dim(grad_out, core, 1, keepdims=False) + flip(
        lax.dynamic_index_in_dim(grad_out, 1 - core, 1, keepdims=False), 1
    )
    grad_out = line_reduce([pick(grad_out, chip ^ shard_index ^ i) for i in range(4)]).astype(bf16)
    left, right = grad_out[:, : width // 2], grad_out[:, width // 2 :]
    left = left + flip(left, 2)
    right = right + flip(right, 4)
    left = left + flip(left, 4)
    right = right + flip(right, 2)
    grad_out = both_cores(jnp.concatenate([left, right], axis=1), 0)
    grad_out = grad_out.reshape(shard_rows, width).astype(f32)

    grad_query, grad_keys, grad_values = heads_backward(
        query,
        keys,
        values,
        key_place,
        query_place,
        scale,
        log_total,
        mixed_heads.reshape(4 * token_rows, group, HEAD_SIZE),
        grad_mixed.reshape(4 * token_rows, group, HEAD_SIZE),
    )
    grad_kv = jnp.concatenate([grad_keys, grad_values], axis=1)
    grad_kv = grad_kv.reshape(4, 2, token_rows, 2 * HEAD_SIZE)
    grad_kv = grad_kv[:, 0] + flip(grad_kv[:, 1].astype(bf16), 1).astype(f32)
    grad_projected = jnp.concatenate(
        [
            grad_query.astype(bf16).reshape(4 * token_rows, group_width),
            grad_kv.astype(bf16).reshape(4 * token_rows, 2 * HEAD_SIZE),
        ],
        axis=1,
    )

    grad_qkv = dot_first(normed_in, grad_projected).astype(bf16)
    grad_qkv = grad_qkv.reshape(4, 2, half_rows, slice_width)
    grad_qkv = lax.dynamic_index_in_dim(grad_qkv, core, 1, keepdims=False) + flip(
        lax.dynamic_index_in_dim(grad_qkv, 1 - core, 1, keepdims=False), 1
    )
    grad_qkv = line_reduce([pick(grad_qkv, shard_index ^ i) for i in range(4)]).astype(bf16)
    grad_qkv = jnp.stack(chips_gather(grad_qkv))
    grad_qkv = jnp.take(both_cores(grad_qkv, 1), chip ^ four, axis=0).astype(f32)
    grad_qkv = grad_qkv.reshape(4, shard_rows, slice_width)

    def side_by_side(columns):
        return jnp.transpose(columns, (1, 0, 2)).reshape(shard_rows, -1)

    grad_qkv = jnp.concatenate(
        [
            side_by_side(grad_qkv[..., :group_width]),
            side_by_side(grad_qkv[..., group_width : group_width + HEAD_SIZE]),
            side_by_side(grad_qkv[..., group_width + HEAD_SIZE :]),
        ],
        axis=1,
    )

    qkv_rel = both_cores(
        jnp.stack(
            chips_gather(lax.dynamic_slice_in_dim(qkv_slice, core * (width // 2), width // 2, 0))
        ),
        1,
    ).reshape(4, width, slice_width)
    grad_projected = grad_projected.reshape(4, token_rows, slice_width)
    grad_projected = jnp.concatenate(
        [grad_projected[0]] + [flip(grad_projected[r], 2 * r) for r in (1, 2, 3)], axis=1
    )
    qkv_rel = jnp.transpose(qkv_rel, (1, 0, 2)).reshape(width, 4 * slice_width)
    grad_normed_in = dot_last(grad_projected, qkv_rel)
    scaled_own, inverse_own = normalize(inputs)
    grad_gain_in = jnp.sum(grad_normed_in * scaled_own, axis=0)
    grad_inputs = grad_middle + norm_back(grad_normed_in, scaled_own, inverse_own, gain_in_float)

    def gain_sum(local):
        parts = local.reshape(shard_count, shard_rows)
        mine = pick(parts, shard_index)
        for i in (1, 2, 3):
            mine = mine + line_swap(pick(parts, shard_index ^ i), i)
        return plane_sum_small(mine)

    return (
        final_state.astype(bf16)[None],
        loss_value,
        grad_inputs[None],
        gain_sum(grad_gain_in),
        grad_qkv,
        grad_out,
        gain_sum(grad_gain_mid),
        grad_shared,
        grad_experts,
    )


def solution(mesh):
    in_specs = (
        P("wt", "ctx", None),
        P("wt", "ctx", None),
        P("wt", "ctx"),
        P("wt", "ctx", None),
        P("wt", "ctx", None),
        P("wt"),
        P("wt", None),
        P("wt", None),
        P("wt"),
        P("wt", None),
        P("wt", None, None),
    )
    out_specs = (
        P("wt", "ctx", None),
        P(),
        P("wt", "ctx", None),
        P("wt"),
        P("wt", None),
        P("wt", None),
        P("wt"),
        P("wt", None),
        P("wt", None, None),
    )
    plane_of_eight = dict(mesh.shape) == {"ctx": 8, "wt": 4}
    return jax.shard_map(
        fast_device if plane_of_eight else on_device, mesh=mesh, in_specs=in_specs, out_specs=out_specs, check_vma=False
    )
```

```python
import functools
import math

import jax
import jax.numpy as jnp
from jax import lax
from jax.experimental import pallas as pl
from jax.experimental.pallas import tpu as pltpu
from jax.sharding import PartitionSpec as P

QUERY_HEADS = 12
KEY_VALUE_HEADS = 4
HEAD_SIZE = 128
F = 512
SF = 1024
EXPERTS = 16
TOP = 6


norm_eps = 1e-05
masked_score = -1e30


def sigmoid_linear(values):
    return values * jax.nn.sigmoid(values)


def silu_slope(values):
    sigma_value = jax.nn.sigmoid(values)
    return sigma_value * (1.0 + values * (1.0 - sigma_value))


def normalize(values):
    inverse = lax.rsqrt(jnp.mean(values * values, axis=-1, keepdims=True) + norm_eps)
    return (values * inverse, inverse)


def norm_back(grad_normed, scaled, inverse, gain_vector):
    grad_scaled = grad_normed * gain_vector
    return inverse * (grad_scaled - scaled * jnp.mean(grad_scaled * scaled, axis=-1, keepdims=True))


def positions(row_ids, token_rows, context_count):
    piece_index = row_ids // token_rows
    within = row_ids % token_rows
    half_rows = token_rows // 2
    mirrored = jnp.where(within < half_rows, piece_index, 2 * context_count - 1 - piece_index)
    return mirrored * half_rows + within % half_rows


def route_tables(local_routes, local_gates, experts, capacity):
    token_rows = local_routes.shape[0]
    flat_routes = local_routes.reshape(-1)
    one_hot = (flat_routes[:, None] == jnp.arange(experts, dtype=jnp.int32)[None, :]).astype(
        jnp.int32
    )
    earlier = jnp.cumsum(one_hot, axis=0) - one_hot
    slot_index = jnp.sum(earlier * one_hot, axis=1)
    token_index = jnp.arange(flat_routes.shape[0], dtype=jnp.int32) // local_routes.shape[1]
    slot_table = (
        jnp.full((experts, capacity), token_rows, jnp.int32)
        .at[flat_routes, slot_index]
        .set(token_index)
    )
    slot_gate = (
        jnp.zeros((experts, capacity), jnp.float32)
        .at[flat_routes, slot_index]
        .set(local_gates.reshape(-1))
    )
    return (slot_table, slot_gate)


def block_scores(query_rows, key_block, key_position, query_place, score_scale):
    scores = (
        jnp.einsum("qhgd,khd->qhgk", query_rows, key_block, preferred_element_type=jnp.float32)
        * score_scale
    )
    allowed = key_position[None, None, None, :] <= query_place[:, None, None, None]
    return jnp.where(allowed, scores, masked_score)


def attend_forward(
    query_rows, blocked_keys, blocked_values, place_blocks, query_place, score_scale
):
    head_shape = query_rows.shape[:3]

    def online_step(running, block_args):
        running_max, running_sum, accumulated = running
        key_block, value_block, key_position = block_args
        scores = block_scores(query_rows, key_block, key_position, query_place, score_scale)
        new_max = jnp.maximum(running_max, jnp.max(scores, axis=-1))
        rescale = jnp.exp(running_max - new_max)
        powers = jnp.exp(scores - new_max[..., None])
        new_sum = running_sum * rescale + jnp.sum(powers, axis=-1)
        weighted = jnp.einsum(
            "qhgk,khd->qhgd",
            powers.astype(jnp.bfloat16),
            value_block,
            preferred_element_type=jnp.float32,
        )
        return ((new_max, new_sum, accumulated * rescale[..., None] + weighted), None)

    initial = (
        jnp.full(head_shape, masked_score, jnp.float32),
        jnp.zeros(head_shape, jnp.float32),
        jnp.zeros(query_rows.shape, jnp.float32),
    )
    row_max, row_sum, accumulated = lax.scan(
        online_step, initial, (blocked_keys, blocked_values, place_blocks)
    )[0]
    log_total = row_max + jnp.log(row_sum)
    return (accumulated / row_sum[..., None], log_total)


def attend_backward(
    query_rows,
    blocked_keys,
    blocked_values,
    place_blocks,
    query_place,
    log_total,
    attention_output_gradient,
    attention_output,
    score_scale,
):
    row_delta = jnp.sum(attention_output_gradient.astype(jnp.float32) * attention_output, axis=-1)

    def block_grads(grad_queries, block_args):
        key_block, value_block, key_position = block_args
        scores = block_scores(query_rows, key_block, key_position, query_place, score_scale)
        probabilities = jnp.exp(scores - log_total[..., None])
        grad_probs = jnp.einsum(
            "qhgd,khd->qhgk",
            attention_output_gradient,
            value_block,
            preferred_element_type=jnp.float32,
        )
        grad_scores = (probabilities * (grad_probs - row_delta[..., None])).astype(jnp.bfloat16)
        grad_queries = grad_queries + jnp.einsum(
            "qhgk,khd->qhgd", grad_scores, key_block, preferred_element_type=jnp.float32
        )
        grad_keys = (
            jnp.einsum(
                "qhgk,qhgd->khd", grad_scores, query_rows, preferred_element_type=jnp.float32
            )
            * score_scale
        )
        grad_values = jnp.einsum(
            "qhgk,qhgd->khd",
            probabilities.astype(jnp.bfloat16),
            attention_output_gradient,
            preferred_element_type=jnp.float32,
        )
        return (grad_queries, (grad_keys, grad_values))

    grad_queries, (grad_keys, grad_values) = lax.scan(
        block_grads,
        jnp.zeros(query_rows.shape, jnp.float32),
        (blocked_keys, blocked_values, place_blocks),
    )
    return (grad_queries * score_scale, grad_keys, grad_values)


def gate_up_grads(grad_act, gate_up, hidden_units):
    gate_part = gate_up[..., :hidden_units]
    up_part = gate_up[..., hidden_units:]
    return jnp.concatenate(
        [grad_act * up_part * silu_slope(gate_part), grad_act * sigmoid_linear(gate_part)], axis=-1
    ).astype(jnp.bfloat16)


def on_device(
    hidden,
    teacher,
    valid_mask,
    routes,
    route_gates,
    gain_in,
    query_key_value_weight,
    out_weight,
    gain_mid,
    shared_weight,
    expert_weight,
):
    token_rows = hidden.shape[1]
    model_width = hidden.shape[2]
    context_count = lax.axis_size("ctx")
    shard_count = lax.axis_size("wt")
    seq_rows = token_rows * context_count
    all_tokens = seq_rows * shard_count
    query_groups = QUERY_HEADS // KEY_VALUE_HEADS
    query_total_width = QUERY_HEADS * HEAD_SIZE
    key_value_width = KEY_VALUE_HEADS * HEAD_SIZE
    score_scale = 1.0 / math.sqrt(HEAD_SIZE)
    key_row_count = min(512, seq_rows)
    number_of_blocks = seq_rows // key_row_count
    capacity = token_rows * TOP // 12
    local_experts = expert_weight.shape[0]
    contract_last = (((1,), (1,)), ((), ()))
    contract_first = (((0,), (0,)), ((), ()))
    full_gain_in, full_qkv, full_out, full_gain_mid, full_shared = (
        lax.all_gather(gain_in, "wt", axis=0, tiled=True),
        lax.all_gather(query_key_value_weight, "wt", axis=0, tiled=True),
        lax.all_gather(out_weight, "wt", axis=0, tiled=True),
        lax.all_gather(gain_mid, "wt", axis=0, tiled=True),
        lax.all_gather(shared_weight, "wt", axis=0, tiled=True),
    )
    gain_in_float = full_gain_in.astype(jnp.float32)
    gain_mid_float = full_gain_mid.astype(jnp.float32)
    inputs = hidden[0].astype(jnp.float32)
    scaled_in, inverse_in = normalize(inputs)
    normed_in = (scaled_in * gain_in_float).astype(jnp.bfloat16)
    projected_rows = jnp.dot(normed_in, full_qkv, preferred_element_type=jnp.float32).astype(
        jnp.bfloat16
    )
    query_rows = projected_rows[:, :query_total_width].reshape(
        token_rows, KEY_VALUE_HEADS, query_groups, HEAD_SIZE
    )
    context_local = projected_rows[:, query_total_width:]
    context_gathered = lax.all_gather(context_local, "ctx", axis=0, tiled=True)
    context_index = lax.axis_index("ctx")
    query_place = positions(
        context_index * token_rows + jnp.arange(token_rows, dtype=jnp.int32),
        token_rows,
        context_count,
    )
    place_blocks = positions(
        jnp.arange(seq_rows, dtype=jnp.int32), token_rows, context_count
    ).reshape(number_of_blocks, key_row_count)
    blocked_keys = context_gathered[:, :key_value_width].reshape(
        number_of_blocks, key_row_count, KEY_VALUE_HEADS, HEAD_SIZE
    )
    blocked_values = context_gathered[:, key_value_width:].reshape(
        number_of_blocks, key_row_count, KEY_VALUE_HEADS, HEAD_SIZE
    )
    attention_output, log_total = attend_forward(
        query_rows, blocked_keys, blocked_values, place_blocks, query_place, score_scale
    )
    mixed_rows = attention_output.reshape(token_rows, query_total_width).astype(jnp.bfloat16)
    middle = inputs + jnp.dot(mixed_rows, full_out, preferred_element_type=jnp.float32)
    scaled_mid, inverse_mid = normalize(middle)
    normed_mid = (scaled_mid * gain_mid_float).astype(jnp.bfloat16)
    shared_gate_up = jnp.dot(
        normed_mid, full_shared[:, : 2 * SF], preferred_element_type=jnp.float32
    )
    shared_act = (sigmoid_linear(shared_gate_up[:, :SF]) * shared_gate_up[:, SF:]).astype(
        jnp.bfloat16
    )
    shared_out = lax.dot_general(
        shared_act, full_shared[:, 2 * SF :], contract_last, preferred_element_type=jnp.float32
    )
    slot_table, slot_gate = route_tables(routes[0], route_gates[0], EXPERTS, capacity)
    padded_rows = jnp.concatenate([normed_mid, jnp.zeros((1, model_width), jnp.bfloat16)], axis=0)
    expert_rows = jnp.take(padded_rows, slot_table, axis=0)
    arrived = lax.all_to_all(expert_rows, "wt", split_axis=0, concat_axis=0, tiled=True)
    slot_count = arrived.shape[1]
    grouped = arrived.reshape(shard_count, local_experts, slot_count, model_width)
    owner_gate_up = jnp.einsum(
        "wesd,edf->wesf", grouped, expert_weight[:, :, : 2 * F], preferred_element_type=jnp.float32
    )
    owner_act = (sigmoid_linear(owner_gate_up[..., :F]) * owner_gate_up[..., F:]).astype(
        jnp.bfloat16
    )
    owner_out = jnp.einsum(
        "wesf,edf->wesd",
        owner_act,
        expert_weight[:, :, 2 * F :],
        preferred_element_type=jnp.float32,
    ).astype(jnp.bfloat16)
    returned = lax.all_to_all(
        owner_out.reshape(shard_count * local_experts, slot_count, model_width),
        "wt",
        split_axis=0,
        concat_axis=0,
        tiled=True,
    )
    expert_out, owner_rows, owner_gate_up, owner_act = (
        returned,
        arrived,
        owner_gate_up.reshape(shard_count * local_experts, slot_count, 2 * F),
        owner_act.reshape(shard_count * local_experts, slot_count, F),
    )
    routed = (
        jnp.zeros((token_rows + 1, model_width), jnp.float32)
        .at[slot_table]
        .add(expert_out.astype(jnp.float32) * slot_gate[..., None])[:token_rows]
    )
    final_state = middle + shared_out + routed
    valid_float = valid_mask[0].astype(jnp.float32)
    deviation = final_state - teacher[0].astype(jnp.float32)
    squared_local = jnp.sum(valid_float[:, None] * deviation * deviation)
    count_local = jnp.sum(valid_float)
    squared_total, valid_count = lax.psum((squared_local, count_local), ("ctx", "wt"))
    loss_value = 0.5 * squared_total / (valid_count * model_width)
    grad_final = all_tokens / valid_count * valid_float[:, None] * deviation
    grad_shared_out = grad_final.astype(jnp.bfloat16)
    grad_shared_act = jnp.dot(
        grad_shared_out, full_shared[:, 2 * SF :], preferred_element_type=jnp.float32
    )
    grad_shared_down = lax.dot_general(
        grad_shared_out, shared_act, contract_first, preferred_element_type=jnp.float32
    )
    grad_shared_gate_up = gate_up_grads(grad_shared_act, shared_gate_up, SF)
    grad_normed_mid = lax.dot_general(
        grad_shared_gate_up,
        full_shared[:, : 2 * SF],
        contract_last,
        preferred_element_type=jnp.float32,
    )
    grad_shared_front = lax.dot_general(
        normed_mid, grad_shared_gate_up, contract_first, preferred_element_type=jnp.float32
    )
    grad_shared_full = jnp.concatenate([grad_shared_front, grad_shared_down], axis=1)
    padded_grads = jnp.concatenate([grad_final, jnp.zeros((1, model_width), jnp.float32)], axis=0)
    grad_expert_out = (jnp.take(padded_grads, slot_table, axis=0) * slot_gate[..., None]).astype(
        jnp.bfloat16
    )
    grad_arrived = lax.all_to_all(grad_expert_out, "wt", split_axis=0, concat_axis=0, tiled=True)
    grad_grouped = grad_arrived.reshape(shard_count, local_experts, capacity, model_width)
    owner_gate_up_grouped = owner_gate_up.reshape(shard_count, local_experts, capacity, 2 * F)
    owner_act_grouped = owner_act.reshape(shard_count, local_experts, capacity, F)
    owner_rows_grouped = owner_rows.reshape(shard_count, local_experts, capacity, model_width)
    grad_owner_act = jnp.einsum(
        "wecd,edf->wecf",
        grad_grouped,
        expert_weight[:, :, 2 * F :],
        preferred_element_type=jnp.float32,
    )
    grad_owner_gate_up = gate_up_grads(grad_owner_act, owner_gate_up_grouped, F)
    grad_owner_rows = jnp.einsum(
        "wecf,edf->wecd",
        grad_owner_gate_up,
        expert_weight[:, :, : 2 * F],
        preferred_element_type=jnp.float32,
    ).astype(jnp.bfloat16)
    front = jnp.einsum(
        "wecd,wecf->edf", owner_rows_grouped, grad_owner_gate_up, preferred_element_type=jnp.float32
    )
    back = jnp.einsum(
        "wecd,wecf->edf", grad_grouped, owner_act_grouped, preferred_element_type=jnp.float32
    )
    expert_grad = jnp.concatenate([front, back], axis=2)
    grad_rows = lax.all_to_all(
        grad_owner_rows.reshape(shard_count * local_experts, capacity, model_width),
        "wt",
        split_axis=0,
        concat_axis=0,
        tiled=True,
    )
    grad_normed_mid = (
        grad_normed_mid
        + jnp.zeros((token_rows + 1, model_width), jnp.float32)
        .at[slot_table]
        .add(grad_rows.astype(jnp.float32))[:token_rows]
    )
    grad_gain_mid_local = jnp.sum(grad_normed_mid * scaled_mid, axis=0)
    grad_middle = grad_final + norm_back(grad_normed_mid, scaled_mid, inverse_mid, gain_mid_float)
    grad_branch = grad_middle.astype(jnp.bfloat16)
    mixed_gradient = lax.dot_general(
        grad_branch, full_out, contract_last, preferred_element_type=jnp.float32
    ).astype(jnp.bfloat16)
    grad_out_local = lax.dot_general(
        mixed_rows, grad_branch, contract_first, preferred_element_type=jnp.float32
    )
    context_recomputed = lax.all_gather(context_local, "ctx", axis=0, tiled=True)
    backward_keys = context_recomputed[:, :key_value_width].reshape(
        number_of_blocks, key_row_count, KEY_VALUE_HEADS, HEAD_SIZE
    )
    backward_values = context_recomputed[:, key_value_width:].reshape(
        number_of_blocks, key_row_count, KEY_VALUE_HEADS, HEAD_SIZE
    )
    attention_output_gradient = mixed_gradient.reshape(
        token_rows, KEY_VALUE_HEADS, query_groups, HEAD_SIZE
    )
    grad_queries, grad_keys, grad_values = attend_backward(
        query_rows,
        backward_keys,
        backward_values,
        place_blocks,
        query_place,
        log_total,
        attention_output_gradient,
        attention_output,
        score_scale,
    )
    grad_context_all = jnp.concatenate(
        [
            grad_keys.reshape(seq_rows, key_value_width),
            grad_values.reshape(seq_rows, key_value_width),
        ],
        axis=1,
    )
    grad_context = lax.psum_scatter(
        grad_context_all.astype(jnp.bfloat16), "ctx", scatter_dimension=0, tiled=True
    ).astype(jnp.float32)
    grad_projected = jnp.concatenate(
        [grad_queries.reshape(token_rows, query_total_width), grad_context], axis=1
    ).astype(jnp.bfloat16)
    grad_normed_in = lax.dot_general(
        grad_projected, full_qkv, contract_last, preferred_element_type=jnp.float32
    )
    grad_qkv_local = lax.dot_general(
        normed_in, grad_projected, contract_first, preferred_element_type=jnp.float32
    )
    grad_gain_in_local = jnp.sum(grad_normed_in * scaled_in, axis=0)
    grad_inputs = grad_middle + norm_back(grad_normed_in, scaled_in, inverse_in, gain_in_float)
    weight_sums = (
        lax.psum_scatter(
            grad_gain_in_local.astype(jnp.bfloat16), "wt", scatter_dimension=0, tiled=True
        ).astype(jnp.float32),
        lax.psum_scatter(
            grad_qkv_local.astype(jnp.bfloat16), "wt", scatter_dimension=0, tiled=True
        ).astype(jnp.float32),
        lax.psum_scatter(
            grad_out_local.astype(jnp.bfloat16), "wt", scatter_dimension=0, tiled=True
        ).astype(jnp.float32),
        lax.psum_scatter(
            grad_gain_mid_local.astype(jnp.bfloat16), "wt", scatter_dimension=0, tiled=True
        ).astype(jnp.float32),
        lax.psum_scatter(
            grad_shared_full.astype(jnp.bfloat16), "wt", scatter_dimension=0, tiled=True
        ).astype(jnp.float32),
    )
    summed = (
        lax.psum(weight_sums[0].astype(jnp.bfloat16), "ctx").astype(jnp.float32),
        lax.psum(weight_sums[1].astype(jnp.bfloat16), "ctx").astype(jnp.float32),
        lax.psum(weight_sums[2].astype(jnp.bfloat16), "ctx").astype(jnp.float32),
        lax.psum(weight_sums[3].astype(jnp.bfloat16), "ctx").astype(jnp.float32),
        lax.psum(weight_sums[4].astype(jnp.bfloat16), "ctx").astype(jnp.float32),
        lax.psum(expert_grad.astype(jnp.bfloat16), "ctx").astype(jnp.float32),
    )
    return (
        final_state.astype(jnp.bfloat16)[None],
        loss_value,
        grad_inputs[None],
        summed[0],
        summed[1],
        summed[2],
        summed[3],
        summed[4],
        summed[5],
    )


def flip(value, bit):
    return lax.ppermute(value, "ctx", [(index, index ^ bit) for index in range(8)])


def line_swap(value, offset):
    return lax.ppermute(value, "wt", [(index, index ^ offset) for index in range(4)])


def line_middle(value):
    return lax.ppermute(value, "wt", [(1, 2), (2, 1)])


def line_outward(value):
    return lax.ppermute(value, "wt", [(1, 0), (2, 3)])


def line_inward(value):
    return lax.ppermute(value, "wt", [(0, 1), (3, 2)])


def line_gather(value, at_end):
    near = line_swap(value, 1)
    middle = line_middle(value)
    middle_far = line_middle(near)
    outward = line_outward(middle)
    outward_far = line_outward(middle_far)
    return [
        value,
        near,
        jnp.where(at_end, outward, middle_far),
        jnp.where(at_end, outward_far, middle),
    ]


def line_reduce(parts):
    far = line_inward(parts[3])
    carried = parts[2] + far
    inward = line_inward(carried)
    crossed = line_middle(carried)
    near = line_swap(parts[1] + crossed, 1)
    middle = line_middle(parts[3] + inward)
    return (
        parts[0].astype(jnp.float32) + near.astype(jnp.float32) + middle.astype(jnp.float32)
    )


def chips_swap(values):
    return [values[0]] + [flip(values[r], 2 * r) for r in (1, 2, 3)]


def chips_gather(value, x_last):
    along_x = flip(value, 2)
    along_y = flip(value, 4)
    corner = flip(along_y, 2) if x_last else flip(along_x, 4)
    return [value, along_x, along_y, corner]


def core_swap(values):
    return [flip(value, 1) for value in values]


def everywhere_sum(value):
    for bit in (1, 2, 4):
        value = value + flip(value, bit)
    for offset in (1, 2):
        value = value + line_swap(value, offset)
    return value


def pick(blocks, index):
    return lax.dynamic_index_in_dim(blocks, index, 0, keepdims=False)


def chips_reduce(keep, came):
    half = keep.shape[1] // 2
    upper = keep[:, :half] + came[:, :half]
    lower = keep[:, half:] + came[:, half:]
    upper_came = flip(upper[1::2], 2)
    lower_came = flip(lower[2:], 4)
    upper = upper[0::2] + upper_came
    lower = lower[:2] + lower_came
    upper_came = flip(upper[1], 4)
    lower_came = flip(lower[1], 2)
    return jnp.concatenate([upper[0] + upper_came, lower[0] + lower_came], axis=0)


def dot_plain(left, right):
    return lax.dot_general(
        left, right, (((1,), (0,)), ((), ())), preferred_element_type=jnp.float32
    )


def dot_last(left, right):
    return lax.dot_general(
        left, right, (((1,), (1,)), ((), ())), preferred_element_type=jnp.float32
    )


def dot_first(left, right):
    return lax.dot_general(
        left, right, (((0,), (0,)), ((), ())), preferred_element_type=jnp.float32
    )


def call(kernel, name, meta, arrays, grid, in_specs, out_specs, out_shape, scratch, flops, moved):
    return pl.pallas_call(
        kernel,
        grid_spec=pltpu.PrefetchScalarGridSpec(
            num_scalar_prefetch=1,
            grid=grid,
            in_specs=in_specs,
            out_specs=out_specs,
            scratch_shapes=scratch,
        ),
        out_shape=out_shape,
        compiler_params=pltpu.CompilerParams(vmem_limit_bytes=48 * 1024 * 1024),
        cost_estimate=pl.CostEstimate(
            flops=int(flops), bytes_accessed=int(moved), transcendentals=0
        ),
        name=name,
    )(meta, *arrays)


def whole(array):
    rank = len(array.shape)
    return pl.BlockSpec(tuple(array.shape), lambda *_: (0,) * rank)


def shape_of(shape, dtype):
    return jax.ShapeDtypeStruct(shape, dtype)


def size_of(arrays):
    return sum(math.prod(a.shape) * a.dtype.itemsize for a in arrays)


def aligned(value, step):
    return pl.multiple_of(value * step, step)


def project_kernel(meta, *refs):
    blocks, gain_ref = refs[:4], refs[4]
    mine, other = refs[5:9], refs[9:13]
    normed_ref, query_ref, pair_ref, weight_ref, held = refs[13:]
    step = pl.program_id(0)
    core, shard = meta[0] & 1, meta[1]
    rows = mine[0].shape[0]

    @pl.when(step == 0)
    def _():
        for i in range(4):
            at = 2 * (shard ^ i)
            weight_ref[pl.ds(aligned(at + core, rows), rows), :] = mine[i][...]
            weight_ref[pl.ds(aligned(at + 1 - core, rows), rows), :] = other[i][...]

    for r in range(4):

        @pl.when(step == r)
        def _():
            held[...] = blocks[r][...]

    states = held[...].astype(jnp.float32)
    inverse = lax.rsqrt(jnp.mean(states * states, axis=-1, keepdims=True) + norm_eps)
    normed = (states * inverse * gain_ref[...]).astype(jnp.bfloat16)
    normed_ref[0] = normed
    projected = dot_plain(normed, weight_ref[...]).astype(jnp.bfloat16)
    query_width = query_ref.shape[-1]
    query_ref[0] = projected[:, :query_width]
    pair_ref[0] = projected[:, query_width:]


def project(meta, blocks, gain, mine, other, query_width):
    token_rows, width = blocks[0].shape
    columns = mine[0].shape[1]
    arrays = list(blocks) + [gain] + list(mine) + list(other)
    outs = [
        shape_of((4, token_rows, width), jnp.bfloat16),
        shape_of((4, token_rows, query_width), jnp.bfloat16),
        shape_of((4, token_rows, columns - query_width), jnp.bfloat16),
        shape_of((width, columns), jnp.bfloat16),
    ]
    return call(
        project_kernel,
        "project",
        meta,
        arrays,
        (4,),
        [whole(a) for a in arrays],
        [
            pl.BlockSpec((1, token_rows, width), lambda r, m: (r, 0, 0)),
            pl.BlockSpec((1, token_rows, query_width), lambda r, m: (r, 0, 0)),
            pl.BlockSpec((1, token_rows, columns - query_width), lambda r, m: (r, 0, 0)),
            whole(outs[3]),
        ],
        outs,
        [pltpu.VMEM((token_rows, width), jnp.bfloat16)],
        2 * 4 * token_rows * width * columns,
        size_of(arrays) + size_of(outs),
    )


def sort_pairs(meta, mine_ref, other_ref, keys, values):
    half = mine_ref.shape[1] // 2
    for slot in range(16):
        block, part = (slot, 0) if slot < 8 else (15 - slot, 1)
        relative = meta[0] ^ block
        place = relative >> 1
        rows = pl.ds(part * half, half)
        to = pl.ds(slot * half, half)

        @pl.when((relative & 1) == 0)
        def _():
            keys[to, :] = mine_ref[place, rows, :HEAD_SIZE]
            values[to, :] = mine_ref[place, rows, HEAD_SIZE:]

        @pl.when((relative & 1) == 1)
        def _():
            keys[to, :] = other_ref[place, rows, :HEAD_SIZE]
            values[to, :] = other_ref[place, rows, HEAD_SIZE:]


def stack_heads(rows):
    count = rows.shape[1] // HEAD_SIZE
    return jnp.concatenate(
        [rows[:, h * HEAD_SIZE : (h + 1) * HEAD_SIZE] for h in range(count)], axis=0
    )


def unstack_heads(rows, count):
    each = rows.shape[0] // count
    return jnp.concatenate([rows[h * each : (h + 1) * each] for h in range(count)], axis=1)


def step_slot(meta):
    step = pl.program_id(0)
    block = meta[0] ^ (2 * (step >> 1))
    return jnp.where((step & 1) == 0, block, 15 - block)


def allowed_pairs(key_block, slot, shape, half):
    key_place = key_block * shape[0] + lax.broadcasted_iota(jnp.int32, shape, 0)
    query_place = slot * half + (lax.broadcasted_iota(jnp.int32, shape, 1) & (half - 1))
    return key_place <= query_place


def attend_kernel(scale, span, meta, query_ref, mine_ref, other_ref, *refs):
    outs, log_ref = refs[:4], refs[4]
    keys, values, values_turned = refs[5:]
    step = pl.program_id(0)
    half, group_width = query_ref.shape[1:]
    count = group_width // HEAD_SIZE

    @pl.when(step == 0)
    def _():
        sort_pairs(meta, mine_ref, other_ref, keys, values)
        values_turned[...] = values[...].T

    slot = step_slot(meta)
    query = stack_heads(query_ref[0])
    last = slot * half // span

    def scores_of(key_block):
        at = pl.ds(aligned(key_block, span), span)
        return at, dot_last(keys[at, :], query) * scale

    def add(carry, at, scores):
        highest, total, mixed = carry
        new = jnp.maximum(highest, jnp.max(scores, axis=0, keepdims=True))
        rescale = jnp.exp(highest - new)
        powers = jnp.exp(scores - new)
        total = total * rescale + jnp.sum(powers, axis=0, keepdims=True)
        mixed = mixed * rescale + dot_plain(values_turned[:, at], powers.astype(jnp.bfloat16))
        return new, total, mixed

    def body(key_block, carry):
        at, scores = scores_of(key_block)
        return add(carry, at, scores)

    wide = count * half
    carry = (
        jnp.full((1, wide), masked_score, jnp.float32),
        jnp.zeros((1, wide), jnp.float32),
        jnp.zeros((HEAD_SIZE, wide), jnp.float32),
    )
    carry = lax.fori_loop(0, last, body, carry)
    at, scores = scores_of(last)
    scores = jnp.where(allowed_pairs(last, slot, scores.shape, half), scores, masked_score)
    highest, total, mixed = add(carry, at, scores)
    log_ref[0] = highest + jnp.log(total)
    result = unstack_heads((mixed / total).T, count).astype(jnp.bfloat16)
    for r in range(4):
        for part in range(2):

            @pl.when(step == 2 * r + part)
            def _():
                outs[r][part * half : (part + 1) * half, :] = result


def attend(meta, query, mine, other, scale):
    token_rows, group_width = query.shape[1:]
    half = token_rows // 2
    count = group_width // HEAD_SIZE
    everything = 8 * token_rows
    span = min(256, everything)
    arrays = [query, mine, other]
    outs = [shape_of((token_rows, group_width), jnp.bfloat16)] * 4
    outs = outs + [shape_of((8, 1, count * half), jnp.float32)]
    result = call(
        functools.partial(attend_kernel, scale, span),
        "attend",
        meta,
        arrays,
        (8,),
        [
            pl.BlockSpec((1, half, group_width), lambda i, m: (i // 2, i % 2, 0)),
            whole(mine),
            whole(other),
        ],
        [whole(a) for a in outs[:4]]
        + [pl.BlockSpec((1, 1, count * half), lambda i, m: (i, 0, 0))],
        outs,
        [
            pltpu.VMEM((everything, HEAD_SIZE), jnp.bfloat16),
            pltpu.VMEM((everything, HEAD_SIZE), jnp.bfloat16),
            pltpu.VMEM((HEAD_SIZE, everything), jnp.bfloat16),
        ],
        2 * 2 * 4 * token_rows * everything * group_width,
        size_of(arrays) + size_of(outs),
    )
    return result[:4], result[4]


def attend_back_kernel(scale, span, meta, query_ref, mine_ref, other_ref, log_ref, *refs):
    mixed_refs, grad_refs = refs[:4], refs[4:8]
    grad_query_ref, grad_mine_ref, grad_other_ref = refs[8:11]
    keys, values, keys_turned, grad_keys, grad_values, mixed_held, grad_held = refs[11:]
    step = pl.program_id(0)
    half, group_width = query_ref.shape[1:]
    count = group_width // HEAD_SIZE

    @pl.when(step == 0)
    def _():
        sort_pairs(meta, mine_ref, other_ref, keys, values)
        keys_turned[...] = keys[...].T
        grad_keys[...] = jnp.zeros_like(grad_keys)
        grad_values[...] = jnp.zeros_like(grad_values)

    for r in range(4):
        for part in range(2):

            @pl.when(step == 2 * r + part)
            def _():
                mixed_held[...] = mixed_refs[r][part * half : (part + 1) * half, :]
                grad_held[...] = grad_refs[r][part * half : (part + 1) * half, :]

    slot = step_slot(meta)
    query = stack_heads(query_ref[0])
    mixed = stack_heads(mixed_held[...]).astype(jnp.float32)
    grad = stack_heads(grad_held[...])
    delta = jnp.sum((mixed * grad.astype(jnp.float32)).T, axis=0, keepdims=True)
    log_total = log_ref[0]
    last = slot * half // span

    def one(key_block, grad_turned, masked):
        at = pl.ds(aligned(key_block, span), span)
        scores = dot_last(keys[at, :], query) * scale
        probs = jnp.exp(scores - log_total)
        if masked:
            probs = jnp.where(allowed_pairs(key_block, slot, probs.shape, half), probs, 0.0)
        grad_probs = dot_last(values[at, :], grad)
        grad_scores = (probs * (grad_probs - delta)).astype(jnp.bfloat16)
        grad_values[at, :] += dot_plain(probs.astype(jnp.bfloat16), grad)
        grad_keys[at, :] += dot_plain(grad_scores, query)
        return grad_turned + dot_plain(keys_turned[:, at], grad_scores)

    grad_turned = jnp.zeros((HEAD_SIZE, count * half), jnp.float32)
    grad_turned = lax.fori_loop(0, last, lambda b, total: one(b, total, False), grad_turned)
    grad_turned = one(last, grad_turned, True)
    grad_query_ref[0] = unstack_heads((grad_turned * scale).T, count).astype(jnp.bfloat16)

    @pl.when(step == 7)
    def _():
        for slot_at in range(16):
            block, part = (slot_at, 0) if slot_at < 8 else (15 - slot_at, 1)
            relative = meta[0] ^ block
            place = relative >> 1
            rows = pl.ds(part * half, half)
            here = pl.ds(slot_at * half, half)
            both = jnp.concatenate([grad_keys[here, :] * scale, grad_values[here, :]], axis=1)

            @pl.when((relative & 1) == 0)
            def _():
                grad_mine_ref[place, rows, :] = both

            @pl.when((relative & 1) == 1)
            def _():
                grad_other_ref[place, rows, :] = both.astype(jnp.bfloat16)


def attend_back(meta, query, mine, other, log_total, mixed, grad, scale):
    token_rows, group_width = query.shape[1:]
    half = token_rows // 2
    count = group_width // HEAD_SIZE
    everything = 8 * token_rows
    span = min(256, everything)
    arrays = [query, mine, other, log_total] + list(mixed) + list(grad)
    outs = [
        shape_of(query.shape, jnp.bfloat16),
        shape_of(mine.shape, jnp.float32),
        shape_of(mine.shape, jnp.bfloat16),
    ]
    return call(
        functools.partial(attend_back_kernel, scale, span),
        "attend_back",
        meta,
        arrays,
        (8,),
        [
            pl.BlockSpec((1, half, group_width), lambda i, m: (i // 2, i % 2, 0)),
            whole(mine),
            whole(other),
            pl.BlockSpec((1, 1, count * half), lambda i, m: (i, 0, 0)),
        ]
        + [whole(a) for a in arrays[4:]],
        [
            pl.BlockSpec((1, half, group_width), lambda i, m: (i // 2, i % 2, 0)),
            whole(outs[1]),
            whole(outs[2]),
        ],
        outs,
        [
            pltpu.VMEM((everything, HEAD_SIZE), jnp.bfloat16),
            pltpu.VMEM((everything, HEAD_SIZE), jnp.bfloat16),
            pltpu.VMEM((HEAD_SIZE, everything), jnp.bfloat16),
            pltpu.VMEM((everything, HEAD_SIZE), jnp.float32),
            pltpu.VMEM((everything, HEAD_SIZE), jnp.float32),
            pltpu.VMEM((half, group_width), jnp.bfloat16),
            pltpu.VMEM((half, group_width), jnp.bfloat16),
        ],
        5 * 2 * 4 * token_rows * everything * group_width,
        size_of(arrays) + size_of(outs),
    )


def leave_kernel(meta, *refs):
    parts, mine, other = refs[:4], refs[4:8], refs[8:12]
    states_ref, gain_ref, weight_ref, middle_ref, normed_ref = refs[12:]
    core, chip, shard = meta[0] & 1, meta[0] >> 1, meta[1]
    rows = mine[0].shape[0]
    for i in range(4):
        at = 2 * (chip ^ shard ^ i)
        weight_ref[pl.ds(aligned(at + core, rows), rows), :] = mine[i][...]
        weight_ref[pl.ds(aligned(at + 1 - core, rows), rows), :] = other[i][...]
    middle = states_ref[...].astype(jnp.float32)
    for r in range(4):
        middle += dot_plain(parts[r][...], weight_ref[2 * rows * r : 2 * rows * (r + 1), :])
    middle_ref[...] = middle
    inverse = lax.rsqrt(jnp.mean(middle * middle, axis=-1, keepdims=True) + norm_eps)
    normed_ref[...] = (middle * inverse * gain_ref[...]).astype(jnp.bfloat16)


def leave(meta, parts, mine, other, states, gain):
    token_rows, width = states.shape
    arrays = list(parts) + list(mine) + list(other) + [states, gain]
    outs = [
        shape_of((8 * mine[0].shape[0], width), jnp.bfloat16),
        shape_of((token_rows, width), jnp.float32),
        shape_of((token_rows, width), jnp.bfloat16),
    ]
    return call(
        leave_kernel,
        "leave",
        meta,
        arrays,
        (1,),
        [whole(a) for a in arrays],
        [whole(a) for a in outs],
        outs,
        [],
        2 * token_rows * width * width,
        size_of(arrays) + size_of(outs),
    )


def norm_back_rows(grad_normed, states, gain):
    inverse = lax.rsqrt(jnp.mean(states * states, axis=-1, keepdims=True) + norm_eps)
    scaled = states * inverse
    gain_grad = jnp.sum(grad_normed * scaled, axis=0, keepdims=True)
    grad_scaled = grad_normed * gain
    shift = jnp.mean(grad_scaled * scaled, axis=-1, keepdims=True)
    return inverse * (grad_scaled - scaled * shift), gain_grad


def enter_back_kernel(meta, final_ref, normed_ref, middle_ref, gain_ref, weight_ref, *refs):
    grad_ref, branch_ref, gain_grad_ref = refs[:3]
    grad, gain_grad = norm_back_rows(normed_ref[...], middle_ref[...], gain_ref[...])
    grad = grad + final_ref[...]
    grad_ref[...] = grad
    gain_grad_ref[...] = gain_grad
    branch = grad.astype(jnp.bfloat16)
    branch_ref[...] = branch
    rows = weight_ref.shape[0] // 4
    for r in range(4):
        refs[3 + r][...] = dot_last(branch, weight_ref[rows * r : rows * (r + 1), :]).astype(
            jnp.bfloat16
        )


def enter_back(meta, grad_final, grad_normed, middle, gain, weight):
    token_rows, width = middle.shape
    arrays = [grad_final, grad_normed, middle, gain, weight]
    outs = [
        shape_of((token_rows, width), jnp.float32),
        shape_of((token_rows, width), jnp.bfloat16),
        shape_of((1, width), jnp.float32),
    ] + [shape_of((token_rows, weight.shape[0] // 4), jnp.bfloat16)] * 4
    return call(
        enter_back_kernel,
        "enter_back",
        meta,
        arrays,
        (1,),
        [whole(a) for a in arrays],
        [whole(a) for a in outs],
        outs,
        [],
        2 * token_rows * width * width,
        size_of(arrays) + size_of(outs),
    )


def finish_kernel(meta, *refs):
    parts, mine, other = refs[:4], refs[4:8], refs[8:12]
    states_ref, middle_ref, gain_ref, grad_ref, gain_grad_ref, total = refs[12:]
    core = meta[0] & 1
    columns = mine[0].shape[0]
    for at, weights in ((core, mine), (1 - core, other)):
        total[:, pl.ds(aligned(at, columns), columns)] = sum(
            dot_last(parts[r][...], weights[r][...]) for r in range(4)
        )
    grad, gain_grad = norm_back_rows(
        total[...], states_ref[...].astype(jnp.float32), gain_ref[...]
    )
    grad_ref[0] = grad + middle_ref[...]
    gain_grad_ref[...] = gain_grad


def finish(meta, parts, mine, other, states, grad_middle, gain):
    token_rows, width = states.shape
    arrays = list(parts) + list(mine) + list(other) + [states, grad_middle, gain]
    outs = [
        shape_of((1, token_rows, width), jnp.float32),
        shape_of((1, width), jnp.float32),
    ]
    return call(
        finish_kernel,
        "finish",
        meta,
        arrays,
        (1,),
        [whole(a) for a in arrays],
        [whole(a) for a in outs],
        outs,
        [pltpu.VMEM((token_rows, width), jnp.float32)],
        2 * token_rows * width * 4 * parts[0].shape[1],
        size_of(arrays) + size_of(outs),
    )


def gated(gate_up, units):
    gate_part = gate_up[:, :units]
    sigma = 1.0 / (1.0 + jnp.exp(-gate_part))
    return gate_part * sigma * gate_up[:, units:]


def gated_back(grad_act, gate_up, units):
    gate_part = gate_up[:, :units].astype(jnp.float32)
    up_part = gate_up[:, units:].astype(jnp.float32)
    sigma = 1.0 / (1.0 + jnp.exp(-gate_part))
    linear = gate_part * sigma
    grad_gate = grad_act * up_part * (sigma * (1.0 + gate_part * (1.0 - sigma)))
    return grad_gate, grad_act * linear, linear * up_part


def experts_kernel(
    meta, rows_ref, gates_ref, expert_ref, shared_ref, gate_up_ref, shared_gate_up_ref, out_ref, total
):
    expert = pl.program_id(0)
    rows = rows_ref[...]

    @pl.when(expert == 0)
    def _():
        units = shared_ref.shape[1] // 3
        gate_up = dot_plain(rows, shared_ref[:, : 2 * units])
        shared_gate_up_ref[...] = gate_up.astype(jnp.bfloat16)
        act = gated(gate_up, units).astype(jnp.bfloat16)
        total[...] = dot_last(act, shared_ref[:, 2 * units :])

    gate_up = dot_plain(rows, expert_ref[0, :, : 2 * F])
    gate_up_ref[0] = gate_up.astype(jnp.bfloat16)
    act = (gated(gate_up, F) * gates_ref[0]).astype(jnp.bfloat16)
    total[...] += dot_last(act, expert_ref[0, :, 2 * F :])

    @pl.when(expert == pl.num_programs(0) - 1)
    def _():
        out_ref[...] = total[...].astype(jnp.bfloat16)


def experts(meta, rows, gates, expert_weight, shared_slice):
    local_experts, width, _ = expert_weight.shape
    token_rows = rows.shape[0]
    shared_units = shared_slice.shape[1] // 3
    arrays = [rows, gates, expert_weight, shared_slice]
    outs = [
        shape_of((local_experts, token_rows, 2 * F), jnp.bfloat16),
        shape_of((token_rows, 2 * shared_units), jnp.bfloat16),
        shape_of((token_rows, width), jnp.bfloat16),
    ]
    return call(
        experts_kernel,
        "experts",
        meta,
        arrays,
        (local_experts,),
        [
            whole(rows),
            pl.BlockSpec((1, token_rows, 1), lambda e, m: (e, 0, 0)),
            pl.BlockSpec((1, width, 3 * F), lambda e, m: (e, 0, 0)),
            whole(shared_slice),
        ],
        [
            pl.BlockSpec((1, token_rows, 2 * F), lambda e, m: (e, 0, 0)),
            whole(outs[1]),
            whole(outs[2]),
        ],
        outs,
        [pltpu.VMEM((token_rows, width), jnp.float32)],
        2 * token_rows * width * 3 * (F * local_experts + shared_units),
        size_of(arrays) + size_of(outs),
    )


def experts_back_kernel(
    meta,
    grad_ref,
    gates_ref,
    gate_up_ref,
    shared_gate_up_ref,
    expert_ref,
    shared_ref,
    grad_gate_up_ref,
    act_ref,
    shared_grad_ref,
    shared_act_ref,
    grad_rows_ref,
    total,
):
    expert = pl.program_id(0)
    grad = grad_ref[...]

    @pl.when(expert == 0)
    def _():
        units = shared_ref.shape[1] // 3
        grad_act = dot_plain(grad, shared_ref[:, 2 * units :])
        grad_gate, grad_up, act = gated_back(grad_act, shared_gate_up_ref[...], units)
        both = jnp.concatenate([grad_gate, grad_up], axis=1).astype(jnp.bfloat16)
        shared_grad_ref[0] = both
        shared_act_ref[0] = act.astype(jnp.bfloat16)
        total[...] = dot_last(both, shared_ref[:, : 2 * units])

    grad_act = dot_plain(grad, expert_ref[0, :, 2 * F :]) * gates_ref[0]
    grad_gate, grad_up, act = gated_back(grad_act, gate_up_ref[0], F)
    both = jnp.concatenate([grad_gate, grad_up], axis=1).astype(jnp.bfloat16)
    grad_gate_up_ref[0] = both
    act_ref[0] = (act * gates_ref[0]).astype(jnp.bfloat16)
    total[...] += dot_last(both, expert_ref[0, :, : 2 * F])

    @pl.when(expert == pl.num_programs(0) - 1)
    def _():
        grad_rows_ref[...] = total[...].astype(jnp.bfloat16)


def experts_back(meta, grad, gates, gate_up, shared_gate_up, expert_weight, shared_slice):
    local_experts, width, _ = expert_weight.shape
    token_rows = grad.shape[0]
    shared_units = shared_slice.shape[1] // 3
    arrays = [grad, gates, gate_up, shared_gate_up, expert_weight, shared_slice]
    outs = [
        shape_of((local_experts, token_rows, 2 * F), jnp.bfloat16),
        shape_of((local_experts, token_rows, F), jnp.bfloat16),
        shape_of((1, token_rows, 2 * shared_units), jnp.bfloat16),
        shape_of((1, token_rows, shared_units), jnp.bfloat16),
        shape_of((token_rows, width), jnp.bfloat16),
    ]
    return call(
        experts_back_kernel,
        "experts_back",
        meta,
        arrays,
        (local_experts,),
        [
            whole(grad),
            pl.BlockSpec((1, token_rows, 1), lambda e, m: (e, 0, 0)),
            pl.BlockSpec((1, token_rows, 2 * F), lambda e, m: (e, 0, 0)),
            whole(shared_gate_up),
            pl.BlockSpec((1, width, 3 * F), lambda e, m: (e, 0, 0)),
            whole(shared_slice),
        ],
        [
            pl.BlockSpec((1, token_rows, 2 * F), lambda e, m: (e, 0, 0)),
            pl.BlockSpec((1, token_rows, F), lambda e, m: (e, 0, 0)),
            whole(outs[2]),
            whole(outs[3]),
            whole(outs[4]),
        ],
        outs,
        [pltpu.VMEM((token_rows, width), jnp.float32)],
        2 * token_rows * width * 3 * (F * local_experts + shared_units),
        size_of(arrays) + size_of(outs),
    )


def weight_grad_kernel(pairs, core_at, meta, *refs):
    keep_ref, give_ref = refs[-2:]
    at = 0
    columns = 0
    parts = []
    for count in pairs:
        lefts, rights = refs[at : at + count], refs[at + count : at + 2 * count]
        at += 2 * count
        parts.append(
            sum(dot_first(a[...], b[0]) for a, b in zip(lefts, rights)).astype(jnp.bfloat16)
        )
    half = keep_ref.shape[1]

    for core, (first, second) in ((0, (keep_ref, give_ref)), (1, (give_ref, keep_ref))):

        @pl.when((meta[core_at] & 1) == core)
        def _():
            start = 0
            for part in parts:
                stop = start + part.shape[1]
                first[0, :, start:stop] = part[:half]
                second[0, :, start:stop] = part[half:]
                start = stop


def weight_grad(meta, order, operands, index):
    token_rows, width = operands[0][0][0].shape
    tile = width // 4
    scalars = jnp.stack([order, meta[0]])
    arrays, in_specs, columns = [], [], 0
    for lefts, rights in operands:
        arrays += list(lefts) + list(rights)
        in_specs += [pl.BlockSpec((token_rows, tile), lambda i, m: (0, i ^ m[0]))] * len(lefts)
        units = rights[0].shape[-1]
        in_specs += [
            pl.BlockSpec((1, token_rows, units), lambda i, m, at=index: (at, 0, 0))
        ] * len(rights)
        columns += units
    outs = [shape_of((4, tile // 2, columns), jnp.bfloat16)] * 2
    tokens = token_rows * len(operands[0][0])
    return call(
        functools.partial(weight_grad_kernel, [len(left) for left, _ in operands], 1),
        "weight_grad",
        scalars,
        arrays,
        (4,),
        in_specs,
        [pl.BlockSpec((1, tile // 2, columns), lambda i, m: (i, 0, 0))] * 2,
        outs,
        [],
        2 * tokens * width * columns,
        size_of(outs) + 4 * tokens * width + 2 * tokens * columns,
    )


def place_expert_kernel(meta, *refs):
    mine, other, out_ref = refs[-9:-5], refs[-5:-1], refs[-1]
    step = pl.program_id(0)
    core = meta[0] & 1
    rows = mine[0].shape[0]
    for r in range(4):

        @pl.when(step == r)
        def _():
            out_ref[0, pl.ds(aligned(core, rows), rows), :] = mine[r][...].astype(jnp.float32)
            out_ref[0, pl.ds(aligned(1 - core, rows), rows), :] = other[r][...].astype(
                jnp.float32
            )


def place_expert(meta, total, index, shape, mine, other):
    rows, columns = mine[0].shape
    arrays = list(mine) + list(other)
    in_specs = [whole(a) for a in arrays]
    aliases = {}
    if total is not None:
        arrays = [total] + arrays
        in_specs = [pl.BlockSpec(memory_space=pl.ANY)] + in_specs
        aliases = {1: 0}
    return pl.pallas_call(
        place_expert_kernel,
        grid_spec=pltpu.PrefetchScalarGridSpec(
            num_scalar_prefetch=1,
            grid=(4,),
            in_specs=in_specs,
            out_specs=pl.BlockSpec(
                (1, 2 * rows, columns), lambda r, m: (index, (m[0] >> 1) ^ r, 0)
            ),
        ),
        out_shape=shape_of(shape, jnp.float32),
        input_output_aliases=aliases,
        compiler_params=pltpu.CompilerParams(vmem_limit_bytes=48 * 1024 * 1024),
        cost_estimate=pl.CostEstimate(
            flops=0, bytes_accessed=8 * rows * columns * 6, transcendentals=0
        ),
        name="place_expert",
    )(meta, *arrays)


def place_shared_kernel(meta, mine, other, out_ref):
    core = meta[0] & 1
    rows = mine.shape[1]
    out_ref[pl.ds(aligned(core, rows), rows), :] = mine[0].astype(jnp.float32)
    out_ref[pl.ds(aligned(1 - core, rows), rows), :] = other[0].astype(jnp.float32)


def place_shared(meta, mine, other):
    _, rows, columns = mine.shape
    units = columns // 3
    block = pl.BlockSpec((1, rows, units), lambda i, j, m: (i, 0, j))
    outs = shape_of((2 * rows, 4 * columns), jnp.float32)
    return call(
        place_shared_kernel,
        "place_shared",
        meta,
        [mine, other],
        (4, 3),
        [block, block],
        pl.BlockSpec((2 * rows, units), lambda i, j, m: (0, 4 * j + (m[1] ^ i))),
        outs,
        [],
        0,
        size_of([mine, other, outs]),
    )


def place_heads_kernel(meta, *refs):
    mine, other, out_ref = refs[:4], refs[4:8], refs[8]
    core, chip = meta[0] & 1, meta[0] >> 1
    rows, columns = mine[0].shape
    group_width = columns - 2 * HEAD_SIZE
    for r in range(4):
        head = chip ^ r
        for at, pieces in ((core, mine), (1 - core, other)):
            to = pl.ds(aligned(at, rows), rows)
            values = pieces[r][...].astype(jnp.float32)
            out_ref[to, pl.ds(aligned(head, group_width), group_width)] = values[:, :group_width]
            out_ref[to, pl.ds(aligned(4 * group_width // HEAD_SIZE + head, HEAD_SIZE), HEAD_SIZE)] = (
                values[:, group_width : group_width + HEAD_SIZE]
            )
            out_ref[
                to, pl.ds(aligned(4 * group_width // HEAD_SIZE + 4 + head, HEAD_SIZE), HEAD_SIZE)
            ] = values[:, group_width + HEAD_SIZE :]


def place_heads(meta, mine, other):
    rows, columns = mine[0].shape
    arrays = list(mine) + list(other)
    outs = shape_of((2 * rows, 4 * columns), jnp.float32)
    return call(
        place_heads_kernel,
        "place_heads",
        meta,
        arrays,
        (1,),
        [whole(a) for a in arrays],
        whole(outs),
        outs,
        [],
        0,
        size_of(arrays + [outs]),
    )


def join_shared_kernel(meta, mine, other, out_ref):
    step = pl.program_id(0)
    rows = mine.shape[2]
    first = meta[0] ^ (2 * step)
    for i in range(4):
        at = 8 * (meta[1] ^ i)
        out_ref[pl.ds(aligned(at + first, rows), rows), :] = mine[0, i]
        out_ref[pl.ds(aligned(at + (first ^ 1), rows), rows), :] = other[0, i]


def join_shared(meta, mine, other):
    _, _, rows, columns = mine.shape
    block = pl.BlockSpec((1, 4, rows, columns), lambda r, m: (r, 0, 0, 0))
    outs = shape_of((32 * rows, columns), jnp.bfloat16)
    return call(
        join_shared_kernel,
        "join_shared",
        meta,
        [mine, other],
        (4,),
        [block, block],
        whole(outs),
        outs,
        [],
        0,
        size_of([mine, other, outs]),
    )


def fast_device(
    hidden,
    teacher,
    valid_mask,
    routes,
    route_gates,
    gain_in,
    query_key_value_weight,
    out_weight,
    gain_mid,
    shared_weight,
    expert_weight,
):
    token_rows, width = hidden.shape[1:]
    context_count, shard_count = 8, 4
    context_index = lax.axis_index("ctx").astype(jnp.int32)
    shard_index = lax.axis_index("wt").astype(jnp.int32)
    meta = jnp.stack([context_index, shard_index])
    core = context_index & 1
    chip = context_index >> 1
    at_end = (shard_index == 0) | (shard_index == shard_count - 1)
    group_width = QUERY_HEADS // KEY_VALUE_HEADS * HEAD_SIZE
    query_width = QUERY_HEADS * HEAD_SIZE
    kv_width = KEY_VALUE_HEADS * HEAD_SIZE
    slice_width = group_width + 2 * HEAD_SIZE
    scale = 1.0 / math.sqrt(HEAD_SIZE)
    all_tokens = token_rows * context_count * shard_count
    shard_rows = query_key_value_weight.shape[0]
    half_rows = shard_rows // 2
    local_experts = expert_weight.shape[0]
    bf16, f32 = jnp.bfloat16, jnp.float32
    states = hidden[0]

    blocks = chips_swap([states] * 4)

    qkv_half = lax.dynamic_slice_in_dim(query_key_value_weight, core * half_rows, half_rows, 0)
    qkv_half = jnp.concatenate(
        [
            lax.dynamic_slice_in_dim(qkv_half, chip * group_width, group_width, 1),
            lax.dynamic_slice_in_dim(qkv_half, query_width + chip * HEAD_SIZE, HEAD_SIZE, 1),
            lax.dynamic_slice_in_dim(
                qkv_half, query_width + kv_width + chip * HEAD_SIZE, HEAD_SIZE, 1
            ),
        ],
        axis=1,
    )
    qkv_mine = [qkv_half] + [line_swap(qkv_half, i) for i in (1, 2, 3)]
    qkv_other = core_swap(qkv_mine)

    gains = jnp.stack([gain_in, gain_mid])
    gains = jnp.stack([gains] + [line_swap(gains, i) for i in (1, 2, 3)])
    gains = jnp.stack([pick(gains, shard_index ^ i) for i in range(4)], axis=1)
    gains = gains.reshape(2, 1, width).astype(f32)

    normed_in, query, pair, qkv_slice = project(
        meta, blocks, gains[0], qkv_mine, qkv_other, group_width
    )
    pair_other = flip(pair, 1)

    out_half = lax.dynamic_slice_in_dim(out_weight, core * half_rows, half_rows, 0)
    out_mine = line_gather(out_half, at_end)
    out_other = core_swap(out_mine)

    eighth = shard_rows // 8
    shared_units = SF // shard_count
    shared_piece = lax.dynamic_slice_in_dim(shared_weight, context_index * eighth, eighth, 0)
    shared_piece = shared_piece.reshape(eighth, 3, shard_count, shared_units)

    def shared_columns(index):
        part = lax.dynamic_index_in_dim(shared_piece, shard_index ^ index, 2, keepdims=False)
        return part.reshape(eighth, 3 * shared_units)

    shared_pieces = jnp.stack(
        [shared_columns(0)] + [line_swap(shared_columns(i), i) for i in (1, 2, 3)]
    )
    shared_mine = jnp.stack(chips_gather(shared_pieces, False))
    shared_slice = join_shared(meta, shared_mine, flip(shared_mine, 1))

    expert_ids = jnp.arange(EXPERTS, dtype=jnp.int32)
    gate_matrix = jnp.sum(
        jnp.where(
            routes[0][None, :, :] == expert_ids[:, None, None], route_gates[0][None, :, :], 0.0
        ),
        axis=-1,
    ).reshape(shard_count, local_experts, token_rows)
    gates = [pick(gate_matrix, shard_index)] + [
        line_swap(pick(gate_matrix, shard_index ^ i), i) for i in (1, 2, 3)
    ]
    gates = [part[..., None] for part in gates]

    valid_float = valid_mask[0].astype(f32)
    valid_count = everywhere_sum(jnp.full((8, 128), jnp.sum(valid_float), f32))[0, 0]

    mixed_heads, log_total = attend(meta, query, pair, pair_other, scale)
    mixed = chips_swap(mixed_heads)
    out_rel, middle, normed_mid = leave(meta, mixed, out_mine, out_other, states, gains[1])

    line_rows = line_gather(normed_mid, at_end)
    forward = [
        experts(meta, line_rows[i], gates[i], expert_weight, shared_slice) for i in range(4)
    ]
    gate_ups, shared_gate_ups, partial_out = zip(*forward)
    final_state = middle + line_reduce(partial_out)

    deviation = final_state - teacher[0].astype(f32)
    squared = jnp.sum(valid_float[:, None] * deviation * deviation)
    grad_final = all_tokens / valid_count * valid_float[:, None] * deviation

    line_grads = line_gather(grad_final.astype(bf16), at_end)
    backward = [
        experts_back(
            meta,
            line_grads[i],
            gates[i],
            gate_ups[i],
            shared_gate_ups[i],
            expert_weight,
            shared_slice,
        )
        for i in range(4)
    ]
    grad_gate_ups, acts, shared_grads, shared_acts, partial_rows = zip(*backward)
    grad_normed_mid = line_reduce(partial_rows)

    grad_middle, grad_branch, grad_gain_mid, *grad_mixed = enter_back(
        meta, grad_final, grad_normed_mid, middle, gains[1], out_rel
    )
    grad_mixed = chips_swap(grad_mixed)

    grad_query, grad_pair, grad_pair_other = attend_back(
        meta, query, pair, pair_other, log_total, mixed_heads, grad_mixed, scale
    )
    grad_pair = grad_pair + flip(grad_pair_other, 1).astype(f32)
    grad_projected = jnp.concatenate([grad_query, grad_pair.astype(bf16)], axis=-1)

    keep, give = weight_grad(
        meta,
        shard_index,
        [([normed_in.reshape(4 * token_rows, width)], [grad_projected.reshape(1, 4 * token_rows, -1)])],
        0,
    )
    came = flip(give, 1)
    grad_qkv = line_reduce([keep[i] + came[i] for i in range(4)]).astype(bf16)
    grad_qkv = chips_gather(grad_qkv, False)
    grad_qkv = place_heads(meta, grad_qkv, core_swap(grad_qkv))

    qkv_rel = chips_gather(
        lax.dynamic_slice_in_dim(qkv_slice, core * (width // 2), width // 2, 0), True
    )
    grad_parts = chips_swap([grad_projected[r] for r in range(4)])
    grad_hidden, grad_gain_in = finish(
        meta, grad_parts, qkv_rel, core_swap(qkv_rel), states, grad_middle, gains[0]
    )

    grad_experts = None
    for expert in range(local_experts):
        keep, give = weight_grad(
            meta, chip, [(line_rows, grad_gate_ups), (line_grads, acts)], expert
        )
        reduced = chips_reduce(keep, flip(give, 1))
        reduced = chips_gather(reduced, expert % 2 == 1)
        grad_experts = place_expert(
            meta, grad_experts, expert, expert_weight.shape, reduced, core_swap(reduced)
        )

    keep, give = weight_grad(
        meta, shard_index, [(line_rows, shared_grads), (line_grads, shared_acts)], 0
    )
    came = flip(give, 1)
    grad_shared = [keep[0] + came[0]] + [line_swap(keep[i] + came[i], i) for i in (1, 2, 3)]
    grad_shared = jnp.stack(grad_shared)

    def chips_sum(value, axis):
        upper, lower = jnp.split(value, 2, axis=axis)
        upper = upper + flip(upper, 2)
        lower = lower + flip(lower, 4)
        upper = upper + flip(upper, 4)
        lower = lower + flip(lower, 2)
        return jnp.concatenate([upper, lower], axis=axis)

    grad_shared = chips_sum(grad_shared, 0)
    grad_shared = place_shared(meta, grad_shared, flip(grad_shared, 1))

    keep, give = weight_grad(
        meta, chip ^ shard_index, [([jnp.concatenate(mixed, axis=1)], [grad_branch[None]])], 0
    )
    came = flip(give, 1)
    grad_out = line_reduce([keep[i] + came[i] for i in range(4)]).astype(bf16)
    grad_out = chips_sum(grad_out, 0)
    came = flip(grad_out, 1)
    grad_out = jnp.where(
        core == 0,
        jnp.concatenate([grad_out, came], axis=0),
        jnp.concatenate([came, grad_out], axis=0),
    ).astype(f32)

    sums = jnp.concatenate(
        [grad_gain_in, grad_gain_mid, jnp.full((6, width), squared, f32)], axis=0
    )
    sums = everywhere_sum(sums)
    own = lax.dynamic_slice_in_dim(sums, shard_index * shard_rows, shard_rows, 1)
    loss_value = 0.5 * sums[2, 0] / (valid_count * width)

    return (
        final_state.astype(bf16)[None],
        loss_value,
        grad_hidden,
        own[0],
        grad_qkv,
        grad_out,
        own[1],
        grad_shared,
        grad_experts,
    )


def solution(mesh):
    in_specs = (
        P("wt", "ctx", None),
        P("wt", "ctx", None),
        P("wt", "ctx"),
        P("wt", "ctx", None),
        P("wt", "ctx", None),
        P("wt"),
        P("wt", None),
        P("wt", None),
        P("wt"),
        P("wt", None),
        P("wt", None, None),
    )
    out_specs = (
        P("wt", "ctx", None),
        P(),
        P("wt", "ctx", None),
        P("wt"),
        P("wt", None),
        P("wt", None),
        P("wt"),
        P("wt", None),
        P("wt", None, None),
    )
    plane_of_eight = dict(mesh.shape) == {"ctx": 8, "wt": 4}
    return jax.shard_map(
        fast_device if plane_of_eight else on_device, mesh=mesh, in_specs=in_specs, out_specs=out_specs, check_vma=False
    )
```

```python
import functools
import math

import jax
import jax.numpy as jnp
from jax import lax
from jax.experimental import pallas as pl
from jax.experimental.pallas import tpu as pltpu
from jax.sharding import PartitionSpec as P

QUERY_HEADS = 12
KEY_VALUE_HEADS = 4
HEAD_SIZE = 128
F = 512
SF = 1024
EXPERTS = 16
TOP = 6


norm_eps = 1e-05
masked_score = -1e30


def sigmoid_linear(values):
    return values * jax.nn.sigmoid(values)


def silu_slope(values):
    sigma_value = jax.nn.sigmoid(values)
    return sigma_value * (1.0 + values * (1.0 - sigma_value))


def normalize(values):
    inverse = lax.rsqrt(jnp.mean(values * values, axis=-1, keepdims=True) + norm_eps)
    return (values * inverse, inverse)


def norm_back(grad_normed, scaled, inverse, gain_vector):
    grad_scaled = grad_normed * gain_vector
    return inverse * (grad_scaled - scaled * jnp.mean(grad_scaled * scaled, axis=-1, keepdims=True))


def positions(row_ids, token_rows, context_count):
    piece_index = row_ids // token_rows
    within = row_ids % token_rows
    half_rows = token_rows // 2
    mirrored = jnp.where(within < half_rows, piece_index, 2 * context_count - 1 - piece_index)
    return mirrored * half_rows + within % half_rows


def route_tables(local_routes, local_gates, experts, capacity):
    token_rows = local_routes.shape[0]
    flat_routes = local_routes.reshape(-1)
    one_hot = (flat_routes[:, None] == jnp.arange(experts, dtype=jnp.int32)[None, :]).astype(
        jnp.int32
    )
    earlier = jnp.cumsum(one_hot, axis=0) - one_hot
    slot_index = jnp.sum(earlier * one_hot, axis=1)
    token_index = jnp.arange(flat_routes.shape[0], dtype=jnp.int32) // local_routes.shape[1]
    slot_table = (
        jnp.full((experts, capacity), token_rows, jnp.int32)
        .at[flat_routes, slot_index]
        .set(token_index)
    )
    slot_gate = (
        jnp.zeros((experts, capacity), jnp.float32)
        .at[flat_routes, slot_index]
        .set(local_gates.reshape(-1))
    )
    return (slot_table, slot_gate)


def block_scores(query_rows, key_block, key_position, query_place, score_scale):
    scores = (
        jnp.einsum("qhgd,khd->qhgk", query_rows, key_block, preferred_element_type=jnp.float32)
        * score_scale
    )
    allowed = key_position[None, None, None, :] <= query_place[:, None, None, None]
    return jnp.where(allowed, scores, masked_score)


def attend_forward(
    query_rows, blocked_keys, blocked_values, place_blocks, query_place, score_scale
):
    head_shape = query_rows.shape[:3]

    def online_step(running, block_args):
        running_max, running_sum, accumulated = running
        key_block, value_block, key_position = block_args
        scores = block_scores(query_rows, key_block, key_position, query_place, score_scale)
        new_max = jnp.maximum(running_max, jnp.max(scores, axis=-1))
        rescale = jnp.exp(running_max - new_max)
        powers = jnp.exp(scores - new_max[..., None])
        new_sum = running_sum * rescale + jnp.sum(powers, axis=-1)
        weighted = jnp.einsum(
            "qhgk,khd->qhgd",
            powers.astype(jnp.bfloat16),
            value_block,
            preferred_element_type=jnp.float32,
        )
        return ((new_max, new_sum, accumulated * rescale[..., None] + weighted), None)

    initial = (
        jnp.full(head_shape, masked_score, jnp.float32),
        jnp.zeros(head_shape, jnp.float32),
        jnp.zeros(query_rows.shape, jnp.float32),
    )
    row_max, row_sum, accumulated = lax.scan(
        online_step, initial, (blocked_keys, blocked_values, place_blocks)
    )[0]
    log_total = row_max + jnp.log(row_sum)
    return (accumulated / row_sum[..., None], log_total)


def attend_backward(
    query_rows,
    blocked_keys,
    blocked_values,
    place_blocks,
    query_place,
    log_total,
    attention_output_gradient,
    attention_output,
    score_scale,
):
    row_delta = jnp.sum(attention_output_gradient.astype(jnp.float32) * attention_output, axis=-1)

    def block_grads(grad_queries, block_args):
        key_block, value_block, key_position = block_args
        scores = block_scores(query_rows, key_block, key_position, query_place, score_scale)
        probabilities = jnp.exp(scores - log_total[..., None])
        grad_probs = jnp.einsum(
            "qhgd,khd->qhgk",
            attention_output_gradient,
            value_block,
            preferred_element_type=jnp.float32,
        )
        grad_scores = (probabilities * (grad_probs - row_delta[..., None])).astype(jnp.bfloat16)
        grad_queries = grad_queries + jnp.einsum(
            "qhgk,khd->qhgd", grad_scores, key_block, preferred_element_type=jnp.float32
        )
        grad_keys = (
            jnp.einsum(
                "qhgk,qhgd->khd", grad_scores, query_rows, preferred_element_type=jnp.float32
            )
            * score_scale
        )
        grad_values = jnp.einsum(
            "qhgk,qhgd->khd",
            probabilities.astype(jnp.bfloat16),
            attention_output_gradient,
            preferred_element_type=jnp.float32,
        )
        return (grad_queries, (grad_keys, grad_values))

    grad_queries, (grad_keys, grad_values) = lax.scan(
        block_grads,
        jnp.zeros(query_rows.shape, jnp.float32),
        (blocked_keys, blocked_values, place_blocks),
    )
    return (grad_queries * score_scale, grad_keys, grad_values)


def gate_up_grads(grad_act, gate_up, hidden_units):
    gate_part = gate_up[..., :hidden_units]
    up_part = gate_up[..., hidden_units:]
    return jnp.concatenate(
        [grad_act * up_part * silu_slope(gate_part), grad_act * sigmoid_linear(gate_part)], axis=-1
    ).astype(jnp.bfloat16)


def on_device(
    hidden,
    teacher,
    valid_mask,
    routes,
    route_gates,
    gain_in,
    query_key_value_weight,
    out_weight,
    gain_mid,
    shared_weight,
    expert_weight,
):
    token_rows = hidden.shape[1]
    model_width = hidden.shape[2]
    context_count = lax.axis_size("ctx")
    shard_count = lax.axis_size("wt")
    seq_rows = token_rows * context_count
    all_tokens = seq_rows * shard_count
    query_groups = QUERY_HEADS // KEY_VALUE_HEADS
    query_total_width = QUERY_HEADS * HEAD_SIZE
    key_value_width = KEY_VALUE_HEADS * HEAD_SIZE
    score_scale = 1.0 / math.sqrt(HEAD_SIZE)
    key_row_count = min(512, seq_rows)
    number_of_blocks = seq_rows // key_row_count
    capacity = token_rows * TOP // 12
    local_experts = expert_weight.shape[0]
    contract_last = (((1,), (1,)), ((), ()))
    contract_first = (((0,), (0,)), ((), ()))
    full_gain_in, full_qkv, full_out, full_gain_mid, full_shared = (
        lax.all_gather(gain_in, "wt", axis=0, tiled=True),
        lax.all_gather(query_key_value_weight, "wt", axis=0, tiled=True),
        lax.all_gather(out_weight, "wt", axis=0, tiled=True),
        lax.all_gather(gain_mid, "wt", axis=0, tiled=True),
        lax.all_gather(shared_weight, "wt", axis=0, tiled=True),
    )
    gain_in_float = full_gain_in.astype(jnp.float32)
    gain_mid_float = full_gain_mid.astype(jnp.float32)
    inputs = hidden[0].astype(jnp.float32)
    scaled_in, inverse_in = normalize(inputs)
    normed_in = (scaled_in * gain_in_float).astype(jnp.bfloat16)
    projected_rows = jnp.dot(normed_in, full_qkv, preferred_element_type=jnp.float32).astype(
        jnp.bfloat16
    )
    query_rows = projected_rows[:, :query_total_width].reshape(
        token_rows, KEY_VALUE_HEADS, query_groups, HEAD_SIZE
    )
    context_local = projected_rows[:, query_total_width:]
    context_gathered = lax.all_gather(context_local, "ctx", axis=0, tiled=True)
    context_index = lax.axis_index("ctx")
    query_place = positions(
        context_index * token_rows + jnp.arange(token_rows, dtype=jnp.int32),
        token_rows,
        context_count,
    )
    place_blocks = positions(
        jnp.arange(seq_rows, dtype=jnp.int32), token_rows, context_count
    ).reshape(number_of_blocks, key_row_count)
    blocked_keys = context_gathered[:, :key_value_width].reshape(
        number_of_blocks, key_row_count, KEY_VALUE_HEADS, HEAD_SIZE
    )
    blocked_values = context_gathered[:, key_value_width:].reshape(
        number_of_blocks, key_row_count, KEY_VALUE_HEADS, HEAD_SIZE
    )
    attention_output, log_total = attend_forward(
        query_rows, blocked_keys, blocked_values, place_blocks, query_place, score_scale
    )
    mixed_rows = attention_output.reshape(token_rows, query_total_width).astype(jnp.bfloat16)
    middle = inputs + jnp.dot(mixed_rows, full_out, preferred_element_type=jnp.float32)
    scaled_mid, inverse_mid = normalize(middle)
    normed_mid = (scaled_mid * gain_mid_float).astype(jnp.bfloat16)
    shared_gate_up = jnp.dot(
        normed_mid, full_shared[:, : 2 * SF], preferred_element_type=jnp.float32
    )
    shared_act = (sigmoid_linear(shared_gate_up[:, :SF]) * shared_gate_up[:, SF:]).astype(
        jnp.bfloat16
    )
    shared_out = lax.dot_general(
        shared_act, full_shared[:, 2 * SF :], contract_last, preferred_element_type=jnp.float32
    )
    slot_table, slot_gate = route_tables(routes[0], route_gates[0], EXPERTS, capacity)
    padded_rows = jnp.concatenate([normed_mid, jnp.zeros((1, model_width), jnp.bfloat16)], axis=0)
    expert_rows = jnp.take(padded_rows, slot_table, axis=0)
    arrived = lax.all_to_all(expert_rows, "wt", split_axis=0, concat_axis=0, tiled=True)
    slot_count = arrived.shape[1]
    grouped = arrived.reshape(shard_count, local_experts, slot_count, model_width)
    owner_gate_up = jnp.einsum(
        "wesd,edf->wesf", grouped, expert_weight[:, :, : 2 * F], preferred_element_type=jnp.float32
    )
    owner_act = (sigmoid_linear(owner_gate_up[..., :F]) * owner_gate_up[..., F:]).astype(
        jnp.bfloat16
    )
    owner_out = jnp.einsum(
        "wesf,edf->wesd",
        owner_act,
        expert_weight[:, :, 2 * F :],
        preferred_element_type=jnp.float32,
    ).astype(jnp.bfloat16)
    returned = lax.all_to_all(
        owner_out.reshape(shard_count * local_experts, slot_count, model_width),
        "wt",
        split_axis=0,
        concat_axis=0,
        tiled=True,
    )
    expert_out, owner_rows, owner_gate_up, owner_act = (
        returned,
        arrived,
        owner_gate_up.reshape(shard_count * local_experts, slot_count, 2 * F),
        owner_act.reshape(shard_count * local_experts, slot_count, F),
    )
    routed = (
        jnp.zeros((token_rows + 1, model_width), jnp.float32)
        .at[slot_table]
        .add(expert_out.astype(jnp.float32) * slot_gate[..., None])[:token_rows]
    )
    final_state = middle + shared_out + routed
    valid_float = valid_mask[0].astype(jnp.float32)
    deviation = final_state - teacher[0].astype(jnp.float32)
    squared_local = jnp.sum(valid_float[:, None] * deviation * deviation)
    count_local = jnp.sum(valid_float)
    squared_total, valid_count = lax.psum((squared_local, count_local), ("ctx", "wt"))
    loss_value = 0.5 * squared_total / (valid_count * model_width)
    grad_final = all_tokens / valid_count * valid_float[:, None] * deviation
    grad_shared_out = grad_final.astype(jnp.bfloat16)
    grad_shared_act = jnp.dot(
        grad_shared_out, full_shared[:, 2 * SF :], preferred_element_type=jnp.float32
    )
    grad_shared_down = lax.dot_general(
        grad_shared_out, shared_act, contract_first, preferred_element_type=jnp.float32
    )
    grad_shared_gate_up = gate_up_grads(grad_shared_act, shared_gate_up, SF)
    grad_normed_mid = lax.dot_general(
        grad_shared_gate_up,
        full_shared[:, : 2 * SF],
        contract_last,
        preferred_element_type=jnp.float32,
    )
    grad_shared_front = lax.dot_general(
        normed_mid, grad_shared_gate_up, contract_first, preferred_element_type=jnp.float32
    )
    grad_shared_full = jnp.concatenate([grad_shared_front, grad_shared_down], axis=1)
    padded_grads = jnp.concatenate([grad_final, jnp.zeros((1, model_width), jnp.float32)], axis=0)
    grad_expert_out = (jnp.take(padded_grads, slot_table, axis=0) * slot_gate[..., None]).astype(
        jnp.bfloat16
    )
    grad_arrived = lax.all_to_all(grad_expert_out, "wt", split_axis=0, concat_axis=0, tiled=True)
    grad_grouped = grad_arrived.reshape(shard_count, local_experts, capacity, model_width)
    owner_gate_up_grouped = owner_gate_up.reshape(shard_count, local_experts, capacity, 2 * F)
    owner_act_grouped = owner_act.reshape(shard_count, local_experts, capacity, F)
    owner_rows_grouped = owner_rows.reshape(shard_count, local_experts, capacity, model_width)
    grad_owner_act = jnp.einsum(
        "wecd,edf->wecf",
        grad_grouped,
        expert_weight[:, :, 2 * F :],
        preferred_element_type=jnp.float32,
    )
    grad_owner_gate_up = gate_up_grads(grad_owner_act, owner_gate_up_grouped, F)
    grad_owner_rows = jnp.einsum(
        "wecf,edf->wecd",
        grad_owner_gate_up,
        expert_weight[:, :, : 2 * F],
        preferred_element_type=jnp.float32,
    ).astype(jnp.bfloat16)
    front = jnp.einsum(
        "wecd,wecf->edf", owner_rows_grouped, grad_owner_gate_up, preferred_element_type=jnp.float32
    )
    back = jnp.einsum(
        "wecd,wecf->edf", grad_grouped, owner_act_grouped, preferred_element_type=jnp.float32
    )
    expert_grad = jnp.concatenate([front, back], axis=2)
    grad_rows = lax.all_to_all(
        grad_owner_rows.reshape(shard_count * local_experts, capacity, model_width),
        "wt",
        split_axis=0,
        concat_axis=0,
        tiled=True,
    )
    grad_normed_mid = (
        grad_normed_mid
        + jnp.zeros((token_rows + 1, model_width), jnp.float32)
        .at[slot_table]
        .add(grad_rows.astype(jnp.float32))[:token_rows]
    )
    grad_gain_mid_local = jnp.sum(grad_normed_mid * scaled_mid, axis=0)
    grad_middle = grad_final + norm_back(grad_normed_mid, scaled_mid, inverse_mid, gain_mid_float)
    grad_branch = grad_middle.astype(jnp.bfloat16)
    mixed_gradient = lax.dot_general(
        grad_branch, full_out, contract_last, preferred_element_type=jnp.float32
    ).astype(jnp.bfloat16)
    grad_out_local = lax.dot_general(
        mixed_rows, grad_branch, contract_first, preferred_element_type=jnp.float32
    )
    context_recomputed = lax.all_gather(context_local, "ctx", axis=0, tiled=True)
    backward_keys = context_recomputed[:, :key_value_width].reshape(
        number_of_blocks, key_row_count, KEY_VALUE_HEADS, HEAD_SIZE
    )
    backward_values = context_recomputed[:, key_value_width:].reshape(
        number_of_blocks, key_row_count, KEY_VALUE_HEADS, HEAD_SIZE
    )
    attention_output_gradient = mixed_gradient.reshape(
        token_rows, KEY_VALUE_HEADS, query_groups, HEAD_SIZE
    )
    grad_queries, grad_keys, grad_values = attend_backward(
        query_rows,
        backward_keys,
        backward_values,
        place_blocks,
        query_place,
        log_total,
        attention_output_gradient,
        attention_output,
        score_scale,
    )
    grad_context_all = jnp.concatenate(
        [
            grad_keys.reshape(seq_rows, key_value_width),
            grad_values.reshape(seq_rows, key_value_width),
        ],
        axis=1,
    )
    grad_context = lax.psum_scatter(
        grad_context_all.astype(jnp.bfloat16), "ctx", scatter_dimension=0, tiled=True
    ).astype(jnp.float32)
    grad_projected = jnp.concatenate(
        [grad_queries.reshape(token_rows, query_total_width), grad_context], axis=1
    ).astype(jnp.bfloat16)
    grad_normed_in = lax.dot_general(
        grad_projected, full_qkv, contract_last, preferred_element_type=jnp.float32
    )
    grad_qkv_local = lax.dot_general(
        normed_in, grad_projected, contract_first, preferred_element_type=jnp.float32
    )
    grad_gain_in_local = jnp.sum(grad_normed_in * scaled_in, axis=0)
    grad_inputs = grad_middle + norm_back(grad_normed_in, scaled_in, inverse_in, gain_in_float)
    weight_sums = (
        lax.psum_scatter(
            grad_gain_in_local.astype(jnp.bfloat16), "wt", scatter_dimension=0, tiled=True
        ).astype(jnp.float32),
        lax.psum_scatter(
            grad_qkv_local.astype(jnp.bfloat16), "wt", scatter_dimension=0, tiled=True
        ).astype(jnp.float32),
        lax.psum_scatter(
            grad_out_local.astype(jnp.bfloat16), "wt", scatter_dimension=0, tiled=True
        ).astype(jnp.float32),
        lax.psum_scatter(
            grad_gain_mid_local.astype(jnp.bfloat16), "wt", scatter_dimension=0, tiled=True
        ).astype(jnp.float32),
        lax.psum_scatter(
            grad_shared_full.astype(jnp.bfloat16), "wt", scatter_dimension=0, tiled=True
        ).astype(jnp.float32),
    )
    summed = (
        lax.psum(weight_sums[0].astype(jnp.bfloat16), "ctx").astype(jnp.float32),
        lax.psum(weight_sums[1].astype(jnp.bfloat16), "ctx").astype(jnp.float32),
        lax.psum(weight_sums[2].astype(jnp.bfloat16), "ctx").astype(jnp.float32),
        lax.psum(weight_sums[3].astype(jnp.bfloat16), "ctx").astype(jnp.float32),
        lax.psum(weight_sums[4].astype(jnp.bfloat16), "ctx").astype(jnp.float32),
        lax.psum(expert_grad.astype(jnp.bfloat16), "ctx").astype(jnp.float32),
    )
    return (
        final_state.astype(jnp.bfloat16)[None],
        loss_value,
        grad_inputs[None],
        summed[0],
        summed[1],
        summed[2],
        summed[3],
        summed[4],
        summed[5],
    )


COST_SHARE = 20


def flip(value, bit):
    return lax.ppermute(value, "ctx", [(index, index ^ bit) for index in range(8)])


def line_swap(value, offset):
    return lax.ppermute(value, "wt", [(index, index ^ offset) for index in range(4)])


def line_middle(value):
    return lax.ppermute(value, "wt", [(1, 2), (2, 1)])


def line_outward(value):
    return lax.ppermute(value, "wt", [(1, 0), (2, 3)])


def line_inward(value):
    return lax.ppermute(value, "wt", [(0, 1), (3, 2)])


def line_gather(value, at_end):
    near = line_swap(value, 1)
    middle = line_middle(value)
    middle_far = line_middle(near)
    outward = line_outward(middle)
    outward_far = line_outward(middle_far)
    return [
        value,
        near,
        jnp.where(at_end, outward, middle_far),
        jnp.where(at_end, outward_far, middle),
    ]


def line_reduce(parts):
    far = line_inward(parts[3])
    carried = parts[2] + far
    inward = line_inward(carried)
    crossed = line_middle(carried)
    near = line_swap(parts[1] + crossed, 1)
    middle = line_middle(parts[3] + inward)
    return (
        parts[0].astype(jnp.float32) + near.astype(jnp.float32) + middle.astype(jnp.float32)
    )


def chips_swap(values):
    return [values[0]] + [flip(values[r], 2 * r) for r in (1, 2, 3)]


def chips_gather(value, x_last):
    along_x = flip(value, 2)
    along_y = flip(value, 4)
    corner = flip(along_y, 2) if x_last else flip(along_x, 4)
    return [value, along_x, along_y, corner]


def core_swap(values):
    return [flip(value, 1) for value in values]


def everywhere_sum(value):
    for bit in (1, 2, 4):
        value = value + flip(value, bit)
    for offset in (1, 2):
        value = value + line_swap(value, offset)
    return value


def pick(blocks, index):
    return lax.dynamic_index_in_dim(blocks, index, 0, keepdims=False)


def chips_reduce(keep, came):
    half = keep.shape[1] // 2
    upper = keep[:, :half] + came[:, :half]
    lower = keep[:, half:] + came[:, half:]
    upper_came = flip(upper[1::2], 2)
    lower_came = flip(lower[2:], 4)
    upper = upper[0::2] + upper_came
    lower = lower[:2] + lower_came
    upper_came = flip(upper[1], 4)
    lower_came = flip(lower[1], 2)
    return jnp.concatenate([upper[0] + upper_came, lower[0] + lower_came], axis=0)


def dot_plain(left, right):
    return lax.dot_general(
        left, right, (((1,), (0,)), ((), ())), preferred_element_type=jnp.float32
    )


def dot_last(left, right):
    return lax.dot_general(
        left, right, (((1,), (1,)), ((), ())), preferred_element_type=jnp.float32
    )


def dot_first(left, right):
    return lax.dot_general(
        left, right, (((0,), (0,)), ((), ())), preferred_element_type=jnp.float32
    )


def call(kernel, name, meta, arrays, grid, in_specs, out_specs, out_shape, scratch, flops, moved):
    return pl.pallas_call(
        kernel,
        grid_spec=pltpu.PrefetchScalarGridSpec(
            num_scalar_prefetch=1,
            grid=grid,
            in_specs=in_specs,
            out_specs=out_specs,
            scratch_shapes=scratch,
        ),
        out_shape=out_shape,
        compiler_params=pltpu.CompilerParams(vmem_limit_bytes=48 * 1024 * 1024),
        cost_estimate=pl.CostEstimate(
            flops=int(flops) // COST_SHARE,
            bytes_accessed=int(moved) // COST_SHARE,
            transcendentals=0,
        ),
        name=name,
    )(meta, *arrays)


def whole(array):
    rank = len(array.shape)
    return pl.BlockSpec(tuple(array.shape), lambda *_: (0,) * rank)


def shape_of(shape, dtype):
    return jax.ShapeDtypeStruct(shape, dtype)


def size_of(arrays):
    return sum(math.prod(a.shape) * a.dtype.itemsize for a in arrays)


def aligned(value, step):
    return pl.multiple_of(value * step, step)


def project_kernel(meta, *refs):
    blocks, gain_ref, mine, other = refs[:4], refs[4], refs[5], refs[6]
    normed_ref, query_ref, pair_ref, weight_ref, held = refs[7:]
    step = pl.program_id(0)
    core, shard = meta[0] & 1, meta[1]
    rows = mine.shape[1]

    @pl.when(step == 0)
    def _():
        for i in range(4):
            at = 2 * (shard ^ i)
            weight_ref[pl.ds(aligned(at + core, rows), rows), :] = mine[i]
            weight_ref[pl.ds(aligned(at + 1 - core, rows), rows), :] = other[i]

    for r in range(4):

        @pl.when(step == r)
        def _():
            held[...] = blocks[r][...]

    states = held[...].astype(jnp.float32)
    inverse = lax.rsqrt(jnp.mean(states * states, axis=-1, keepdims=True) + norm_eps)
    normed = (states * inverse * gain_ref[...]).astype(jnp.bfloat16)
    normed_ref[0] = normed
    projected = dot_plain(normed, weight_ref[...]).astype(jnp.bfloat16)
    query_width = query_ref.shape[-1]
    query_ref[0] = projected[:, :query_width]
    pair_ref[0] = projected[:, query_width:]


def project(meta, blocks, gain, mine, other, query_width):
    token_rows, width = blocks[0].shape
    columns = mine.shape[2]
    arrays = list(blocks) + [gain, mine, other]
    outs = [
        shape_of((4, token_rows, width), jnp.bfloat16),
        shape_of((4, token_rows, query_width), jnp.bfloat16),
        shape_of((4, token_rows, columns - query_width), jnp.bfloat16),
        shape_of((width, columns), jnp.bfloat16),
    ]
    return call(
        project_kernel,
        "project",
        meta,
        arrays,
        (4,),
        [whole(a) for a in arrays],
        [
            pl.BlockSpec((1, token_rows, width), lambda r, m: (r, 0, 0)),
            pl.BlockSpec((1, token_rows, query_width), lambda r, m: (r, 0, 0)),
            pl.BlockSpec((1, token_rows, columns - query_width), lambda r, m: (r, 0, 0)),
            whole(outs[3]),
        ],
        outs,
        [pltpu.VMEM((token_rows, width), jnp.bfloat16)],
        2 * 4 * token_rows * width * columns,
        size_of(arrays) + size_of(outs),
    )


def sort_pairs(meta, mine_ref, other_ref, keys, values):
    half = mine_ref.shape[1] // 2
    for slot in range(16):
        block, part = (slot, 0) if slot < 8 else (15 - slot, 1)
        relative = meta[0] ^ block
        place = relative >> 1
        rows = pl.ds(part * half, half)
        to = pl.ds(slot * half, half)

        @pl.when((relative & 1) == 0)
        def _():
            keys[to, :] = mine_ref[place, rows, :HEAD_SIZE]
            values[to, :] = mine_ref[place, rows, HEAD_SIZE:]

        @pl.when((relative & 1) == 1)
        def _():
            keys[to, :] = other_ref[place, rows, :HEAD_SIZE]
            values[to, :] = other_ref[place, rows, HEAD_SIZE:]


def stack_heads(rows):
    count = rows.shape[1] // HEAD_SIZE
    return jnp.concatenate(
        [rows[:, h * HEAD_SIZE : (h + 1) * HEAD_SIZE] for h in range(count)], axis=0
    )


def unstack_heads(rows, count):
    each = rows.shape[0] // count
    return jnp.concatenate([rows[h * each : (h + 1) * each] for h in range(count)], axis=1)


def step_slot(meta):
    step = pl.program_id(0)
    block = meta[0] ^ (2 * (step >> 1))
    return jnp.where((step & 1) == 0, block, 15 - block)


def allowed_pairs(key_block, slot, shape, half):
    key_place = key_block * shape[0] + lax.broadcasted_iota(jnp.int32, shape, 0)
    query_place = slot * half + (lax.broadcasted_iota(jnp.int32, shape, 1) & (half - 1))
    return key_place <= query_place


def attend_kernel(scale, span, meta, query_ref, mine_ref, other_ref, *refs):
    outs, log_ref = refs[:4], refs[4]
    keys, values, values_turned = refs[5:]
    step = pl.program_id(0)
    half, group_width = query_ref.shape[1:]
    count = group_width // HEAD_SIZE

    @pl.when(step == 0)
    def _():
        sort_pairs(meta, mine_ref, other_ref, keys, values)
        values_turned[...] = values[...].T

    slot = step_slot(meta)
    query = stack_heads(query_ref[0])
    last = slot * half // span

    def scores_of(key_block):
        at = pl.ds(aligned(key_block, span), span)
        return at, dot_last(keys[at, :], query) * scale

    def add(carry, at, scores):
        highest, total, mixed = carry
        new = jnp.maximum(highest, jnp.max(scores, axis=0, keepdims=True))
        rescale = jnp.exp(highest - new)
        powers = jnp.exp(scores - new)
        total = total * rescale + jnp.sum(powers, axis=0, keepdims=True)
        mixed = mixed * rescale + dot_plain(values_turned[:, at], powers.astype(jnp.bfloat16))
        return new, total, mixed

    def body(key_block, carry):
        at, scores = scores_of(key_block)
        return add(carry, at, scores)

    wide = count * half
    carry = (
        jnp.full((1, wide), masked_score, jnp.float32),
        jnp.zeros((1, wide), jnp.float32),
        jnp.zeros((HEAD_SIZE, wide), jnp.float32),
    )
    carry = lax.fori_loop(0, last, body, carry)
    at, scores = scores_of(last)
    scores = jnp.where(allowed_pairs(last, slot, scores.shape, half), scores, masked_score)
    highest, total, mixed = add(carry, at, scores)
    log_ref[0] = highest + jnp.log(total)
    result = unstack_heads((mixed / total).T, count).astype(jnp.bfloat16)
    for r in range(4):
        for part in range(2):

            @pl.when(step == 2 * r + part)
            def _():
                outs[r][part * half : (part + 1) * half, :] = result


def attend(meta, query, mine, other, scale):
    token_rows, group_width = query.shape[1:]
    half = token_rows // 2
    count = group_width // HEAD_SIZE
    everything = 8 * token_rows
    span = min(256, everything)
    arrays = [query, mine, other]
    outs = [shape_of((token_rows, group_width), jnp.bfloat16)] * 4
    outs = outs + [shape_of((8, 1, count * half), jnp.float32)]
    result = call(
        functools.partial(attend_kernel, scale, span),
        "attend",
        meta,
        arrays,
        (8,),
        [
            pl.BlockSpec((1, half, group_width), lambda i, m: (i // 2, i % 2, 0)),
            whole(mine),
            whole(other),
        ],
        [whole(a) for a in outs[:4]]
        + [pl.BlockSpec((1, 1, count * half), lambda i, m: (i, 0, 0))],
        outs,
        [
            pltpu.VMEM((everything, HEAD_SIZE), jnp.bfloat16),
            pltpu.VMEM((everything, HEAD_SIZE), jnp.bfloat16),
            pltpu.VMEM((HEAD_SIZE, everything), jnp.bfloat16),
        ],
        2 * 2 * 4 * token_rows * everything * group_width,
        size_of(arrays) + size_of(outs),
    )
    return result[:4], result[4]


def attend_back_kernel(scale, span, meta, query_ref, mine_ref, other_ref, log_ref, *refs):
    mixed_refs, grad_refs = refs[:4], refs[4:8]
    grad_query_ref, grad_mine_ref, grad_other_ref = refs[8:11]
    keys, values, keys_turned, grad_keys, grad_values, mixed_held, grad_held = refs[11:]
    step = pl.program_id(0)
    half, group_width = query_ref.shape[1:]
    count = group_width // HEAD_SIZE

    @pl.when(step == 0)
    def _():
        sort_pairs(meta, mine_ref, other_ref, keys, values)
        keys_turned[...] = keys[...].T
        grad_keys[...] = jnp.zeros_like(grad_keys)
        grad_values[...] = jnp.zeros_like(grad_values)

    for r in range(4):
        for part in range(2):

            @pl.when(step == 2 * r + part)
            def _():
                mixed_held[...] = mixed_refs[r][part * half : (part + 1) * half, :]
                grad_held[...] = grad_refs[r][part * half : (part + 1) * half, :]

    slot = step_slot(meta)
    query = stack_heads(query_ref[0])
    mixed = stack_heads(mixed_held[...]).astype(jnp.float32)
    grad = stack_heads(grad_held[...])
    delta = jnp.sum((mixed * grad.astype(jnp.float32)).T, axis=0, keepdims=True)
    log_total = log_ref[0]
    last = slot * half // span

    def one(key_block, grad_turned, masked):
        at = pl.ds(aligned(key_block, span), span)
        scores = dot_last(keys[at, :], query) * scale
        probs = jnp.exp(scores - log_total)
        if masked:
            probs = jnp.where(allowed_pairs(key_block, slot, probs.shape, half), probs, 0.0)
        grad_probs = dot_last(values[at, :], grad)
        grad_scores = (probs * (grad_probs - delta)).astype(jnp.bfloat16)
        grad_values[at, :] += dot_plain(probs.astype(jnp.bfloat16), grad)
        grad_keys[at, :] += dot_plain(grad_scores, query)
        return grad_turned + dot_plain(keys_turned[:, at], grad_scores)

    grad_turned = jnp.zeros((HEAD_SIZE, count * half), jnp.float32)
    grad_turned = lax.fori_loop(0, last, lambda b, total: one(b, total, False), grad_turned)
    grad_turned = one(last, grad_turned, True)
    grad_query_ref[0] = unstack_heads((grad_turned * scale).T, count).astype(jnp.bfloat16)

    @pl.when(step == 7)
    def _():
        for slot_at in range(16):
            block, part = (slot_at, 0) if slot_at < 8 else (15 - slot_at, 1)
            relative = meta[0] ^ block
            place = relative >> 1
            rows = pl.ds(part * half, half)
            here = pl.ds(slot_at * half, half)
            both = jnp.concatenate([grad_keys[here, :] * scale, grad_values[here, :]], axis=1)

            @pl.when((relative & 1) == 0)
            def _():
                grad_mine_ref[place, rows, :] = both

            @pl.when((relative & 1) == 1)
            def _():
                grad_other_ref[place, rows, :] = both.astype(jnp.bfloat16)


def attend_back(meta, query, mine, other, log_total, mixed, grad, scale):
    token_rows, group_width = query.shape[1:]
    half = token_rows // 2
    count = group_width // HEAD_SIZE
    everything = 8 * token_rows
    span = min(256, everything)
    arrays = [query, mine, other, log_total] + list(mixed) + list(grad)
    outs = [
        shape_of(query.shape, jnp.bfloat16),
        shape_of(mine.shape, jnp.float32),
        shape_of(mine.shape, jnp.bfloat16),
    ]
    return call(
        functools.partial(attend_back_kernel, scale, span),
        "attend_back",
        meta,
        arrays,
        (8,),
        [
            pl.BlockSpec((1, half, group_width), lambda i, m: (i // 2, i % 2, 0)),
            whole(mine),
            whole(other),
            pl.BlockSpec((1, 1, count * half), lambda i, m: (i, 0, 0)),
        ]
        + [whole(a) for a in arrays[4:]],
        [
            pl.BlockSpec((1, half, group_width), lambda i, m: (i // 2, i % 2, 0)),
            whole(outs[1]),
            whole(outs[2]),
        ],
        outs,
        [
            pltpu.VMEM((everything, HEAD_SIZE), jnp.bfloat16),
            pltpu.VMEM((everything, HEAD_SIZE), jnp.bfloat16),
            pltpu.VMEM((HEAD_SIZE, everything), jnp.bfloat16),
            pltpu.VMEM((everything, HEAD_SIZE), jnp.float32),
            pltpu.VMEM((everything, HEAD_SIZE), jnp.float32),
            pltpu.VMEM((half, group_width), jnp.bfloat16),
            pltpu.VMEM((half, group_width), jnp.bfloat16),
        ],
        5 * 2 * 4 * token_rows * everything * group_width,
        size_of(arrays) + size_of(outs),
    )


def leave_kernel(meta, *refs):
    parts, mine, other = refs[:4], refs[4:8], refs[8]
    states_ref, gain_ref, weight_ref, middle_ref, normed_ref = refs[9:]
    core, chip, shard = meta[0] & 1, meta[0] >> 1, meta[1]
    rows = mine[0].shape[0]
    for i in range(4):
        at = 2 * (chip ^ shard ^ i)
        weight_ref[pl.ds(aligned(at + core, rows), rows), :] = mine[i][...]
        weight_ref[pl.ds(aligned(at + 1 - core, rows), rows), :] = other[i]
    middle = states_ref[...].astype(jnp.float32)
    for r in range(4):
        middle += dot_plain(parts[r][...], weight_ref[2 * rows * r : 2 * rows * (r + 1), :])
    middle_ref[...] = middle
    inverse = lax.rsqrt(jnp.mean(middle * middle, axis=-1, keepdims=True) + norm_eps)
    normed_ref[...] = (middle * inverse * gain_ref[...]).astype(jnp.bfloat16)


def leave(meta, parts, mine, other, states, gain):
    token_rows, width = states.shape
    arrays = list(parts) + list(mine) + [other, states, gain]
    outs = [
        shape_of((8 * mine[0].shape[0], width), jnp.bfloat16),
        shape_of((token_rows, width), jnp.float32),
        shape_of((token_rows, width), jnp.bfloat16),
    ]
    return call(
        leave_kernel,
        "leave",
        meta,
        arrays,
        (1,),
        [whole(a) for a in arrays],
        [whole(a) for a in outs],
        outs,
        [],
        2 * token_rows * width * width,
        size_of(arrays) + size_of(outs),
    )


def norm_back_rows(grad_normed, states, gain):
    inverse = lax.rsqrt(jnp.mean(states * states, axis=-1, keepdims=True) + norm_eps)
    scaled = states * inverse
    gain_grad = jnp.sum(grad_normed * scaled, axis=0, keepdims=True)
    grad_scaled = grad_normed * gain
    shift = jnp.mean(grad_scaled * scaled, axis=-1, keepdims=True)
    return inverse * (grad_scaled - scaled * shift), gain_grad


def enter_back_kernel(meta, final_ref, normed_ref, middle_ref, gain_ref, weight_ref, *refs):
    grad_ref, branch_ref, gain_grad_ref = refs[:3]
    grad, gain_grad = norm_back_rows(normed_ref[...], middle_ref[...], gain_ref[...])
    grad = grad + final_ref[...]
    grad_ref[...] = grad
    gain_grad_ref[...] = gain_grad
    branch = grad.astype(jnp.bfloat16)
    branch_ref[...] = branch
    rows = weight_ref.shape[0] // 4
    for r in range(4):
        refs[3 + r][...] = dot_last(branch, weight_ref[rows * r : rows * (r + 1), :]).astype(
            jnp.bfloat16
        )


def enter_back(meta, grad_final, grad_normed, middle, gain, weight):
    token_rows, width = middle.shape
    arrays = [grad_final, grad_normed, middle, gain, weight]
    outs = [
        shape_of((token_rows, width), jnp.float32),
        shape_of((token_rows, width), jnp.bfloat16),
        shape_of((1, width), jnp.float32),
    ] + [shape_of((token_rows, weight.shape[0] // 4), jnp.bfloat16)] * 4
    return call(
        enter_back_kernel,
        "enter_back",
        meta,
        arrays,
        (1,),
        [whole(a) for a in arrays],
        [whole(a) for a in outs],
        outs,
        [],
        2 * token_rows * width * width,
        size_of(arrays) + size_of(outs),
    )


def finish_kernel(meta, *refs):
    parts, mine, other = refs[:4], refs[4], refs[5]
    states_ref, middle_ref, gain_ref, grad_ref, gain_grad_ref, total = refs[6:]
    core = meta[0] & 1
    columns = mine.shape[1]
    for at, weights in ((core, mine), (1 - core, other)):
        total[:, pl.ds(aligned(at, columns), columns)] = sum(
            dot_last(parts[r][...], weights[r]) for r in range(4)
        )
    grad, gain_grad = norm_back_rows(
        total[...], states_ref[...].astype(jnp.float32), gain_ref[...]
    )
    grad_ref[0] = grad + middle_ref[...]
    gain_grad_ref[...] = gain_grad


def finish(meta, parts, mine, other, states, grad_middle, gain):
    token_rows, width = states.shape
    arrays = list(parts) + [mine, other, states, grad_middle, gain]
    outs = [
        shape_of((1, token_rows, width), jnp.float32),
        shape_of((1, width), jnp.float32),
    ]
    return call(
        finish_kernel,
        "finish",
        meta,
        arrays,
        (1,),
        [whole(a) for a in arrays],
        [whole(a) for a in outs],
        outs,
        [pltpu.VMEM((token_rows, width), jnp.float32)],
        2 * token_rows * width * 4 * parts[0].shape[1],
        size_of(arrays) + size_of(outs),
    )


def gated(gate_up, units):
    gate_part = gate_up[:, :units]
    sigma = 1.0 / (1.0 + jnp.exp(-gate_part))
    return gate_part * sigma * gate_up[:, units:]


def gated_back(grad_act, gate_up, units):
    gate_part = gate_up[:, :units].astype(jnp.float32)
    up_part = gate_up[:, units:].astype(jnp.float32)
    sigma = 1.0 / (1.0 + jnp.exp(-gate_part))
    linear = gate_part * sigma
    grad_gate = grad_act * up_part * (sigma * (1.0 + gate_part * (1.0 - sigma)))
    return grad_gate, grad_act * linear, linear * up_part


def experts_kernel(
    meta, rows_ref, gates_ref, expert_ref, shared_ref, gate_up_ref, shared_gate_up_ref, out_ref, total
):
    expert = pl.program_id(0)
    rows = rows_ref[...]

    @pl.when(expert == 0)
    def _():
        units = shared_ref.shape[1] // 3
        gate_up = dot_plain(rows, shared_ref[:, : 2 * units])
        shared_gate_up_ref[...] = gate_up.astype(jnp.bfloat16)
        act = gated(gate_up, units).astype(jnp.bfloat16)
        total[...] = dot_last(act, shared_ref[:, 2 * units :])

    gate_up = dot_plain(rows, expert_ref[0, :, : 2 * F])
    gate_up_ref[0] = gate_up.astype(jnp.bfloat16)
    act = (gated(gate_up, F) * gates_ref[0]).astype(jnp.bfloat16)
    total[...] += dot_last(act, expert_ref[0, :, 2 * F :])

    @pl.when(expert == pl.num_programs(0) - 1)
    def _():
        out_ref[...] = total[...].astype(jnp.bfloat16)


def experts(meta, rows, gates, expert_weight, shared_slice):
    local_experts, width, _ = expert_weight.shape
    token_rows = rows.shape[0]
    shared_units = shared_slice.shape[1] // 3
    arrays = [rows, gates, expert_weight, shared_slice]
    outs = [
        shape_of((local_experts, token_rows, 2 * F), jnp.bfloat16),
        shape_of((token_rows, 2 * shared_units), jnp.bfloat16),
        shape_of((token_rows, width), jnp.bfloat16),
    ]
    return call(
        experts_kernel,
        "experts",
        meta,
        arrays,
        (local_experts,),
        [
            whole(rows),
            pl.BlockSpec((1, token_rows, 1), lambda e, m: (e, 0, 0)),
            pl.BlockSpec((1, width, 3 * F), lambda e, m: (e, 0, 0)),
            whole(shared_slice),
        ],
        [
            pl.BlockSpec((1, token_rows, 2 * F), lambda e, m: (e, 0, 0)),
            whole(outs[1]),
            whole(outs[2]),
        ],
        outs,
        [pltpu.VMEM((token_rows, width), jnp.float32)],
        2 * token_rows * width * 3 * (F * local_experts + shared_units),
        size_of(arrays) + size_of(outs),
    )


def experts_back_kernel(
    meta,
    grad_ref,
    gates_ref,
    gate_up_ref,
    shared_gate_up_ref,
    expert_ref,
    shared_ref,
    grad_gate_up_ref,
    act_ref,
    shared_grad_ref,
    shared_act_ref,
    grad_rows_ref,
    total,
):
    expert = pl.program_id(0)
    grad = grad_ref[...]

    @pl.when(expert == 0)
    def _():
        units = shared_ref.shape[1] // 3
        grad_act = dot_plain(grad, shared_ref[:, 2 * units :])
        grad_gate, grad_up, act = gated_back(grad_act, shared_gate_up_ref[...], units)
        both = jnp.concatenate([grad_gate, grad_up], axis=1).astype(jnp.bfloat16)
        shared_grad_ref[0] = both
        shared_act_ref[0] = act.astype(jnp.bfloat16)
        total[...] = dot_last(both, shared_ref[:, : 2 * units])

    grad_act = dot_plain(grad, expert_ref[0, :, 2 * F :]) * gates_ref[0]
    grad_gate, grad_up, act = gated_back(grad_act, gate_up_ref[0], F)
    both = jnp.concatenate([grad_gate, grad_up], axis=1).astype(jnp.bfloat16)
    grad_gate_up_ref[0] = both
    act_ref[0] = (act * gates_ref[0]).astype(jnp.bfloat16)
    total[...] += dot_last(both, expert_ref[0, :, : 2 * F])

    @pl.when(expert == pl.num_programs(0) - 1)
    def _():
        grad_rows_ref[...] = total[...].astype(jnp.bfloat16)


def experts_back(meta, grad, gates, gate_up, shared_gate_up, expert_weight, shared_slice):
    local_experts, width, _ = expert_weight.shape
    token_rows = grad.shape[0]
    shared_units = shared_slice.shape[1] // 3
    arrays = [grad, gates, gate_up, shared_gate_up, expert_weight, shared_slice]
    outs = [
        shape_of((local_experts, token_rows, 2 * F), jnp.bfloat16),
        shape_of((local_experts, token_rows, F), jnp.bfloat16),
        shape_of((1, token_rows, 2 * shared_units), jnp.bfloat16),
        shape_of((1, token_rows, shared_units), jnp.bfloat16),
        shape_of((token_rows, width), jnp.bfloat16),
    ]
    return call(
        experts_back_kernel,
        "experts_back",
        meta,
        arrays,
        (local_experts,),
        [
            whole(grad),
            pl.BlockSpec((1, token_rows, 1), lambda e, m: (e, 0, 0)),
            pl.BlockSpec((1, token_rows, 2 * F), lambda e, m: (e, 0, 0)),
            whole(shared_gate_up),
            pl.BlockSpec((1, width, 3 * F), lambda e, m: (e, 0, 0)),
            whole(shared_slice),
        ],
        [
            pl.BlockSpec((1, token_rows, 2 * F), lambda e, m: (e, 0, 0)),
            pl.BlockSpec((1, token_rows, F), lambda e, m: (e, 0, 0)),
            whole(outs[2]),
            whole(outs[3]),
            whole(outs[4]),
        ],
        outs,
        [pltpu.VMEM((token_rows, width), jnp.float32)],
        2 * token_rows * width * 3 * (F * local_experts + shared_units),
        size_of(arrays) + size_of(outs),
    )


def weight_grad_kernel(pairs, core_at, meta, *refs):
    keep_ref, give_ref = refs[-2:]
    at = 0
    columns = 0
    parts = []
    for count in pairs:
        lefts, rights = refs[at : at + count], refs[at + count : at + 2 * count]
        at += 2 * count
        parts.append(
            sum(dot_first(a[...], b[0]) for a, b in zip(lefts, rights)).astype(jnp.bfloat16)
        )
    half = keep_ref.shape[1]

    for core, (first, second) in ((0, (keep_ref, give_ref)), (1, (give_ref, keep_ref))):

        @pl.when((meta[core_at] & 1) == core)
        def _():
            start = 0
            for part in parts:
                stop = start + part.shape[1]
                first[0, :, start:stop] = part[:half]
                second[0, :, start:stop] = part[half:]
                start = stop


def weight_grad_whole_kernel(pairs, meta, *refs):
    at, start = 0, 0
    for count in pairs:
        lefts, rights = refs[at : at + count], refs[at + count : at + 2 * count]
        at += 2 * count
        part = sum(dot_first(a[...], b[0]) for a, b in zip(lefts, rights)).astype(jnp.bfloat16)
        refs[-1][:, start : start + part.shape[1]] = part
        start += part.shape[1]


def weight_grad(meta, order, operands, index, split=True):
    token_rows, width = operands[0][0][0].shape
    tile = width // 4
    scalars = jnp.stack([order, meta[0]])
    arrays, in_specs, columns = [], [], 0
    for lefts, rights in operands:
        arrays += list(lefts) + list(rights)
        in_specs += [pl.BlockSpec((token_rows, tile), lambda i, m: (0, i ^ m[0]))] * len(lefts)
        units = rights[0].shape[-1]
        at = index if rights[0].shape[0] > 1 else 0
        in_specs += [
            pl.BlockSpec((1, token_rows, units), lambda i, m, at=at: (at, 0, 0))
        ] * len(rights)
        columns += units
    tokens = token_rows * len(operands[0][0])
    counts = [len(left) for left, _ in operands]
    if not split:
        return call(
            functools.partial(weight_grad_whole_kernel, counts),
            "weight_grad_whole",
            scalars,
            arrays,
            (4,),
            in_specs,
            pl.BlockSpec((tile, columns), lambda i, m: (i, 0)),
            shape_of((width, columns), jnp.bfloat16),
            [],
            2 * tokens * width * columns,
            2 * width * columns + 4 * tokens * width + 2 * tokens * columns,
        )
    outs = [shape_of((4, tile // 2, columns), jnp.bfloat16)] * 2
    return call(
        functools.partial(weight_grad_kernel, counts, 1),
        "weight_grad",
        scalars,
        arrays,
        (4,),
        in_specs,
        [pl.BlockSpec((1, tile // 2, columns), lambda i, m: (i, 0, 0))] * 2,
        outs,
        [],
        2 * tokens * width * columns,
        size_of(outs) + 4 * tokens * width + 2 * tokens * columns,
    )


def place_expert_kernel(meta, *refs):
    mine, other, out_ref = refs[-6:-2], refs[-2], refs[-1]
    step = pl.program_id(0)
    core = meta[0] & 1
    rows = mine[0].shape[0]
    columns = out_ref.shape[2]
    out_ref[0, pl.ds(aligned(1 - core, rows), rows), :] = other[0, :, :columns].astype(
        jnp.float32
    )
    for r in range(4):

        @pl.when(step == r)
        def _():
            out_ref[0, pl.ds(aligned(core, rows), rows), :] = mine[r][:, :columns].astype(
                jnp.float32
            )


def place_total_kernel(meta, *refs):
    refs[-1][0] = refs[-2][...].astype(jnp.float32)


def place_call(kernel, name, meta, total, arrays, in_specs, out_spec, shape, moved):
    aliases = {}
    if total is not None:
        arrays = [total] + arrays
        in_specs = [pl.BlockSpec(memory_space=pl.ANY)] + in_specs
        aliases = {1: 0}
    return pl.pallas_call(
        kernel,
        grid_spec=pltpu.PrefetchScalarGridSpec(
            num_scalar_prefetch=1, grid=(4,), in_specs=in_specs, out_specs=out_spec
        ),
        out_shape=shape_of(shape, jnp.float32),
        input_output_aliases=aliases,
        compiler_params=pltpu.CompilerParams(vmem_limit_bytes=48 * 1024 * 1024),
        cost_estimate=pl.CostEstimate(flops=0, bytes_accessed=moved // COST_SHARE, transcendentals=0),
        name=name,
    )(meta, *arrays)


def place_expert(meta, total, index, shape, mine, other):
    rows, columns = mine[0].shape
    return place_call(
        place_expert_kernel,
        "place_expert",
        meta,
        total,
        list(mine) + [other],
        [whole(a) for a in mine] + [pl.BlockSpec((1, rows, columns), lambda r, m: (r, 0, 0))],
        pl.BlockSpec((1, 2 * rows, shape[2]), lambda r, m: (index, (m[0] >> 1) ^ r, 0)),
        shape,
        8 * rows * columns * 6,
    )


def place_total(meta, total, index, shape, value):
    rows, columns = value.shape
    return place_call(
        place_total_kernel,
        "place_total",
        meta,
        total,
        [value],
        [pl.BlockSpec((rows // 4, columns), lambda r, m: (r, 0))],
        pl.BlockSpec((1, rows // 4, columns), lambda r, m: (index, r, 0)),
        shape,
        rows * columns * 6,
    )


def place_shared_kernel(meta, mine, other, out_ref):
    core = meta[0] & 1
    rows = mine.shape[1]
    out_ref[pl.ds(aligned(core, rows), rows), :] = mine[0].astype(jnp.float32)
    out_ref[pl.ds(aligned(1 - core, rows), rows), :] = other[0].astype(jnp.float32)


def place_shared(meta, mine, other):
    _, rows, columns = mine.shape
    units = columns // 3
    block = pl.BlockSpec((1, rows, units), lambda i, j, m: (i, 0, j))
    outs = shape_of((2 * rows, 4 * columns), jnp.float32)
    return call(
        place_shared_kernel,
        "place_shared",
        meta,
        [mine, other],
        (4, 3),
        [block, block],
        pl.BlockSpec((2 * rows, units), lambda i, j, m: (0, 4 * j + (m[1] ^ i))),
        outs,
        [],
        0,
        size_of([mine, other, outs]),
    )


def place_heads_kernel(meta, *refs):
    mine, other, out_ref = refs[:4], refs[4], refs[5]
    core, chip = meta[0] & 1, meta[0] >> 1
    rows, columns = mine[0].shape
    group_width = columns - 2 * HEAD_SIZE
    for r in range(4):
        head = chip ^ r
        for at, pieces in ((core, [piece[...] for piece in mine]), (1 - core, other)):
            to = pl.ds(aligned(at, rows), rows)
            values = pieces[r].astype(jnp.float32)
            out_ref[to, pl.ds(aligned(head, group_width), group_width)] = values[:, :group_width]
            out_ref[to, pl.ds(aligned(4 * group_width // HEAD_SIZE + head, HEAD_SIZE), HEAD_SIZE)] = (
                values[:, group_width : group_width + HEAD_SIZE]
            )
            out_ref[
                to, pl.ds(aligned(4 * group_width // HEAD_SIZE + 4 + head, HEAD_SIZE), HEAD_SIZE)
            ] = values[:, group_width + HEAD_SIZE :]


def place_heads(meta, mine, other):
    rows, columns = mine[0].shape
    arrays = list(mine) + [other]
    outs = shape_of((2 * rows, 4 * columns), jnp.float32)
    return call(
        place_heads_kernel,
        "place_heads",
        meta,
        arrays,
        (1,),
        [whole(a) for a in arrays],
        whole(outs),
        outs,
        [],
        0,
        size_of(arrays + [outs]),
    )


def join_shared_kernel(meta, mine, other, out_ref):
    step = pl.program_id(0)
    rows = mine.shape[2]
    first = meta[0] ^ (2 * step)
    for i in range(4):
        at = 8 * (meta[1] ^ i)
        out_ref[pl.ds(aligned(at + first, rows), rows), :] = mine[0, i]
        out_ref[pl.ds(aligned(at + (first ^ 1), rows), rows), :] = other[0, i]


def join_shared(meta, mine, other):
    _, _, rows, columns = mine.shape
    block = pl.BlockSpec((1, 4, rows, columns), lambda r, m: (r, 0, 0, 0))
    outs = shape_of((32 * rows, columns), jnp.bfloat16)
    return call(
        join_shared_kernel,
        "join_shared",
        meta,
        [mine, other],
        (4,),
        [block, block],
        whole(outs),
        outs,
        [],
        0,
        size_of([mine, other, outs]),
    )


class Clock:
    def __init__(self):
        self.last = None

    def __call__(self, *values):
        if self.last is None:
            return values if len(values) > 1 else values[0]
        held = lax.optimization_barrier(tuple(values) + (self.last,))[:-1]
        return held if len(held) > 1 else held[0]

    def mark(self, value):
        self.last = value
        return value


SUMMED = 0
SHARED_WITH = 0
EARLY = (
    "H", "W", "K", "K", "W", "S", "O", "K", "S", "W", "O", "M", "S", "O", "M", "S", "O", "O", "S", "M", "S", "M", "R", "K",
    "M", "M", "K", "M", "R", "K", "M", "M", "K", "M", "R", "M", "M", "M", "M",
)
LATE = (
    "L", "2", "0", "2", "3", "0", "L", "3", "1", "2", "L", "1", "3", "L", "2", "O", "0", "3", "1", "O", "L", "2", "O", "3",
    "0", "1", "O", "2", "3", "O", "L", "2", "Q", "O", "3", "Q", "0", "1", "L", "O", "Q", "O", "L", "Q", "Q", "1", "0", "S",
    "Q", "1", "0", "L", "Q", "L", "Q", "S", "L", "L", "S",
)


def fast_device(
    hidden,
    teacher,
    valid_mask,
    routes,
    route_gates,
    gain_in,
    query_key_value_weight,
    out_weight,
    gain_mid,
    shared_weight,
    expert_weight,
):
    token_rows, width = hidden.shape[1:]
    context_count, shard_count = 8, 4
    context_index = lax.axis_index("ctx").astype(jnp.int32)
    shard_index = lax.axis_index("wt").astype(jnp.int32)
    plain_meta = jnp.stack([context_index, shard_index])
    core = context_index & 1
    chip = context_index >> 1
    at_end = (shard_index == 0) | (shard_index == shard_count - 1)
    group_width = QUERY_HEADS // KEY_VALUE_HEADS * HEAD_SIZE
    query_width = QUERY_HEADS * HEAD_SIZE
    kv_width = KEY_VALUE_HEADS * HEAD_SIZE
    scale = 1.0 / math.sqrt(HEAD_SIZE)
    all_tokens = token_rows * context_count * shard_count
    shard_rows = query_key_value_weight.shape[0]
    half_rows = shard_rows // 2
    local_experts = expert_weight.shape[0]
    bf16, f32 = jnp.bfloat16, jnp.float32
    states = hidden[0]
    clock = Clock()
    have = {}

    def meta():
        return clock(plain_meta)

    def now(*values):
        return clock(*values)


    def hidden_chain():
        have["blocks"] = chips_swap([states] * 4)
        yield

    def qkv_chain():
        rows = lax.dynamic_slice_in_dim(query_key_value_weight, core * half_rows, half_rows, 0)
        half = jnp.concatenate(
            [
                lax.dynamic_slice_in_dim(rows, chip * group_width, group_width, 1),
                lax.dynamic_slice_in_dim(rows, query_width + chip * HEAD_SIZE, HEAD_SIZE, 1),
                lax.dynamic_slice_in_dim(
                    rows, query_width + kv_width + chip * HEAD_SIZE, HEAD_SIZE, 1
                ),
            ],
            axis=1,
        )
        came = line_swap(half, 1)
        yield
        pair = clock.mark(jnp.stack([half, now(came)]))
        came = line_swap(pair, 2)
        yield
        have["qkv_mine"] = clock.mark(jnp.concatenate([pair, now(came)]))
        have["qkv_other"] = flip(have["qkv_mine"], 1)
        yield

    def small_chain():
        expert_ids = jnp.arange(EXPERTS, dtype=jnp.int32)
        matrix = jnp.sum(
            jnp.where(
                routes[0][None, :, :] == expert_ids[:, None, None], route_gates[0][None, :, :], 0.0
            ),
            axis=-1,
        )
        have["valid"] = valid_mask[0].astype(f32)
        gains = jnp.concatenate([gain_in, gain_mid]).astype(f32).reshape(-1, token_rows)
        gain_rows = gains.shape[0]
        filled = EXPERTS + gain_rows
        pack = jnp.concatenate(
            [
                matrix,
                gains,
                jnp.full((32 - filled, token_rows), jnp.sum(have["valid"]), f32),
            ]
        )
        came = line_swap(pack, 1)
        yield
        pair = clock.mark(jnp.stack([pack, now(came)]))
        came = line_swap(pair, 2)
        yield
        all_packs = clock.mark(jnp.concatenate([pair, now(came)]))
        have["gates"] = [
            lax.dynamic_slice_in_dim(
                all_packs[i], shard_index * local_experts, local_experts, 0
            )[..., None]
            for i in range(4)
        ]
        gains = all_packs[:, EXPERTS:filled].reshape(4, 2, shard_rows)
        gains = jnp.stack([pick(gains, shard_index ^ i) for i in range(4)], axis=1)
        have["gains"] = gains.reshape(2, 1, width)
        total = jnp.broadcast_to(jnp.sum(all_packs[:, filled, 0]), (8, 128))
        yield
        total = now(total)
        for bit in (1, 2, 4):
            came = flip(total, bit)
            yield
            total = clock.mark(total + now(came))
        have["count"] = total[0, 0]
        yield

    def shared_chain():
        eighth = shard_rows // 8
        units = SF // shard_count
        piece = lax.dynamic_slice_in_dim(shared_weight, context_index * eighth, eighth, 0)
        piece = piece.reshape(eighth, 3, shard_count, units)

        def columns(index):
            part = lax.dynamic_index_in_dim(piece, shard_index ^ index, 2, keepdims=False)
            return part.reshape(eighth, 3 * units)

        first = now(jnp.stack([columns(0), columns(2)]))
        came = line_swap(now(jnp.stack([columns(1), columns(3)])), 1)
        yield
        came = now(came)
        mine = jnp.stack([first[0], came[0]])
        came = line_swap(clock.mark(jnp.stack([first[1], came[1]])), 2)
        yield
        pieces = clock.mark(jnp.concatenate([mine, now(came)]))
        came = flip(pieces, 2)
        yield
        pair = clock.mark(jnp.stack([pieces, now(came)]))
        came = flip(pair, 4)
        yield
        mine = clock.mark(jnp.concatenate([pair, now(came)]))
        other = flip(mine, 1)
        yield
        have["shared"] = join_shared(meta(), mine, other)
        clock.mark(have["shared"])
        yield

    def out_chain():
        half = lax.dynamic_slice_in_dim(now(out_weight), core * half_rows, half_rows, 0)
        near = line_swap(half, 1)
        yield
        near = now(near)
        middle = line_middle(now(half))
        middle_far = line_middle(near)
        yield
        outward = line_outward(now(middle))
        yield
        outward_far = line_outward(now(middle_far))
        yield
        outward, outward_far = now(outward, outward_far)
        third = jnp.where(at_end, outward, middle_far)
        fourth = jnp.where(at_end, outward_far, middle)
        have["out_mine"] = [half, near, third, fourth]
        have["out_other"] = flip(clock.mark(jnp.stack(have["out_mine"])), 1)
        yield

    def qkv_all_chain():
        half = lax.dynamic_slice_in_dim(
            now(have["qkv_slice"]), core * (width // 2), width // 2, 0
        )
        came = flip(half, 2)
        yield
        pair = clock.mark(jnp.stack([half, now(came)]))
        came = flip(pair, 4)
        yield
        have["rel_mine"] = clock.mark(jnp.concatenate([pair, now(came)]))
        have["rel_other"] = flip(have["rel_mine"], 1)
        yield

    def main_chain():
        gains = have["gains"]
        normed_in, query, pair, qkv_slice = project(
            meta(), have["blocks"], gains[0], have["qkv_mine"], have["qkv_other"], group_width
        )
        clock.mark(pair)
        have["normed_in"], have["qkv_slice"] = normed_in, qkv_slice
        pair_other = flip(pair, 1)
        yield
        mixed_heads, log_total = attend(meta(), query, pair, pair_other, scale)
        clock.mark(log_total)
        have["attend"] = (query, pair, pair_other, log_total, mixed_heads)
        mixed = chips_swap(mixed_heads)
        have["mixed"] = mixed
        yield
        out_rel, middle, normed_mid = leave(
            meta(), mixed, have["out_mine"], have["out_other"], states, gains[1]
        )
        have["out_rel"], have["middle"] = out_rel, middle
        clock.mark(normed_mid)

        near, center = line_swap(normed_mid, 1), line_middle(normed_mid)
        yield
        gates, shared_slice = have["gates"], have["shared"]
        gate_ups, shared_gate_ups, outs = [], [], []

        def forward(rows, i):
            result = experts(meta(), rows, gates[i], expert_weight, shared_slice)
            clock.mark(result[2])
            gate_ups.append(result[0])
            shared_gate_ups.append(result[1])
            outs.append(result[2])

        forward(normed_mid, 0)
        yield
        near, center = now(near, center)
        far, outward = line_middle(near), line_outward(center)
        forward(near, 1)
        yield
        far, outward = now(far, outward)
        outward_far = line_outward(far)
        third = clock.mark(jnp.where(at_end, outward, far))
        forward(third, 2)
        yield
        outward_far = now(outward_far)
        fourth = clock.mark(jnp.where(at_end, outward_far, center))
        forward(fourth, 3)
        line_rows = [normed_mid, near, third, fourth]
        came = line_inward(outs[3])
        yield
        carried = clock.mark(outs[2] + now(came))
        inward, crossed = line_inward(carried), line_middle(carried)
        yield
        inward, crossed = now(inward, crossed)
        near_out = clock.mark(outs[1] + crossed)
        middle_out = clock.mark(outs[3] + inward)
        near_out, middle_out = line_swap(near_out, 1), line_middle(middle_out)
        yield
        near_out, middle_out = now(near_out, middle_out)
        final_state = (
            middle + outs[0].astype(f32) + near_out.astype(f32) + middle_out.astype(f32)
        )
        valid = have["valid"]
        deviation = final_state - teacher[0].astype(f32)
        have["squared"] = jnp.sum(valid[:, None] * deviation * deviation)
        grad_final = all_tokens / have["count"] * valid[:, None] * deviation
        have["final"], have["grad_final"] = final_state.astype(bf16)[None], grad_final
        grad_low = clock.mark(grad_final.astype(bf16))
        near, center = line_swap(grad_low, 1), line_middle(grad_low)
        yield
        kept = []

        def backward(grads, i):
            kept.append(
                experts_back(
                    meta(),
                    grads,
                    gates[i],
                    gate_ups[i],
                    shared_gate_ups[i],
                    expert_weight,
                    shared_slice,
                )
            )
            clock.mark(kept[-1][4])

        backward(grad_low, 0)
        yield
        near, center = now(near, center)
        far, outward = line_middle(near), line_outward(center)
        backward(near, 1)
        yield
        far, outward = now(far, outward)
        outward_far = line_outward(far)
        third = clock.mark(jnp.where(at_end, outward, far))
        backward(third, 2)
        yield
        outward_far = now(outward_far)
        fourth = clock.mark(jnp.where(at_end, outward_far, center))
        backward(fourth, 3)
        have["line"] = (line_rows, [grad_low, near, third, fourth])
        have["experts"] = list(zip(*kept))
        yield


    def states_chain():
        outs = have["experts"][4]
        came = line_inward(outs[3])
        yield
        carried = clock.mark(outs[2] + now(came))
        inward, crossed = line_inward(carried), line_middle(carried)
        yield
        inward, crossed = now(inward, crossed)
        near_out = clock.mark(outs[1] + crossed)
        middle_out = clock.mark(outs[3] + inward)
        near_out, middle_out = line_swap(near_out, 1), line_middle(middle_out)
        yield
        near_out, middle_out = now(near_out, middle_out)
        grad_normed = clock.mark(
            outs[0].astype(f32) + near_out.astype(f32) + middle_out.astype(f32)
        )
        grad_middle, grad_branch, grad_gain_mid, *grad_mixed = enter_back(
            meta(),
            have["grad_final"],
            grad_normed,
            have["middle"],
            have["gains"][1],
            have["out_rel"],
        )
        clock.mark(grad_branch)
        have["grad_branch"], have["grad_gain_mid"] = grad_branch, grad_gain_mid
        grad_mixed = chips_swap(grad_mixed)
        yield
        query, pair, pair_other, log_total, mixed_heads = have["attend"]
        grad_query, grad_pair, grad_other = attend_back(
            meta(), query, pair, pair_other, log_total, mixed_heads, grad_mixed, scale
        )
        clock.mark(grad_query)
        came = flip(grad_other, 1)
        yield
        grad_pair = grad_pair + now(came).astype(f32)
        projected = clock.mark(jnp.concatenate([grad_query, grad_pair.astype(bf16)], axis=-1))
        have["grad_projected"] = projected
        parts = chips_swap([projected[r] for r in range(4)])
        yield
        grad_hidden, grad_gain_in = finish(
            meta(),
            parts,
            have["rel_mine"],
            have["rel_other"],
            states,
            grad_middle,
            have["gains"][0],
        )
        clock.mark(grad_gain_in)
        have["grad_hidden"] = grad_hidden
        sums = jnp.concatenate(
            [grad_gain_in, have["grad_gain_mid"], jnp.full((6, width), have["squared"], f32)],
            axis=0,
        )
        for bit in (1, 2, 4):
            came = flip(sums, bit)
            yield
            sums = clock.mark(sums + now(came))
        for offset in (1, 2):
            came = line_swap(sums, offset)
            yield
            sums = clock.mark(sums + now(came))
        own = lax.dynamic_slice_in_dim(sums, shard_index * shard_rows, shard_rows, 1)
        have["sums"] = (own, 0.5 * sums[2, 0] / (have["count"] * width))
        yield

    def expert_chain(expert):
        line_rows, line_grads = have["line"]
        grad_gate_ups, acts, shared_grads, shared_acts = have["experts"][:4]
        operands = [(line_rows, grad_gate_ups), (line_grads, acts)]
        if expert == SHARED_WITH:
            operands += [(line_rows, shared_grads), (line_grads, shared_acts)]
        keep, give = weight_grad(meta(), chip, operands, expert)
        clock.mark(keep)
        came = flip(give, 1)
        yield
        came = now(came)
        if expert % 2 == 0:
            first, second = 2, 4
            give = clock.mark(keep[1::2] + came[1::2])
            keep = keep[0::2] + came[0::2]
        else:
            first, second = 4, 2
            give = clock.mark(keep[2:] + came[2:])
            keep = keep[:2] + came[:2]
        came = flip(give, first)
        yield
        came = now(came)
        give = clock.mark(keep[1] + came[1])
        keep = keep[0] + came[0]
        came = flip(give, second)
        yield
        own = clock.mark(keep + now(came))
        came = flip(own, second)
        yield
        pair = clock.mark(jnp.stack([own, now(came)]))
        came = flip(pair, first)
        yield
        came = now(came)
        if expert % 2 == 0:
            mine = [own, came[0], pair[1], came[1]]
        else:
            mine = [own, pair[1], came[0], came[1]]
        stacked = clock.mark(jnp.stack(mine))
        other = flip(stacked, 1)
        if expert == SHARED_WITH:
            have["shared_sum"] = stacked[:, :, 3 * F :]
        yield
        have["grad_experts"] = place_expert(
            meta(), have.get("grad_experts"), expert, expert_weight.shape, mine, other
        )
        clock.mark(have["grad_experts"])
        yield

    def shared_grad_chain():
        total = now(have["shared_sum"])
        parts = [pick(total, chip ^ shard_index ^ i) for i in range(4)]
        parts = [parts[0]] + [line_swap(clock.mark(parts[i]), i) for i in (1, 2, 3)]
        yield
        mine = clock.mark(jnp.stack(now(*parts)))
        other = flip(mine, 1)
        yield
        have["grad_shared"] = clock.mark(place_shared(meta(), mine, other))
        yield

    def summed_chain():
        line_rows, line_grads = have["line"]
        grad_gate_ups, acts = have["experts"][:2]
        sums = []
        for expert in range(SUMMED):
            sums.append(
                weight_grad(
                    meta(),
                    jnp.int32(0),
                    [(line_rows, grad_gate_ups), (line_grads, acts)],
                    expert,
                    split=False,
                )
            )
            clock.mark(sums[-1])
        sums = lax.psum(sums, "ctx")
        yield
        for expert in range(SUMMED):
            have["grad_experts"] = place_total(
                meta(), have.get("grad_experts"), expert, expert_weight.shape, sums[expert]
            )
            clock.mark(have["grad_experts"])
        yield

    def line_reduce_steps(keep, came):
        came = now(came)
        parts = [keep[i] + came[i] for i in range(4)]
        came = line_inward(clock.mark(parts[3]))
        yield
        carried = clock.mark(parts[2] + now(came))
        inward, crossed = line_inward(carried), line_middle(carried)
        yield
        inward, crossed = now(inward, crossed)
        near_out = clock.mark(parts[1] + crossed)
        middle_out = clock.mark(parts[3] + inward)
        near_out, middle_out = line_swap(near_out, 1), line_middle(middle_out)
        yield
        near_out, middle_out = now(near_out, middle_out)
        have["line_sum"] = clock.mark(
            (parts[0].astype(f32) + near_out.astype(f32) + middle_out.astype(f32)).astype(bf16)
        )

    def out_grad_chain():
        mixed = jnp.concatenate(have["mixed"], axis=1)
        keep, give = weight_grad(
            meta(), chip ^ shard_index, [([mixed], [have["grad_branch"][None]])], 0
        )
        clock.mark(keep)
        came = flip(give, 1)
        yield
        yield from line_reduce_steps(keep, came)
        total = have["line_sum"]
        came = flip(total, 2)
        yield
        total = clock.mark(total + now(came))
        came = flip(total, 4)
        yield
        mine = clock.mark(total + now(came))
        other = flip(mine, 1)
        yield
        mine, other = now(mine, other)
        have["grad_out"] = clock.mark(
            jnp.where(
                core == 0,
                jnp.concatenate([mine, other], axis=0),
                jnp.concatenate([other, mine], axis=0),
            ).astype(f32)
        )
        yield

    def qkv_grad_chain():
        normed_in = have["normed_in"].reshape(4 * token_rows, width)
        projected = have["grad_projected"].reshape(1, 4 * token_rows, -1)
        keep, give = weight_grad(meta(), shard_index, [([normed_in], [projected])], 0)
        clock.mark(keep)
        came = flip(give, 1)
        yield
        yield from line_reduce_steps(keep, came)
        own = have["line_sum"]
        came = flip(own, 2)
        yield
        pair = clock.mark(jnp.stack([own, now(came)]))
        came = flip(pair, 4)
        yield
        mine = clock.mark(jnp.concatenate([pair, now(came)]))
        other = flip(mine, 1)
        yield
        have["grad_qkv"] = clock.mark(place_heads(meta(), [mine[r] for r in range(4)], other))
        yield

    early = {
        "H": hidden_chain(),
        "W": qkv_chain(),
        "S": shared_chain(),
        "O": out_chain(),
        "K": small_chain(),
        "R": qkv_all_chain(),
        "M": main_chain(),
    }
    late = {
        "L": states_chain(),
        "S": shared_grad_chain(),
        "O": out_grad_chain(),
        "Q": qkv_grad_chain(),
    }
    if SUMMED:
        late["A"] = summed_chain()
    for expert in range(SUMMED, local_experts):
        late[str(expert)] = expert_chain(expert)
    for chains, order in ((early, EARLY), (late, LATE)):
        for name in order:
            next(chains[name], None)
        for name in chains:
            for _ in chains[name]:
                pass

    own, loss_value = have["sums"]
    return (
        have["final"],
        loss_value,
        have["grad_hidden"],
        own[0],
        have["grad_qkv"],
        have["grad_out"],
        own[1],
        have["grad_shared"],
        have["grad_experts"],
    )


def solution(mesh):
    in_specs = (
        P("wt", "ctx", None),
        P("wt", "ctx", None),
        P("wt", "ctx"),
        P("wt", "ctx", None),
        P("wt", "ctx", None),
        P("wt"),
        P("wt", None),
        P("wt", None),
        P("wt"),
        P("wt", None),
        P("wt", None, None),
    )
    out_specs = (
        P("wt", "ctx", None),
        P(),
        P("wt", "ctx", None),
        P("wt"),
        P("wt", None),
        P("wt", None),
        P("wt"),
        P("wt", None),
        P("wt", None, None),
    )
    plane_of_eight = dict(mesh.shape) == {"ctx": 8, "wt": 4}
    return jax.shard_map(
        fast_device if plane_of_eight else on_device, mesh=mesh, in_specs=in_specs, out_specs=out_specs, check_vma=False
    )
```

```python
import functools
import math

import jax
import jax.numpy as jnp
from jax import lax
from jax.experimental import pallas as pl
from jax.experimental.pallas import tpu as pltpu
from jax.sharding import PartitionSpec as P

QUERY_HEADS = 12
KEY_VALUE_HEADS = 4
HEAD_SIZE = 128
F = 512
SF = 1024
EXPERTS = 16
TOP = 6


norm_eps = 1e-05
masked_score = -1e30


def sigmoid_linear(values):
    return values * jax.nn.sigmoid(values)


def silu_slope(values):
    sigma_value = jax.nn.sigmoid(values)
    return sigma_value * (1.0 + values * (1.0 - sigma_value))


def normalize(values):
    inverse = lax.rsqrt(jnp.mean(values * values, axis=-1, keepdims=True) + norm_eps)
    return (values * inverse, inverse)


def norm_back(grad_normed, scaled, inverse, gain_vector):
    grad_scaled = grad_normed * gain_vector
    return inverse * (grad_scaled - scaled * jnp.mean(grad_scaled * scaled, axis=-1, keepdims=True))


def positions(row_ids, token_rows, context_count):
    piece_index = row_ids // token_rows
    within = row_ids % token_rows
    half_rows = token_rows // 2
    mirrored = jnp.where(within < half_rows, piece_index, 2 * context_count - 1 - piece_index)
    return mirrored * half_rows + within % half_rows


def route_tables(local_routes, local_gates, experts, capacity):
    token_rows = local_routes.shape[0]
    flat_routes = local_routes.reshape(-1)
    one_hot = (flat_routes[:, None] == jnp.arange(experts, dtype=jnp.int32)[None, :]).astype(
        jnp.int32
    )
    earlier = jnp.cumsum(one_hot, axis=0) - one_hot
    slot_index = jnp.sum(earlier * one_hot, axis=1)
    token_index = jnp.arange(flat_routes.shape[0], dtype=jnp.int32) // local_routes.shape[1]
    slot_table = (
        jnp.full((experts, capacity), token_rows, jnp.int32)
        .at[flat_routes, slot_index]
        .set(token_index)
    )
    slot_gate = (
        jnp.zeros((experts, capacity), jnp.float32)
        .at[flat_routes, slot_index]
        .set(local_gates.reshape(-1))
    )
    return (slot_table, slot_gate)


def block_scores(query_rows, key_block, key_position, query_place, score_scale):
    scores = (
        jnp.einsum("qhgd,khd->qhgk", query_rows, key_block, preferred_element_type=jnp.float32)
        * score_scale
    )
    allowed = key_position[None, None, None, :] <= query_place[:, None, None, None]
    return jnp.where(allowed, scores, masked_score)


def attend_forward(
    query_rows, blocked_keys, blocked_values, place_blocks, query_place, score_scale
):
    head_shape = query_rows.shape[:3]

    def online_step(running, block_args):
        running_max, running_sum, accumulated = running
        key_block, value_block, key_position = block_args
        scores = block_scores(query_rows, key_block, key_position, query_place, score_scale)
        new_max = jnp.maximum(running_max, jnp.max(scores, axis=-1))
        rescale = jnp.exp(running_max - new_max)
        powers = jnp.exp(scores - new_max[..., None])
        new_sum = running_sum * rescale + jnp.sum(powers, axis=-1)
        weighted = jnp.einsum(
            "qhgk,khd->qhgd",
            powers.astype(jnp.bfloat16),
            value_block,
            preferred_element_type=jnp.float32,
        )
        return ((new_max, new_sum, accumulated * rescale[..., None] + weighted), None)

    initial = (
        jnp.full(head_shape, masked_score, jnp.float32),
        jnp.zeros(head_shape, jnp.float32),
        jnp.zeros(query_rows.shape, jnp.float32),
    )
    row_max, row_sum, accumulated = lax.scan(
        online_step, initial, (blocked_keys, blocked_values, place_blocks)
    )[0]
    log_total = row_max + jnp.log(row_sum)
    return (accumulated / row_sum[..., None], log_total)


def attend_backward(
    query_rows,
    blocked_keys,
    blocked_values,
    place_blocks,
    query_place,
    log_total,
    attention_output_gradient,
    attention_output,
    score_scale,
):
    row_delta = jnp.sum(attention_output_gradient.astype(jnp.float32) * attention_output, axis=-1)

    def block_grads(grad_queries, block_args):
        key_block, value_block, key_position = block_args
        scores = block_scores(query_rows, key_block, key_position, query_place, score_scale)
        probabilities = jnp.exp(scores - log_total[..., None])
        grad_probs = jnp.einsum(
            "qhgd,khd->qhgk",
            attention_output_gradient,
            value_block,
            preferred_element_type=jnp.float32,
        )
        grad_scores = (probabilities * (grad_probs - row_delta[..., None])).astype(jnp.bfloat16)
        grad_queries = grad_queries + jnp.einsum(
            "qhgk,khd->qhgd", grad_scores, key_block, preferred_element_type=jnp.float32
        )
        grad_keys = (
            jnp.einsum(
                "qhgk,qhgd->khd", grad_scores, query_rows, preferred_element_type=jnp.float32
            )
            * score_scale
        )
        grad_values = jnp.einsum(
            "qhgk,qhgd->khd",
            probabilities.astype(jnp.bfloat16),
            attention_output_gradient,
            preferred_element_type=jnp.float32,
        )
        return (grad_queries, (grad_keys, grad_values))

    grad_queries, (grad_keys, grad_values) = lax.scan(
        block_grads,
        jnp.zeros(query_rows.shape, jnp.float32),
        (blocked_keys, blocked_values, place_blocks),
    )
    return (grad_queries * score_scale, grad_keys, grad_values)


def gate_up_grads(grad_act, gate_up, hidden_units):
    gate_part = gate_up[..., :hidden_units]
    up_part = gate_up[..., hidden_units:]
    return jnp.concatenate(
        [grad_act * up_part * silu_slope(gate_part), grad_act * sigmoid_linear(gate_part)], axis=-1
    ).astype(jnp.bfloat16)


def on_device(
    hidden,
    teacher,
    valid_mask,
    routes,
    route_gates,
    gain_in,
    query_key_value_weight,
    out_weight,
    gain_mid,
    shared_weight,
    expert_weight,
):
    token_rows = hidden.shape[1]
    model_width = hidden.shape[2]
    context_count = lax.axis_size("ctx")
    shard_count = lax.axis_size("wt")
    seq_rows = token_rows * context_count
    all_tokens = seq_rows * shard_count
    query_groups = QUERY_HEADS // KEY_VALUE_HEADS
    query_total_width = QUERY_HEADS * HEAD_SIZE
    key_value_width = KEY_VALUE_HEADS * HEAD_SIZE
    score_scale = 1.0 / math.sqrt(HEAD_SIZE)
    key_row_count = min(512, seq_rows)
    number_of_blocks = seq_rows // key_row_count
    capacity = token_rows * TOP // 12
    local_experts = expert_weight.shape[0]
    contract_last = (((1,), (1,)), ((), ()))
    contract_first = (((0,), (0,)), ((), ()))
    full_gain_in, full_qkv, full_out, full_gain_mid, full_shared = (
        lax.all_gather(gain_in, "wt", axis=0, tiled=True),
        lax.all_gather(query_key_value_weight, "wt", axis=0, tiled=True),
        lax.all_gather(out_weight, "wt", axis=0, tiled=True),
        lax.all_gather(gain_mid, "wt", axis=0, tiled=True),
        lax.all_gather(shared_weight, "wt", axis=0, tiled=True),
    )
    gain_in_float = full_gain_in.astype(jnp.float32)
    gain_mid_float = full_gain_mid.astype(jnp.float32)
    inputs = hidden[0].astype(jnp.float32)
    scaled_in, inverse_in = normalize(inputs)
    normed_in = (scaled_in * gain_in_float).astype(jnp.bfloat16)
    projected_rows = jnp.dot(normed_in, full_qkv, preferred_element_type=jnp.float32).astype(
        jnp.bfloat16
    )
    query_rows = projected_rows[:, :query_total_width].reshape(
        token_rows, KEY_VALUE_HEADS, query_groups, HEAD_SIZE
    )
    context_local = projected_rows[:, query_total_width:]
    context_gathered = lax.all_gather(context_local, "ctx", axis=0, tiled=True)
    context_index = lax.axis_index("ctx")
    query_place = positions(
        context_index * token_rows + jnp.arange(token_rows, dtype=jnp.int32),
        token_rows,
        context_count,
    )
    place_blocks = positions(
        jnp.arange(seq_rows, dtype=jnp.int32), token_rows, context_count
    ).reshape(number_of_blocks, key_row_count)
    blocked_keys = context_gathered[:, :key_value_width].reshape(
        number_of_blocks, key_row_count, KEY_VALUE_HEADS, HEAD_SIZE
    )
    blocked_values = context_gathered[:, key_value_width:].reshape(
        number_of_blocks, key_row_count, KEY_VALUE_HEADS, HEAD_SIZE
    )
    attention_output, log_total = attend_forward(
        query_rows, blocked_keys, blocked_values, place_blocks, query_place, score_scale
    )
    mixed_rows = attention_output.reshape(token_rows, query_total_width).astype(jnp.bfloat16)
    middle = inputs + jnp.dot(mixed_rows, full_out, preferred_element_type=jnp.float32)
    scaled_mid, inverse_mid = normalize(middle)
    normed_mid = (scaled_mid * gain_mid_float).astype(jnp.bfloat16)
    shared_gate_up = jnp.dot(
        normed_mid, full_shared[:, : 2 * SF], preferred_element_type=jnp.float32
    )
    shared_act = (sigmoid_linear(shared_gate_up[:, :SF]) * shared_gate_up[:, SF:]).astype(
        jnp.bfloat16
    )
    shared_out = lax.dot_general(
        shared_act, full_shared[:, 2 * SF :], contract_last, preferred_element_type=jnp.float32
    )
    slot_table, slot_gate = route_tables(routes[0], route_gates[0], EXPERTS, capacity)
    padded_rows = jnp.concatenate([normed_mid, jnp.zeros((1, model_width), jnp.bfloat16)], axis=0)
    expert_rows = jnp.take(padded_rows, slot_table, axis=0)
    arrived = lax.all_to_all(expert_rows, "wt", split_axis=0, concat_axis=0, tiled=True)
    slot_count = arrived.shape[1]
    grouped = arrived.reshape(shard_count, local_experts, slot_count, model_width)
    owner_gate_up = jnp.einsum(
        "wesd,edf->wesf", grouped, expert_weight[:, :, : 2 * F], preferred_element_type=jnp.float32
    )
    owner_act = (sigmoid_linear(owner_gate_up[..., :F]) * owner_gate_up[..., F:]).astype(
        jnp.bfloat16
    )
    owner_out = jnp.einsum(
        "wesf,edf->wesd",
        owner_act,
        expert_weight[:, :, 2 * F :],
        preferred_element_type=jnp.float32,
    ).astype(jnp.bfloat16)
    returned = lax.all_to_all(
        owner_out.reshape(shard_count * local_experts, slot_count, model_width),
        "wt",
        split_axis=0,
        concat_axis=0,
        tiled=True,
    )
    expert_out, owner_rows, owner_gate_up, owner_act = (
        returned,
        arrived,
        owner_gate_up.reshape(shard_count * local_experts, slot_count, 2 * F),
        owner_act.reshape(shard_count * local_experts, slot_count, F),
    )
    routed = (
        jnp.zeros((token_rows + 1, model_width), jnp.float32)
        .at[slot_table]
        .add(expert_out.astype(jnp.float32) * slot_gate[..., None])[:token_rows]
    )
    final_state = middle + shared_out + routed
    valid_float = valid_mask[0].astype(jnp.float32)
    deviation = final_state - teacher[0].astype(jnp.float32)
    squared_local = jnp.sum(valid_float[:, None] * deviation * deviation)
    count_local = jnp.sum(valid_float)
    squared_total, valid_count = lax.psum((squared_local, count_local), ("ctx", "wt"))
    loss_value = 0.5 * squared_total / (valid_count * model_width)
    grad_final = all_tokens / valid_count * valid_float[:, None] * deviation
    grad_shared_out = grad_final.astype(jnp.bfloat16)
    grad_shared_act = jnp.dot(
        grad_shared_out, full_shared[:, 2 * SF :], preferred_element_type=jnp.float32
    )
    grad_shared_down = lax.dot_general(
        grad_shared_out, shared_act, contract_first, preferred_element_type=jnp.float32
    )
    grad_shared_gate_up = gate_up_grads(grad_shared_act, shared_gate_up, SF)
    grad_normed_mid = lax.dot_general(
        grad_shared_gate_up,
        full_shared[:, : 2 * SF],
        contract_last,
        preferred_element_type=jnp.float32,
    )
    grad_shared_front = lax.dot_general(
        normed_mid, grad_shared_gate_up, contract_first, preferred_element_type=jnp.float32
    )
    grad_shared_full = jnp.concatenate([grad_shared_front, grad_shared_down], axis=1)
    padded_grads = jnp.concatenate([grad_final, jnp.zeros((1, model_width), jnp.float32)], axis=0)
    grad_expert_out = (jnp.take(padded_grads, slot_table, axis=0) * slot_gate[..., None]).astype(
        jnp.bfloat16
    )
    grad_arrived = lax.all_to_all(grad_expert_out, "wt", split_axis=0, concat_axis=0, tiled=True)
    grad_grouped = grad_arrived.reshape(shard_count, local_experts, capacity, model_width)
    owner_gate_up_grouped = owner_gate_up.reshape(shard_count, local_experts, capacity, 2 * F)
    owner_act_grouped = owner_act.reshape(shard_count, local_experts, capacity, F)
    owner_rows_grouped = owner_rows.reshape(shard_count, local_experts, capacity, model_width)
    grad_owner_act = jnp.einsum(
        "wecd,edf->wecf",
        grad_grouped,
        expert_weight[:, :, 2 * F :],
        preferred_element_type=jnp.float32,
    )
    grad_owner_gate_up = gate_up_grads(grad_owner_act, owner_gate_up_grouped, F)
    grad_owner_rows = jnp.einsum(
        "wecf,edf->wecd",
        grad_owner_gate_up,
        expert_weight[:, :, : 2 * F],
        preferred_element_type=jnp.float32,
    ).astype(jnp.bfloat16)
    front = jnp.einsum(
        "wecd,wecf->edf", owner_rows_grouped, grad_owner_gate_up, preferred_element_type=jnp.float32
    )
    back = jnp.einsum(
        "wecd,wecf->edf", grad_grouped, owner_act_grouped, preferred_element_type=jnp.float32
    )
    expert_grad = jnp.concatenate([front, back], axis=2)
    grad_rows = lax.all_to_all(
        grad_owner_rows.reshape(shard_count * local_experts, capacity, model_width),
        "wt",
        split_axis=0,
        concat_axis=0,
        tiled=True,
    )
    grad_normed_mid = (
        grad_normed_mid
        + jnp.zeros((token_rows + 1, model_width), jnp.float32)
        .at[slot_table]
        .add(grad_rows.astype(jnp.float32))[:token_rows]
    )
    grad_gain_mid_local = jnp.sum(grad_normed_mid * scaled_mid, axis=0)
    grad_middle = grad_final + norm_back(grad_normed_mid, scaled_mid, inverse_mid, gain_mid_float)
    grad_branch = grad_middle.astype(jnp.bfloat16)
    mixed_gradient = lax.dot_general(
        grad_branch, full_out, contract_last, preferred_element_type=jnp.float32
    ).astype(jnp.bfloat16)
    grad_out_local = lax.dot_general(
        mixed_rows, grad_branch, contract_first, preferred_element_type=jnp.float32
    )
    context_recomputed = lax.all_gather(context_local, "ctx", axis=0, tiled=True)
    backward_keys = context_recomputed[:, :key_value_width].reshape(
        number_of_blocks, key_row_count, KEY_VALUE_HEADS, HEAD_SIZE
    )
    backward_values = context_recomputed[:, key_value_width:].reshape(
        number_of_blocks, key_row_count, KEY_VALUE_HEADS, HEAD_SIZE
    )
    attention_output_gradient = mixed_gradient.reshape(
        token_rows, KEY_VALUE_HEADS, query_groups, HEAD_SIZE
    )
    grad_queries, grad_keys, grad_values = attend_backward(
        query_rows,
        backward_keys,
        backward_values,
        place_blocks,
        query_place,
        log_total,
        attention_output_gradient,
        attention_output,
        score_scale,
    )
    grad_context_all = jnp.concatenate(
        [
            grad_keys.reshape(seq_rows, key_value_width),
            grad_values.reshape(seq_rows, key_value_width),
        ],
        axis=1,
    )
    grad_context = lax.psum_scatter(
        grad_context_all.astype(jnp.bfloat16), "ctx", scatter_dimension=0, tiled=True
    ).astype(jnp.float32)
    grad_projected = jnp.concatenate(
        [grad_queries.reshape(token_rows, query_total_width), grad_context], axis=1
    ).astype(jnp.bfloat16)
    grad_normed_in = lax.dot_general(
        grad_projected, full_qkv, contract_last, preferred_element_type=jnp.float32
    )
    grad_qkv_local = lax.dot_general(
        normed_in, grad_projected, contract_first, preferred_element_type=jnp.float32
    )
    grad_gain_in_local = jnp.sum(grad_normed_in * scaled_in, axis=0)
    grad_inputs = grad_middle + norm_back(grad_normed_in, scaled_in, inverse_in, gain_in_float)
    weight_sums = (
        lax.psum_scatter(
            grad_gain_in_local.astype(jnp.bfloat16), "wt", scatter_dimension=0, tiled=True
        ).astype(jnp.float32),
        lax.psum_scatter(
            grad_qkv_local.astype(jnp.bfloat16), "wt", scatter_dimension=0, tiled=True
        ).astype(jnp.float32),
        lax.psum_scatter(
            grad_out_local.astype(jnp.bfloat16), "wt", scatter_dimension=0, tiled=True
        ).astype(jnp.float32),
        lax.psum_scatter(
            grad_gain_mid_local.astype(jnp.bfloat16), "wt", scatter_dimension=0, tiled=True
        ).astype(jnp.float32),
        lax.psum_scatter(
            grad_shared_full.astype(jnp.bfloat16), "wt", scatter_dimension=0, tiled=True
        ).astype(jnp.float32),
    )
    summed = (
        lax.psum(weight_sums[0].astype(jnp.bfloat16), "ctx").astype(jnp.float32),
        lax.psum(weight_sums[1].astype(jnp.bfloat16), "ctx").astype(jnp.float32),
        lax.psum(weight_sums[2].astype(jnp.bfloat16), "ctx").astype(jnp.float32),
        lax.psum(weight_sums[3].astype(jnp.bfloat16), "ctx").astype(jnp.float32),
        lax.psum(weight_sums[4].astype(jnp.bfloat16), "ctx").astype(jnp.float32),
        lax.psum(expert_grad.astype(jnp.bfloat16), "ctx").astype(jnp.float32),
    )
    return (
        final_state.astype(jnp.bfloat16)[None],
        loss_value,
        grad_inputs[None],
        summed[0],
        summed[1],
        summed[2],
        summed[3],
        summed[4],
        summed[5],
    )


PLANE = [[0, 2, 4, 6], [1, 3, 5, 7]]
COSTS = {
    "project": 0.3,
    "attend": 0.3,
    "leave": 0.3,
    "join_shared": 0.3,
    "experts": 0.3,
    "experts_back": 0.3,
    "enter_back": 0.3,
    "attend_back": 0.3,
    "finish": 0.3,
    "weight_grad": 0.3,
    "expert_grad": 0.3,
    "blend_split": 0.3,
    "blend_pair": 0.3,
    "blend_sum": 0.3,
    "blend_stack": 0.3,
    "blend_four": 0.3,
    "place_pair": 0.3,
    "place_shared": 0.3,
    "place_heads": 0.3,
}


def flip(value, bit):
    return lax.ppermute(value, "ctx", [(index, index ^ bit) for index in range(8)])


def line_swap(value, offset):
    return lax.ppermute(value, "wt", [(index, index ^ offset) for index in range(4)])


def line_middle(value):
    return lax.ppermute(value, "wt", [(1, 2), (2, 1)])


def line_outward(value):
    return lax.ppermute(value, "wt", [(1, 0), (2, 3)])


def line_inward(value):
    return lax.ppermute(value, "wt", [(0, 1), (3, 2)])


def line_gather(value, at_end):
    near = line_swap(value, 1)
    middle = line_middle(value)
    middle_far = line_middle(near)
    outward = line_outward(middle)
    outward_far = line_outward(middle_far)
    return [
        value,
        near,
        jnp.where(at_end, outward, middle_far),
        jnp.where(at_end, outward_far, middle),
    ]


def line_reduce(parts):
    far = line_inward(parts[3])
    carried = parts[2] + far
    inward = line_inward(carried)
    crossed = line_middle(carried)
    near = line_swap(parts[1] + crossed, 1)
    middle = line_middle(parts[3] + inward)
    return (
        parts[0].astype(jnp.float32) + near.astype(jnp.float32) + middle.astype(jnp.float32)
    )


def chips_exchange(blocks):
    return lax.all_to_all(
        blocks,
        "ctx",
        split_axis=0,
        concat_axis=0,
        tiled=True,
        axis_index_groups=PLANE,
    )


def line_exchange(blocks):
    return lax.all_to_all(blocks, "wt", split_axis=0, concat_axis=0, tiled=True)


def chips_gather(value, x_last):
    along_x = flip(value, 2)
    along_y = flip(value, 4)
    corner = flip(along_y, 2) if x_last else flip(along_x, 4)
    return [value, along_x, along_y, corner]


def core_swap(values):
    return [flip(value, 1) for value in values]


def everywhere_sum(value):
    for bit in (1, 2, 4):
        value = value + flip(value, bit)
    for offset in (1, 2):
        value = value + line_swap(value, offset)
    return value


def pick(blocks, index):
    return lax.dynamic_index_in_dim(blocks, index, 0, keepdims=False)


def chips_reduce(keep, came):
    half = keep.shape[1] // 2
    upper = keep[:, :half] + came[:, :half]
    lower = keep[:, half:] + came[:, half:]
    upper_came = flip(upper[1::2], 2)
    lower_came = flip(lower[2:], 4)
    upper = upper[0::2] + upper_came
    lower = lower[:2] + lower_came
    upper_came = flip(upper[1], 4)
    lower_came = flip(lower[1], 2)
    return jnp.concatenate([upper[0] + upper_came, lower[0] + lower_came], axis=0)


def dot_plain(left, right):
    return lax.dot_general(
        left, right, (((1,), (0,)), ((), ())), preferred_element_type=jnp.float32
    )


def dot_last(left, right):
    return lax.dot_general(
        left, right, (((1,), (1,)), ((), ())), preferred_element_type=jnp.float32
    )


def dot_first(left, right):
    return lax.dot_general(
        left, right, (((0,), (0,)), ((), ())), preferred_element_type=jnp.float32
    )


def call(kernel, name, meta, arrays, grid, in_specs, out_specs, out_shape, scratch, flops, moved):
    return pl.pallas_call(
        kernel,
        grid_spec=pltpu.PrefetchScalarGridSpec(
            num_scalar_prefetch=1,
            grid=grid,
            in_specs=in_specs,
            out_specs=out_specs,
            scratch_shapes=scratch,
        ),
        out_shape=out_shape,
        compiler_params=pltpu.CompilerParams(vmem_limit_bytes=48 * 1024 * 1024),
        cost_estimate=pl.CostEstimate(
            flops=int(COSTS.get(name, 1.0) * 1e9), bytes_accessed=1000, transcendentals=0
        ),
        name=name,
    )(meta, *arrays)


def whole(array):
    rank = len(array.shape)
    return pl.BlockSpec(tuple(array.shape), lambda *_: (0,) * rank)


def shape_of(shape, dtype):
    return jax.ShapeDtypeStruct(shape, dtype)


def size_of(arrays):
    return sum(math.prod(a.shape) * a.dtype.itemsize for a in arrays)


def blend(meta, name, function, arrays, pieces=4):
    rows = arrays[0].shape[-2]
    tile = rows // pieces
    outs = jax.eval_shape(function, *[shape_of(a.shape, a.dtype) for a in arrays])
    many = isinstance(outs, (list, tuple))
    outs = list(outs) if many else [outs]

    def spec(a):
        rank = len(a.shape)
        lead = a.shape[:-2]
        return pl.BlockSpec(
            tuple(lead) + (tile, a.shape[-1]),
            lambda i, m: (0,) * (rank - 2) + (i, 0),
        )

    def kernel(meta_ref, *refs):
        result = function(*[ref[...] for ref in refs[: len(arrays)]])
        result = list(result) if many else [result]
        for ref, value in zip(refs[len(arrays) :], result):
            ref[...] = value

    result = call(
        kernel,
        name,
        meta,
        arrays,
        (pieces,),
        [spec(a) for a in arrays],
        [spec(a) for a in outs],
        outs,
        [],
        0,
        0,
    )
    return result if many else result[0]


def aligned(value, step):
    return pl.multiple_of(value * step, step)


def project_kernel(meta, *refs):
    blocks, (gain_ref, mine, other) = refs[:4], refs[4:7]
    normed_ref, query_ref, pair_ref, weight_ref, held = refs[7:]
    step = pl.program_id(0)
    core = meta[0] & 1
    rows = mine.shape[1]

    @pl.when(step == 0)
    def _():
        for i in range(4):
            weight_ref[pl.ds(aligned(2 * i + core, rows), rows), :] = mine[i]
            weight_ref[pl.ds(aligned(2 * i + 1 - core, rows), rows), :] = other[i]

    for r in range(4):

        @pl.when(step == r)
        def _():
            held[...] = blocks[r][...]

    states = held[...].astype(jnp.float32)
    inverse = lax.rsqrt(jnp.mean(states * states, axis=-1, keepdims=True) + norm_eps)
    normed = (states * inverse * gain_ref[...]).astype(jnp.bfloat16)
    normed_ref[0] = normed
    projected = dot_plain(normed, weight_ref[...]).astype(jnp.bfloat16)
    query_width = query_ref.shape[-1]
    query_ref[0] = projected[:, :query_width]
    pair_ref[0] = projected[:, query_width:]


def project(meta, blocks, gain, mine, other, query_width):
    token_rows, width = blocks[0].shape
    columns = mine.shape[2]
    arrays = list(blocks) + [gain, mine, other]
    outs = [
        shape_of((4, token_rows, width), jnp.bfloat16),
        shape_of((4, token_rows, query_width), jnp.bfloat16),
        shape_of((4, token_rows, columns - query_width), jnp.bfloat16),
        shape_of((width, columns), jnp.bfloat16),
    ]

    def at_chip(r, m):
        return ((m[0] >> 1) ^ r, 0, 0)

    return call(
        project_kernel,
        "project",
        meta,
        arrays,
        (4,),
        [whole(a) for a in arrays],
        [
            pl.BlockSpec((1, token_rows, width), at_chip),
            pl.BlockSpec((1, token_rows, query_width), at_chip),
            pl.BlockSpec((1, token_rows, columns - query_width), at_chip),
            whole(outs[3]),
        ],
        outs,
        [pltpu.VMEM((token_rows, width), jnp.bfloat16)],
        2 * 4 * token_rows * width * columns,
        size_of(arrays) + size_of(outs),
    )


def sort_pairs(meta, mine_ref, other_ref, keys, values):
    half = mine_ref.shape[1] // 2
    for slot in range(16):
        block, part = (slot, 0) if slot < 8 else (15 - slot, 1)
        place = block >> 1
        rows = pl.ds(part * half, half)
        to = pl.ds(slot * half, half)

        @pl.when((meta[0] & 1) == (block & 1))
        def _():
            keys[to, :] = mine_ref[place, rows, :HEAD_SIZE]
            values[to, :] = mine_ref[place, rows, HEAD_SIZE:]

        @pl.when((meta[0] & 1) != (block & 1))
        def _():
            keys[to, :] = other_ref[place, rows, :HEAD_SIZE]
            values[to, :] = other_ref[place, rows, HEAD_SIZE:]


def stack_heads(rows):
    count = rows.shape[1] // HEAD_SIZE
    return jnp.concatenate(
        [rows[:, h * HEAD_SIZE : (h + 1) * HEAD_SIZE] for h in range(count)], axis=0
    )


def unstack_heads(rows, count):
    each = rows.shape[0] // count
    return jnp.concatenate([rows[h * each : (h + 1) * each] for h in range(count)], axis=1)


def step_slot(meta):
    step = pl.program_id(0)
    block = 2 * (step >> 1) + (meta[0] & 1)
    return jnp.where((step & 1) == 0, block, 15 - block)


def allowed_pairs(start, slot, shape, half):
    key_place = start + lax.broadcasted_iota(jnp.int32, shape, 0)
    query_place = slot * half + (lax.broadcasted_iota(jnp.int32, shape, 1) & (half - 1))
    return key_place <= query_place


def key_spans(step, half, span):
    pairs = (step // 2 if step % 2 == 0 else 7 - step // 2) + 1
    rows = pairs * 2 * half
    return [(at, min(span, rows - at)) for at in range(0, rows, span)]


def attend_kernel(scale, span, meta, query_ref, mine_ref, other_ref, *refs):
    out_ref, log_ref, keys, values, values_turned = refs
    half, group_width = query_ref.shape[1:]
    count = group_width // HEAD_SIZE

    @pl.when(pl.program_id(0) == 0)
    def _():
        sort_pairs(meta, mine_ref, other_ref, keys, values)
        values_turned[...] = values[...].T

    slot = step_slot(meta)
    query = stack_heads(query_ref[0])
    wide = count * half

    def run(spans):
        highest = jnp.full((1, wide), masked_score, jnp.float32)
        total = jnp.zeros((1, wide), jnp.float32)
        mixed = jnp.zeros((HEAD_SIZE, wide), jnp.float32)
        for start, size in spans:
            at = pl.ds(start, size)
            scores = dot_last(keys[at, :], query) * scale
            if start == spans[-1][0]:
                seen = allowed_pairs(start, slot, scores.shape, half)
                scores = jnp.where(seen, scores, masked_score)
            new = jnp.maximum(highest, jnp.max(scores, axis=0, keepdims=True))
            rescale = jnp.exp(highest - new)
            powers = jnp.exp(scores - new)
            total = total * rescale + jnp.sum(powers, axis=0, keepdims=True)
            mixed = mixed * rescale + dot_plain(
                values_turned[:, at], powers.astype(jnp.bfloat16)
            )
            highest = new
        log_ref[0] = highest + jnp.log(total)
        out_ref[0] = unstack_heads((mixed / total).T, count).astype(jnp.bfloat16)

    for step in range(8):

        @pl.when(pl.program_id(0) == step)
        def _():
            run(key_spans(step, half, span))


def attend(meta, query, mine, other, scale):
    token_rows, group_width = query.shape[1:]
    half = token_rows // 2
    count = group_width // HEAD_SIZE
    everything = 8 * token_rows
    span = 1024
    arrays = [query, mine, other]
    outs = [
        shape_of(query.shape, jnp.bfloat16),
        shape_of((8, 1, count * half), jnp.float32),
    ]
    return call(
        functools.partial(attend_kernel, scale, span),
        "attend",
        meta,
        arrays,
        (8,),
        [
            pl.BlockSpec((1, half, group_width), lambda i, m: (i // 2, i % 2, 0)),
            whole(mine),
            whole(other),
        ],
        [
            pl.BlockSpec((1, half, group_width), lambda i, m: (i // 2, i % 2, 0)),
            pl.BlockSpec((1, 1, count * half), lambda i, m: (i, 0, 0)),
        ],
        outs,
        [
            pltpu.VMEM((everything, HEAD_SIZE), jnp.bfloat16),
            pltpu.VMEM((everything, HEAD_SIZE), jnp.bfloat16),
            pltpu.VMEM((HEAD_SIZE, everything), jnp.bfloat16),
        ],
        2 * 2 * 4 * token_rows * everything * group_width,
        size_of(arrays) + size_of(outs),
    )


def attend_back_kernel(scale, span, meta, query_ref, mine_ref, other_ref, log_ref, *refs):
    mixed_ref, grad_ref, grad_query_ref, grad_mine_ref, grad_other_ref = refs[:5]
    keys, values, keys_turned, grad_keys, grad_values = refs[5:]
    step = pl.program_id(0)
    half, group_width = query_ref.shape[1:]
    count = group_width // HEAD_SIZE

    @pl.when(step == 0)
    def _():
        sort_pairs(meta, mine_ref, other_ref, keys, values)
        keys_turned[...] = keys[...].T
        grad_keys[...] = jnp.zeros_like(grad_keys)
        grad_values[...] = jnp.zeros_like(grad_values)

    slot = step_slot(meta)
    query = stack_heads(query_ref[0])
    mixed = stack_heads(mixed_ref[0]).astype(jnp.float32)
    grad = stack_heads(grad_ref[0])
    delta = jnp.sum((mixed * grad.astype(jnp.float32)).T, axis=0, keepdims=True)
    log_total = log_ref[0]

    def run(spans):
        grad_turned = jnp.zeros((HEAD_SIZE, count * half), jnp.float32)
        for start, size in spans:
            at = pl.ds(start, size)
            scores = dot_last(keys[at, :], query) * scale
            probs = jnp.exp(scores - log_total)
            if start == spans[-1][0]:
                probs = jnp.where(allowed_pairs(start, slot, probs.shape, half), probs, 0.0)
            grad_probs = dot_last(values[at, :], grad)
            grad_scores = (probs * (grad_probs - delta)).astype(jnp.bfloat16)
            grad_values[at, :] += dot_plain(probs.astype(jnp.bfloat16), grad)
            grad_keys[at, :] += dot_plain(grad_scores, query)
            grad_turned += dot_plain(keys_turned[:, at], grad_scores)
        grad_query_ref[0] = unstack_heads((grad_turned * scale).T, count).astype(jnp.bfloat16)

    for at_step in range(8):

        @pl.when(step == at_step)
        def _():
            run(key_spans(at_step, half, span))

    @pl.when(step == 7)
    def _():
        for slot_at in range(16):
            block, part = (slot_at, 0) if slot_at < 8 else (15 - slot_at, 1)
            place = block >> 1
            rows = pl.ds(part * half, half)
            here = pl.ds(slot_at * half, half)
            both = jnp.concatenate([grad_keys[here, :] * scale, grad_values[here, :]], axis=1)

            @pl.when((meta[0] & 1) == (block & 1))
            def _():
                grad_mine_ref[place, rows, :] = both

            @pl.when((meta[0] & 1) != (block & 1))
            def _():
                grad_other_ref[place, rows, :] = both.astype(jnp.bfloat16)


def attend_back(meta, query, mine, other, log_total, mixed, grad, scale):
    token_rows, group_width = query.shape[1:]
    half = token_rows // 2
    count = group_width // HEAD_SIZE
    everything = 8 * token_rows
    span = 512
    arrays = [query, mine, other, log_total, mixed, grad]
    outs = [
        shape_of(query.shape, jnp.bfloat16),
        shape_of(mine.shape, jnp.float32),
        shape_of(mine.shape, jnp.bfloat16),
    ]
    return call(
        functools.partial(attend_back_kernel, scale, span),
        "attend_back",
        meta,
        arrays,
        (8,),
        [
            pl.BlockSpec((1, half, group_width), lambda i, m: (i // 2, i % 2, 0)),
            whole(mine),
            whole(other),
            pl.BlockSpec((1, 1, count * half), lambda i, m: (i, 0, 0)),
            pl.BlockSpec((1, half, group_width), lambda i, m: (i // 2, i % 2, 0)),
            pl.BlockSpec((1, half, group_width), lambda i, m: (i // 2, i % 2, 0)),
        ],
        [
            pl.BlockSpec((1, half, group_width), lambda i, m: (i // 2, i % 2, 0)),
            whole(outs[1]),
            whole(outs[2]),
        ],
        outs,
        [
            pltpu.VMEM((everything, HEAD_SIZE), jnp.bfloat16),
            pltpu.VMEM((everything, HEAD_SIZE), jnp.bfloat16),
            pltpu.VMEM((HEAD_SIZE, everything), jnp.bfloat16),
            pltpu.VMEM((everything, HEAD_SIZE), jnp.float32),
            pltpu.VMEM((everything, HEAD_SIZE), jnp.float32),
        ],
        5 * 2 * 4 * token_rows * everything * group_width,
        size_of(arrays) + size_of(outs),
    )


def leave_kernel(meta, *refs):
    parts, mine, other, states_ref, gain_ref = refs[:4], *refs[4:8]
    weight_ref, middle_ref, normed_ref = refs[8:]
    core, chip = meta[0] & 1, meta[0] >> 1
    rows = mine.shape[1]
    for i in range(4):
        weight_ref[pl.ds(aligned(2 * i + core, rows), rows), :] = mine[i]
        weight_ref[pl.ds(aligned(2 * i + 1 - core, rows), rows), :] = other[i]
    middle = states_ref[...].astype(jnp.float32)
    for r in range(4):
        at = pl.ds(aligned(chip ^ r, 2 * rows), 2 * rows)
        middle += dot_plain(parts[r][...], weight_ref[at, :])
    middle_ref[...] = middle
    inverse = lax.rsqrt(jnp.mean(middle * middle, axis=-1, keepdims=True) + norm_eps)
    normed_ref[...] = (middle * inverse * gain_ref[...]).astype(jnp.bfloat16)


def leave(meta, parts, mine, other, states, gain):
    token_rows, width = states.shape
    arrays = list(parts) + [mine, other, states, gain]
    outs = [
        shape_of((8 * mine.shape[1], width), jnp.bfloat16),
        shape_of((token_rows, width), jnp.float32),
        shape_of((token_rows, width), jnp.bfloat16),
    ]
    return call(
        leave_kernel,
        "leave",
        meta,
        arrays,
        (1,),
        [whole(a) for a in arrays],
        [whole(a) for a in outs],
        outs,
        [],
        2 * token_rows * width * width,
        size_of(arrays) + size_of(outs),
    )


def norm_back_rows(grad_normed, states, gain):
    inverse = lax.rsqrt(jnp.mean(states * states, axis=-1, keepdims=True) + norm_eps)
    scaled = states * inverse
    gain_grad = jnp.sum(grad_normed * scaled, axis=0, keepdims=True)
    grad_scaled = grad_normed * gain
    shift = jnp.mean(grad_scaled * scaled, axis=-1, keepdims=True)
    return inverse * (grad_scaled - scaled * shift), gain_grad


def enter_back_kernel(meta, final_ref, normed_ref, middle_ref, gain_ref, weight_ref, *refs):
    grad_ref, branch_ref, gain_grad_ref, mixed_ref = refs
    grad, gain_grad = norm_back_rows(normed_ref[...], middle_ref[...], gain_ref[...])
    grad = grad + final_ref[...]
    grad_ref[...] = grad
    gain_grad_ref[...] = gain_grad
    branch = grad.astype(jnp.bfloat16)
    branch_ref[...] = branch
    rows = weight_ref.shape[0] // 4
    for r in range(4):
        mixed_ref[r] = dot_last(branch, weight_ref[rows * r : rows * (r + 1), :]).astype(
            jnp.bfloat16
        )


def enter_back(meta, grad_final, grad_normed, middle, gain, weight):
    token_rows, width = middle.shape
    arrays = [grad_final, grad_normed, middle, gain, weight]
    outs = [
        shape_of((token_rows, width), jnp.float32),
        shape_of((token_rows, width), jnp.bfloat16),
        shape_of((1, width), jnp.float32),
        shape_of((4, token_rows, weight.shape[0] // 4), jnp.bfloat16),
    ]
    return call(
        enter_back_kernel,
        "enter_back",
        meta,
        arrays,
        (1,),
        [whole(a) for a in arrays],
        [whole(a) for a in outs],
        outs,
        [],
        2 * token_rows * width * width,
        size_of(arrays) + size_of(outs),
    )


def finish_kernel(meta, *refs):
    parts, mine, other = refs[:3]
    states_ref, middle_ref, gain_ref, grad_ref, gain_grad_ref, total = refs[3:]
    core, chip = meta[0] & 1, meta[0] >> 1
    columns = mine.shape[1]
    for at, weights in ((core, mine), (1 - core, other)):
        total[:, pl.ds(aligned(at, columns), columns)] = sum(
            dot_last(parts[r], weights[chip ^ r]) for r in range(4)
        )
    grad, gain_grad = norm_back_rows(
        total[...], states_ref[...].astype(jnp.float32), gain_ref[...]
    )
    grad_ref[0] = grad + middle_ref[...]
    gain_grad_ref[...] = gain_grad


def finish(meta, parts, mine, other, states, grad_middle, gain):
    token_rows, width = states.shape
    arrays = [parts, mine, other, states, grad_middle, gain]
    outs = [
        shape_of((1, token_rows, width), jnp.float32),
        shape_of((1, width), jnp.float32),
    ]
    return call(
        finish_kernel,
        "finish",
        meta,
        arrays,
        (1,),
        [whole(a) for a in arrays],
        [whole(a) for a in outs],
        outs,
        [pltpu.VMEM((token_rows, width), jnp.float32)],
        2 * token_rows * width * 4 * parts.shape[2],
        size_of(arrays) + size_of(outs),
    )


def gated(gate_up, units):
    gate_part = gate_up[:, :units]
    sigma = 1.0 / (1.0 + jnp.exp(-gate_part))
    return gate_part * sigma * gate_up[:, units:]


def gated_back(grad_act, gate_up, units):
    gate_part = gate_up[:, :units].astype(jnp.float32)
    up_part = gate_up[:, units:].astype(jnp.float32)
    sigma = 1.0 / (1.0 + jnp.exp(-gate_part))
    linear = gate_part * sigma
    grad_gate = grad_act * up_part * (sigma * (1.0 + gate_part * (1.0 - sigma)))
    return grad_gate, grad_act * linear, linear * up_part


def experts_kernel(
    meta, rows_ref, gates_ref, expert_ref, shared_ref, gate_up_ref, shared_gate_up_ref, out_ref, total
):
    expert = pl.program_id(0)
    rows = rows_ref[...]

    @pl.when(expert == 0)
    def _():
        units = shared_ref.shape[1] // 3
        gate_up = dot_plain(rows, shared_ref[:, : 2 * units])
        shared_gate_up_ref[...] = gate_up.astype(jnp.bfloat16)
        act = gated(gate_up, units).astype(jnp.bfloat16)
        total[...] = dot_last(act, shared_ref[:, 2 * units :])

    gate_up = dot_plain(rows, expert_ref[0, :, : 2 * F])
    gate_up_ref[0] = gate_up.astype(jnp.bfloat16)
    act = (gated(gate_up, F) * gates_ref[0]).astype(jnp.bfloat16)
    total[...] += dot_last(act, expert_ref[0, :, 2 * F :])

    @pl.when(expert == pl.num_programs(0) - 1)
    def _():
        out_ref[...] = total[...].astype(jnp.bfloat16)


def experts(meta, rows, gates, expert_weight, shared_slice):
    local_experts, width, _ = expert_weight.shape
    token_rows = rows.shape[0]
    shared_units = shared_slice.shape[1] // 3
    arrays = [rows, gates, expert_weight, shared_slice]
    outs = [
        shape_of((local_experts, token_rows, 2 * F), jnp.bfloat16),
        shape_of((token_rows, 2 * shared_units), jnp.bfloat16),
        shape_of((token_rows, width), jnp.bfloat16),
    ]
    return call(
        experts_kernel,
        "experts",
        meta,
        arrays,
        (local_experts,),
        [
            whole(rows),
            pl.BlockSpec((1, token_rows, 1), lambda e, m: (e, 0, 0)),
            pl.BlockSpec((1, width, 3 * F), lambda e, m: (e, 0, 0)),
            whole(shared_slice),
        ],
        [
            pl.BlockSpec((1, token_rows, 2 * F), lambda e, m: (e, 0, 0)),
            whole(outs[1]),
            whole(outs[2]),
        ],
        outs,
        [pltpu.VMEM((token_rows, width), jnp.float32)],
        2 * token_rows * width * 3 * (F * local_experts + shared_units),
        size_of(arrays) + size_of(outs),
    )


def experts_back_kernel(
    meta,
    grad_ref,
    gates_ref,
    gate_up_ref,
    shared_gate_up_ref,
    expert_ref,
    shared_ref,
    grad_gate_up_ref,
    act_ref,
    shared_grad_ref,
    shared_act_ref,
    grad_rows_ref,
    total,
):
    expert = pl.program_id(0)
    grad = grad_ref[...]

    @pl.when(expert == 0)
    def _():
        units = shared_ref.shape[1] // 3
        grad_act = dot_plain(grad, shared_ref[:, 2 * units :])
        grad_gate, grad_up, act = gated_back(grad_act, shared_gate_up_ref[...], units)
        both = jnp.concatenate([grad_gate, grad_up], axis=1).astype(jnp.bfloat16)
        shared_grad_ref[0] = both
        shared_act_ref[0] = act.astype(jnp.bfloat16)
        total[...] = dot_last(both, shared_ref[:, : 2 * units])

    grad_act = dot_plain(grad, expert_ref[0, :, 2 * F :]) * gates_ref[0]
    grad_gate, grad_up, act = gated_back(grad_act, gate_up_ref[0], F)
    both = jnp.concatenate([grad_gate, grad_up], axis=1).astype(jnp.bfloat16)
    grad_gate_up_ref[0] = both
    act_ref[0] = (act * gates_ref[0]).astype(jnp.bfloat16)
    total[...] += dot_last(both, expert_ref[0, :, : 2 * F])

    @pl.when(expert == pl.num_programs(0) - 1)
    def _():
        grad_rows_ref[...] = total[...].astype(jnp.bfloat16)


def experts_back(meta, grad, gates, gate_up, shared_gate_up, expert_weight, shared_slice):
    local_experts, width, _ = expert_weight.shape
    token_rows = grad.shape[0]
    shared_units = shared_slice.shape[1] // 3
    arrays = [grad, gates, gate_up, shared_gate_up, expert_weight, shared_slice]
    outs = [
        shape_of((local_experts, token_rows, 2 * F), jnp.bfloat16),
        shape_of((local_experts, token_rows, F), jnp.bfloat16),
        shape_of((1, token_rows, 2 * shared_units), jnp.bfloat16),
        shape_of((1, token_rows, shared_units), jnp.bfloat16),
        shape_of((token_rows, width), jnp.bfloat16),
    ]
    return call(
        experts_back_kernel,
        "experts_back",
        meta,
        arrays,
        (local_experts,),
        [
            whole(grad),
            pl.BlockSpec((1, token_rows, 1), lambda e, m: (e, 0, 0)),
            pl.BlockSpec((1, token_rows, 2 * F), lambda e, m: (e, 0, 0)),
            whole(shared_gate_up),
            pl.BlockSpec((1, width, 3 * F), lambda e, m: (e, 0, 0)),
            whole(shared_slice),
        ],
        [
            pl.BlockSpec((1, token_rows, 2 * F), lambda e, m: (e, 0, 0)),
            pl.BlockSpec((1, token_rows, F), lambda e, m: (e, 0, 0)),
            whole(outs[2]),
            whole(outs[3]),
            whole(outs[4]),
        ],
        outs,
        [pltpu.VMEM((token_rows, width), jnp.float32)],
        2 * token_rows * width * 3 * (F * local_experts + shared_units),
        size_of(arrays) + size_of(outs),
    )


def weight_grad_kernel(pairs, core_at, meta, *refs):
    keep_ref, give_ref = refs[-2:]
    at = 0
    columns = 0
    parts = []
    for count in pairs:
        lefts, rights = refs[at : at + count], refs[at + count : at + 2 * count]
        at += 2 * count
        parts.append(
            sum(dot_first(a[...], b[0]) for a, b in zip(lefts, rights)).astype(jnp.bfloat16)
        )
    half = keep_ref.shape[1]

    for core, (first, second) in ((0, (keep_ref, give_ref)), (1, (give_ref, keep_ref))):

        @pl.when((meta[core_at] & 1) == core)
        def _():
            start = 0
            for part in parts:
                stop = start + part.shape[1]
                first[0, :, start:stop] = part[:half]
                second[0, :, start:stop] = part[half:]
                start = stop


def expert_grad_kernel(count, meta, *refs):
    rows, grads, front, acts = (refs[i * count : (i + 1) * count] for i in range(4))
    out_ref = refs[-1] if len(refs) == 4 * count + 1 else refs[-2]
    tile = rows[0].shape[1]
    both = 3 * F

    def pair(front_refs, act_refs):
        return [
            sum(dot_first(a[...], b[0]) for a, b in zip(left, right)).astype(jnp.bfloat16)
            for left, right in ((rows, front_refs), (grads, act_refs))
        ]

    left, right = pair(front, acts)
    out_ref[0, :tile, : left.shape[1]] = left
    out_ref[0, :tile, left.shape[1] : both] = right
    if len(refs) > 4 * count + 1:
        held = refs[-1]
        left, right = pair(refs[4 * count : 5 * count], refs[5 * count : 6 * count])
        split, columns = left.shape[1], left.shape[1] + right.shape[1]
        held[:, :split] = left
        held[:, split:] = right
        quarter = tile // 4
        first = 2 * meta[2]
        out_ref[0, tile:, :columns] = held[pl.ds(aligned(first, quarter), quarter), :]
        out_ref[0, tile:, columns:] = held[pl.ds(aligned(first + 1, quarter), quarter), :]


def expert_grad(meta, expert, half, rows, grads, front, acts, shared=None):
    count = len(rows)
    token_rows, width = rows[0].shape
    tile = width // 4
    arrays = list(rows) + list(grads) + list(front) + list(acts)
    column = pl.BlockSpec((token_rows, tile), lambda i, m: (0, i ^ m[0]))

    def of_expert(a):
        return pl.BlockSpec((1,) + a.shape[1:], lambda i, m: (m[1], 0, 0))

    in_specs = [column] * (2 * count) + [of_expert(a) for a in arrays[2 * count :]]
    below, scratch = 0, []
    if shared is not None:
        arrays += list(shared[0]) + list(shared[1])
        in_specs += [whole(a) for a in arrays[4 * count :]]
        below = tile // 4
        columns = shared[0][0].shape[-1] + shared[1][0].shape[-1]
        scratch = [pltpu.VMEM((tile, columns), jnp.bfloat16)]
    return call(
        functools.partial(expert_grad_kernel, count),
        "expert_grad",
        jnp.stack([meta[0] >> 1, expert, half]),
        arrays,
        (4,),
        in_specs,
        pl.BlockSpec((1, tile + below, 3 * F), lambda i, m: (i, 0, 0)),
        shape_of((4, tile + below, 3 * F), jnp.bfloat16),
        scratch,
        0,
        0,
    )


def weight_grad(meta, order, operands, index):
    token_rows, width = operands[0][0][0].shape
    tile = width // 4
    scalars = jnp.stack([order, meta[0]])
    arrays, in_specs, columns = [], [], 0
    for lefts, rights in operands:
        arrays += list(lefts) + list(rights)
        in_specs += [pl.BlockSpec((token_rows, tile), lambda i, m: (0, i ^ m[0]))] * len(lefts)
        units = rights[0].shape[-1]
        at = index if rights[0].shape[0] > 1 else 0
        in_specs += [
            pl.BlockSpec((1, token_rows, units), lambda i, m, at=at: (at, 0, 0))
        ] * len(rights)
        columns += units
    tokens = token_rows * len(operands[0][0])
    counts = [len(left) for left, _ in operands]
    outs = [shape_of((4, tile // 2, columns), jnp.bfloat16)] * 2
    return call(
        functools.partial(weight_grad_kernel, counts, 1),
        "weight_grad",
        scalars,
        arrays,
        (4,),
        in_specs,
        [pl.BlockSpec((1, tile // 2, columns), lambda i, m: (i, 0, 0))] * 2,
        outs,
        [],
        2 * tokens * width * columns,
        size_of(outs) + 4 * tokens * width + 2 * tokens * columns,
    )


def place_pair_kernel(meta, *refs):
    mine, other, out_ref = refs[-3:]
    rows = out_ref.shape[1]

    @pl.when(pl.program_id(0) == 0)
    def _():
        out_ref[0] = mine[0, :rows].astype(jnp.float32)

    @pl.when(pl.program_id(0) == 1)
    def _():
        out_ref[0] = other[0, :rows].astype(jnp.float32)


def place_pair(meta, total, index, shape, mine, other):
    _, rows, columns = mine.shape
    arrays = [mine, other]
    in_specs = [
        pl.BlockSpec((1, rows, columns), lambda k, r, m: ((1 - k) * r + 3 * k, 0, 0)),
        pl.BlockSpec((1, rows, columns), lambda k, r, m: (k * r, 0, 0)),
    ]
    aliases = {}
    if total is not None:
        arrays = [total] + arrays
        in_specs = [pl.BlockSpec(memory_space=pl.ANY)] + in_specs
        aliases = {1: 0}
    return pl.pallas_call(
        place_pair_kernel,
        grid_spec=pltpu.PrefetchScalarGridSpec(
            num_scalar_prefetch=1,
            grid=(2, 4),
            in_specs=in_specs,
            out_specs=pl.BlockSpec(
                (1, shape[1] // 4, shape[2]),
                lambda k, r, m: (2 * ((m[0] & 1) ^ k) + index, (m[0] >> 1) ^ r, 0),
            ),
        ),
        out_shape=shape_of(shape, jnp.float32),
        input_output_aliases=aliases,
        compiler_params=pltpu.CompilerParams(vmem_limit_bytes=48 * 1024 * 1024),
        cost_estimate=pl.CostEstimate(
            flops=int(COSTS.get("place_pair", 1.0) * 1e9), bytes_accessed=1000, transcendentals=0
        ),
        name="place_pair",
    )(meta, *arrays)


def place_shared_kernel(meta, mine_low, mine_high, other_low, other_high, out_ref):
    core = meta[0] & 1
    rows = mine_low.shape[1]
    for at, low, high in ((core, mine_low, mine_high), (1 - core, other_low, other_high)):
        out_ref[pl.ds(aligned(2 * at, rows), rows), :] = low[0].astype(jnp.float32)
        out_ref[pl.ds(aligned(2 * at + 1, rows), rows), :] = high[0].astype(jnp.float32)


def place_shared(meta, mine, other):
    _, rows, columns = mine.shape
    units = columns // 6
    low = pl.BlockSpec((1, rows, units), lambda i, j, m: (i, 0, j))
    high = pl.BlockSpec((1, rows, units), lambda i, j, m: (i, 0, 3 + j))
    outs = shape_of((4 * rows, 2 * columns), jnp.float32)
    return call(
        place_shared_kernel,
        "place_shared",
        meta,
        [mine, mine, other, other],
        (4, 3),
        [low, high, low, high],
        pl.BlockSpec((4 * rows, units), lambda i, j, m: (0, 4 * j + (m[1] ^ i))),
        outs,
        [],
        0,
        0,
    )


def place_heads_kernel(meta, *refs):
    mine, other, out_ref = refs[:4], refs[4], refs[5]
    core, chip = meta[0] & 1, meta[0] >> 1
    rows, columns = mine[0].shape
    group_width = columns - 2 * HEAD_SIZE
    for r in range(4):
        head = chip ^ r
        for at, pieces in ((core, [piece[...] for piece in mine]), (1 - core, other)):
            to = pl.ds(aligned(at, rows), rows)
            values = pieces[r].astype(jnp.float32)
            out_ref[to, pl.ds(aligned(head, group_width), group_width)] = values[:, :group_width]
            out_ref[to, pl.ds(aligned(4 * group_width // HEAD_SIZE + head, HEAD_SIZE), HEAD_SIZE)] = (
                values[:, group_width : group_width + HEAD_SIZE]
            )
            out_ref[
                to, pl.ds(aligned(4 * group_width // HEAD_SIZE + 4 + head, HEAD_SIZE), HEAD_SIZE)
            ] = values[:, group_width + HEAD_SIZE :]


def place_heads(meta, mine, other):
    rows, columns = mine[0].shape
    arrays = list(mine) + [other]
    outs = shape_of((2 * rows, 4 * columns), jnp.float32)
    return call(
        place_heads_kernel,
        "place_heads",
        meta,
        arrays,
        (1,),
        [whole(a) for a in arrays],
        whole(outs),
        outs,
        [],
        0,
        size_of(arrays + [outs]),
    )


def join_shared_kernel(meta, mine, other, out_ref):
    step = pl.program_id(0)
    rows = mine.shape[2]
    first = meta[0] ^ (2 * step)
    for i in range(4):
        at = 8 * (meta[1] ^ i)
        out_ref[pl.ds(aligned(at + first, rows), rows), :] = mine[0, i]
        out_ref[pl.ds(aligned(at + (first ^ 1), rows), rows), :] = other[0, i]


def join_shared(meta, mine, other):
    _, _, rows, columns = mine.shape
    block = pl.BlockSpec((1, 4, rows, columns), lambda r, m: (r, 0, 0, 0))
    outs = shape_of((32 * rows, columns), jnp.bfloat16)
    return call(
        join_shared_kernel,
        "join_shared",
        meta,
        [mine, other],
        (4,),
        [block, block],
        whole(outs),
        outs,
        [],
        0,
        size_of([mine, other, outs]),
    )


class Clock:
    def __init__(self):
        self.last = None

    def __call__(self, *values):
        last = () if self.last is None else (self.last,)
        held = lax.optimization_barrier(tuple(values) + last)[: len(values)]
        return held if len(held) > 1 else held[0]

    def mark(self, value):
        self.last = value
        return value


EARLY = (
    "H", "W", "K", "S", "K", "S", "W", "K", "O", "S", "S", "M", "M", "S", "O", "M", "S", "M", "R", "M", "K", "M", "K", "M",
    "K", "R", "M", "K", "M", "M", "M", "M", "R", "M", "M",
)
LATE = (
    "L", "0", "0", "1", "0", "L", "1", "1", "L", "L", "0", "1", "L", "O", "L", "1", "0", "O", "Q", "1", "O", "L", "Q", "0",
    "O", "L", "Q", "Q", "O", "Q", "1", "0", "S", "L", "O", "Q", "1", "0", "O", "Q", "S", "L", "O", "Q", "S", "L", "L",
)


def fast_device(
    hidden,
    teacher,
    valid_mask,
    routes,
    route_gates,
    gain_in,
    query_key_value_weight,
    out_weight,
    gain_mid,
    shared_weight,
    expert_weight,
):
    token_rows, width = hidden.shape[1:]
    context_count, shard_count = 8, 4
    context_index = lax.axis_index("ctx").astype(jnp.int32)
    shard_index = lax.axis_index("wt").astype(jnp.int32)
    plain_meta = jnp.stack([context_index, shard_index])
    core = context_index & 1
    chip = context_index >> 1
    at_end = (shard_index == 0) | (shard_index == shard_count - 1)
    group_width = QUERY_HEADS // KEY_VALUE_HEADS * HEAD_SIZE
    query_width = QUERY_HEADS * HEAD_SIZE
    kv_width = KEY_VALUE_HEADS * HEAD_SIZE
    scale = 1.0 / math.sqrt(HEAD_SIZE)
    all_tokens = token_rows * context_count * shard_count
    shard_rows = query_key_value_weight.shape[0]
    half_rows = shard_rows // 2
    local_experts = expert_weight.shape[0]
    bf16, f32 = jnp.bfloat16, jnp.float32
    states = hidden[0]
    clock = Clock()
    have = {}

    def meta():
        return clock(plain_meta)

    def now(*values):
        return clock(*values)

    def ready(*values):
        values = clock(*values)
        clock.mark(values[0] if isinstance(values, tuple) or isinstance(values, list) else values)
        return values


    def hidden_chain():
        own = ready(states)
        have["blocks"] = [own] + [flip(own, 2 * r) for r in (1, 2, 3)]
        yield

    def qkv_chain():
        rows = lax.dynamic_slice_in_dim(query_key_value_weight, core * half_rows, half_rows, 0)
        half = jnp.concatenate(
            [
                lax.dynamic_slice_in_dim(rows, chip * group_width, group_width, 1),
                lax.dynamic_slice_in_dim(rows, query_width + chip * HEAD_SIZE, HEAD_SIZE, 1),
                lax.dynamic_slice_in_dim(
                    rows, query_width + kv_width + chip * HEAD_SIZE, HEAD_SIZE, 1
                ),
            ],
            axis=1,
        )
        came = line_exchange(ready(jnp.broadcast_to(half, (4,) + half.shape)))
        yield
        have["qkv_mine"] = clock.mark(now(came))
        have["qkv_other"] = flip(have["qkv_mine"], 1)
        yield

    def small_chain():
        expert_ids = jnp.arange(EXPERTS, dtype=jnp.int32)
        matrix = jnp.sum(
            jnp.where(
                routes[0][None, :, :] == expert_ids[:, None, None], route_gates[0][None, :, :], 0.0
            ),
            axis=-1,
        )
        have["valid"] = valid_mask[0].astype(f32)
        gains = jnp.concatenate([gain_in, gain_mid]).astype(f32).reshape(-1, token_rows)
        gain_rows = gains.shape[0]
        filled = EXPERTS + gain_rows
        pack = jnp.concatenate(
            [
                matrix,
                gains,
                jnp.full((32 - filled, token_rows), jnp.sum(have["valid"]), f32),
            ]
        )
        came = line_swap(pack, 1)
        yield
        pair = clock.mark(jnp.stack([pack, now(came)]))
        came = line_swap(pair, 2)
        yield
        all_packs = clock.mark(jnp.concatenate([pair, now(came)]))
        have["gates"] = [
            lax.dynamic_slice_in_dim(
                all_packs[i], shard_index * local_experts, local_experts, 0
            )[..., None]
            for i in range(4)
        ]
        gains = all_packs[:, EXPERTS:filled].reshape(4, 2, shard_rows)
        gains = jnp.stack([pick(gains, shard_index ^ i) for i in range(4)], axis=1)
        have["gains"] = gains.reshape(2, 1, width)
        total = jnp.broadcast_to(jnp.sum(all_packs[:, filled, 0]), (8, 128))
        yield
        total = now(total)
        for bit in (1, 2, 4):
            came = flip(total, bit)
            yield
            total = clock.mark(total + now(came))
        have["count"] = total[0, 0]
        yield

    def shared_chain():
        eighth = shard_rows // 8
        units = SF // shard_count
        piece = lax.dynamic_slice_in_dim(shared_weight, context_index * eighth, eighth, 0)
        piece = piece.reshape(eighth, 3, shard_count, units)

        piece = jnp.transpose(piece, (2, 0, 1, 3)).reshape(shard_count, eighth, 3 * units)
        parts = [pick(piece, shard_index ^ i) for i in range(4)]
        came = line_swap(now(jnp.stack([parts[1], parts[3]])), 1)
        yield
        came = now(came)
        mine = jnp.stack([parts[0], came[0]])
        came = line_swap(clock.mark(jnp.stack([parts[2], came[1]])), 2)
        yield
        pieces = clock.mark(jnp.concatenate([mine, now(came)]))
        came = flip(pieces, 2)
        yield
        pair = clock.mark(jnp.stack([pieces, now(came)]))
        came = flip(pair, 4)
        yield
        mine = clock.mark(jnp.concatenate([pair, now(came)]))
        other = flip(mine, 1)
        yield
        have["shared"] = join_shared(meta(), mine, other)
        clock.mark(have["shared"])
        yield

    def out_chain():
        half = lax.dynamic_slice_in_dim(now(out_weight), core * half_rows, half_rows, 0)
        came = line_exchange(ready(jnp.broadcast_to(half, (4,) + half.shape)))
        yield
        have["out_mine"] = clock.mark(now(came))
        have["out_other"] = flip(have["out_mine"], 1)
        yield

    def qkv_all_chain():
        half = lax.dynamic_slice_in_dim(
            now(have["qkv_slice"]), core * (width // 2), width // 2, 0
        )
        came = flip(half, 2)
        yield
        pair = clock.mark(jnp.stack([half, now(came)]))
        came = flip(pair, 4)
        yield
        have["rel_mine"] = clock.mark(jnp.concatenate([pair, now(came)]))
        have["rel_other"] = flip(have["rel_mine"], 1)
        yield

    def main_chain():
        gains = have["gains"]
        normed_in, query, pair, qkv_slice = project(
            meta(), have["blocks"], gains[0], have["qkv_mine"], have["qkv_other"], group_width
        )
        clock.mark(pair)
        have["normed_in"], have["qkv_slice"] = normed_in, qkv_slice
        pair_other = flip(pair, 1)
        yield
        mixed_heads, log_total = attend(meta(), query, pair, pair_other, scale)
        clock.mark(log_total)
        have["attend"] = (query, pair, pair_other, log_total, mixed_heads)
        parts = ready(*[pick(mixed_heads, chip ^ r) for r in range(4)])
        mixed = [parts[0]] + [flip(parts[r], 2 * r) for r in (1, 2, 3)]
        have["mixed"] = mixed
        yield
        out_full, middle, normed_mid = leave(
            meta(), mixed, have["out_mine"], have["out_other"], states, gains[1]
        )
        have["out_full"], have["middle"] = out_full, middle
        clock.mark(normed_mid)

        near, center = line_swap(normed_mid, 1), line_middle(normed_mid)
        yield
        gates, shared_slice = have["gates"], have["shared"]
        gate_ups, shared_gate_ups, outs = [], [], []

        def forward(rows, i):
            result = experts(meta(), rows, gates[i], expert_weight, shared_slice)
            clock.mark(result[2])
            gate_ups.append(result[0])
            shared_gate_ups.append(result[1])
            outs.append(result[2])

        forward(normed_mid, 0)
        yield
        near, center = now(near, center)
        far, outward = line_middle(near), line_outward(center)
        forward(near, 1)
        yield
        far, outward = now(far, outward)
        outward_far = line_outward(far)
        third = clock.mark(jnp.where(at_end, outward, far))
        forward(third, 2)
        yield
        outward_far = now(outward_far)
        fourth = clock.mark(jnp.where(at_end, outward_far, center))
        forward(fourth, 3)
        line_rows = [normed_mid, near, third, fourth]
        came = line_inward(outs[3])
        yield
        carried = clock.mark(outs[2] + now(came))
        inward, crossed = line_inward(carried), line_middle(carried)
        yield
        inward, crossed = now(inward, crossed)
        near_out, middle_out = ready(outs[1] + crossed, outs[3] + inward)
        near_out, middle_out = line_swap(near_out, 1), line_middle(middle_out)
        yield
        near_out, middle_out = now(near_out, middle_out)
        final_state = (
            middle + outs[0].astype(f32) + near_out.astype(f32) + middle_out.astype(f32)
        )
        valid = have["valid"]
        deviation = final_state - teacher[0].astype(f32)
        have["squared"] = jnp.sum(valid[:, None] * deviation * deviation)
        grad_final = all_tokens / have["count"] * valid[:, None] * deviation
        have["final"], have["grad_final"] = final_state.astype(bf16)[None], grad_final
        grad_low = clock.mark(grad_final.astype(bf16))
        near, center = line_swap(grad_low, 1), line_middle(grad_low)
        yield
        kept = []

        def backward(grads, i):
            kept.append(
                experts_back(
                    meta(),
                    grads,
                    gates[i],
                    gate_ups[i],
                    shared_gate_ups[i],
                    expert_weight,
                    shared_slice,
                )
            )
            clock.mark(kept[-1][4])

        backward(grad_low, 0)
        yield
        near, center = now(near, center)
        far, outward = line_middle(near), line_outward(center)
        backward(near, 1)
        yield
        far, outward = now(far, outward)
        outward_far = line_outward(far)
        third = clock.mark(jnp.where(at_end, outward, far))
        backward(third, 2)
        yield
        outward_far = now(outward_far)
        fourth = clock.mark(jnp.where(at_end, outward_far, center))
        backward(fourth, 3)
        have["line"] = (line_rows, [grad_low, near, third, fourth])
        have["experts"] = list(zip(*kept))
        yield


    def states_chain():
        outs = have["experts"][4]
        came = line_inward(outs[3])
        yield
        carried = clock.mark(outs[2] + now(came))
        inward, crossed = line_inward(carried), line_middle(carried)
        yield
        inward, crossed = now(inward, crossed)
        near_out, middle_out = ready(outs[1] + crossed, outs[3] + inward)
        near_out, middle_out = line_swap(near_out, 1), line_middle(middle_out)
        yield
        near_out, middle_out = now(near_out, middle_out)
        grad_normed = clock.mark(
            outs[0].astype(f32) + near_out.astype(f32) + middle_out.astype(f32)
        )
        grad_middle, grad_branch, grad_gain_mid, grad_mixed = enter_back(
            meta(),
            have["grad_final"],
            grad_normed,
            have["middle"],
            have["gains"][1],
            have["out_full"],
        )
        clock.mark(grad_branch)
        have["grad_branch"], have["grad_gain_mid"] = grad_branch, grad_gain_mid
        grad_mixed = chips_exchange(ready(grad_mixed))
        yield
        query, pair, pair_other, log_total, mixed_heads = have["attend"]
        grad_query, grad_pair, grad_other = attend_back(
            meta(), query, pair, pair_other, log_total, mixed_heads, grad_mixed, scale
        )
        clock.mark(grad_query)
        came = flip(grad_other, 1)
        yield
        grad_pair = grad_pair + now(came).astype(f32)
        projected = clock.mark(jnp.concatenate([grad_query, grad_pair.astype(bf16)], axis=-1))
        have["grad_projected"] = projected
        parts = chips_exchange(ready(projected))
        yield
        grad_hidden, grad_gain_in = finish(
            meta(),
            parts,
            have["rel_mine"],
            have["rel_other"],
            states,
            grad_middle,
            have["gains"][0],
        )
        clock.mark(grad_gain_in)
        have["grad_hidden"] = grad_hidden
        sums = jnp.concatenate(
            [grad_gain_in, have["grad_gain_mid"], jnp.full((6, width), have["squared"], f32)],
            axis=0,
        )
        for offset in (1, 2):
            came = line_swap(sums, offset)
            yield
            sums = clock.mark(sums + now(came))
        for bit in (1, 2, 4):
            came = flip(sums, bit)
            yield
            sums = clock.mark(sums + now(came))
        own = lax.dynamic_slice_in_dim(sums, shard_index * shard_rows, shard_rows, 1)
        have["sums"] = (own, 0.5 * sums[2, 0] / (have["count"] * width))
        yield

    def expert_chain(index):
        line_rows, line_grads = have["line"]
        grad_gate_ups, acts, shared_grads, shared_acts = have["experts"][:4]
        shared = (shared_grads, shared_acts) if index == 0 else None

        def grad_of(at):
            return clock.mark(
                expert_grad(
                    meta(),
                    2 * at + index,
                    at,
                    line_rows,
                    line_grads,
                    grad_gate_ups,
                    acts,
                    shared,
                )
            )

        came = flip(grad_of(1 - core), 1)
        yield
        keep = grad_of(core)
        yield
        x_first = index % 2 == 0
        first, second = (2, 4) if x_first else (4, 2)
        picked = ((1, 3), (0, 2)) if x_first else ((2, 3), (0, 1))
        pieces = keep.shape[1] // 96

        def split_sum(keep, came):
            return [
                jnp.stack([keep[i] + came[i] for i in places]) for places in picked
            ]

        give, keep = blend(meta(), "blend_split", split_sum, [keep, came], pieces)
        clock.mark(give)
        came = flip(give, first)
        yield
        give, keep = blend(
            meta(), "blend_pair", lambda k, c: [k[1] + c[1], k[0] + c[0]], [keep, came], pieces
        )
        clock.mark(give)
        came = flip(give, second)
        yield
        own = clock.mark(blend(meta(), "blend_sum", lambda k, c: k + c, [keep, came], pieces))
        came = flip(own, second)
        yield
        pair = clock.mark(
            blend(meta(), "blend_stack", lambda a, b: jnp.stack([a, b]), [own, came], pieces)
        )
        came = flip(pair, first)
        yield

        def stack_four(near, far):
            if x_first:
                return jnp.stack([near[0], far[0], near[1], far[1]])
            return jnp.stack([near[0], near[1], far[0], far[1]])

        stacked = clock.mark(blend(meta(), "blend_four", stack_four, [pair, came], pieces))
        other = flip(stacked, 1)
        if index == 0:
            have["shared_sum"] = stacked[:, shard_rows:]
        yield
        have["grad_experts"] = place_pair(
            meta(), have.get("grad_experts"), index, expert_weight.shape, stacked, other
        )
        clock.mark(have["grad_experts"])
        yield

    def shared_grad_chain():
        total = now(have["shared_sum"])
        parts = ready(*[pick(total, chip ^ shard_index ^ i) for i in range(4)])
        came = [line_swap(parts[i], i) for i in (1, 2, 3)]
        yield
        mine = clock.mark(jnp.stack([parts[0]] + list(now(*came))))
        other = flip(mine, 1)
        yield
        have["grad_shared"] = clock.mark(place_shared(meta(), mine, other))
        yield

    def line_reduce_steps(keep, came):
        came = now(came)
        parts = [keep[i] + came[i] for i in range(4)]
        came = line_inward(clock.mark(parts[3]))
        yield
        carried = clock.mark(parts[2] + now(came))
        inward, crossed = line_inward(carried), line_middle(carried)
        yield
        inward, crossed = now(inward, crossed)
        near_out, middle_out = ready(parts[1] + crossed, parts[3] + inward)
        near_out, middle_out = line_swap(near_out, 1), line_middle(middle_out)
        yield
        near_out, middle_out = now(near_out, middle_out)
        have["line_sum"] = clock.mark(
            (parts[0].astype(f32) + near_out.astype(f32) + middle_out.astype(f32)).astype(bf16)
        )

    def out_grad_chain():
        mixed = jnp.concatenate(have["mixed"], axis=1)
        keep, give = weight_grad(
            meta(), chip ^ shard_index, [([mixed], [have["grad_branch"][None]])], 0
        )
        clock.mark(keep)
        came = flip(give, 1)
        yield
        yield from line_reduce_steps(keep, came)
        total = have["line_sum"]
        came = flip(total, 2)
        yield
        total = clock.mark(total + now(came))
        came = flip(total, 4)
        yield
        mine = clock.mark(total + now(came))
        other = flip(mine, 1)
        yield
        mine, other = now(mine, other)
        have["grad_out"] = clock.mark(
            jnp.where(
                core == 0,
                jnp.concatenate([mine, other], axis=0),
                jnp.concatenate([other, mine], axis=0),
            ).astype(f32)
        )
        yield

    def qkv_grad_chain():
        normed_in = have["normed_in"].reshape(4 * token_rows, width)
        projected = have["grad_projected"].reshape(1, 4 * token_rows, -1)
        keep, give = weight_grad(meta(), shard_index, [([normed_in], [projected])], 0)
        clock.mark(keep)
        came = flip(give, 1)
        yield
        yield from line_reduce_steps(keep, came)
        own = have["line_sum"]
        came = flip(own, 2)
        yield
        pair = clock.mark(jnp.stack([own, now(came)]))
        came = flip(pair, 4)
        yield
        mine = clock.mark(jnp.concatenate([pair, now(came)]))
        other = flip(mine, 1)
        yield
        have["grad_qkv"] = clock.mark(place_heads(meta(), [mine[r] for r in range(4)], other))
        yield

    early = {
        "H": hidden_chain(),
        "W": qkv_chain(),
        "S": shared_chain(),
        "O": out_chain(),
        "K": small_chain(),
        "R": qkv_all_chain(),
        "M": main_chain(),
    }
    late = {
        "L": states_chain(),
        "S": shared_grad_chain(),
        "O": out_grad_chain(),
        "Q": qkv_grad_chain(),
    }
    for index in range(local_experts // 2):
        late[str(index)] = expert_chain(index)
    for chains, order in ((early, EARLY), (late, LATE)):
        for name in order:
            next(chains[name], None)
        for name in chains:
            for _ in chains[name]:
                pass

    own, loss_value = have["sums"]
    return (
        have["final"],
        loss_value,
        have["grad_hidden"],
        own[0],
        have["grad_qkv"],
        have["grad_out"],
        own[1],
        have["grad_shared"],
        have["grad_experts"],
    )


def solution(mesh):
    in_specs = (
        P("wt", "ctx", None),
        P("wt", "ctx", None),
        P("wt", "ctx"),
        P("wt", "ctx", None),
        P("wt", "ctx", None),
        P("wt"),
        P("wt", None),
        P("wt", None),
        P("wt"),
        P("wt", None),
        P("wt", None, None),
    )
    out_specs = (
        P("wt", "ctx", None),
        P(),
        P("wt", "ctx", None),
        P("wt"),
        P("wt", None),
        P("wt", None),
        P("wt"),
        P("wt", None),
        P("wt", None, None),
    )
    plane_of_eight = dict(mesh.shape) == {"ctx": 8, "wt": 4}
    return jax.shard_map(
        fast_device if plane_of_eight else on_device, mesh=mesh, in_specs=in_specs, out_specs=out_specs, check_vma=False
    )
```

```python
import functools
import math

import jax
import jax.numpy as jnp
from jax import lax
from jax.experimental import pallas as pl
from jax.experimental.pallas import tpu as pltpu
from jax.sharding import PartitionSpec as P

QUERY_HEADS = 12
KEY_VALUE_HEADS = 4
HEAD_SIZE = 128
F = 512
SF = 1024
EXPERTS = 16
TOP = 6


norm_eps = 1e-05
masked_score = -1e30


def sigmoid_linear(values):
    return values * jax.nn.sigmoid(values)


def silu_slope(values):
    sigma_value = jax.nn.sigmoid(values)
    return sigma_value * (1.0 + values * (1.0 - sigma_value))


def normalize(values):
    inverse = lax.rsqrt(jnp.mean(values * values, axis=-1, keepdims=True) + norm_eps)
    return (values * inverse, inverse)


def norm_back(grad_normed, scaled, inverse, gain_vector):
    grad_scaled = grad_normed * gain_vector
    return inverse * (grad_scaled - scaled * jnp.mean(grad_scaled * scaled, axis=-1, keepdims=True))


def positions(row_ids, token_rows, context_count):
    piece_index = row_ids // token_rows
    within = row_ids % token_rows
    half_rows = token_rows // 2
    mirrored = jnp.where(within < half_rows, piece_index, 2 * context_count - 1 - piece_index)
    return mirrored * half_rows + within % half_rows


def route_tables(local_routes, local_gates, experts, capacity):
    token_rows = local_routes.shape[0]
    flat_routes = local_routes.reshape(-1)
    one_hot = (flat_routes[:, None] == jnp.arange(experts, dtype=jnp.int32)[None, :]).astype(
        jnp.int32
    )
    earlier = jnp.cumsum(one_hot, axis=0) - one_hot
    slot_index = jnp.sum(earlier * one_hot, axis=1)
    token_index = jnp.arange(flat_routes.shape[0], dtype=jnp.int32) // local_routes.shape[1]
    slot_table = (
        jnp.full((experts, capacity), token_rows, jnp.int32)
        .at[flat_routes, slot_index]
        .set(token_index)
    )
    slot_gate = (
        jnp.zeros((experts, capacity), jnp.float32)
        .at[flat_routes, slot_index]
        .set(local_gates.reshape(-1))
    )
    return (slot_table, slot_gate)


def block_scores(query_rows, key_block, key_position, query_place, score_scale):
    scores = (
        jnp.einsum("qhgd,khd->qhgk", query_rows, key_block, preferred_element_type=jnp.float32)
        * score_scale
    )
    allowed = key_position[None, None, None, :] <= query_place[:, None, None, None]
    return jnp.where(allowed, scores, masked_score)


def attend_forward(
    query_rows, blocked_keys, blocked_values, place_blocks, query_place, score_scale
):
    head_shape = query_rows.shape[:3]

    def online_step(running, block_args):
        running_max, running_sum, accumulated = running
        key_block, value_block, key_position = block_args
        scores = block_scores(query_rows, key_block, key_position, query_place, score_scale)
        new_max = jnp.maximum(running_max, jnp.max(scores, axis=-1))
        rescale = jnp.exp(running_max - new_max)
        powers = jnp.exp(scores - new_max[..., None])
        new_sum = running_sum * rescale + jnp.sum(powers, axis=-1)
        weighted = jnp.einsum(
            "qhgk,khd->qhgd",
            powers.astype(jnp.bfloat16),
            value_block,
            preferred_element_type=jnp.float32,
        )
        return ((new_max, new_sum, accumulated * rescale[..., None] + weighted), None)

    initial = (
        jnp.full(head_shape, masked_score, jnp.float32),
        jnp.zeros(head_shape, jnp.float32),
        jnp.zeros(query_rows.shape, jnp.float32),
    )
    row_max, row_sum, accumulated = lax.scan(
        online_step, initial, (blocked_keys, blocked_values, place_blocks)
    )[0]
    log_total = row_max + jnp.log(row_sum)
    return (accumulated / row_sum[..., None], log_total)


def attend_backward(
    query_rows,
    blocked_keys,
    blocked_values,
    place_blocks,
    query_place,
    log_total,
    attention_output_gradient,
    attention_output,
    score_scale,
):
    row_delta = jnp.sum(attention_output_gradient.astype(jnp.float32) * attention_output, axis=-1)

    def block_grads(grad_queries, block_args):
        key_block, value_block, key_position = block_args
        scores = block_scores(query_rows, key_block, key_position, query_place, score_scale)
        probabilities = jnp.exp(scores - log_total[..., None])
        grad_probs = jnp.einsum(
            "qhgd,khd->qhgk",
            attention_output_gradient,
            value_block,
            preferred_element_type=jnp.float32,
        )
        grad_scores = (probabilities * (grad_probs - row_delta[..., None])).astype(jnp.bfloat16)
        grad_queries = grad_queries + jnp.einsum(
            "qhgk,khd->qhgd", grad_scores, key_block, preferred_element_type=jnp.float32
        )
        grad_keys = (
            jnp.einsum(
                "qhgk,qhgd->khd", grad_scores, query_rows, preferred_element_type=jnp.float32
            )
            * score_scale
        )
        grad_values = jnp.einsum(
            "qhgk,qhgd->khd",
            probabilities.astype(jnp.bfloat16),
            attention_output_gradient,
            preferred_element_type=jnp.float32,
        )
        return (grad_queries, (grad_keys, grad_values))

    grad_queries, (grad_keys, grad_values) = lax.scan(
        block_grads,
        jnp.zeros(query_rows.shape, jnp.float32),
        (blocked_keys, blocked_values, place_blocks),
    )
    return (grad_queries * score_scale, grad_keys, grad_values)


def gate_up_grads(grad_act, gate_up, hidden_units):
    gate_part = gate_up[..., :hidden_units]
    up_part = gate_up[..., hidden_units:]
    return jnp.concatenate(
        [grad_act * up_part * silu_slope(gate_part), grad_act * sigmoid_linear(gate_part)], axis=-1
    ).astype(jnp.bfloat16)


def on_device(
    hidden,
    teacher,
    valid_mask,
    routes,
    route_gates,
    gain_in,
    query_key_value_weight,
    out_weight,
    gain_mid,
    shared_weight,
    expert_weight,
):
    token_rows = hidden.shape[1]
    model_width = hidden.shape[2]
    context_count = lax.axis_size("ctx")
    shard_count = lax.axis_size("wt")
    seq_rows = token_rows * context_count
    all_tokens = seq_rows * shard_count
    query_groups = QUERY_HEADS // KEY_VALUE_HEADS
    query_total_width = QUERY_HEADS * HEAD_SIZE
    key_value_width = KEY_VALUE_HEADS * HEAD_SIZE
    score_scale = 1.0 / math.sqrt(HEAD_SIZE)
    key_row_count = min(512, seq_rows)
    number_of_blocks = seq_rows // key_row_count
    capacity = token_rows * TOP // 12
    local_experts = expert_weight.shape[0]
    contract_last = (((1,), (1,)), ((), ()))
    contract_first = (((0,), (0,)), ((), ()))
    full_gain_in, full_qkv, full_out, full_gain_mid, full_shared = (
        lax.all_gather(gain_in, "wt", axis=0, tiled=True),
        lax.all_gather(query_key_value_weight, "wt", axis=0, tiled=True),
        lax.all_gather(out_weight, "wt", axis=0, tiled=True),
        lax.all_gather(gain_mid, "wt", axis=0, tiled=True),
        lax.all_gather(shared_weight, "wt", axis=0, tiled=True),
    )
    gain_in_float = full_gain_in.astype(jnp.float32)
    gain_mid_float = full_gain_mid.astype(jnp.float32)
    inputs = hidden[0].astype(jnp.float32)
    scaled_in, inverse_in = normalize(inputs)
    normed_in = (scaled_in * gain_in_float).astype(jnp.bfloat16)
    projected_rows = jnp.dot(normed_in, full_qkv, preferred_element_type=jnp.float32).astype(
        jnp.bfloat16
    )
    query_rows = projected_rows[:, :query_total_width].reshape(
        token_rows, KEY_VALUE_HEADS, query_groups, HEAD_SIZE
    )
    context_local = projected_rows[:, query_total_width:]
    context_gathered = lax.all_gather(context_local, "ctx", axis=0, tiled=True)
    context_index = lax.axis_index("ctx")
    query_place = positions(
        context_index * token_rows + jnp.arange(token_rows, dtype=jnp.int32),
        token_rows,
        context_count,
    )
    place_blocks = positions(
        jnp.arange(seq_rows, dtype=jnp.int32), token_rows, context_count
    ).reshape(number_of_blocks, key_row_count)
    blocked_keys = context_gathered[:, :key_value_width].reshape(
        number_of_blocks, key_row_count, KEY_VALUE_HEADS, HEAD_SIZE
    )
    blocked_values = context_gathered[:, key_value_width:].reshape(
        number_of_blocks, key_row_count, KEY_VALUE_HEADS, HEAD_SIZE
    )
    attention_output, log_total = attend_forward(
        query_rows, blocked_keys, blocked_values, place_blocks, query_place, score_scale
    )
    mixed_rows = attention_output.reshape(token_rows, query_total_width).astype(jnp.bfloat16)
    middle = inputs + jnp.dot(mixed_rows, full_out, preferred_element_type=jnp.float32)
    scaled_mid, inverse_mid = normalize(middle)
    normed_mid = (scaled_mid * gain_mid_float).astype(jnp.bfloat16)
    shared_gate_up = jnp.dot(
        normed_mid, full_shared[:, : 2 * SF], preferred_element_type=jnp.float32
    )
    shared_act = (sigmoid_linear(shared_gate_up[:, :SF]) * shared_gate_up[:, SF:]).astype(
        jnp.bfloat16
    )
    shared_out = lax.dot_general(
        shared_act, full_shared[:, 2 * SF :], contract_last, preferred_element_type=jnp.float32
    )
    slot_table, slot_gate = route_tables(routes[0], route_gates[0], EXPERTS, capacity)
    padded_rows = jnp.concatenate([normed_mid, jnp.zeros((1, model_width), jnp.bfloat16)], axis=0)
    expert_rows = jnp.take(padded_rows, slot_table, axis=0)
    arrived = lax.all_to_all(expert_rows, "wt", split_axis=0, concat_axis=0, tiled=True)
    slot_count = arrived.shape[1]
    grouped = arrived.reshape(shard_count, local_experts, slot_count, model_width)
    owner_gate_up = jnp.einsum(
        "wesd,edf->wesf", grouped, expert_weight[:, :, : 2 * F], preferred_element_type=jnp.float32
    )
    owner_act = (sigmoid_linear(owner_gate_up[..., :F]) * owner_gate_up[..., F:]).astype(
        jnp.bfloat16
    )
    owner_out = jnp.einsum(
        "wesf,edf->wesd",
        owner_act,
        expert_weight[:, :, 2 * F :],
        preferred_element_type=jnp.float32,
    ).astype(jnp.bfloat16)
    returned = lax.all_to_all(
        owner_out.reshape(shard_count * local_experts, slot_count, model_width),
        "wt",
        split_axis=0,
        concat_axis=0,
        tiled=True,
    )
    expert_out, owner_rows, owner_gate_up, owner_act = (
        returned,
        arrived,
        owner_gate_up.reshape(shard_count * local_experts, slot_count, 2 * F),
        owner_act.reshape(shard_count * local_experts, slot_count, F),
    )
    routed = (
        jnp.zeros((token_rows + 1, model_width), jnp.float32)
        .at[slot_table]
        .add(expert_out.astype(jnp.float32) * slot_gate[..., None])[:token_rows]
    )
    final_state = middle + shared_out + routed
    valid_float = valid_mask[0].astype(jnp.float32)
    deviation = final_state - teacher[0].astype(jnp.float32)
    squared_local = jnp.sum(valid_float[:, None] * deviation * deviation)
    count_local = jnp.sum(valid_float)
    squared_total, valid_count = lax.psum((squared_local, count_local), ("ctx", "wt"))
    loss_value = 0.5 * squared_total / (valid_count * model_width)
    grad_final = all_tokens / valid_count * valid_float[:, None] * deviation
    grad_shared_out = grad_final.astype(jnp.bfloat16)
    grad_shared_act = jnp.dot(
        grad_shared_out, full_shared[:, 2 * SF :], preferred_element_type=jnp.float32
    )
    grad_shared_down = lax.dot_general(
        grad_shared_out, shared_act, contract_first, preferred_element_type=jnp.float32
    )
    grad_shared_gate_up = gate_up_grads(grad_shared_act, shared_gate_up, SF)
    grad_normed_mid = lax.dot_general(
        grad_shared_gate_up,
        full_shared[:, : 2 * SF],
        contract_last,
        preferred_element_type=jnp.float32,
    )
    grad_shared_front = lax.dot_general(
        normed_mid, grad_shared_gate_up, contract_first, preferred_element_type=jnp.float32
    )
    grad_shared_full = jnp.concatenate([grad_shared_front, grad_shared_down], axis=1)
    padded_grads = jnp.concatenate([grad_final, jnp.zeros((1, model_width), jnp.float32)], axis=0)
    grad_expert_out = (jnp.take(padded_grads, slot_table, axis=0) * slot_gate[..., None]).astype(
        jnp.bfloat16
    )
    grad_arrived = lax.all_to_all(grad_expert_out, "wt", split_axis=0, concat_axis=0, tiled=True)
    grad_grouped = grad_arrived.reshape(shard_count, local_experts, capacity, model_width)
    owner_gate_up_grouped = owner_gate_up.reshape(shard_count, local_experts, capacity, 2 * F)
    owner_act_grouped = owner_act.reshape(shard_count, local_experts, capacity, F)
    owner_rows_grouped = owner_rows.reshape(shard_count, local_experts, capacity, model_width)
    grad_owner_act = jnp.einsum(
        "wecd,edf->wecf",
        grad_grouped,
        expert_weight[:, :, 2 * F :],
        preferred_element_type=jnp.float32,
    )
    grad_owner_gate_up = gate_up_grads(grad_owner_act, owner_gate_up_grouped, F)
    grad_owner_rows = jnp.einsum(
        "wecf,edf->wecd",
        grad_owner_gate_up,
        expert_weight[:, :, : 2 * F],
        preferred_element_type=jnp.float32,
    ).astype(jnp.bfloat16)
    front = jnp.einsum(
        "wecd,wecf->edf", owner_rows_grouped, grad_owner_gate_up, preferred_element_type=jnp.float32
    )
    back = jnp.einsum(
        "wecd,wecf->edf", grad_grouped, owner_act_grouped, preferred_element_type=jnp.float32
    )
    expert_grad = jnp.concatenate([front, back], axis=2)
    grad_rows = lax.all_to_all(
        grad_owner_rows.reshape(shard_count * local_experts, capacity, model_width),
        "wt",
        split_axis=0,
        concat_axis=0,
        tiled=True,
    )
    grad_normed_mid = (
        grad_normed_mid
        + jnp.zeros((token_rows + 1, model_width), jnp.float32)
        .at[slot_table]
        .add(grad_rows.astype(jnp.float32))[:token_rows]
    )
    grad_gain_mid_local = jnp.sum(grad_normed_mid * scaled_mid, axis=0)
    grad_middle = grad_final + norm_back(grad_normed_mid, scaled_mid, inverse_mid, gain_mid_float)
    grad_branch = grad_middle.astype(jnp.bfloat16)
    mixed_gradient = lax.dot_general(
        grad_branch, full_out, contract_last, preferred_element_type=jnp.float32
    ).astype(jnp.bfloat16)
    grad_out_local = lax.dot_general(
        mixed_rows, grad_branch, contract_first, preferred_element_type=jnp.float32
    )
    context_recomputed = lax.all_gather(context_local, "ctx", axis=0, tiled=True)
    backward_keys = context_recomputed[:, :key_value_width].reshape(
        number_of_blocks, key_row_count, KEY_VALUE_HEADS, HEAD_SIZE
    )
    backward_values = context_recomputed[:, key_value_width:].reshape(
        number_of_blocks, key_row_count, KEY_VALUE_HEADS, HEAD_SIZE
    )
    attention_output_gradient = mixed_gradient.reshape(
        token_rows, KEY_VALUE_HEADS, query_groups, HEAD_SIZE
    )
    grad_queries, grad_keys, grad_values = attend_backward(
        query_rows,
        backward_keys,
        backward_values,
        place_blocks,
        query_place,
        log_total,
        attention_output_gradient,
        attention_output,
        score_scale,
    )
    grad_context_all = jnp.concatenate(
        [
            grad_keys.reshape(seq_rows, key_value_width),
            grad_values.reshape(seq_rows, key_value_width),
        ],
        axis=1,
    )
    grad_context = lax.psum_scatter(
        grad_context_all.astype(jnp.bfloat16), "ctx", scatter_dimension=0, tiled=True
    ).astype(jnp.float32)
    grad_projected = jnp.concatenate(
        [grad_queries.reshape(token_rows, query_total_width), grad_context], axis=1
    ).astype(jnp.bfloat16)
    grad_normed_in = lax.dot_general(
        grad_projected, full_qkv, contract_last, preferred_element_type=jnp.float32
    )
    grad_qkv_local = lax.dot_general(
        normed_in, grad_projected, contract_first, preferred_element_type=jnp.float32
    )
    grad_gain_in_local = jnp.sum(grad_normed_in * scaled_in, axis=0)
    grad_inputs = grad_middle + norm_back(grad_normed_in, scaled_in, inverse_in, gain_in_float)
    weight_sums = (
        lax.psum_scatter(
            grad_gain_in_local.astype(jnp.bfloat16), "wt", scatter_dimension=0, tiled=True
        ).astype(jnp.float32),
        lax.psum_scatter(
            grad_qkv_local.astype(jnp.bfloat16), "wt", scatter_dimension=0, tiled=True
        ).astype(jnp.float32),
        lax.psum_scatter(
            grad_out_local.astype(jnp.bfloat16), "wt", scatter_dimension=0, tiled=True
        ).astype(jnp.float32),
        lax.psum_scatter(
            grad_gain_mid_local.astype(jnp.bfloat16), "wt", scatter_dimension=0, tiled=True
        ).astype(jnp.float32),
        lax.psum_scatter(
            grad_shared_full.astype(jnp.bfloat16), "wt", scatter_dimension=0, tiled=True
        ).astype(jnp.float32),
    )
    summed = (
        lax.psum(weight_sums[0].astype(jnp.bfloat16), "ctx").astype(jnp.float32),
        lax.psum(weight_sums[1].astype(jnp.bfloat16), "ctx").astype(jnp.float32),
        lax.psum(weight_sums[2].astype(jnp.bfloat16), "ctx").astype(jnp.float32),
        lax.psum(weight_sums[3].astype(jnp.bfloat16), "ctx").astype(jnp.float32),
        lax.psum(weight_sums[4].astype(jnp.bfloat16), "ctx").astype(jnp.float32),
        lax.psum(expert_grad.astype(jnp.bfloat16), "ctx").astype(jnp.float32),
    )
    return (
        final_state.astype(jnp.bfloat16)[None],
        loss_value,
        grad_inputs[None],
        summed[0],
        summed[1],
        summed[2],
        summed[3],
        summed[4],
        summed[5],
    )


PLANE = [[0, 2, 4, 6], [1, 3, 5, 7]]
COSTS = {
    "project": 0.3,
    "attend": 0.3,
    "leave": 0.3,
    "join_shared": 0.3,
    "experts": 0.3,
    "experts_back": 0.3,
    "enter_back": 0.3,
    "attend_back": 0.3,
    "finish": 0.3,
    "weight_grad": 0.3,
    "expert_grad": 0.3,
    "blend_split": 0.3,
    "blend_pair": 0.3,
    "blend_sum": 0.3,
    "blend_stack": 0.3,
    "blend_four": 0.3,
    "place_pair": 0.3,
    "place_shared": 0.3,
    "place_heads": 0.3,
}


def flip(value, bit):
    return lax.ppermute(value, "ctx", [(index, index ^ bit) for index in range(8)])


def line_swap(value, offset):
    return lax.ppermute(value, "wt", [(index, index ^ offset) for index in range(4)])


def line_middle(value):
    return lax.ppermute(value, "wt", [(1, 2), (2, 1)])


def line_outward(value):
    return lax.ppermute(value, "wt", [(1, 0), (2, 3)])


def line_inward(value):
    return lax.ppermute(value, "wt", [(0, 1), (3, 2)])


def line_gather(value, at_end):
    near = line_swap(value, 1)
    middle = line_middle(value)
    middle_far = line_middle(near)
    outward = line_outward(middle)
    outward_far = line_outward(middle_far)
    return [
        value,
        near,
        jnp.where(at_end, outward, middle_far),
        jnp.where(at_end, outward_far, middle),
    ]


def line_reduce(parts):
    far = line_inward(parts[3])
    carried = parts[2] + far
    inward = line_inward(carried)
    crossed = line_middle(carried)
    near = line_swap(parts[1] + crossed, 1)
    middle = line_middle(parts[3] + inward)
    return (
        parts[0].astype(jnp.float32) + near.astype(jnp.float32) + middle.astype(jnp.float32)
    )


def chips_exchange(blocks):
    return lax.all_to_all(
        blocks,
        "ctx",
        split_axis=0,
        concat_axis=0,
        tiled=True,
        axis_index_groups=PLANE,
    )


def line_exchange(blocks):
    return lax.all_to_all(blocks, "wt", split_axis=0, concat_axis=0, tiled=True)


def chips_gather(value, x_last):
    along_x = flip(value, 2)
    along_y = flip(value, 4)
    corner = flip(along_y, 2) if x_last else flip(along_x, 4)
    return [value, along_x, along_y, corner]


def core_swap(values):
    return [flip(value, 1) for value in values]


def everywhere_sum(value):
    for bit in (1, 2, 4):
        value = value + flip(value, bit)
    for offset in (1, 2):
        value = value + line_swap(value, offset)
    return value


def pick(blocks, index):
    return lax.dynamic_index_in_dim(blocks, index, 0, keepdims=False)


def chips_reduce(keep, came):
    half = keep.shape[1] // 2
    upper = keep[:, :half] + came[:, :half]
    lower = keep[:, half:] + came[:, half:]
    upper_came = flip(upper[1::2], 2)
    lower_came = flip(lower[2:], 4)
    upper = upper[0::2] + upper_came
    lower = lower[:2] + lower_came
    upper_came = flip(upper[1], 4)
    lower_came = flip(lower[1], 2)
    return jnp.concatenate([upper[0] + upper_came, lower[0] + lower_came], axis=0)


def dot_plain(left, right):
    return lax.dot_general(
        left, right, (((1,), (0,)), ((), ())), preferred_element_type=jnp.float32
    )


def dot_last(left, right):
    return lax.dot_general(
        left, right, (((1,), (1,)), ((), ())), preferred_element_type=jnp.float32
    )


def dot_first(left, right):
    return lax.dot_general(
        left, right, (((0,), (0,)), ((), ())), preferred_element_type=jnp.float32
    )


def call(kernel, name, meta, arrays, grid, in_specs, out_specs, out_shape, scratch, flops, moved):
    return pl.pallas_call(
        kernel,
        grid_spec=pltpu.PrefetchScalarGridSpec(
            num_scalar_prefetch=1,
            grid=grid,
            in_specs=in_specs,
            out_specs=out_specs,
            scratch_shapes=scratch,
        ),
        out_shape=out_shape,
        compiler_params=pltpu.CompilerParams(vmem_limit_bytes=48 * 1024 * 1024),
        cost_estimate=pl.CostEstimate(
            flops=int(COSTS.get(name, 1.0) * 1e9), bytes_accessed=1000, transcendentals=0
        ),
        name=name,
    )(meta, *arrays)


def whole(array):
    rank = len(array.shape)
    return pl.BlockSpec(tuple(array.shape), lambda *_: (0,) * rank)


def shape_of(shape, dtype):
    return jax.ShapeDtypeStruct(shape, dtype)


def size_of(arrays):
    return sum(math.prod(a.shape) * a.dtype.itemsize for a in arrays)


def blend(meta, name, function, arrays, pieces=4):
    rows = arrays[0].shape[-2]
    tile = rows // pieces
    outs = jax.eval_shape(function, *[shape_of(a.shape, a.dtype) for a in arrays])
    many = isinstance(outs, (list, tuple))
    outs = list(outs) if many else [outs]

    def spec(a):
        rank = len(a.shape)
        lead = a.shape[:-2]
        return pl.BlockSpec(
            tuple(lead) + (tile, a.shape[-1]),
            lambda i, m: (0,) * (rank - 2) + (i, 0),
        )

    def kernel(meta_ref, *refs):
        result = function(*[ref[...] for ref in refs[: len(arrays)]])
        result = list(result) if many else [result]
        for ref, value in zip(refs[len(arrays) :], result):
            ref[...] = value

    result = call(
        kernel,
        name,
        meta,
        arrays,
        (pieces,),
        [spec(a) for a in arrays],
        [spec(a) for a in outs],
        outs,
        [],
        0,
        0,
    )
    return result if many else result[0]


def aligned(value, step):
    return pl.multiple_of(value * step, step)


def project_kernel(meta, blocks_ref, gain_ref, mine, other, *refs):
    normed_ref, query_ref, pair_ref, weight_ref = refs
    core = meta[0] & 1
    rows = mine.shape[1]

    @pl.when(pl.program_id(0) == 0)
    def _():
        for i in range(4):
            at = 2 * (meta[1] ^ i)
            weight_ref[pl.ds(aligned(at + core, rows), rows), :] = mine[i]
            weight_ref[pl.ds(aligned(at + 1 - core, rows), rows), :] = other[i]

    states = blocks_ref[0].astype(jnp.float32)
    inverse = lax.rsqrt(jnp.mean(states * states, axis=-1, keepdims=True) + norm_eps)
    normed = (states * inverse * gain_ref[...]).astype(jnp.bfloat16)
    normed_ref[0] = normed
    projected = dot_plain(normed, weight_ref[...]).astype(jnp.bfloat16)
    query_width = query_ref.shape[-1]
    query_ref[0] = projected[:, :query_width]
    pair_ref[0] = projected[:, query_width:]


def project(meta, blocks, gain, mine, other, query_width):
    _, token_rows, width = blocks.shape
    columns = mine.shape[2]
    arrays = [blocks, gain, mine, other]
    outs = [
        shape_of((4, token_rows, width), jnp.bfloat16),
        shape_of((4, token_rows, query_width), jnp.bfloat16),
        shape_of((4, token_rows, columns - query_width), jnp.bfloat16),
        shape_of((width, columns), jnp.bfloat16),
    ]
    return call(
        project_kernel,
        "project",
        meta,
        arrays,
        (4,),
        [pl.BlockSpec((1, token_rows, width), lambda r, m: (r, 0, 0))]
        + [whole(a) for a in arrays[1:]],
        [
            pl.BlockSpec((1, token_rows, width), lambda r, m: (r, 0, 0)),
            pl.BlockSpec((1, token_rows, query_width), lambda r, m: (r, 0, 0)),
            pl.BlockSpec((1, token_rows, columns - query_width), lambda r, m: (r, 0, 0)),
            whole(outs[3]),
        ],
        outs,
        [],
        2 * 4 * token_rows * width * columns,
        size_of(arrays) + size_of(outs),
    )


def sort_pairs(meta, mine_ref, other_ref, keys, values):
    half = mine_ref.shape[1] // 2
    for slot in range(16):
        block, part = (slot, 0) if slot < 8 else (15 - slot, 1)
        place = block >> 1
        rows = pl.ds(part * half, half)
        to = pl.ds(slot * half, half)

        @pl.when((meta[0] & 1) == (block & 1))
        def _():
            keys[to, :] = mine_ref[place, rows, :HEAD_SIZE]
            values[to, :] = mine_ref[place, rows, HEAD_SIZE:]

        @pl.when((meta[0] & 1) != (block & 1))
        def _():
            keys[to, :] = other_ref[place, rows, :HEAD_SIZE]
            values[to, :] = other_ref[place, rows, HEAD_SIZE:]


def stack_heads(rows):
    count = rows.shape[1] // HEAD_SIZE
    return jnp.concatenate(
        [rows[:, h * HEAD_SIZE : (h + 1) * HEAD_SIZE] for h in range(count)], axis=0
    )


def unstack_heads(rows, count):
    each = rows.shape[0] // count
    return jnp.concatenate([rows[h * each : (h + 1) * each] for h in range(count)], axis=1)


def step_slot(meta):
    step = pl.program_id(0)
    block = 2 * (step >> 1) + (meta[0] & 1)
    return jnp.where((step & 1) == 0, block, 15 - block)


def allowed_pairs(start, slot, shape, half):
    key_place = start + lax.broadcasted_iota(jnp.int32, shape, 0)
    query_place = slot * half + (lax.broadcasted_iota(jnp.int32, shape, 1) & (half - 1))
    return key_place <= query_place


def key_spans(step, half, span):
    pairs = (step // 2 if step % 2 == 0 else 7 - step // 2) + 1
    rows = pairs * 2 * half
    return [(at, min(span, rows - at)) for at in range(0, rows, span)]


def attend_kernel(scale, span, meta, query_ref, mine_ref, other_ref, *refs):
    out_ref, log_ref, keys, values, values_turned = refs
    half, group_width = query_ref.shape[1:]
    count = group_width // HEAD_SIZE

    @pl.when(pl.program_id(0) == 0)
    def _():
        sort_pairs(meta, mine_ref, other_ref, keys, values)
        values_turned[...] = values[...].T

    slot = step_slot(meta)
    query = stack_heads(query_ref[0])
    wide = count * half

    def run(spans):
        highest = jnp.full((1, wide), masked_score, jnp.float32)
        total = jnp.zeros((1, wide), jnp.float32)
        mixed = jnp.zeros((HEAD_SIZE, wide), jnp.float32)
        for start, size in spans:
            at = pl.ds(start, size)
            scores = dot_last(keys[at, :], query) * scale
            if start == spans[-1][0]:
                seen = allowed_pairs(start, slot, scores.shape, half)
                scores = jnp.where(seen, scores, masked_score)
            new = jnp.maximum(highest, jnp.max(scores, axis=0, keepdims=True))
            rescale = jnp.exp(highest - new)
            powers = jnp.exp(scores - new)
            total = total * rescale + jnp.sum(powers, axis=0, keepdims=True)
            mixed = mixed * rescale + dot_plain(
                values_turned[:, at], powers.astype(jnp.bfloat16)
            )
            highest = new
        log_ref[0] = highest + jnp.log(total)
        out_ref[0] = unstack_heads((mixed / total).T, count).astype(jnp.bfloat16)

    for step in range(8):

        @pl.when(pl.program_id(0) == step)
        def _():
            run(key_spans(step, half, span))


def attend(meta, query, mine, other, scale):
    token_rows, group_width = query.shape[1:]
    half = token_rows // 2
    count = group_width // HEAD_SIZE
    everything = 8 * token_rows
    span = 1024
    arrays = [query, mine, other]
    outs = [
        shape_of(query.shape, jnp.bfloat16),
        shape_of((8, 1, count * half), jnp.float32),
    ]
    return call(
        functools.partial(attend_kernel, scale, span),
        "attend",
        meta,
        arrays,
        (8,),
        [
            pl.BlockSpec((1, half, group_width), lambda i, m: (i // 2, i % 2, 0)),
            whole(mine),
            whole(other),
        ],
        [
            pl.BlockSpec((1, half, group_width), lambda i, m: (i // 2, i % 2, 0)),
            pl.BlockSpec((1, 1, count * half), lambda i, m: (i, 0, 0)),
        ],
        outs,
        [
            pltpu.VMEM((everything, HEAD_SIZE), jnp.bfloat16),
            pltpu.VMEM((everything, HEAD_SIZE), jnp.bfloat16),
            pltpu.VMEM((HEAD_SIZE, everything), jnp.bfloat16),
        ],
        2 * 2 * 4 * token_rows * everything * group_width,
        size_of(arrays) + size_of(outs),
    )


def attend_back_kernel(scale, span, meta, query_ref, mine_ref, other_ref, log_ref, *refs):
    mixed_ref, grad_ref, grad_query_ref, grad_mine_ref, grad_other_ref = refs[:5]
    keys, values, keys_turned, grad_keys, grad_values = refs[5:]
    step = pl.program_id(0)
    half, group_width = query_ref.shape[1:]
    count = group_width // HEAD_SIZE

    @pl.when(step == 0)
    def _():
        sort_pairs(meta, mine_ref, other_ref, keys, values)
        keys_turned[...] = keys[...].T
        grad_keys[...] = jnp.zeros_like(grad_keys)
        grad_values[...] = jnp.zeros_like(grad_values)

    slot = step_slot(meta)
    query = stack_heads(query_ref[0])
    mixed = stack_heads(mixed_ref[0]).astype(jnp.float32)
    grad = stack_heads(grad_ref[0])
    delta = jnp.sum((mixed * grad.astype(jnp.float32)).T, axis=0, keepdims=True)
    log_total = log_ref[0]

    def run(spans):
        grad_turned = jnp.zeros((HEAD_SIZE, count * half), jnp.float32)
        for start, size in spans:
            at = pl.ds(start, size)
            scores = dot_last(keys[at, :], query) * scale
            probs = jnp.exp(scores - log_total)
            if start == spans[-1][0]:
                probs = jnp.where(allowed_pairs(start, slot, probs.shape, half), probs, 0.0)
            grad_probs = dot_last(values[at, :], grad)
            grad_scores = (probs * (grad_probs - delta)).astype(jnp.bfloat16)
            grad_values[at, :] += dot_plain(probs.astype(jnp.bfloat16), grad)
            grad_keys[at, :] += dot_plain(grad_scores, query)
            grad_turned += dot_plain(keys_turned[:, at], grad_scores)
        grad_query_ref[0] = unstack_heads((grad_turned * scale).T, count).astype(jnp.bfloat16)

    for at_step in range(8):

        @pl.when(step == at_step)
        def _():
            run(key_spans(at_step, half, span))

    @pl.when(step == 7)
    def _():
        for slot_at in range(16):
            block, part = (slot_at, 0) if slot_at < 8 else (15 - slot_at, 1)
            place = block >> 1
            rows = pl.ds(part * half, half)
            here = pl.ds(slot_at * half, half)
            both = jnp.concatenate([grad_keys[here, :] * scale, grad_values[here, :]], axis=1)

            @pl.when((meta[0] & 1) == (block & 1))
            def _():
                grad_mine_ref[place, rows, :] = both

            @pl.when((meta[0] & 1) != (block & 1))
            def _():
                grad_other_ref[place, rows, :] = both.astype(jnp.bfloat16)


def attend_back(meta, query, mine, other, log_total, mixed, grad, scale):
    token_rows, group_width = query.shape[1:]
    half = token_rows // 2
    count = group_width // HEAD_SIZE
    everything = 8 * token_rows
    span = 512
    arrays = [query, mine, other, log_total, mixed, grad]
    outs = [
        shape_of(query.shape, jnp.bfloat16),
        shape_of(mine.shape, jnp.float32),
        shape_of(mine.shape, jnp.bfloat16),
    ]
    return call(
        functools.partial(attend_back_kernel, scale, span),
        "attend_back",
        meta,
        arrays,
        (8,),
        [
            pl.BlockSpec((1, half, group_width), lambda i, m: (i // 2, i % 2, 0)),
            whole(mine),
            whole(other),
            pl.BlockSpec((1, 1, count * half), lambda i, m: (i, 0, 0)),
            pl.BlockSpec((1, half, group_width), lambda i, m: (i // 2, i % 2, 0)),
            pl.BlockSpec((1, half, group_width), lambda i, m: (i // 2, i % 2, 0)),
        ],
        [
            pl.BlockSpec((1, half, group_width), lambda i, m: (i // 2, i % 2, 0)),
            whole(outs[1]),
            whole(outs[2]),
        ],
        outs,
        [
            pltpu.VMEM((everything, HEAD_SIZE), jnp.bfloat16),
            pltpu.VMEM((everything, HEAD_SIZE), jnp.bfloat16),
            pltpu.VMEM((HEAD_SIZE, everything), jnp.bfloat16),
            pltpu.VMEM((everything, HEAD_SIZE), jnp.float32),
            pltpu.VMEM((everything, HEAD_SIZE), jnp.float32),
        ],
        5 * 2 * 4 * token_rows * everything * group_width,
        size_of(arrays) + size_of(outs),
    )


def leave_kernel(meta, *refs):
    parts, mine, other, states_ref, gain_ref = refs[:4], *refs[4:8]
    weight_ref, middle_ref, normed_ref = refs[8:]
    core, chip = meta[0] & 1, meta[0] >> 1
    rows = mine.shape[1]
    for i in range(4):
        weight_ref[pl.ds(aligned(2 * i + core, rows), rows), :] = mine[i]
        weight_ref[pl.ds(aligned(2 * i + 1 - core, rows), rows), :] = other[i]
    middle = states_ref[...].astype(jnp.float32)
    for r in range(4):
        at = pl.ds(aligned(chip ^ r, 2 * rows), 2 * rows)
        middle += dot_plain(parts[r][...], weight_ref[at, :])
    middle_ref[...] = middle
    inverse = lax.rsqrt(jnp.mean(middle * middle, axis=-1, keepdims=True) + norm_eps)
    normed_ref[...] = (middle * inverse * gain_ref[...]).astype(jnp.bfloat16)


def leave(meta, parts, mine, other, states, gain):
    token_rows, width = states.shape
    arrays = list(parts) + [mine, other, states, gain]
    outs = [
        shape_of((8 * mine.shape[1], width), jnp.bfloat16),
        shape_of((token_rows, width), jnp.float32),
        shape_of((token_rows, width), jnp.bfloat16),
    ]
    return call(
        leave_kernel,
        "leave",
        meta,
        arrays,
        (1,),
        [whole(a) for a in arrays],
        [whole(a) for a in outs],
        outs,
        [],
        2 * token_rows * width * width,
        size_of(arrays) + size_of(outs),
    )


def norm_back_rows(grad_normed, states, gain):
    inverse = lax.rsqrt(jnp.mean(states * states, axis=-1, keepdims=True) + norm_eps)
    scaled = states * inverse
    gain_grad = jnp.sum(grad_normed * scaled, axis=0, keepdims=True)
    grad_scaled = grad_normed * gain
    shift = jnp.mean(grad_scaled * scaled, axis=-1, keepdims=True)
    return inverse * (grad_scaled - scaled * shift), gain_grad


def enter_back_kernel(meta, final_ref, normed_ref, middle_ref, gain_ref, weight_ref, *refs):
    grad_ref, branch_ref, gain_grad_ref, mixed_ref = refs
    grad, gain_grad = norm_back_rows(normed_ref[...], middle_ref[...], gain_ref[...])
    grad = grad + final_ref[...]
    grad_ref[...] = grad
    gain_grad_ref[...] = gain_grad
    branch = grad.astype(jnp.bfloat16)
    branch_ref[...] = branch
    rows = weight_ref.shape[0] // 4
    for r in range(4):
        mixed_ref[r] = dot_last(branch, weight_ref[rows * r : rows * (r + 1), :]).astype(
            jnp.bfloat16
        )


def enter_back(meta, grad_final, grad_normed, middle, gain, weight):
    token_rows, width = middle.shape
    arrays = [grad_final, grad_normed, middle, gain, weight]
    outs = [
        shape_of((token_rows, width), jnp.float32),
        shape_of((token_rows, width), jnp.bfloat16),
        shape_of((1, width), jnp.float32),
        shape_of((4, token_rows, weight.shape[0] // 4), jnp.bfloat16),
    ]
    return call(
        enter_back_kernel,
        "enter_back",
        meta,
        arrays,
        (1,),
        [whole(a) for a in arrays],
        [whole(a) for a in outs],
        outs,
        [],
        2 * token_rows * width * width,
        size_of(arrays) + size_of(outs),
    )


def finish_kernel(meta, *refs):
    parts, mine, other = refs[:3]
    states_ref, middle_ref, gain_ref, grad_ref, gain_grad_ref, total = refs[3:]
    core, chip = meta[0] & 1, meta[0] >> 1
    columns = mine.shape[1]
    for at, weights in ((core, mine), (1 - core, other)):
        total[:, pl.ds(aligned(at, columns), columns)] = sum(
            dot_last(parts[r], weights[chip ^ r]) for r in range(4)
        )
    grad, gain_grad = norm_back_rows(
        total[...], states_ref[...].astype(jnp.float32), gain_ref[...]
    )
    grad_ref[0] = grad + middle_ref[...]
    gain_grad_ref[...] = gain_grad


def finish(meta, parts, mine, other, states, grad_middle, gain):
    token_rows, width = states.shape
    arrays = [parts, mine, other, states, grad_middle, gain]
    outs = [
        shape_of((1, token_rows, width), jnp.float32),
        shape_of((1, width), jnp.float32),
    ]
    return call(
        finish_kernel,
        "finish",
        meta,
        arrays,
        (1,),
        [whole(a) for a in arrays],
        [whole(a) for a in outs],
        outs,
        [pltpu.VMEM((token_rows, width), jnp.float32)],
        2 * token_rows * width * 4 * parts.shape[2],
        size_of(arrays) + size_of(outs),
    )


def gated(gate_up, units):
    gate_part = gate_up[:, :units]
    sigma = 1.0 / (1.0 + jnp.exp(-gate_part))
    return gate_part * sigma * gate_up[:, units:]


def gated_back(grad_act, gate_up, units):
    gate_part = gate_up[:, :units].astype(jnp.float32)
    up_part = gate_up[:, units:].astype(jnp.float32)
    sigma = 1.0 / (1.0 + jnp.exp(-gate_part))
    linear = gate_part * sigma
    grad_gate = grad_act * up_part * (sigma * (1.0 + gate_part * (1.0 - sigma)))
    return grad_gate, grad_act * linear, linear * up_part


def experts_kernel(
    meta, rows_ref, gates_ref, expert_ref, shared_ref, gate_up_ref, shared_gate_up_ref, out_ref, total
):
    expert = pl.program_id(0)
    rows = rows_ref[...]

    @pl.when(expert == 0)
    def _():
        units = shared_ref.shape[1] // 3
        gate_up = dot_plain(rows, shared_ref[:, : 2 * units])
        shared_gate_up_ref[...] = gate_up.astype(jnp.bfloat16)
        act = gated(gate_up, units).astype(jnp.bfloat16)
        total[...] = dot_last(act, shared_ref[:, 2 * units :])

    gate_up = dot_plain(rows, expert_ref[0, :, : 2 * F])
    gate_up_ref[0] = gate_up.astype(jnp.bfloat16)
    act = (gated(gate_up, F) * gates_ref[0]).astype(jnp.bfloat16)
    total[...] += dot_last(act, expert_ref[0, :, 2 * F :])

    @pl.when(expert == pl.num_programs(0) - 1)
    def _():
        out_ref[...] = total[...].astype(jnp.bfloat16)


def experts(meta, rows, gates, expert_weight, shared_slice):
    local_experts, width, _ = expert_weight.shape
    token_rows = rows.shape[0]
    shared_units = shared_slice.shape[1] // 3
    arrays = [rows, gates, expert_weight, shared_slice]
    outs = [
        shape_of((local_experts, token_rows, 2 * F), jnp.bfloat16),
        shape_of((token_rows, 2 * shared_units), jnp.bfloat16),
        shape_of((token_rows, width), jnp.bfloat16),
    ]
    return call(
        experts_kernel,
        "experts",
        meta,
        arrays,
        (local_experts,),
        [
            whole(rows),
            pl.BlockSpec((1, token_rows, 1), lambda e, m: (e, 0, 0)),
            pl.BlockSpec((1, width, 3 * F), lambda e, m: (e, 0, 0)),
            whole(shared_slice),
        ],
        [
            pl.BlockSpec((1, token_rows, 2 * F), lambda e, m: (e, 0, 0)),
            whole(outs[1]),
            whole(outs[2]),
        ],
        outs,
        [pltpu.VMEM((token_rows, width), jnp.float32)],
        2 * token_rows * width * 3 * (F * local_experts + shared_units),
        size_of(arrays) + size_of(outs),
    )


def experts_back_kernel(
    meta,
    grad_ref,
    gates_ref,
    gate_up_ref,
    shared_gate_up_ref,
    expert_ref,
    shared_ref,
    grad_gate_up_ref,
    act_ref,
    shared_grad_ref,
    shared_act_ref,
    grad_rows_ref,
    total,
):
    expert = pl.program_id(0)
    grad = grad_ref[...]

    @pl.when(expert == 0)
    def _():
        units = shared_ref.shape[1] // 3
        grad_act = dot_plain(grad, shared_ref[:, 2 * units :])
        grad_gate, grad_up, act = gated_back(grad_act, shared_gate_up_ref[...], units)
        both = jnp.concatenate([grad_gate, grad_up], axis=1).astype(jnp.bfloat16)
        shared_grad_ref[0] = both
        shared_act_ref[0] = act.astype(jnp.bfloat16)
        total[...] = dot_last(both, shared_ref[:, : 2 * units])

    grad_act = dot_plain(grad, expert_ref[0, :, 2 * F :]) * gates_ref[0]
    grad_gate, grad_up, act = gated_back(grad_act, gate_up_ref[0], F)
    both = jnp.concatenate([grad_gate, grad_up], axis=1).astype(jnp.bfloat16)
    grad_gate_up_ref[0] = both
    act_ref[0] = (act * gates_ref[0]).astype(jnp.bfloat16)
    total[...] += dot_last(both, expert_ref[0, :, : 2 * F])

    @pl.when(expert == pl.num_programs(0) - 1)
    def _():
        grad_rows_ref[...] = total[...].astype(jnp.bfloat16)


def experts_back(meta, grad, gates, gate_up, shared_gate_up, expert_weight, shared_slice):
    local_experts, width, _ = expert_weight.shape
    token_rows = grad.shape[0]
    shared_units = shared_slice.shape[1] // 3
    arrays = [grad, gates, gate_up, shared_gate_up, expert_weight, shared_slice]
    outs = [
        shape_of((local_experts, token_rows, 2 * F), jnp.bfloat16),
        shape_of((local_experts, token_rows, F), jnp.bfloat16),
        shape_of((1, token_rows, 2 * shared_units), jnp.bfloat16),
        shape_of((1, token_rows, shared_units), jnp.bfloat16),
        shape_of((token_rows, width), jnp.bfloat16),
    ]
    return call(
        experts_back_kernel,
        "experts_back",
        meta,
        arrays,
        (local_experts,),
        [
            whole(grad),
            pl.BlockSpec((1, token_rows, 1), lambda e, m: (e, 0, 0)),
            pl.BlockSpec((1, token_rows, 2 * F), lambda e, m: (e, 0, 0)),
            whole(shared_gate_up),
            pl.BlockSpec((1, width, 3 * F), lambda e, m: (e, 0, 0)),
            whole(shared_slice),
        ],
        [
            pl.BlockSpec((1, token_rows, 2 * F), lambda e, m: (e, 0, 0)),
            pl.BlockSpec((1, token_rows, F), lambda e, m: (e, 0, 0)),
            whole(outs[2]),
            whole(outs[3]),
            whole(outs[4]),
        ],
        outs,
        [pltpu.VMEM((token_rows, width), jnp.float32)],
        2 * token_rows * width * 3 * (F * local_experts + shared_units),
        size_of(arrays) + size_of(outs),
    )


def weight_grad_kernel(pairs, core_at, meta, *refs):
    keep_ref, give_ref = refs[-2:]
    at = 0
    columns = 0
    parts = []
    for count in pairs:
        lefts, rights = refs[at : at + count], refs[at + count : at + 2 * count]
        at += 2 * count
        parts.append(
            sum(dot_first(a[...], b[0]) for a, b in zip(lefts, rights)).astype(jnp.bfloat16)
        )
    half = keep_ref.shape[1]

    for core, (first, second) in ((0, (keep_ref, give_ref)), (1, (give_ref, keep_ref))):

        @pl.when((meta[core_at] & 1) == core)
        def _():
            start = 0
            for part in parts:
                stop = start + part.shape[1]
                first[0, :, start:stop] = part[:half]
                second[0, :, start:stop] = part[half:]
                start = stop


def expert_grad_kernel(count, meta, *refs):
    rows, grads, front, acts = (refs[i * count : (i + 1) * count] for i in range(4))
    out_ref = refs[-1] if len(refs) == 4 * count + 1 else refs[-2]
    tile = rows[0].shape[1]
    both = 3 * F

    def pair(front_refs, act_refs):
        return [
            sum(dot_first(a[...], b[0]) for a, b in zip(left, right)).astype(jnp.bfloat16)
            for left, right in ((rows, front_refs), (grads, act_refs))
        ]

    left, right = pair(front, acts)
    out_ref[0, :tile, : left.shape[1]] = left
    out_ref[0, :tile, left.shape[1] : both] = right
    if len(refs) > 4 * count + 1:
        held = refs[-1]
        left, right = pair(refs[4 * count : 5 * count], refs[5 * count : 6 * count])
        split, columns = left.shape[1], left.shape[1] + right.shape[1]
        held[:, :split] = left
        held[:, split:] = right
        quarter = tile // 4
        first = 2 * meta[2]
        out_ref[0, tile:, :columns] = held[pl.ds(aligned(first, quarter), quarter), :]
        out_ref[0, tile:, columns:] = held[pl.ds(aligned(first + 1, quarter), quarter), :]


def expert_grad(meta, expert, half, rows, grads, front, acts, shared=None):
    count = len(rows)
    token_rows, width = rows[0].shape
    tile = width // 4
    arrays = list(rows) + list(grads) + list(front) + list(acts)
    column = pl.BlockSpec((token_rows, tile), lambda i, m: (0, i ^ m[0]))

    def of_expert(a):
        return pl.BlockSpec((1,) + a.shape[1:], lambda i, m: (m[1], 0, 0))

    in_specs = [column] * (2 * count) + [of_expert(a) for a in arrays[2 * count :]]
    below, scratch = 0, []
    if shared is not None:
        arrays += list(shared[0]) + list(shared[1])
        in_specs += [whole(a) for a in arrays[4 * count :]]
        below = tile // 4
        columns = shared[0][0].shape[-1] + shared[1][0].shape[-1]
        scratch = [pltpu.VMEM((tile, columns), jnp.bfloat16)]
    return call(
        functools.partial(expert_grad_kernel, count),
        "expert_grad",
        jnp.stack([meta[0] >> 1, expert, half]),
        arrays,
        (4,),
        in_specs,
        pl.BlockSpec((1, tile + below, 3 * F), lambda i, m: (i, 0, 0)),
        shape_of((4, tile + below, 3 * F), jnp.bfloat16),
        scratch,
        0,
        0,
    )


def weight_grad(meta, order, operands, index):
    token_rows, width = operands[0][0][0].shape
    tile = width // 4
    scalars = jnp.stack([order, meta[0]])
    arrays, in_specs, columns = [], [], 0
    for lefts, rights in operands:
        arrays += list(lefts) + list(rights)
        in_specs += [pl.BlockSpec((token_rows, tile), lambda i, m: (0, i ^ m[0]))] * len(lefts)
        units = rights[0].shape[-1]
        at = index if rights[0].shape[0] > 1 else 0
        in_specs += [
            pl.BlockSpec((1, token_rows, units), lambda i, m, at=at: (at, 0, 0))
        ] * len(rights)
        columns += units
    tokens = token_rows * len(operands[0][0])
    counts = [len(left) for left, _ in operands]
    outs = [shape_of((4, tile // 2, columns), jnp.bfloat16)] * 2
    return call(
        functools.partial(weight_grad_kernel, counts, 1),
        "weight_grad",
        scalars,
        arrays,
        (4,),
        in_specs,
        [pl.BlockSpec((1, tile // 2, columns), lambda i, m: (i, 0, 0))] * 2,
        outs,
        [],
        2 * tokens * width * columns,
        size_of(outs) + 4 * tokens * width + 2 * tokens * columns,
    )


def place_pair_kernel(meta, *refs):
    mine, other, out_ref = refs[-3:]
    rows = out_ref.shape[1]

    @pl.when(pl.program_id(0) == 0)
    def _():
        out_ref[0] = mine[0, :rows].astype(jnp.float32)

    @pl.when(pl.program_id(0) == 1)
    def _():
        out_ref[0] = other[0, :rows].astype(jnp.float32)


def place_pair(meta, total, index, shape, mine, other):
    _, rows, columns = mine.shape
    arrays = [mine, other]
    in_specs = [
        pl.BlockSpec((1, rows, columns), lambda k, r, m: ((1 - k) * r + 3 * k, 0, 0)),
        pl.BlockSpec((1, rows, columns), lambda k, r, m: (k * r, 0, 0)),
    ]
    aliases = {}
    if total is not None:
        arrays = [total] + arrays
        in_specs = [pl.BlockSpec(memory_space=pl.ANY)] + in_specs
        aliases = {1: 0}
    return pl.pallas_call(
        place_pair_kernel,
        grid_spec=pltpu.PrefetchScalarGridSpec(
            num_scalar_prefetch=1,
            grid=(2, 4),
            in_specs=in_specs,
            out_specs=pl.BlockSpec(
                (1, shape[1] // 4, shape[2]),
                lambda k, r, m: (2 * ((m[0] & 1) ^ k) + index, (m[0] >> 1) ^ r, 0),
            ),
        ),
        out_shape=shape_of(shape, jnp.float32),
        input_output_aliases=aliases,
        compiler_params=pltpu.CompilerParams(vmem_limit_bytes=48 * 1024 * 1024),
        cost_estimate=pl.CostEstimate(
            flops=int(COSTS.get("place_pair", 1.0) * 1e9), bytes_accessed=1000, transcendentals=0
        ),
        name="place_pair",
    )(meta, *arrays)


def place_shared_kernel(meta, mine_low, mine_high, other_low, other_high, out_ref):
    core = meta[0] & 1
    rows = mine_low.shape[1]
    for at, low, high in ((core, mine_low, mine_high), (1 - core, other_low, other_high)):
        out_ref[pl.ds(aligned(2 * at, rows), rows), :] = low[0].astype(jnp.float32)
        out_ref[pl.ds(aligned(2 * at + 1, rows), rows), :] = high[0].astype(jnp.float32)


def place_shared(meta, mine, other):
    _, rows, columns = mine.shape
    units = columns // 6
    low = pl.BlockSpec((1, rows, units), lambda i, j, m: (i, 0, j))
    high = pl.BlockSpec((1, rows, units), lambda i, j, m: (i, 0, 3 + j))
    outs = shape_of((4 * rows, 2 * columns), jnp.float32)
    return call(
        place_shared_kernel,
        "place_shared",
        meta,
        [mine, mine, other, other],
        (4, 3),
        [low, high, low, high],
        pl.BlockSpec((4 * rows, units), lambda i, j, m: (0, 4 * j + (m[1] ^ i))),
        outs,
        [],
        0,
        0,
    )


def place_heads_kernel(meta, *refs):
    mine, other, out_ref = refs[:4], refs[4], refs[5]
    core, chip = meta[0] & 1, meta[0] >> 1
    rows, columns = mine[0].shape
    group_width = columns - 2 * HEAD_SIZE
    for r in range(4):
        head = chip ^ r
        for at, pieces in ((core, [piece[...] for piece in mine]), (1 - core, other)):
            to = pl.ds(aligned(at, rows), rows)
            values = pieces[r].astype(jnp.float32)
            out_ref[to, pl.ds(aligned(head, group_width), group_width)] = values[:, :group_width]
            out_ref[to, pl.ds(aligned(4 * group_width // HEAD_SIZE + head, HEAD_SIZE), HEAD_SIZE)] = (
                values[:, group_width : group_width + HEAD_SIZE]
            )
            out_ref[
                to, pl.ds(aligned(4 * group_width // HEAD_SIZE + 4 + head, HEAD_SIZE), HEAD_SIZE)
            ] = values[:, group_width + HEAD_SIZE :]


def place_heads(meta, mine, other):
    rows, columns = mine[0].shape
    arrays = list(mine) + [other]
    outs = shape_of((2 * rows, 4 * columns), jnp.float32)
    return call(
        place_heads_kernel,
        "place_heads",
        meta,
        arrays,
        (1,),
        [whole(a) for a in arrays],
        whole(outs),
        outs,
        [],
        0,
        size_of(arrays + [outs]),
    )


def join_shared_kernel(meta, mine, other, out_ref):
    step = pl.program_id(0)
    rows = mine.shape[2]
    first = meta[0] ^ (2 * step)
    for i in range(4):
        at = 8 * (meta[1] ^ i)
        out_ref[pl.ds(aligned(at + first, rows), rows), :] = mine[0, i]
        out_ref[pl.ds(aligned(at + (first ^ 1), rows), rows), :] = other[0, i]


def join_shared(meta, mine, other):
    _, _, rows, columns = mine.shape
    block = pl.BlockSpec((1, 4, rows, columns), lambda r, m: (r, 0, 0, 0))
    outs = shape_of((32 * rows, columns), jnp.bfloat16)
    return call(
        join_shared_kernel,
        "join_shared",
        meta,
        [mine, other],
        (4,),
        [block, block],
        whole(outs),
        outs,
        [],
        0,
        size_of([mine, other, outs]),
    )


class Clock:
    def __init__(self):
        self.last = None

    def __call__(self, *values):
        if self.last is None:
            return values if len(values) > 1 else values[0]
        held = lax.optimization_barrier(tuple(values) + (self.last,))[:-1]
        return held if len(held) > 1 else held[0]

    def mark(self, value):
        self.last = value
        return value


EARLY = (
    "H", "W", "K", "S", "K", "W", "S", "W", "K", "S", "O", "S", "M", "M", "S", "O", "M", "S", "M", "R", "M", "K", "M", "K",
    "M", "K", "R", "M", "K", "M", "M", "M", "M", "R", "M", "M",
)
LATE = (
    "L", "0", "0", "0", "1", "L", "1", "1", "L", "L", "O", "0", "1", "L", "L", "1", "0", "O", "Q", "1", "O", "L", "Q", "0",
    "O", "L", "Q", "Q", "O", "Q", "1", "0", "O", "Q", "S", "O", "Q", "1", "0", "S", "O", "Q", "L", "L", "L", "Q", "O", "S",
    "L",
)


def fast_device(
    hidden,
    teacher,
    valid_mask,
    routes,
    route_gates,
    gain_in,
    query_key_value_weight,
    out_weight,
    gain_mid,
    shared_weight,
    expert_weight,
):
    token_rows, width = hidden.shape[1:]
    context_count, shard_count = 8, 4
    context_index = lax.axis_index("ctx").astype(jnp.int32)
    shard_index = lax.axis_index("wt").astype(jnp.int32)
    plain_meta = jnp.stack([context_index, shard_index])
    core = context_index & 1
    chip = context_index >> 1
    at_end = (shard_index == 0) | (shard_index == shard_count - 1)
    group_width = QUERY_HEADS // KEY_VALUE_HEADS * HEAD_SIZE
    query_width = QUERY_HEADS * HEAD_SIZE
    kv_width = KEY_VALUE_HEADS * HEAD_SIZE
    scale = 1.0 / math.sqrt(HEAD_SIZE)
    all_tokens = token_rows * context_count * shard_count
    shard_rows = query_key_value_weight.shape[0]
    half_rows = shard_rows // 2
    local_experts = expert_weight.shape[0]
    bf16, f32 = jnp.bfloat16, jnp.float32
    states = hidden[0]
    clock = Clock()
    have = {}

    def meta():
        return clock(plain_meta)

    def now(*values):
        return clock(*values)

    def ready(*values):
        values = clock(*values)
        clock.mark(values[0] if isinstance(values, tuple) or isinstance(values, list) else values)
        return values


    def hidden_chain():
        have["blocks"] = chips_exchange(jnp.broadcast_to(states, (4,) + states.shape))
        yield

    def qkv_chain():
        rows = lax.dynamic_slice_in_dim(query_key_value_weight, core * half_rows, half_rows, 0)
        half = jnp.concatenate(
            [
                lax.dynamic_slice_in_dim(rows, chip * group_width, group_width, 1),
                lax.dynamic_slice_in_dim(rows, query_width + chip * HEAD_SIZE, HEAD_SIZE, 1),
                lax.dynamic_slice_in_dim(
                    rows, query_width + kv_width + chip * HEAD_SIZE, HEAD_SIZE, 1
                ),
            ],
            axis=1,
        )
        came = line_swap(half, 1)
        yield
        pair = clock.mark(jnp.stack([half, now(came)]))
        came = line_swap(pair, 2)
        yield
        have["qkv_mine"] = clock.mark(jnp.concatenate([pair, now(came)]))
        have["qkv_other"] = flip(have["qkv_mine"], 1)
        yield

    def small_chain():
        expert_ids = jnp.arange(EXPERTS, dtype=jnp.int32)
        matrix = jnp.sum(
            jnp.where(
                routes[0][None, :, :] == expert_ids[:, None, None], route_gates[0][None, :, :], 0.0
            ),
            axis=-1,
        )
        have["valid"] = valid_mask[0].astype(f32)
        gains = jnp.concatenate([gain_in, gain_mid]).astype(f32).reshape(-1, token_rows)
        gain_rows = gains.shape[0]
        filled = EXPERTS + gain_rows
        pack = jnp.concatenate(
            [
                matrix,
                gains,
                jnp.full((32 - filled, token_rows), jnp.sum(have["valid"]), f32),
            ]
        )
        came = line_swap(pack, 1)
        yield
        pair = clock.mark(jnp.stack([pack, now(came)]))
        came = line_swap(pair, 2)
        yield
        all_packs = clock.mark(jnp.concatenate([pair, now(came)]))
        have["gates"] = [
            lax.dynamic_slice_in_dim(
                all_packs[i], shard_index * local_experts, local_experts, 0
            )[..., None]
            for i in range(4)
        ]
        gains = all_packs[:, EXPERTS:filled].reshape(4, 2, shard_rows)
        gains = jnp.stack([pick(gains, shard_index ^ i) for i in range(4)], axis=1)
        have["gains"] = gains.reshape(2, 1, width)
        total = jnp.broadcast_to(jnp.sum(all_packs[:, filled, 0]), (8, 128))
        yield
        total = now(total)
        for bit in (1, 2, 4):
            came = flip(total, bit)
            yield
            total = clock.mark(total + now(came))
        have["count"] = total[0, 0]
        yield

    def shared_chain():
        eighth = shard_rows // 8
        units = SF // shard_count
        piece = lax.dynamic_slice_in_dim(shared_weight, context_index * eighth, eighth, 0)
        piece = piece.reshape(eighth, 3, shard_count, units)

        piece = jnp.transpose(piece, (2, 0, 1, 3)).reshape(shard_count, eighth, 3 * units)
        parts = [pick(piece, shard_index ^ i) for i in range(4)]
        came = line_swap(now(jnp.stack([parts[1], parts[3]])), 1)
        yield
        came = now(came)
        mine = jnp.stack([parts[0], came[0]])
        came = line_swap(clock.mark(jnp.stack([parts[2], came[1]])), 2)
        yield
        pieces = clock.mark(jnp.concatenate([mine, now(came)]))
        came = flip(pieces, 2)
        yield
        pair = clock.mark(jnp.stack([pieces, now(came)]))
        came = flip(pair, 4)
        yield
        mine = clock.mark(jnp.concatenate([pair, now(came)]))
        other = flip(mine, 1)
        yield
        have["shared"] = join_shared(meta(), mine, other)
        clock.mark(have["shared"])
        yield

    def out_chain():
        half = lax.dynamic_slice_in_dim(now(out_weight), core * half_rows, half_rows, 0)
        came = line_exchange(jnp.broadcast_to(half, (4,) + half.shape))
        yield
        have["out_mine"] = clock.mark(now(came))
        have["out_other"] = flip(have["out_mine"], 1)
        yield

    def qkv_all_chain():
        half = lax.dynamic_slice_in_dim(
            now(have["qkv_slice"]), core * (width // 2), width // 2, 0
        )
        came = flip(half, 2)
        yield
        pair = clock.mark(jnp.stack([half, now(came)]))
        came = flip(pair, 4)
        yield
        have["rel_mine"] = clock.mark(jnp.concatenate([pair, now(came)]))
        have["rel_other"] = flip(have["rel_mine"], 1)
        yield

    def main_chain():
        gains = have["gains"]
        normed_in, query, pair, qkv_slice = project(
            meta(), have["blocks"], gains[0], have["qkv_mine"], have["qkv_other"], group_width
        )
        clock.mark(pair)
        have["normed_in"], have["qkv_slice"] = normed_in, qkv_slice
        pair_other = flip(pair, 1)
        yield
        mixed_heads, log_total = attend(meta(), query, pair, pair_other, scale)
        clock.mark(log_total)
        have["attend"] = (query, pair, pair_other, log_total, mixed_heads)
        parts = ready(*[pick(mixed_heads, chip ^ r) for r in range(4)])
        mixed = [parts[0]] + [flip(parts[r], 2 * r) for r in (1, 2, 3)]
        have["mixed"] = mixed
        yield
        out_full, middle, normed_mid = leave(
            meta(), mixed, have["out_mine"], have["out_other"], states, gains[1]
        )
        have["out_full"], have["middle"] = out_full, middle
        clock.mark(normed_mid)

        near, center = line_swap(normed_mid, 1), line_middle(normed_mid)
        yield
        gates, shared_slice = have["gates"], have["shared"]
        gate_ups, shared_gate_ups, outs = [], [], []

        def forward(rows, i):
            result = experts(meta(), rows, gates[i], expert_weight, shared_slice)
            clock.mark(result[2])
            gate_ups.append(result[0])
            shared_gate_ups.append(result[1])
            outs.append(result[2])

        forward(normed_mid, 0)
        yield
        near, center = now(near, center)
        far, outward = line_middle(near), line_outward(center)
        forward(near, 1)
        yield
        far, outward = now(far, outward)
        outward_far = line_outward(far)
        third = clock.mark(jnp.where(at_end, outward, far))
        forward(third, 2)
        yield
        outward_far = now(outward_far)
        fourth = clock.mark(jnp.where(at_end, outward_far, center))
        forward(fourth, 3)
        line_rows = [normed_mid, near, third, fourth]
        came = line_inward(outs[3])
        yield
        carried = clock.mark(outs[2] + now(came))
        inward, crossed = line_inward(carried), line_middle(carried)
        yield
        inward, crossed = now(inward, crossed)
        near_out, middle_out = ready(outs[1] + crossed, outs[3] + inward)
        near_out, middle_out = line_swap(near_out, 1), line_middle(middle_out)
        yield
        near_out, middle_out = now(near_out, middle_out)
        final_state = (
            middle + outs[0].astype(f32) + near_out.astype(f32) + middle_out.astype(f32)
        )
        valid = have["valid"]
        deviation = final_state - teacher[0].astype(f32)
        have["squared"] = jnp.sum(valid[:, None] * deviation * deviation)
        grad_final = all_tokens / have["count"] * valid[:, None] * deviation
        have["final"], have["grad_final"] = final_state.astype(bf16)[None], grad_final
        grad_low = clock.mark(grad_final.astype(bf16))
        near, center = line_swap(grad_low, 1), line_middle(grad_low)
        yield
        kept = []

        def backward(grads, i):
            kept.append(
                experts_back(
                    meta(),
                    grads,
                    gates[i],
                    gate_ups[i],
                    shared_gate_ups[i],
                    expert_weight,
                    shared_slice,
                )
            )
            clock.mark(kept[-1][4])

        backward(grad_low, 0)
        yield
        near, center = now(near, center)
        far, outward = line_middle(near), line_outward(center)
        backward(near, 1)
        yield
        far, outward = now(far, outward)
        outward_far = line_outward(far)
        third = clock.mark(jnp.where(at_end, outward, far))
        backward(third, 2)
        yield
        outward_far = now(outward_far)
        fourth = clock.mark(jnp.where(at_end, outward_far, center))
        backward(fourth, 3)
        have["line"] = (line_rows, [grad_low, near, third, fourth])
        have["experts"] = list(zip(*kept))
        yield


    def states_chain():
        outs = have["experts"][4]
        came = line_inward(outs[3])
        yield
        carried = clock.mark(outs[2] + now(came))
        inward, crossed = line_inward(carried), line_middle(carried)
        yield
        inward, crossed = now(inward, crossed)
        near_out, middle_out = ready(outs[1] + crossed, outs[3] + inward)
        near_out, middle_out = line_swap(near_out, 1), line_middle(middle_out)
        yield
        near_out, middle_out = now(near_out, middle_out)
        grad_normed = clock.mark(
            outs[0].astype(f32) + near_out.astype(f32) + middle_out.astype(f32)
        )
        grad_middle, grad_branch, grad_gain_mid, grad_mixed = enter_back(
            meta(),
            have["grad_final"],
            grad_normed,
            have["middle"],
            have["gains"][1],
            have["out_full"],
        )
        clock.mark(grad_branch)
        have["grad_branch"], have["grad_gain_mid"] = grad_branch, grad_gain_mid
        grad_mixed = chips_exchange(ready(grad_mixed))
        yield
        query, pair, pair_other, log_total, mixed_heads = have["attend"]
        grad_query, grad_pair, grad_other = attend_back(
            meta(), query, pair, pair_other, log_total, mixed_heads, grad_mixed, scale
        )
        clock.mark(grad_query)
        came = flip(grad_other, 1)
        yield
        grad_pair = grad_pair + now(came).astype(f32)
        projected = clock.mark(jnp.concatenate([grad_query, grad_pair.astype(bf16)], axis=-1))
        have["grad_projected"] = projected
        parts = chips_exchange(ready(projected))
        yield
        grad_hidden, grad_gain_in = finish(
            meta(),
            parts,
            have["rel_mine"],
            have["rel_other"],
            states,
            grad_middle,
            have["gains"][0],
        )
        clock.mark(grad_gain_in)
        have["grad_hidden"] = grad_hidden
        sums = jnp.concatenate(
            [grad_gain_in, have["grad_gain_mid"], jnp.full((6, width), have["squared"], f32)],
            axis=0,
        )
        for offset in (1, 2):
            came = line_swap(sums, offset)
            yield
            sums = clock.mark(sums + now(came))
        for bit in (1, 2, 4):
            came = flip(sums, bit)
            yield
            sums = clock.mark(sums + now(came))
        own = lax.dynamic_slice_in_dim(sums, shard_index * shard_rows, shard_rows, 1)
        have["sums"] = (own, 0.5 * sums[2, 0] / (have["count"] * width))
        yield

    def expert_chain(index):
        line_rows, line_grads = have["line"]
        grad_gate_ups, acts, shared_grads, shared_acts = have["experts"][:4]
        shared = (shared_grads, shared_acts) if index == 0 else None

        def grad_of(at):
            return clock.mark(
                expert_grad(
                    meta(),
                    2 * at + index,
                    at,
                    line_rows,
                    line_grads,
                    grad_gate_ups,
                    acts,
                    shared,
                )
            )

        if index == 0:
            came = flip(grad_of(1 - core), 1)
            yield
            keep = grad_of(core)
            yield
        else:
            keep = grad_of(core)
            yield
            came = flip(grad_of(1 - core), 1)
            yield
        x_first = index % 2 == 0
        first, second = (2, 4) if x_first else (4, 2)
        picked = ((1, 3), (0, 2)) if x_first else ((2, 3), (0, 1))
        pieces = keep.shape[1] // 96

        def split_sum(keep, came):
            return [
                jnp.stack([keep[i] + came[i] for i in places]) for places in picked
            ]

        give, keep = blend(meta(), "blend_split", split_sum, [keep, came], pieces)
        clock.mark(give)
        came = flip(give, first)
        yield
        give, keep = blend(
            meta(), "blend_pair", lambda k, c: [k[1] + c[1], k[0] + c[0]], [keep, came], pieces
        )
        clock.mark(give)
        came = flip(give, second)
        yield
        own = clock.mark(blend(meta(), "blend_sum", lambda k, c: k + c, [keep, came], pieces))
        came = flip(own, second)
        yield
        pair = clock.mark(
            blend(meta(), "blend_stack", lambda a, b: jnp.stack([a, b]), [own, came], pieces)
        )
        came = flip(pair, first)
        yield

        def stack_four(near, far):
            if x_first:
                return jnp.stack([near[0], far[0], near[1], far[1]])
            return jnp.stack([near[0], near[1], far[0], far[1]])

        stacked = clock.mark(blend(meta(), "blend_four", stack_four, [pair, came], pieces))
        other = flip(stacked, 1)
        if index == 0:
            have["shared_sum"] = stacked[:, shard_rows:]
        yield
        have["grad_experts"] = place_pair(
            meta(), have.get("grad_experts"), index, expert_weight.shape, stacked, other
        )
        clock.mark(have["grad_experts"])
        yield

    def shared_grad_chain():
        total = now(have["shared_sum"])
        parts = ready(*[pick(total, chip ^ shard_index ^ i) for i in range(4)])
        came = [line_swap(parts[i], i) for i in (1, 2, 3)]
        yield
        mine = clock.mark(jnp.stack([parts[0]] + list(now(*came))))
        other = flip(mine, 1)
        yield
        have["grad_shared"] = clock.mark(place_shared(meta(), mine, other))
        yield

    def line_reduce_steps(keep, came):
        came = now(came)
        parts = [keep[i] + came[i] for i in range(4)]
        came = line_inward(clock.mark(parts[3]))
        yield
        carried = clock.mark(parts[2] + now(came))
        inward, crossed = line_inward(carried), line_middle(carried)
        yield
        inward, crossed = now(inward, crossed)
        near_out, middle_out = ready(parts[1] + crossed, parts[3] + inward)
        near_out, middle_out = line_swap(near_out, 1), line_middle(middle_out)
        yield
        near_out, middle_out = now(near_out, middle_out)
        have["line_sum"] = clock.mark(
            (parts[0].astype(f32) + near_out.astype(f32) + middle_out.astype(f32)).astype(bf16)
        )

    def out_grad_chain():
        mixed = jnp.concatenate(have["mixed"], axis=1)
        keep, give = weight_grad(
            meta(), chip ^ shard_index, [([mixed], [have["grad_branch"][None]])], 0
        )
        clock.mark(keep)
        came = flip(give, 1)
        yield
        yield from line_reduce_steps(keep, came)
        total = have["line_sum"]
        yield
        total = ready(total)
        came = flip(total, 2)
        yield
        total = clock.mark(total + now(came))
        came = flip(total, 4)
        yield
        mine = clock.mark(total + now(came))
        other = flip(mine, 1)
        yield
        mine, other = now(mine, other)
        have["grad_out"] = clock.mark(
            jnp.where(
                core == 0,
                jnp.concatenate([mine, other], axis=0),
                jnp.concatenate([other, mine], axis=0),
            ).astype(f32)
        )
        yield

    def qkv_grad_chain():
        normed_in = have["normed_in"].reshape(4 * token_rows, width)
        projected = have["grad_projected"].reshape(1, 4 * token_rows, -1)
        keep, give = weight_grad(meta(), shard_index, [([normed_in], [projected])], 0)
        clock.mark(keep)
        came = flip(give, 1)
        yield
        yield from line_reduce_steps(keep, came)
        own = have["line_sum"]
        yield
        own = ready(own)
        came = flip(own, 2)
        yield
        pair = clock.mark(jnp.stack([own, now(came)]))
        came = flip(pair, 4)
        yield
        mine = clock.mark(jnp.concatenate([pair, now(came)]))
        other = flip(mine, 1)
        yield
        have["grad_qkv"] = clock.mark(place_heads(meta(), [mine[r] for r in range(4)], other))
        yield

    early = {
        "H": hidden_chain(),
        "W": qkv_chain(),
        "S": shared_chain(),
        "O": out_chain(),
        "K": small_chain(),
        "R": qkv_all_chain(),
        "M": main_chain(),
    }
    late = {
        "L": states_chain(),
        "S": shared_grad_chain(),
        "O": out_grad_chain(),
        "Q": qkv_grad_chain(),
    }
    for index in range(local_experts // 2):
        late[str(index)] = expert_chain(index)
    for chains, order in ((early, EARLY), (late, LATE)):
        for name in order:
            next(chains[name], None)
        for name in chains:
            for _ in chains[name]:
                pass

    own, loss_value = have["sums"]
    return (
        have["final"],
        loss_value,
        have["grad_hidden"],
        own[0],
        have["grad_qkv"],
        have["grad_out"],
        own[1],
        have["grad_shared"],
        have["grad_experts"],
    )


def solution(mesh):
    in_specs = (
        P("wt", "ctx", None),
        P("wt", "ctx", None),
        P("wt", "ctx"),
        P("wt", "ctx", None),
        P("wt", "ctx", None),
        P("wt"),
        P("wt", None),
        P("wt", None),
        P("wt"),
        P("wt", None),
        P("wt", None, None),
    )
    out_specs = (
        P("wt", "ctx", None),
        P(),
        P("wt", "ctx", None),
        P("wt"),
        P("wt", None),
        P("wt", None),
        P("wt"),
        P("wt", None),
        P("wt", None, None),
    )
    plane_of_eight = dict(mesh.shape) == {"ctx": 8, "wt": 4}
    return jax.shard_map(
        fast_device if plane_of_eight else on_device, mesh=mesh, in_specs=in_specs, out_specs=out_specs, check_vma=False
    )
```

```python
import functools
import math

import jax
import jax.numpy as jnp
from jax import lax
from jax.experimental import pallas as pl
from jax.experimental.pallas import tpu as pltpu
from jax.sharding import PartitionSpec as P

QUERY_HEADS = 12
KEY_VALUE_HEADS = 4
HEAD_SIZE = 128
F = 512
SF = 1024
EXPERTS = 16
TOP = 6


norm_eps = 1e-05
masked_score = -1e30


def sigmoid_linear(values):
    return values * jax.nn.sigmoid(values)


def silu_slope(values):
    sigma_value = jax.nn.sigmoid(values)
    return sigma_value * (1.0 + values * (1.0 - sigma_value))


def normalize(values):
    inverse = lax.rsqrt(jnp.mean(values * values, axis=-1, keepdims=True) + norm_eps)
    return (values * inverse, inverse)


def norm_back(grad_normed, scaled, inverse, gain_vector):
    grad_scaled = grad_normed * gain_vector
    return inverse * (grad_scaled - scaled * jnp.mean(grad_scaled * scaled, axis=-1, keepdims=True))


def positions(row_ids, token_rows, context_count):
    piece_index = row_ids // token_rows
    within = row_ids % token_rows
    half_rows = token_rows // 2
    mirrored = jnp.where(within < half_rows, piece_index, 2 * context_count - 1 - piece_index)
    return mirrored * half_rows + within % half_rows


def route_tables(local_routes, local_gates, experts, capacity):
    token_rows = local_routes.shape[0]
    flat_routes = local_routes.reshape(-1)
    one_hot = (flat_routes[:, None] == jnp.arange(experts, dtype=jnp.int32)[None, :]).astype(
        jnp.int32
    )
    earlier = jnp.cumsum(one_hot, axis=0) - one_hot
    slot_index = jnp.sum(earlier * one_hot, axis=1)
    token_index = jnp.arange(flat_routes.shape[0], dtype=jnp.int32) // local_routes.shape[1]
    slot_table = (
        jnp.full((experts, capacity), token_rows, jnp.int32)
        .at[flat_routes, slot_index]
        .set(token_index)
    )
    slot_gate = (
        jnp.zeros((experts, capacity), jnp.float32)
        .at[flat_routes, slot_index]
        .set(local_gates.reshape(-1))
    )
    return (slot_table, slot_gate)


def block_scores(query_rows, key_block, key_position, query_place, score_scale):
    scores = (
        jnp.einsum("qhgd,khd->qhgk", query_rows, key_block, preferred_element_type=jnp.float32)
        * score_scale
    )
    allowed = key_position[None, None, None, :] <= query_place[:, None, None, None]
    return jnp.where(allowed, scores, masked_score)


def attend_forward(
    query_rows, blocked_keys, blocked_values, place_blocks, query_place, score_scale
):
    head_shape = query_rows.shape[:3]

    def online_step(running, block_args):
        running_max, running_sum, accumulated = running
        key_block, value_block, key_position = block_args
        scores = block_scores(query_rows, key_block, key_position, query_place, score_scale)
        new_max = jnp.maximum(running_max, jnp.max(scores, axis=-1))
        rescale = jnp.exp(running_max - new_max)
        powers = jnp.exp(scores - new_max[..., None])
        new_sum = running_sum * rescale + jnp.sum(powers, axis=-1)
        weighted = jnp.einsum(
            "qhgk,khd->qhgd",
            powers.astype(jnp.bfloat16),
            value_block,
            preferred_element_type=jnp.float32,
        )
        return ((new_max, new_sum, accumulated * rescale[..., None] + weighted), None)

    initial = (
        jnp.full(head_shape, masked_score, jnp.float32),
        jnp.zeros(head_shape, jnp.float32),
        jnp.zeros(query_rows.shape, jnp.float32),
    )
    row_max, row_sum, accumulated = lax.scan(
        online_step, initial, (blocked_keys, blocked_values, place_blocks)
    )[0]
    log_total = row_max + jnp.log(row_sum)
    return (accumulated / row_sum[..., None], log_total)


def attend_backward(
    query_rows,
    blocked_keys,
    blocked_values,
    place_blocks,
    query_place,
    log_total,
    attention_output_gradient,
    attention_output,
    score_scale,
):
    row_delta = jnp.sum(attention_output_gradient.astype(jnp.float32) * attention_output, axis=-1)

    def block_grads(grad_queries, block_args):
        key_block, value_block, key_position = block_args
        scores = block_scores(query_rows, key_block, key_position, query_place, score_scale)
        probabilities = jnp.exp(scores - log_total[..., None])
        grad_probs = jnp.einsum(
            "qhgd,khd->qhgk",
            attention_output_gradient,
            value_block,
            preferred_element_type=jnp.float32,
        )
        grad_scores = (probabilities * (grad_probs - row_delta[..., None])).astype(jnp.bfloat16)
        grad_queries = grad_queries + jnp.einsum(
            "qhgk,khd->qhgd", grad_scores, key_block, preferred_element_type=jnp.float32
        )
        grad_keys = (
            jnp.einsum(
                "qhgk,qhgd->khd", grad_scores, query_rows, preferred_element_type=jnp.float32
            )
            * score_scale
        )
        grad_values = jnp.einsum(
            "qhgk,qhgd->khd",
            probabilities.astype(jnp.bfloat16),
            attention_output_gradient,
            preferred_element_type=jnp.float32,
        )
        return (grad_queries, (grad_keys, grad_values))

    grad_queries, (grad_keys, grad_values) = lax.scan(
        block_grads,
        jnp.zeros(query_rows.shape, jnp.float32),
        (blocked_keys, blocked_values, place_blocks),
    )
    return (grad_queries * score_scale, grad_keys, grad_values)


def gate_up_grads(grad_act, gate_up, hidden_units):
    gate_part = gate_up[..., :hidden_units]
    up_part = gate_up[..., hidden_units:]
    return jnp.concatenate(
        [grad_act * up_part * silu_slope(gate_part), grad_act * sigmoid_linear(gate_part)], axis=-1
    ).astype(jnp.bfloat16)


def on_device(
    hidden,
    teacher,
    valid_mask,
    routes,
    route_gates,
    gain_in,
    query_key_value_weight,
    out_weight,
    gain_mid,
    shared_weight,
    expert_weight,
):
    token_rows = hidden.shape[1]
    model_width = hidden.shape[2]
    context_count = lax.axis_size("ctx")
    shard_count = lax.axis_size("wt")
    seq_rows = token_rows * context_count
    all_tokens = seq_rows * shard_count
    query_groups = QUERY_HEADS // KEY_VALUE_HEADS
    query_total_width = QUERY_HEADS * HEAD_SIZE
    key_value_width = KEY_VALUE_HEADS * HEAD_SIZE
    score_scale = 1.0 / math.sqrt(HEAD_SIZE)
    key_row_count = min(512, seq_rows)
    number_of_blocks = seq_rows // key_row_count
    capacity = token_rows * TOP // 12
    local_experts = expert_weight.shape[0]
    contract_last = (((1,), (1,)), ((), ()))
    contract_first = (((0,), (0,)), ((), ()))
    full_gain_in, full_qkv, full_out, full_gain_mid, full_shared = (
        lax.all_gather(gain_in, "wt", axis=0, tiled=True),
        lax.all_gather(query_key_value_weight, "wt", axis=0, tiled=True),
        lax.all_gather(out_weight, "wt", axis=0, tiled=True),
        lax.all_gather(gain_mid, "wt", axis=0, tiled=True),
        lax.all_gather(shared_weight, "wt", axis=0, tiled=True),
    )
    gain_in_float = full_gain_in.astype(jnp.float32)
    gain_mid_float = full_gain_mid.astype(jnp.float32)
    inputs = hidden[0].astype(jnp.float32)
    scaled_in, inverse_in = normalize(inputs)
    normed_in = (scaled_in * gain_in_float).astype(jnp.bfloat16)
    projected_rows = jnp.dot(normed_in, full_qkv, preferred_element_type=jnp.float32).astype(
        jnp.bfloat16
    )
    query_rows = projected_rows[:, :query_total_width].reshape(
        token_rows, KEY_VALUE_HEADS, query_groups, HEAD_SIZE
    )
    context_local = projected_rows[:, query_total_width:]
    context_gathered = lax.all_gather(context_local, "ctx", axis=0, tiled=True)
    context_index = lax.axis_index("ctx")
    query_place = positions(
        context_index * token_rows + jnp.arange(token_rows, dtype=jnp.int32),
        token_rows,
        context_count,
    )
    place_blocks = positions(
        jnp.arange(seq_rows, dtype=jnp.int32), token_rows, context_count
    ).reshape(number_of_blocks, key_row_count)
    blocked_keys = context_gathered[:, :key_value_width].reshape(
        number_of_blocks, key_row_count, KEY_VALUE_HEADS, HEAD_SIZE
    )
    blocked_values = context_gathered[:, key_value_width:].reshape(
        number_of_blocks, key_row_count, KEY_VALUE_HEADS, HEAD_SIZE
    )
    attention_output, log_total = attend_forward(
        query_rows, blocked_keys, blocked_values, place_blocks, query_place, score_scale
    )
    mixed_rows = attention_output.reshape(token_rows, query_total_width).astype(jnp.bfloat16)
    middle = inputs + jnp.dot(mixed_rows, full_out, preferred_element_type=jnp.float32)
    scaled_mid, inverse_mid = normalize(middle)
    normed_mid = (scaled_mid * gain_mid_float).astype(jnp.bfloat16)
    shared_gate_up = jnp.dot(
        normed_mid, full_shared[:, : 2 * SF], preferred_element_type=jnp.float32
    )
    shared_act = (sigmoid_linear(shared_gate_up[:, :SF]) * shared_gate_up[:, SF:]).astype(
        jnp.bfloat16
    )
    shared_out = lax.dot_general(
        shared_act, full_shared[:, 2 * SF :], contract_last, preferred_element_type=jnp.float32
    )
    slot_table, slot_gate = route_tables(routes[0], route_gates[0], EXPERTS, capacity)
    padded_rows = jnp.concatenate([normed_mid, jnp.zeros((1, model_width), jnp.bfloat16)], axis=0)
    expert_rows = jnp.take(padded_rows, slot_table, axis=0)
    arrived = lax.all_to_all(expert_rows, "wt", split_axis=0, concat_axis=0, tiled=True)
    slot_count = arrived.shape[1]
    grouped = arrived.reshape(shard_count, local_experts, slot_count, model_width)
    owner_gate_up = jnp.einsum(
        "wesd,edf->wesf", grouped, expert_weight[:, :, : 2 * F], preferred_element_type=jnp.float32
    )
    owner_act = (sigmoid_linear(owner_gate_up[..., :F]) * owner_gate_up[..., F:]).astype(
        jnp.bfloat16
    )
    owner_out = jnp.einsum(
        "wesf,edf->wesd",
        owner_act,
        expert_weight[:, :, 2 * F :],
        preferred_element_type=jnp.float32,
    ).astype(jnp.bfloat16)
    returned = lax.all_to_all(
        owner_out.reshape(shard_count * local_experts, slot_count, model_width),
        "wt",
        split_axis=0,
        concat_axis=0,
        tiled=True,
    )
    expert_out, owner_rows, owner_gate_up, owner_act = (
        returned,
        arrived,
        owner_gate_up.reshape(shard_count * local_experts, slot_count, 2 * F),
        owner_act.reshape(shard_count * local_experts, slot_count, F),
    )
    routed = (
        jnp.zeros((token_rows + 1, model_width), jnp.float32)
        .at[slot_table]
        .add(expert_out.astype(jnp.float32) * slot_gate[..., None])[:token_rows]
    )
    final_state = middle + shared_out + routed
    valid_float = valid_mask[0].astype(jnp.float32)
    deviation = final_state - teacher[0].astype(jnp.float32)
    squared_local = jnp.sum(valid_float[:, None] * deviation * deviation)
    count_local = jnp.sum(valid_float)
    squared_total, valid_count = lax.psum((squared_local, count_local), ("ctx", "wt"))
    loss_value = 0.5 * squared_total / (valid_count * model_width)
    grad_final = all_tokens / valid_count * valid_float[:, None] * deviation
    grad_shared_out = grad_final.astype(jnp.bfloat16)
    grad_shared_act = jnp.dot(
        grad_shared_out, full_shared[:, 2 * SF :], preferred_element_type=jnp.float32
    )
    grad_shared_down = lax.dot_general(
        grad_shared_out, shared_act, contract_first, preferred_element_type=jnp.float32
    )
    grad_shared_gate_up = gate_up_grads(grad_shared_act, shared_gate_up, SF)
    grad_normed_mid = lax.dot_general(
        grad_shared_gate_up,
        full_shared[:, : 2 * SF],
        contract_last,
        preferred_element_type=jnp.float32,
    )
    grad_shared_front = lax.dot_general(
        normed_mid, grad_shared_gate_up, contract_first, preferred_element_type=jnp.float32
    )
    grad_shared_full = jnp.concatenate([grad_shared_front, grad_shared_down], axis=1)
    padded_grads = jnp.concatenate([grad_final, jnp.zeros((1, model_width), jnp.float32)], axis=0)
    grad_expert_out = (jnp.take(padded_grads, slot_table, axis=0) * slot_gate[..., None]).astype(
        jnp.bfloat16
    )
    grad_arrived = lax.all_to_all(grad_expert_out, "wt", split_axis=0, concat_axis=0, tiled=True)
    grad_grouped = grad_arrived.reshape(shard_count, local_experts, capacity, model_width)
    owner_gate_up_grouped = owner_gate_up.reshape(shard_count, local_experts, capacity, 2 * F)
    owner_act_grouped = owner_act.reshape(shard_count, local_experts, capacity, F)
    owner_rows_grouped = owner_rows.reshape(shard_count, local_experts, capacity, model_width)
    grad_owner_act = jnp.einsum(
        "wecd,edf->wecf",
        grad_grouped,
        expert_weight[:, :, 2 * F :],
        preferred_element_type=jnp.float32,
    )
    grad_owner_gate_up = gate_up_grads(grad_owner_act, owner_gate_up_grouped, F)
    grad_owner_rows = jnp.einsum(
        "wecf,edf->wecd",
        grad_owner_gate_up,
        expert_weight[:, :, : 2 * F],
        preferred_element_type=jnp.float32,
    ).astype(jnp.bfloat16)
    front = jnp.einsum(
        "wecd,wecf->edf", owner_rows_grouped, grad_owner_gate_up, preferred_element_type=jnp.float32
    )
    back = jnp.einsum(
        "wecd,wecf->edf", grad_grouped, owner_act_grouped, preferred_element_type=jnp.float32
    )
    expert_grad = jnp.concatenate([front, back], axis=2)
    grad_rows = lax.all_to_all(
        grad_owner_rows.reshape(shard_count * local_experts, capacity, model_width),
        "wt",
        split_axis=0,
        concat_axis=0,
        tiled=True,
    )
    grad_normed_mid = (
        grad_normed_mid
        + jnp.zeros((token_rows + 1, model_width), jnp.float32)
        .at[slot_table]
        .add(grad_rows.astype(jnp.float32))[:token_rows]
    )
    grad_gain_mid_local = jnp.sum(grad_normed_mid * scaled_mid, axis=0)
    grad_middle = grad_final + norm_back(grad_normed_mid, scaled_mid, inverse_mid, gain_mid_float)
    grad_branch = grad_middle.astype(jnp.bfloat16)
    mixed_gradient = lax.dot_general(
        grad_branch, full_out, contract_last, preferred_element_type=jnp.float32
    ).astype(jnp.bfloat16)
    grad_out_local = lax.dot_general(
        mixed_rows, grad_branch, contract_first, preferred_element_type=jnp.float32
    )
    context_recomputed = lax.all_gather(context_local, "ctx", axis=0, tiled=True)
    backward_keys = context_recomputed[:, :key_value_width].reshape(
        number_of_blocks, key_row_count, KEY_VALUE_HEADS, HEAD_SIZE
    )
    backward_values = context_recomputed[:, key_value_width:].reshape(
        number_of_blocks, key_row_count, KEY_VALUE_HEADS, HEAD_SIZE
    )
    attention_output_gradient = mixed_gradient.reshape(
        token_rows, KEY_VALUE_HEADS, query_groups, HEAD_SIZE
    )
    grad_queries, grad_keys, grad_values = attend_backward(
        query_rows,
        backward_keys,
        backward_values,
        place_blocks,
        query_place,
        log_total,
        attention_output_gradient,
        attention_output,
        score_scale,
    )
    grad_context_all = jnp.concatenate(
        [
            grad_keys.reshape(seq_rows, key_value_width),
            grad_values.reshape(seq_rows, key_value_width),
        ],
        axis=1,
    )
    grad_context = lax.psum_scatter(
        grad_context_all.astype(jnp.bfloat16), "ctx", scatter_dimension=0, tiled=True
    ).astype(jnp.float32)
    grad_projected = jnp.concatenate(
        [grad_queries.reshape(token_rows, query_total_width), grad_context], axis=1
    ).astype(jnp.bfloat16)
    grad_normed_in = lax.dot_general(
        grad_projected, full_qkv, contract_last, preferred_element_type=jnp.float32
    )
    grad_qkv_local = lax.dot_general(
        normed_in, grad_projected, contract_first, preferred_element_type=jnp.float32
    )
    grad_gain_in_local = jnp.sum(grad_normed_in * scaled_in, axis=0)
    grad_inputs = grad_middle + norm_back(grad_normed_in, scaled_in, inverse_in, gain_in_float)
    weight_sums = (
        lax.psum_scatter(
            grad_gain_in_local.astype(jnp.bfloat16), "wt", scatter_dimension=0, tiled=True
        ).astype(jnp.float32),
        lax.psum_scatter(
            grad_qkv_local.astype(jnp.bfloat16), "wt", scatter_dimension=0, tiled=True
        ).astype(jnp.float32),
        lax.psum_scatter(
            grad_out_local.astype(jnp.bfloat16), "wt", scatter_dimension=0, tiled=True
        ).astype(jnp.float32),
        lax.psum_scatter(
            grad_gain_mid_local.astype(jnp.bfloat16), "wt", scatter_dimension=0, tiled=True
        ).astype(jnp.float32),
        lax.psum_scatter(
            grad_shared_full.astype(jnp.bfloat16), "wt", scatter_dimension=0, tiled=True
        ).astype(jnp.float32),
    )
    summed = (
        lax.psum(weight_sums[0].astype(jnp.bfloat16), "ctx").astype(jnp.float32),
        lax.psum(weight_sums[1].astype(jnp.bfloat16), "ctx").astype(jnp.float32),
        lax.psum(weight_sums[2].astype(jnp.bfloat16), "ctx").astype(jnp.float32),
        lax.psum(weight_sums[3].astype(jnp.bfloat16), "ctx").astype(jnp.float32),
        lax.psum(weight_sums[4].astype(jnp.bfloat16), "ctx").astype(jnp.float32),
        lax.psum(expert_grad.astype(jnp.bfloat16), "ctx").astype(jnp.float32),
    )
    return (
        final_state.astype(jnp.bfloat16)[None],
        loss_value,
        grad_inputs[None],
        summed[0],
        summed[1],
        summed[2],
        summed[3],
        summed[4],
        summed[5],
    )


PLANE = [[0, 2, 4, 6], [1, 3, 5, 7]]
COSTS = {
    "project": 0.3,
    "attend": 0.3,
    "leave": 0.3,
    "join_shared": 0.3,
    "experts": 0.3,
    "experts_back": 0.3,
    "enter_back": 0.3,
    "attend_back": 0.3,
    "finish": 0.3,
    "weight_grad": 0.3,
    "expert_grad": 0.3,
    "blend_split": 0.3,
    "blend_pair": 0.3,
    "blend_sum": 0.3,
    "blend_stack": 0.3,
    "blend_four": 0.3,
    "place_pair": 0.3,
    "place_shared": 0.3,
    "place_heads": 0.3,
}


def flip(value, bit):
    return lax.ppermute(value, "ctx", [(index, index ^ bit) for index in range(8)])


def line_swap(value, offset):
    return lax.ppermute(value, "wt", [(index, index ^ offset) for index in range(4)])


def line_middle(value):
    return lax.ppermute(value, "wt", [(1, 2), (2, 1)])


def line_outward(value):
    return lax.ppermute(value, "wt", [(1, 0), (2, 3)])


def line_inward(value):
    return lax.ppermute(value, "wt", [(0, 1), (3, 2)])


def line_gather(value, at_end):
    near = line_swap(value, 1)
    middle = line_middle(value)
    middle_far = line_middle(near)
    outward = line_outward(middle)
    outward_far = line_outward(middle_far)
    return [
        value,
        near,
        jnp.where(at_end, outward, middle_far),
        jnp.where(at_end, outward_far, middle),
    ]


def line_reduce(parts):
    far = line_inward(parts[3])
    carried = parts[2] + far
    inward = line_inward(carried)
    crossed = line_middle(carried)
    near = line_swap(parts[1] + crossed, 1)
    middle = line_middle(parts[3] + inward)
    return (
        parts[0].astype(jnp.float32) + near.astype(jnp.float32) + middle.astype(jnp.float32)
    )


def chips_exchange(blocks):
    return lax.all_to_all(
        blocks,
        "ctx",
        split_axis=0,
        concat_axis=0,
        tiled=True,
        axis_index_groups=PLANE,
    )


def line_exchange(blocks):
    return lax.all_to_all(blocks, "wt", split_axis=0, concat_axis=0, tiled=True)


def chips_gather(value, x_last):
    along_x = flip(value, 2)
    along_y = flip(value, 4)
    corner = flip(along_y, 2) if x_last else flip(along_x, 4)
    return [value, along_x, along_y, corner]


def core_swap(values):
    return [flip(value, 1) for value in values]


def everywhere_sum(value):
    for bit in (1, 2, 4):
        value = value + flip(value, bit)
    for offset in (1, 2):
        value = value + line_swap(value, offset)
    return value


def pick(blocks, index):
    return lax.dynamic_index_in_dim(blocks, index, 0, keepdims=False)


def chips_reduce(keep, came):
    half = keep.shape[1] // 2
    upper = keep[:, :half] + came[:, :half]
    lower = keep[:, half:] + came[:, half:]
    upper_came = flip(upper[1::2], 2)
    lower_came = flip(lower[2:], 4)
    upper = upper[0::2] + upper_came
    lower = lower[:2] + lower_came
    upper_came = flip(upper[1], 4)
    lower_came = flip(lower[1], 2)
    return jnp.concatenate([upper[0] + upper_came, lower[0] + lower_came], axis=0)


def dot_plain(left, right):
    return lax.dot_general(
        left, right, (((1,), (0,)), ((), ())), preferred_element_type=jnp.float32
    )


def dot_last(left, right):
    return lax.dot_general(
        left, right, (((1,), (1,)), ((), ())), preferred_element_type=jnp.float32
    )


def dot_first(left, right):
    return lax.dot_general(
        left, right, (((0,), (0,)), ((), ())), preferred_element_type=jnp.float32
    )


def call(kernel, name, meta, arrays, grid, in_specs, out_specs, out_shape, scratch, flops, moved):
    return pl.pallas_call(
        kernel,
        grid_spec=pltpu.PrefetchScalarGridSpec(
            num_scalar_prefetch=1,
            grid=grid,
            in_specs=in_specs,
            out_specs=out_specs,
            scratch_shapes=scratch,
        ),
        out_shape=out_shape,
        compiler_params=pltpu.CompilerParams(vmem_limit_bytes=48 * 1024 * 1024),
        cost_estimate=pl.CostEstimate(
            flops=int(COSTS.get(name, 1.0) * 1e9), bytes_accessed=1000, transcendentals=0
        ),
        name=name,
    )(meta, *arrays)


def whole(array):
    rank = len(array.shape)
    return pl.BlockSpec(tuple(array.shape), lambda *_: (0,) * rank)


def shape_of(shape, dtype):
    return jax.ShapeDtypeStruct(shape, dtype)


def size_of(arrays):
    return sum(math.prod(a.shape) * a.dtype.itemsize for a in arrays)


def blend(meta, name, function, arrays, pieces=4):
    rows = arrays[0].shape[-2]
    tile = rows // pieces
    outs = jax.eval_shape(function, *[shape_of(a.shape, a.dtype) for a in arrays])
    many = isinstance(outs, (list, tuple))
    outs = list(outs) if many else [outs]

    def spec(a):
        rank = len(a.shape)
        lead = a.shape[:-2]
        return pl.BlockSpec(
            tuple(lead) + (tile, a.shape[-1]),
            lambda i, m: (0,) * (rank - 2) + (i, 0),
        )

    def kernel(meta_ref, *refs):
        result = function(*[ref[...] for ref in refs[: len(arrays)]])
        result = list(result) if many else [result]
        for ref, value in zip(refs[len(arrays) :], result):
            ref[...] = value

    result = call(
        kernel,
        name,
        meta,
        arrays,
        (pieces,),
        [spec(a) for a in arrays],
        [spec(a) for a in outs],
        outs,
        [],
        0,
        0,
    )
    return result if many else result[0]


def aligned(value, step):
    return pl.multiple_of(value * step, step)


def project_kernel(meta, blocks_ref, gain_ref, mine, other, *refs):
    normed_ref, query_ref, pair_ref, weight_ref = refs
    core = meta[0] & 1
    rows = mine.shape[1]

    @pl.when(pl.program_id(0) == 0)
    def _():
        for i in range(4):
            at = 2 * (meta[1] ^ i)
            weight_ref[pl.ds(aligned(at + core, rows), rows), :] = mine[i]
            weight_ref[pl.ds(aligned(at + 1 - core, rows), rows), :] = other[i]

    states = blocks_ref[0].astype(jnp.float32)
    inverse = lax.rsqrt(jnp.mean(states * states, axis=-1, keepdims=True) + norm_eps)
    normed = (states * inverse * gain_ref[...]).astype(jnp.bfloat16)
    normed_ref[0] = normed
    projected = dot_plain(normed, weight_ref[...]).astype(jnp.bfloat16)
    query_width = query_ref.shape[-1]
    query_ref[0] = projected[:, :query_width]
    pair_ref[0] = projected[:, query_width:]


def project(meta, blocks, gain, mine, other, query_width):
    _, token_rows, width = blocks.shape
    columns = mine.shape[2]
    arrays = [blocks, gain, mine, other]
    outs = [
        shape_of((4, token_rows, width), jnp.bfloat16),
        shape_of((4, token_rows, query_width), jnp.bfloat16),
        shape_of((4, token_rows, columns - query_width), jnp.bfloat16),
        shape_of((width, columns), jnp.bfloat16),
    ]
    return call(
        project_kernel,
        "project",
        meta,
        arrays,
        (4,),
        [pl.BlockSpec((1, token_rows, width), lambda r, m: (r, 0, 0))]
        + [whole(a) for a in arrays[1:]],
        [
            pl.BlockSpec((1, token_rows, width), lambda r, m: (r, 0, 0)),
            pl.BlockSpec((1, token_rows, query_width), lambda r, m: (r, 0, 0)),
            pl.BlockSpec((1, token_rows, columns - query_width), lambda r, m: (r, 0, 0)),
            whole(outs[3]),
        ],
        outs,
        [],
        2 * 4 * token_rows * width * columns,
        size_of(arrays) + size_of(outs),
    )


def sort_pairs(meta, mine_ref, other_ref, keys, values):
    half = mine_ref.shape[1] // 2
    for slot in range(16):
        block, part = (slot, 0) if slot < 8 else (15 - slot, 1)
        place = block >> 1
        rows = pl.ds(part * half, half)
        to = pl.ds(slot * half, half)

        @pl.when((meta[0] & 1) == (block & 1))
        def _():
            keys[to, :] = mine_ref[place, rows, :HEAD_SIZE]
            values[to, :] = mine_ref[place, rows, HEAD_SIZE:]

        @pl.when((meta[0] & 1) != (block & 1))
        def _():
            keys[to, :] = other_ref[place, rows, :HEAD_SIZE]
            values[to, :] = other_ref[place, rows, HEAD_SIZE:]


def stack_heads(rows):
    count = rows.shape[1] // HEAD_SIZE
    return jnp.concatenate(
        [rows[:, h * HEAD_SIZE : (h + 1) * HEAD_SIZE] for h in range(count)], axis=0
    )


def unstack_heads(rows, count):
    each = rows.shape[0] // count
    return jnp.concatenate([rows[h * each : (h + 1) * each] for h in range(count)], axis=1)


def step_slot(meta):
    step = pl.program_id(0)
    block = 2 * (step >> 1) + (meta[0] & 1)
    return jnp.where((step & 1) == 0, block, 15 - block)


def allowed_pairs(start, slot, shape, half):
    key_place = start + lax.broadcasted_iota(jnp.int32, shape, 0)
    query_place = slot * half + (lax.broadcasted_iota(jnp.int32, shape, 1) & (half - 1))
    return key_place <= query_place


def key_spans(step, half, span):
    pairs = (step // 2 if step % 2 == 0 else 7 - step // 2) + 1
    rows = pairs * 2 * half
    return [(at, min(span, rows - at)) for at in range(0, rows, span)]


def attend_kernel(scale, span, meta, query_ref, mine_ref, other_ref, *refs):
    out_ref, log_ref, keys, values, values_turned = refs
    half, group_width = query_ref.shape[1:]
    count = group_width // HEAD_SIZE

    @pl.when(pl.program_id(0) == 0)
    def _():
        sort_pairs(meta, mine_ref, other_ref, keys, values)
        values_turned[...] = values[...].T

    slot = step_slot(meta)
    query = stack_heads(query_ref[0])
    wide = count * half

    def run(spans):
        highest = jnp.full((1, wide), masked_score, jnp.float32)
        total = jnp.zeros((1, wide), jnp.float32)
        mixed = jnp.zeros((HEAD_SIZE, wide), jnp.float32)
        for start, size in spans:
            at = pl.ds(start, size)
            scores = dot_last(keys[at, :], query) * scale
            if start == spans[-1][0]:
                seen = allowed_pairs(start, slot, scores.shape, half)
                scores = jnp.where(seen, scores, masked_score)
            new = jnp.maximum(highest, jnp.max(scores, axis=0, keepdims=True))
            rescale = jnp.exp(highest - new)
            powers = jnp.exp(scores - new)
            total = total * rescale + jnp.sum(powers, axis=0, keepdims=True)
            mixed = mixed * rescale + dot_plain(
                values_turned[:, at], powers.astype(jnp.bfloat16)
            )
            highest = new
        log_ref[0] = highest + jnp.log(total)
        out_ref[0] = unstack_heads((mixed / total).T, count).astype(jnp.bfloat16)

    for step in range(8):

        @pl.when(pl.program_id(0) == step)
        def _():
            run(key_spans(step, half, span))


def attend(meta, query, mine, other, scale):
    token_rows, group_width = query.shape[1:]
    half = token_rows // 2
    count = group_width // HEAD_SIZE
    everything = 8 * token_rows
    span = 1024
    arrays = [query, mine, other]
    outs = [
        shape_of(query.shape, jnp.bfloat16),
        shape_of((8, 1, count * half), jnp.float32),
    ]
    return call(
        functools.partial(attend_kernel, scale, span),
        "attend",
        meta,
        arrays,
        (8,),
        [
            pl.BlockSpec((1, half, group_width), lambda i, m: (i // 2, i % 2, 0)),
            whole(mine),
            whole(other),
        ],
        [
            pl.BlockSpec((1, half, group_width), lambda i, m: (i // 2, i % 2, 0)),
            pl.BlockSpec((1, 1, count * half), lambda i, m: (i, 0, 0)),
        ],
        outs,
        [
            pltpu.VMEM((everything, HEAD_SIZE), jnp.bfloat16),
            pltpu.VMEM((everything, HEAD_SIZE), jnp.bfloat16),
            pltpu.VMEM((HEAD_SIZE, everything), jnp.bfloat16),
        ],
        2 * 2 * 4 * token_rows * everything * group_width,
        size_of(arrays) + size_of(outs),
    )


def attend_back_kernel(scale, span, meta, query_ref, mine_ref, other_ref, log_ref, *refs):
    mixed_ref, grad_ref, grad_query_ref, grad_mine_ref, grad_other_ref = refs[:5]
    keys, values, keys_turned, grad_keys, grad_values = refs[5:]
    step = pl.program_id(0)
    half, group_width = query_ref.shape[1:]
    count = group_width // HEAD_SIZE

    @pl.when(step == 0)
    def _():
        sort_pairs(meta, mine_ref, other_ref, keys, values)
        keys_turned[...] = keys[...].T
        grad_keys[...] = jnp.zeros_like(grad_keys)
        grad_values[...] = jnp.zeros_like(grad_values)

    slot = step_slot(meta)
    query = stack_heads(query_ref[0])
    mixed = stack_heads(mixed_ref[0]).astype(jnp.float32)
    grad = stack_heads(grad_ref[0])
    delta = jnp.sum((mixed * grad.astype(jnp.float32)).T, axis=0, keepdims=True)
    log_total = log_ref[0]

    def run(spans):
        grad_turned = jnp.zeros((HEAD_SIZE, count * half), jnp.float32)
        for start, size in spans:
            at = pl.ds(start, size)
            scores = dot_last(keys[at, :], query) * scale
            probs = jnp.exp(scores - log_total)
            if start == spans[-1][0]:
                probs = jnp.where(allowed_pairs(start, slot, probs.shape, half), probs, 0.0)
            grad_probs = dot_last(values[at, :], grad)
            grad_scores = (probs * (grad_probs - delta)).astype(jnp.bfloat16)
            grad_values[at, :] += dot_plain(probs.astype(jnp.bfloat16), grad)
            grad_keys[at, :] += dot_plain(grad_scores, query)
            grad_turned += dot_plain(keys_turned[:, at], grad_scores)
        grad_query_ref[0] = unstack_heads((grad_turned * scale).T, count).astype(jnp.bfloat16)

    for at_step in range(8):

        @pl.when(step == at_step)
        def _():
            run(key_spans(at_step, half, span))

    @pl.when(step == 7)
    def _():
        for slot_at in range(16):
            block, part = (slot_at, 0) if slot_at < 8 else (15 - slot_at, 1)
            place = block >> 1
            rows = pl.ds(part * half, half)
            here = pl.ds(slot_at * half, half)
            both = jnp.concatenate([grad_keys[here, :] * scale, grad_values[here, :]], axis=1)

            @pl.when((meta[0] & 1) == (block & 1))
            def _():
                grad_mine_ref[place, rows, :] = both

            @pl.when((meta[0] & 1) != (block & 1))
            def _():
                grad_other_ref[place, rows, :] = both.astype(jnp.bfloat16)


def attend_back(meta, query, mine, other, log_total, mixed, grad, scale):
    token_rows, group_width = query.shape[1:]
    half = token_rows // 2
    count = group_width // HEAD_SIZE
    everything = 8 * token_rows
    span = 512
    arrays = [query, mine, other, log_total, mixed, grad]
    outs = [
        shape_of(query.shape, jnp.bfloat16),
        shape_of(mine.shape, jnp.float32),
        shape_of(mine.shape, jnp.bfloat16),
    ]
    return call(
        functools.partial(attend_back_kernel, scale, span),
        "attend_back",
        meta,
        arrays,
        (8,),
        [
            pl.BlockSpec((1, half, group_width), lambda i, m: (i // 2, i % 2, 0)),
            whole(mine),
            whole(other),
            pl.BlockSpec((1, 1, count * half), lambda i, m: (i, 0, 0)),
            pl.BlockSpec((1, half, group_width), lambda i, m: (i // 2, i % 2, 0)),
            pl.BlockSpec((1, half, group_width), lambda i, m: (i // 2, i % 2, 0)),
        ],
        [
            pl.BlockSpec((1, half, group_width), lambda i, m: (i // 2, i % 2, 0)),
            whole(outs[1]),
            whole(outs[2]),
        ],
        outs,
        [
            pltpu.VMEM((everything, HEAD_SIZE), jnp.bfloat16),
            pltpu.VMEM((everything, HEAD_SIZE), jnp.bfloat16),
            pltpu.VMEM((HEAD_SIZE, everything), jnp.bfloat16),
            pltpu.VMEM((everything, HEAD_SIZE), jnp.float32),
            pltpu.VMEM((everything, HEAD_SIZE), jnp.float32),
        ],
        5 * 2 * 4 * token_rows * everything * group_width,
        size_of(arrays) + size_of(outs),
    )


def leave_kernel(meta, *refs):
    parts, mine, other, states_ref, gain_ref = refs[:4], *refs[4:8]
    weight_ref, middle_ref, normed_ref = refs[8:]
    core, chip = meta[0] & 1, meta[0] >> 1
    rows = mine.shape[1]
    for i in range(4):
        weight_ref[pl.ds(aligned(2 * i + core, rows), rows), :] = mine[i]
        weight_ref[pl.ds(aligned(2 * i + 1 - core, rows), rows), :] = other[i]
    middle = states_ref[...].astype(jnp.float32)
    for r in range(4):
        at = pl.ds(aligned(chip ^ r, 2 * rows), 2 * rows)
        middle += dot_plain(parts[r][...], weight_ref[at, :])
    middle_ref[...] = middle
    inverse = lax.rsqrt(jnp.mean(middle * middle, axis=-1, keepdims=True) + norm_eps)
    normed_ref[...] = (middle * inverse * gain_ref[...]).astype(jnp.bfloat16)


def leave(meta, parts, mine, other, states, gain):
    token_rows, width = states.shape
    arrays = list(parts) + [mine, other, states, gain]
    outs = [
        shape_of((8 * mine.shape[1], width), jnp.bfloat16),
        shape_of((token_rows, width), jnp.float32),
        shape_of((token_rows, width), jnp.bfloat16),
    ]
    return call(
        leave_kernel,
        "leave",
        meta,
        arrays,
        (1,),
        [whole(a) for a in arrays],
        [whole(a) for a in outs],
        outs,
        [],
        2 * token_rows * width * width,
        size_of(arrays) + size_of(outs),
    )


def norm_back_rows(grad_normed, states, gain):
    inverse = lax.rsqrt(jnp.mean(states * states, axis=-1, keepdims=True) + norm_eps)
    scaled = states * inverse
    gain_grad = jnp.sum(grad_normed * scaled, axis=0, keepdims=True)
    grad_scaled = grad_normed * gain
    shift = jnp.mean(grad_scaled * scaled, axis=-1, keepdims=True)
    return inverse * (grad_scaled - scaled * shift), gain_grad


def enter_back_kernel(meta, final_ref, normed_ref, middle_ref, gain_ref, weight_ref, *refs):
    grad_ref, branch_ref, gain_grad_ref, mixed_ref = refs
    grad, gain_grad = norm_back_rows(normed_ref[...], middle_ref[...], gain_ref[...])
    grad = grad + final_ref[...]
    grad_ref[...] = grad
    gain_grad_ref[...] = gain_grad
    branch = grad.astype(jnp.bfloat16)
    branch_ref[...] = branch
    rows = weight_ref.shape[0] // 4
    for r in range(4):
        mixed_ref[r] = dot_last(branch, weight_ref[rows * r : rows * (r + 1), :]).astype(
            jnp.bfloat16
        )


def enter_back(meta, grad_final, grad_normed, middle, gain, weight):
    token_rows, width = middle.shape
    arrays = [grad_final, grad_normed, middle, gain, weight]
    outs = [
        shape_of((token_rows, width), jnp.float32),
        shape_of((token_rows, width), jnp.bfloat16),
        shape_of((1, width), jnp.float32),
        shape_of((4, token_rows, weight.shape[0] // 4), jnp.bfloat16),
    ]
    return call(
        enter_back_kernel,
        "enter_back",
        meta,
        arrays,
        (1,),
        [whole(a) for a in arrays],
        [whole(a) for a in outs],
        outs,
        [],
        2 * token_rows * width * width,
        size_of(arrays) + size_of(outs),
    )


def finish_kernel(meta, *refs):
    parts, mine, other = refs[:3]
    states_ref, middle_ref, gain_ref, grad_ref, gain_grad_ref, total = refs[3:]
    core, chip = meta[0] & 1, meta[0] >> 1
    columns = mine.shape[1]
    for at, weights in ((core, mine), (1 - core, other)):
        total[:, pl.ds(aligned(at, columns), columns)] = sum(
            dot_last(parts[r], weights[chip ^ r]) for r in range(4)
        )
    grad, gain_grad = norm_back_rows(
        total[...], states_ref[...].astype(jnp.float32), gain_ref[...]
    )
    grad_ref[0] = grad + middle_ref[...]
    gain_grad_ref[...] = gain_grad


def finish(meta, parts, mine, other, states, grad_middle, gain):
    token_rows, width = states.shape
    arrays = [parts, mine, other, states, grad_middle, gain]
    outs = [
        shape_of((1, token_rows, width), jnp.float32),
        shape_of((1, width), jnp.float32),
    ]
    return call(
        finish_kernel,
        "finish",
        meta,
        arrays,
        (1,),
        [whole(a) for a in arrays],
        [whole(a) for a in outs],
        outs,
        [pltpu.VMEM((token_rows, width), jnp.float32)],
        2 * token_rows * width * 4 * parts.shape[2],
        size_of(arrays) + size_of(outs),
    )


def gated(gate_up, units):
    gate_part = gate_up[:, :units]
    sigma = 1.0 / (1.0 + jnp.exp(-gate_part))
    return gate_part * sigma * gate_up[:, units:]


def gated_back(grad_act, gate_up, units):
    gate_part = gate_up[:, :units].astype(jnp.float32)
    up_part = gate_up[:, units:].astype(jnp.float32)
    sigma = 1.0 / (1.0 + jnp.exp(-gate_part))
    linear = gate_part * sigma
    grad_gate = grad_act * up_part * (sigma * (1.0 + gate_part * (1.0 - sigma)))
    return grad_gate, grad_act * linear, linear * up_part


def experts_kernel(
    meta, rows_ref, gates_ref, expert_ref, shared_ref, gate_up_ref, shared_gate_up_ref, out_ref, total
):
    expert = pl.program_id(0)
    rows = rows_ref[...]

    @pl.when(expert == 0)
    def _():
        units = shared_ref.shape[1] // 3
        gate_up = dot_plain(rows, shared_ref[:, : 2 * units])
        shared_gate_up_ref[...] = gate_up.astype(jnp.bfloat16)
        act = gated(gate_up, units).astype(jnp.bfloat16)
        total[...] = dot_last(act, shared_ref[:, 2 * units :])

    gate_up = dot_plain(rows, expert_ref[0, :, : 2 * F])
    gate_up_ref[0] = gate_up.astype(jnp.bfloat16)
    act = (gated(gate_up, F) * gates_ref[0]).astype(jnp.bfloat16)
    total[...] += dot_last(act, expert_ref[0, :, 2 * F :])

    @pl.when(expert == pl.num_programs(0) - 1)
    def _():
        out_ref[...] = total[...].astype(jnp.bfloat16)


def experts(meta, rows, gates, expert_weight, shared_slice):
    local_experts, width, _ = expert_weight.shape
    token_rows = rows.shape[0]
    shared_units = shared_slice.shape[1] // 3
    arrays = [rows, gates, expert_weight, shared_slice]
    outs = [
        shape_of((local_experts, token_rows, 2 * F), jnp.bfloat16),
        shape_of((token_rows, 2 * shared_units), jnp.bfloat16),
        shape_of((token_rows, width), jnp.bfloat16),
    ]
    return call(
        experts_kernel,
        "experts",
        meta,
        arrays,
        (local_experts,),
        [
            whole(rows),
            pl.BlockSpec((1, token_rows, 1), lambda e, m: (e, 0, 0)),
            pl.BlockSpec((1, width, 3 * F), lambda e, m: (e, 0, 0)),
            whole(shared_slice),
        ],
        [
            pl.BlockSpec((1, token_rows, 2 * F), lambda e, m: (e, 0, 0)),
            whole(outs[1]),
            whole(outs[2]),
        ],
        outs,
        [pltpu.VMEM((token_rows, width), jnp.float32)],
        2 * token_rows * width * 3 * (F * local_experts + shared_units),
        size_of(arrays) + size_of(outs),
    )


def experts_back_kernel(
    meta,
    grad_ref,
    gates_ref,
    gate_up_ref,
    shared_gate_up_ref,
    expert_ref,
    shared_ref,
    grad_gate_up_ref,
    act_ref,
    shared_grad_ref,
    shared_act_ref,
    grad_rows_ref,
    total,
):
    expert = pl.program_id(0)
    grad = grad_ref[...]

    @pl.when(expert == 0)
    def _():
        units = shared_ref.shape[1] // 3
        grad_act = dot_plain(grad, shared_ref[:, 2 * units :])
        grad_gate, grad_up, act = gated_back(grad_act, shared_gate_up_ref[...], units)
        both = jnp.concatenate([grad_gate, grad_up], axis=1).astype(jnp.bfloat16)
        shared_grad_ref[0] = both
        shared_act_ref[0] = act.astype(jnp.bfloat16)
        total[...] = dot_last(both, shared_ref[:, : 2 * units])

    grad_act = dot_plain(grad, expert_ref[0, :, 2 * F :]) * gates_ref[0]
    grad_gate, grad_up, act = gated_back(grad_act, gate_up_ref[0], F)
    both = jnp.concatenate([grad_gate, grad_up], axis=1).astype(jnp.bfloat16)
    grad_gate_up_ref[0] = both
    act_ref[0] = (act * gates_ref[0]).astype(jnp.bfloat16)
    total[...] += dot_last(both, expert_ref[0, :, : 2 * F])

    @pl.when(expert == pl.num_programs(0) - 1)
    def _():
        grad_rows_ref[...] = total[...].astype(jnp.bfloat16)


def experts_back(meta, grad, gates, gate_up, shared_gate_up, expert_weight, shared_slice):
    local_experts, width, _ = expert_weight.shape
    token_rows = grad.shape[0]
    shared_units = shared_slice.shape[1] // 3
    arrays = [grad, gates, gate_up, shared_gate_up, expert_weight, shared_slice]
    outs = [
        shape_of((local_experts, token_rows, 2 * F), jnp.bfloat16),
        shape_of((local_experts, token_rows, F), jnp.bfloat16),
        shape_of((1, token_rows, 2 * shared_units), jnp.bfloat16),
        shape_of((1, token_rows, shared_units), jnp.bfloat16),
        shape_of((token_rows, width), jnp.bfloat16),
    ]
    return call(
        experts_back_kernel,
        "experts_back",
        meta,
        arrays,
        (local_experts,),
        [
            whole(grad),
            pl.BlockSpec((1, token_rows, 1), lambda e, m: (e, 0, 0)),
            pl.BlockSpec((1, token_rows, 2 * F), lambda e, m: (e, 0, 0)),
            whole(shared_gate_up),
            pl.BlockSpec((1, width, 3 * F), lambda e, m: (e, 0, 0)),
            whole(shared_slice),
        ],
        [
            pl.BlockSpec((1, token_rows, 2 * F), lambda e, m: (e, 0, 0)),
            pl.BlockSpec((1, token_rows, F), lambda e, m: (e, 0, 0)),
            whole(outs[2]),
            whole(outs[3]),
            whole(outs[4]),
        ],
        outs,
        [pltpu.VMEM((token_rows, width), jnp.float32)],
        2 * token_rows * width * 3 * (F * local_experts + shared_units),
        size_of(arrays) + size_of(outs),
    )


def weight_grad_kernel(pairs, core_at, meta, *refs):
    keep_ref, give_ref = refs[-2:]
    at = 0
    columns = 0
    parts = []
    for count in pairs:
        lefts, rights = refs[at : at + count], refs[at + count : at + 2 * count]
        at += 2 * count
        parts.append(
            sum(dot_first(a[...], b[0]) for a, b in zip(lefts, rights)).astype(jnp.bfloat16)
        )
    half = keep_ref.shape[1]

    for core, (first, second) in ((0, (keep_ref, give_ref)), (1, (give_ref, keep_ref))):

        @pl.when((meta[core_at] & 1) == core)
        def _():
            start = 0
            for part in parts:
                stop = start + part.shape[1]
                first[0, :, start:stop] = part[:half]
                second[0, :, start:stop] = part[half:]
                start = stop


def expert_grad_kernel(count, meta, *refs):
    rows, grads, front, acts = (refs[i * count : (i + 1) * count] for i in range(4))
    out_ref = refs[-1] if len(refs) == 4 * count + 1 else refs[-2]
    tile = rows[0].shape[1]
    both = 3 * F

    def pair(front_refs, act_refs):
        return [
            sum(dot_first(a[...], b[0]) for a, b in zip(left, right)).astype(jnp.bfloat16)
            for left, right in ((rows, front_refs), (grads, act_refs))
        ]

    left, right = pair(front, acts)
    out_ref[0, :tile, : left.shape[1]] = left
    out_ref[0, :tile, left.shape[1] : both] = right
    if len(refs) > 4 * count + 1:
        held = refs[-1]
        left, right = pair(refs[4 * count : 5 * count], refs[5 * count : 6 * count])
        split, columns = left.shape[1], left.shape[1] + right.shape[1]
        held[:, :split] = left
        held[:, split:] = right
        quarter = tile // 4
        first = 2 * meta[2]
        out_ref[0, tile:, :columns] = held[pl.ds(aligned(first, quarter), quarter), :]
        out_ref[0, tile:, columns:] = held[pl.ds(aligned(first + 1, quarter), quarter), :]


def expert_grad(meta, expert, half, rows, grads, front, acts, shared=None):
    count = len(rows)
    token_rows, width = rows[0].shape
    tile = width // 4
    arrays = list(rows) + list(grads) + list(front) + list(acts)
    column = pl.BlockSpec((token_rows, tile), lambda i, m: (0, i ^ m[0]))

    def of_expert(a):
        return pl.BlockSpec((1,) + a.shape[1:], lambda i, m: (m[1], 0, 0))

    in_specs = [column] * (2 * count) + [of_expert(a) for a in arrays[2 * count :]]
    below, scratch = 0, []
    if shared is not None:
        arrays += list(shared[0]) + list(shared[1])
        in_specs += [whole(a) for a in arrays[4 * count :]]
        below = tile // 4
        columns = shared[0][0].shape[-1] + shared[1][0].shape[-1]
        scratch = [pltpu.VMEM((tile, columns), jnp.bfloat16)]
    return call(
        functools.partial(expert_grad_kernel, count),
        "expert_grad",
        jnp.stack([meta[0] >> 1, expert, half]),
        arrays,
        (4,),
        in_specs,
        pl.BlockSpec((1, tile + below, 3 * F), lambda i, m: (i, 0, 0)),
        shape_of((4, tile + below, 3 * F), jnp.bfloat16),
        scratch,
        0,
        0,
    )


def weight_grad(meta, order, operands, index):
    token_rows, width = operands[0][0][0].shape
    tile = width // 4
    scalars = jnp.stack([order, meta[0]])
    arrays, in_specs, columns = [], [], 0
    for lefts, rights in operands:
        arrays += list(lefts) + list(rights)
        in_specs += [pl.BlockSpec((token_rows, tile), lambda i, m: (0, i ^ m[0]))] * len(lefts)
        units = rights[0].shape[-1]
        at = index if rights[0].shape[0] > 1 else 0
        in_specs += [
            pl.BlockSpec((1, token_rows, units), lambda i, m, at=at: (at, 0, 0))
        ] * len(rights)
        columns += units
    tokens = token_rows * len(operands[0][0])
    counts = [len(left) for left, _ in operands]
    outs = [shape_of((4, tile // 2, columns), jnp.bfloat16)] * 2
    return call(
        functools.partial(weight_grad_kernel, counts, 1),
        "weight_grad",
        scalars,
        arrays,
        (4,),
        in_specs,
        [pl.BlockSpec((1, tile // 2, columns), lambda i, m: (i, 0, 0))] * 2,
        outs,
        [],
        2 * tokens * width * columns,
        size_of(outs) + 4 * tokens * width + 2 * tokens * columns,
    )


def place_pair_kernel(meta, *refs):
    mine, other, out_ref = refs[-3:]
    rows = out_ref.shape[1]

    @pl.when(pl.program_id(0) == 0)
    def _():
        out_ref[0] = mine[0, :rows].astype(jnp.float32)

    @pl.when(pl.program_id(0) == 1)
    def _():
        out_ref[0] = other[0, :rows].astype(jnp.float32)


def place_pair(meta, total, index, shape, mine, other):
    _, rows, columns = mine.shape
    arrays = [mine, other]
    in_specs = [
        pl.BlockSpec((1, rows, columns), lambda k, r, m: ((1 - k) * r + 3 * k, 0, 0)),
        pl.BlockSpec((1, rows, columns), lambda k, r, m: (k * r, 0, 0)),
    ]
    aliases = {}
    if total is not None:
        arrays = [total] + arrays
        in_specs = [pl.BlockSpec(memory_space=pl.ANY)] + in_specs
        aliases = {1: 0}
    return pl.pallas_call(
        place_pair_kernel,
        grid_spec=pltpu.PrefetchScalarGridSpec(
            num_scalar_prefetch=1,
            grid=(2, 4),
            in_specs=in_specs,
            out_specs=pl.BlockSpec(
                (1, shape[1] // 4, shape[2]),
                lambda k, r, m: (2 * ((m[0] & 1) ^ k) + index, (m[0] >> 1) ^ r, 0),
            ),
        ),
        out_shape=shape_of(shape, jnp.float32),
        input_output_aliases=aliases,
        compiler_params=pltpu.CompilerParams(vmem_limit_bytes=48 * 1024 * 1024),
        cost_estimate=pl.CostEstimate(
            flops=int(COSTS.get("place_pair", 1.0) * 1e9), bytes_accessed=1000, transcendentals=0
        ),
        name="place_pair",
    )(meta, *arrays)


def place_shared_kernel(meta, mine_low, mine_high, other_low, other_high, out_ref):
    core = meta[0] & 1
    rows = mine_low.shape[1]
    for at, low, high in ((core, mine_low, mine_high), (1 - core, other_low, other_high)):
        out_ref[pl.ds(aligned(2 * at, rows), rows), :] = low[0].astype(jnp.float32)
        out_ref[pl.ds(aligned(2 * at + 1, rows), rows), :] = high[0].astype(jnp.float32)


def place_shared(meta, mine, other):
    _, rows, columns = mine.shape
    units = columns // 6
    low = pl.BlockSpec((1, rows, units), lambda i, j, m: (i, 0, j))
    high = pl.BlockSpec((1, rows, units), lambda i, j, m: (i, 0, 3 + j))
    outs = shape_of((4 * rows, 2 * columns), jnp.float32)
    return call(
        place_shared_kernel,
        "place_shared",
        meta,
        [mine, mine, other, other],
        (4, 3),
        [low, high, low, high],
        pl.BlockSpec((4 * rows, units), lambda i, j, m: (0, 4 * j + (m[1] ^ i))),
        outs,
        [],
        0,
        0,
    )


def place_heads_kernel(meta, *refs):
    mine, other, out_ref = refs[:4], refs[4], refs[5]
    core, chip = meta[0] & 1, meta[0] >> 1
    rows, columns = mine[0].shape
    group_width = columns - 2 * HEAD_SIZE
    for r in range(4):
        head = chip ^ r
        for at, pieces in ((core, [piece[...] for piece in mine]), (1 - core, other)):
            to = pl.ds(aligned(at, rows), rows)
            values = pieces[r].astype(jnp.float32)
            out_ref[to, pl.ds(aligned(head, group_width), group_width)] = values[:, :group_width]
            out_ref[to, pl.ds(aligned(4 * group_width // HEAD_SIZE + head, HEAD_SIZE), HEAD_SIZE)] = (
                values[:, group_width : group_width + HEAD_SIZE]
            )
            out_ref[
                to, pl.ds(aligned(4 * group_width // HEAD_SIZE + 4 + head, HEAD_SIZE), HEAD_SIZE)
            ] = values[:, group_width + HEAD_SIZE :]


def place_heads(meta, mine, other):
    rows, columns = mine[0].shape
    arrays = list(mine) + [other]
    outs = shape_of((2 * rows, 4 * columns), jnp.float32)
    return call(
        place_heads_kernel,
        "place_heads",
        meta,
        arrays,
        (1,),
        [whole(a) for a in arrays],
        whole(outs),
        outs,
        [],
        0,
        size_of(arrays + [outs]),
    )


def join_shared_kernel(meta, mine, other, out_ref):
    step = pl.program_id(0)
    rows = mine.shape[2]
    first = meta[0] ^ (2 * step)
    for i in range(4):
        at = 8 * (meta[1] ^ i)
        out_ref[pl.ds(aligned(at + first, rows), rows), :] = mine[0, i]
        out_ref[pl.ds(aligned(at + (first ^ 1), rows), rows), :] = other[0, i]


def join_shared(meta, mine, other):
    _, _, rows, columns = mine.shape
    block = pl.BlockSpec((1, 4, rows, columns), lambda r, m: (r, 0, 0, 0))
    outs = shape_of((32 * rows, columns), jnp.bfloat16)
    return call(
        join_shared_kernel,
        "join_shared",
        meta,
        [mine, other],
        (4,),
        [block, block],
        whole(outs),
        outs,
        [],
        0,
        size_of([mine, other, outs]),
    )


class Clock:
    def __init__(self):
        self.last = None

    def __call__(self, *values):
        if self.last is None:
            return values if len(values) > 1 else values[0]
        held = lax.optimization_barrier(tuple(values) + (self.last,))[:-1]
        return held if len(held) > 1 else held[0]

    def mark(self, value):
        self.last = value
        return value


EARLY = (
    "H", "W", "K", "S", "K", "W", "S", "W", "K", "S", "O", "S", "M", "M", "S", "O", "M", "S", "M", "R", "M", "K", "M", "K",
    "M", "K", "R", "M", "K", "M", "M", "M", "M", "R", "M", "M",
)
LATE = (
    "L", "0", "1", "0", "0", "L", "1", "1", "L", "L", "0", "L", "L", "1", "O", "0", "1", "L", "Q", "1", "0", "O", "Q", "L",
    "O", "Q", "O", "Q", "O", "Q", "1", "0", "O", "Q", "S", "O", "Q", "1", "0", "S", "O", "Q", "L", "L", "L", "Q", "O", "S",
    "L",
)


def fast_device(
    hidden,
    teacher,
    valid_mask,
    routes,
    route_gates,
    gain_in,
    query_key_value_weight,
    out_weight,
    gain_mid,
    shared_weight,
    expert_weight,
):
    token_rows, width = hidden.shape[1:]
    context_count, shard_count = 8, 4
    context_index = lax.axis_index("ctx").astype(jnp.int32)
    shard_index = lax.axis_index("wt").astype(jnp.int32)
    plain_meta = jnp.stack([context_index, shard_index])
    core = context_index & 1
    chip = context_index >> 1
    at_end = (shard_index == 0) | (shard_index == shard_count - 1)
    group_width = QUERY_HEADS // KEY_VALUE_HEADS * HEAD_SIZE
    query_width = QUERY_HEADS * HEAD_SIZE
    kv_width = KEY_VALUE_HEADS * HEAD_SIZE
    scale = 1.0 / math.sqrt(HEAD_SIZE)
    all_tokens = token_rows * context_count * shard_count
    shard_rows = query_key_value_weight.shape[0]
    half_rows = shard_rows // 2
    local_experts = expert_weight.shape[0]
    bf16, f32 = jnp.bfloat16, jnp.float32
    states = hidden[0]
    clock = Clock()
    have = {}

    def meta():
        return clock(plain_meta)

    def now(*values):
        return clock(*values)

    def ready(*values):
        values = clock(*values)
        clock.mark(values[0] if isinstance(values, tuple) or isinstance(values, list) else values)
        return values


    def hidden_chain():
        have["blocks"] = chips_exchange(jnp.broadcast_to(states, (4,) + states.shape))
        yield

    def qkv_chain():
        rows = lax.dynamic_slice_in_dim(query_key_value_weight, core * half_rows, half_rows, 0)
        half = jnp.concatenate(
            [
                lax.dynamic_slice_in_dim(rows, chip * group_width, group_width, 1),
                lax.dynamic_slice_in_dim(rows, query_width + chip * HEAD_SIZE, HEAD_SIZE, 1),
                lax.dynamic_slice_in_dim(
                    rows, query_width + kv_width + chip * HEAD_SIZE, HEAD_SIZE, 1
                ),
            ],
            axis=1,
        )
        came = line_swap(half, 1)
        yield
        pair = clock.mark(jnp.stack([half, now(came)]))
        came = line_swap(pair, 2)
        yield
        have["qkv_mine"] = clock.mark(jnp.concatenate([pair, now(came)]))
        have["qkv_other"] = flip(have["qkv_mine"], 1)
        yield

    def small_chain():
        expert_ids = jnp.arange(EXPERTS, dtype=jnp.int32)
        matrix = jnp.sum(
            jnp.where(
                routes[0][None, :, :] == expert_ids[:, None, None], route_gates[0][None, :, :], 0.0
            ),
            axis=-1,
        )
        have["valid"] = valid_mask[0].astype(f32)
        gains = jnp.concatenate([gain_in, gain_mid]).astype(f32).reshape(-1, token_rows)
        gain_rows = gains.shape[0]
        filled = EXPERTS + gain_rows
        pack = jnp.concatenate(
            [
                matrix,
                gains,
                jnp.full((32 - filled, token_rows), jnp.sum(have["valid"]), f32),
            ]
        )
        came = line_swap(pack, 1)
        yield
        pair = clock.mark(jnp.stack([pack, now(came)]))
        came = line_swap(pair, 2)
        yield
        all_packs = clock.mark(jnp.concatenate([pair, now(came)]))
        have["gates"] = [
            lax.dynamic_slice_in_dim(
                all_packs[i], shard_index * local_experts, local_experts, 0
            )[..., None]
            for i in range(4)
        ]
        gains = all_packs[:, EXPERTS:filled].reshape(4, 2, shard_rows)
        gains = jnp.stack([pick(gains, shard_index ^ i) for i in range(4)], axis=1)
        have["gains"] = gains.reshape(2, 1, width)
        total = jnp.broadcast_to(jnp.sum(all_packs[:, filled, 0]), (8, 128))
        yield
        total = now(total)
        for bit in (1, 2, 4):
            came = flip(total, bit)
            yield
            total = clock.mark(total + now(came))
        have["count"] = total[0, 0]
        yield

    def shared_chain():
        eighth = shard_rows // 8
        units = SF // shard_count
        piece = lax.dynamic_slice_in_dim(shared_weight, context_index * eighth, eighth, 0)
        piece = piece.reshape(eighth, 3, shard_count, units)

        piece = jnp.transpose(piece, (2, 0, 1, 3)).reshape(shard_count, eighth, 3 * units)
        parts = [pick(piece, shard_index ^ i) for i in range(4)]
        came = line_swap(now(jnp.stack([parts[1], parts[3]])), 1)
        yield
        came = now(came)
        mine = jnp.stack([parts[0], came[0]])
        came = line_swap(clock.mark(jnp.stack([parts[2], came[1]])), 2)
        yield
        pieces = clock.mark(jnp.concatenate([mine, now(came)]))
        came = flip(pieces, 2)
        yield
        pair = clock.mark(jnp.stack([pieces, now(came)]))
        came = flip(pair, 4)
        yield
        mine = clock.mark(jnp.concatenate([pair, now(came)]))
        other = flip(mine, 1)
        yield
        have["shared"] = join_shared(meta(), mine, other)
        clock.mark(have["shared"])
        yield

    def out_chain():
        half = lax.dynamic_slice_in_dim(now(out_weight), core * half_rows, half_rows, 0)
        came = line_exchange(jnp.broadcast_to(half, (4,) + half.shape))
        yield
        have["out_mine"] = clock.mark(now(came))
        have["out_other"] = flip(have["out_mine"], 1)
        yield

    def qkv_all_chain():
        half = lax.dynamic_slice_in_dim(
            now(have["qkv_slice"]), core * (width // 2), width // 2, 0
        )
        came = flip(half, 2)
        yield
        pair = clock.mark(jnp.stack([half, now(came)]))
        came = flip(pair, 4)
        yield
        have["rel_mine"] = clock.mark(jnp.concatenate([pair, now(came)]))
        have["rel_other"] = flip(have["rel_mine"], 1)
        yield

    def main_chain():
        gains = have["gains"]
        normed_in, query, pair, qkv_slice = project(
            meta(), have["blocks"], gains[0], have["qkv_mine"], have["qkv_other"], group_width
        )
        clock.mark(pair)
        have["normed_in"], have["qkv_slice"] = normed_in, qkv_slice
        pair_other = flip(pair, 1)
        yield
        mixed_heads, log_total = attend(meta(), query, pair, pair_other, scale)
        clock.mark(log_total)
        have["attend"] = (query, pair, pair_other, log_total, mixed_heads)
        parts = ready(*[pick(mixed_heads, chip ^ r) for r in range(4)])
        mixed = [parts[0]] + [flip(parts[r], 2 * r) for r in (1, 2, 3)]
        have["mixed"] = mixed
        yield
        out_full, middle, normed_mid = leave(
            meta(), mixed, have["out_mine"], have["out_other"], states, gains[1]
        )
        have["out_full"], have["middle"] = out_full, middle
        clock.mark(normed_mid)

        near, center = line_swap(normed_mid, 1), line_middle(normed_mid)
        yield
        gates, shared_slice = have["gates"], have["shared"]
        gate_ups, shared_gate_ups, outs = [], [], []

        def forward(rows, i):
            result = experts(meta(), rows, gates[i], expert_weight, shared_slice)
            clock.mark(result[2])
            gate_ups.append(result[0])
            shared_gate_ups.append(result[1])
            outs.append(result[2])

        forward(normed_mid, 0)
        yield
        near, center = now(near, center)
        far, outward = line_middle(near), line_outward(center)
        forward(near, 1)
        yield
        far, outward = now(far, outward)
        outward_far = line_outward(far)
        third = clock.mark(jnp.where(at_end, outward, far))
        forward(third, 2)
        yield
        outward_far = now(outward_far)
        fourth = clock.mark(jnp.where(at_end, outward_far, center))
        forward(fourth, 3)
        line_rows = [normed_mid, near, third, fourth]
        came = line_inward(outs[3])
        yield
        carried = clock.mark(outs[2] + now(came))
        inward, crossed = line_inward(carried), line_middle(carried)
        yield
        inward, crossed = now(inward, crossed)
        near_out, middle_out = ready(outs[1] + crossed, outs[3] + inward)
        near_out, middle_out = line_swap(near_out, 1), line_middle(middle_out)
        yield
        near_out, middle_out = now(near_out, middle_out)
        final_state = (
            middle + outs[0].astype(f32) + near_out.astype(f32) + middle_out.astype(f32)
        )
        valid = have["valid"]
        deviation = final_state - teacher[0].astype(f32)
        have["squared"] = jnp.sum(valid[:, None] * deviation * deviation)
        grad_final = all_tokens / have["count"] * valid[:, None] * deviation
        have["final"], have["grad_final"] = final_state.astype(bf16)[None], grad_final
        grad_low = clock.mark(grad_final.astype(bf16))
        near, center = line_swap(grad_low, 1), line_middle(grad_low)
        yield
        kept = []

        def backward(grads, i):
            kept.append(
                experts_back(
                    meta(),
                    grads,
                    gates[i],
                    gate_ups[i],
                    shared_gate_ups[i],
                    expert_weight,
                    shared_slice,
                )
            )
            clock.mark(kept[-1][4])

        backward(grad_low, 0)
        yield
        near, center = now(near, center)
        far, outward = line_middle(near), line_outward(center)
        backward(near, 1)
        yield
        far, outward = now(far, outward)
        outward_far = line_outward(far)
        third = clock.mark(jnp.where(at_end, outward, far))
        backward(third, 2)
        yield
        outward_far = now(outward_far)
        fourth = clock.mark(jnp.where(at_end, outward_far, center))
        backward(fourth, 3)
        have["line"] = (line_rows, [grad_low, near, third, fourth])
        have["experts"] = list(zip(*kept))
        yield


    def states_chain():
        outs = have["experts"][4]
        came = line_inward(outs[3])
        yield
        carried = clock.mark(outs[2] + now(came))
        inward, crossed = line_inward(carried), line_middle(carried)
        yield
        inward, crossed = now(inward, crossed)
        near_out, middle_out = ready(outs[1] + crossed, outs[3] + inward)
        near_out, middle_out = line_swap(near_out, 1), line_middle(middle_out)
        yield
        near_out, middle_out = now(near_out, middle_out)
        grad_normed = clock.mark(
            outs[0].astype(f32) + near_out.astype(f32) + middle_out.astype(f32)
        )
        grad_middle, grad_branch, grad_gain_mid, grad_mixed = enter_back(
            meta(),
            have["grad_final"],
            grad_normed,
            have["middle"],
            have["gains"][1],
            have["out_full"],
        )
        clock.mark(grad_branch)
        have["grad_branch"], have["grad_gain_mid"] = grad_branch, grad_gain_mid
        grad_mixed = chips_exchange(ready(grad_mixed))
        yield
        query, pair, pair_other, log_total, mixed_heads = have["attend"]
        grad_query, grad_pair, grad_other = attend_back(
            meta(), query, pair, pair_other, log_total, mixed_heads, grad_mixed, scale
        )
        clock.mark(grad_query)
        came = flip(grad_other, 1)
        yield
        grad_pair = grad_pair + now(came).astype(f32)
        projected = clock.mark(jnp.concatenate([grad_query, grad_pair.astype(bf16)], axis=-1))
        have["grad_projected"] = projected
        parts = chips_exchange(ready(projected))
        yield
        grad_hidden, grad_gain_in = finish(
            meta(),
            parts,
            have["rel_mine"],
            have["rel_other"],
            states,
            grad_middle,
            have["gains"][0],
        )
        clock.mark(grad_gain_in)
        have["grad_hidden"] = grad_hidden
        sums = jnp.concatenate(
            [grad_gain_in, have["grad_gain_mid"], jnp.full((6, width), have["squared"], f32)],
            axis=0,
        )
        for offset in (1, 2):
            came = line_swap(sums, offset)
            yield
            sums = clock.mark(sums + now(came))
        for bit in (1, 2, 4):
            came = flip(sums, bit)
            yield
            sums = clock.mark(sums + now(came))
        own = lax.dynamic_slice_in_dim(sums, shard_index * shard_rows, shard_rows, 1)
        have["sums"] = (own, 0.5 * sums[2, 0] / (have["count"] * width))
        yield

    def expert_chain(index):
        line_rows, line_grads = have["line"]
        grad_gate_ups, acts, shared_grads, shared_acts = have["experts"][:4]
        shared = (shared_grads, shared_acts) if index == 0 else None

        def grad_of(at):
            return clock.mark(
                expert_grad(
                    meta(),
                    2 * at + index,
                    at,
                    line_rows,
                    line_grads,
                    grad_gate_ups,
                    acts,
                    shared,
                )
            )

        came = flip(grad_of(1 - core), 1)
        yield
        keep = grad_of(core)
        yield
        x_first = index % 2 == 0
        first, second = (2, 4) if x_first else (4, 2)
        picked = ((1, 3), (0, 2)) if x_first else ((2, 3), (0, 1))
        pieces = keep.shape[1] // 96

        def split_sum(keep, came):
            return [
                jnp.stack([keep[i] + came[i] for i in places]) for places in picked
            ]

        give, keep = blend(meta(), "blend_split", split_sum, [keep, came], pieces)
        clock.mark(give)
        came = flip(give, first)
        yield
        give, keep = blend(
            meta(), "blend_pair", lambda k, c: [k[1] + c[1], k[0] + c[0]], [keep, came], pieces
        )
        clock.mark(give)
        came = flip(give, second)
        yield
        own = clock.mark(blend(meta(), "blend_sum", lambda k, c: k + c, [keep, came], pieces))
        came = flip(own, second)
        yield
        pair = clock.mark(
            blend(meta(), "blend_stack", lambda a, b: jnp.stack([a, b]), [own, came], pieces)
        )
        came = flip(pair, first)
        yield

        def stack_four(near, far):
            if x_first:
                return jnp.stack([near[0], far[0], near[1], far[1]])
            return jnp.stack([near[0], near[1], far[0], far[1]])

        stacked = clock.mark(blend(meta(), "blend_four", stack_four, [pair, came], pieces))
        other = flip(stacked, 1)
        if index == 0:
            have["shared_sum"] = stacked[:, shard_rows:]
        yield
        have["grad_experts"] = place_pair(
            meta(), have.get("grad_experts"), index, expert_weight.shape, stacked, other
        )
        clock.mark(have["grad_experts"])
        yield

    def shared_grad_chain():
        total = now(have["shared_sum"])
        parts = ready(*[pick(total, chip ^ shard_index ^ i) for i in range(4)])
        came = [line_swap(parts[i], i) for i in (1, 2, 3)]
        yield
        mine = clock.mark(jnp.stack([parts[0]] + list(now(*came))))
        other = flip(mine, 1)
        yield
        have["grad_shared"] = clock.mark(place_shared(meta(), mine, other))
        yield

    def line_reduce_steps(keep, came):
        came = now(came)
        parts = [keep[i] + came[i] for i in range(4)]
        came = line_inward(clock.mark(parts[3]))
        yield
        carried = clock.mark(parts[2] + now(came))
        inward, crossed = line_inward(carried), line_middle(carried)
        yield
        inward, crossed = now(inward, crossed)
        near_out, middle_out = ready(parts[1] + crossed, parts[3] + inward)
        near_out, middle_out = line_swap(near_out, 1), line_middle(middle_out)
        yield
        near_out, middle_out = now(near_out, middle_out)
        have["line_sum"] = clock.mark(
            (parts[0].astype(f32) + near_out.astype(f32) + middle_out.astype(f32)).astype(bf16)
        )

    def out_grad_chain():
        mixed = jnp.concatenate(have["mixed"], axis=1)
        keep, give = weight_grad(
            meta(), chip ^ shard_index, [([mixed], [have["grad_branch"][None]])], 0
        )
        clock.mark(keep)
        came = flip(give, 1)
        yield
        yield from line_reduce_steps(keep, came)
        total = have["line_sum"]
        yield
        total = ready(total)
        came = flip(total, 2)
        yield
        total = clock.mark(total + now(came))
        came = flip(total, 4)
        yield
        mine = clock.mark(total + now(came))
        other = flip(mine, 1)
        yield
        mine, other = now(mine, other)
        have["grad_out"] = clock.mark(
            jnp.where(
                core == 0,
                jnp.concatenate([mine, other], axis=0),
                jnp.concatenate([other, mine], axis=0),
            ).astype(f32)
        )
        yield

    def qkv_grad_chain():
        normed_in = have["normed_in"].reshape(4 * token_rows, width)
        projected = have["grad_projected"].reshape(1, 4 * token_rows, -1)
        keep, give = weight_grad(meta(), shard_index, [([normed_in], [projected])], 0)
        clock.mark(keep)
        came = flip(give, 1)
        yield
        yield from line_reduce_steps(keep, came)
        own = have["line_sum"]
        yield
        own = ready(own)
        came = flip(own, 2)
        yield
        pair = clock.mark(jnp.stack([own, now(came)]))
        came = flip(pair, 4)
        yield
        mine = clock.mark(jnp.concatenate([pair, now(came)]))
        other = flip(mine, 1)
        yield
        have["grad_qkv"] = clock.mark(place_heads(meta(), [mine[r] for r in range(4)], other))
        yield

    early = {
        "H": hidden_chain(),
        "W": qkv_chain(),
        "S": shared_chain(),
        "O": out_chain(),
        "K": small_chain(),
        "R": qkv_all_chain(),
        "M": main_chain(),
    }
    late = {
        "L": states_chain(),
        "S": shared_grad_chain(),
        "O": out_grad_chain(),
        "Q": qkv_grad_chain(),
    }
    for index in range(local_experts // 2):
        late[str(index)] = expert_chain(index)
    for chains, order in ((early, EARLY), (late, LATE)):
        for name in order:
            next(chains[name], None)
        for name in chains:
            for _ in chains[name]:
                pass

    own, loss_value = have["sums"]
    return (
        have["final"],
        loss_value,
        have["grad_hidden"],
        own[0],
        have["grad_qkv"],
        have["grad_out"],
        own[1],
        have["grad_shared"],
        have["grad_experts"],
    )


def solution(mesh):
    in_specs = (
        P("wt", "ctx", None),
        P("wt", "ctx", None),
        P("wt", "ctx"),
        P("wt", "ctx", None),
        P("wt", "ctx", None),
        P("wt"),
        P("wt", None),
        P("wt", None),
        P("wt"),
        P("wt", None),
        P("wt", None, None),
    )
    out_specs = (
        P("wt", "ctx", None),
        P(),
        P("wt", "ctx", None),
        P("wt"),
        P("wt", None),
        P("wt", None),
        P("wt"),
        P("wt", None),
        P("wt", None, None),
    )
    plane_of_eight = dict(mesh.shape) == {"ctx": 8, "wt": 4}
    return jax.shard_map(
        fast_device if plane_of_eight else on_device, mesh=mesh, in_specs=in_specs, out_specs=out_specs, check_vma=False
    )
```

```python
import functools
import math

import jax
import jax.numpy as jnp
from jax import lax
from jax.experimental import pallas as pl
from jax.experimental.pallas import tpu as pltpu
from jax.sharding import PartitionSpec as P

QUERY_HEADS = 12
KEY_VALUE_HEADS = 4
HEAD_SIZE = 128
F = 512
SF = 1024
EXPERTS = 16
TOP = 6


norm_eps = 1e-05
masked_score = -1e30


def sigmoid_linear(values):
    return values * jax.nn.sigmoid(values)


def silu_slope(values):
    sigma_value = jax.nn.sigmoid(values)
    return sigma_value * (1.0 + values * (1.0 - sigma_value))


def normalize(values):
    inverse = lax.rsqrt(jnp.mean(values * values, axis=-1, keepdims=True) + norm_eps)
    return (values * inverse, inverse)


def norm_back(grad_normed, scaled, inverse, gain_vector):
    grad_scaled = grad_normed * gain_vector
    return inverse * (grad_scaled - scaled * jnp.mean(grad_scaled * scaled, axis=-1, keepdims=True))


def positions(row_ids, token_rows, context_count):
    piece_index = row_ids // token_rows
    within = row_ids % token_rows
    half_rows = token_rows // 2
    mirrored = jnp.where(within < half_rows, piece_index, 2 * context_count - 1 - piece_index)
    return mirrored * half_rows + within % half_rows


def route_tables(local_routes, local_gates, experts, capacity):
    token_rows = local_routes.shape[0]
    flat_routes = local_routes.reshape(-1)
    one_hot = (flat_routes[:, None] == jnp.arange(experts, dtype=jnp.int32)[None, :]).astype(
        jnp.int32
    )
    earlier = jnp.cumsum(one_hot, axis=0) - one_hot
    slot_index = jnp.sum(earlier * one_hot, axis=1)
    token_index = jnp.arange(flat_routes.shape[0], dtype=jnp.int32) // local_routes.shape[1]
    slot_table = (
        jnp.full((experts, capacity), token_rows, jnp.int32)
        .at[flat_routes, slot_index]
        .set(token_index)
    )
    slot_gate = (
        jnp.zeros((experts, capacity), jnp.float32)
        .at[flat_routes, slot_index]
        .set(local_gates.reshape(-1))
    )
    return (slot_table, slot_gate)


def block_scores(query_rows, key_block, key_position, query_place, score_scale):
    scores = (
        jnp.einsum("qhgd,khd->qhgk", query_rows, key_block, preferred_element_type=jnp.float32)
        * score_scale
    )
    allowed = key_position[None, None, None, :] <= query_place[:, None, None, None]
    return jnp.where(allowed, scores, masked_score)


def attend_forward(
    query_rows, blocked_keys, blocked_values, place_blocks, query_place, score_scale
):
    head_shape = query_rows.shape[:3]

    def online_step(running, block_args):
        running_max, running_sum, accumulated = running
        key_block, value_block, key_position = block_args
        scores = block_scores(query_rows, key_block, key_position, query_place, score_scale)
        new_max = jnp.maximum(running_max, jnp.max(scores, axis=-1))
        rescale = jnp.exp(running_max - new_max)
        powers = jnp.exp(scores - new_max[..., None])
        new_sum = running_sum * rescale + jnp.sum(powers, axis=-1)
        weighted = jnp.einsum(
            "qhgk,khd->qhgd",
            powers.astype(jnp.bfloat16),
            value_block,
            preferred_element_type=jnp.float32,
        )
        return ((new_max, new_sum, accumulated * rescale[..., None] + weighted), None)

    initial = (
        jnp.full(head_shape, masked_score, jnp.float32),
        jnp.zeros(head_shape, jnp.float32),
        jnp.zeros(query_rows.shape, jnp.float32),
    )
    row_max, row_sum, accumulated = lax.scan(
        online_step, initial, (blocked_keys, blocked_values, place_blocks)
    )[0]
    log_total = row_max + jnp.log(row_sum)
    return (accumulated / row_sum[..., None], log_total)


def attend_backward(
    query_rows,
    blocked_keys,
    blocked_values,
    place_blocks,
    query_place,
    log_total,
    attention_output_gradient,
    attention_output,
    score_scale,
):
    row_delta = jnp.sum(attention_output_gradient.astype(jnp.float32) * attention_output, axis=-1)

    def block_grads(grad_queries, block_args):
        key_block, value_block, key_position = block_args
        scores = block_scores(query_rows, key_block, key_position, query_place, score_scale)
        probabilities = jnp.exp(scores - log_total[..., None])
        grad_probs = jnp.einsum(
            "qhgd,khd->qhgk",
            attention_output_gradient,
            value_block,
            preferred_element_type=jnp.float32,
        )
        grad_scores = (probabilities * (grad_probs - row_delta[..., None])).astype(jnp.bfloat16)
        grad_queries = grad_queries + jnp.einsum(
            "qhgk,khd->qhgd", grad_scores, key_block, preferred_element_type=jnp.float32
        )
        grad_keys = (
            jnp.einsum(
                "qhgk,qhgd->khd", grad_scores, query_rows, preferred_element_type=jnp.float32
            )
            * score_scale
        )
        grad_values = jnp.einsum(
            "qhgk,qhgd->khd",
            probabilities.astype(jnp.bfloat16),
            attention_output_gradient,
            preferred_element_type=jnp.float32,
        )
        return (grad_queries, (grad_keys, grad_values))

    grad_queries, (grad_keys, grad_values) = lax.scan(
        block_grads,
        jnp.zeros(query_rows.shape, jnp.float32),
        (blocked_keys, blocked_values, place_blocks),
    )
    return (grad_queries * score_scale, grad_keys, grad_values)


def gate_up_grads(grad_act, gate_up, hidden_units):
    gate_part = gate_up[..., :hidden_units]
    up_part = gate_up[..., hidden_units:]
    return jnp.concatenate(
        [grad_act * up_part * silu_slope(gate_part), grad_act * sigmoid_linear(gate_part)], axis=-1
    ).astype(jnp.bfloat16)


def on_device(
    hidden,
    teacher,
    valid_mask,
    routes,
    route_gates,
    gain_in,
    query_key_value_weight,
    out_weight,
    gain_mid,
    shared_weight,
    expert_weight,
):
    token_rows = hidden.shape[1]
    model_width = hidden.shape[2]
    context_count = lax.axis_size("ctx")
    shard_count = lax.axis_size("wt")
    seq_rows = token_rows * context_count
    all_tokens = seq_rows * shard_count
    query_groups = QUERY_HEADS // KEY_VALUE_HEADS
    query_total_width = QUERY_HEADS * HEAD_SIZE
    key_value_width = KEY_VALUE_HEADS * HEAD_SIZE
    score_scale = 1.0 / math.sqrt(HEAD_SIZE)
    key_row_count = min(512, seq_rows)
    number_of_blocks = seq_rows // key_row_count
    capacity = token_rows * TOP // 12
    local_experts = expert_weight.shape[0]
    contract_last = (((1,), (1,)), ((), ()))
    contract_first = (((0,), (0,)), ((), ()))
    full_gain_in, full_qkv, full_out, full_gain_mid, full_shared = (
        lax.all_gather(gain_in, "wt", axis=0, tiled=True),
        lax.all_gather(query_key_value_weight, "wt", axis=0, tiled=True),
        lax.all_gather(out_weight, "wt", axis=0, tiled=True),
        lax.all_gather(gain_mid, "wt", axis=0, tiled=True),
        lax.all_gather(shared_weight, "wt", axis=0, tiled=True),
    )
    gain_in_float = full_gain_in.astype(jnp.float32)
    gain_mid_float = full_gain_mid.astype(jnp.float32)
    inputs = hidden[0].astype(jnp.float32)
    scaled_in, inverse_in = normalize(inputs)
    normed_in = (scaled_in * gain_in_float).astype(jnp.bfloat16)
    projected_rows = jnp.dot(normed_in, full_qkv, preferred_element_type=jnp.float32).astype(
        jnp.bfloat16
    )
    query_rows = projected_rows[:, :query_total_width].reshape(
        token_rows, KEY_VALUE_HEADS, query_groups, HEAD_SIZE
    )
    context_local = projected_rows[:, query_total_width:]
    context_gathered = lax.all_gather(context_local, "ctx", axis=0, tiled=True)
    context_index = lax.axis_index("ctx")
    query_place = positions(
        context_index * token_rows + jnp.arange(token_rows, dtype=jnp.int32),
        token_rows,
        context_count,
    )
    place_blocks = positions(
        jnp.arange(seq_rows, dtype=jnp.int32), token_rows, context_count
    ).reshape(number_of_blocks, key_row_count)
    blocked_keys = context_gathered[:, :key_value_width].reshape(
        number_of_blocks, key_row_count, KEY_VALUE_HEADS, HEAD_SIZE
    )
    blocked_values = context_gathered[:, key_value_width:].reshape(
        number_of_blocks, key_row_count, KEY_VALUE_HEADS, HEAD_SIZE
    )
    attention_output, log_total = attend_forward(
        query_rows, blocked_keys, blocked_values, place_blocks, query_place, score_scale
    )
    mixed_rows = attention_output.reshape(token_rows, query_total_width).astype(jnp.bfloat16)
    middle = inputs + jnp.dot(mixed_rows, full_out, preferred_element_type=jnp.float32)
    scaled_mid, inverse_mid = normalize(middle)
    normed_mid = (scaled_mid * gain_mid_float).astype(jnp.bfloat16)
    shared_gate_up = jnp.dot(
        normed_mid, full_shared[:, : 2 * SF], preferred_element_type=jnp.float32
    )
    shared_act = (sigmoid_linear(shared_gate_up[:, :SF]) * shared_gate_up[:, SF:]).astype(
        jnp.bfloat16
    )
    shared_out = lax.dot_general(
        shared_act, full_shared[:, 2 * SF :], contract_last, preferred_element_type=jnp.float32
    )
    slot_table, slot_gate = route_tables(routes[0], route_gates[0], EXPERTS, capacity)
    padded_rows = jnp.concatenate([normed_mid, jnp.zeros((1, model_width), jnp.bfloat16)], axis=0)
    expert_rows = jnp.take(padded_rows, slot_table, axis=0)
    arrived = lax.all_to_all(expert_rows, "wt", split_axis=0, concat_axis=0, tiled=True)
    slot_count = arrived.shape[1]
    grouped = arrived.reshape(shard_count, local_experts, slot_count, model_width)
    owner_gate_up = jnp.einsum(
        "wesd,edf->wesf", grouped, expert_weight[:, :, : 2 * F], preferred_element_type=jnp.float32
    )
    owner_act = (sigmoid_linear(owner_gate_up[..., :F]) * owner_gate_up[..., F:]).astype(
        jnp.bfloat16
    )
    owner_out = jnp.einsum(
        "wesf,edf->wesd",
        owner_act,
        expert_weight[:, :, 2 * F :],
        preferred_element_type=jnp.float32,
    ).astype(jnp.bfloat16)
    returned = lax.all_to_all(
        owner_out.reshape(shard_count * local_experts, slot_count, model_width),
        "wt",
        split_axis=0,
        concat_axis=0,
        tiled=True,
    )
    expert_out, owner_rows, owner_gate_up, owner_act = (
        returned,
        arrived,
        owner_gate_up.reshape(shard_count * local_experts, slot_count, 2 * F),
        owner_act.reshape(shard_count * local_experts, slot_count, F),
    )
    routed = (
        jnp.zeros((token_rows + 1, model_width), jnp.float32)
        .at[slot_table]
        .add(expert_out.astype(jnp.float32) * slot_gate[..., None])[:token_rows]
    )
    final_state = middle + shared_out + routed
    valid_float = valid_mask[0].astype(jnp.float32)
    deviation = final_state - teacher[0].astype(jnp.float32)
    squared_local = jnp.sum(valid_float[:, None] * deviation * deviation)
    count_local = jnp.sum(valid_float)
    squared_total, valid_count = lax.psum((squared_local, count_local), ("ctx", "wt"))
    loss_value = 0.5 * squared_total / (valid_count * model_width)
    grad_final = all_tokens / valid_count * valid_float[:, None] * deviation
    grad_shared_out = grad_final.astype(jnp.bfloat16)
    grad_shared_act = jnp.dot(
        grad_shared_out, full_shared[:, 2 * SF :], preferred_element_type=jnp.float32
    )
    grad_shared_down = lax.dot_general(
        grad_shared_out, shared_act, contract_first, preferred_element_type=jnp.float32
    )
    grad_shared_gate_up = gate_up_grads(grad_shared_act, shared_gate_up, SF)
    grad_normed_mid = lax.dot_general(
        grad_shared_gate_up,
        full_shared[:, : 2 * SF],
        contract_last,
        preferred_element_type=jnp.float32,
    )
    grad_shared_front = lax.dot_general(
        normed_mid, grad_shared_gate_up, contract_first, preferred_element_type=jnp.float32
    )
    grad_shared_full = jnp.concatenate([grad_shared_front, grad_shared_down], axis=1)
    padded_grads = jnp.concatenate([grad_final, jnp.zeros((1, model_width), jnp.float32)], axis=0)
    grad_expert_out = (jnp.take(padded_grads, slot_table, axis=0) * slot_gate[..., None]).astype(
        jnp.bfloat16
    )
    grad_arrived = lax.all_to_all(grad_expert_out, "wt", split_axis=0, concat_axis=0, tiled=True)
    grad_grouped = grad_arrived.reshape(shard_count, local_experts, capacity, model_width)
    owner_gate_up_grouped = owner_gate_up.reshape(shard_count, local_experts, capacity, 2 * F)
    owner_act_grouped = owner_act.reshape(shard_count, local_experts, capacity, F)
    owner_rows_grouped = owner_rows.reshape(shard_count, local_experts, capacity, model_width)
    grad_owner_act = jnp.einsum(
        "wecd,edf->wecf",
        grad_grouped,
        expert_weight[:, :, 2 * F :],
        preferred_element_type=jnp.float32,
    )
    grad_owner_gate_up = gate_up_grads(grad_owner_act, owner_gate_up_grouped, F)
    grad_owner_rows = jnp.einsum(
        "wecf,edf->wecd",
        grad_owner_gate_up,
        expert_weight[:, :, : 2 * F],
        preferred_element_type=jnp.float32,
    ).astype(jnp.bfloat16)
    front = jnp.einsum(
        "wecd,wecf->edf", owner_rows_grouped, grad_owner_gate_up, preferred_element_type=jnp.float32
    )
    back = jnp.einsum(
        "wecd,wecf->edf", grad_grouped, owner_act_grouped, preferred_element_type=jnp.float32
    )
    expert_grad = jnp.concatenate([front, back], axis=2)
    grad_rows = lax.all_to_all(
        grad_owner_rows.reshape(shard_count * local_experts, capacity, model_width),
        "wt",
        split_axis=0,
        concat_axis=0,
        tiled=True,
    )
    grad_normed_mid = (
        grad_normed_mid
        + jnp.zeros((token_rows + 1, model_width), jnp.float32)
        .at[slot_table]
        .add(grad_rows.astype(jnp.float32))[:token_rows]
    )
    grad_gain_mid_local = jnp.sum(grad_normed_mid * scaled_mid, axis=0)
    grad_middle = grad_final + norm_back(grad_normed_mid, scaled_mid, inverse_mid, gain_mid_float)
    grad_branch = grad_middle.astype(jnp.bfloat16)
    mixed_gradient = lax.dot_general(
        grad_branch, full_out, contract_last, preferred_element_type=jnp.float32
    ).astype(jnp.bfloat16)
    grad_out_local = lax.dot_general(
        mixed_rows, grad_branch, contract_first, preferred_element_type=jnp.float32
    )
    context_recomputed = lax.all_gather(context_local, "ctx", axis=0, tiled=True)
    backward_keys = context_recomputed[:, :key_value_width].reshape(
        number_of_blocks, key_row_count, KEY_VALUE_HEADS, HEAD_SIZE
    )
    backward_values = context_recomputed[:, key_value_width:].reshape(
        number_of_blocks, key_row_count, KEY_VALUE_HEADS, HEAD_SIZE
    )
    attention_output_gradient = mixed_gradient.reshape(
        token_rows, KEY_VALUE_HEADS, query_groups, HEAD_SIZE
    )
    grad_queries, grad_keys, grad_values = attend_backward(
        query_rows,
        backward_keys,
        backward_values,
        place_blocks,
        query_place,
        log_total,
        attention_output_gradient,
        attention_output,
        score_scale,
    )
    grad_context_all = jnp.concatenate(
        [
            grad_keys.reshape(seq_rows, key_value_width),
            grad_values.reshape(seq_rows, key_value_width),
        ],
        axis=1,
    )
    grad_context = lax.psum_scatter(
        grad_context_all.astype(jnp.bfloat16), "ctx", scatter_dimension=0, tiled=True
    ).astype(jnp.float32)
    grad_projected = jnp.concatenate(
        [grad_queries.reshape(token_rows, query_total_width), grad_context], axis=1
    ).astype(jnp.bfloat16)
    grad_normed_in = lax.dot_general(
        grad_projected, full_qkv, contract_last, preferred_element_type=jnp.float32
    )
    grad_qkv_local = lax.dot_general(
        normed_in, grad_projected, contract_first, preferred_element_type=jnp.float32
    )
    grad_gain_in_local = jnp.sum(grad_normed_in * scaled_in, axis=0)
    grad_inputs = grad_middle + norm_back(grad_normed_in, scaled_in, inverse_in, gain_in_float)
    weight_sums = (
        lax.psum_scatter(
            grad_gain_in_local.astype(jnp.bfloat16), "wt", scatter_dimension=0, tiled=True
        ).astype(jnp.float32),
        lax.psum_scatter(
            grad_qkv_local.astype(jnp.bfloat16), "wt", scatter_dimension=0, tiled=True
        ).astype(jnp.float32),
        lax.psum_scatter(
            grad_out_local.astype(jnp.bfloat16), "wt", scatter_dimension=0, tiled=True
        ).astype(jnp.float32),
        lax.psum_scatter(
            grad_gain_mid_local.astype(jnp.bfloat16), "wt", scatter_dimension=0, tiled=True
        ).astype(jnp.float32),
        lax.psum_scatter(
            grad_shared_full.astype(jnp.bfloat16), "wt", scatter_dimension=0, tiled=True
        ).astype(jnp.float32),
    )
    summed = (
        lax.psum(weight_sums[0].astype(jnp.bfloat16), "ctx").astype(jnp.float32),
        lax.psum(weight_sums[1].astype(jnp.bfloat16), "ctx").astype(jnp.float32),
        lax.psum(weight_sums[2].astype(jnp.bfloat16), "ctx").astype(jnp.float32),
        lax.psum(weight_sums[3].astype(jnp.bfloat16), "ctx").astype(jnp.float32),
        lax.psum(weight_sums[4].astype(jnp.bfloat16), "ctx").astype(jnp.float32),
        lax.psum(expert_grad.astype(jnp.bfloat16), "ctx").astype(jnp.float32),
    )
    return (
        final_state.astype(jnp.bfloat16)[None],
        loss_value,
        grad_inputs[None],
        summed[0],
        summed[1],
        summed[2],
        summed[3],
        summed[4],
        summed[5],
    )


PLANE = [[0, 2, 4, 6], [1, 3, 5, 7]]
COSTS = {
    "project": 0.3,
    "attend": 0.3,
    "leave": 0.3,
    "join_shared": 0.3,
    "experts": 0.3,
    "experts_back": 0.3,
    "enter_back": 0.3,
    "attend_back": 0.3,
    "finish": 0.3,
    "weight_grad": 0.3,
    "expert_grad": 0.3,
    "blend_split": 0.3,
    "blend_pair": 0.3,
    "blend_sum": 0.3,
    "blend_stack": 0.3,
    "blend_four": 0.3,
    "place_pair": 0.3,
    "place_shared": 0.3,
    "place_heads": 0.3,
}


def flip(value, bit):
    return lax.ppermute(value, "ctx", [(index, index ^ bit) for index in range(8)])


def line_swap(value, offset):
    return lax.ppermute(value, "wt", [(index, index ^ offset) for index in range(4)])


def line_middle(value):
    return lax.ppermute(value, "wt", [(1, 2), (2, 1)])


def line_outward(value):
    return lax.ppermute(value, "wt", [(1, 0), (2, 3)])


def line_inward(value):
    return lax.ppermute(value, "wt", [(0, 1), (3, 2)])


def line_gather(value, at_end):
    near = line_swap(value, 1)
    middle = line_middle(value)
    middle_far = line_middle(near)
    outward = line_outward(middle)
    outward_far = line_outward(middle_far)
    return [
        value,
        near,
        jnp.where(at_end, outward, middle_far),
        jnp.where(at_end, outward_far, middle),
    ]


def line_reduce(parts):
    far = line_inward(parts[3])
    carried = parts[2] + far
    inward = line_inward(carried)
    crossed = line_middle(carried)
    near = line_swap(parts[1] + crossed, 1)
    middle = line_middle(parts[3] + inward)
    return (
        parts[0].astype(jnp.float32) + near.astype(jnp.float32) + middle.astype(jnp.float32)
    )


def chips_exchange(blocks):
    return lax.all_to_all(
        blocks,
        "ctx",
        split_axis=0,
        concat_axis=0,
        tiled=True,
        axis_index_groups=PLANE,
    )


def line_exchange(blocks):
    return lax.all_to_all(blocks, "wt", split_axis=0, concat_axis=0, tiled=True)


def chips_gather(value, x_last):
    along_x = flip(value, 2)
    along_y = flip(value, 4)
    corner = flip(along_y, 2) if x_last else flip(along_x, 4)
    return [value, along_x, along_y, corner]


def core_swap(values):
    return [flip(value, 1) for value in values]


def everywhere_sum(value):
    for bit in (1, 2, 4):
        value = value + flip(value, bit)
    for offset in (1, 2):
        value = value + line_swap(value, offset)
    return value


def pick(blocks, index):
    return lax.dynamic_index_in_dim(blocks, index, 0, keepdims=False)


def chips_reduce(keep, came):
    half = keep.shape[1] // 2
    upper = keep[:, :half] + came[:, :half]
    lower = keep[:, half:] + came[:, half:]
    upper_came = flip(upper[1::2], 2)
    lower_came = flip(lower[2:], 4)
    upper = upper[0::2] + upper_came
    lower = lower[:2] + lower_came
    upper_came = flip(upper[1], 4)
    lower_came = flip(lower[1], 2)
    return jnp.concatenate([upper[0] + upper_came, lower[0] + lower_came], axis=0)


def dot_plain(left, right):
    return lax.dot_general(
        left, right, (((1,), (0,)), ((), ())), preferred_element_type=jnp.float32
    )


def dot_last(left, right):
    return lax.dot_general(
        left, right, (((1,), (1,)), ((), ())), preferred_element_type=jnp.float32
    )


def dot_first(left, right):
    return lax.dot_general(
        left, right, (((0,), (0,)), ((), ())), preferred_element_type=jnp.float32
    )


def call(kernel, name, meta, arrays, grid, in_specs, out_specs, out_shape, scratch, flops, moved):
    return pl.pallas_call(
        kernel,
        grid_spec=pltpu.PrefetchScalarGridSpec(
            num_scalar_prefetch=1,
            grid=grid,
            in_specs=in_specs,
            out_specs=out_specs,
            scratch_shapes=scratch,
        ),
        out_shape=out_shape,
        compiler_params=pltpu.CompilerParams(vmem_limit_bytes=48 * 1024 * 1024),
        cost_estimate=pl.CostEstimate(
            flops=int(COSTS.get(name, 1.0) * 1e9), bytes_accessed=1000, transcendentals=0
        ),
        name=name,
    )(meta, *arrays)


def whole(array):
    rank = len(array.shape)
    return pl.BlockSpec(tuple(array.shape), lambda *_: (0,) * rank)


def shape_of(shape, dtype):
    return jax.ShapeDtypeStruct(shape, dtype)


def size_of(arrays):
    return sum(math.prod(a.shape) * a.dtype.itemsize for a in arrays)


def blend(meta, name, function, arrays, pieces=4):
    rows = arrays[0].shape[-2]
    tile = rows // pieces
    outs = jax.eval_shape(function, *[shape_of(a.shape, a.dtype) for a in arrays])
    many = isinstance(outs, (list, tuple))
    outs = list(outs) if many else [outs]

    def spec(a):
        rank = len(a.shape)
        lead = a.shape[:-2]
        return pl.BlockSpec(
            tuple(lead) + (tile, a.shape[-1]),
            lambda i, m: (0,) * (rank - 2) + (i, 0),
        )

    def kernel(meta_ref, *refs):
        result = function(*[ref[...] for ref in refs[: len(arrays)]])
        result = list(result) if many else [result]
        for ref, value in zip(refs[len(arrays) :], result):
            ref[...] = value

    result = call(
        kernel,
        name,
        meta,
        arrays,
        (pieces,),
        [spec(a) for a in arrays],
        [spec(a) for a in outs],
        outs,
        [],
        0,
        0,
    )
    return result if many else result[0]


def aligned(value, step):
    return pl.multiple_of(value * step, step)


def project_kernel(meta, blocks_ref, gain_ref, mine, other, *refs):
    normed_ref, query_ref, pair_ref, weight_ref = refs
    core = meta[0] & 1
    rows = mine.shape[1]

    @pl.when(pl.program_id(0) == 0)
    def _():
        for i in range(4):
            at = 2 * (meta[1] ^ i)
            weight_ref[pl.ds(aligned(at + core, rows), rows), :] = mine[i]
            weight_ref[pl.ds(aligned(at + 1 - core, rows), rows), :] = other[i]

    states = blocks_ref[0].astype(jnp.float32)
    inverse = lax.rsqrt(jnp.mean(states * states, axis=-1, keepdims=True) + norm_eps)
    normed = (states * inverse * gain_ref[...]).astype(jnp.bfloat16)
    normed_ref[0] = normed
    projected = dot_plain(normed, weight_ref[...]).astype(jnp.bfloat16)
    query_width = query_ref.shape[-1]
    query_ref[0] = projected[:, :query_width]
    pair_ref[0] = projected[:, query_width:]


def project(meta, blocks, gain, mine, other, query_width):
    _, token_rows, width = blocks.shape
    columns = mine.shape[2]
    arrays = [blocks, gain, mine, other]
    outs = [
        shape_of((4, token_rows, width), jnp.bfloat16),
        shape_of((4, token_rows, query_width), jnp.bfloat16),
        shape_of((4, token_rows, columns - query_width), jnp.bfloat16),
        shape_of((width, columns), jnp.bfloat16),
    ]
    return call(
        project_kernel,
        "project",
        meta,
        arrays,
        (4,),
        [pl.BlockSpec((1, token_rows, width), lambda r, m: (r, 0, 0))]
        + [whole(a) for a in arrays[1:]],
        [
            pl.BlockSpec((1, token_rows, width), lambda r, m: (r, 0, 0)),
            pl.BlockSpec((1, token_rows, query_width), lambda r, m: (r, 0, 0)),
            pl.BlockSpec((1, token_rows, columns - query_width), lambda r, m: (r, 0, 0)),
            whole(outs[3]),
        ],
        outs,
        [],
        2 * 4 * token_rows * width * columns,
        size_of(arrays) + size_of(outs),
    )


def sort_pairs(meta, mine_ref, other_ref, keys, values):
    half = mine_ref.shape[1] // 2
    for slot in range(16):
        block, part = (slot, 0) if slot < 8 else (15 - slot, 1)
        place = block >> 1
        rows = pl.ds(part * half, half)
        to = pl.ds(slot * half, half)

        @pl.when((meta[0] & 1) == (block & 1))
        def _():
            keys[to, :] = mine_ref[place, rows, :HEAD_SIZE]
            values[to, :] = mine_ref[place, rows, HEAD_SIZE:]

        @pl.when((meta[0] & 1) != (block & 1))
        def _():
            keys[to, :] = other_ref[place, rows, :HEAD_SIZE]
            values[to, :] = other_ref[place, rows, HEAD_SIZE:]


def stack_heads(rows):
    count = rows.shape[1] // HEAD_SIZE
    return jnp.concatenate(
        [rows[:, h * HEAD_SIZE : (h + 1) * HEAD_SIZE] for h in range(count)], axis=0
    )


def unstack_heads(rows, count):
    each = rows.shape[0] // count
    return jnp.concatenate([rows[h * each : (h + 1) * each] for h in range(count)], axis=1)


def step_slot(meta):
    step = pl.program_id(0)
    block = 2 * (step >> 1) + (meta[0] & 1)
    return jnp.where((step & 1) == 0, block, 15 - block)


def allowed_pairs(start, slot, shape, half):
    key_place = start + lax.broadcasted_iota(jnp.int32, shape, 0)
    query_place = slot * half + (lax.broadcasted_iota(jnp.int32, shape, 1) & (half - 1))
    return key_place <= query_place


def key_spans(step, half, span):
    pairs = (step // 2 if step % 2 == 0 else 7 - step // 2) + 1
    rows = pairs * 2 * half
    return [(at, min(span, rows - at)) for at in range(0, rows, span)]


def attend_kernel(scale, span, meta, query_ref, mine_ref, other_ref, *refs):
    out_ref, log_ref, keys, values, values_turned = refs
    half, group_width = query_ref.shape[1:]
    count = group_width // HEAD_SIZE

    @pl.when(pl.program_id(0) == 0)
    def _():
        sort_pairs(meta, mine_ref, other_ref, keys, values)
        values_turned[...] = values[...].T

    slot = step_slot(meta)
    query = stack_heads(query_ref[0])
    wide = count * half

    def run(spans):
        highest = jnp.full((1, wide), masked_score, jnp.float32)
        total = jnp.zeros((1, wide), jnp.float32)
        mixed = jnp.zeros((HEAD_SIZE, wide), jnp.float32)
        for start, size in spans:
            at = pl.ds(start, size)
            scores = dot_last(keys[at, :], query) * scale
            if start == spans[-1][0]:
                seen = allowed_pairs(start, slot, scores.shape, half)
                scores = jnp.where(seen, scores, masked_score)
            new = jnp.maximum(highest, jnp.max(scores, axis=0, keepdims=True))
            rescale = jnp.exp(highest - new)
            powers = jnp.exp(scores - new)
            total = total * rescale + jnp.sum(powers, axis=0, keepdims=True)
            mixed = mixed * rescale + dot_plain(
                values_turned[:, at], powers.astype(jnp.bfloat16)
            )
            highest = new
        log_ref[0] = highest + jnp.log(total)
        out_ref[0] = unstack_heads((mixed / total).T, count).astype(jnp.bfloat16)

    for step in range(8):

        @pl.when(pl.program_id(0) == step)
        def _():
            run(key_spans(step, half, span))


def attend(meta, query, mine, other, scale):
    token_rows, group_width = query.shape[1:]
    half = token_rows // 2
    count = group_width // HEAD_SIZE
    everything = 8 * token_rows
    span = 1024
    arrays = [query, mine, other]
    outs = [
        shape_of(query.shape, jnp.bfloat16),
        shape_of((8, 1, count * half), jnp.float32),
    ]
    return call(
        functools.partial(attend_kernel, scale, span),
        "attend",
        meta,
        arrays,
        (8,),
        [
            pl.BlockSpec((1, half, group_width), lambda i, m: (i // 2, i % 2, 0)),
            whole(mine),
            whole(other),
        ],
        [
            pl.BlockSpec((1, half, group_width), lambda i, m: (i // 2, i % 2, 0)),
            pl.BlockSpec((1, 1, count * half), lambda i, m: (i, 0, 0)),
        ],
        outs,
        [
            pltpu.VMEM((everything, HEAD_SIZE), jnp.bfloat16),
            pltpu.VMEM((everything, HEAD_SIZE), jnp.bfloat16),
            pltpu.VMEM((HEAD_SIZE, everything), jnp.bfloat16),
        ],
        2 * 2 * 4 * token_rows * everything * group_width,
        size_of(arrays) + size_of(outs),
    )


def attend_back_kernel(scale, span, meta, query_ref, mine_ref, other_ref, log_ref, *refs):
    mixed_ref, grad_ref, grad_query_ref, grad_mine_ref, grad_other_ref = refs[:5]
    keys, values, keys_turned, grad_keys, grad_values = refs[5:]
    step = pl.program_id(0)
    half, group_width = query_ref.shape[1:]
    count = group_width // HEAD_SIZE

    @pl.when(step == 0)
    def _():
        sort_pairs(meta, mine_ref, other_ref, keys, values)
        keys_turned[...] = keys[...].T
        grad_keys[...] = jnp.zeros_like(grad_keys)
        grad_values[...] = jnp.zeros_like(grad_values)

    slot = step_slot(meta)
    query = stack_heads(query_ref[0])
    mixed = stack_heads(mixed_ref[0]).astype(jnp.float32)
    grad = stack_heads(grad_ref[0])
    delta = jnp.sum((mixed * grad.astype(jnp.float32)).T, axis=0, keepdims=True)
    log_total = log_ref[0]

    def run(spans):
        grad_turned = jnp.zeros((HEAD_SIZE, count * half), jnp.float32)
        for start, size in spans:
            at = pl.ds(start, size)
            scores = dot_last(keys[at, :], query) * scale
            probs = jnp.exp(scores - log_total)
            if start == spans[-1][0]:
                probs = jnp.where(allowed_pairs(start, slot, probs.shape, half), probs, 0.0)
            grad_probs = dot_last(values[at, :], grad)
            grad_scores = (probs * (grad_probs - delta)).astype(jnp.bfloat16)
            grad_values[at, :] += dot_plain(probs.astype(jnp.bfloat16), grad)
            grad_keys[at, :] += dot_plain(grad_scores, query)
            grad_turned += dot_plain(keys_turned[:, at], grad_scores)
        grad_query_ref[0] = unstack_heads((grad_turned * scale).T, count).astype(jnp.bfloat16)

    for at_step in range(8):

        @pl.when(step == at_step)
        def _():
            run(key_spans(at_step, half, span))

    @pl.when(step == 7)
    def _():
        for slot_at in range(16):
            block, part = (slot_at, 0) if slot_at < 8 else (15 - slot_at, 1)
            place = block >> 1
            rows = pl.ds(part * half, half)
            here = pl.ds(slot_at * half, half)
            both = jnp.concatenate([grad_keys[here, :] * scale, grad_values[here, :]], axis=1)

            @pl.when((meta[0] & 1) == (block & 1))
            def _():
                grad_mine_ref[place, rows, :] = both

            @pl.when((meta[0] & 1) != (block & 1))
            def _():
                grad_other_ref[place, rows, :] = both.astype(jnp.bfloat16)


def attend_back(meta, query, mine, other, log_total, mixed, grad, scale):
    token_rows, group_width = query.shape[1:]
    half = token_rows // 2
    count = group_width // HEAD_SIZE
    everything = 8 * token_rows
    span = 512
    arrays = [query, mine, other, log_total, mixed, grad]
    outs = [
        shape_of(query.shape, jnp.bfloat16),
        shape_of(mine.shape, jnp.float32),
        shape_of(mine.shape, jnp.bfloat16),
    ]
    return call(
        functools.partial(attend_back_kernel, scale, span),
        "attend_back",
        meta,
        arrays,
        (8,),
        [
            pl.BlockSpec((1, half, group_width), lambda i, m: (i // 2, i % 2, 0)),
            whole(mine),
            whole(other),
            pl.BlockSpec((1, 1, count * half), lambda i, m: (i, 0, 0)),
            pl.BlockSpec((1, half, group_width), lambda i, m: (i // 2, i % 2, 0)),
            pl.BlockSpec((1, half, group_width), lambda i, m: (i // 2, i % 2, 0)),
        ],
        [
            pl.BlockSpec((1, half, group_width), lambda i, m: (i // 2, i % 2, 0)),
            whole(outs[1]),
            whole(outs[2]),
        ],
        outs,
        [
            pltpu.VMEM((everything, HEAD_SIZE), jnp.bfloat16),
            pltpu.VMEM((everything, HEAD_SIZE), jnp.bfloat16),
            pltpu.VMEM((HEAD_SIZE, everything), jnp.bfloat16),
            pltpu.VMEM((everything, HEAD_SIZE), jnp.float32),
            pltpu.VMEM((everything, HEAD_SIZE), jnp.float32),
        ],
        5 * 2 * 4 * token_rows * everything * group_width,
        size_of(arrays) + size_of(outs),
    )


def leave_kernel(meta, *refs):
    parts, mine, other, states_ref, gain_ref = refs[:4], *refs[4:8]
    weight_ref, middle_ref, normed_ref = refs[8:]
    core, chip = meta[0] & 1, meta[0] >> 1
    rows = mine.shape[1]
    for i in range(4):
        weight_ref[pl.ds(aligned(2 * i + core, rows), rows), :] = mine[i]
        weight_ref[pl.ds(aligned(2 * i + 1 - core, rows), rows), :] = other[i]
    middle = states_ref[...].astype(jnp.float32)
    for r in range(4):
        at = pl.ds(aligned(chip ^ r, 2 * rows), 2 * rows)
        middle += dot_plain(parts[r][...], weight_ref[at, :])
    middle_ref[...] = middle
    inverse = lax.rsqrt(jnp.mean(middle * middle, axis=-1, keepdims=True) + norm_eps)
    normed_ref[...] = (middle * inverse * gain_ref[...]).astype(jnp.bfloat16)


def leave(meta, parts, mine, other, states, gain):
    token_rows, width = states.shape
    arrays = list(parts) + [mine, other, states, gain]
    outs = [
        shape_of((8 * mine.shape[1], width), jnp.bfloat16),
        shape_of((token_rows, width), jnp.float32),
        shape_of((token_rows, width), jnp.bfloat16),
    ]
    return call(
        leave_kernel,
        "leave",
        meta,
        arrays,
        (1,),
        [whole(a) for a in arrays],
        [whole(a) for a in outs],
        outs,
        [],
        2 * token_rows * width * width,
        size_of(arrays) + size_of(outs),
    )


def norm_back_rows(grad_normed, states, gain):
    inverse = lax.rsqrt(jnp.mean(states * states, axis=-1, keepdims=True) + norm_eps)
    scaled = states * inverse
    gain_grad = jnp.sum(grad_normed * scaled, axis=0, keepdims=True)
    grad_scaled = grad_normed * gain
    shift = jnp.mean(grad_scaled * scaled, axis=-1, keepdims=True)
    return inverse * (grad_scaled - scaled * shift), gain_grad


def enter_back_kernel(meta, final_ref, normed_ref, middle_ref, gain_ref, weight_ref, *refs):
    grad_ref, branch_ref, gain_grad_ref, mixed_ref = refs
    grad, gain_grad = norm_back_rows(normed_ref[...], middle_ref[...], gain_ref[...])
    grad = grad + final_ref[...]
    grad_ref[...] = grad
    gain_grad_ref[...] = gain_grad
    branch = grad.astype(jnp.bfloat16)
    branch_ref[...] = branch
    rows = weight_ref.shape[0] // 4
    for r in range(4):
        mixed_ref[r] = dot_last(branch, weight_ref[rows * r : rows * (r + 1), :]).astype(
            jnp.bfloat16
        )


def enter_back(meta, grad_final, grad_normed, middle, gain, weight):
    token_rows, width = middle.shape
    arrays = [grad_final, grad_normed, middle, gain, weight]
    outs = [
        shape_of((token_rows, width), jnp.float32),
        shape_of((token_rows, width), jnp.bfloat16),
        shape_of((1, width), jnp.float32),
        shape_of((4, token_rows, weight.shape[0] // 4), jnp.bfloat16),
    ]
    return call(
        enter_back_kernel,
        "enter_back",
        meta,
        arrays,
        (1,),
        [whole(a) for a in arrays],
        [whole(a) for a in outs],
        outs,
        [],
        2 * token_rows * width * width,
        size_of(arrays) + size_of(outs),
    )


def finish_kernel(meta, *refs):
    parts, mine, other = refs[:3]
    states_ref, middle_ref, gain_ref, grad_ref, gain_grad_ref, total = refs[3:]
    core, chip = meta[0] & 1, meta[0] >> 1
    columns = mine.shape[1]
    for at, weights in ((core, mine), (1 - core, other)):
        total[:, pl.ds(aligned(at, columns), columns)] = sum(
            dot_last(parts[r], weights[chip ^ r]) for r in range(4)
        )
    grad, gain_grad = norm_back_rows(
        total[...], states_ref[...].astype(jnp.float32), gain_ref[...]
    )
    grad_ref[0] = grad + middle_ref[...]
    gain_grad_ref[...] = gain_grad


def finish(meta, parts, mine, other, states, grad_middle, gain):
    token_rows, width = states.shape
    arrays = [parts, mine, other, states, grad_middle, gain]
    outs = [
        shape_of((1, token_rows, width), jnp.float32),
        shape_of((1, width), jnp.float32),
    ]
    return call(
        finish_kernel,
        "finish",
        meta,
        arrays,
        (1,),
        [whole(a) for a in arrays],
        [whole(a) for a in outs],
        outs,
        [pltpu.VMEM((token_rows, width), jnp.float32)],
        2 * token_rows * width * 4 * parts.shape[2],
        size_of(arrays) + size_of(outs),
    )


def gated(gate_up, units):
    gate_part = gate_up[:, :units]
    sigma = 1.0 / (1.0 + jnp.exp(-gate_part))
    return gate_part * sigma * gate_up[:, units:]


def gated_back(grad_act, gate_up, units):
    gate_part = gate_up[:, :units].astype(jnp.float32)
    up_part = gate_up[:, units:].astype(jnp.float32)
    sigma = 1.0 / (1.0 + jnp.exp(-gate_part))
    linear = gate_part * sigma
    grad_gate = grad_act * up_part * (sigma * (1.0 + gate_part * (1.0 - sigma)))
    return grad_gate, grad_act * linear, linear * up_part


def experts_kernel(
    meta, rows_ref, gates_ref, expert_ref, shared_ref, gate_up_ref, shared_gate_up_ref, out_ref, total
):
    expert = pl.program_id(0)
    rows = rows_ref[...]

    @pl.when(expert == 0)
    def _():
        units = shared_ref.shape[1] // 3
        gate_up = dot_plain(rows, shared_ref[:, : 2 * units])
        shared_gate_up_ref[...] = gate_up.astype(jnp.bfloat16)
        act = gated(gate_up, units).astype(jnp.bfloat16)
        total[...] = dot_last(act, shared_ref[:, 2 * units :])

    gate_up = dot_plain(rows, expert_ref[0, :, : 2 * F])
    gate_up_ref[0] = gate_up.astype(jnp.bfloat16)
    act = (gated(gate_up, F) * gates_ref[0]).astype(jnp.bfloat16)
    total[...] += dot_last(act, expert_ref[0, :, 2 * F :])

    @pl.when(expert == pl.num_programs(0) - 1)
    def _():
        out_ref[...] = total[...].astype(jnp.bfloat16)


def experts(meta, rows, gates, expert_weight, shared_slice):
    local_experts, width, _ = expert_weight.shape
    token_rows = rows.shape[0]
    shared_units = shared_slice.shape[1] // 3
    arrays = [rows, gates, expert_weight, shared_slice]
    outs = [
        shape_of((local_experts, token_rows, 2 * F), jnp.bfloat16),
        shape_of((token_rows, 2 * shared_units), jnp.bfloat16),
        shape_of((token_rows, width), jnp.bfloat16),
    ]
    return call(
        experts_kernel,
        "experts",
        meta,
        arrays,
        (local_experts,),
        [
            whole(rows),
            pl.BlockSpec((1, token_rows, 1), lambda e, m: (e, 0, 0)),
            pl.BlockSpec((1, width, 3 * F), lambda e, m: (e, 0, 0)),
            whole(shared_slice),
        ],
        [
            pl.BlockSpec((1, token_rows, 2 * F), lambda e, m: (e, 0, 0)),
            whole(outs[1]),
            whole(outs[2]),
        ],
        outs,
        [pltpu.VMEM((token_rows, width), jnp.float32)],
        2 * token_rows * width * 3 * (F * local_experts + shared_units),
        size_of(arrays) + size_of(outs),
    )


def experts_back_kernel(
    meta,
    grad_ref,
    gates_ref,
    gate_up_ref,
    shared_gate_up_ref,
    expert_ref,
    shared_ref,
    grad_gate_up_ref,
    act_ref,
    shared_grad_ref,
    shared_act_ref,
    grad_rows_ref,
    total,
):
    expert = pl.program_id(0)
    grad = grad_ref[...]

    @pl.when(expert == 0)
    def _():
        units = shared_ref.shape[1] // 3
        grad_act = dot_plain(grad, shared_ref[:, 2 * units :])
        grad_gate, grad_up, act = gated_back(grad_act, shared_gate_up_ref[...], units)
        both = jnp.concatenate([grad_gate, grad_up], axis=1).astype(jnp.bfloat16)
        shared_grad_ref[0] = both
        shared_act_ref[0] = act.astype(jnp.bfloat16)
        total[...] = dot_last(both, shared_ref[:, : 2 * units])

    grad_act = dot_plain(grad, expert_ref[0, :, 2 * F :]) * gates_ref[0]
    grad_gate, grad_up, act = gated_back(grad_act, gate_up_ref[0], F)
    both = jnp.concatenate([grad_gate, grad_up], axis=1).astype(jnp.bfloat16)
    grad_gate_up_ref[0] = both
    act_ref[0] = (act * gates_ref[0]).astype(jnp.bfloat16)
    total[...] += dot_last(both, expert_ref[0, :, : 2 * F])

    @pl.when(expert == pl.num_programs(0) - 1)
    def _():
        grad_rows_ref[...] = total[...].astype(jnp.bfloat16)


def experts_back(meta, grad, gates, gate_up, shared_gate_up, expert_weight, shared_slice):
    local_experts, width, _ = expert_weight.shape
    token_rows = grad.shape[0]
    shared_units = shared_slice.shape[1] // 3
    arrays = [grad, gates, gate_up, shared_gate_up, expert_weight, shared_slice]
    outs = [
        shape_of((local_experts, token_rows, 2 * F), jnp.bfloat16),
        shape_of((local_experts, token_rows, F), jnp.bfloat16),
        shape_of((1, token_rows, 2 * shared_units), jnp.bfloat16),
        shape_of((1, token_rows, shared_units), jnp.bfloat16),
        shape_of((token_rows, width), jnp.bfloat16),
    ]
    return call(
        experts_back_kernel,
        "experts_back",
        meta,
        arrays,
        (local_experts,),
        [
            whole(grad),
            pl.BlockSpec((1, token_rows, 1), lambda e, m: (e, 0, 0)),
            pl.BlockSpec((1, token_rows, 2 * F), lambda e, m: (e, 0, 0)),
            whole(shared_gate_up),
            pl.BlockSpec((1, width, 3 * F), lambda e, m: (e, 0, 0)),
            whole(shared_slice),
        ],
        [
            pl.BlockSpec((1, token_rows, 2 * F), lambda e, m: (e, 0, 0)),
            pl.BlockSpec((1, token_rows, F), lambda e, m: (e, 0, 0)),
            whole(outs[2]),
            whole(outs[3]),
            whole(outs[4]),
        ],
        outs,
        [pltpu.VMEM((token_rows, width), jnp.float32)],
        2 * token_rows * width * 3 * (F * local_experts + shared_units),
        size_of(arrays) + size_of(outs),
    )


def weight_grad_kernel(pairs, core_at, meta, *refs):
    keep_ref, give_ref = refs[-2:]
    at = 0
    columns = 0
    parts = []
    for count in pairs:
        lefts, rights = refs[at : at + count], refs[at + count : at + 2 * count]
        at += 2 * count
        parts.append(
            sum(dot_first(a[...], b[0]) for a, b in zip(lefts, rights)).astype(jnp.bfloat16)
        )
    half = keep_ref.shape[1]

    for core, (first, second) in ((0, (keep_ref, give_ref)), (1, (give_ref, keep_ref))):

        @pl.when((meta[core_at] & 1) == core)
        def _():
            start = 0
            for part in parts:
                stop = start + part.shape[1]
                first[0, :, start:stop] = part[:half]
                second[0, :, start:stop] = part[half:]
                start = stop


def expert_grad_kernel(count, meta, *refs):
    rows, grads, front, acts = (refs[i * count : (i + 1) * count] for i in range(4))
    out_ref = refs[-1] if len(refs) == 4 * count + 1 else refs[-2]
    tile = rows[0].shape[1]
    both = 3 * F

    def pair(front_refs, act_refs):
        return [
            sum(dot_first(a[...], b[0]) for a, b in zip(left, right)).astype(jnp.bfloat16)
            for left, right in ((rows, front_refs), (grads, act_refs))
        ]

    left, right = pair(front, acts)
    out_ref[0, :tile, : left.shape[1]] = left
    out_ref[0, :tile, left.shape[1] : both] = right
    if len(refs) > 4 * count + 1:
        held = refs[-1]
        left, right = pair(refs[4 * count : 5 * count], refs[5 * count : 6 * count])
        split, columns = left.shape[1], left.shape[1] + right.shape[1]
        held[:, :split] = left
        held[:, split:] = right
        quarter = tile // 4
        first = 2 * meta[2]
        out_ref[0, tile:, :columns] = held[pl.ds(aligned(first, quarter), quarter), :]
        out_ref[0, tile:, columns:] = held[pl.ds(aligned(first + 1, quarter), quarter), :]


def expert_grad(meta, expert, half, rows, grads, front, acts, shared=None):
    count = len(rows)
    token_rows, width = rows[0].shape
    tile = width // 4
    arrays = list(rows) + list(grads) + list(front) + list(acts)
    column = pl.BlockSpec((token_rows, tile), lambda i, m: (0, i ^ m[0]))

    def of_expert(a):
        return pl.BlockSpec((1,) + a.shape[1:], lambda i, m: (m[1], 0, 0))

    in_specs = [column] * (2 * count) + [of_expert(a) for a in arrays[2 * count :]]
    below, scratch = 0, []
    if shared is not None:
        arrays += list(shared[0]) + list(shared[1])
        in_specs += [whole(a) for a in arrays[4 * count :]]
        below = tile // 4
        columns = shared[0][0].shape[-1] + shared[1][0].shape[-1]
        scratch = [pltpu.VMEM((tile, columns), jnp.bfloat16)]
    return call(
        functools.partial(expert_grad_kernel, count),
        "expert_grad",
        jnp.stack([meta[0] >> 1, expert, half]),
        arrays,
        (4,),
        in_specs,
        pl.BlockSpec((1, tile + below, 3 * F), lambda i, m: (i, 0, 0)),
        shape_of((4, tile + below, 3 * F), jnp.bfloat16),
        scratch,
        0,
        0,
    )


def weight_grad(meta, order, operands, index):
    token_rows, width = operands[0][0][0].shape
    tile = width // 4
    scalars = jnp.stack([order, meta[0]])
    arrays, in_specs, columns = [], [], 0
    for lefts, rights in operands:
        arrays += list(lefts) + list(rights)
        in_specs += [pl.BlockSpec((token_rows, tile), lambda i, m: (0, i ^ m[0]))] * len(lefts)
        units = rights[0].shape[-1]
        at = index if rights[0].shape[0] > 1 else 0
        in_specs += [
            pl.BlockSpec((1, token_rows, units), lambda i, m, at=at: (at, 0, 0))
        ] * len(rights)
        columns += units
    tokens = token_rows * len(operands[0][0])
    counts = [len(left) for left, _ in operands]
    outs = [shape_of((4, tile // 2, columns), jnp.bfloat16)] * 2
    return call(
        functools.partial(weight_grad_kernel, counts, 1),
        "weight_grad",
        scalars,
        arrays,
        (4,),
        in_specs,
        [pl.BlockSpec((1, tile // 2, columns), lambda i, m: (i, 0, 0))] * 2,
        outs,
        [],
        2 * tokens * width * columns,
        size_of(outs) + 4 * tokens * width + 2 * tokens * columns,
    )


def place_pair_kernel(meta, *refs):
    mine, other, out_ref = refs[-3:]
    rows = out_ref.shape[1]

    @pl.when(pl.program_id(0) == 0)
    def _():
        out_ref[0] = mine[0, :rows].astype(jnp.float32)

    @pl.when(pl.program_id(0) == 1)
    def _():
        out_ref[0] = other[0, :rows].astype(jnp.float32)


def place_pair(meta, total, index, shape, mine, other):
    _, rows, columns = mine.shape
    arrays = [mine, other]
    in_specs = [
        pl.BlockSpec((1, rows, columns), lambda k, r, m: ((1 - k) * r + 3 * k, 0, 0)),
        pl.BlockSpec((1, rows, columns), lambda k, r, m: (k * r, 0, 0)),
    ]
    aliases = {}
    if total is not None:
        arrays = [total] + arrays
        in_specs = [pl.BlockSpec(memory_space=pl.ANY)] + in_specs
        aliases = {1: 0}
    return pl.pallas_call(
        place_pair_kernel,
        grid_spec=pltpu.PrefetchScalarGridSpec(
            num_scalar_prefetch=1,
            grid=(2, 4),
            in_specs=in_specs,
            out_specs=pl.BlockSpec(
                (1, shape[1] // 4, shape[2]),
                lambda k, r, m: (2 * ((m[0] & 1) ^ k) + index, (m[0] >> 1) ^ r, 0),
            ),
        ),
        out_shape=shape_of(shape, jnp.float32),
        input_output_aliases=aliases,
        compiler_params=pltpu.CompilerParams(vmem_limit_bytes=48 * 1024 * 1024),
        cost_estimate=pl.CostEstimate(
            flops=int(COSTS.get("place_pair", 1.0) * 1e9), bytes_accessed=1000, transcendentals=0
        ),
        name="place_pair",
    )(meta, *arrays)


def place_shared_kernel(meta, mine_low, mine_high, other_low, other_high, out_ref):
    core = meta[0] & 1
    rows = mine_low.shape[1]
    for at, low, high in ((core, mine_low, mine_high), (1 - core, other_low, other_high)):
        out_ref[pl.ds(aligned(2 * at, rows), rows), :] = low[0].astype(jnp.float32)
        out_ref[pl.ds(aligned(2 * at + 1, rows), rows), :] = high[0].astype(jnp.float32)


def place_shared(meta, mine, other):
    _, rows, columns = mine.shape
    units = columns // 6
    low = pl.BlockSpec((1, rows, units), lambda i, j, m: (i, 0, j))
    high = pl.BlockSpec((1, rows, units), lambda i, j, m: (i, 0, 3 + j))
    outs = shape_of((4 * rows, 2 * columns), jnp.float32)
    return call(
        place_shared_kernel,
        "place_shared",
        meta,
        [mine, mine, other, other],
        (4, 3),
        [low, high, low, high],
        pl.BlockSpec((4 * rows, units), lambda i, j, m: (0, 4 * j + (m[1] ^ i))),
        outs,
        [],
        0,
        0,
    )


def place_heads_kernel(meta, *refs):
    mine, other, out_ref = refs[:4], refs[4], refs[5]
    core, chip = meta[0] & 1, meta[0] >> 1
    rows, columns = mine[0].shape
    group_width = columns - 2 * HEAD_SIZE
    for r in range(4):
        head = chip ^ r
        for at, pieces in ((core, [piece[...] for piece in mine]), (1 - core, other)):
            to = pl.ds(aligned(at, rows), rows)
            values = pieces[r].astype(jnp.float32)
            out_ref[to, pl.ds(aligned(head, group_width), group_width)] = values[:, :group_width]
            out_ref[to, pl.ds(aligned(4 * group_width // HEAD_SIZE + head, HEAD_SIZE), HEAD_SIZE)] = (
                values[:, group_width : group_width + HEAD_SIZE]
            )
            out_ref[
                to, pl.ds(aligned(4 * group_width // HEAD_SIZE + 4 + head, HEAD_SIZE), HEAD_SIZE)
            ] = values[:, group_width + HEAD_SIZE :]


def place_heads(meta, mine, other):
    rows, columns = mine[0].shape
    arrays = list(mine) + [other]
    outs = shape_of((2 * rows, 4 * columns), jnp.float32)
    return call(
        place_heads_kernel,
        "place_heads",
        meta,
        arrays,
        (1,),
        [whole(a) for a in arrays],
        whole(outs),
        outs,
        [],
        0,
        size_of(arrays + [outs]),
    )


def join_shared_kernel(meta, mine, other, out_ref):
    step = pl.program_id(0)
    rows = mine.shape[2]
    first = meta[0] ^ (2 * step)
    for i in range(4):
        at = 8 * (meta[1] ^ i)
        out_ref[pl.ds(aligned(at + first, rows), rows), :] = mine[0, i]
        out_ref[pl.ds(aligned(at + (first ^ 1), rows), rows), :] = other[0, i]


def join_shared(meta, mine, other):
    _, _, rows, columns = mine.shape
    block = pl.BlockSpec((1, 4, rows, columns), lambda r, m: (r, 0, 0, 0))
    outs = shape_of((32 * rows, columns), jnp.bfloat16)
    return call(
        join_shared_kernel,
        "join_shared",
        meta,
        [mine, other],
        (4,),
        [block, block],
        whole(outs),
        outs,
        [],
        0,
        size_of([mine, other, outs]),
    )


class Clock:
    def __init__(self):
        self.last = None

    def __call__(self, *values):
        if self.last is None:
            return values if len(values) > 1 else values[0]
        held = lax.optimization_barrier(tuple(values) + (self.last,))[:-1]
        return held if len(held) > 1 else held[0]

    def mark(self, value):
        self.last = value
        return value


EARLY = (
    "H", "W", "K", "S", "K", "W", "S", "W", "K", "S", "O", "S", "M", "M", "S", "O", "M", "S", "M", "R", "M", "K", "M", "K",
    "M", "K", "R", "M", "K", "M", "M", "M", "M", "R", "M", "M",
)
LATE = (
    "L", "0", "1", "0", "0", "L", "1", "1", "L", "L", "O", "0", "L", "1", "L", "1", "0", "O", "Q", "1", "O", "L", "Q", "0",
    "O", "L", "Q", "Q", "O", "Q", "L", "1", "0", "O", "Q", "S", "L", "O", "Q", "1", "S", "L", "0", "O", "Q", "L", "Q", "O",
    "S",
)


def fast_device(
    hidden,
    teacher,
    valid_mask,
    routes,
    route_gates,
    gain_in,
    query_key_value_weight,
    out_weight,
    gain_mid,
    shared_weight,
    expert_weight,
):
    token_rows, width = hidden.shape[1:]
    context_count, shard_count = 8, 4
    context_index = lax.axis_index("ctx").astype(jnp.int32)
    shard_index = lax.axis_index("wt").astype(jnp.int32)
    plain_meta = jnp.stack([context_index, shard_index])
    core = context_index & 1
    chip = context_index >> 1
    at_end = (shard_index == 0) | (shard_index == shard_count - 1)
    group_width = QUERY_HEADS // KEY_VALUE_HEADS * HEAD_SIZE
    query_width = QUERY_HEADS * HEAD_SIZE
    kv_width = KEY_VALUE_HEADS * HEAD_SIZE
    scale = 1.0 / math.sqrt(HEAD_SIZE)
    all_tokens = token_rows * context_count * shard_count
    shard_rows = query_key_value_weight.shape[0]
    half_rows = shard_rows // 2
    local_experts = expert_weight.shape[0]
    bf16, f32 = jnp.bfloat16, jnp.float32
    states = hidden[0]
    clock = Clock()
    have = {}

    def meta():
        return clock(plain_meta)

    def now(*values):
        return clock(*values)

    def ready(*values):
        values = clock(*values)
        clock.mark(values[0] if isinstance(values, tuple) or isinstance(values, list) else values)
        return values


    def hidden_chain():
        have["blocks"] = chips_exchange(jnp.broadcast_to(states, (4,) + states.shape))
        yield

    def qkv_chain():
        rows = lax.dynamic_slice_in_dim(query_key_value_weight, core * half_rows, half_rows, 0)
        half = jnp.concatenate(
            [
                lax.dynamic_slice_in_dim(rows, chip * group_width, group_width, 1),
                lax.dynamic_slice_in_dim(rows, query_width + chip * HEAD_SIZE, HEAD_SIZE, 1),
                lax.dynamic_slice_in_dim(
                    rows, query_width + kv_width + chip * HEAD_SIZE, HEAD_SIZE, 1
                ),
            ],
            axis=1,
        )
        came = line_swap(half, 1)
        yield
        pair = clock.mark(jnp.stack([half, now(came)]))
        came = line_swap(pair, 2)
        yield
        have["qkv_mine"] = clock.mark(jnp.concatenate([pair, now(came)]))
        have["qkv_other"] = flip(have["qkv_mine"], 1)
        yield

    def small_chain():
        expert_ids = jnp.arange(EXPERTS, dtype=jnp.int32)
        matrix = jnp.sum(
            jnp.where(
                routes[0][None, :, :] == expert_ids[:, None, None], route_gates[0][None, :, :], 0.0
            ),
            axis=-1,
        )
        have["valid"] = valid_mask[0].astype(f32)
        gains = jnp.concatenate([gain_in, gain_mid]).astype(f32).reshape(-1, token_rows)
        gain_rows = gains.shape[0]
        filled = EXPERTS + gain_rows
        pack = jnp.concatenate(
            [
                matrix,
                gains,
                jnp.full((32 - filled, token_rows), jnp.sum(have["valid"]), f32),
            ]
        )
        came = line_swap(pack, 1)
        yield
        pair = clock.mark(jnp.stack([pack, now(came)]))
        came = line_swap(pair, 2)
        yield
        all_packs = clock.mark(jnp.concatenate([pair, now(came)]))
        have["gates"] = [
            lax.dynamic_slice_in_dim(
                all_packs[i], shard_index * local_experts, local_experts, 0
            )[..., None]
            for i in range(4)
        ]
        gains = all_packs[:, EXPERTS:filled].reshape(4, 2, shard_rows)
        gains = jnp.stack([pick(gains, shard_index ^ i) for i in range(4)], axis=1)
        have["gains"] = gains.reshape(2, 1, width)
        total = jnp.broadcast_to(jnp.sum(all_packs[:, filled, 0]), (8, 128))
        yield
        total = now(total)
        for bit in (1, 2, 4):
            came = flip(total, bit)
            yield
            total = clock.mark(total + now(came))
        have["count"] = total[0, 0]
        yield

    def shared_chain():
        eighth = shard_rows // 8
        units = SF // shard_count
        piece = lax.dynamic_slice_in_dim(shared_weight, context_index * eighth, eighth, 0)
        piece = piece.reshape(eighth, 3, shard_count, units)

        piece = jnp.transpose(piece, (2, 0, 1, 3)).reshape(shard_count, eighth, 3 * units)
        parts = [pick(piece, shard_index ^ i) for i in range(4)]
        came = line_swap(now(jnp.stack([parts[1], parts[3]])), 1)
        yield
        came = now(came)
        mine = jnp.stack([parts[0], came[0]])
        came = line_swap(clock.mark(jnp.stack([parts[2], came[1]])), 2)
        yield
        pieces = clock.mark(jnp.concatenate([mine, now(came)]))
        came = flip(pieces, 2)
        yield
        pair = clock.mark(jnp.stack([pieces, now(came)]))
        came = flip(pair, 4)
        yield
        mine = clock.mark(jnp.concatenate([pair, now(came)]))
        other = flip(mine, 1)
        yield
        have["shared"] = join_shared(meta(), mine, other)
        clock.mark(have["shared"])
        yield

    def out_chain():
        half = lax.dynamic_slice_in_dim(now(out_weight), core * half_rows, half_rows, 0)
        came = line_exchange(jnp.broadcast_to(half, (4,) + half.shape))
        yield
        have["out_mine"] = clock.mark(now(came))
        have["out_other"] = flip(have["out_mine"], 1)
        yield

    def qkv_all_chain():
        half = lax.dynamic_slice_in_dim(
            now(have["qkv_slice"]), core * (width // 2), width // 2, 0
        )
        came = flip(half, 2)
        yield
        pair = clock.mark(jnp.stack([half, now(came)]))
        came = flip(pair, 4)
        yield
        have["rel_mine"] = clock.mark(jnp.concatenate([pair, now(came)]))
        have["rel_other"] = flip(have["rel_mine"], 1)
        yield

    def main_chain():
        gains = have["gains"]
        normed_in, query, pair, qkv_slice = project(
            meta(), have["blocks"], gains[0], have["qkv_mine"], have["qkv_other"], group_width
        )
        clock.mark(pair)
        have["normed_in"], have["qkv_slice"] = normed_in, qkv_slice
        pair_other = flip(pair, 1)
        yield
        mixed_heads, log_total = attend(meta(), query, pair, pair_other, scale)
        clock.mark(log_total)
        have["attend"] = (query, pair, pair_other, log_total, mixed_heads)
        parts = ready(*[pick(mixed_heads, chip ^ r) for r in range(4)])
        mixed = [parts[0]] + [flip(parts[r], 2 * r) for r in (1, 2, 3)]
        have["mixed"] = mixed
        yield
        out_full, middle, normed_mid = leave(
            meta(), mixed, have["out_mine"], have["out_other"], states, gains[1]
        )
        have["out_full"], have["middle"] = out_full, middle
        clock.mark(normed_mid)

        near, center = line_swap(normed_mid, 1), line_middle(normed_mid)
        yield
        gates, shared_slice = have["gates"], have["shared"]
        gate_ups, shared_gate_ups, outs = [], [], []

        def forward(rows, i):
            result = experts(meta(), rows, gates[i], expert_weight, shared_slice)
            clock.mark(result[2])
            gate_ups.append(result[0])
            shared_gate_ups.append(result[1])
            outs.append(result[2])

        forward(normed_mid, 0)
        yield
        near, center = now(near, center)
        far, outward = line_middle(near), line_outward(center)
        forward(near, 1)
        yield
        far, outward = now(far, outward)
        outward_far = line_outward(far)
        third = clock.mark(jnp.where(at_end, outward, far))
        forward(third, 2)
        yield
        outward_far = now(outward_far)
        fourth = clock.mark(jnp.where(at_end, outward_far, center))
        forward(fourth, 3)
        line_rows = [normed_mid, near, third, fourth]
        came = line_inward(outs[3])
        yield
        carried = clock.mark(outs[2] + now(came))
        inward, crossed = line_inward(carried), line_middle(carried)
        yield
        inward, crossed = now(inward, crossed)
        near_out, middle_out = ready(outs[1] + crossed, outs[3] + inward)
        near_out, middle_out = line_swap(near_out, 1), line_middle(middle_out)
        yield
        near_out, middle_out = now(near_out, middle_out)
        final_state = (
            middle + outs[0].astype(f32) + near_out.astype(f32) + middle_out.astype(f32)
        )
        valid = have["valid"]
        deviation = final_state - teacher[0].astype(f32)
        have["squared"] = jnp.sum(valid[:, None] * deviation * deviation)
        grad_final = all_tokens / have["count"] * valid[:, None] * deviation
        have["final"], have["grad_final"] = final_state.astype(bf16)[None], grad_final
        grad_low = clock.mark(grad_final.astype(bf16))
        near, center = line_swap(grad_low, 1), line_middle(grad_low)
        yield
        kept = []

        def backward(grads, i):
            kept.append(
                experts_back(
                    meta(),
                    grads,
                    gates[i],
                    gate_ups[i],
                    shared_gate_ups[i],
                    expert_weight,
                    shared_slice,
                )
            )
            clock.mark(kept[-1][4])

        backward(grad_low, 0)
        yield
        near, center = now(near, center)
        far, outward = line_middle(near), line_outward(center)
        backward(near, 1)
        yield
        far, outward = now(far, outward)
        outward_far = line_outward(far)
        third = clock.mark(jnp.where(at_end, outward, far))
        backward(third, 2)
        yield
        outward_far = now(outward_far)
        fourth = clock.mark(jnp.where(at_end, outward_far, center))
        backward(fourth, 3)
        have["line"] = (line_rows, [grad_low, near, third, fourth])
        have["experts"] = list(zip(*kept))
        yield


    def states_chain():
        outs = have["experts"][4]
        came = line_inward(outs[3])
        yield
        carried = clock.mark(outs[2] + now(came))
        inward, crossed = line_inward(carried), line_middle(carried)
        yield
        inward, crossed = now(inward, crossed)
        near_out, middle_out = ready(outs[1] + crossed, outs[3] + inward)
        near_out, middle_out = line_swap(near_out, 1), line_middle(middle_out)
        yield
        near_out, middle_out = now(near_out, middle_out)
        grad_normed = clock.mark(
            outs[0].astype(f32) + near_out.astype(f32) + middle_out.astype(f32)
        )
        grad_middle, grad_branch, grad_gain_mid, grad_mixed = enter_back(
            meta(),
            have["grad_final"],
            grad_normed,
            have["middle"],
            have["gains"][1],
            have["out_full"],
        )
        clock.mark(grad_branch)
        have["grad_branch"], have["grad_gain_mid"] = grad_branch, grad_gain_mid
        grad_mixed = chips_exchange(ready(grad_mixed))
        yield
        query, pair, pair_other, log_total, mixed_heads = have["attend"]
        grad_query, grad_pair, grad_other = attend_back(
            meta(), query, pair, pair_other, log_total, mixed_heads, grad_mixed, scale
        )
        clock.mark(grad_query)
        came = flip(grad_other, 1)
        yield
        grad_pair = grad_pair + now(came).astype(f32)
        projected = clock.mark(jnp.concatenate([grad_query, grad_pair.astype(bf16)], axis=-1))
        have["grad_projected"] = projected
        parts = chips_exchange(ready(projected))
        yield
        grad_hidden, grad_gain_in = finish(
            meta(),
            parts,
            have["rel_mine"],
            have["rel_other"],
            states,
            grad_middle,
            have["gains"][0],
        )
        clock.mark(grad_gain_in)
        have["grad_hidden"] = grad_hidden
        sums = jnp.concatenate(
            [grad_gain_in, have["grad_gain_mid"], jnp.full((6, width), have["squared"], f32)],
            axis=0,
        )
        for offset in (1, 2):
            came = line_swap(sums, offset)
            yield
            sums = clock.mark(sums + now(came))
        for bit in (1, 2, 4):
            came = flip(sums, bit)
            yield
            sums = clock.mark(sums + now(came))
        own = lax.dynamic_slice_in_dim(sums, shard_index * shard_rows, shard_rows, 1)
        have["sums"] = (own, 0.5 * sums[2, 0] / (have["count"] * width))
        yield

    def expert_chain(index):
        line_rows, line_grads = have["line"]
        grad_gate_ups, acts, shared_grads, shared_acts = have["experts"][:4]
        shared = (shared_grads, shared_acts) if index == 0 else None

        def grad_of(at):
            return clock.mark(
                expert_grad(
                    meta(),
                    2 * at + index,
                    at,
                    line_rows,
                    line_grads,
                    grad_gate_ups,
                    acts,
                    shared,
                )
            )

        came = flip(grad_of(1 - core), 1)
        yield
        keep = grad_of(core)
        yield
        x_first = index % 2 == 0
        first, second = (2, 4) if x_first else (4, 2)
        picked = ((1, 3), (0, 2)) if x_first else ((2, 3), (0, 1))
        pieces = keep.shape[1] // 96

        def split_sum(keep, came):
            return [
                jnp.stack([keep[i] + came[i] for i in places]) for places in picked
            ]

        give, keep = blend(meta(), "blend_split", split_sum, [keep, came], pieces)
        clock.mark(give)
        came = flip(give, first)
        yield
        give, keep = blend(
            meta(), "blend_pair", lambda k, c: [k[1] + c[1], k[0] + c[0]], [keep, came], pieces
        )
        clock.mark(give)
        came = flip(give, second)
        yield
        own = clock.mark(blend(meta(), "blend_sum", lambda k, c: k + c, [keep, came], pieces))
        came = flip(own, second)
        yield
        pair = clock.mark(
            blend(meta(), "blend_stack", lambda a, b: jnp.stack([a, b]), [own, came], pieces)
        )
        came = flip(pair, first)
        yield

        def stack_four(near, far):
            if x_first:
                return jnp.stack([near[0], far[0], near[1], far[1]])
            return jnp.stack([near[0], near[1], far[0], far[1]])

        stacked = clock.mark(blend(meta(), "blend_four", stack_four, [pair, came], pieces))
        other = flip(stacked, 1)
        if index == 0:
            have["shared_sum"] = stacked[:, shard_rows:]
        yield
        have["grad_experts"] = place_pair(
            meta(), have.get("grad_experts"), index, expert_weight.shape, stacked, other
        )
        clock.mark(have["grad_experts"])
        yield

    def shared_grad_chain():
        total = now(have["shared_sum"])
        parts = ready(*[pick(total, chip ^ shard_index ^ i) for i in range(4)])
        came = [line_swap(parts[i], i) for i in (1, 2, 3)]
        yield
        mine = clock.mark(jnp.stack([parts[0]] + list(now(*came))))
        other = flip(mine, 1)
        yield
        have["grad_shared"] = clock.mark(place_shared(meta(), mine, other))
        yield

    def line_reduce_steps(keep, came):
        came = now(came)
        parts = [keep[i] + came[i] for i in range(4)]
        came = line_inward(clock.mark(parts[3]))
        yield
        carried = clock.mark(parts[2] + now(came))
        inward, crossed = line_inward(carried), line_middle(carried)
        yield
        inward, crossed = now(inward, crossed)
        near_out, middle_out = ready(parts[1] + crossed, parts[3] + inward)
        near_out, middle_out = line_swap(near_out, 1), line_middle(middle_out)
        yield
        near_out, middle_out = now(near_out, middle_out)
        have["line_sum"] = clock.mark(
            (parts[0].astype(f32) + near_out.astype(f32) + middle_out.astype(f32)).astype(bf16)
        )

    def out_grad_chain():
        mixed = jnp.concatenate(have["mixed"], axis=1)
        keep, give = weight_grad(
            meta(), chip ^ shard_index, [([mixed], [have["grad_branch"][None]])], 0
        )
        clock.mark(keep)
        came = flip(give, 1)
        yield
        yield from line_reduce_steps(keep, came)
        total = have["line_sum"]
        yield
        total = ready(total)
        came = flip(total, 2)
        yield
        total = clock.mark(total + now(came))
        came = flip(total, 4)
        yield
        mine = clock.mark(total + now(came))
        other = flip(mine, 1)
        yield
        mine, other = now(mine, other)
        have["grad_out"] = clock.mark(
            jnp.where(
                core == 0,
                jnp.concatenate([mine, other], axis=0),
                jnp.concatenate([other, mine], axis=0),
            ).astype(f32)
        )
        yield

    def qkv_grad_chain():
        normed_in = have["normed_in"].reshape(4 * token_rows, width)
        projected = have["grad_projected"].reshape(1, 4 * token_rows, -1)
        keep, give = weight_grad(meta(), shard_index, [([normed_in], [projected])], 0)
        clock.mark(keep)
        came = flip(give, 1)
        yield
        yield from line_reduce_steps(keep, came)
        own = have["line_sum"]
        yield
        own = ready(own)
        came = flip(own, 2)
        yield
        pair = clock.mark(jnp.stack([own, now(came)]))
        came = flip(pair, 4)
        yield
        mine = clock.mark(jnp.concatenate([pair, now(came)]))
        other = flip(mine, 1)
        yield
        have["grad_qkv"] = clock.mark(place_heads(meta(), [mine[r] for r in range(4)], other))
        yield

    early = {
        "H": hidden_chain(),
        "W": qkv_chain(),
        "S": shared_chain(),
        "O": out_chain(),
        "K": small_chain(),
        "R": qkv_all_chain(),
        "M": main_chain(),
    }
    late = {
        "L": states_chain(),
        "S": shared_grad_chain(),
        "O": out_grad_chain(),
        "Q": qkv_grad_chain(),
    }
    for index in range(local_experts // 2):
        late[str(index)] = expert_chain(index)
    for chains, order in ((early, EARLY), (late, LATE)):
        for name in order:
            next(chains[name], None)
        for name in chains:
            for _ in chains[name]:
                pass

    own, loss_value = have["sums"]
    return (
        have["final"],
        loss_value,
        have["grad_hidden"],
        own[0],
        have["grad_qkv"],
        have["grad_out"],
        own[1],
        have["grad_shared"],
        have["grad_experts"],
    )


def solution(mesh):
    in_specs = (
        P("wt", "ctx", None),
        P("wt", "ctx", None),
        P("wt", "ctx"),
        P("wt", "ctx", None),
        P("wt", "ctx", None),
        P("wt"),
        P("wt", None),
        P("wt", None),
        P("wt"),
        P("wt", None),
        P("wt", None, None),
    )
    out_specs = (
        P("wt", "ctx", None),
        P(),
        P("wt", "ctx", None),
        P("wt"),
        P("wt", None),
        P("wt", None),
        P("wt"),
        P("wt", None),
        P("wt", None, None),
    )
    plane_of_eight = dict(mesh.shape) == {"ctx": 8, "wt": 4}
    return jax.shard_map(
        fast_device if plane_of_eight else on_device, mesh=mesh, in_specs=in_specs, out_specs=out_specs, check_vma=False
    )
```

```python
import functools
import math

import jax
import jax.numpy as jnp
from jax import lax
from jax.experimental import pallas as pl
from jax.experimental.pallas import tpu as pltpu
from jax.sharding import PartitionSpec as P

QUERY_HEADS = 12
KEY_VALUE_HEADS = 4
HEAD_SIZE = 128
F = 512
SF = 1024
EXPERTS = 16
TOP = 6


norm_eps = 1e-05
masked_score = -1e30


def sigmoid_linear(values):
    return values * jax.nn.sigmoid(values)


def silu_slope(values):
    sigma_value = jax.nn.sigmoid(values)
    return sigma_value * (1.0 + values * (1.0 - sigma_value))


def normalize(values):
    inverse = lax.rsqrt(jnp.mean(values * values, axis=-1, keepdims=True) + norm_eps)
    return (values * inverse, inverse)


def norm_back(grad_normed, scaled, inverse, gain_vector):
    grad_scaled = grad_normed * gain_vector
    return inverse * (grad_scaled - scaled * jnp.mean(grad_scaled * scaled, axis=-1, keepdims=True))


def positions(row_ids, token_rows, context_count):
    piece_index = row_ids // token_rows
    within = row_ids % token_rows
    half_rows = token_rows // 2
    mirrored = jnp.where(within < half_rows, piece_index, 2 * context_count - 1 - piece_index)
    return mirrored * half_rows + within % half_rows


def route_tables(local_routes, local_gates, experts, capacity):
    token_rows = local_routes.shape[0]
    flat_routes = local_routes.reshape(-1)
    one_hot = (flat_routes[:, None] == jnp.arange(experts, dtype=jnp.int32)[None, :]).astype(
        jnp.int32
    )
    earlier = jnp.cumsum(one_hot, axis=0) - one_hot
    slot_index = jnp.sum(earlier * one_hot, axis=1)
    token_index = jnp.arange(flat_routes.shape[0], dtype=jnp.int32) // local_routes.shape[1]
    slot_table = (
        jnp.full((experts, capacity), token_rows, jnp.int32)
        .at[flat_routes, slot_index]
        .set(token_index)
    )
    slot_gate = (
        jnp.zeros((experts, capacity), jnp.float32)
        .at[flat_routes, slot_index]
        .set(local_gates.reshape(-1))
    )
    return (slot_table, slot_gate)


def block_scores(query_rows, key_block, key_position, query_place, score_scale):
    scores = (
        jnp.einsum("qhgd,khd->qhgk", query_rows, key_block, preferred_element_type=jnp.float32)
        * score_scale
    )
    allowed = key_position[None, None, None, :] <= query_place[:, None, None, None]
    return jnp.where(allowed, scores, masked_score)


def attend_forward(
    query_rows, blocked_keys, blocked_values, place_blocks, query_place, score_scale
):
    head_shape = query_rows.shape[:3]

    def online_step(running, block_args):
        running_max, running_sum, accumulated = running
        key_block, value_block, key_position = block_args
        scores = block_scores(query_rows, key_block, key_position, query_place, score_scale)
        new_max = jnp.maximum(running_max, jnp.max(scores, axis=-1))
        rescale = jnp.exp(running_max - new_max)
        powers = jnp.exp(scores - new_max[..., None])
        new_sum = running_sum * rescale + jnp.sum(powers, axis=-1)
        weighted = jnp.einsum(
            "qhgk,khd->qhgd",
            powers.astype(jnp.bfloat16),
            value_block,
            preferred_element_type=jnp.float32,
        )
        return ((new_max, new_sum, accumulated * rescale[..., None] + weighted), None)

    initial = (
        jnp.full(head_shape, masked_score, jnp.float32),
        jnp.zeros(head_shape, jnp.float32),
        jnp.zeros(query_rows.shape, jnp.float32),
    )
    row_max, row_sum, accumulated = lax.scan(
        online_step, initial, (blocked_keys, blocked_values, place_blocks)
    )[0]
    log_total = row_max + jnp.log(row_sum)
    return (accumulated / row_sum[..., None], log_total)


def attend_backward(
    query_rows,
    blocked_keys,
    blocked_values,
    place_blocks,
    query_place,
    log_total,
    attention_output_gradient,
    attention_output,
    score_scale,
):
    row_delta = jnp.sum(attention_output_gradient.astype(jnp.float32) * attention_output, axis=-1)

    def block_grads(grad_queries, block_args):
        key_block, value_block, key_position = block_args
        scores = block_scores(query_rows, key_block, key_position, query_place, score_scale)
        probabilities = jnp.exp(scores - log_total[..., None])
        grad_probs = jnp.einsum(
            "qhgd,khd->qhgk",
            attention_output_gradient,
            value_block,
            preferred_element_type=jnp.float32,
        )
        grad_scores = (probabilities * (grad_probs - row_delta[..., None])).astype(jnp.bfloat16)
        grad_queries = grad_queries + jnp.einsum(
            "qhgk,khd->qhgd", grad_scores, key_block, preferred_element_type=jnp.float32
        )
        grad_keys = (
            jnp.einsum(
                "qhgk,qhgd->khd", grad_scores, query_rows, preferred_element_type=jnp.float32
            )
            * score_scale
        )
        grad_values = jnp.einsum(
            "qhgk,qhgd->khd",
            probabilities.astype(jnp.bfloat16),
            attention_output_gradient,
            preferred_element_type=jnp.float32,
        )
        return (grad_queries, (grad_keys, grad_values))

    grad_queries, (grad_keys, grad_values) = lax.scan(
        block_grads,
        jnp.zeros(query_rows.shape, jnp.float32),
        (blocked_keys, blocked_values, place_blocks),
    )
    return (grad_queries * score_scale, grad_keys, grad_values)


def gate_up_grads(grad_act, gate_up, hidden_units):
    gate_part = gate_up[..., :hidden_units]
    up_part = gate_up[..., hidden_units:]
    return jnp.concatenate(
        [grad_act * up_part * silu_slope(gate_part), grad_act * sigmoid_linear(gate_part)], axis=-1
    ).astype(jnp.bfloat16)


def on_device(
    hidden,
    teacher,
    valid_mask,
    routes,
    route_gates,
    gain_in,
    query_key_value_weight,
    out_weight,
    gain_mid,
    shared_weight,
    expert_weight,
):
    token_rows = hidden.shape[1]
    model_width = hidden.shape[2]
    context_count = lax.axis_size("ctx")
    shard_count = lax.axis_size("wt")
    seq_rows = token_rows * context_count
    all_tokens = seq_rows * shard_count
    query_groups = QUERY_HEADS // KEY_VALUE_HEADS
    query_total_width = QUERY_HEADS * HEAD_SIZE
    key_value_width = KEY_VALUE_HEADS * HEAD_SIZE
    score_scale = 1.0 / math.sqrt(HEAD_SIZE)
    key_row_count = min(512, seq_rows)
    number_of_blocks = seq_rows // key_row_count
    capacity = token_rows * TOP // 12
    local_experts = expert_weight.shape[0]
    contract_last = (((1,), (1,)), ((), ()))
    contract_first = (((0,), (0,)), ((), ()))
    full_gain_in, full_qkv, full_out, full_gain_mid, full_shared = (
        lax.all_gather(gain_in, "wt", axis=0, tiled=True),
        lax.all_gather(query_key_value_weight, "wt", axis=0, tiled=True),
        lax.all_gather(out_weight, "wt", axis=0, tiled=True),
        lax.all_gather(gain_mid, "wt", axis=0, tiled=True),
        lax.all_gather(shared_weight, "wt", axis=0, tiled=True),
    )
    gain_in_float = full_gain_in.astype(jnp.float32)
    gain_mid_float = full_gain_mid.astype(jnp.float32)
    inputs = hidden[0].astype(jnp.float32)
    scaled_in, inverse_in = normalize(inputs)
    normed_in = (scaled_in * gain_in_float).astype(jnp.bfloat16)
    projected_rows = jnp.dot(normed_in, full_qkv, preferred_element_type=jnp.float32).astype(
        jnp.bfloat16
    )
    query_rows = projected_rows[:, :query_total_width].reshape(
        token_rows, KEY_VALUE_HEADS, query_groups, HEAD_SIZE
    )
    context_local = projected_rows[:, query_total_width:]
    context_gathered = lax.all_gather(context_local, "ctx", axis=0, tiled=True)
    context_index = lax.axis_index("ctx")
    query_place = positions(
        context_index * token_rows + jnp.arange(token_rows, dtype=jnp.int32),
        token_rows,
        context_count,
    )
    place_blocks = positions(
        jnp.arange(seq_rows, dtype=jnp.int32), token_rows, context_count
    ).reshape(number_of_blocks, key_row_count)
    blocked_keys = context_gathered[:, :key_value_width].reshape(
        number_of_blocks, key_row_count, KEY_VALUE_HEADS, HEAD_SIZE
    )
    blocked_values = context_gathered[:, key_value_width:].reshape(
        number_of_blocks, key_row_count, KEY_VALUE_HEADS, HEAD_SIZE
    )
    attention_output, log_total = attend_forward(
        query_rows, blocked_keys, blocked_values, place_blocks, query_place, score_scale
    )
    mixed_rows = attention_output.reshape(token_rows, query_total_width).astype(jnp.bfloat16)
    middle = inputs + jnp.dot(mixed_rows, full_out, preferred_element_type=jnp.float32)
    scaled_mid, inverse_mid = normalize(middle)
    normed_mid = (scaled_mid * gain_mid_float).astype(jnp.bfloat16)
    shared_gate_up = jnp.dot(
        normed_mid, full_shared[:, : 2 * SF], preferred_element_type=jnp.float32
    )
    shared_act = (sigmoid_linear(shared_gate_up[:, :SF]) * shared_gate_up[:, SF:]).astype(
        jnp.bfloat16
    )
    shared_out = lax.dot_general(
        shared_act, full_shared[:, 2 * SF :], contract_last, preferred_element_type=jnp.float32
    )
    slot_table, slot_gate = route_tables(routes[0], route_gates[0], EXPERTS, capacity)
    padded_rows = jnp.concatenate([normed_mid, jnp.zeros((1, model_width), jnp.bfloat16)], axis=0)
    expert_rows = jnp.take(padded_rows, slot_table, axis=0)
    arrived = lax.all_to_all(expert_rows, "wt", split_axis=0, concat_axis=0, tiled=True)
    slot_count = arrived.shape[1]
    grouped = arrived.reshape(shard_count, local_experts, slot_count, model_width)
    owner_gate_up = jnp.einsum(
        "wesd,edf->wesf", grouped, expert_weight[:, :, : 2 * F], preferred_element_type=jnp.float32
    )
    owner_act = (sigmoid_linear(owner_gate_up[..., :F]) * owner_gate_up[..., F:]).astype(
        jnp.bfloat16
    )
    owner_out = jnp.einsum(
        "wesf,edf->wesd",
        owner_act,
        expert_weight[:, :, 2 * F :],
        preferred_element_type=jnp.float32,
    ).astype(jnp.bfloat16)
    returned = lax.all_to_all(
        owner_out.reshape(shard_count * local_experts, slot_count, model_width),
        "wt",
        split_axis=0,
        concat_axis=0,
        tiled=True,
    )
    expert_out, owner_rows, owner_gate_up, owner_act = (
        returned,
        arrived,
        owner_gate_up.reshape(shard_count * local_experts, slot_count, 2 * F),
        owner_act.reshape(shard_count * local_experts, slot_count, F),
    )
    routed = (
        jnp.zeros((token_rows + 1, model_width), jnp.float32)
        .at[slot_table]
        .add(expert_out.astype(jnp.float32) * slot_gate[..., None])[:token_rows]
    )
    final_state = middle + shared_out + routed
    valid_float = valid_mask[0].astype(jnp.float32)
    deviation = final_state - teacher[0].astype(jnp.float32)
    squared_local = jnp.sum(valid_float[:, None] * deviation * deviation)
    count_local = jnp.sum(valid_float)
    squared_total, valid_count = lax.psum((squared_local, count_local), ("ctx", "wt"))
    loss_value = 0.5 * squared_total / (valid_count * model_width)
    grad_final = all_tokens / valid_count * valid_float[:, None] * deviation
    grad_shared_out = grad_final.astype(jnp.bfloat16)
    grad_shared_act = jnp.dot(
        grad_shared_out, full_shared[:, 2 * SF :], preferred_element_type=jnp.float32
    )
    grad_shared_down = lax.dot_general(
        grad_shared_out, shared_act, contract_first, preferred_element_type=jnp.float32
    )
    grad_shared_gate_up = gate_up_grads(grad_shared_act, shared_gate_up, SF)
    grad_normed_mid = lax.dot_general(
        grad_shared_gate_up,
        full_shared[:, : 2 * SF],
        contract_last,
        preferred_element_type=jnp.float32,
    )
    grad_shared_front = lax.dot_general(
        normed_mid, grad_shared_gate_up, contract_first, preferred_element_type=jnp.float32
    )
    grad_shared_full = jnp.concatenate([grad_shared_front, grad_shared_down], axis=1)
    padded_grads = jnp.concatenate([grad_final, jnp.zeros((1, model_width), jnp.float32)], axis=0)
    grad_expert_out = (jnp.take(padded_grads, slot_table, axis=0) * slot_gate[..., None]).astype(
        jnp.bfloat16
    )
    grad_arrived = lax.all_to_all(grad_expert_out, "wt", split_axis=0, concat_axis=0, tiled=True)
    grad_grouped = grad_arrived.reshape(shard_count, local_experts, capacity, model_width)
    owner_gate_up_grouped = owner_gate_up.reshape(shard_count, local_experts, capacity, 2 * F)
    owner_act_grouped = owner_act.reshape(shard_count, local_experts, capacity, F)
    owner_rows_grouped = owner_rows.reshape(shard_count, local_experts, capacity, model_width)
    grad_owner_act = jnp.einsum(
        "wecd,edf->wecf",
        grad_grouped,
        expert_weight[:, :, 2 * F :],
        preferred_element_type=jnp.float32,
    )
    grad_owner_gate_up = gate_up_grads(grad_owner_act, owner_gate_up_grouped, F)
    grad_owner_rows = jnp.einsum(
        "wecf,edf->wecd",
        grad_owner_gate_up,
        expert_weight[:, :, : 2 * F],
        preferred_element_type=jnp.float32,
    ).astype(jnp.bfloat16)
    front = jnp.einsum(
        "wecd,wecf->edf", owner_rows_grouped, grad_owner_gate_up, preferred_element_type=jnp.float32
    )
    back = jnp.einsum(
        "wecd,wecf->edf", grad_grouped, owner_act_grouped, preferred_element_type=jnp.float32
    )
    expert_grad = jnp.concatenate([front, back], axis=2)
    grad_rows = lax.all_to_all(
        grad_owner_rows.reshape(shard_count * local_experts, capacity, model_width),
        "wt",
        split_axis=0,
        concat_axis=0,
        tiled=True,
    )
    grad_normed_mid = (
        grad_normed_mid
        + jnp.zeros((token_rows + 1, model_width), jnp.float32)
        .at[slot_table]
        .add(grad_rows.astype(jnp.float32))[:token_rows]
    )
    grad_gain_mid_local = jnp.sum(grad_normed_mid * scaled_mid, axis=0)
    grad_middle = grad_final + norm_back(grad_normed_mid, scaled_mid, inverse_mid, gain_mid_float)
    grad_branch = grad_middle.astype(jnp.bfloat16)
    mixed_gradient = lax.dot_general(
        grad_branch, full_out, contract_last, preferred_element_type=jnp.float32
    ).astype(jnp.bfloat16)
    grad_out_local = lax.dot_general(
        mixed_rows, grad_branch, contract_first, preferred_element_type=jnp.float32
    )
    context_recomputed = lax.all_gather(context_local, "ctx", axis=0, tiled=True)
    backward_keys = context_recomputed[:, :key_value_width].reshape(
        number_of_blocks, key_row_count, KEY_VALUE_HEADS, HEAD_SIZE
    )
    backward_values = context_recomputed[:, key_value_width:].reshape(
        number_of_blocks, key_row_count, KEY_VALUE_HEADS, HEAD_SIZE
    )
    attention_output_gradient = mixed_gradient.reshape(
        token_rows, KEY_VALUE_HEADS, query_groups, HEAD_SIZE
    )
    grad_queries, grad_keys, grad_values = attend_backward(
        query_rows,
        backward_keys,
        backward_values,
        place_blocks,
        query_place,
        log_total,
        attention_output_gradient,
        attention_output,
        score_scale,
    )
    grad_context_all = jnp.concatenate(
        [
            grad_keys.reshape(seq_rows, key_value_width),
            grad_values.reshape(seq_rows, key_value_width),
        ],
        axis=1,
    )
    grad_context = lax.psum_scatter(
        grad_context_all.astype(jnp.bfloat16), "ctx", scatter_dimension=0, tiled=True
    ).astype(jnp.float32)
    grad_projected = jnp.concatenate(
        [grad_queries.reshape(token_rows, query_total_width), grad_context], axis=1
    ).astype(jnp.bfloat16)
    grad_normed_in = lax.dot_general(
        grad_projected, full_qkv, contract_last, preferred_element_type=jnp.float32
    )
    grad_qkv_local = lax.dot_general(
        normed_in, grad_projected, contract_first, preferred_element_type=jnp.float32
    )
    grad_gain_in_local = jnp.sum(grad_normed_in * scaled_in, axis=0)
    grad_inputs = grad_middle + norm_back(grad_normed_in, scaled_in, inverse_in, gain_in_float)
    weight_sums = (
        lax.psum_scatter(
            grad_gain_in_local.astype(jnp.bfloat16), "wt", scatter_dimension=0, tiled=True
        ).astype(jnp.float32),
        lax.psum_scatter(
            grad_qkv_local.astype(jnp.bfloat16), "wt", scatter_dimension=0, tiled=True
        ).astype(jnp.float32),
        lax.psum_scatter(
            grad_out_local.astype(jnp.bfloat16), "wt", scatter_dimension=0, tiled=True
        ).astype(jnp.float32),
        lax.psum_scatter(
            grad_gain_mid_local.astype(jnp.bfloat16), "wt", scatter_dimension=0, tiled=True
        ).astype(jnp.float32),
        lax.psum_scatter(
            grad_shared_full.astype(jnp.bfloat16), "wt", scatter_dimension=0, tiled=True
        ).astype(jnp.float32),
    )
    summed = (
        lax.psum(weight_sums[0].astype(jnp.bfloat16), "ctx").astype(jnp.float32),
        lax.psum(weight_sums[1].astype(jnp.bfloat16), "ctx").astype(jnp.float32),
        lax.psum(weight_sums[2].astype(jnp.bfloat16), "ctx").astype(jnp.float32),
        lax.psum(weight_sums[3].astype(jnp.bfloat16), "ctx").astype(jnp.float32),
        lax.psum(weight_sums[4].astype(jnp.bfloat16), "ctx").astype(jnp.float32),
        lax.psum(expert_grad.astype(jnp.bfloat16), "ctx").astype(jnp.float32),
    )
    return (
        final_state.astype(jnp.bfloat16)[None],
        loss_value,
        grad_inputs[None],
        summed[0],
        summed[1],
        summed[2],
        summed[3],
        summed[4],
        summed[5],
    )


PLANE = [[0, 2, 4, 6], [1, 3, 5, 7]]
COSTS = {
    "project": 0.3,
    "attend": 0.3,
    "leave": 0.3,
    "join_shared": 0.3,
    "experts": 0.3,
    "experts_back": 0.3,
    "enter_back": 0.3,
    "attend_back": 0.3,
    "finish": 0.3,
    "weight_grad": 0.3,
    "expert_grad": 0.3,
    "blend_split": 0.3,
    "blend_pair": 0.3,
    "blend_sum": 0.3,
    "blend_stack": 0.3,
    "blend_four": 0.3,
    "place_pair": 0.3,
    "place_shared": 0.3,
    "place_heads": 0.3,
}


def flip(value, bit):
    return lax.ppermute(value, "ctx", [(index, index ^ bit) for index in range(8)])


def line_swap(value, offset):
    return lax.ppermute(value, "wt", [(index, index ^ offset) for index in range(4)])


def line_middle(value):
    return lax.ppermute(value, "wt", [(1, 2), (2, 1)])


def line_outward(value):
    return lax.ppermute(value, "wt", [(1, 0), (2, 3)])


def line_inward(value):
    return lax.ppermute(value, "wt", [(0, 1), (3, 2)])


def line_gather(value, at_end):
    near = line_swap(value, 1)
    middle = line_middle(value)
    middle_far = line_middle(near)
    outward = line_outward(middle)
    outward_far = line_outward(middle_far)
    return [
        value,
        near,
        jnp.where(at_end, outward, middle_far),
        jnp.where(at_end, outward_far, middle),
    ]


def line_reduce(parts):
    far = line_inward(parts[3])
    carried = parts[2] + far
    inward = line_inward(carried)
    crossed = line_middle(carried)
    near = line_swap(parts[1] + crossed, 1)
    middle = line_middle(parts[3] + inward)
    return (
        parts[0].astype(jnp.float32) + near.astype(jnp.float32) + middle.astype(jnp.float32)
    )


def chips_exchange(blocks):
    return lax.all_to_all(
        blocks,
        "ctx",
        split_axis=0,
        concat_axis=0,
        tiled=True,
        axis_index_groups=PLANE,
    )


def line_exchange(blocks):
    return lax.all_to_all(blocks, "wt", split_axis=0, concat_axis=0, tiled=True)


def chips_gather(value, x_last):
    along_x = flip(value, 2)
    along_y = flip(value, 4)
    corner = flip(along_y, 2) if x_last else flip(along_x, 4)
    return [value, along_x, along_y, corner]


def core_swap(values):
    return [flip(value, 1) for value in values]


def everywhere_sum(value):
    for bit in (1, 2, 4):
        value = value + flip(value, bit)
    for offset in (1, 2):
        value = value + line_swap(value, offset)
    return value


def pick(blocks, index):
    return lax.dynamic_index_in_dim(blocks, index, 0, keepdims=False)


def chips_reduce(keep, came):
    half = keep.shape[1] // 2
    upper = keep[:, :half] + came[:, :half]
    lower = keep[:, half:] + came[:, half:]
    upper_came = flip(upper[1::2], 2)
    lower_came = flip(lower[2:], 4)
    upper = upper[0::2] + upper_came
    lower = lower[:2] + lower_came
    upper_came = flip(upper[1], 4)
    lower_came = flip(lower[1], 2)
    return jnp.concatenate([upper[0] + upper_came, lower[0] + lower_came], axis=0)


def dot_plain(left, right):
    return lax.dot_general(
        left, right, (((1,), (0,)), ((), ())), preferred_element_type=jnp.float32
    )


def dot_last(left, right):
    return lax.dot_general(
        left, right, (((1,), (1,)), ((), ())), preferred_element_type=jnp.float32
    )


def dot_first(left, right):
    return lax.dot_general(
        left, right, (((0,), (0,)), ((), ())), preferred_element_type=jnp.float32
    )


def call(kernel, name, meta, arrays, grid, in_specs, out_specs, out_shape, scratch, flops, moved):
    return pl.pallas_call(
        kernel,
        grid_spec=pltpu.PrefetchScalarGridSpec(
            num_scalar_prefetch=1,
            grid=grid,
            in_specs=in_specs,
            out_specs=out_specs,
            scratch_shapes=scratch,
        ),
        out_shape=out_shape,
        compiler_params=pltpu.CompilerParams(vmem_limit_bytes=48 * 1024 * 1024),
        cost_estimate=pl.CostEstimate(
            flops=int(COSTS.get(name, 1.0) * 1e9), bytes_accessed=1000, transcendentals=0
        ),
        name=name,
    )(meta, *arrays)


def whole(array):
    rank = len(array.shape)
    return pl.BlockSpec(tuple(array.shape), lambda *_: (0,) * rank)


def shape_of(shape, dtype):
    return jax.ShapeDtypeStruct(shape, dtype)


def size_of(arrays):
    return sum(math.prod(a.shape) * a.dtype.itemsize for a in arrays)


def blend(meta, name, function, arrays, pieces=4):
    rows = arrays[0].shape[-2]
    tile = rows // pieces
    outs = jax.eval_shape(function, *[shape_of(a.shape, a.dtype) for a in arrays])
    many = isinstance(outs, (list, tuple))
    outs = list(outs) if many else [outs]

    def spec(a):
        rank = len(a.shape)
        lead = a.shape[:-2]
        return pl.BlockSpec(
            tuple(lead) + (tile, a.shape[-1]),
            lambda i, m: (0,) * (rank - 2) + (i, 0),
        )

    def kernel(meta_ref, *refs):
        result = function(*[ref[...] for ref in refs[: len(arrays)]])
        result = list(result) if many else [result]
        for ref, value in zip(refs[len(arrays) :], result):
            ref[...] = value

    result = call(
        kernel,
        name,
        meta,
        arrays,
        (pieces,),
        [spec(a) for a in arrays],
        [spec(a) for a in outs],
        outs,
        [],
        0,
        0,
    )
    return result if many else result[0]


def aligned(value, step):
    return pl.multiple_of(value * step, step)


def project_kernel(meta, blocks_ref, gain_ref, mine, other, *refs):
    normed_ref, query_ref, pair_ref, weight_ref = refs
    core = meta[0] & 1
    rows = mine.shape[1]

    @pl.when(pl.program_id(0) == 0)
    def _():
        for i in range(4):
            at = 2 * (meta[1] ^ i)
            weight_ref[pl.ds(aligned(at + core, rows), rows), :] = mine[i]
            weight_ref[pl.ds(aligned(at + 1 - core, rows), rows), :] = other[i]

    states = blocks_ref[0].astype(jnp.float32)
    inverse = lax.rsqrt(jnp.mean(states * states, axis=-1, keepdims=True) + norm_eps)
    normed = (states * inverse * gain_ref[...]).astype(jnp.bfloat16)
    normed_ref[0] = normed
    projected = dot_plain(normed, weight_ref[...]).astype(jnp.bfloat16)
    query_width = query_ref.shape[-1]
    query_ref[0] = projected[:, :query_width]
    pair_ref[0] = projected[:, query_width:]


def project(meta, blocks, gain, mine, other, query_width):
    _, token_rows, width = blocks.shape
    columns = mine.shape[2]
    arrays = [blocks, gain, mine, other]
    outs = [
        shape_of((4, token_rows, width), jnp.bfloat16),
        shape_of((4, token_rows, query_width), jnp.bfloat16),
        shape_of((4, token_rows, columns - query_width), jnp.bfloat16),
        shape_of((width, columns), jnp.bfloat16),
    ]
    return call(
        project_kernel,
        "project",
        meta,
        arrays,
        (4,),
        [pl.BlockSpec((1, token_rows, width), lambda r, m: (r, 0, 0))]
        + [whole(a) for a in arrays[1:]],
        [
            pl.BlockSpec((1, token_rows, width), lambda r, m: (r, 0, 0)),
            pl.BlockSpec((1, token_rows, query_width), lambda r, m: (r, 0, 0)),
            pl.BlockSpec((1, token_rows, columns - query_width), lambda r, m: (r, 0, 0)),
            whole(outs[3]),
        ],
        outs,
        [],
        2 * 4 * token_rows * width * columns,
        size_of(arrays) + size_of(outs),
    )


def sort_pairs(meta, mine_ref, other_ref, keys, values):
    half = mine_ref.shape[1] // 2
    for slot in range(16):
        block, part = (slot, 0) if slot < 8 else (15 - slot, 1)
        place = block >> 1
        rows = pl.ds(part * half, half)
        to = pl.ds(slot * half, half)

        @pl.when((meta[0] & 1) == (block & 1))
        def _():
            keys[to, :] = mine_ref[place, rows, :HEAD_SIZE]
            values[to, :] = mine_ref[place, rows, HEAD_SIZE:]

        @pl.when((meta[0] & 1) != (block & 1))
        def _():
            keys[to, :] = other_ref[place, rows, :HEAD_SIZE]
            values[to, :] = other_ref[place, rows, HEAD_SIZE:]


def stack_heads(rows):
    count = rows.shape[1] // HEAD_SIZE
    return jnp.concatenate(
        [rows[:, h * HEAD_SIZE : (h + 1) * HEAD_SIZE] for h in range(count)], axis=0
    )


def unstack_heads(rows, count):
    each = rows.shape[0] // count
    return jnp.concatenate([rows[h * each : (h + 1) * each] for h in range(count)], axis=1)


def step_slot(meta):
    step = pl.program_id(0)
    block = 2 * (step >> 1) + (meta[0] & 1)
    return jnp.where((step & 1) == 0, block, 15 - block)


def allowed_pairs(start, slot, shape, half):
    key_place = start + lax.broadcasted_iota(jnp.int32, shape, 0)
    query_place = slot * half + (lax.broadcasted_iota(jnp.int32, shape, 1) & (half - 1))
    return key_place <= query_place


def key_spans(step, half, span):
    pairs = (step // 2 if step % 2 == 0 else 7 - step // 2) + 1
    rows = pairs * 2 * half
    return [(at, min(span, rows - at)) for at in range(0, rows, span)]


def attend_kernel(scale, span, meta, query_ref, mine_ref, other_ref, *refs):
    out_ref, log_ref, keys, values, values_turned = refs
    half, group_width = query_ref.shape[1:]
    count = group_width // HEAD_SIZE

    @pl.when(pl.program_id(0) == 0)
    def _():
        sort_pairs(meta, mine_ref, other_ref, keys, values)
        values_turned[...] = values[...].T

    slot = step_slot(meta)
    query = stack_heads(query_ref[0])
    wide = count * half

    def run(spans):
        highest = jnp.full((1, wide), masked_score, jnp.float32)
        total = jnp.zeros((1, wide), jnp.float32)
        mixed = jnp.zeros((HEAD_SIZE, wide), jnp.float32)
        for start, size in spans:
            at = pl.ds(start, size)
            scores = dot_last(keys[at, :], query) * scale
            if start == spans[-1][0]:
                seen = allowed_pairs(start, slot, scores.shape, half)
                scores = jnp.where(seen, scores, masked_score)
            new = jnp.maximum(highest, jnp.max(scores, axis=0, keepdims=True))
            rescale = jnp.exp(highest - new)
            powers = jnp.exp(scores - new)
            total = total * rescale + jnp.sum(powers, axis=0, keepdims=True)
            mixed = mixed * rescale + dot_plain(
                values_turned[:, at], powers.astype(jnp.bfloat16)
            )
            highest = new
        log_ref[0] = highest + jnp.log(total)
        out_ref[0] = unstack_heads((mixed / total).T, count).astype(jnp.bfloat16)

    for step in range(8):

        @pl.when(pl.program_id(0) == step)
        def _():
            run(key_spans(step, half, span))


def attend(meta, query, mine, other, scale):
    token_rows, group_width = query.shape[1:]
    half = token_rows // 2
    count = group_width // HEAD_SIZE
    everything = 8 * token_rows
    span = 1024
    arrays = [query, mine, other]
    outs = [
        shape_of(query.shape, jnp.bfloat16),
        shape_of((8, 1, count * half), jnp.float32),
    ]
    return call(
        functools.partial(attend_kernel, scale, span),
        "attend",
        meta,
        arrays,
        (8,),
        [
            pl.BlockSpec((1, half, group_width), lambda i, m: (i // 2, i % 2, 0)),
            whole(mine),
            whole(other),
        ],
        [
            pl.BlockSpec((1, half, group_width), lambda i, m: (i // 2, i % 2, 0)),
            pl.BlockSpec((1, 1, count * half), lambda i, m: (i, 0, 0)),
        ],
        outs,
        [
            pltpu.VMEM((everything, HEAD_SIZE), jnp.bfloat16),
            pltpu.VMEM((everything, HEAD_SIZE), jnp.bfloat16),
            pltpu.VMEM((HEAD_SIZE, everything), jnp.bfloat16),
        ],
        2 * 2 * 4 * token_rows * everything * group_width,
        size_of(arrays) + size_of(outs),
    )


def attend_back_kernel(scale, span, meta, query_ref, mine_ref, other_ref, log_ref, *refs):
    mixed_ref, grad_ref, grad_query_ref, grad_mine_ref, grad_other_ref = refs[:5]
    keys, values, keys_turned, grad_keys, grad_values = refs[5:]
    step = pl.program_id(0)
    half, group_width = query_ref.shape[1:]
    count = group_width // HEAD_SIZE

    @pl.when(step == 0)
    def _():
        sort_pairs(meta, mine_ref, other_ref, keys, values)
        keys_turned[...] = keys[...].T
        grad_keys[...] = jnp.zeros_like(grad_keys)
        grad_values[...] = jnp.zeros_like(grad_values)

    slot = step_slot(meta)
    query = stack_heads(query_ref[0])
    mixed = stack_heads(mixed_ref[0]).astype(jnp.float32)
    grad = stack_heads(grad_ref[0])
    delta = jnp.sum((mixed * grad.astype(jnp.float32)).T, axis=0, keepdims=True)
    log_total = log_ref[0]

    def run(spans):
        grad_turned = jnp.zeros((HEAD_SIZE, count * half), jnp.float32)
        for start, size in spans:
            at = pl.ds(start, size)
            scores = dot_last(keys[at, :], query) * scale
            probs = jnp.exp(scores - log_total)
            if start == spans[-1][0]:
                probs = jnp.where(allowed_pairs(start, slot, probs.shape, half), probs, 0.0)
            grad_probs = dot_last(values[at, :], grad)
            grad_scores = (probs * (grad_probs - delta)).astype(jnp.bfloat16)
            grad_values[at, :] += dot_plain(probs.astype(jnp.bfloat16), grad)
            grad_keys[at, :] += dot_plain(grad_scores, query)
            grad_turned += dot_plain(keys_turned[:, at], grad_scores)
        grad_query_ref[0] = unstack_heads((grad_turned * scale).T, count).astype(jnp.bfloat16)

    for at_step in range(8):

        @pl.when(step == at_step)
        def _():
            run(key_spans(at_step, half, span))

    @pl.when(step == 7)
    def _():
        for slot_at in range(16):
            block, part = (slot_at, 0) if slot_at < 8 else (15 - slot_at, 1)
            place = block >> 1
            rows = pl.ds(part * half, half)
            here = pl.ds(slot_at * half, half)
            both = jnp.concatenate([grad_keys[here, :] * scale, grad_values[here, :]], axis=1)

            @pl.when((meta[0] & 1) == (block & 1))
            def _():
                grad_mine_ref[place, rows, :] = both

            @pl.when((meta[0] & 1) != (block & 1))
            def _():
                grad_other_ref[place, rows, :] = both.astype(jnp.bfloat16)


def attend_back(meta, query, mine, other, log_total, mixed, grad, scale):
    token_rows, group_width = query.shape[1:]
    half = token_rows // 2
    count = group_width // HEAD_SIZE
    everything = 8 * token_rows
    span = 512
    arrays = [query, mine, other, log_total, mixed, grad]
    outs = [
        shape_of(query.shape, jnp.bfloat16),
        shape_of(mine.shape, jnp.float32),
        shape_of(mine.shape, jnp.bfloat16),
    ]
    return call(
        functools.partial(attend_back_kernel, scale, span),
        "attend_back",
        meta,
        arrays,
        (8,),
        [
            pl.BlockSpec((1, half, group_width), lambda i, m: (i // 2, i % 2, 0)),
            whole(mine),
            whole(other),
            pl.BlockSpec((1, 1, count * half), lambda i, m: (i, 0, 0)),
            pl.BlockSpec((1, half, group_width), lambda i, m: (i // 2, i % 2, 0)),
            pl.BlockSpec((1, half, group_width), lambda i, m: (i // 2, i % 2, 0)),
        ],
        [
            pl.BlockSpec((1, half, group_width), lambda i, m: (i // 2, i % 2, 0)),
            whole(outs[1]),
            whole(outs[2]),
        ],
        outs,
        [
            pltpu.VMEM((everything, HEAD_SIZE), jnp.bfloat16),
            pltpu.VMEM((everything, HEAD_SIZE), jnp.bfloat16),
            pltpu.VMEM((HEAD_SIZE, everything), jnp.bfloat16),
            pltpu.VMEM((everything, HEAD_SIZE), jnp.float32),
            pltpu.VMEM((everything, HEAD_SIZE), jnp.float32),
        ],
        5 * 2 * 4 * token_rows * everything * group_width,
        size_of(arrays) + size_of(outs),
    )


def leave_kernel(meta, *refs):
    parts, mine, other, states_ref, gain_ref = refs[:4], *refs[4:8]
    weight_ref, middle_ref, normed_ref = refs[8:]
    core, chip = meta[0] & 1, meta[0] >> 1
    rows = mine.shape[1]
    for i in range(4):
        weight_ref[pl.ds(aligned(2 * i + core, rows), rows), :] = mine[i]
        weight_ref[pl.ds(aligned(2 * i + 1 - core, rows), rows), :] = other[i]
    middle = states_ref[...].astype(jnp.float32)
    for r in range(4):
        at = pl.ds(aligned(chip ^ r, 2 * rows), 2 * rows)
        middle += dot_plain(parts[r][...], weight_ref[at, :])
    middle_ref[...] = middle
    inverse = lax.rsqrt(jnp.mean(middle * middle, axis=-1, keepdims=True) + norm_eps)
    normed_ref[...] = (middle * inverse * gain_ref[...]).astype(jnp.bfloat16)


def leave(meta, parts, mine, other, states, gain):
    token_rows, width = states.shape
    arrays = list(parts) + [mine, other, states, gain]
    outs = [
        shape_of((8 * mine.shape[1], width), jnp.bfloat16),
        shape_of((token_rows, width), jnp.float32),
        shape_of((token_rows, width), jnp.bfloat16),
    ]
    return call(
        leave_kernel,
        "leave",
        meta,
        arrays,
        (1,),
        [whole(a) for a in arrays],
        [whole(a) for a in outs],
        outs,
        [],
        2 * token_rows * width * width,
        size_of(arrays) + size_of(outs),
    )


def norm_back_rows(grad_normed, states, gain):
    inverse = lax.rsqrt(jnp.mean(states * states, axis=-1, keepdims=True) + norm_eps)
    scaled = states * inverse
    gain_grad = jnp.sum(grad_normed * scaled, axis=0, keepdims=True)
    grad_scaled = grad_normed * gain
    shift = jnp.mean(grad_scaled * scaled, axis=-1, keepdims=True)
    return inverse * (grad_scaled - scaled * shift), gain_grad


def enter_back_kernel(meta, final_ref, normed_ref, middle_ref, gain_ref, weight_ref, *refs):
    grad_ref, branch_ref, gain_grad_ref, mixed_ref = refs
    grad, gain_grad = norm_back_rows(normed_ref[...], middle_ref[...], gain_ref[...])
    grad = grad + final_ref[...]
    grad_ref[...] = grad
    gain_grad_ref[...] = gain_grad
    branch = grad.astype(jnp.bfloat16)
    branch_ref[...] = branch
    rows = weight_ref.shape[0] // 4
    for r in range(4):
        mixed_ref[r] = dot_last(branch, weight_ref[rows * r : rows * (r + 1), :]).astype(
            jnp.bfloat16
        )


def enter_back(meta, grad_final, grad_normed, middle, gain, weight):
    token_rows, width = middle.shape
    arrays = [grad_final, grad_normed, middle, gain, weight]
    outs = [
        shape_of((token_rows, width), jnp.float32),
        shape_of((token_rows, width), jnp.bfloat16),
        shape_of((1, width), jnp.float32),
        shape_of((4, token_rows, weight.shape[0] // 4), jnp.bfloat16),
    ]
    return call(
        enter_back_kernel,
        "enter_back",
        meta,
        arrays,
        (1,),
        [whole(a) for a in arrays],
        [whole(a) for a in outs],
        outs,
        [],
        2 * token_rows * width * width,
        size_of(arrays) + size_of(outs),
    )


def finish_kernel(meta, *refs):
    parts, mine, other = refs[:3]
    states_ref, middle_ref, gain_ref, grad_ref, gain_grad_ref, total = refs[3:]
    core, chip = meta[0] & 1, meta[0] >> 1
    columns = mine.shape[1]
    for at, weights in ((core, mine), (1 - core, other)):
        total[:, pl.ds(aligned(at, columns), columns)] = sum(
            dot_last(parts[r], weights[chip ^ r]) for r in range(4)
        )
    grad, gain_grad = norm_back_rows(
        total[...], states_ref[...].astype(jnp.float32), gain_ref[...]
    )
    grad_ref[0] = grad + middle_ref[...]
    gain_grad_ref[...] = gain_grad


def finish(meta, parts, mine, other, states, grad_middle, gain):
    token_rows, width = states.shape
    arrays = [parts, mine, other, states, grad_middle, gain]
    outs = [
        shape_of((1, token_rows, width), jnp.float32),
        shape_of((1, width), jnp.float32),
    ]
    return call(
        finish_kernel,
        "finish",
        meta,
        arrays,
        (1,),
        [whole(a) for a in arrays],
        [whole(a) for a in outs],
        outs,
        [pltpu.VMEM((token_rows, width), jnp.float32)],
        2 * token_rows * width * 4 * parts.shape[2],
        size_of(arrays) + size_of(outs),
    )


def gated(gate_up, units):
    gate_part = gate_up[:, :units]
    sigma = 1.0 / (1.0 + jnp.exp(-gate_part))
    return gate_part * sigma * gate_up[:, units:]


def gated_back(grad_act, gate_up, units):
    gate_part = gate_up[:, :units].astype(jnp.float32)
    up_part = gate_up[:, units:].astype(jnp.float32)
    sigma = 1.0 / (1.0 + jnp.exp(-gate_part))
    linear = gate_part * sigma
    grad_gate = grad_act * up_part * (sigma * (1.0 + gate_part * (1.0 - sigma)))
    return grad_gate, grad_act * linear, linear * up_part


def experts_kernel(
    meta, rows_ref, gates_ref, expert_ref, shared_ref, gate_up_ref, shared_gate_up_ref, out_ref, total
):
    expert = pl.program_id(0)
    rows = rows_ref[...]

    @pl.when(expert == 0)
    def _():
        units = shared_ref.shape[1] // 3
        gate_up = dot_plain(rows, shared_ref[:, : 2 * units])
        shared_gate_up_ref[...] = gate_up.astype(jnp.bfloat16)
        act = gated(gate_up, units).astype(jnp.bfloat16)
        total[...] = dot_last(act, shared_ref[:, 2 * units :])

    gate_up = dot_plain(rows, expert_ref[0, :, : 2 * F])
    gate_up_ref[0] = gate_up.astype(jnp.bfloat16)
    act = (gated(gate_up, F) * gates_ref[0]).astype(jnp.bfloat16)
    total[...] += dot_last(act, expert_ref[0, :, 2 * F :])

    @pl.when(expert == pl.num_programs(0) - 1)
    def _():
        out_ref[...] = total[...].astype(jnp.bfloat16)


def experts(meta, rows, gates, expert_weight, shared_slice):
    local_experts, width, _ = expert_weight.shape
    token_rows = rows.shape[0]
    shared_units = shared_slice.shape[1] // 3
    arrays = [rows, gates, expert_weight, shared_slice]
    outs = [
        shape_of((local_experts, token_rows, 2 * F), jnp.bfloat16),
        shape_of((token_rows, 2 * shared_units), jnp.bfloat16),
        shape_of((token_rows, width), jnp.bfloat16),
    ]
    return call(
        experts_kernel,
        "experts",
        meta,
        arrays,
        (local_experts,),
        [
            whole(rows),
            pl.BlockSpec((1, token_rows, 1), lambda e, m: (e, 0, 0)),
            pl.BlockSpec((1, width, 3 * F), lambda e, m: (e, 0, 0)),
            whole(shared_slice),
        ],
        [
            pl.BlockSpec((1, token_rows, 2 * F), lambda e, m: (e, 0, 0)),
            whole(outs[1]),
            whole(outs[2]),
        ],
        outs,
        [pltpu.VMEM((token_rows, width), jnp.float32)],
        2 * token_rows * width * 3 * (F * local_experts + shared_units),
        size_of(arrays) + size_of(outs),
    )


def experts_back_kernel(
    meta,
    grad_ref,
    gates_ref,
    gate_up_ref,
    shared_gate_up_ref,
    expert_ref,
    shared_ref,
    grad_gate_up_ref,
    act_ref,
    shared_grad_ref,
    shared_act_ref,
    grad_rows_ref,
    total,
):
    expert = pl.program_id(0)
    grad = grad_ref[...]

    @pl.when(expert == 0)
    def _():
        units = shared_ref.shape[1] // 3
        grad_act = dot_plain(grad, shared_ref[:, 2 * units :])
        grad_gate, grad_up, act = gated_back(grad_act, shared_gate_up_ref[...], units)
        both = jnp.concatenate([grad_gate, grad_up], axis=1).astype(jnp.bfloat16)
        shared_grad_ref[0] = both
        shared_act_ref[0] = act.astype(jnp.bfloat16)
        total[...] = dot_last(both, shared_ref[:, : 2 * units])

    grad_act = dot_plain(grad, expert_ref[0, :, 2 * F :]) * gates_ref[0]
    grad_gate, grad_up, act = gated_back(grad_act, gate_up_ref[0], F)
    both = jnp.concatenate([grad_gate, grad_up], axis=1).astype(jnp.bfloat16)
    grad_gate_up_ref[0] = both
    act_ref[0] = (act * gates_ref[0]).astype(jnp.bfloat16)
    total[...] += dot_last(both, expert_ref[0, :, : 2 * F])

    @pl.when(expert == pl.num_programs(0) - 1)
    def _():
        grad_rows_ref[...] = total[...].astype(jnp.bfloat16)


def experts_back(meta, grad, gates, gate_up, shared_gate_up, expert_weight, shared_slice):
    local_experts, width, _ = expert_weight.shape
    token_rows = grad.shape[0]
    shared_units = shared_slice.shape[1] // 3
    arrays = [grad, gates, gate_up, shared_gate_up, expert_weight, shared_slice]
    outs = [
        shape_of((local_experts, token_rows, 2 * F), jnp.bfloat16),
        shape_of((local_experts, token_rows, F), jnp.bfloat16),
        shape_of((1, token_rows, 2 * shared_units), jnp.bfloat16),
        shape_of((1, token_rows, shared_units), jnp.bfloat16),
        shape_of((token_rows, width), jnp.bfloat16),
    ]
    return call(
        experts_back_kernel,
        "experts_back",
        meta,
        arrays,
        (local_experts,),
        [
            whole(grad),
            pl.BlockSpec((1, token_rows, 1), lambda e, m: (e, 0, 0)),
            pl.BlockSpec((1, token_rows, 2 * F), lambda e, m: (e, 0, 0)),
            whole(shared_gate_up),
            pl.BlockSpec((1, width, 3 * F), lambda e, m: (e, 0, 0)),
            whole(shared_slice),
        ],
        [
            pl.BlockSpec((1, token_rows, 2 * F), lambda e, m: (e, 0, 0)),
            pl.BlockSpec((1, token_rows, F), lambda e, m: (e, 0, 0)),
            whole(outs[2]),
            whole(outs[3]),
            whole(outs[4]),
        ],
        outs,
        [pltpu.VMEM((token_rows, width), jnp.float32)],
        2 * token_rows * width * 3 * (F * local_experts + shared_units),
        size_of(arrays) + size_of(outs),
    )


def weight_grad_kernel(pairs, core_at, meta, *refs):
    keep_ref, give_ref = refs[-2:]
    at = 0
    columns = 0
    parts = []
    for count in pairs:
        lefts, rights = refs[at : at + count], refs[at + count : at + 2 * count]
        at += 2 * count
        parts.append(
            sum(dot_first(a[...], b[0]) for a, b in zip(lefts, rights)).astype(jnp.bfloat16)
        )
    half = keep_ref.shape[1]

    for core, (first, second) in ((0, (keep_ref, give_ref)), (1, (give_ref, keep_ref))):

        @pl.when((meta[core_at] & 1) == core)
        def _():
            start = 0
            for part in parts:
                stop = start + part.shape[1]
                first[0, :, start:stop] = part[:half]
                second[0, :, start:stop] = part[half:]
                start = stop


def expert_grad_kernel(count, meta, *refs):
    rows, grads, front, acts = (refs[i * count : (i + 1) * count] for i in range(4))
    out_ref = refs[-1] if len(refs) == 4 * count + 1 else refs[-2]
    tile = rows[0].shape[1]
    both = 3 * F

    def pair(front_refs, act_refs):
        return [
            sum(dot_first(a[...], b[0]) for a, b in zip(left, right)).astype(jnp.bfloat16)
            for left, right in ((rows, front_refs), (grads, act_refs))
        ]

    left, right = pair(front, acts)
    out_ref[0, :tile, : left.shape[1]] = left
    out_ref[0, :tile, left.shape[1] : both] = right
    if len(refs) > 4 * count + 1:
        held = refs[-1]
        left, right = pair(refs[4 * count : 5 * count], refs[5 * count : 6 * count])
        split, columns = left.shape[1], left.shape[1] + right.shape[1]
        held[:, :split] = left
        held[:, split:] = right
        quarter = tile // 4
        first = 2 * meta[2]
        out_ref[0, tile:, :columns] = held[pl.ds(aligned(first, quarter), quarter), :]
        out_ref[0, tile:, columns:] = held[pl.ds(aligned(first + 1, quarter), quarter), :]


def expert_grad(meta, expert, half, rows, grads, front, acts, shared=None):
    count = len(rows)
    token_rows, width = rows[0].shape
    tile = width // 4
    arrays = list(rows) + list(grads) + list(front) + list(acts)
    column = pl.BlockSpec((token_rows, tile), lambda i, m: (0, i ^ m[0]))

    def of_expert(a):
        return pl.BlockSpec((1,) + a.shape[1:], lambda i, m: (m[1], 0, 0))

    in_specs = [column] * (2 * count) + [of_expert(a) for a in arrays[2 * count :]]
    below, scratch = 0, []
    if shared is not None:
        arrays += list(shared[0]) + list(shared[1])
        in_specs += [whole(a) for a in arrays[4 * count :]]
        below = tile // 4
        columns = shared[0][0].shape[-1] + shared[1][0].shape[-1]
        scratch = [pltpu.VMEM((tile, columns), jnp.bfloat16)]
    return call(
        functools.partial(expert_grad_kernel, count),
        "expert_grad",
        jnp.stack([meta[0] >> 1, expert, half]),
        arrays,
        (4,),
        in_specs,
        pl.BlockSpec((1, tile + below, 3 * F), lambda i, m: (i, 0, 0)),
        shape_of((4, tile + below, 3 * F), jnp.bfloat16),
        scratch,
        0,
        0,
    )


def weight_grad(meta, order, operands, index):
    token_rows, width = operands[0][0][0].shape
    tile = width // 4
    scalars = jnp.stack([order, meta[0]])
    arrays, in_specs, columns = [], [], 0
    for lefts, rights in operands:
        arrays += list(lefts) + list(rights)
        in_specs += [pl.BlockSpec((token_rows, tile), lambda i, m: (0, i ^ m[0]))] * len(lefts)
        units = rights[0].shape[-1]
        at = index if rights[0].shape[0] > 1 else 0
        in_specs += [
            pl.BlockSpec((1, token_rows, units), lambda i, m, at=at: (at, 0, 0))
        ] * len(rights)
        columns += units
    tokens = token_rows * len(operands[0][0])
    counts = [len(left) for left, _ in operands]
    outs = [shape_of((4, tile // 2, columns), jnp.bfloat16)] * 2
    return call(
        functools.partial(weight_grad_kernel, counts, 1),
        "weight_grad",
        scalars,
        arrays,
        (4,),
        in_specs,
        [pl.BlockSpec((1, tile // 2, columns), lambda i, m: (i, 0, 0))] * 2,
        outs,
        [],
        2 * tokens * width * columns,
        size_of(outs) + 4 * tokens * width + 2 * tokens * columns,
    )


def place_pair_kernel(meta, *refs):
    mine, other, out_ref = refs[-3:]
    rows = out_ref.shape[1]

    @pl.when(pl.program_id(0) == 0)
    def _():
        out_ref[0] = mine[0, :rows].astype(jnp.float32)

    @pl.when(pl.program_id(0) == 1)
    def _():
        out_ref[0] = other[0, :rows].astype(jnp.float32)


def place_pair(meta, total, index, shape, mine, other):
    _, rows, columns = mine.shape
    arrays = [mine, other]
    in_specs = [
        pl.BlockSpec((1, rows, columns), lambda k, r, m: ((1 - k) * r + 3 * k, 0, 0)),
        pl.BlockSpec((1, rows, columns), lambda k, r, m: (k * r, 0, 0)),
    ]
    aliases = {}
    if total is not None:
        arrays = [total] + arrays
        in_specs = [pl.BlockSpec(memory_space=pl.ANY)] + in_specs
        aliases = {1: 0}
    return pl.pallas_call(
        place_pair_kernel,
        grid_spec=pltpu.PrefetchScalarGridSpec(
            num_scalar_prefetch=1,
            grid=(2, 4),
            in_specs=in_specs,
            out_specs=pl.BlockSpec(
                (1, shape[1] // 4, shape[2]),
                lambda k, r, m: (2 * ((m[0] & 1) ^ k) + index, (m[0] >> 1) ^ r, 0),
            ),
        ),
        out_shape=shape_of(shape, jnp.float32),
        input_output_aliases=aliases,
        compiler_params=pltpu.CompilerParams(vmem_limit_bytes=48 * 1024 * 1024),
        cost_estimate=pl.CostEstimate(
            flops=int(COSTS.get("place_pair", 1.0) * 1e9), bytes_accessed=1000, transcendentals=0
        ),
        name="place_pair",
    )(meta, *arrays)


def place_shared_kernel(meta, mine_low, mine_high, other_low, other_high, out_ref):
    core = meta[0] & 1
    rows = mine_low.shape[1]
    for at, low, high in ((core, mine_low, mine_high), (1 - core, other_low, other_high)):
        out_ref[pl.ds(aligned(2 * at, rows), rows), :] = low[0].astype(jnp.float32)
        out_ref[pl.ds(aligned(2 * at + 1, rows), rows), :] = high[0].astype(jnp.float32)


def place_shared(meta, mine, other):
    _, rows, columns = mine.shape
    units = columns // 6
    low = pl.BlockSpec((1, rows, units), lambda i, j, m: (i, 0, j))
    high = pl.BlockSpec((1, rows, units), lambda i, j, m: (i, 0, 3 + j))
    outs = shape_of((4 * rows, 2 * columns), jnp.float32)
    return call(
        place_shared_kernel,
        "place_shared",
        meta,
        [mine, mine, other, other],
        (4, 3),
        [low, high, low, high],
        pl.BlockSpec((4 * rows, units), lambda i, j, m: (0, 4 * j + (m[1] ^ i))),
        outs,
        [],
        0,
        0,
    )


def place_heads_kernel(meta, *refs):
    mine, other, out_ref = refs[:4], refs[4], refs[5]
    core, chip = meta[0] & 1, meta[0] >> 1
    rows, columns = mine[0].shape
    group_width = columns - 2 * HEAD_SIZE
    for r in range(4):
        head = chip ^ r
        for at, pieces in ((core, [piece[...] for piece in mine]), (1 - core, other)):
            to = pl.ds(aligned(at, rows), rows)
            values = pieces[r].astype(jnp.float32)
            out_ref[to, pl.ds(aligned(head, group_width), group_width)] = values[:, :group_width]
            out_ref[to, pl.ds(aligned(4 * group_width // HEAD_SIZE + head, HEAD_SIZE), HEAD_SIZE)] = (
                values[:, group_width : group_width + HEAD_SIZE]
            )
            out_ref[
                to, pl.ds(aligned(4 * group_width // HEAD_SIZE + 4 + head, HEAD_SIZE), HEAD_SIZE)
            ] = values[:, group_width + HEAD_SIZE :]


def place_heads(meta, mine, other):
    rows, columns = mine[0].shape
    arrays = list(mine) + [other]
    outs = shape_of((2 * rows, 4 * columns), jnp.float32)
    return call(
        place_heads_kernel,
        "place_heads",
        meta,
        arrays,
        (1,),
        [whole(a) for a in arrays],
        whole(outs),
        outs,
        [],
        0,
        size_of(arrays + [outs]),
    )


def join_shared_kernel(meta, mine, other, out_ref):
    step = pl.program_id(0)
    rows = mine.shape[2]
    first = meta[0] ^ (2 * step)
    for i in range(4):
        at = 8 * (meta[1] ^ i)
        out_ref[pl.ds(aligned(at + first, rows), rows), :] = mine[0, i]
        out_ref[pl.ds(aligned(at + (first ^ 1), rows), rows), :] = other[0, i]


def join_shared(meta, mine, other):
    _, _, rows, columns = mine.shape
    block = pl.BlockSpec((1, 4, rows, columns), lambda r, m: (r, 0, 0, 0))
    outs = shape_of((32 * rows, columns), jnp.bfloat16)
    return call(
        join_shared_kernel,
        "join_shared",
        meta,
        [mine, other],
        (4,),
        [block, block],
        whole(outs),
        outs,
        [],
        0,
        size_of([mine, other, outs]),
    )


class Clock:
    def __init__(self):
        self.last = None

    def __call__(self, *values):
        if self.last is None:
            return values if len(values) > 1 else values[0]
        held = lax.optimization_barrier(tuple(values) + (self.last,))[:-1]
        return held if len(held) > 1 else held[0]

    def mark(self, value):
        self.last = value
        return value


EARLY = (
    "H", "W", "K", "S", "K", "W", "S", "W", "K", "S", "O", "S", "M", "M", "S", "O", "M", "S", "M", "R", "M", "K", "M", "K",
    "M", "K", "R", "M", "K", "M", "M", "M", "M", "R", "M", "M",
)
LATE = (
    "L", "0", "1", "0", "0", "L", "1", "1", "L", "L", "O", "0", "1", "L", "L", "1", "0", "O", "Q", "1", "O", "0", "L", "Q",
    "O", "L", "Q", "Q", "O", "Q", "L", "1", "0", "O", "Q", "S", "L", "O", "Q", "1", "S", "L", "0", "O", "Q", "L", "Q", "O",
    "S",
)


def fast_device(
    hidden,
    teacher,
    valid_mask,
    routes,
    route_gates,
    gain_in,
    query_key_value_weight,
    out_weight,
    gain_mid,
    shared_weight,
    expert_weight,
):
    token_rows, width = hidden.shape[1:]
    context_count, shard_count = 8, 4
    context_index = lax.axis_index("ctx").astype(jnp.int32)
    shard_index = lax.axis_index("wt").astype(jnp.int32)
    plain_meta = jnp.stack([context_index, shard_index])
    core = context_index & 1
    chip = context_index >> 1
    at_end = (shard_index == 0) | (shard_index == shard_count - 1)
    group_width = QUERY_HEADS // KEY_VALUE_HEADS * HEAD_SIZE
    query_width = QUERY_HEADS * HEAD_SIZE
    kv_width = KEY_VALUE_HEADS * HEAD_SIZE
    scale = 1.0 / math.sqrt(HEAD_SIZE)
    all_tokens = token_rows * context_count * shard_count
    shard_rows = query_key_value_weight.shape[0]
    half_rows = shard_rows // 2
    local_experts = expert_weight.shape[0]
    bf16, f32 = jnp.bfloat16, jnp.float32
    states = hidden[0]
    clock = Clock()
    have = {}

    def meta():
        return clock(plain_meta)

    def now(*values):
        return clock(*values)

    def ready(*values):
        values = clock(*values)
        clock.mark(values[0] if isinstance(values, tuple) or isinstance(values, list) else values)
        return values


    def hidden_chain():
        have["blocks"] = chips_exchange(jnp.broadcast_to(states, (4,) + states.shape))
        yield

    def qkv_chain():
        rows = lax.dynamic_slice_in_dim(query_key_value_weight, core * half_rows, half_rows, 0)
        half = jnp.concatenate(
            [
                lax.dynamic_slice_in_dim(rows, chip * group_width, group_width, 1),
                lax.dynamic_slice_in_dim(rows, query_width + chip * HEAD_SIZE, HEAD_SIZE, 1),
                lax.dynamic_slice_in_dim(
                    rows, query_width + kv_width + chip * HEAD_SIZE, HEAD_SIZE, 1
                ),
            ],
            axis=1,
        )
        came = line_swap(half, 1)
        yield
        pair = clock.mark(jnp.stack([half, now(came)]))
        came = line_swap(pair, 2)
        yield
        have["qkv_mine"] = clock.mark(jnp.concatenate([pair, now(came)]))
        have["qkv_other"] = flip(have["qkv_mine"], 1)
        yield

    def small_chain():
        expert_ids = jnp.arange(EXPERTS, dtype=jnp.int32)
        matrix = jnp.sum(
            jnp.where(
                routes[0][None, :, :] == expert_ids[:, None, None], route_gates[0][None, :, :], 0.0
            ),
            axis=-1,
        )
        have["valid"] = valid_mask[0].astype(f32)
        gains = jnp.concatenate([gain_in, gain_mid]).astype(f32).reshape(-1, token_rows)
        gain_rows = gains.shape[0]
        filled = EXPERTS + gain_rows
        pack = jnp.concatenate(
            [
                matrix,
                gains,
                jnp.full((32 - filled, token_rows), jnp.sum(have["valid"]), f32),
            ]
        )
        came = line_swap(pack, 1)
        yield
        pair = clock.mark(jnp.stack([pack, now(came)]))
        came = line_swap(pair, 2)
        yield
        all_packs = clock.mark(jnp.concatenate([pair, now(came)]))
        have["gates"] = [
            lax.dynamic_slice_in_dim(
                all_packs[i], shard_index * local_experts, local_experts, 0
            )[..., None]
            for i in range(4)
        ]
        gains = all_packs[:, EXPERTS:filled].reshape(4, 2, shard_rows)
        gains = jnp.stack([pick(gains, shard_index ^ i) for i in range(4)], axis=1)
        have["gains"] = gains.reshape(2, 1, width)
        total = jnp.broadcast_to(jnp.sum(all_packs[:, filled, 0]), (8, 128))
        yield
        total = now(total)
        for bit in (1, 2, 4):
            came = flip(total, bit)
            yield
            total = clock.mark(total + now(came))
        have["count"] = total[0, 0]
        yield

    def shared_chain():
        eighth = shard_rows // 8
        units = SF // shard_count
        piece = lax.dynamic_slice_in_dim(shared_weight, context_index * eighth, eighth, 0)
        piece = piece.reshape(eighth, 3, shard_count, units)

        piece = jnp.transpose(piece, (2, 0, 1, 3)).reshape(shard_count, eighth, 3 * units)
        parts = [pick(piece, shard_index ^ i) for i in range(4)]
        came = line_swap(now(jnp.stack([parts[1], parts[3]])), 1)
        yield
        came = now(came)
        mine = jnp.stack([parts[0], came[0]])
        came = line_swap(clock.mark(jnp.stack([parts[2], came[1]])), 2)
        yield
        pieces = clock.mark(jnp.concatenate([mine, now(came)]))
        came = flip(pieces, 2)
        yield
        pair = clock.mark(jnp.stack([pieces, now(came)]))
        came = flip(pair, 4)
        yield
        mine = clock.mark(jnp.concatenate([pair, now(came)]))
        other = flip(mine, 1)
        yield
        have["shared"] = join_shared(meta(), mine, other)
        clock.mark(have["shared"])
        yield

    def out_chain():
        half = lax.dynamic_slice_in_dim(now(out_weight), core * half_rows, half_rows, 0)
        came = line_exchange(jnp.broadcast_to(half, (4,) + half.shape))
        yield
        have["out_mine"] = clock.mark(now(came))
        have["out_other"] = flip(have["out_mine"], 1)
        yield

    def qkv_all_chain():
        half = lax.dynamic_slice_in_dim(
            now(have["qkv_slice"]), core * (width // 2), width // 2, 0
        )
        came = flip(half, 2)
        yield
        pair = clock.mark(jnp.stack([half, now(came)]))
        came = flip(pair, 4)
        yield
        have["rel_mine"] = clock.mark(jnp.concatenate([pair, now(came)]))
        have["rel_other"] = flip(have["rel_mine"], 1)
        yield

    def main_chain():
        gains = have["gains"]
        normed_in, query, pair, qkv_slice = project(
            meta(), have["blocks"], gains[0], have["qkv_mine"], have["qkv_other"], group_width
        )
        clock.mark(pair)
        have["normed_in"], have["qkv_slice"] = normed_in, qkv_slice
        pair_other = flip(pair, 1)
        yield
        mixed_heads, log_total = attend(meta(), query, pair, pair_other, scale)
        clock.mark(log_total)
        have["attend"] = (query, pair, pair_other, log_total, mixed_heads)
        parts = ready(*[pick(mixed_heads, chip ^ r) for r in range(4)])
        mixed = [parts[0]] + [flip(parts[r], 2 * r) for r in (1, 2, 3)]
        have["mixed"] = mixed
        yield
        out_full, middle, normed_mid = leave(
            meta(), mixed, have["out_mine"], have["out_other"], states, gains[1]
        )
        have["out_full"], have["middle"] = out_full, middle
        clock.mark(normed_mid)

        near, center = line_swap(normed_mid, 1), line_middle(normed_mid)
        yield
        gates, shared_slice = have["gates"], have["shared"]
        gate_ups, shared_gate_ups, outs = [], [], []

        def forward(rows, i):
            result = experts(meta(), rows, gates[i], expert_weight, shared_slice)
            clock.mark(result[2])
            gate_ups.append(result[0])
            shared_gate_ups.append(result[1])
            outs.append(result[2])

        forward(normed_mid, 0)
        yield
        near, center = now(near, center)
        far, outward = line_middle(near), line_outward(center)
        forward(near, 1)
        yield
        far, outward = now(far, outward)
        outward_far = line_outward(far)
        third = clock.mark(jnp.where(at_end, outward, far))
        forward(third, 2)
        yield
        outward_far = now(outward_far)
        fourth = clock.mark(jnp.where(at_end, outward_far, center))
        forward(fourth, 3)
        line_rows = [normed_mid, near, third, fourth]
        came = line_inward(outs[3])
        yield
        carried = clock.mark(outs[2] + now(came))
        inward, crossed = line_inward(carried), line_middle(carried)
        yield
        inward, crossed = now(inward, crossed)
        near_out, middle_out = ready(outs[1] + crossed, outs[3] + inward)
        near_out, middle_out = line_swap(near_out, 1), line_middle(middle_out)
        yield
        near_out, middle_out = now(near_out, middle_out)
        final_state = (
            middle + outs[0].astype(f32) + near_out.astype(f32) + middle_out.astype(f32)
        )
        valid = have["valid"]
        deviation = final_state - teacher[0].astype(f32)
        have["squared"] = jnp.sum(valid[:, None] * deviation * deviation)
        grad_final = all_tokens / have["count"] * valid[:, None] * deviation
        have["final"], have["grad_final"] = final_state.astype(bf16)[None], grad_final
        grad_low = clock.mark(grad_final.astype(bf16))
        near, center = line_swap(grad_low, 1), line_middle(grad_low)
        yield
        kept = []

        def backward(grads, i):
            kept.append(
                experts_back(
                    meta(),
                    grads,
                    gates[i],
                    gate_ups[i],
                    shared_gate_ups[i],
                    expert_weight,
                    shared_slice,
                )
            )
            clock.mark(kept[-1][4])

        backward(grad_low, 0)
        yield
        near, center = now(near, center)
        far, outward = line_middle(near), line_outward(center)
        backward(near, 1)
        yield
        far, outward = now(far, outward)
        outward_far = line_outward(far)
        third = clock.mark(jnp.where(at_end, outward, far))
        backward(third, 2)
        yield
        outward_far = now(outward_far)
        fourth = clock.mark(jnp.where(at_end, outward_far, center))
        backward(fourth, 3)
        have["line"] = (line_rows, [grad_low, near, third, fourth])
        have["experts"] = list(zip(*kept))
        yield


    def states_chain():
        outs = have["experts"][4]
        came = line_inward(outs[3])
        yield
        carried = clock.mark(outs[2] + now(came))
        inward, crossed = line_inward(carried), line_middle(carried)
        yield
        inward, crossed = now(inward, crossed)
        near_out, middle_out = ready(outs[1] + crossed, outs[3] + inward)
        near_out, middle_out = line_swap(near_out, 1), line_middle(middle_out)
        yield
        near_out, middle_out = now(near_out, middle_out)
        grad_normed = clock.mark(
            outs[0].astype(f32) + near_out.astype(f32) + middle_out.astype(f32)
        )
        grad_middle, grad_branch, grad_gain_mid, grad_mixed = enter_back(
            meta(),
            have["grad_final"],
            grad_normed,
            have["middle"],
            have["gains"][1],
            have["out_full"],
        )
        clock.mark(grad_branch)
        have["grad_branch"], have["grad_gain_mid"] = grad_branch, grad_gain_mid
        grad_mixed = chips_exchange(ready(grad_mixed))
        yield
        query, pair, pair_other, log_total, mixed_heads = have["attend"]
        grad_query, grad_pair, grad_other = attend_back(
            meta(), query, pair, pair_other, log_total, mixed_heads, grad_mixed, scale
        )
        clock.mark(grad_query)
        came = flip(grad_other, 1)
        yield
        grad_pair = grad_pair + now(came).astype(f32)
        projected = clock.mark(jnp.concatenate([grad_query, grad_pair.astype(bf16)], axis=-1))
        have["grad_projected"] = projected
        parts = chips_exchange(ready(projected))
        yield
        grad_hidden, grad_gain_in = finish(
            meta(),
            parts,
            have["rel_mine"],
            have["rel_other"],
            states,
            grad_middle,
            have["gains"][0],
        )
        clock.mark(grad_gain_in)
        have["grad_hidden"] = grad_hidden
        sums = jnp.concatenate(
            [grad_gain_in, have["grad_gain_mid"], jnp.full((6, width), have["squared"], f32)],
            axis=0,
        )
        for offset in (1, 2):
            came = line_swap(sums, offset)
            yield
            sums = clock.mark(sums + now(came))
        for bit in (1, 2, 4):
            came = flip(sums, bit)
            yield
            sums = clock.mark(sums + now(came))
        own = lax.dynamic_slice_in_dim(sums, shard_index * shard_rows, shard_rows, 1)
        have["sums"] = (own, 0.5 * sums[2, 0] / (have["count"] * width))
        yield

    def expert_chain(index):
        line_rows, line_grads = have["line"]
        grad_gate_ups, acts, shared_grads, shared_acts = have["experts"][:4]
        shared = (shared_grads, shared_acts) if index == 0 else None

        def grad_of(at):
            return clock.mark(
                expert_grad(
                    meta(),
                    2 * at + index,
                    at,
                    line_rows,
                    line_grads,
                    grad_gate_ups,
                    acts,
                    shared,
                )
            )

        came = flip(grad_of(1 - core), 1)
        yield
        keep = grad_of(core)
        yield
        x_first = index % 2 == 0
        first, second = (2, 4) if x_first else (4, 2)
        picked = ((1, 3), (0, 2)) if x_first else ((2, 3), (0, 1))
        pieces = keep.shape[1] // 96

        def split_sum(keep, came):
            return [
                jnp.stack([keep[i] + came[i] for i in places]) for places in picked
            ]

        give, keep = blend(meta(), "blend_split", split_sum, [keep, came], pieces)
        clock.mark(give)
        came = flip(give, first)
        yield
        give, keep = blend(
            meta(), "blend_pair", lambda k, c: [k[1] + c[1], k[0] + c[0]], [keep, came], pieces
        )
        clock.mark(give)
        came = flip(give, second)
        yield
        own = clock.mark(blend(meta(), "blend_sum", lambda k, c: k + c, [keep, came], pieces))
        came = flip(own, second)
        yield
        pair = clock.mark(
            blend(meta(), "blend_stack", lambda a, b: jnp.stack([a, b]), [own, came], pieces)
        )
        came = flip(pair, first)
        yield

        def stack_four(near, far):
            if x_first:
                return jnp.stack([near[0], far[0], near[1], far[1]])
            return jnp.stack([near[0], near[1], far[0], far[1]])

        stacked = clock.mark(blend(meta(), "blend_four", stack_four, [pair, came], pieces))
        other = flip(stacked, 1)
        if index == 0:
            have["shared_sum"] = stacked[:, shard_rows:]
        yield
        have["grad_experts"] = place_pair(
            meta(), have.get("grad_experts"), index, expert_weight.shape, stacked, other
        )
        clock.mark(have["grad_experts"])
        yield

    def shared_grad_chain():
        total = now(have["shared_sum"])
        parts = ready(*[pick(total, chip ^ shard_index ^ i) for i in range(4)])
        came = [line_swap(parts[i], i) for i in (1, 2, 3)]
        yield
        mine = clock.mark(jnp.stack([parts[0]] + list(now(*came))))
        other = flip(mine, 1)
        yield
        have["grad_shared"] = clock.mark(place_shared(meta(), mine, other))
        yield

    def line_reduce_steps(keep, came):
        came = now(came)
        parts = [keep[i] + came[i] for i in range(4)]
        came = line_inward(clock.mark(parts[3]))
        yield
        carried = clock.mark(parts[2] + now(came))
        inward, crossed = line_inward(carried), line_middle(carried)
        yield
        inward, crossed = now(inward, crossed)
        near_out, middle_out = ready(parts[1] + crossed, parts[3] + inward)
        near_out, middle_out = line_swap(near_out, 1), line_middle(middle_out)
        yield
        near_out, middle_out = now(near_out, middle_out)
        have["line_sum"] = clock.mark(
            (parts[0].astype(f32) + near_out.astype(f32) + middle_out.astype(f32)).astype(bf16)
        )

    def out_grad_chain():
        mixed = jnp.concatenate(have["mixed"], axis=1)
        keep, give = weight_grad(
            meta(), chip ^ shard_index, [([mixed], [have["grad_branch"][None]])], 0
        )
        clock.mark(keep)
        came = flip(give, 1)
        yield
        yield from line_reduce_steps(keep, came)
        total = have["line_sum"]
        yield
        total = ready(total)
        came = flip(total, 2)
        yield
        total = clock.mark(total + now(came))
        came = flip(total, 4)
        yield
        mine = clock.mark(total + now(came))
        other = flip(mine, 1)
        yield
        mine, other = now(mine, other)
        have["grad_out"] = clock.mark(
            jnp.where(
                core == 0,
                jnp.concatenate([mine, other], axis=0),
                jnp.concatenate([other, mine], axis=0),
            ).astype(f32)
        )
        yield

    def qkv_grad_chain():
        normed_in = have["normed_in"].reshape(4 * token_rows, width)
        projected = have["grad_projected"].reshape(1, 4 * token_rows, -1)
        keep, give = weight_grad(meta(), shard_index, [([normed_in], [projected])], 0)
        clock.mark(keep)
        came = flip(give, 1)
        yield
        yield from line_reduce_steps(keep, came)
        own = have["line_sum"]
        yield
        own = ready(own)
        came = flip(own, 2)
        yield
        pair = clock.mark(jnp.stack([own, now(came)]))
        came = flip(pair, 4)
        yield
        mine = clock.mark(jnp.concatenate([pair, now(came)]))
        other = flip(mine, 1)
        yield
        have["grad_qkv"] = clock.mark(place_heads(meta(), [mine[r] for r in range(4)], other))
        yield

    early = {
        "H": hidden_chain(),
        "W": qkv_chain(),
        "S": shared_chain(),
        "O": out_chain(),
        "K": small_chain(),
        "R": qkv_all_chain(),
        "M": main_chain(),
    }
    late = {
        "L": states_chain(),
        "S": shared_grad_chain(),
        "O": out_grad_chain(),
        "Q": qkv_grad_chain(),
    }
    for index in range(local_experts // 2):
        late[str(index)] = expert_chain(index)
    for chains, order in ((early, EARLY), (late, LATE)):
        for name in order:
            next(chains[name], None)
        for name in chains:
            for _ in chains[name]:
                pass

    own, loss_value = have["sums"]
    return (
        have["final"],
        loss_value,
        have["grad_hidden"],
        own[0],
        have["grad_qkv"],
        have["grad_out"],
        own[1],
        have["grad_shared"],
        have["grad_experts"],
    )


def solution(mesh):
    in_specs = (
        P("wt", "ctx", None),
        P("wt", "ctx", None),
        P("wt", "ctx"),
        P("wt", "ctx", None),
        P("wt", "ctx", None),
        P("wt"),
        P("wt", None),
        P("wt", None),
        P("wt"),
        P("wt", None),
        P("wt", None, None),
    )
    out_specs = (
        P("wt", "ctx", None),
        P(),
        P("wt", "ctx", None),
        P("wt"),
        P("wt", None),
        P("wt", None),
        P("wt"),
        P("wt", None),
        P("wt", None, None),
    )
    plane_of_eight = dict(mesh.shape) == {"ctx": 8, "wt": 4}
    return jax.shard_map(
        fast_device if plane_of_eight else on_device, mesh=mesh, in_specs=in_specs, out_specs=out_specs, check_vma=False
    )
```

```python
import functools
import math

import jax
import jax.numpy as jnp
from jax import lax
from jax.experimental import pallas as pl
from jax.experimental.pallas import tpu as pltpu
from jax.sharding import PartitionSpec as P

QUERY_HEADS = 12
KEY_VALUE_HEADS = 4
HEAD_SIZE = 128
F = 512
SF = 1024
EXPERTS = 16
TOP = 6


norm_eps = 1e-05
masked_score = -1e30


def sigmoid_linear(values):
    return values * jax.nn.sigmoid(values)


def silu_slope(values):
    sigma_value = jax.nn.sigmoid(values)
    return sigma_value * (1.0 + values * (1.0 - sigma_value))


def normalize(values):
    inverse = lax.rsqrt(jnp.mean(values * values, axis=-1, keepdims=True) + norm_eps)
    return (values * inverse, inverse)


def norm_back(grad_normed, scaled, inverse, gain_vector):
    grad_scaled = grad_normed * gain_vector
    return inverse * (grad_scaled - scaled * jnp.mean(grad_scaled * scaled, axis=-1, keepdims=True))


def positions(row_ids, token_rows, context_count):
    piece_index = row_ids // token_rows
    within = row_ids % token_rows
    half_rows = token_rows // 2
    mirrored = jnp.where(within < half_rows, piece_index, 2 * context_count - 1 - piece_index)
    return mirrored * half_rows + within % half_rows


def route_tables(local_routes, local_gates, experts, capacity):
    token_rows = local_routes.shape[0]
    flat_routes = local_routes.reshape(-1)
    one_hot = (flat_routes[:, None] == jnp.arange(experts, dtype=jnp.int32)[None, :]).astype(
        jnp.int32
    )
    earlier = jnp.cumsum(one_hot, axis=0) - one_hot
    slot_index = jnp.sum(earlier * one_hot, axis=1)
    token_index = jnp.arange(flat_routes.shape[0], dtype=jnp.int32) // local_routes.shape[1]
    slot_table = (
        jnp.full((experts, capacity), token_rows, jnp.int32)
        .at[flat_routes, slot_index]
        .set(token_index)
    )
    slot_gate = (
        jnp.zeros((experts, capacity), jnp.float32)
        .at[flat_routes, slot_index]
        .set(local_gates.reshape(-1))
    )
    return (slot_table, slot_gate)


def block_scores(query_rows, key_block, key_position, query_place, score_scale):
    scores = (
        jnp.einsum("qhgd,khd->qhgk", query_rows, key_block, preferred_element_type=jnp.float32)
        * score_scale
    )
    allowed = key_position[None, None, None, :] <= query_place[:, None, None, None]
    return jnp.where(allowed, scores, masked_score)


def attend_forward(
    query_rows, blocked_keys, blocked_values, place_blocks, query_place, score_scale
):
    head_shape = query_rows.shape[:3]

    def online_step(running, block_args):
        running_max, running_sum, accumulated = running
        key_block, value_block, key_position = block_args
        scores = block_scores(query_rows, key_block, key_position, query_place, score_scale)
        new_max = jnp.maximum(running_max, jnp.max(scores, axis=-1))
        rescale = jnp.exp(running_max - new_max)
        powers = jnp.exp(scores - new_max[..., None])
        new_sum = running_sum * rescale + jnp.sum(powers, axis=-1)
        weighted = jnp.einsum(
            "qhgk,khd->qhgd",
            powers.astype(jnp.bfloat16),
            value_block,
            preferred_element_type=jnp.float32,
        )
        return ((new_max, new_sum, accumulated * rescale[..., None] + weighted), None)

    initial = (
        jnp.full(head_shape, masked_score, jnp.float32),
        jnp.zeros(head_shape, jnp.float32),
        jnp.zeros(query_rows.shape, jnp.float32),
    )
    row_max, row_sum, accumulated = lax.scan(
        online_step, initial, (blocked_keys, blocked_values, place_blocks)
    )[0]
    log_total = row_max + jnp.log(row_sum)
    return (accumulated / row_sum[..., None], log_total)


def attend_backward(
    query_rows,
    blocked_keys,
    blocked_values,
    place_blocks,
    query_place,
    log_total,
    attention_output_gradient,
    attention_output,
    score_scale,
):
    row_delta = jnp.sum(attention_output_gradient.astype(jnp.float32) * attention_output, axis=-1)

    def block_grads(grad_queries, block_args):
        key_block, value_block, key_position = block_args
        scores = block_scores(query_rows, key_block, key_position, query_place, score_scale)
        probabilities = jnp.exp(scores - log_total[..., None])
        grad_probs = jnp.einsum(
            "qhgd,khd->qhgk",
            attention_output_gradient,
            value_block,
            preferred_element_type=jnp.float32,
        )
        grad_scores = (probabilities * (grad_probs - row_delta[..., None])).astype(jnp.bfloat16)
        grad_queries = grad_queries + jnp.einsum(
            "qhgk,khd->qhgd", grad_scores, key_block, preferred_element_type=jnp.float32
        )
        grad_keys = (
            jnp.einsum(
                "qhgk,qhgd->khd", grad_scores, query_rows, preferred_element_type=jnp.float32
            )
            * score_scale
        )
        grad_values = jnp.einsum(
            "qhgk,qhgd->khd",
            probabilities.astype(jnp.bfloat16),
            attention_output_gradient,
            preferred_element_type=jnp.float32,
        )
        return (grad_queries, (grad_keys, grad_values))

    grad_queries, (grad_keys, grad_values) = lax.scan(
        block_grads,
        jnp.zeros(query_rows.shape, jnp.float32),
        (blocked_keys, blocked_values, place_blocks),
    )
    return (grad_queries * score_scale, grad_keys, grad_values)


def gate_up_grads(grad_act, gate_up, hidden_units):
    gate_part = gate_up[..., :hidden_units]
    up_part = gate_up[..., hidden_units:]
    return jnp.concatenate(
        [grad_act * up_part * silu_slope(gate_part), grad_act * sigmoid_linear(gate_part)], axis=-1
    ).astype(jnp.bfloat16)


def on_device(
    hidden,
    teacher,
    valid_mask,
    routes,
    route_gates,
    gain_in,
    query_key_value_weight,
    out_weight,
    gain_mid,
    shared_weight,
    expert_weight,
):
    token_rows = hidden.shape[1]
    model_width = hidden.shape[2]
    context_count = lax.axis_size("ctx")
    shard_count = lax.axis_size("wt")
    seq_rows = token_rows * context_count
    all_tokens = seq_rows * shard_count
    query_groups = QUERY_HEADS // KEY_VALUE_HEADS
    query_total_width = QUERY_HEADS * HEAD_SIZE
    key_value_width = KEY_VALUE_HEADS * HEAD_SIZE
    score_scale = 1.0 / math.sqrt(HEAD_SIZE)
    key_row_count = min(512, seq_rows)
    number_of_blocks = seq_rows // key_row_count
    capacity = token_rows * TOP // 12
    local_experts = expert_weight.shape[0]
    contract_last = (((1,), (1,)), ((), ()))
    contract_first = (((0,), (0,)), ((), ()))
    full_gain_in, full_qkv, full_out, full_gain_mid, full_shared = (
        lax.all_gather(gain_in, "wt", axis=0, tiled=True),
        lax.all_gather(query_key_value_weight, "wt", axis=0, tiled=True),
        lax.all_gather(out_weight, "wt", axis=0, tiled=True),
        lax.all_gather(gain_mid, "wt", axis=0, tiled=True),
        lax.all_gather(shared_weight, "wt", axis=0, tiled=True),
    )
    gain_in_float = full_gain_in.astype(jnp.float32)
    gain_mid_float = full_gain_mid.astype(jnp.float32)
    inputs = hidden[0].astype(jnp.float32)
    scaled_in, inverse_in = normalize(inputs)
    normed_in = (scaled_in * gain_in_float).astype(jnp.bfloat16)
    projected_rows = jnp.dot(normed_in, full_qkv, preferred_element_type=jnp.float32).astype(
        jnp.bfloat16
    )
    query_rows = projected_rows[:, :query_total_width].reshape(
        token_rows, KEY_VALUE_HEADS, query_groups, HEAD_SIZE
    )
    context_local = projected_rows[:, query_total_width:]
    context_gathered = lax.all_gather(context_local, "ctx", axis=0, tiled=True)
    context_index = lax.axis_index("ctx")
    query_place = positions(
        context_index * token_rows + jnp.arange(token_rows, dtype=jnp.int32),
        token_rows,
        context_count,
    )
    place_blocks = positions(
        jnp.arange(seq_rows, dtype=jnp.int32), token_rows, context_count
    ).reshape(number_of_blocks, key_row_count)
    blocked_keys = context_gathered[:, :key_value_width].reshape(
        number_of_blocks, key_row_count, KEY_VALUE_HEADS, HEAD_SIZE
    )
    blocked_values = context_gathered[:, key_value_width:].reshape(
        number_of_blocks, key_row_count, KEY_VALUE_HEADS, HEAD_SIZE
    )
    attention_output, log_total = attend_forward(
        query_rows, blocked_keys, blocked_values, place_blocks, query_place, score_scale
    )
    mixed_rows = attention_output.reshape(token_rows, query_total_width).astype(jnp.bfloat16)
    middle = inputs + jnp.dot(mixed_rows, full_out, preferred_element_type=jnp.float32)
    scaled_mid, inverse_mid = normalize(middle)
    normed_mid = (scaled_mid * gain_mid_float).astype(jnp.bfloat16)
    shared_gate_up = jnp.dot(
        normed_mid, full_shared[:, : 2 * SF], preferred_element_type=jnp.float32
    )
    shared_act = (sigmoid_linear(shared_gate_up[:, :SF]) * shared_gate_up[:, SF:]).astype(
        jnp.bfloat16
    )
    shared_out = lax.dot_general(
        shared_act, full_shared[:, 2 * SF :], contract_last, preferred_element_type=jnp.float32
    )
    slot_table, slot_gate = route_tables(routes[0], route_gates[0], EXPERTS, capacity)
    padded_rows = jnp.concatenate([normed_mid, jnp.zeros((1, model_width), jnp.bfloat16)], axis=0)
    expert_rows = jnp.take(padded_rows, slot_table, axis=0)
    arrived = lax.all_to_all(expert_rows, "wt", split_axis=0, concat_axis=0, tiled=True)
    slot_count = arrived.shape[1]
    grouped = arrived.reshape(shard_count, local_experts, slot_count, model_width)
    owner_gate_up = jnp.einsum(
        "wesd,edf->wesf", grouped, expert_weight[:, :, : 2 * F], preferred_element_type=jnp.float32
    )
    owner_act = (sigmoid_linear(owner_gate_up[..., :F]) * owner_gate_up[..., F:]).astype(
        jnp.bfloat16
    )
    owner_out = jnp.einsum(
        "wesf,edf->wesd",
        owner_act,
        expert_weight[:, :, 2 * F :],
        preferred_element_type=jnp.float32,
    ).astype(jnp.bfloat16)
    returned = lax.all_to_all(
        owner_out.reshape(shard_count * local_experts, slot_count, model_width),
        "wt",
        split_axis=0,
        concat_axis=0,
        tiled=True,
    )
    expert_out, owner_rows, owner_gate_up, owner_act = (
        returned,
        arrived,
        owner_gate_up.reshape(shard_count * local_experts, slot_count, 2 * F),
        owner_act.reshape(shard_count * local_experts, slot_count, F),
    )
    routed = (
        jnp.zeros((token_rows + 1, model_width), jnp.float32)
        .at[slot_table]
        .add(expert_out.astype(jnp.float32) * slot_gate[..., None])[:token_rows]
    )
    final_state = middle + shared_out + routed
    valid_float = valid_mask[0].astype(jnp.float32)
    deviation = final_state - teacher[0].astype(jnp.float32)
    squared_local = jnp.sum(valid_float[:, None] * deviation * deviation)
    count_local = jnp.sum(valid_float)
    squared_total, valid_count = lax.psum((squared_local, count_local), ("ctx", "wt"))
    loss_value = 0.5 * squared_total / (valid_count * model_width)
    grad_final = all_tokens / valid_count * valid_float[:, None] * deviation
    grad_shared_out = grad_final.astype(jnp.bfloat16)
    grad_shared_act = jnp.dot(
        grad_shared_out, full_shared[:, 2 * SF :], preferred_element_type=jnp.float32
    )
    grad_shared_down = lax.dot_general(
        grad_shared_out, shared_act, contract_first, preferred_element_type=jnp.float32
    )
    grad_shared_gate_up = gate_up_grads(grad_shared_act, shared_gate_up, SF)
    grad_normed_mid = lax.dot_general(
        grad_shared_gate_up,
        full_shared[:, : 2 * SF],
        contract_last,
        preferred_element_type=jnp.float32,
    )
    grad_shared_front = lax.dot_general(
        normed_mid, grad_shared_gate_up, contract_first, preferred_element_type=jnp.float32
    )
    grad_shared_full = jnp.concatenate([grad_shared_front, grad_shared_down], axis=1)
    padded_grads = jnp.concatenate([grad_final, jnp.zeros((1, model_width), jnp.float32)], axis=0)
    grad_expert_out = (jnp.take(padded_grads, slot_table, axis=0) * slot_gate[..., None]).astype(
        jnp.bfloat16
    )
    grad_arrived = lax.all_to_all(grad_expert_out, "wt", split_axis=0, concat_axis=0, tiled=True)
    grad_grouped = grad_arrived.reshape(shard_count, local_experts, capacity, model_width)
    owner_gate_up_grouped = owner_gate_up.reshape(shard_count, local_experts, capacity, 2 * F)
    owner_act_grouped = owner_act.reshape(shard_count, local_experts, capacity, F)
    owner_rows_grouped = owner_rows.reshape(shard_count, local_experts, capacity, model_width)
    grad_owner_act = jnp.einsum(
        "wecd,edf->wecf",
        grad_grouped,
        expert_weight[:, :, 2 * F :],
        preferred_element_type=jnp.float32,
    )
    grad_owner_gate_up = gate_up_grads(grad_owner_act, owner_gate_up_grouped, F)
    grad_owner_rows = jnp.einsum(
        "wecf,edf->wecd",
        grad_owner_gate_up,
        expert_weight[:, :, : 2 * F],
        preferred_element_type=jnp.float32,
    ).astype(jnp.bfloat16)
    front = jnp.einsum(
        "wecd,wecf->edf", owner_rows_grouped, grad_owner_gate_up, preferred_element_type=jnp.float32
    )
    back = jnp.einsum(
        "wecd,wecf->edf", grad_grouped, owner_act_grouped, preferred_element_type=jnp.float32
    )
    expert_grad = jnp.concatenate([front, back], axis=2)
    grad_rows = lax.all_to_all(
        grad_owner_rows.reshape(shard_count * local_experts, capacity, model_width),
        "wt",
        split_axis=0,
        concat_axis=0,
        tiled=True,
    )
    grad_normed_mid = (
        grad_normed_mid
        + jnp.zeros((token_rows + 1, model_width), jnp.float32)
        .at[slot_table]
        .add(grad_rows.astype(jnp.float32))[:token_rows]
    )
    grad_gain_mid_local = jnp.sum(grad_normed_mid * scaled_mid, axis=0)
    grad_middle = grad_final + norm_back(grad_normed_mid, scaled_mid, inverse_mid, gain_mid_float)
    grad_branch = grad_middle.astype(jnp.bfloat16)
    mixed_gradient = lax.dot_general(
        grad_branch, full_out, contract_last, preferred_element_type=jnp.float32
    ).astype(jnp.bfloat16)
    grad_out_local = lax.dot_general(
        mixed_rows, grad_branch, contract_first, preferred_element_type=jnp.float32
    )
    context_recomputed = lax.all_gather(context_local, "ctx", axis=0, tiled=True)
    backward_keys = context_recomputed[:, :key_value_width].reshape(
        number_of_blocks, key_row_count, KEY_VALUE_HEADS, HEAD_SIZE
    )
    backward_values = context_recomputed[:, key_value_width:].reshape(
        number_of_blocks, key_row_count, KEY_VALUE_HEADS, HEAD_SIZE
    )
    attention_output_gradient = mixed_gradient.reshape(
        token_rows, KEY_VALUE_HEADS, query_groups, HEAD_SIZE
    )
    grad_queries, grad_keys, grad_values = attend_backward(
        query_rows,
        backward_keys,
        backward_values,
        place_blocks,
        query_place,
        log_total,
        attention_output_gradient,
        attention_output,
        score_scale,
    )
    grad_context_all = jnp.concatenate(
        [
            grad_keys.reshape(seq_rows, key_value_width),
            grad_values.reshape(seq_rows, key_value_width),
        ],
        axis=1,
    )
    grad_context = lax.psum_scatter(
        grad_context_all.astype(jnp.bfloat16), "ctx", scatter_dimension=0, tiled=True
    ).astype(jnp.float32)
    grad_projected = jnp.concatenate(
        [grad_queries.reshape(token_rows, query_total_width), grad_context], axis=1
    ).astype(jnp.bfloat16)
    grad_normed_in = lax.dot_general(
        grad_projected, full_qkv, contract_last, preferred_element_type=jnp.float32
    )
    grad_qkv_local = lax.dot_general(
        normed_in, grad_projected, contract_first, preferred_element_type=jnp.float32
    )
    grad_gain_in_local = jnp.sum(grad_normed_in * scaled_in, axis=0)
    grad_inputs = grad_middle + norm_back(grad_normed_in, scaled_in, inverse_in, gain_in_float)
    weight_sums = (
        lax.psum_scatter(
            grad_gain_in_local.astype(jnp.bfloat16), "wt", scatter_dimension=0, tiled=True
        ).astype(jnp.float32),
        lax.psum_scatter(
            grad_qkv_local.astype(jnp.bfloat16), "wt", scatter_dimension=0, tiled=True
        ).astype(jnp.float32),
        lax.psum_scatter(
            grad_out_local.astype(jnp.bfloat16), "wt", scatter_dimension=0, tiled=True
        ).astype(jnp.float32),
        lax.psum_scatter(
            grad_gain_mid_local.astype(jnp.bfloat16), "wt", scatter_dimension=0, tiled=True
        ).astype(jnp.float32),
        lax.psum_scatter(
            grad_shared_full.astype(jnp.bfloat16), "wt", scatter_dimension=0, tiled=True
        ).astype(jnp.float32),
    )
    summed = (
        lax.psum(weight_sums[0].astype(jnp.bfloat16), "ctx").astype(jnp.float32),
        lax.psum(weight_sums[1].astype(jnp.bfloat16), "ctx").astype(jnp.float32),
        lax.psum(weight_sums[2].astype(jnp.bfloat16), "ctx").astype(jnp.float32),
        lax.psum(weight_sums[3].astype(jnp.bfloat16), "ctx").astype(jnp.float32),
        lax.psum(weight_sums[4].astype(jnp.bfloat16), "ctx").astype(jnp.float32),
        lax.psum(expert_grad.astype(jnp.bfloat16), "ctx").astype(jnp.float32),
    )
    return (
        final_state.astype(jnp.bfloat16)[None],
        loss_value,
        grad_inputs[None],
        summed[0],
        summed[1],
        summed[2],
        summed[3],
        summed[4],
        summed[5],
    )


PLANE = [[0, 2, 4, 6], [1, 3, 5, 7]]
COSTS = {
    "project": 0.3,
    "attend": 0.3,
    "leave": 0.3,
    "join_shared": 0.3,
    "experts": 0.3,
    "experts_back": 0.3,
    "enter_back": 0.3,
    "attend_back": 0.3,
    "finish": 0.3,
    "weight_grad": 0.3,
    "expert_grad": 0.3,
    "blend_split": 0.3,
    "blend_pair": 0.3,
    "blend_sum": 0.3,
    "blend_stack": 0.3,
    "blend_four": 0.3,
    "place_pair": 0.3,
    "place_shared": 0.3,
    "place_heads": 0.3,
}


def flip(value, bit):
    return lax.ppermute(value, "ctx", [(index, index ^ bit) for index in range(8)])


def line_swap(value, offset):
    return lax.ppermute(value, "wt", [(index, index ^ offset) for index in range(4)])


def line_middle(value):
    return lax.ppermute(value, "wt", [(1, 2), (2, 1)])


def line_outward(value):
    return lax.ppermute(value, "wt", [(1, 0), (2, 3)])


def line_inward(value):
    return lax.ppermute(value, "wt", [(0, 1), (3, 2)])


def line_gather(value, at_end):
    near = line_swap(value, 1)
    middle = line_middle(value)
    middle_far = line_middle(near)
    outward = line_outward(middle)
    outward_far = line_outward(middle_far)
    return [
        value,
        near,
        jnp.where(at_end, outward, middle_far),
        jnp.where(at_end, outward_far, middle),
    ]


def line_reduce(parts):
    far = line_inward(parts[3])
    carried = parts[2] + far
    inward = line_inward(carried)
    crossed = line_middle(carried)
    near = line_swap(parts[1] + crossed, 1)
    middle = line_middle(parts[3] + inward)
    return (
        parts[0].astype(jnp.float32) + near.astype(jnp.float32) + middle.astype(jnp.float32)
    )


def chips_exchange(blocks):
    return lax.all_to_all(
        blocks,
        "ctx",
        split_axis=0,
        concat_axis=0,
        tiled=True,
        axis_index_groups=PLANE,
    )


def line_exchange(blocks):
    return lax.all_to_all(blocks, "wt", split_axis=0, concat_axis=0, tiled=True)


def chips_gather(value, x_last):
    along_x = flip(value, 2)
    along_y = flip(value, 4)
    corner = flip(along_y, 2) if x_last else flip(along_x, 4)
    return [value, along_x, along_y, corner]


def core_swap(values):
    return [flip(value, 1) for value in values]


def everywhere_sum(value):
    for bit in (1, 2, 4):
        value = value + flip(value, bit)
    for offset in (1, 2):
        value = value + line_swap(value, offset)
    return value


def pick(blocks, index):
    return lax.dynamic_index_in_dim(blocks, index, 0, keepdims=False)


def chips_reduce(keep, came):
    half = keep.shape[1] // 2
    upper = keep[:, :half] + came[:, :half]
    lower = keep[:, half:] + came[:, half:]
    upper_came = flip(upper[1::2], 2)
    lower_came = flip(lower[2:], 4)
    upper = upper[0::2] + upper_came
    lower = lower[:2] + lower_came
    upper_came = flip(upper[1], 4)
    lower_came = flip(lower[1], 2)
    return jnp.concatenate([upper[0] + upper_came, lower[0] + lower_came], axis=0)


def dot_plain(left, right):
    return lax.dot_general(
        left, right, (((1,), (0,)), ((), ())), preferred_element_type=jnp.float32
    )


def dot_last(left, right):
    return lax.dot_general(
        left, right, (((1,), (1,)), ((), ())), preferred_element_type=jnp.float32
    )


def dot_first(left, right):
    return lax.dot_general(
        left, right, (((0,), (0,)), ((), ())), preferred_element_type=jnp.float32
    )


def call(kernel, name, meta, arrays, grid, in_specs, out_specs, out_shape, scratch, flops, moved):
    return pl.pallas_call(
        kernel,
        grid_spec=pltpu.PrefetchScalarGridSpec(
            num_scalar_prefetch=1,
            grid=grid,
            in_specs=in_specs,
            out_specs=out_specs,
            scratch_shapes=scratch,
        ),
        out_shape=out_shape,
        compiler_params=pltpu.CompilerParams(vmem_limit_bytes=48 * 1024 * 1024),
        cost_estimate=pl.CostEstimate(
            flops=int(COSTS.get(name, 1.0) * 1e9), bytes_accessed=1000, transcendentals=0
        ),
        name=name,
    )(meta, *arrays)


def whole(array):
    rank = len(array.shape)
    return pl.BlockSpec(tuple(array.shape), lambda *_: (0,) * rank)


def shape_of(shape, dtype):
    return jax.ShapeDtypeStruct(shape, dtype)


def size_of(arrays):
    return sum(math.prod(a.shape) * a.dtype.itemsize for a in arrays)


def blend(meta, name, function, arrays, pieces=4):
    rows = arrays[0].shape[-2]
    tile = rows // pieces
    outs = jax.eval_shape(function, *[shape_of(a.shape, a.dtype) for a in arrays])
    many = isinstance(outs, (list, tuple))
    outs = list(outs) if many else [outs]

    def spec(a):
        rank = len(a.shape)
        lead = a.shape[:-2]
        return pl.BlockSpec(
            tuple(lead) + (tile, a.shape[-1]),
            lambda i, m: (0,) * (rank - 2) + (i, 0),
        )

    def kernel(meta_ref, *refs):
        result = function(*[ref[...] for ref in refs[: len(arrays)]])
        result = list(result) if many else [result]
        for ref, value in zip(refs[len(arrays) :], result):
            ref[...] = value

    result = call(
        kernel,
        name,
        meta,
        arrays,
        (pieces,),
        [spec(a) for a in arrays],
        [spec(a) for a in outs],
        outs,
        [],
        0,
        0,
    )
    return result if many else result[0]


def aligned(value, step):
    return pl.multiple_of(value * step, step)


def project_kernel(meta, blocks_ref, gain_ref, mine, other, *refs):
    normed_ref, query_ref, pair_ref, weight_ref = refs
    core = meta[0] & 1
    rows = mine.shape[1]

    @pl.when(pl.program_id(0) == 0)
    def _():
        for i in range(4):
            at = 2 * (meta[1] ^ i)
            weight_ref[pl.ds(aligned(at + core, rows), rows), :] = mine[i]
            weight_ref[pl.ds(aligned(at + 1 - core, rows), rows), :] = other[i]

    states = blocks_ref[0].astype(jnp.float32)
    inverse = lax.rsqrt(jnp.mean(states * states, axis=-1, keepdims=True) + norm_eps)
    normed = (states * inverse * gain_ref[...]).astype(jnp.bfloat16)
    normed_ref[0] = normed
    projected = dot_plain(normed, weight_ref[...]).astype(jnp.bfloat16)
    query_width = query_ref.shape[-1]
    query_ref[0] = projected[:, :query_width]
    pair_ref[0] = projected[:, query_width:]


def project(meta, blocks, gain, mine, other, query_width):
    _, token_rows, width = blocks.shape
    columns = mine.shape[2]
    arrays = [blocks, gain, mine, other]
    outs = [
        shape_of((4, token_rows, width), jnp.bfloat16),
        shape_of((4, token_rows, query_width), jnp.bfloat16),
        shape_of((4, token_rows, columns - query_width), jnp.bfloat16),
        shape_of((width, columns), jnp.bfloat16),
    ]
    return call(
        project_kernel,
        "project",
        meta,
        arrays,
        (4,),
        [pl.BlockSpec((1, token_rows, width), lambda r, m: (r, 0, 0))]
        + [whole(a) for a in arrays[1:]],
        [
            pl.BlockSpec((1, token_rows, width), lambda r, m: (r, 0, 0)),
            pl.BlockSpec((1, token_rows, query_width), lambda r, m: (r, 0, 0)),
            pl.BlockSpec((1, token_rows, columns - query_width), lambda r, m: (r, 0, 0)),
            whole(outs[3]),
        ],
        outs,
        [],
        2 * 4 * token_rows * width * columns,
        size_of(arrays) + size_of(outs),
    )


def sort_pairs(meta, mine_ref, other_ref, keys, values):
    half = mine_ref.shape[1] // 2
    for slot in range(16):
        block, part = (slot, 0) if slot < 8 else (15 - slot, 1)
        place = block >> 1
        rows = pl.ds(part * half, half)
        to = pl.ds(slot * half, half)

        @pl.when((meta[0] & 1) == (block & 1))
        def _():
            keys[to, :] = mine_ref[place, rows, :HEAD_SIZE]
            values[to, :] = mine_ref[place, rows, HEAD_SIZE:]

        @pl.when((meta[0] & 1) != (block & 1))
        def _():
            keys[to, :] = other_ref[place, rows, :HEAD_SIZE]
            values[to, :] = other_ref[place, rows, HEAD_SIZE:]


def stack_heads(rows):
    count = rows.shape[1] // HEAD_SIZE
    return jnp.concatenate(
        [rows[:, h * HEAD_SIZE : (h + 1) * HEAD_SIZE] for h in range(count)], axis=0
    )


def unstack_heads(rows, count):
    each = rows.shape[0] // count
    return jnp.concatenate([rows[h * each : (h + 1) * each] for h in range(count)], axis=1)


def step_slot(meta):
    step = pl.program_id(0)
    block = 2 * (step >> 1) + (meta[0] & 1)
    return jnp.where((step & 1) == 0, block, 15 - block)


def allowed_pairs(start, slot, shape, half):
    key_place = start + lax.broadcasted_iota(jnp.int32, shape, 0)
    query_place = slot * half + (lax.broadcasted_iota(jnp.int32, shape, 1) & (half - 1))
    return key_place <= query_place


def key_spans(step, half, span):
    pairs = (step // 2 if step % 2 == 0 else 7 - step // 2) + 1
    rows = pairs * 2 * half
    return [(at, min(span, rows - at)) for at in range(0, rows, span)]


def attend_kernel(scale, span, meta, query_ref, mine_ref, other_ref, *refs):
    out_ref, log_ref, keys, values, values_turned = refs
    half, group_width = query_ref.shape[1:]
    count = group_width // HEAD_SIZE

    @pl.when(pl.program_id(0) == 0)
    def _():
        sort_pairs(meta, mine_ref, other_ref, keys, values)
        values_turned[...] = values[...].T

    slot = step_slot(meta)
    query = stack_heads(query_ref[0])
    wide = count * half

    def run(spans):
        highest = jnp.full((1, wide), masked_score, jnp.float32)
        total = jnp.zeros((1, wide), jnp.float32)
        mixed = jnp.zeros((HEAD_SIZE, wide), jnp.float32)
        for start, size in spans:
            at = pl.ds(start, size)
            scores = dot_last(keys[at, :], query) * scale
            if start == spans[-1][0]:
                seen = allowed_pairs(start, slot, scores.shape, half)
                scores = jnp.where(seen, scores, masked_score)
            new = jnp.maximum(highest, jnp.max(scores, axis=0, keepdims=True))
            rescale = jnp.exp(highest - new)
            powers = jnp.exp(scores - new)
            total = total * rescale + jnp.sum(powers, axis=0, keepdims=True)
            mixed = mixed * rescale + dot_plain(
                values_turned[:, at], powers.astype(jnp.bfloat16)
            )
            highest = new
        log_ref[0] = highest + jnp.log(total)
        out_ref[0] = unstack_heads((mixed / total).T, count).astype(jnp.bfloat16)

    for step in range(8):

        @pl.when(pl.program_id(0) == step)
        def _():
            run(key_spans(step, half, span))


def attend(meta, query, mine, other, scale):
    token_rows, group_width = query.shape[1:]
    half = token_rows // 2
    count = group_width // HEAD_SIZE
    everything = 8 * token_rows
    span = 1024
    arrays = [query, mine, other]
    outs = [
        shape_of(query.shape, jnp.bfloat16),
        shape_of((8, 1, count * half), jnp.float32),
    ]
    return call(
        functools.partial(attend_kernel, scale, span),
        "attend",
        meta,
        arrays,
        (8,),
        [
            pl.BlockSpec((1, half, group_width), lambda i, m: (i // 2, i % 2, 0)),
            whole(mine),
            whole(other),
        ],
        [
            pl.BlockSpec((1, half, group_width), lambda i, m: (i // 2, i % 2, 0)),
            pl.BlockSpec((1, 1, count * half), lambda i, m: (i, 0, 0)),
        ],
        outs,
        [
            pltpu.VMEM((everything, HEAD_SIZE), jnp.bfloat16),
            pltpu.VMEM((everything, HEAD_SIZE), jnp.bfloat16),
            pltpu.VMEM((HEAD_SIZE, everything), jnp.bfloat16),
        ],
        2 * 2 * 4 * token_rows * everything * group_width,
        size_of(arrays) + size_of(outs),
    )


def attend_back_kernel(scale, span, meta, query_ref, mine_ref, other_ref, log_ref, *refs):
    mixed_ref, grad_ref, grad_query_ref, grad_mine_ref, grad_other_ref = refs[:5]
    keys, values, keys_turned, grad_keys, grad_values = refs[5:]
    step = pl.program_id(0)
    half, group_width = query_ref.shape[1:]
    count = group_width // HEAD_SIZE

    @pl.when(step == 0)
    def _():
        sort_pairs(meta, mine_ref, other_ref, keys, values)
        keys_turned[...] = keys[...].T
        grad_keys[...] = jnp.zeros_like(grad_keys)
        grad_values[...] = jnp.zeros_like(grad_values)

    slot = step_slot(meta)
    query = stack_heads(query_ref[0])
    mixed = stack_heads(mixed_ref[0]).astype(jnp.float32)
    grad = stack_heads(grad_ref[0])
    delta = jnp.sum((mixed * grad.astype(jnp.float32)).T, axis=0, keepdims=True)
    log_total = log_ref[0]

    def run(spans):
        grad_turned = jnp.zeros((HEAD_SIZE, count * half), jnp.float32)
        for start, size in spans:
            at = pl.ds(start, size)
            scores = dot_last(keys[at, :], query) * scale
            probs = jnp.exp(scores - log_total)
            if start == spans[-1][0]:
                probs = jnp.where(allowed_pairs(start, slot, probs.shape, half), probs, 0.0)
            grad_probs = dot_last(values[at, :], grad)
            grad_scores = (probs * (grad_probs - delta)).astype(jnp.bfloat16)
            grad_values[at, :] += dot_plain(probs.astype(jnp.bfloat16), grad)
            grad_keys[at, :] += dot_plain(grad_scores, query)
            grad_turned += dot_plain(keys_turned[:, at], grad_scores)
        grad_query_ref[0] = unstack_heads((grad_turned * scale).T, count).astype(jnp.bfloat16)

    for at_step in range(8):

        @pl.when(step == at_step)
        def _():
            run(key_spans(at_step, half, span))

    @pl.when(step == 7)
    def _():
        for slot_at in range(16):
            block, part = (slot_at, 0) if slot_at < 8 else (15 - slot_at, 1)
            place = block >> 1
            rows = pl.ds(part * half, half)
            here = pl.ds(slot_at * half, half)
            both = jnp.concatenate([grad_keys[here, :] * scale, grad_values[here, :]], axis=1)

            @pl.when((meta[0] & 1) == (block & 1))
            def _():
                grad_mine_ref[place, rows, :] = both

            @pl.when((meta[0] & 1) != (block & 1))
            def _():
                grad_other_ref[place, rows, :] = both.astype(jnp.bfloat16)


def attend_back(meta, query, mine, other, log_total, mixed, grad, scale):
    token_rows, group_width = query.shape[1:]
    half = token_rows // 2
    count = group_width // HEAD_SIZE
    everything = 8 * token_rows
    span = 512
    arrays = [query, mine, other, log_total, mixed, grad]
    outs = [
        shape_of(query.shape, jnp.bfloat16),
        shape_of(mine.shape, jnp.float32),
        shape_of(mine.shape, jnp.bfloat16),
    ]
    return call(
        functools.partial(attend_back_kernel, scale, span),
        "attend_back",
        meta,
        arrays,
        (8,),
        [
            pl.BlockSpec((1, half, group_width), lambda i, m: (i // 2, i % 2, 0)),
            whole(mine),
            whole(other),
            pl.BlockSpec((1, 1, count * half), lambda i, m: (i, 0, 0)),
            pl.BlockSpec((1, half, group_width), lambda i, m: (i // 2, i % 2, 0)),
            pl.BlockSpec((1, half, group_width), lambda i, m: (i // 2, i % 2, 0)),
        ],
        [
            pl.BlockSpec((1, half, group_width), lambda i, m: (i // 2, i % 2, 0)),
            whole(outs[1]),
            whole(outs[2]),
        ],
        outs,
        [
            pltpu.VMEM((everything, HEAD_SIZE), jnp.bfloat16),
            pltpu.VMEM((everything, HEAD_SIZE), jnp.bfloat16),
            pltpu.VMEM((HEAD_SIZE, everything), jnp.bfloat16),
            pltpu.VMEM((everything, HEAD_SIZE), jnp.float32),
            pltpu.VMEM((everything, HEAD_SIZE), jnp.float32),
        ],
        5 * 2 * 4 * token_rows * everything * group_width,
        size_of(arrays) + size_of(outs),
    )


def leave_kernel(meta, *refs):
    parts, mine, other, states_ref, gain_ref = refs[:4], *refs[4:8]
    weight_ref, middle_ref, normed_ref = refs[8:]
    core, chip = meta[0] & 1, meta[0] >> 1
    rows = mine.shape[1]
    for i in range(4):
        weight_ref[pl.ds(aligned(2 * i + core, rows), rows), :] = mine[i]
        weight_ref[pl.ds(aligned(2 * i + 1 - core, rows), rows), :] = other[i]
    middle = states_ref[...].astype(jnp.float32)
    for r in range(4):
        at = pl.ds(aligned(chip ^ r, 2 * rows), 2 * rows)
        middle += dot_plain(parts[r][...], weight_ref[at, :])
    middle_ref[...] = middle
    inverse = lax.rsqrt(jnp.mean(middle * middle, axis=-1, keepdims=True) + norm_eps)
    normed_ref[...] = (middle * inverse * gain_ref[...]).astype(jnp.bfloat16)


def leave(meta, parts, mine, other, states, gain):
    token_rows, width = states.shape
    arrays = list(parts) + [mine, other, states, gain]
    outs = [
        shape_of((8 * mine.shape[1], width), jnp.bfloat16),
        shape_of((token_rows, width), jnp.float32),
        shape_of((token_rows, width), jnp.bfloat16),
    ]
    return call(
        leave_kernel,
        "leave",
        meta,
        arrays,
        (1,),
        [whole(a) for a in arrays],
        [whole(a) for a in outs],
        outs,
        [],
        2 * token_rows * width * width,
        size_of(arrays) + size_of(outs),
    )


def norm_back_rows(grad_normed, states, gain):
    inverse = lax.rsqrt(jnp.mean(states * states, axis=-1, keepdims=True) + norm_eps)
    scaled = states * inverse
    gain_grad = jnp.sum(grad_normed * scaled, axis=0, keepdims=True)
    grad_scaled = grad_normed * gain
    shift = jnp.mean(grad_scaled * scaled, axis=-1, keepdims=True)
    return inverse * (grad_scaled - scaled * shift), gain_grad


def enter_back_kernel(meta, final_ref, normed_ref, middle_ref, gain_ref, weight_ref, *refs):
    grad_ref, branch_ref, gain_grad_ref, mixed_ref = refs
    grad, gain_grad = norm_back_rows(normed_ref[...], middle_ref[...], gain_ref[...])
    grad = grad + final_ref[...]
    grad_ref[...] = grad
    gain_grad_ref[...] = gain_grad
    branch = grad.astype(jnp.bfloat16)
    branch_ref[...] = branch
    rows = weight_ref.shape[0] // 4
    for r in range(4):
        mixed_ref[r] = dot_last(branch, weight_ref[rows * r : rows * (r + 1), :]).astype(
            jnp.bfloat16
        )


def enter_back(meta, grad_final, grad_normed, middle, gain, weight):
    token_rows, width = middle.shape
    arrays = [grad_final, grad_normed, middle, gain, weight]
    outs = [
        shape_of((token_rows, width), jnp.float32),
        shape_of((token_rows, width), jnp.bfloat16),
        shape_of((1, width), jnp.float32),
        shape_of((4, token_rows, weight.shape[0] // 4), jnp.bfloat16),
    ]
    return call(
        enter_back_kernel,
        "enter_back",
        meta,
        arrays,
        (1,),
        [whole(a) for a in arrays],
        [whole(a) for a in outs],
        outs,
        [],
        2 * token_rows * width * width,
        size_of(arrays) + size_of(outs),
    )


def finish_kernel(meta, *refs):
    parts, mine, other = refs[:3]
    states_ref, middle_ref, gain_ref, grad_ref, gain_grad_ref, total = refs[3:]
    core, chip = meta[0] & 1, meta[0] >> 1
    columns = mine.shape[1]
    for at, weights in ((core, mine), (1 - core, other)):
        total[:, pl.ds(aligned(at, columns), columns)] = sum(
            dot_last(parts[r], weights[chip ^ r]) for r in range(4)
        )
    grad, gain_grad = norm_back_rows(
        total[...], states_ref[...].astype(jnp.float32), gain_ref[...]
    )
    grad_ref[0] = grad + middle_ref[...]
    gain_grad_ref[...] = gain_grad


def finish(meta, parts, mine, other, states, grad_middle, gain):
    token_rows, width = states.shape
    arrays = [parts, mine, other, states, grad_middle, gain]
    outs = [
        shape_of((1, token_rows, width), jnp.float32),
        shape_of((1, width), jnp.float32),
    ]
    return call(
        finish_kernel,
        "finish",
        meta,
        arrays,
        (1,),
        [whole(a) for a in arrays],
        [whole(a) for a in outs],
        outs,
        [pltpu.VMEM((token_rows, width), jnp.float32)],
        2 * token_rows * width * 4 * parts.shape[2],
        size_of(arrays) + size_of(outs),
    )


def gated(gate_up, units):
    gate_part = gate_up[:, :units]
    sigma = 1.0 / (1.0 + jnp.exp(-gate_part))
    return gate_part * sigma * gate_up[:, units:]


def gated_back(grad_act, gate_up, units):
    gate_part = gate_up[:, :units].astype(jnp.float32)
    up_part = gate_up[:, units:].astype(jnp.float32)
    sigma = 1.0 / (1.0 + jnp.exp(-gate_part))
    linear = gate_part * sigma
    grad_gate = grad_act * up_part * (sigma * (1.0 + gate_part * (1.0 - sigma)))
    return grad_gate, grad_act * linear, linear * up_part


def experts_kernel(
    meta, rows_ref, gates_ref, expert_ref, shared_ref, gate_up_ref, shared_gate_up_ref, out_ref, total
):
    expert = pl.program_id(0)
    rows = rows_ref[...]

    @pl.when(expert == 0)
    def _():
        units = shared_ref.shape[1] // 3
        gate_up = dot_plain(rows, shared_ref[:, : 2 * units])
        shared_gate_up_ref[...] = gate_up.astype(jnp.bfloat16)
        act = gated(gate_up, units).astype(jnp.bfloat16)
        total[...] = dot_last(act, shared_ref[:, 2 * units :])

    gate_up = dot_plain(rows, expert_ref[0, :, : 2 * F])
    gate_up_ref[0] = gate_up.astype(jnp.bfloat16)
    act = (gated(gate_up, F) * gates_ref[0]).astype(jnp.bfloat16)
    total[...] += dot_last(act, expert_ref[0, :, 2 * F :])

    @pl.when(expert == pl.num_programs(0) - 1)
    def _():
        out_ref[...] = total[...].astype(jnp.bfloat16)


def experts(meta, rows, gates, expert_weight, shared_slice):
    local_experts, width, _ = expert_weight.shape
    token_rows = rows.shape[0]
    shared_units = shared_slice.shape[1] // 3
    arrays = [rows, gates, expert_weight, shared_slice]
    outs = [
        shape_of((local_experts, token_rows, 2 * F), jnp.bfloat16),
        shape_of((token_rows, 2 * shared_units), jnp.bfloat16),
        shape_of((token_rows, width), jnp.bfloat16),
    ]
    return call(
        experts_kernel,
        "experts",
        meta,
        arrays,
        (local_experts,),
        [
            whole(rows),
            pl.BlockSpec((1, token_rows, 1), lambda e, m: (e, 0, 0)),
            pl.BlockSpec((1, width, 3 * F), lambda e, m: (e, 0, 0)),
            whole(shared_slice),
        ],
        [
            pl.BlockSpec((1, token_rows, 2 * F), lambda e, m: (e, 0, 0)),
            whole(outs[1]),
            whole(outs[2]),
        ],
        outs,
        [pltpu.VMEM((token_rows, width), jnp.float32)],
        2 * token_rows * width * 3 * (F * local_experts + shared_units),
        size_of(arrays) + size_of(outs),
    )


def experts_back_kernel(
    meta,
    grad_ref,
    gates_ref,
    gate_up_ref,
    shared_gate_up_ref,
    expert_ref,
    shared_ref,
    grad_gate_up_ref,
    act_ref,
    shared_grad_ref,
    shared_act_ref,
    grad_rows_ref,
    total,
):
    expert = pl.program_id(0)
    grad = grad_ref[...]

    @pl.when(expert == 0)
    def _():
        units = shared_ref.shape[1] // 3
        grad_act = dot_plain(grad, shared_ref[:, 2 * units :])
        grad_gate, grad_up, act = gated_back(grad_act, shared_gate_up_ref[...], units)
        both = jnp.concatenate([grad_gate, grad_up], axis=1).astype(jnp.bfloat16)
        shared_grad_ref[0] = both
        shared_act_ref[0] = act.astype(jnp.bfloat16)
        total[...] = dot_last(both, shared_ref[:, : 2 * units])

    grad_act = dot_plain(grad, expert_ref[0, :, 2 * F :]) * gates_ref[0]
    grad_gate, grad_up, act = gated_back(grad_act, gate_up_ref[0], F)
    both = jnp.concatenate([grad_gate, grad_up], axis=1).astype(jnp.bfloat16)
    grad_gate_up_ref[0] = both
    act_ref[0] = (act * gates_ref[0]).astype(jnp.bfloat16)
    total[...] += dot_last(both, expert_ref[0, :, : 2 * F])

    @pl.when(expert == pl.num_programs(0) - 1)
    def _():
        grad_rows_ref[...] = total[...].astype(jnp.bfloat16)


def experts_back(meta, grad, gates, gate_up, shared_gate_up, expert_weight, shared_slice):
    local_experts, width, _ = expert_weight.shape
    token_rows = grad.shape[0]
    shared_units = shared_slice.shape[1] // 3
    arrays = [grad, gates, gate_up, shared_gate_up, expert_weight, shared_slice]
    outs = [
        shape_of((local_experts, token_rows, 2 * F), jnp.bfloat16),
        shape_of((local_experts, token_rows, F), jnp.bfloat16),
        shape_of((1, token_rows, 2 * shared_units), jnp.bfloat16),
        shape_of((1, token_rows, shared_units), jnp.bfloat16),
        shape_of((token_rows, width), jnp.bfloat16),
    ]
    return call(
        experts_back_kernel,
        "experts_back",
        meta,
        arrays,
        (local_experts,),
        [
            whole(grad),
            pl.BlockSpec((1, token_rows, 1), lambda e, m: (e, 0, 0)),
            pl.BlockSpec((1, token_rows, 2 * F), lambda e, m: (e, 0, 0)),
            whole(shared_gate_up),
            pl.BlockSpec((1, width, 3 * F), lambda e, m: (e, 0, 0)),
            whole(shared_slice),
        ],
        [
            pl.BlockSpec((1, token_rows, 2 * F), lambda e, m: (e, 0, 0)),
            pl.BlockSpec((1, token_rows, F), lambda e, m: (e, 0, 0)),
            whole(outs[2]),
            whole(outs[3]),
            whole(outs[4]),
        ],
        outs,
        [pltpu.VMEM((token_rows, width), jnp.float32)],
        2 * token_rows * width * 3 * (F * local_experts + shared_units),
        size_of(arrays) + size_of(outs),
    )


def weight_grad_kernel(pairs, core_at, meta, *refs):
    keep_ref, give_ref = refs[-2:]
    at = 0
    columns = 0
    parts = []
    for count in pairs:
        lefts, rights = refs[at : at + count], refs[at + count : at + 2 * count]
        at += 2 * count
        parts.append(
            sum(dot_first(a[...], b[0]) for a, b in zip(lefts, rights)).astype(jnp.bfloat16)
        )
    half = keep_ref.shape[1]

    for core, (first, second) in ((0, (keep_ref, give_ref)), (1, (give_ref, keep_ref))):

        @pl.when((meta[core_at] & 1) == core)
        def _():
            start = 0
            for part in parts:
                stop = start + part.shape[1]
                first[0, :, start:stop] = part[:half]
                second[0, :, start:stop] = part[half:]
                start = stop


def expert_grad_kernel(count, meta, *refs):
    rows, grads, front, acts = (refs[i * count : (i + 1) * count] for i in range(4))
    out_ref = refs[-1] if len(refs) == 4 * count + 1 else refs[-2]
    tile = rows[0].shape[1]
    both = 3 * F

    def pair(front_refs, act_refs):
        return [
            sum(dot_first(a[...], b[0]) for a, b in zip(left, right)).astype(jnp.bfloat16)
            for left, right in ((rows, front_refs), (grads, act_refs))
        ]

    left, right = pair(front, acts)
    out_ref[0, :tile, : left.shape[1]] = left
    out_ref[0, :tile, left.shape[1] : both] = right
    if len(refs) > 4 * count + 1:
        held = refs[-1]
        left, right = pair(refs[4 * count : 5 * count], refs[5 * count : 6 * count])
        split, columns = left.shape[1], left.shape[1] + right.shape[1]
        held[:, :split] = left
        held[:, split:] = right
        quarter = tile // 4
        first = 2 * meta[2]
        out_ref[0, tile:, :columns] = held[pl.ds(aligned(first, quarter), quarter), :]
        out_ref[0, tile:, columns:] = held[pl.ds(aligned(first + 1, quarter), quarter), :]


def expert_grad(meta, expert, half, rows, grads, front, acts, shared=None):
    count = len(rows)
    token_rows, width = rows[0].shape
    tile = width // 4
    arrays = list(rows) + list(grads) + list(front) + list(acts)
    column = pl.BlockSpec((token_rows, tile), lambda i, m: (0, i ^ m[0]))

    def of_expert(a):
        return pl.BlockSpec((1,) + a.shape[1:], lambda i, m: (m[1], 0, 0))

    in_specs = [column] * (2 * count) + [of_expert(a) for a in arrays[2 * count :]]
    below, scratch = 0, []
    if shared is not None:
        arrays += list(shared[0]) + list(shared[1])
        in_specs += [whole(a) for a in arrays[4 * count :]]
        below = tile // 4
        columns = shared[0][0].shape[-1] + shared[1][0].shape[-1]
        scratch = [pltpu.VMEM((tile, columns), jnp.bfloat16)]
    return call(
        functools.partial(expert_grad_kernel, count),
        "expert_grad",
        jnp.stack([meta[0] >> 1, expert, half]),
        arrays,
        (4,),
        in_specs,
        pl.BlockSpec((1, tile + below, 3 * F), lambda i, m: (i, 0, 0)),
        shape_of((4, tile + below, 3 * F), jnp.bfloat16),
        scratch,
        0,
        0,
    )


def weight_grad(meta, order, operands, index):
    token_rows, width = operands[0][0][0].shape
    tile = width // 4
    scalars = jnp.stack([order, meta[0]])
    arrays, in_specs, columns = [], [], 0
    for lefts, rights in operands:
        arrays += list(lefts) + list(rights)
        in_specs += [pl.BlockSpec((token_rows, tile), lambda i, m: (0, i ^ m[0]))] * len(lefts)
        units = rights[0].shape[-1]
        at = index if rights[0].shape[0] > 1 else 0
        in_specs += [
            pl.BlockSpec((1, token_rows, units), lambda i, m, at=at: (at, 0, 0))
        ] * len(rights)
        columns += units
    tokens = token_rows * len(operands[0][0])
    counts = [len(left) for left, _ in operands]
    outs = [shape_of((4, tile // 2, columns), jnp.bfloat16)] * 2
    return call(
        functools.partial(weight_grad_kernel, counts, 1),
        "weight_grad",
        scalars,
        arrays,
        (4,),
        in_specs,
        [pl.BlockSpec((1, tile // 2, columns), lambda i, m: (i, 0, 0))] * 2,
        outs,
        [],
        2 * tokens * width * columns,
        size_of(outs) + 4 * tokens * width + 2 * tokens * columns,
    )


def place_pair_kernel(meta, *refs):
    mine, other, out_ref = refs[-3:]
    rows = out_ref.shape[1]

    @pl.when(pl.program_id(0) == 0)
    def _():
        out_ref[0] = mine[0, :rows].astype(jnp.float32)

    @pl.when(pl.program_id(0) == 1)
    def _():
        out_ref[0] = other[0, :rows].astype(jnp.float32)


def place_pair(meta, total, index, shape, mine, other):
    _, rows, columns = mine.shape
    arrays = [mine, other]
    in_specs = [
        pl.BlockSpec((1, rows, columns), lambda k, r, m: ((1 - k) * r + 3 * k, 0, 0)),
        pl.BlockSpec((1, rows, columns), lambda k, r, m: (k * r, 0, 0)),
    ]
    aliases = {}
    if total is not None:
        arrays = [total] + arrays
        in_specs = [pl.BlockSpec(memory_space=pl.ANY)] + in_specs
        aliases = {1: 0}
    return pl.pallas_call(
        place_pair_kernel,
        grid_spec=pltpu.PrefetchScalarGridSpec(
            num_scalar_prefetch=1,
            grid=(2, 4),
            in_specs=in_specs,
            out_specs=pl.BlockSpec(
                (1, shape[1] // 4, shape[2]),
                lambda k, r, m: (2 * ((m[0] & 1) ^ k) + index, (m[0] >> 1) ^ r, 0),
            ),
        ),
        out_shape=shape_of(shape, jnp.float32),
        input_output_aliases=aliases,
        compiler_params=pltpu.CompilerParams(vmem_limit_bytes=48 * 1024 * 1024),
        cost_estimate=pl.CostEstimate(
            flops=int(COSTS.get("place_pair", 1.0) * 1e9), bytes_accessed=1000, transcendentals=0
        ),
        name="place_pair",
    )(meta, *arrays)


def place_shared_kernel(meta, mine_low, mine_high, other_low, other_high, out_ref):
    core = meta[0] & 1
    rows = mine_low.shape[1]
    for at, low, high in ((core, mine_low, mine_high), (1 - core, other_low, other_high)):
        out_ref[pl.ds(aligned(2 * at, rows), rows), :] = low[0].astype(jnp.float32)
        out_ref[pl.ds(aligned(2 * at + 1, rows), rows), :] = high[0].astype(jnp.float32)


def place_shared(meta, mine, other):
    _, rows, columns = mine.shape
    units = columns // 6
    low = pl.BlockSpec((1, rows, units), lambda i, j, m: (i, 0, j))
    high = pl.BlockSpec((1, rows, units), lambda i, j, m: (i, 0, 3 + j))
    outs = shape_of((4 * rows, 2 * columns), jnp.float32)
    return call(
        place_shared_kernel,
        "place_shared",
        meta,
        [mine, mine, other, other],
        (4, 3),
        [low, high, low, high],
        pl.BlockSpec((4 * rows, units), lambda i, j, m: (0, 4 * j + (m[1] ^ i))),
        outs,
        [],
        0,
        0,
    )


def place_heads_kernel(meta, *refs):
    mine, other, out_ref = refs[:4], refs[4], refs[5]
    core, chip = meta[0] & 1, meta[0] >> 1
    rows, columns = mine[0].shape
    group_width = columns - 2 * HEAD_SIZE
    for r in range(4):
        head = chip ^ r
        for at, pieces in ((core, [piece[...] for piece in mine]), (1 - core, other)):
            to = pl.ds(aligned(at, rows), rows)
            values = pieces[r].astype(jnp.float32)
            out_ref[to, pl.ds(aligned(head, group_width), group_width)] = values[:, :group_width]
            out_ref[to, pl.ds(aligned(4 * group_width // HEAD_SIZE + head, HEAD_SIZE), HEAD_SIZE)] = (
                values[:, group_width : group_width + HEAD_SIZE]
            )
            out_ref[
                to, pl.ds(aligned(4 * group_width // HEAD_SIZE + 4 + head, HEAD_SIZE), HEAD_SIZE)
            ] = values[:, group_width + HEAD_SIZE :]


def place_heads(meta, mine, other):
    rows, columns = mine[0].shape
    arrays = list(mine) + [other]
    outs = shape_of((2 * rows, 4 * columns), jnp.float32)
    return call(
        place_heads_kernel,
        "place_heads",
        meta,
        arrays,
        (1,),
        [whole(a) for a in arrays],
        whole(outs),
        outs,
        [],
        0,
        size_of(arrays + [outs]),
    )


def join_shared_kernel(meta, mine, other, out_ref):
    step = pl.program_id(0)
    rows = mine.shape[2]
    first = meta[0] ^ (2 * step)
    for i in range(4):
        at = 8 * (meta[1] ^ i)
        out_ref[pl.ds(aligned(at + first, rows), rows), :] = mine[0, i]
        out_ref[pl.ds(aligned(at + (first ^ 1), rows), rows), :] = other[0, i]


def join_shared(meta, mine, other):
    _, _, rows, columns = mine.shape
    block = pl.BlockSpec((1, 4, rows, columns), lambda r, m: (r, 0, 0, 0))
    outs = shape_of((32 * rows, columns), jnp.bfloat16)
    return call(
        join_shared_kernel,
        "join_shared",
        meta,
        [mine, other],
        (4,),
        [block, block],
        whole(outs),
        outs,
        [],
        0,
        size_of([mine, other, outs]),
    )


class Clock:
    def __init__(self):
        self.last = None

    def __call__(self, *values):
        if self.last is None:
            return values if len(values) > 1 else values[0]
        held = lax.optimization_barrier(tuple(values) + (self.last,))[:-1]
        return held if len(held) > 1 else held[0]

    def mark(self, value):
        self.last = value
        return value


EARLY = (
    "H", "W", "K", "S", "K", "W", "S", "W", "K", "S", "O", "S", "M", "M", "S", "O", "M", "S", "M", "R", "M", "K", "M", "K",
    "M", "K", "R", "M", "K", "M", "M", "M", "M", "R", "M", "M",
)
LATE = (
    "L", "0", "1", "0", "L", "0", "1", "1", "L", "L", "O", "0", "1", "L", "0", "L", "1", "O", "Q", "O", "0", "1", "L", "Q",
    "O", "L", "Q", "Q", "O", "Q", "L", "1", "0", "O", "Q", "S", "L", "O", "Q", "1", "S", "L", "0", "O", "Q", "L", "Q", "O",
    "S",
)


def fast_device(
    hidden,
    teacher,
    valid_mask,
    routes,
    route_gates,
    gain_in,
    query_key_value_weight,
    out_weight,
    gain_mid,
    shared_weight,
    expert_weight,
):
    token_rows, width = hidden.shape[1:]
    context_count, shard_count = 8, 4
    context_index = lax.axis_index("ctx").astype(jnp.int32)
    shard_index = lax.axis_index("wt").astype(jnp.int32)
    plain_meta = jnp.stack([context_index, shard_index])
    core = context_index & 1
    chip = context_index >> 1
    at_end = (shard_index == 0) | (shard_index == shard_count - 1)
    group_width = QUERY_HEADS // KEY_VALUE_HEADS * HEAD_SIZE
    query_width = QUERY_HEADS * HEAD_SIZE
    kv_width = KEY_VALUE_HEADS * HEAD_SIZE
    scale = 1.0 / math.sqrt(HEAD_SIZE)
    all_tokens = token_rows * context_count * shard_count
    shard_rows = query_key_value_weight.shape[0]
    half_rows = shard_rows // 2
    local_experts = expert_weight.shape[0]
    bf16, f32 = jnp.bfloat16, jnp.float32
    states = hidden[0]
    clock = Clock()
    have = {}

    def meta():
        return clock(plain_meta)

    def now(*values):
        return clock(*values)

    def ready(*values):
        values = clock(*values)
        clock.mark(values[0] if isinstance(values, tuple) or isinstance(values, list) else values)
        return values


    def hidden_chain():
        have["blocks"] = chips_exchange(jnp.broadcast_to(states, (4,) + states.shape))
        yield

    def qkv_chain():
        rows = lax.dynamic_slice_in_dim(query_key_value_weight, core * half_rows, half_rows, 0)
        half = jnp.concatenate(
            [
                lax.dynamic_slice_in_dim(rows, chip * group_width, group_width, 1),
                lax.dynamic_slice_in_dim(rows, query_width + chip * HEAD_SIZE, HEAD_SIZE, 1),
                lax.dynamic_slice_in_dim(
                    rows, query_width + kv_width + chip * HEAD_SIZE, HEAD_SIZE, 1
                ),
            ],
            axis=1,
        )
        came = line_swap(half, 1)
        yield
        pair = clock.mark(jnp.stack([half, now(came)]))
        came = line_swap(pair, 2)
        yield
        have["qkv_mine"] = clock.mark(jnp.concatenate([pair, now(came)]))
        have["qkv_other"] = flip(have["qkv_mine"], 1)
        yield

    def small_chain():
        expert_ids = jnp.arange(EXPERTS, dtype=jnp.int32)
        matrix = jnp.sum(
            jnp.where(
                routes[0][None, :, :] == expert_ids[:, None, None], route_gates[0][None, :, :], 0.0
            ),
            axis=-1,
        )
        have["valid"] = valid_mask[0].astype(f32)
        gains = jnp.concatenate([gain_in, gain_mid]).astype(f32).reshape(-1, token_rows)
        gain_rows = gains.shape[0]
        filled = EXPERTS + gain_rows
        pack = jnp.concatenate(
            [
                matrix,
                gains,
                jnp.full((32 - filled, token_rows), jnp.sum(have["valid"]), f32),
            ]
        )
        came = line_swap(pack, 1)
        yield
        pair = clock.mark(jnp.stack([pack, now(came)]))
        came = line_swap(pair, 2)
        yield
        all_packs = clock.mark(jnp.concatenate([pair, now(came)]))
        have["gates"] = [
            lax.dynamic_slice_in_dim(
                all_packs[i], shard_index * local_experts, local_experts, 0
            )[..., None]
            for i in range(4)
        ]
        gains = all_packs[:, EXPERTS:filled].reshape(4, 2, shard_rows)
        gains = jnp.stack([pick(gains, shard_index ^ i) for i in range(4)], axis=1)
        have["gains"] = gains.reshape(2, 1, width)
        total = jnp.broadcast_to(jnp.sum(all_packs[:, filled, 0]), (8, 128))
        yield
        total = now(total)
        for bit in (1, 2, 4):
            came = flip(total, bit)
            yield
            total = clock.mark(total + now(came))
        have["count"] = total[0, 0]
        yield

    def shared_chain():
        eighth = shard_rows // 8
        units = SF // shard_count
        piece = lax.dynamic_slice_in_dim(shared_weight, context_index * eighth, eighth, 0)
        piece = piece.reshape(eighth, 3, shard_count, units)

        piece = jnp.transpose(piece, (2, 0, 1, 3)).reshape(shard_count, eighth, 3 * units)
        parts = [pick(piece, shard_index ^ i) for i in range(4)]
        came = line_swap(now(jnp.stack([parts[1], parts[3]])), 1)
        yield
        came = now(came)
        mine = jnp.stack([parts[0], came[0]])
        came = line_swap(clock.mark(jnp.stack([parts[2], came[1]])), 2)
        yield
        pieces = clock.mark(jnp.concatenate([mine, now(came)]))
        came = flip(pieces, 2)
        yield
        pair = clock.mark(jnp.stack([pieces, now(came)]))
        came = flip(pair, 4)
        yield
        mine = clock.mark(jnp.concatenate([pair, now(came)]))
        other = flip(mine, 1)
        yield
        have["shared"] = join_shared(meta(), mine, other)
        clock.mark(have["shared"])
        yield

    def out_chain():
        half = lax.dynamic_slice_in_dim(now(out_weight), core * half_rows, half_rows, 0)
        came = line_exchange(jnp.broadcast_to(half, (4,) + half.shape))
        yield
        have["out_mine"] = clock.mark(now(came))
        have["out_other"] = flip(have["out_mine"], 1)
        yield

    def qkv_all_chain():
        half = lax.dynamic_slice_in_dim(
            now(have["qkv_slice"]), core * (width // 2), width // 2, 0
        )
        came = flip(half, 2)
        yield
        pair = clock.mark(jnp.stack([half, now(came)]))
        came = flip(pair, 4)
        yield
        have["rel_mine"] = clock.mark(jnp.concatenate([pair, now(came)]))
        have["rel_other"] = flip(have["rel_mine"], 1)
        yield

    def main_chain():
        gains = have["gains"]
        normed_in, query, pair, qkv_slice = project(
            meta(), have["blocks"], gains[0], have["qkv_mine"], have["qkv_other"], group_width
        )
        clock.mark(pair)
        have["normed_in"], have["qkv_slice"] = normed_in, qkv_slice
        pair_other = flip(pair, 1)
        yield
        mixed_heads, log_total = attend(meta(), query, pair, pair_other, scale)
        clock.mark(log_total)
        have["attend"] = (query, pair, pair_other, log_total, mixed_heads)
        parts = ready(*[pick(mixed_heads, chip ^ r) for r in range(4)])
        mixed = [parts[0]] + [flip(parts[r], 2 * r) for r in (1, 2, 3)]
        have["mixed"] = mixed
        yield
        out_full, middle, normed_mid = leave(
            meta(), mixed, have["out_mine"], have["out_other"], states, gains[1]
        )
        have["out_full"], have["middle"] = out_full, middle
        clock.mark(normed_mid)

        near, center = line_swap(normed_mid, 1), line_middle(normed_mid)
        yield
        gates, shared_slice = have["gates"], have["shared"]
        gate_ups, shared_gate_ups, outs = [], [], []

        def forward(rows, i):
            result = experts(meta(), rows, gates[i], expert_weight, shared_slice)
            clock.mark(result[2])
            gate_ups.append(result[0])
            shared_gate_ups.append(result[1])
            outs.append(result[2])

        forward(normed_mid, 0)
        yield
        near, center = now(near, center)
        far, outward = line_middle(near), line_outward(center)
        forward(near, 1)
        yield
        far, outward = now(far, outward)
        outward_far = line_outward(far)
        third = clock.mark(jnp.where(at_end, outward, far))
        forward(third, 2)
        yield
        outward_far = now(outward_far)
        fourth = clock.mark(jnp.where(at_end, outward_far, center))
        forward(fourth, 3)
        line_rows = [normed_mid, near, third, fourth]
        came = line_inward(outs[3])
        yield
        carried = clock.mark(outs[2] + now(came))
        inward, crossed = line_inward(carried), line_middle(carried)
        yield
        inward, crossed = now(inward, crossed)
        near_out, middle_out = ready(outs[1] + crossed, outs[3] + inward)
        near_out, middle_out = line_swap(near_out, 1), line_middle(middle_out)
        yield
        near_out, middle_out = now(near_out, middle_out)
        final_state = (
            middle + outs[0].astype(f32) + near_out.astype(f32) + middle_out.astype(f32)
        )
        valid = have["valid"]
        deviation = final_state - teacher[0].astype(f32)
        have["squared"] = jnp.sum(valid[:, None] * deviation * deviation)
        grad_final = all_tokens / have["count"] * valid[:, None] * deviation
        have["final"], have["grad_final"] = final_state.astype(bf16)[None], grad_final
        grad_low = clock.mark(grad_final.astype(bf16))
        near, center = line_swap(grad_low, 1), line_middle(grad_low)
        yield
        kept = []

        def backward(grads, i):
            kept.append(
                experts_back(
                    meta(),
                    grads,
                    gates[i],
                    gate_ups[i],
                    shared_gate_ups[i],
                    expert_weight,
                    shared_slice,
                )
            )
            clock.mark(kept[-1][4])

        backward(grad_low, 0)
        yield
        near, center = now(near, center)
        far, outward = line_middle(near), line_outward(center)
        backward(near, 1)
        yield
        far, outward = now(far, outward)
        outward_far = line_outward(far)
        third = clock.mark(jnp.where(at_end, outward, far))
        backward(third, 2)
        yield
        outward_far = now(outward_far)
        fourth = clock.mark(jnp.where(at_end, outward_far, center))
        backward(fourth, 3)
        have["line"] = (line_rows, [grad_low, near, third, fourth])
        have["experts"] = list(zip(*kept))
        yield


    def states_chain():
        outs = have["experts"][4]
        came = line_inward(outs[3])
        yield
        carried = clock.mark(outs[2] + now(came))
        inward, crossed = line_inward(carried), line_middle(carried)
        yield
        inward, crossed = now(inward, crossed)
        near_out, middle_out = ready(outs[1] + crossed, outs[3] + inward)
        near_out, middle_out = line_swap(near_out, 1), line_middle(middle_out)
        yield
        near_out, middle_out = now(near_out, middle_out)
        grad_normed = clock.mark(
            outs[0].astype(f32) + near_out.astype(f32) + middle_out.astype(f32)
        )
        grad_middle, grad_branch, grad_gain_mid, grad_mixed = enter_back(
            meta(),
            have["grad_final"],
            grad_normed,
            have["middle"],
            have["gains"][1],
            have["out_full"],
        )
        clock.mark(grad_branch)
        have["grad_branch"], have["grad_gain_mid"] = grad_branch, grad_gain_mid
        grad_mixed = chips_exchange(ready(grad_mixed))
        yield
        query, pair, pair_other, log_total, mixed_heads = have["attend"]
        grad_query, grad_pair, grad_other = attend_back(
            meta(), query, pair, pair_other, log_total, mixed_heads, grad_mixed, scale
        )
        clock.mark(grad_query)
        came = flip(grad_other, 1)
        yield
        grad_pair = grad_pair + now(came).astype(f32)
        projected = clock.mark(jnp.concatenate([grad_query, grad_pair.astype(bf16)], axis=-1))
        have["grad_projected"] = projected
        parts = chips_exchange(ready(projected))
        yield
        grad_hidden, grad_gain_in = finish(
            meta(),
            parts,
            have["rel_mine"],
            have["rel_other"],
            states,
            grad_middle,
            have["gains"][0],
        )
        clock.mark(grad_gain_in)
        have["grad_hidden"] = grad_hidden
        sums = jnp.concatenate(
            [grad_gain_in, have["grad_gain_mid"], jnp.full((6, width), have["squared"], f32)],
            axis=0,
        )
        for offset in (1, 2):
            came = line_swap(sums, offset)
            yield
            sums = clock.mark(sums + now(came))
        for bit in (1, 2, 4):
            came = flip(sums, bit)
            yield
            sums = clock.mark(sums + now(came))
        own = lax.dynamic_slice_in_dim(sums, shard_index * shard_rows, shard_rows, 1)
        have["sums"] = (own, 0.5 * sums[2, 0] / (have["count"] * width))
        yield

    def expert_chain(index):
        line_rows, line_grads = have["line"]
        grad_gate_ups, acts, shared_grads, shared_acts = have["experts"][:4]
        shared = (shared_grads, shared_acts) if index == 0 else None

        def grad_of(at):
            return clock.mark(
                expert_grad(
                    meta(),
                    2 * at + index,
                    at,
                    line_rows,
                    line_grads,
                    grad_gate_ups,
                    acts,
                    shared,
                )
            )

        came = flip(grad_of(1 - core), 1)
        yield
        keep = grad_of(core)
        yield
        x_first = index % 2 == 0
        first, second = (2, 4) if x_first else (4, 2)
        picked = ((1, 3), (0, 2)) if x_first else ((2, 3), (0, 1))
        pieces = keep.shape[1] // 96

        def split_sum(keep, came):
            return [
                jnp.stack([keep[i] + came[i] for i in places]) for places in picked
            ]

        give, keep = blend(meta(), "blend_split", split_sum, [keep, came], pieces)
        clock.mark(give)
        came = flip(give, first)
        yield
        give, keep = blend(
            meta(), "blend_pair", lambda k, c: [k[1] + c[1], k[0] + c[0]], [keep, came], pieces
        )
        clock.mark(give)
        came = flip(give, second)
        yield
        own = clock.mark(blend(meta(), "blend_sum", lambda k, c: k + c, [keep, came], pieces))
        came = flip(own, second)
        yield
        pair = clock.mark(
            blend(meta(), "blend_stack", lambda a, b: jnp.stack([a, b]), [own, came], pieces)
        )
        came = flip(pair, first)
        yield

        def stack_four(near, far):
            if x_first:
                return jnp.stack([near[0], far[0], near[1], far[1]])
            return jnp.stack([near[0], near[1], far[0], far[1]])

        stacked = clock.mark(blend(meta(), "blend_four", stack_four, [pair, came], pieces))
        other = flip(stacked, 1)
        if index == 0:
            have["shared_sum"] = stacked[:, shard_rows:]
        yield
        have["grad_experts"] = place_pair(
            meta(), have.get("grad_experts"), index, expert_weight.shape, stacked, other
        )
        clock.mark(have["grad_experts"])
        yield

    def shared_grad_chain():
        total = now(have["shared_sum"])
        parts = ready(*[pick(total, chip ^ shard_index ^ i) for i in range(4)])
        came = [line_swap(parts[i], i) for i in (1, 2, 3)]
        yield
        mine = clock.mark(jnp.stack([parts[0]] + list(now(*came))))
        other = flip(mine, 1)
        yield
        have["grad_shared"] = clock.mark(place_shared(meta(), mine, other))
        yield

    def line_reduce_steps(keep, came):
        came = now(came)
        parts = [keep[i] + came[i] for i in range(4)]
        came = line_inward(clock.mark(parts[3]))
        yield
        carried = clock.mark(parts[2] + now(came))
        inward, crossed = line_inward(carried), line_middle(carried)
        yield
        inward, crossed = now(inward, crossed)
        near_out, middle_out = ready(parts[1] + crossed, parts[3] + inward)
        near_out, middle_out = line_swap(near_out, 1), line_middle(middle_out)
        yield
        near_out, middle_out = now(near_out, middle_out)
        have["line_sum"] = clock.mark(
            (parts[0].astype(f32) + near_out.astype(f32) + middle_out.astype(f32)).astype(bf16)
        )

    def out_grad_chain():
        mixed = jnp.concatenate(have["mixed"], axis=1)
        keep, give = weight_grad(
            meta(), chip ^ shard_index, [([mixed], [have["grad_branch"][None]])], 0
        )
        clock.mark(keep)
        came = flip(give, 1)
        yield
        yield from line_reduce_steps(keep, came)
        total = have["line_sum"]
        yield
        total = ready(total)
        came = flip(total, 2)
        yield
        total = clock.mark(total + now(came))
        came = flip(total, 4)
        yield
        mine = clock.mark(total + now(came))
        other = flip(mine, 1)
        yield
        mine, other = now(mine, other)
        have["grad_out"] = clock.mark(
            jnp.where(
                core == 0,
                jnp.concatenate([mine, other], axis=0),
                jnp.concatenate([other, mine], axis=0),
            ).astype(f32)
        )
        yield

    def qkv_grad_chain():
        normed_in = have["normed_in"].reshape(4 * token_rows, width)
        projected = have["grad_projected"].reshape(1, 4 * token_rows, -1)
        keep, give = weight_grad(meta(), shard_index, [([normed_in], [projected])], 0)
        clock.mark(keep)
        came = flip(give, 1)
        yield
        yield from line_reduce_steps(keep, came)
        own = have["line_sum"]
        yield
        own = ready(own)
        came = flip(own, 2)
        yield
        pair = clock.mark(jnp.stack([own, now(came)]))
        came = flip(pair, 4)
        yield
        mine = clock.mark(jnp.concatenate([pair, now(came)]))
        other = flip(mine, 1)
        yield
        have["grad_qkv"] = clock.mark(place_heads(meta(), [mine[r] for r in range(4)], other))
        yield

    early = {
        "H": hidden_chain(),
        "W": qkv_chain(),
        "S": shared_chain(),
        "O": out_chain(),
        "K": small_chain(),
        "R": qkv_all_chain(),
        "M": main_chain(),
    }
    late = {
        "L": states_chain(),
        "S": shared_grad_chain(),
        "O": out_grad_chain(),
        "Q": qkv_grad_chain(),
    }
    for index in range(local_experts // 2):
        late[str(index)] = expert_chain(index)
    for chains, order in ((early, EARLY), (late, LATE)):
        for name in order:
            next(chains[name], None)
        for name in chains:
            for _ in chains[name]:
                pass

    own, loss_value = have["sums"]
    return (
        have["final"],
        loss_value,
        have["grad_hidden"],
        own[0],
        have["grad_qkv"],
        have["grad_out"],
        own[1],
        have["grad_shared"],
        have["grad_experts"],
    )


def solution(mesh):
    in_specs = (
        P("wt", "ctx", None),
        P("wt", "ctx", None),
        P("wt", "ctx"),
        P("wt", "ctx", None),
        P("wt", "ctx", None),
        P("wt"),
        P("wt", None),
        P("wt", None),
        P("wt"),
        P("wt", None),
        P("wt", None, None),
    )
    out_specs = (
        P("wt", "ctx", None),
        P(),
        P("wt", "ctx", None),
        P("wt"),
        P("wt", None),
        P("wt", None),
        P("wt"),
        P("wt", None),
        P("wt", None, None),
    )
    plane_of_eight = dict(mesh.shape) == {"ctx": 8, "wt": 4}
    return jax.shard_map(
        fast_device if plane_of_eight else on_device, mesh=mesh, in_specs=in_specs, out_specs=out_specs, check_vma=False
    )
```

```python
import functools
import math

import jax
import jax.numpy as jnp
from jax import lax
from jax.experimental import pallas as pl
from jax.experimental.pallas import tpu as pltpu
from jax.sharding import PartitionSpec as P

QUERY_HEADS = 12
KEY_VALUE_HEADS = 4
HEAD_SIZE = 128
F = 512
SF = 1024
EXPERTS = 16
TOP = 6


norm_eps = 1e-05
masked_score = -1e30


def sigmoid_linear(values):
    return values * jax.nn.sigmoid(values)


def silu_slope(values):
    sigma_value = jax.nn.sigmoid(values)
    return sigma_value * (1.0 + values * (1.0 - sigma_value))


def normalize(values):
    inverse = lax.rsqrt(jnp.mean(values * values, axis=-1, keepdims=True) + norm_eps)
    return (values * inverse, inverse)


def norm_back(grad_normed, scaled, inverse, gain_vector):
    grad_scaled = grad_normed * gain_vector
    return inverse * (grad_scaled - scaled * jnp.mean(grad_scaled * scaled, axis=-1, keepdims=True))


def positions(row_ids, token_rows, context_count):
    piece_index = row_ids // token_rows
    within = row_ids % token_rows
    half_rows = token_rows // 2
    mirrored = jnp.where(within < half_rows, piece_index, 2 * context_count - 1 - piece_index)
    return mirrored * half_rows + within % half_rows


def route_tables(local_routes, local_gates, experts, capacity):
    token_rows = local_routes.shape[0]
    flat_routes = local_routes.reshape(-1)
    one_hot = (flat_routes[:, None] == jnp.arange(experts, dtype=jnp.int32)[None, :]).astype(
        jnp.int32
    )
    earlier = jnp.cumsum(one_hot, axis=0) - one_hot
    slot_index = jnp.sum(earlier * one_hot, axis=1)
    token_index = jnp.arange(flat_routes.shape[0], dtype=jnp.int32) // local_routes.shape[1]
    slot_table = (
        jnp.full((experts, capacity), token_rows, jnp.int32)
        .at[flat_routes, slot_index]
        .set(token_index)
    )
    slot_gate = (
        jnp.zeros((experts, capacity), jnp.float32)
        .at[flat_routes, slot_index]
        .set(local_gates.reshape(-1))
    )
    return (slot_table, slot_gate)


def block_scores(query_rows, key_block, key_position, query_place, score_scale):
    scores = (
        jnp.einsum("qhgd,khd->qhgk", query_rows, key_block, preferred_element_type=jnp.float32)
        * score_scale
    )
    allowed = key_position[None, None, None, :] <= query_place[:, None, None, None]
    return jnp.where(allowed, scores, masked_score)


def attend_forward(
    query_rows, blocked_keys, blocked_values, place_blocks, query_place, score_scale
):
    head_shape = query_rows.shape[:3]

    def online_step(running, block_args):
        running_max, running_sum, accumulated = running
        key_block, value_block, key_position = block_args
        scores = block_scores(query_rows, key_block, key_position, query_place, score_scale)
        new_max = jnp.maximum(running_max, jnp.max(scores, axis=-1))
        rescale = jnp.exp(running_max - new_max)
        powers = jnp.exp(scores - new_max[..., None])
        new_sum = running_sum * rescale + jnp.sum(powers, axis=-1)
        weighted = jnp.einsum(
            "qhgk,khd->qhgd",
            powers.astype(jnp.bfloat16),
            value_block,
            preferred_element_type=jnp.float32,
        )
        return ((new_max, new_sum, accumulated * rescale[..., None] + weighted), None)

    initial = (
        jnp.full(head_shape, masked_score, jnp.float32),
        jnp.zeros(head_shape, jnp.float32),
        jnp.zeros(query_rows.shape, jnp.float32),
    )
    row_max, row_sum, accumulated = lax.scan(
        online_step, initial, (blocked_keys, blocked_values, place_blocks)
    )[0]
    log_total = row_max + jnp.log(row_sum)
    return (accumulated / row_sum[..., None], log_total)


def attend_backward(
    query_rows,
    blocked_keys,
    blocked_values,
    place_blocks,
    query_place,
    log_total,
    attention_output_gradient,
    attention_output,
    score_scale,
):
    row_delta = jnp.sum(attention_output_gradient.astype(jnp.float32) * attention_output, axis=-1)

    def block_grads(grad_queries, block_args):
        key_block, value_block, key_position = block_args
        scores = block_scores(query_rows, key_block, key_position, query_place, score_scale)
        probabilities = jnp.exp(scores - log_total[..., None])
        grad_probs = jnp.einsum(
            "qhgd,khd->qhgk",
            attention_output_gradient,
            value_block,
            preferred_element_type=jnp.float32,
        )
        grad_scores = (probabilities * (grad_probs - row_delta[..., None])).astype(jnp.bfloat16)
        grad_queries = grad_queries + jnp.einsum(
            "qhgk,khd->qhgd", grad_scores, key_block, preferred_element_type=jnp.float32
        )
        grad_keys = (
            jnp.einsum(
                "qhgk,qhgd->khd", grad_scores, query_rows, preferred_element_type=jnp.float32
            )
            * score_scale
        )
        grad_values = jnp.einsum(
            "qhgk,qhgd->khd",
            probabilities.astype(jnp.bfloat16),
            attention_output_gradient,
            preferred_element_type=jnp.float32,
        )
        return (grad_queries, (grad_keys, grad_values))

    grad_queries, (grad_keys, grad_values) = lax.scan(
        block_grads,
        jnp.zeros(query_rows.shape, jnp.float32),
        (blocked_keys, blocked_values, place_blocks),
    )
    return (grad_queries * score_scale, grad_keys, grad_values)


def gate_up_grads(grad_act, gate_up, hidden_units):
    gate_part = gate_up[..., :hidden_units]
    up_part = gate_up[..., hidden_units:]
    return jnp.concatenate(
        [grad_act * up_part * silu_slope(gate_part), grad_act * sigmoid_linear(gate_part)], axis=-1
    ).astype(jnp.bfloat16)


def on_device(
    hidden,
    teacher,
    valid_mask,
    routes,
    route_gates,
    gain_in,
    query_key_value_weight,
    out_weight,
    gain_mid,
    shared_weight,
    expert_weight,
):
    token_rows = hidden.shape[1]
    model_width = hidden.shape[2]
    context_count = lax.axis_size("ctx")
    shard_count = lax.axis_size("wt")
    seq_rows = token_rows * context_count
    all_tokens = seq_rows * shard_count
    query_groups = QUERY_HEADS // KEY_VALUE_HEADS
    query_total_width = QUERY_HEADS * HEAD_SIZE
    key_value_width = KEY_VALUE_HEADS * HEAD_SIZE
    score_scale = 1.0 / math.sqrt(HEAD_SIZE)
    key_row_count = min(512, seq_rows)
    number_of_blocks = seq_rows // key_row_count
    capacity = token_rows * TOP // 12
    local_experts = expert_weight.shape[0]
    contract_last = (((1,), (1,)), ((), ()))
    contract_first = (((0,), (0,)), ((), ()))
    full_gain_in, full_qkv, full_out, full_gain_mid, full_shared = (
        lax.all_gather(gain_in, "wt", axis=0, tiled=True),
        lax.all_gather(query_key_value_weight, "wt", axis=0, tiled=True),
        lax.all_gather(out_weight, "wt", axis=0, tiled=True),
        lax.all_gather(gain_mid, "wt", axis=0, tiled=True),
        lax.all_gather(shared_weight, "wt", axis=0, tiled=True),
    )
    gain_in_float = full_gain_in.astype(jnp.float32)
    gain_mid_float = full_gain_mid.astype(jnp.float32)
    inputs = hidden[0].astype(jnp.float32)
    scaled_in, inverse_in = normalize(inputs)
    normed_in = (scaled_in * gain_in_float).astype(jnp.bfloat16)
    projected_rows = jnp.dot(normed_in, full_qkv, preferred_element_type=jnp.float32).astype(
        jnp.bfloat16
    )
    query_rows = projected_rows[:, :query_total_width].reshape(
        token_rows, KEY_VALUE_HEADS, query_groups, HEAD_SIZE
    )
    context_local = projected_rows[:, query_total_width:]
    context_gathered = lax.all_gather(context_local, "ctx", axis=0, tiled=True)
    context_index = lax.axis_index("ctx")
    query_place = positions(
        context_index * token_rows + jnp.arange(token_rows, dtype=jnp.int32),
        token_rows,
        context_count,
    )
    place_blocks = positions(
        jnp.arange(seq_rows, dtype=jnp.int32), token_rows, context_count
    ).reshape(number_of_blocks, key_row_count)
    blocked_keys = context_gathered[:, :key_value_width].reshape(
        number_of_blocks, key_row_count, KEY_VALUE_HEADS, HEAD_SIZE
    )
    blocked_values = context_gathered[:, key_value_width:].reshape(
        number_of_blocks, key_row_count, KEY_VALUE_HEADS, HEAD_SIZE
    )
    attention_output, log_total = attend_forward(
        query_rows, blocked_keys, blocked_values, place_blocks, query_place, score_scale
    )
    mixed_rows = attention_output.reshape(token_rows, query_total_width).astype(jnp.bfloat16)
    middle = inputs + jnp.dot(mixed_rows, full_out, preferred_element_type=jnp.float32)
    scaled_mid, inverse_mid = normalize(middle)
    normed_mid = (scaled_mid * gain_mid_float).astype(jnp.bfloat16)
    shared_gate_up = jnp.dot(
        normed_mid, full_shared[:, : 2 * SF], preferred_element_type=jnp.float32
    )
    shared_act = (sigmoid_linear(shared_gate_up[:, :SF]) * shared_gate_up[:, SF:]).astype(
        jnp.bfloat16
    )
    shared_out = lax.dot_general(
        shared_act, full_shared[:, 2 * SF :], contract_last, preferred_element_type=jnp.float32
    )
    slot_table, slot_gate = route_tables(routes[0], route_gates[0], EXPERTS, capacity)
    padded_rows = jnp.concatenate([normed_mid, jnp.zeros((1, model_width), jnp.bfloat16)], axis=0)
    expert_rows = jnp.take(padded_rows, slot_table, axis=0)
    arrived = lax.all_to_all(expert_rows, "wt", split_axis=0, concat_axis=0, tiled=True)
    slot_count = arrived.shape[1]
    grouped = arrived.reshape(shard_count, local_experts, slot_count, model_width)
    owner_gate_up = jnp.einsum(
        "wesd,edf->wesf", grouped, expert_weight[:, :, : 2 * F], preferred_element_type=jnp.float32
    )
    owner_act = (sigmoid_linear(owner_gate_up[..., :F]) * owner_gate_up[..., F:]).astype(
        jnp.bfloat16
    )
    owner_out = jnp.einsum(
        "wesf,edf->wesd",
        owner_act,
        expert_weight[:, :, 2 * F :],
        preferred_element_type=jnp.float32,
    ).astype(jnp.bfloat16)
    returned = lax.all_to_all(
        owner_out.reshape(shard_count * local_experts, slot_count, model_width),
        "wt",
        split_axis=0,
        concat_axis=0,
        tiled=True,
    )
    expert_out, owner_rows, owner_gate_up, owner_act = (
        returned,
        arrived,
        owner_gate_up.reshape(shard_count * local_experts, slot_count, 2 * F),
        owner_act.reshape(shard_count * local_experts, slot_count, F),
    )
    routed = (
        jnp.zeros((token_rows + 1, model_width), jnp.float32)
        .at[slot_table]
        .add(expert_out.astype(jnp.float32) * slot_gate[..., None])[:token_rows]
    )
    final_state = middle + shared_out + routed
    valid_float = valid_mask[0].astype(jnp.float32)
    deviation = final_state - teacher[0].astype(jnp.float32)
    squared_local = jnp.sum(valid_float[:, None] * deviation * deviation)
    count_local = jnp.sum(valid_float)
    squared_total, valid_count = lax.psum((squared_local, count_local), ("ctx", "wt"))
    loss_value = 0.5 * squared_total / (valid_count * model_width)
    grad_final = all_tokens / valid_count * valid_float[:, None] * deviation
    grad_shared_out = grad_final.astype(jnp.bfloat16)
    grad_shared_act = jnp.dot(
        grad_shared_out, full_shared[:, 2 * SF :], preferred_element_type=jnp.float32
    )
    grad_shared_down = lax.dot_general(
        grad_shared_out, shared_act, contract_first, preferred_element_type=jnp.float32
    )
    grad_shared_gate_up = gate_up_grads(grad_shared_act, shared_gate_up, SF)
    grad_normed_mid = lax.dot_general(
        grad_shared_gate_up,
        full_shared[:, : 2 * SF],
        contract_last,
        preferred_element_type=jnp.float32,
    )
    grad_shared_front = lax.dot_general(
        normed_mid, grad_shared_gate_up, contract_first, preferred_element_type=jnp.float32
    )
    grad_shared_full = jnp.concatenate([grad_shared_front, grad_shared_down], axis=1)
    padded_grads = jnp.concatenate([grad_final, jnp.zeros((1, model_width), jnp.float32)], axis=0)
    grad_expert_out = (jnp.take(padded_grads, slot_table, axis=0) * slot_gate[..., None]).astype(
        jnp.bfloat16
    )
    grad_arrived = lax.all_to_all(grad_expert_out, "wt", split_axis=0, concat_axis=0, tiled=True)
    grad_grouped = grad_arrived.reshape(shard_count, local_experts, capacity, model_width)
    owner_gate_up_grouped = owner_gate_up.reshape(shard_count, local_experts, capacity, 2 * F)
    owner_act_grouped = owner_act.reshape(shard_count, local_experts, capacity, F)
    owner_rows_grouped = owner_rows.reshape(shard_count, local_experts, capacity, model_width)
    grad_owner_act = jnp.einsum(
        "wecd,edf->wecf",
        grad_grouped,
        expert_weight[:, :, 2 * F :],
        preferred_element_type=jnp.float32,
    )
    grad_owner_gate_up = gate_up_grads(grad_owner_act, owner_gate_up_grouped, F)
    grad_owner_rows = jnp.einsum(
        "wecf,edf->wecd",
        grad_owner_gate_up,
        expert_weight[:, :, : 2 * F],
        preferred_element_type=jnp.float32,
    ).astype(jnp.bfloat16)
    front = jnp.einsum(
        "wecd,wecf->edf", owner_rows_grouped, grad_owner_gate_up, preferred_element_type=jnp.float32
    )
    back = jnp.einsum(
        "wecd,wecf->edf", grad_grouped, owner_act_grouped, preferred_element_type=jnp.float32
    )
    expert_grad = jnp.concatenate([front, back], axis=2)
    grad_rows = lax.all_to_all(
        grad_owner_rows.reshape(shard_count * local_experts, capacity, model_width),
        "wt",
        split_axis=0,
        concat_axis=0,
        tiled=True,
    )
    grad_normed_mid = (
        grad_normed_mid
        + jnp.zeros((token_rows + 1, model_width), jnp.float32)
        .at[slot_table]
        .add(grad_rows.astype(jnp.float32))[:token_rows]
    )
    grad_gain_mid_local = jnp.sum(grad_normed_mid * scaled_mid, axis=0)
    grad_middle = grad_final + norm_back(grad_normed_mid, scaled_mid, inverse_mid, gain_mid_float)
    grad_branch = grad_middle.astype(jnp.bfloat16)
    mixed_gradient = lax.dot_general(
        grad_branch, full_out, contract_last, preferred_element_type=jnp.float32
    ).astype(jnp.bfloat16)
    grad_out_local = lax.dot_general(
        mixed_rows, grad_branch, contract_first, preferred_element_type=jnp.float32
    )
    context_recomputed = lax.all_gather(context_local, "ctx", axis=0, tiled=True)
    backward_keys = context_recomputed[:, :key_value_width].reshape(
        number_of_blocks, key_row_count, KEY_VALUE_HEADS, HEAD_SIZE
    )
    backward_values = context_recomputed[:, key_value_width:].reshape(
        number_of_blocks, key_row_count, KEY_VALUE_HEADS, HEAD_SIZE
    )
    attention_output_gradient = mixed_gradient.reshape(
        token_rows, KEY_VALUE_HEADS, query_groups, HEAD_SIZE
    )
    grad_queries, grad_keys, grad_values = attend_backward(
        query_rows,
        backward_keys,
        backward_values,
        place_blocks,
        query_place,
        log_total,
        attention_output_gradient,
        attention_output,
        score_scale,
    )
    grad_context_all = jnp.concatenate(
        [
            grad_keys.reshape(seq_rows, key_value_width),
            grad_values.reshape(seq_rows, key_value_width),
        ],
        axis=1,
    )
    grad_context = lax.psum_scatter(
        grad_context_all.astype(jnp.bfloat16), "ctx", scatter_dimension=0, tiled=True
    ).astype(jnp.float32)
    grad_projected = jnp.concatenate(
        [grad_queries.reshape(token_rows, query_total_width), grad_context], axis=1
    ).astype(jnp.bfloat16)
    grad_normed_in = lax.dot_general(
        grad_projected, full_qkv, contract_last, preferred_element_type=jnp.float32
    )
    grad_qkv_local = lax.dot_general(
        normed_in, grad_projected, contract_first, preferred_element_type=jnp.float32
    )
    grad_gain_in_local = jnp.sum(grad_normed_in * scaled_in, axis=0)
    grad_inputs = grad_middle + norm_back(grad_normed_in, scaled_in, inverse_in, gain_in_float)
    weight_sums = (
        lax.psum_scatter(
            grad_gain_in_local.astype(jnp.bfloat16), "wt", scatter_dimension=0, tiled=True
        ).astype(jnp.float32),
        lax.psum_scatter(
            grad_qkv_local.astype(jnp.bfloat16), "wt", scatter_dimension=0, tiled=True
        ).astype(jnp.float32),
        lax.psum_scatter(
            grad_out_local.astype(jnp.bfloat16), "wt", scatter_dimension=0, tiled=True
        ).astype(jnp.float32),
        lax.psum_scatter(
            grad_gain_mid_local.astype(jnp.bfloat16), "wt", scatter_dimension=0, tiled=True
        ).astype(jnp.float32),
        lax.psum_scatter(
            grad_shared_full.astype(jnp.bfloat16), "wt", scatter_dimension=0, tiled=True
        ).astype(jnp.float32),
    )
    summed = (
        lax.psum(weight_sums[0].astype(jnp.bfloat16), "ctx").astype(jnp.float32),
        lax.psum(weight_sums[1].astype(jnp.bfloat16), "ctx").astype(jnp.float32),
        lax.psum(weight_sums[2].astype(jnp.bfloat16), "ctx").astype(jnp.float32),
        lax.psum(weight_sums[3].astype(jnp.bfloat16), "ctx").astype(jnp.float32),
        lax.psum(weight_sums[4].astype(jnp.bfloat16), "ctx").astype(jnp.float32),
        lax.psum(expert_grad.astype(jnp.bfloat16), "ctx").astype(jnp.float32),
    )
    return (
        final_state.astype(jnp.bfloat16)[None],
        loss_value,
        grad_inputs[None],
        summed[0],
        summed[1],
        summed[2],
        summed[3],
        summed[4],
        summed[5],
    )


PLANE = [[0, 2, 4, 6], [1, 3, 5, 7]]
COSTS = {
    "project": 0.3,
    "attend": 0.3,
    "leave": 0.3,
    "join_shared": 0.3,
    "experts": 0.3,
    "experts_back": 0.3,
    "enter_back": 0.3,
    "attend_back": 0.3,
    "finish": 0.3,
    "weight_grad": 0.3,
    "expert_grad": 0.3,
    "blend_split": 0.3,
    "blend_pair": 0.3,
    "blend_sum": 0.3,
    "blend_stack": 0.3,
    "blend_four": 0.3,
    "place_sum": 0.3,
    "place_shared": 0.3,
    "place_heads": 0.3,
}


def flip(value, bit):
    return lax.ppermute(value, "ctx", [(index, index ^ bit) for index in range(8)])


def line_swap(value, offset):
    return lax.ppermute(value, "wt", [(index, index ^ offset) for index in range(4)])


def line_middle(value):
    return lax.ppermute(value, "wt", [(1, 2), (2, 1)])


def line_outward(value):
    return lax.ppermute(value, "wt", [(1, 0), (2, 3)])


def line_inward(value):
    return lax.ppermute(value, "wt", [(0, 1), (3, 2)])


def line_gather(value, at_end):
    near = line_swap(value, 1)
    middle = line_middle(value)
    middle_far = line_middle(near)
    outward = line_outward(middle)
    outward_far = line_outward(middle_far)
    return [
        value,
        near,
        jnp.where(at_end, outward, middle_far),
        jnp.where(at_end, outward_far, middle),
    ]


def line_reduce(parts):
    far = line_inward(parts[3])
    carried = parts[2] + far
    inward = line_inward(carried)
    crossed = line_middle(carried)
    near = line_swap(parts[1] + crossed, 1)
    middle = line_middle(parts[3] + inward)
    return (
        parts[0].astype(jnp.float32) + near.astype(jnp.float32) + middle.astype(jnp.float32)
    )


def chips_exchange(blocks):
    return lax.all_to_all(
        blocks,
        "ctx",
        split_axis=0,
        concat_axis=0,
        tiled=True,
        axis_index_groups=PLANE,
    )


def line_exchange(blocks):
    return lax.all_to_all(blocks, "wt", split_axis=0, concat_axis=0, tiled=True)


def chips_gather(value, x_last):
    along_x = flip(value, 2)
    along_y = flip(value, 4)
    corner = flip(along_y, 2) if x_last else flip(along_x, 4)
    return [value, along_x, along_y, corner]


def core_swap(values):
    return [flip(value, 1) for value in values]


def everywhere_sum(value):
    for bit in (1, 2, 4):
        value = value + flip(value, bit)
    for offset in (1, 2):
        value = value + line_swap(value, offset)
    return value


def pick(blocks, index):
    return lax.dynamic_index_in_dim(blocks, index, 0, keepdims=False)


def chips_reduce(keep, came):
    half = keep.shape[1] // 2
    upper = keep[:, :half] + came[:, :half]
    lower = keep[:, half:] + came[:, half:]
    upper_came = flip(upper[1::2], 2)
    lower_came = flip(lower[2:], 4)
    upper = upper[0::2] + upper_came
    lower = lower[:2] + lower_came
    upper_came = flip(upper[1], 4)
    lower_came = flip(lower[1], 2)
    return jnp.concatenate([upper[0] + upper_came, lower[0] + lower_came], axis=0)


def dot_plain(left, right):
    return lax.dot_general(
        left, right, (((1,), (0,)), ((), ())), preferred_element_type=jnp.float32
    )


def dot_last(left, right):
    return lax.dot_general(
        left, right, (((1,), (1,)), ((), ())), preferred_element_type=jnp.float32
    )


def dot_first(left, right):
    return lax.dot_general(
        left, right, (((0,), (0,)), ((), ())), preferred_element_type=jnp.float32
    )


def call(kernel, name, meta, arrays, grid, in_specs, out_specs, out_shape, scratch, flops, moved):
    return pl.pallas_call(
        kernel,
        grid_spec=pltpu.PrefetchScalarGridSpec(
            num_scalar_prefetch=1,
            grid=grid,
            in_specs=in_specs,
            out_specs=out_specs,
            scratch_shapes=scratch,
        ),
        out_shape=out_shape,
        compiler_params=pltpu.CompilerParams(vmem_limit_bytes=48 * 1024 * 1024),
        cost_estimate=pl.CostEstimate(
            flops=int(COSTS.get(name, 1.0) * 1e9), bytes_accessed=1000, transcendentals=0
        ),
        name=name,
    )(meta, *arrays)


def whole(array):
    rank = len(array.shape)
    return pl.BlockSpec(tuple(array.shape), lambda *_: (0,) * rank)


def shape_of(shape, dtype):
    return jax.ShapeDtypeStruct(shape, dtype)


def size_of(arrays):
    return sum(math.prod(a.shape) * a.dtype.itemsize for a in arrays)


def blend(meta, name, function, arrays, pieces=4):
    rows = arrays[0].shape[-2]
    tile = rows // pieces
    outs = jax.eval_shape(function, *[shape_of(a.shape, a.dtype) for a in arrays])
    many = isinstance(outs, (list, tuple))
    outs = list(outs) if many else [outs]

    def spec(a):
        rank = len(a.shape)
        lead = a.shape[:-2]
        return pl.BlockSpec(
            tuple(lead) + (tile, a.shape[-1]),
            lambda i, m: (0,) * (rank - 2) + (i, 0),
        )

    def kernel(meta_ref, *refs):
        result = function(*[ref[...] for ref in refs[: len(arrays)]])
        result = list(result) if many else [result]
        for ref, value in zip(refs[len(arrays) :], result):
            ref[...] = value

    result = call(
        kernel,
        name,
        meta,
        arrays,
        (pieces,),
        [spec(a) for a in arrays],
        [spec(a) for a in outs],
        outs,
        [],
        0,
        0,
    )
    return result if many else result[0]


def aligned(value, step):
    return pl.multiple_of(value * step, step)


def project_kernel(meta, blocks_ref, gain_ref, mine, other, *refs):
    normed_ref, query_ref, pair_ref, weight_ref = refs
    core = meta[0] & 1
    rows = mine.shape[1]

    @pl.when(pl.program_id(0) == 0)
    def _():
        for i in range(4):
            at = 2 * (meta[1] ^ i)
            weight_ref[pl.ds(aligned(at + core, rows), rows), :] = mine[i]
            weight_ref[pl.ds(aligned(at + 1 - core, rows), rows), :] = other[i]

    states = blocks_ref[0].astype(jnp.float32)
    inverse = lax.rsqrt(jnp.mean(states * states, axis=-1, keepdims=True) + norm_eps)
    normed = (states * inverse * gain_ref[...]).astype(jnp.bfloat16)
    normed_ref[0] = normed
    projected = dot_plain(normed, weight_ref[...]).astype(jnp.bfloat16)
    query_width = query_ref.shape[-1]
    query_ref[0] = projected[:, :query_width]
    pair_ref[0] = projected[:, query_width:]


def project(meta, blocks, gain, mine, other, query_width):
    _, token_rows, width = blocks.shape
    columns = mine.shape[2]
    arrays = [blocks, gain, mine, other]
    outs = [
        shape_of((4, token_rows, width), jnp.bfloat16),
        shape_of((4, token_rows, query_width), jnp.bfloat16),
        shape_of((4, token_rows, columns - query_width), jnp.bfloat16),
        shape_of((width, columns), jnp.bfloat16),
    ]
    return call(
        project_kernel,
        "project",
        meta,
        arrays,
        (4,),
        [pl.BlockSpec((1, token_rows, width), lambda r, m: (r, 0, 0))]
        + [whole(a) for a in arrays[1:]],
        [
            pl.BlockSpec((1, token_rows, width), lambda r, m: (r, 0, 0)),
            pl.BlockSpec((1, token_rows, query_width), lambda r, m: (r, 0, 0)),
            pl.BlockSpec((1, token_rows, columns - query_width), lambda r, m: (r, 0, 0)),
            whole(outs[3]),
        ],
        outs,
        [],
        2 * 4 * token_rows * width * columns,
        size_of(arrays) + size_of(outs),
    )


def sort_pairs(meta, mine_ref, other_ref, keys, values):
    half = mine_ref.shape[1] // 2
    for slot in range(16):
        block, part = (slot, 0) if slot < 8 else (15 - slot, 1)
        place = block >> 1
        rows = pl.ds(part * half, half)
        to = pl.ds(slot * half, half)

        @pl.when((meta[0] & 1) == (block & 1))
        def _():
            keys[to, :] = mine_ref[place, rows, :HEAD_SIZE]
            values[to, :] = mine_ref[place, rows, HEAD_SIZE:]

        @pl.when((meta[0] & 1) != (block & 1))
        def _():
            keys[to, :] = other_ref[place, rows, :HEAD_SIZE]
            values[to, :] = other_ref[place, rows, HEAD_SIZE:]


def stack_heads(rows):
    count = rows.shape[1] // HEAD_SIZE
    return jnp.concatenate(
        [rows[:, h * HEAD_SIZE : (h + 1) * HEAD_SIZE] for h in range(count)], axis=0
    )


def unstack_heads(rows, count):
    each = rows.shape[0] // count
    return jnp.concatenate([rows[h * each : (h + 1) * each] for h in range(count)], axis=1)


def step_slot(meta):
    step = pl.program_id(0)
    block = 2 * (step >> 1) + (meta[0] & 1)
    return jnp.where((step & 1) == 0, block, 15 - block)


def allowed_pairs(start, slot, shape, half):
    key_place = start + lax.broadcasted_iota(jnp.int32, shape, 0)
    query_place = slot * half + (lax.broadcasted_iota(jnp.int32, shape, 1) & (half - 1))
    return key_place <= query_place


def key_spans(step, half, span):
    pairs = (step // 2 if step % 2 == 0 else 7 - step // 2) + 1
    rows = pairs * 2 * half
    return [(at, min(span, rows - at)) for at in range(0, rows, span)]


def attend_kernel(scale, span, meta, query_ref, mine_ref, other_ref, *refs):
    out_ref, log_ref, keys, values, values_turned = refs
    half, group_width = query_ref.shape[1:]
    count = group_width // HEAD_SIZE

    @pl.when(pl.program_id(0) == 0)
    def _():
        sort_pairs(meta, mine_ref, other_ref, keys, values)
        values_turned[...] = values[...].T

    slot = step_slot(meta)
    query = stack_heads(query_ref[0])
    wide = count * half

    def run(spans):
        highest = jnp.full((1, wide), masked_score, jnp.float32)
        total = jnp.zeros((1, wide), jnp.float32)
        mixed = jnp.zeros((HEAD_SIZE, wide), jnp.float32)
        for start, size in spans:
            at = pl.ds(start, size)
            scores = dot_last(keys[at, :], query) * scale
            if start == spans[-1][0]:
                seen = allowed_pairs(start, slot, scores.shape, half)
                scores = jnp.where(seen, scores, masked_score)
            new = jnp.maximum(highest, jnp.max(scores, axis=0, keepdims=True))
            rescale = jnp.exp(highest - new)
            powers = jnp.exp(scores - new)
            total = total * rescale + jnp.sum(powers, axis=0, keepdims=True)
            mixed = mixed * rescale + dot_plain(
                values_turned[:, at], powers.astype(jnp.bfloat16)
            )
            highest = new
        log_ref[0] = highest + jnp.log(total)
        out_ref[0] = unstack_heads((mixed / total).T, count).astype(jnp.bfloat16)

    for step in range(8):

        @pl.when(pl.program_id(0) == step)
        def _():
            run(key_spans(step, half, span))


def attend(meta, query, mine, other, scale):
    token_rows, group_width = query.shape[1:]
    half = token_rows // 2
    count = group_width // HEAD_SIZE
    everything = 8 * token_rows
    span = 1024
    arrays = [query, mine, other]
    outs = [
        shape_of(query.shape, jnp.bfloat16),
        shape_of((8, 1, count * half), jnp.float32),
    ]
    return call(
        functools.partial(attend_kernel, scale, span),
        "attend",
        meta,
        arrays,
        (8,),
        [
            pl.BlockSpec((1, half, group_width), lambda i, m: (i // 2, i % 2, 0)),
            whole(mine),
            whole(other),
        ],
        [
            pl.BlockSpec((1, half, group_width), lambda i, m: (i // 2, i % 2, 0)),
            pl.BlockSpec((1, 1, count * half), lambda i, m: (i, 0, 0)),
        ],
        outs,
        [
            pltpu.VMEM((everything, HEAD_SIZE), jnp.bfloat16),
            pltpu.VMEM((everything, HEAD_SIZE), jnp.bfloat16),
            pltpu.VMEM((HEAD_SIZE, everything), jnp.bfloat16),
        ],
        2 * 2 * 4 * token_rows * everything * group_width,
        size_of(arrays) + size_of(outs),
    )


def attend_back_kernel(scale, span, meta, query_ref, mine_ref, other_ref, log_ref, *refs):
    mixed_ref, grad_ref, grad_query_ref, grad_mine_ref, grad_other_ref = refs[:5]
    keys, values, keys_turned, grad_keys, grad_values = refs[5:]
    step = pl.program_id(0)
    half, group_width = query_ref.shape[1:]
    count = group_width // HEAD_SIZE

    @pl.when(step == 0)
    def _():
        sort_pairs(meta, mine_ref, other_ref, keys, values)
        keys_turned[...] = keys[...].T
        grad_keys[...] = jnp.zeros_like(grad_keys)
        grad_values[...] = jnp.zeros_like(grad_values)

    slot = step_slot(meta)
    query = stack_heads(query_ref[0])
    mixed = stack_heads(mixed_ref[0]).astype(jnp.float32)
    grad = stack_heads(grad_ref[0])
    delta = jnp.sum((mixed * grad.astype(jnp.float32)).T, axis=0, keepdims=True)
    log_total = log_ref[0]

    def run(spans):
        grad_turned = jnp.zeros((HEAD_SIZE, count * half), jnp.float32)
        for start, size in spans:
            at = pl.ds(start, size)
            scores = dot_last(keys[at, :], query) * scale
            probs = jnp.exp(scores - log_total)
            if start == spans[-1][0]:
                probs = jnp.where(allowed_pairs(start, slot, probs.shape, half), probs, 0.0)
            grad_probs = dot_last(values[at, :], grad)
            grad_scores = (probs * (grad_probs - delta)).astype(jnp.bfloat16)
            grad_values[at, :] += dot_plain(probs.astype(jnp.bfloat16), grad)
            grad_keys[at, :] += dot_plain(grad_scores, query)
            grad_turned += dot_plain(keys_turned[:, at], grad_scores)
        grad_query_ref[0] = unstack_heads((grad_turned * scale).T, count).astype(jnp.bfloat16)

    for at_step in range(8):

        @pl.when(step == at_step)
        def _():
            run(key_spans(at_step, half, span))

    @pl.when(step == 7)
    def _():
        for slot_at in range(16):
            block, part = (slot_at, 0) if slot_at < 8 else (15 - slot_at, 1)
            place = block >> 1
            rows = pl.ds(part * half, half)
            here = pl.ds(slot_at * half, half)
            both = jnp.concatenate([grad_keys[here, :] * scale, grad_values[here, :]], axis=1)

            @pl.when((meta[0] & 1) == (block & 1))
            def _():
                grad_mine_ref[place, rows, :] = both

            @pl.when((meta[0] & 1) != (block & 1))
            def _():
                grad_other_ref[place, rows, :] = both.astype(jnp.bfloat16)


def attend_back(meta, query, mine, other, log_total, mixed, grad, scale):
    token_rows, group_width = query.shape[1:]
    half = token_rows // 2
    count = group_width // HEAD_SIZE
    everything = 8 * token_rows
    span = 512
    arrays = [query, mine, other, log_total, mixed, grad]
    outs = [
        shape_of(query.shape, jnp.bfloat16),
        shape_of(mine.shape, jnp.float32),
        shape_of(mine.shape, jnp.bfloat16),
    ]
    return call(
        functools.partial(attend_back_kernel, scale, span),
        "attend_back",
        meta,
        arrays,
        (8,),
        [
            pl.BlockSpec((1, half, group_width), lambda i, m: (i // 2, i % 2, 0)),
            whole(mine),
            whole(other),
            pl.BlockSpec((1, 1, count * half), lambda i, m: (i, 0, 0)),
            pl.BlockSpec((1, half, group_width), lambda i, m: (i // 2, i % 2, 0)),
            pl.BlockSpec((1, half, group_width), lambda i, m: (i // 2, i % 2, 0)),
        ],
        [
            pl.BlockSpec((1, half, group_width), lambda i, m: (i // 2, i % 2, 0)),
            whole(outs[1]),
            whole(outs[2]),
        ],
        outs,
        [
            pltpu.VMEM((everything, HEAD_SIZE), jnp.bfloat16),
            pltpu.VMEM((everything, HEAD_SIZE), jnp.bfloat16),
            pltpu.VMEM((HEAD_SIZE, everything), jnp.bfloat16),
            pltpu.VMEM((everything, HEAD_SIZE), jnp.float32),
            pltpu.VMEM((everything, HEAD_SIZE), jnp.float32),
        ],
        5 * 2 * 4 * token_rows * everything * group_width,
        size_of(arrays) + size_of(outs),
    )


def leave_kernel(meta, *refs):
    parts, mine, other, states_ref, gain_ref = refs[:4], *refs[4:8]
    weight_ref, middle_ref, normed_ref = refs[8:]
    core, chip = meta[0] & 1, meta[0] >> 1
    rows = mine.shape[1]
    for i in range(4):
        weight_ref[pl.ds(aligned(2 * i + core, rows), rows), :] = mine[i]
        weight_ref[pl.ds(aligned(2 * i + 1 - core, rows), rows), :] = other[i]
    middle = states_ref[...].astype(jnp.float32)
    for r in range(4):
        at = pl.ds(aligned(chip ^ r, 2 * rows), 2 * rows)
        middle += dot_plain(parts[r][...], weight_ref[at, :])
    middle_ref[...] = middle
    inverse = lax.rsqrt(jnp.mean(middle * middle, axis=-1, keepdims=True) + norm_eps)
    normed_ref[...] = (middle * inverse * gain_ref[...]).astype(jnp.bfloat16)


def leave(meta, parts, mine, other, states, gain):
    token_rows, width = states.shape
    arrays = list(parts) + [mine, other, states, gain]
    outs = [
        shape_of((8 * mine.shape[1], width), jnp.bfloat16),
        shape_of((token_rows, width), jnp.float32),
        shape_of((token_rows, width), jnp.bfloat16),
    ]
    return call(
        leave_kernel,
        "leave",
        meta,
        arrays,
        (1,),
        [whole(a) for a in arrays],
        [whole(a) for a in outs],
        outs,
        [],
        2 * token_rows * width * width,
        size_of(arrays) + size_of(outs),
    )


def norm_back_rows(grad_normed, states, gain):
    inverse = lax.rsqrt(jnp.mean(states * states, axis=-1, keepdims=True) + norm_eps)
    scaled = states * inverse
    gain_grad = jnp.sum(grad_normed * scaled, axis=0, keepdims=True)
    grad_scaled = grad_normed * gain
    shift = jnp.mean(grad_scaled * scaled, axis=-1, keepdims=True)
    return inverse * (grad_scaled - scaled * shift), gain_grad


def enter_back_kernel(meta, final_ref, normed_ref, middle_ref, gain_ref, weight_ref, *refs):
    grad_ref, branch_ref, gain_grad_ref, mixed_ref = refs
    grad, gain_grad = norm_back_rows(normed_ref[...], middle_ref[...], gain_ref[...])
    grad = grad + final_ref[...]
    grad_ref[...] = grad
    gain_grad_ref[...] = gain_grad
    branch = grad.astype(jnp.bfloat16)
    branch_ref[...] = branch
    rows = weight_ref.shape[0] // 4
    for r in range(4):
        mixed_ref[r] = dot_last(branch, weight_ref[rows * r : rows * (r + 1), :]).astype(
            jnp.bfloat16
        )


def enter_back(meta, grad_final, grad_normed, middle, gain, weight):
    token_rows, width = middle.shape
    arrays = [grad_final, grad_normed, middle, gain, weight]
    outs = [
        shape_of((token_rows, width), jnp.float32),
        shape_of((token_rows, width), jnp.bfloat16),
        shape_of((1, width), jnp.float32),
        shape_of((4, token_rows, weight.shape[0] // 4), jnp.bfloat16),
    ]
    return call(
        enter_back_kernel,
        "enter_back",
        meta,
        arrays,
        (1,),
        [whole(a) for a in arrays],
        [whole(a) for a in outs],
        outs,
        [],
        2 * token_rows * width * width,
        size_of(arrays) + size_of(outs),
    )


def finish_kernel(meta, *refs):
    parts, mine, other = refs[:3]
    states_ref, middle_ref, gain_ref, grad_ref, gain_grad_ref, total = refs[3:]
    core, chip = meta[0] & 1, meta[0] >> 1
    columns = mine.shape[1]
    for at, weights in ((core, mine), (1 - core, other)):
        total[:, pl.ds(aligned(at, columns), columns)] = sum(
            dot_last(parts[r], weights[chip ^ r]) for r in range(4)
        )
    grad, gain_grad = norm_back_rows(
        total[...], states_ref[...].astype(jnp.float32), gain_ref[...]
    )
    grad_ref[0] = grad + middle_ref[...]
    gain_grad_ref[...] = gain_grad


def finish(meta, parts, mine, other, states, grad_middle, gain):
    token_rows, width = states.shape
    arrays = [parts, mine, other, states, grad_middle, gain]
    outs = [
        shape_of((1, token_rows, width), jnp.float32),
        shape_of((1, width), jnp.float32),
    ]
    return call(
        finish_kernel,
        "finish",
        meta,
        arrays,
        (1,),
        [whole(a) for a in arrays],
        [whole(a) for a in outs],
        outs,
        [pltpu.VMEM((token_rows, width), jnp.float32)],
        2 * token_rows * width * 4 * parts.shape[2],
        size_of(arrays) + size_of(outs),
    )


def gated(gate_up, units):
    gate_part = gate_up[:, :units]
    sigma = 1.0 / (1.0 + jnp.exp(-gate_part))
    return gate_part * sigma * gate_up[:, units:]


def gated_back(grad_act, gate_up, units):
    gate_part = gate_up[:, :units].astype(jnp.float32)
    up_part = gate_up[:, units:].astype(jnp.float32)
    sigma = 1.0 / (1.0 + jnp.exp(-gate_part))
    linear = gate_part * sigma
    grad_gate = grad_act * up_part * (sigma * (1.0 + gate_part * (1.0 - sigma)))
    return grad_gate, grad_act * linear, linear * up_part


def experts_kernel(
    meta, rows_ref, gates_ref, expert_ref, shared_ref, gate_up_ref, shared_gate_up_ref, out_ref, total
):
    expert = pl.program_id(0)
    rows = rows_ref[...]

    @pl.when(expert == 0)
    def _():
        units = shared_ref.shape[1] // 3
        gate_up = dot_plain(rows, shared_ref[:, : 2 * units])
        shared_gate_up_ref[...] = gate_up.astype(jnp.bfloat16)
        act = gated(gate_up, units).astype(jnp.bfloat16)
        total[...] = dot_last(act, shared_ref[:, 2 * units :])

    gate_up = dot_plain(rows, expert_ref[0, :, : 2 * F])
    gate_up_ref[0] = gate_up.astype(jnp.bfloat16)
    act = (gated(gate_up, F) * gates_ref[0]).astype(jnp.bfloat16)
    total[...] += dot_last(act, expert_ref[0, :, 2 * F :])

    @pl.when(expert == pl.num_programs(0) - 1)
    def _():
        out_ref[...] = total[...].astype(jnp.bfloat16)


def experts(meta, rows, gates, expert_weight, shared_slice):
    local_experts, width, _ = expert_weight.shape
    token_rows = rows.shape[0]
    shared_units = shared_slice.shape[1] // 3
    arrays = [rows, gates, expert_weight, shared_slice]
    outs = [
        shape_of((local_experts, token_rows, 2 * F), jnp.bfloat16),
        shape_of((token_rows, 2 * shared_units), jnp.bfloat16),
        shape_of((token_rows, width), jnp.bfloat16),
    ]
    return call(
        experts_kernel,
        "experts",
        meta,
        arrays,
        (local_experts,),
        [
            whole(rows),
            pl.BlockSpec((1, token_rows, 1), lambda e, m: (e, 0, 0)),
            pl.BlockSpec((1, width, 3 * F), lambda e, m: (e, 0, 0)),
            whole(shared_slice),
        ],
        [
            pl.BlockSpec((1, token_rows, 2 * F), lambda e, m: (e, 0, 0)),
            whole(outs[1]),
            whole(outs[2]),
        ],
        outs,
        [pltpu.VMEM((token_rows, width), jnp.float32)],
        2 * token_rows * width * 3 * (F * local_experts + shared_units),
        size_of(arrays) + size_of(outs),
    )


def experts_back_kernel(
    meta,
    grad_ref,
    gates_ref,
    gate_up_ref,
    shared_gate_up_ref,
    expert_ref,
    shared_ref,
    grad_gate_up_ref,
    act_ref,
    shared_grad_ref,
    shared_act_ref,
    grad_rows_ref,
    total,
):
    expert = pl.program_id(0)
    grad = grad_ref[...]

    @pl.when(expert == 0)
    def _():
        units = shared_ref.shape[1] // 3
        grad_act = dot_plain(grad, shared_ref[:, 2 * units :])
        grad_gate, grad_up, act = gated_back(grad_act, shared_gate_up_ref[...], units)
        both = jnp.concatenate([grad_gate, grad_up], axis=1).astype(jnp.bfloat16)
        shared_grad_ref[0] = both
        shared_act_ref[0] = act.astype(jnp.bfloat16)
        total[...] = dot_last(both, shared_ref[:, : 2 * units])

    grad_act = dot_plain(grad, expert_ref[0, :, 2 * F :]) * gates_ref[0]
    grad_gate, grad_up, act = gated_back(grad_act, gate_up_ref[0], F)
    both = jnp.concatenate([grad_gate, grad_up], axis=1).astype(jnp.bfloat16)
    grad_gate_up_ref[0] = both
    act_ref[0] = (act * gates_ref[0]).astype(jnp.bfloat16)
    total[...] += dot_last(both, expert_ref[0, :, : 2 * F])

    @pl.when(expert == pl.num_programs(0) - 1)
    def _():
        grad_rows_ref[...] = total[...].astype(jnp.bfloat16)


def experts_back(meta, grad, gates, gate_up, shared_gate_up, expert_weight, shared_slice):
    local_experts, width, _ = expert_weight.shape
    token_rows = grad.shape[0]
    shared_units = shared_slice.shape[1] // 3
    arrays = [grad, gates, gate_up, shared_gate_up, expert_weight, shared_slice]
    outs = [
        shape_of((local_experts, token_rows, 2 * F), jnp.bfloat16),
        shape_of((local_experts, token_rows, F), jnp.bfloat16),
        shape_of((1, token_rows, 2 * shared_units), jnp.bfloat16),
        shape_of((1, token_rows, shared_units), jnp.bfloat16),
        shape_of((token_rows, width), jnp.bfloat16),
    ]
    return call(
        experts_back_kernel,
        "experts_back",
        meta,
        arrays,
        (local_experts,),
        [
            whole(grad),
            pl.BlockSpec((1, token_rows, 1), lambda e, m: (e, 0, 0)),
            pl.BlockSpec((1, token_rows, 2 * F), lambda e, m: (e, 0, 0)),
            whole(shared_gate_up),
            pl.BlockSpec((1, width, 3 * F), lambda e, m: (e, 0, 0)),
            whole(shared_slice),
        ],
        [
            pl.BlockSpec((1, token_rows, 2 * F), lambda e, m: (e, 0, 0)),
            pl.BlockSpec((1, token_rows, F), lambda e, m: (e, 0, 0)),
            whole(outs[2]),
            whole(outs[3]),
            whole(outs[4]),
        ],
        outs,
        [pltpu.VMEM((token_rows, width), jnp.float32)],
        2 * token_rows * width * 3 * (F * local_experts + shared_units),
        size_of(arrays) + size_of(outs),
    )


def weight_grad_kernel(pairs, core_at, meta, *refs):
    keep_ref, give_ref = refs[-2:]
    at = 0
    columns = 0
    parts = []
    for count in pairs:
        lefts, rights = refs[at : at + count], refs[at + count : at + 2 * count]
        at += 2 * count
        parts.append(
            sum(dot_first(a[...], b[0]) for a, b in zip(lefts, rights)).astype(jnp.bfloat16)
        )
    half = keep_ref.shape[1]

    for core, (first, second) in ((0, (keep_ref, give_ref)), (1, (give_ref, keep_ref))):

        @pl.when((meta[core_at] & 1) == core)
        def _():
            start = 0
            for part in parts:
                stop = start + part.shape[1]
                first[0, :, start:stop] = part[:half]
                second[0, :, start:stop] = part[half:]
                start = stop


def expert_grad_kernel(count, meta, *refs):
    rows, grads, front, acts = (refs[i * count : (i + 1) * count] for i in range(4))
    out_ref = refs[-1] if len(refs) == 4 * count + 1 else refs[-2]
    tile = rows[0].shape[1]
    both = 3 * F

    def pair(front_refs, act_refs):
        return [
            sum(dot_first(a[...], b[0]) for a, b in zip(left, right)).astype(jnp.bfloat16)
            for left, right in ((rows, front_refs), (grads, act_refs))
        ]

    left, right = pair(front, acts)
    out_ref[0, :tile, : left.shape[1]] = left
    out_ref[0, :tile, left.shape[1] : both] = right
    if len(refs) > 4 * count + 1:
        held = refs[-1]
        left, right = pair(refs[4 * count : 5 * count], refs[5 * count : 6 * count])
        split, columns = left.shape[1], left.shape[1] + right.shape[1]
        held[:, :split] = left
        held[:, split:] = right
        quarter = tile // 4
        first = 2 * meta[2]
        out_ref[0, tile:, :columns] = held[pl.ds(aligned(first, quarter), quarter), :]
        out_ref[0, tile:, columns:] = held[pl.ds(aligned(first + 1, quarter), quarter), :]


def expert_grad(meta, expert, half, rows, grads, front, acts, shared=None):
    count = len(rows)
    token_rows, width = rows[0].shape
    tile = width // 4
    arrays = list(rows) + list(grads) + list(front) + list(acts)
    column = pl.BlockSpec((token_rows, tile), lambda i, m: (0, i ^ m[0]))

    def of_expert(a):
        return pl.BlockSpec((1,) + a.shape[1:], lambda i, m: (m[1], 0, 0))

    in_specs = [column] * (2 * count) + [of_expert(a) for a in arrays[2 * count :]]
    below, scratch = 0, []
    if shared is not None:
        arrays += list(shared[0]) + list(shared[1])
        in_specs += [whole(a) for a in arrays[4 * count :]]
        below = tile // 4
        columns = shared[0][0].shape[-1] + shared[1][0].shape[-1]
        scratch = [pltpu.VMEM((tile, columns), jnp.bfloat16)]
    return call(
        functools.partial(expert_grad_kernel, count),
        "expert_grad",
        jnp.stack([meta[0] >> 1, expert, half]),
        arrays,
        (4,),
        in_specs,
        pl.BlockSpec((1, tile + below, 3 * F), lambda i, m: (i, 0, 0)),
        shape_of((4, tile + below, 3 * F), jnp.bfloat16),
        scratch,
        0,
        0,
    )


def weight_grad(meta, order, operands, index):
    token_rows, width = operands[0][0][0].shape
    tile = width // 4
    scalars = jnp.stack([order, meta[0]])
    arrays, in_specs, columns = [], [], 0
    for lefts, rights in operands:
        arrays += list(lefts) + list(rights)
        in_specs += [pl.BlockSpec((token_rows, tile), lambda i, m: (0, i ^ m[0]))] * len(lefts)
        units = rights[0].shape[-1]
        at = index if rights[0].shape[0] > 1 else 0
        in_specs += [
            pl.BlockSpec((1, token_rows, units), lambda i, m, at=at: (at, 0, 0))
        ] * len(rights)
        columns += units
    tokens = token_rows * len(operands[0][0])
    counts = [len(left) for left, _ in operands]
    outs = [shape_of((4, tile // 2, columns), jnp.bfloat16)] * 2
    return call(
        functools.partial(weight_grad_kernel, counts, 1),
        "weight_grad",
        scalars,
        arrays,
        (4,),
        in_specs,
        [pl.BlockSpec((1, tile // 2, columns), lambda i, m: (i, 0, 0))] * 2,
        outs,
        [],
        2 * tokens * width * columns,
        size_of(outs) + 4 * tokens * width + 2 * tokens * columns,
    )


def place_sum_kernel(meta, *refs):
    rows = refs[-1].shape[1]
    refs[-1][0] = refs[-2][0, :rows].astype(jnp.float32)


def place_sum(meta, total, index, of_other, shape, value):
    _, rows, columns = value.shape
    arrays = [value]
    in_specs = [pl.BlockSpec((1, rows, columns), lambda r, m: (r, 0, 0))]
    aliases = {}
    if total is not None:
        arrays = [total] + arrays
        in_specs = [pl.BlockSpec(memory_space=pl.ANY)] + in_specs
        aliases = {1: 0}
    return pl.pallas_call(
        place_sum_kernel,
        grid_spec=pltpu.PrefetchScalarGridSpec(
            num_scalar_prefetch=1,
            grid=(4,),
            in_specs=in_specs,
            out_specs=pl.BlockSpec(
                (1, shape[1] // 4, shape[2]),
                lambda r, m: (2 * ((m[0] & 1) ^ of_other) + index, (m[0] >> 1) ^ r, 0),
            ),
        ),
        out_shape=shape_of(shape, jnp.float32),
        input_output_aliases=aliases,
        compiler_params=pltpu.CompilerParams(vmem_limit_bytes=48 * 1024 * 1024),
        cost_estimate=pl.CostEstimate(
            flops=int(COSTS.get("place_sum", 1.0) * 1e9), bytes_accessed=1000, transcendentals=0
        ),
        name="place_sum",
    )(meta, *arrays)


def place_shared_kernel(meta, mine_low, mine_high, other_low, other_high, out_ref):
    core = meta[0] & 1
    rows = mine_low.shape[1]
    for at, low, high in ((core, mine_low, mine_high), (1 - core, other_low, other_high)):
        out_ref[pl.ds(aligned(2 * at, rows), rows), :] = low[0].astype(jnp.float32)
        out_ref[pl.ds(aligned(2 * at + 1, rows), rows), :] = high[0].astype(jnp.float32)


def place_shared(meta, mine, other):
    _, rows, columns = mine.shape
    units = columns // 6
    low = pl.BlockSpec((1, rows, units), lambda i, j, m: (i, 0, j))
    high = pl.BlockSpec((1, rows, units), lambda i, j, m: (i, 0, 3 + j))
    outs = shape_of((4 * rows, 2 * columns), jnp.float32)
    return call(
        place_shared_kernel,
        "place_shared",
        meta,
        [mine, mine, other, other],
        (4, 3),
        [low, high, low, high],
        pl.BlockSpec((4 * rows, units), lambda i, j, m: (0, 4 * j + (m[1] ^ i))),
        outs,
        [],
        0,
        0,
    )


def place_heads_kernel(meta, *refs):
    mine, other, out_ref = refs[:4], refs[4], refs[5]
    core, chip = meta[0] & 1, meta[0] >> 1
    rows, columns = mine[0].shape
    group_width = columns - 2 * HEAD_SIZE
    for r in range(4):
        head = chip ^ r
        for at, pieces in ((core, [piece[...] for piece in mine]), (1 - core, other)):
            to = pl.ds(aligned(at, rows), rows)
            values = pieces[r].astype(jnp.float32)
            out_ref[to, pl.ds(aligned(head, group_width), group_width)] = values[:, :group_width]
            out_ref[to, pl.ds(aligned(4 * group_width // HEAD_SIZE + head, HEAD_SIZE), HEAD_SIZE)] = (
                values[:, group_width : group_width + HEAD_SIZE]
            )
            out_ref[
                to, pl.ds(aligned(4 * group_width // HEAD_SIZE + 4 + head, HEAD_SIZE), HEAD_SIZE)
            ] = values[:, group_width + HEAD_SIZE :]


def place_heads(meta, mine, other):
    rows, columns = mine[0].shape
    arrays = list(mine) + [other]
    outs = shape_of((2 * rows, 4 * columns), jnp.float32)
    return call(
        place_heads_kernel,
        "place_heads",
        meta,
        arrays,
        (1,),
        [whole(a) for a in arrays],
        whole(outs),
        outs,
        [],
        0,
        size_of(arrays + [outs]),
    )


def join_shared_kernel(meta, mine, other, out_ref):
    step = pl.program_id(0)
    rows = mine.shape[2]
    first = meta[0] ^ (2 * step)
    for i in range(4):
        at = 8 * (meta[1] ^ i)
        out_ref[pl.ds(aligned(at + first, rows), rows), :] = mine[0, i]
        out_ref[pl.ds(aligned(at + (first ^ 1), rows), rows), :] = other[0, i]


def join_shared(meta, mine, other):
    _, _, rows, columns = mine.shape
    block = pl.BlockSpec((1, 4, rows, columns), lambda r, m: (r, 0, 0, 0))
    outs = shape_of((32 * rows, columns), jnp.bfloat16)
    return call(
        join_shared_kernel,
        "join_shared",
        meta,
        [mine, other],
        (4,),
        [block, block],
        whole(outs),
        outs,
        [],
        0,
        size_of([mine, other, outs]),
    )


class Clock:
    def __init__(self):
        self.last = None

    def __call__(self, *values):
        if self.last is None:
            return values if len(values) > 1 else values[0]
        held = lax.optimization_barrier(tuple(values) + (self.last,))[:-1]
        return held if len(held) > 1 else held[0]

    def mark(self, value):
        self.last = value
        return value


EARLY = (
    "H", "W", "K", "S", "K", "W", "S", "W", "K", "S", "O", "S", "M", "M", "S", "O", "M", "S", "M", "R", "M", "K", "M", "K",
    "M", "K", "R", "M", "K", "M", "M", "M", "M", "R", "M", "M",
)
LATE = (
    "L", "0", "1", "0", "0", "L", "1", "1", "L", "L", "O", "0", "1", "L", "0", "L", "1", "O", "Q", "1", "O", "0", "L", "Q",
    "O", "L", "Q", "Q", "O", "Q", "L", "1", "0", "O", "Q", "S", "1", "0", "L", "O", "Q", "1", "S", "L", "0", "O", "Q", "L",
    "Q", "O", "S",
)


def fast_device(
    hidden,
    teacher,
    valid_mask,
    routes,
    route_gates,
    gain_in,
    query_key_value_weight,
    out_weight,
    gain_mid,
    shared_weight,
    expert_weight,
):
    token_rows, width = hidden.shape[1:]
    context_count, shard_count = 8, 4
    context_index = lax.axis_index("ctx").astype(jnp.int32)
    shard_index = lax.axis_index("wt").astype(jnp.int32)
    plain_meta = jnp.stack([context_index, shard_index])
    core = context_index & 1
    chip = context_index >> 1
    at_end = (shard_index == 0) | (shard_index == shard_count - 1)
    group_width = QUERY_HEADS // KEY_VALUE_HEADS * HEAD_SIZE
    query_width = QUERY_HEADS * HEAD_SIZE
    kv_width = KEY_VALUE_HEADS * HEAD_SIZE
    scale = 1.0 / math.sqrt(HEAD_SIZE)
    all_tokens = token_rows * context_count * shard_count
    shard_rows = query_key_value_weight.shape[0]
    half_rows = shard_rows // 2
    local_experts = expert_weight.shape[0]
    bf16, f32 = jnp.bfloat16, jnp.float32
    states = hidden[0]
    clock = Clock()
    have = {}

    def meta():
        return clock(plain_meta)

    def now(*values):
        return clock(*values)

    def ready(*values):
        values = clock(*values)
        clock.mark(values[0] if isinstance(values, tuple) or isinstance(values, list) else values)
        return values


    def hidden_chain():
        have["blocks"] = chips_exchange(jnp.broadcast_to(states, (4,) + states.shape))
        yield

    def qkv_chain():
        rows = lax.dynamic_slice_in_dim(query_key_value_weight, core * half_rows, half_rows, 0)
        half = jnp.concatenate(
            [
                lax.dynamic_slice_in_dim(rows, chip * group_width, group_width, 1),
                lax.dynamic_slice_in_dim(rows, query_width + chip * HEAD_SIZE, HEAD_SIZE, 1),
                lax.dynamic_slice_in_dim(
                    rows, query_width + kv_width + chip * HEAD_SIZE, HEAD_SIZE, 1
                ),
            ],
            axis=1,
        )
        came = line_swap(half, 1)
        yield
        pair = clock.mark(jnp.stack([half, now(came)]))
        came = line_swap(pair, 2)
        yield
        have["qkv_mine"] = clock.mark(jnp.concatenate([pair, now(came)]))
        have["qkv_other"] = flip(have["qkv_mine"], 1)
        yield

    def small_chain():
        expert_ids = jnp.arange(EXPERTS, dtype=jnp.int32)
        matrix = jnp.sum(
            jnp.where(
                routes[0][None, :, :] == expert_ids[:, None, None], route_gates[0][None, :, :], 0.0
            ),
            axis=-1,
        )
        have["valid"] = valid_mask[0].astype(f32)
        gains = jnp.concatenate([gain_in, gain_mid]).astype(f32).reshape(-1, token_rows)
        gain_rows = gains.shape[0]
        filled = EXPERTS + gain_rows
        pack = jnp.concatenate(
            [
                matrix,
                gains,
                jnp.full((32 - filled, token_rows), jnp.sum(have["valid"]), f32),
            ]
        )
        came = line_swap(pack, 1)
        yield
        pair = clock.mark(jnp.stack([pack, now(came)]))
        came = line_swap(pair, 2)
        yield
        all_packs = clock.mark(jnp.concatenate([pair, now(came)]))
        have["gates"] = [
            lax.dynamic_slice_in_dim(
                all_packs[i], shard_index * local_experts, local_experts, 0
            )[..., None]
            for i in range(4)
        ]
        gains = all_packs[:, EXPERTS:filled].reshape(4, 2, shard_rows)
        gains = jnp.stack([pick(gains, shard_index ^ i) for i in range(4)], axis=1)
        have["gains"] = gains.reshape(2, 1, width)
        total = jnp.broadcast_to(jnp.sum(all_packs[:, filled, 0]), (8, 128))
        yield
        total = now(total)
        for bit in (1, 2, 4):
            came = flip(total, bit)
            yield
            total = clock.mark(total + now(came))
        have["count"] = total[0, 0]
        yield

    def shared_chain():
        eighth = shard_rows // 8
        units = SF // shard_count
        piece = lax.dynamic_slice_in_dim(shared_weight, context_index * eighth, eighth, 0)
        piece = piece.reshape(eighth, 3, shard_count, units)

        piece = jnp.transpose(piece, (2, 0, 1, 3)).reshape(shard_count, eighth, 3 * units)
        parts = [pick(piece, shard_index ^ i) for i in range(4)]
        came = line_swap(now(jnp.stack([parts[1], parts[3]])), 1)
        yield
        came = now(came)
        mine = jnp.stack([parts[0], came[0]])
        came = line_swap(clock.mark(jnp.stack([parts[2], came[1]])), 2)
        yield
        pieces = clock.mark(jnp.concatenate([mine, now(came)]))
        came = flip(pieces, 2)
        yield
        pair = clock.mark(jnp.stack([pieces, now(came)]))
        came = flip(pair, 4)
        yield
        mine = clock.mark(jnp.concatenate([pair, now(came)]))
        other = flip(mine, 1)
        yield
        have["shared"] = join_shared(meta(), mine, other)
        clock.mark(have["shared"])
        yield

    def out_chain():
        half = lax.dynamic_slice_in_dim(now(out_weight), core * half_rows, half_rows, 0)
        came = line_exchange(jnp.broadcast_to(half, (4,) + half.shape))
        yield
        have["out_mine"] = clock.mark(now(came))
        have["out_other"] = flip(have["out_mine"], 1)
        yield

    def qkv_all_chain():
        half = lax.dynamic_slice_in_dim(
            now(have["qkv_slice"]), core * (width // 2), width // 2, 0
        )
        came = flip(half, 2)
        yield
        pair = clock.mark(jnp.stack([half, now(came)]))
        came = flip(pair, 4)
        yield
        have["rel_mine"] = clock.mark(jnp.concatenate([pair, now(came)]))
        have["rel_other"] = flip(have["rel_mine"], 1)
        yield

    def main_chain():
        gains = have["gains"]
        normed_in, query, pair, qkv_slice = project(
            meta(), have["blocks"], gains[0], have["qkv_mine"], have["qkv_other"], group_width
        )
        clock.mark(pair)
        have["normed_in"], have["qkv_slice"] = normed_in, qkv_slice
        pair_other = flip(pair, 1)
        yield
        mixed_heads, log_total = attend(meta(), query, pair, pair_other, scale)
        clock.mark(log_total)
        have["attend"] = (query, pair, pair_other, log_total, mixed_heads)
        parts = ready(*[pick(mixed_heads, chip ^ r) for r in range(4)])
        mixed = [parts[0]] + [flip(parts[r], 2 * r) for r in (1, 2, 3)]
        have["mixed"] = mixed
        yield
        out_full, middle, normed_mid = leave(
            meta(), mixed, have["out_mine"], have["out_other"], states, gains[1]
        )
        have["out_full"], have["middle"] = out_full, middle
        clock.mark(normed_mid)

        near, center = line_swap(normed_mid, 1), line_middle(normed_mid)
        yield
        gates, shared_slice = have["gates"], have["shared"]
        gate_ups, shared_gate_ups, outs = [], [], []

        def forward(rows, i):
            result = experts(meta(), rows, gates[i], expert_weight, shared_slice)
            clock.mark(result[2])
            gate_ups.append(result[0])
            shared_gate_ups.append(result[1])
            outs.append(result[2])

        forward(normed_mid, 0)
        yield
        near, center = now(near, center)
        far, outward = line_middle(near), line_outward(center)
        forward(near, 1)
        yield
        far, outward = now(far, outward)
        outward_far = line_outward(far)
        third = clock.mark(jnp.where(at_end, outward, far))
        forward(third, 2)
        yield
        outward_far = now(outward_far)
        fourth = clock.mark(jnp.where(at_end, outward_far, center))
        forward(fourth, 3)
        line_rows = [normed_mid, near, third, fourth]
        came = line_inward(outs[3])
        yield
        carried = clock.mark(outs[2] + now(came))
        inward, crossed = line_inward(carried), line_middle(carried)
        yield
        inward, crossed = now(inward, crossed)
        near_out, middle_out = ready(outs[1] + crossed, outs[3] + inward)
        near_out, middle_out = line_swap(near_out, 1), line_middle(middle_out)
        yield
        near_out, middle_out = now(near_out, middle_out)
        final_state = (
            middle + outs[0].astype(f32) + near_out.astype(f32) + middle_out.astype(f32)
        )
        valid = have["valid"]
        deviation = final_state - teacher[0].astype(f32)
        have["squared"] = jnp.sum(valid[:, None] * deviation * deviation)
        grad_final = all_tokens / have["count"] * valid[:, None] * deviation
        have["final"], have["grad_final"] = final_state.astype(bf16)[None], grad_final
        grad_low = clock.mark(grad_final.astype(bf16))
        near, center = line_swap(grad_low, 1), line_middle(grad_low)
        yield
        kept = []

        def backward(grads, i):
            kept.append(
                experts_back(
                    meta(),
                    grads,
                    gates[i],
                    gate_ups[i],
                    shared_gate_ups[i],
                    expert_weight,
                    shared_slice,
                )
            )
            clock.mark(kept[-1][4])

        backward(grad_low, 0)
        yield
        near, center = now(near, center)
        far, outward = line_middle(near), line_outward(center)
        backward(near, 1)
        yield
        far, outward = now(far, outward)
        outward_far = line_outward(far)
        third = clock.mark(jnp.where(at_end, outward, far))
        backward(third, 2)
        yield
        outward_far = now(outward_far)
        fourth = clock.mark(jnp.where(at_end, outward_far, center))
        backward(fourth, 3)
        have["line"] = (line_rows, [grad_low, near, third, fourth])
        have["experts"] = list(zip(*kept))
        yield


    def states_chain():
        outs = have["experts"][4]
        came = line_inward(outs[3])
        yield
        carried = clock.mark(outs[2] + now(came))
        inward, crossed = line_inward(carried), line_middle(carried)
        yield
        inward, crossed = now(inward, crossed)
        near_out, middle_out = ready(outs[1] + crossed, outs[3] + inward)
        near_out, middle_out = line_swap(near_out, 1), line_middle(middle_out)
        yield
        near_out, middle_out = now(near_out, middle_out)
        grad_normed = clock.mark(
            outs[0].astype(f32) + near_out.astype(f32) + middle_out.astype(f32)
        )
        grad_middle, grad_branch, grad_gain_mid, grad_mixed = enter_back(
            meta(),
            have["grad_final"],
            grad_normed,
            have["middle"],
            have["gains"][1],
            have["out_full"],
        )
        clock.mark(grad_branch)
        have["grad_branch"], have["grad_gain_mid"] = grad_branch, grad_gain_mid
        grad_mixed = chips_exchange(ready(grad_mixed))
        yield
        query, pair, pair_other, log_total, mixed_heads = have["attend"]
        grad_query, grad_pair, grad_other = attend_back(
            meta(), query, pair, pair_other, log_total, mixed_heads, grad_mixed, scale
        )
        clock.mark(grad_query)
        came = flip(grad_other, 1)
        yield
        grad_pair = grad_pair + now(came).astype(f32)
        projected = clock.mark(jnp.concatenate([grad_query, grad_pair.astype(bf16)], axis=-1))
        have["grad_projected"] = projected
        parts = chips_exchange(ready(projected))
        yield
        grad_hidden, grad_gain_in = finish(
            meta(),
            parts,
            have["rel_mine"],
            have["rel_other"],
            states,
            grad_middle,
            have["gains"][0],
        )
        clock.mark(grad_gain_in)
        have["grad_hidden"] = grad_hidden
        sums = jnp.concatenate(
            [grad_gain_in, have["grad_gain_mid"], jnp.full((6, width), have["squared"], f32)],
            axis=0,
        )
        for offset in (1, 2):
            came = line_swap(sums, offset)
            yield
            sums = clock.mark(sums + now(came))
        for bit in (1, 2, 4):
            came = flip(sums, bit)
            yield
            sums = clock.mark(sums + now(came))
        own = lax.dynamic_slice_in_dim(sums, shard_index * shard_rows, shard_rows, 1)
        have["sums"] = (own, 0.5 * sums[2, 0] / (have["count"] * width))
        yield

    def expert_chain(index):
        line_rows, line_grads = have["line"]
        grad_gate_ups, acts, shared_grads, shared_acts = have["experts"][:4]
        shared = (shared_grads, shared_acts) if index == 0 else None

        def grad_of(at):
            return clock.mark(
                expert_grad(
                    meta(),
                    2 * at + index,
                    at,
                    line_rows,
                    line_grads,
                    grad_gate_ups,
                    acts,
                    shared,
                )
            )

        came = flip(grad_of(1 - core), 1)
        yield
        keep = grad_of(core)
        yield
        x_first = index % 2 == 0
        first, second = (2, 4) if x_first else (4, 2)
        picked = ((1, 3), (0, 2)) if x_first else ((2, 3), (0, 1))
        pieces = keep.shape[1] // 96

        def split_sum(keep, came):
            return [
                jnp.stack([keep[i] + came[i] for i in places]) for places in picked
            ]

        give, keep = blend(meta(), "blend_split", split_sum, [keep, came], pieces)
        clock.mark(give)
        came = flip(give, first)
        yield
        give, keep = blend(
            meta(), "blend_pair", lambda k, c: [k[1] + c[1], k[0] + c[0]], [keep, came], pieces
        )
        clock.mark(give)
        came = flip(give, second)
        yield
        own = clock.mark(blend(meta(), "blend_sum", lambda k, c: k + c, [keep, came], pieces))
        came = flip(own, second)
        yield
        pair = clock.mark(
            blend(meta(), "blend_stack", lambda a, b: jnp.stack([a, b]), [own, came], pieces)
        )
        came = flip(pair, first)
        yield

        def stack_four(near, far):
            if x_first:
                return jnp.stack([near[0], far[0], near[1], far[1]])
            return jnp.stack([near[0], near[1], far[0], far[1]])

        stacked = clock.mark(blend(meta(), "blend_four", stack_four, [pair, came], pieces))
        other = flip(stacked, 1)
        if index == 0:
            have["shared_sum"] = stacked[:, shard_rows:]
        yield
        for of_other, value in ((0, stacked), (1, other)):
            have["grad_experts"] = place_sum(
                meta(), have.get("grad_experts"), index, of_other, expert_weight.shape, value
            )
            clock.mark(have["grad_experts"])
            yield

    def shared_grad_chain():
        total = now(have["shared_sum"])
        parts = ready(*[pick(total, chip ^ shard_index ^ i) for i in range(4)])
        came = [line_swap(parts[i], i) for i in (1, 2, 3)]
        yield
        mine = clock.mark(jnp.stack([parts[0]] + list(now(*came))))
        other = flip(mine, 1)
        yield
        have["grad_shared"] = clock.mark(place_shared(meta(), mine, other))
        yield

    def line_reduce_steps(keep, came):
        came = now(came)
        parts = [keep[i] + came[i] for i in range(4)]
        came = line_inward(clock.mark(parts[3]))
        yield
        carried = clock.mark(parts[2] + now(came))
        inward, crossed = line_inward(carried), line_middle(carried)
        yield
        inward, crossed = now(inward, crossed)
        near_out, middle_out = ready(parts[1] + crossed, parts[3] + inward)
        near_out, middle_out = line_swap(near_out, 1), line_middle(middle_out)
        yield
        near_out, middle_out = now(near_out, middle_out)
        have["line_sum"] = clock.mark(
            (parts[0].astype(f32) + near_out.astype(f32) + middle_out.astype(f32)).astype(bf16)
        )

    def out_grad_chain():
        mixed = jnp.concatenate(have["mixed"], axis=1)
        keep, give = weight_grad(
            meta(), chip ^ shard_index, [([mixed], [have["grad_branch"][None]])], 0
        )
        clock.mark(keep)
        came = flip(give, 1)
        yield
        yield from line_reduce_steps(keep, came)
        total = have["line_sum"]
        yield
        total = ready(total)
        came = flip(total, 2)
        yield
        total = clock.mark(total + now(came))
        came = flip(total, 4)
        yield
        mine = clock.mark(total + now(came))
        other = flip(mine, 1)
        yield
        mine, other = now(mine, other)
        have["grad_out"] = clock.mark(
            jnp.where(
                core == 0,
                jnp.concatenate([mine, other], axis=0),
                jnp.concatenate([other, mine], axis=0),
            ).astype(f32)
        )
        yield

    def qkv_grad_chain():
        normed_in = have["normed_in"].reshape(4 * token_rows, width)
        projected = have["grad_projected"].reshape(1, 4 * token_rows, -1)
        keep, give = weight_grad(meta(), shard_index, [([normed_in], [projected])], 0)
        clock.mark(keep)
        came = flip(give, 1)
        yield
        yield from line_reduce_steps(keep, came)
        own = have["line_sum"]
        yield
        own = ready(own)
        came = flip(own, 2)
        yield
        pair = clock.mark(jnp.stack([own, now(came)]))
        came = flip(pair, 4)
        yield
        mine = clock.mark(jnp.concatenate([pair, now(came)]))
        other = flip(mine, 1)
        yield
        have["grad_qkv"] = clock.mark(place_heads(meta(), [mine[r] for r in range(4)], other))
        yield

    early = {
        "H": hidden_chain(),
        "W": qkv_chain(),
        "S": shared_chain(),
        "O": out_chain(),
        "K": small_chain(),
        "R": qkv_all_chain(),
        "M": main_chain(),
    }
    late = {
        "L": states_chain(),
        "S": shared_grad_chain(),
        "O": out_grad_chain(),
        "Q": qkv_grad_chain(),
    }
    for index in range(local_experts // 2):
        late[str(index)] = expert_chain(index)
    for chains, order in ((early, EARLY), (late, LATE)):
        for name in order:
            next(chains[name], None)
        for name in chains:
            for _ in chains[name]:
                pass

    own, loss_value = have["sums"]
    return (
        have["final"],
        loss_value,
        have["grad_hidden"],
        own[0],
        have["grad_qkv"],
        have["grad_out"],
        own[1],
        have["grad_shared"],
        have["grad_experts"],
    )


def solution(mesh):
    in_specs = (
        P("wt", "ctx", None),
        P("wt", "ctx", None),
        P("wt", "ctx"),
        P("wt", "ctx", None),
        P("wt", "ctx", None),
        P("wt"),
        P("wt", None),
        P("wt", None),
        P("wt"),
        P("wt", None),
        P("wt", None, None),
    )
    out_specs = (
        P("wt", "ctx", None),
        P(),
        P("wt", "ctx", None),
        P("wt"),
        P("wt", None),
        P("wt", None),
        P("wt"),
        P("wt", None),
        P("wt", None, None),
    )
    plane_of_eight = dict(mesh.shape) == {"ctx": 8, "wt": 4}
    return jax.shard_map(
        fast_device if plane_of_eight else on_device, mesh=mesh, in_specs=in_specs, out_specs=out_specs, check_vma=False
    )
```

```python
import functools
import math

import jax
import jax.numpy as jnp
from jax import lax
from jax.experimental import pallas as pl
from jax.experimental.pallas import tpu as pltpu
from jax.sharding import PartitionSpec as P

QUERY_HEADS = 12
KEY_VALUE_HEADS = 4
HEAD_SIZE = 128
F = 512
SF = 1024
EXPERTS = 16
TOP = 6


norm_eps = 1e-05
masked_score = -1e30


def sigmoid_linear(values):
    return values * jax.nn.sigmoid(values)


def silu_slope(values):
    sigma_value = jax.nn.sigmoid(values)
    return sigma_value * (1.0 + values * (1.0 - sigma_value))


def normalize(values):
    inverse = lax.rsqrt(jnp.mean(values * values, axis=-1, keepdims=True) + norm_eps)
    return (values * inverse, inverse)


def norm_back(grad_normed, scaled, inverse, gain_vector):
    grad_scaled = grad_normed * gain_vector
    return inverse * (grad_scaled - scaled * jnp.mean(grad_scaled * scaled, axis=-1, keepdims=True))


def positions(row_ids, token_rows, context_count):
    piece_index = row_ids // token_rows
    within = row_ids % token_rows
    half_rows = token_rows // 2
    mirrored = jnp.where(within < half_rows, piece_index, 2 * context_count - 1 - piece_index)
    return mirrored * half_rows + within % half_rows


def route_tables(local_routes, local_gates, experts, capacity):
    token_rows = local_routes.shape[0]
    flat_routes = local_routes.reshape(-1)
    one_hot = (flat_routes[:, None] == jnp.arange(experts, dtype=jnp.int32)[None, :]).astype(
        jnp.int32
    )
    earlier = jnp.cumsum(one_hot, axis=0) - one_hot
    slot_index = jnp.sum(earlier * one_hot, axis=1)
    token_index = jnp.arange(flat_routes.shape[0], dtype=jnp.int32) // local_routes.shape[1]
    slot_table = (
        jnp.full((experts, capacity), token_rows, jnp.int32)
        .at[flat_routes, slot_index]
        .set(token_index)
    )
    slot_gate = (
        jnp.zeros((experts, capacity), jnp.float32)
        .at[flat_routes, slot_index]
        .set(local_gates.reshape(-1))
    )
    return (slot_table, slot_gate)


def block_scores(query_rows, key_block, key_position, query_place, score_scale):
    scores = (
        jnp.einsum("qhgd,khd->qhgk", query_rows, key_block, preferred_element_type=jnp.float32)
        * score_scale
    )
    allowed = key_position[None, None, None, :] <= query_place[:, None, None, None]
    return jnp.where(allowed, scores, masked_score)


def attend_forward(
    query_rows, blocked_keys, blocked_values, place_blocks, query_place, score_scale
):
    head_shape = query_rows.shape[:3]

    def online_step(running, block_args):
        running_max, running_sum, accumulated = running
        key_block, value_block, key_position = block_args
        scores = block_scores(query_rows, key_block, key_position, query_place, score_scale)
        new_max = jnp.maximum(running_max, jnp.max(scores, axis=-1))
        rescale = jnp.exp(running_max - new_max)
        powers = jnp.exp(scores - new_max[..., None])
        new_sum = running_sum * rescale + jnp.sum(powers, axis=-1)
        weighted = jnp.einsum(
            "qhgk,khd->qhgd",
            powers.astype(jnp.bfloat16),
            value_block,
            preferred_element_type=jnp.float32,
        )
        return ((new_max, new_sum, accumulated * rescale[..., None] + weighted), None)

    initial = (
        jnp.full(head_shape, masked_score, jnp.float32),
        jnp.zeros(head_shape, jnp.float32),
        jnp.zeros(query_rows.shape, jnp.float32),
    )
    row_max, row_sum, accumulated = lax.scan(
        online_step, initial, (blocked_keys, blocked_values, place_blocks)
    )[0]
    log_total = row_max + jnp.log(row_sum)
    return (accumulated / row_sum[..., None], log_total)


def attend_backward(
    query_rows,
    blocked_keys,
    blocked_values,
    place_blocks,
    query_place,
    log_total,
    attention_output_gradient,
    attention_output,
    score_scale,
):
    row_delta = jnp.sum(attention_output_gradient.astype(jnp.float32) * attention_output, axis=-1)

    def block_grads(grad_queries, block_args):
        key_block, value_block, key_position = block_args
        scores = block_scores(query_rows, key_block, key_position, query_place, score_scale)
        probabilities = jnp.exp(scores - log_total[..., None])
        grad_probs = jnp.einsum(
            "qhgd,khd->qhgk",
            attention_output_gradient,
            value_block,
            preferred_element_type=jnp.float32,
        )
        grad_scores = (probabilities * (grad_probs - row_delta[..., None])).astype(jnp.bfloat16)
        grad_queries = grad_queries + jnp.einsum(
            "qhgk,khd->qhgd", grad_scores, key_block, preferred_element_type=jnp.float32
        )
        grad_keys = (
            jnp.einsum(
                "qhgk,qhgd->khd", grad_scores, query_rows, preferred_element_type=jnp.float32
            )
            * score_scale
        )
        grad_values = jnp.einsum(
            "qhgk,qhgd->khd",
            probabilities.astype(jnp.bfloat16),
            attention_output_gradient,
            preferred_element_type=jnp.float32,
        )
        return (grad_queries, (grad_keys, grad_values))

    grad_queries, (grad_keys, grad_values) = lax.scan(
        block_grads,
        jnp.zeros(query_rows.shape, jnp.float32),
        (blocked_keys, blocked_values, place_blocks),
    )
    return (grad_queries * score_scale, grad_keys, grad_values)


def gate_up_grads(grad_act, gate_up, hidden_units):
    gate_part = gate_up[..., :hidden_units]
    up_part = gate_up[..., hidden_units:]
    return jnp.concatenate(
        [grad_act * up_part * silu_slope(gate_part), grad_act * sigmoid_linear(gate_part)], axis=-1
    ).astype(jnp.bfloat16)


def on_device(
    hidden,
    teacher,
    valid_mask,
    routes,
    route_gates,
    gain_in,
    query_key_value_weight,
    out_weight,
    gain_mid,
    shared_weight,
    expert_weight,
):
    token_rows = hidden.shape[1]
    model_width = hidden.shape[2]
    context_count = lax.axis_size("ctx")
    shard_count = lax.axis_size("wt")
    seq_rows = token_rows * context_count
    all_tokens = seq_rows * shard_count
    query_groups = QUERY_HEADS // KEY_VALUE_HEADS
    query_total_width = QUERY_HEADS * HEAD_SIZE
    key_value_width = KEY_VALUE_HEADS * HEAD_SIZE
    score_scale = 1.0 / math.sqrt(HEAD_SIZE)
    key_row_count = min(512, seq_rows)
    number_of_blocks = seq_rows // key_row_count
    capacity = token_rows * TOP // 12
    local_experts = expert_weight.shape[0]
    contract_last = (((1,), (1,)), ((), ()))
    contract_first = (((0,), (0,)), ((), ()))
    full_gain_in, full_qkv, full_out, full_gain_mid, full_shared = (
        lax.all_gather(gain_in, "wt", axis=0, tiled=True),
        lax.all_gather(query_key_value_weight, "wt", axis=0, tiled=True),
        lax.all_gather(out_weight, "wt", axis=0, tiled=True),
        lax.all_gather(gain_mid, "wt", axis=0, tiled=True),
        lax.all_gather(shared_weight, "wt", axis=0, tiled=True),
    )
    gain_in_float = full_gain_in.astype(jnp.float32)
    gain_mid_float = full_gain_mid.astype(jnp.float32)
    inputs = hidden[0].astype(jnp.float32)
    scaled_in, inverse_in = normalize(inputs)
    normed_in = (scaled_in * gain_in_float).astype(jnp.bfloat16)
    projected_rows = jnp.dot(normed_in, full_qkv, preferred_element_type=jnp.float32).astype(
        jnp.bfloat16
    )
    query_rows = projected_rows[:, :query_total_width].reshape(
        token_rows, KEY_VALUE_HEADS, query_groups, HEAD_SIZE
    )
    context_local = projected_rows[:, query_total_width:]
    context_gathered = lax.all_gather(context_local, "ctx", axis=0, tiled=True)
    context_index = lax.axis_index("ctx")
    query_place = positions(
        context_index * token_rows + jnp.arange(token_rows, dtype=jnp.int32),
        token_rows,
        context_count,
    )
    place_blocks = positions(
        jnp.arange(seq_rows, dtype=jnp.int32), token_rows, context_count
    ).reshape(number_of_blocks, key_row_count)
    blocked_keys = context_gathered[:, :key_value_width].reshape(
        number_of_blocks, key_row_count, KEY_VALUE_HEADS, HEAD_SIZE
    )
    blocked_values = context_gathered[:, key_value_width:].reshape(
        number_of_blocks, key_row_count, KEY_VALUE_HEADS, HEAD_SIZE
    )
    attention_output, log_total = attend_forward(
        query_rows, blocked_keys, blocked_values, place_blocks, query_place, score_scale
    )
    mixed_rows = attention_output.reshape(token_rows, query_total_width).astype(jnp.bfloat16)
    middle = inputs + jnp.dot(mixed_rows, full_out, preferred_element_type=jnp.float32)
    scaled_mid, inverse_mid = normalize(middle)
    normed_mid = (scaled_mid * gain_mid_float).astype(jnp.bfloat16)
    shared_gate_up = jnp.dot(
        normed_mid, full_shared[:, : 2 * SF], preferred_element_type=jnp.float32
    )
    shared_act = (sigmoid_linear(shared_gate_up[:, :SF]) * shared_gate_up[:, SF:]).astype(
        jnp.bfloat16
    )
    shared_out = lax.dot_general(
        shared_act, full_shared[:, 2 * SF :], contract_last, preferred_element_type=jnp.float32
    )
    slot_table, slot_gate = route_tables(routes[0], route_gates[0], EXPERTS, capacity)
    padded_rows = jnp.concatenate([normed_mid, jnp.zeros((1, model_width), jnp.bfloat16)], axis=0)
    expert_rows = jnp.take(padded_rows, slot_table, axis=0)
    arrived = lax.all_to_all(expert_rows, "wt", split_axis=0, concat_axis=0, tiled=True)
    slot_count = arrived.shape[1]
    grouped = arrived.reshape(shard_count, local_experts, slot_count, model_width)
    owner_gate_up = jnp.einsum(
        "wesd,edf->wesf", grouped, expert_weight[:, :, : 2 * F], preferred_element_type=jnp.float32
    )
    owner_act = (sigmoid_linear(owner_gate_up[..., :F]) * owner_gate_up[..., F:]).astype(
        jnp.bfloat16
    )
    owner_out = jnp.einsum(
        "wesf,edf->wesd",
        owner_act,
        expert_weight[:, :, 2 * F :],
        preferred_element_type=jnp.float32,
    ).astype(jnp.bfloat16)
    returned = lax.all_to_all(
        owner_out.reshape(shard_count * local_experts, slot_count, model_width),
        "wt",
        split_axis=0,
        concat_axis=0,
        tiled=True,
    )
    expert_out, owner_rows, owner_gate_up, owner_act = (
        returned,
        arrived,
        owner_gate_up.reshape(shard_count * local_experts, slot_count, 2 * F),
        owner_act.reshape(shard_count * local_experts, slot_count, F),
    )
    routed = (
        jnp.zeros((token_rows + 1, model_width), jnp.float32)
        .at[slot_table]
        .add(expert_out.astype(jnp.float32) * slot_gate[..., None])[:token_rows]
    )
    final_state = middle + shared_out + routed
    valid_float = valid_mask[0].astype(jnp.float32)
    deviation = final_state - teacher[0].astype(jnp.float32)
    squared_local = jnp.sum(valid_float[:, None] * deviation * deviation)
    count_local = jnp.sum(valid_float)
    squared_total, valid_count = lax.psum((squared_local, count_local), ("ctx", "wt"))
    loss_value = 0.5 * squared_total / (valid_count * model_width)
    grad_final = all_tokens / valid_count * valid_float[:, None] * deviation
    grad_shared_out = grad_final.astype(jnp.bfloat16)
    grad_shared_act = jnp.dot(
        grad_shared_out, full_shared[:, 2 * SF :], preferred_element_type=jnp.float32
    )
    grad_shared_down = lax.dot_general(
        grad_shared_out, shared_act, contract_first, preferred_element_type=jnp.float32
    )
    grad_shared_gate_up = gate_up_grads(grad_shared_act, shared_gate_up, SF)
    grad_normed_mid = lax.dot_general(
        grad_shared_gate_up,
        full_shared[:, : 2 * SF],
        contract_last,
        preferred_element_type=jnp.float32,
    )
    grad_shared_front = lax.dot_general(
        normed_mid, grad_shared_gate_up, contract_first, preferred_element_type=jnp.float32
    )
    grad_shared_full = jnp.concatenate([grad_shared_front, grad_shared_down], axis=1)
    padded_grads = jnp.concatenate([grad_final, jnp.zeros((1, model_width), jnp.float32)], axis=0)
    grad_expert_out = (jnp.take(padded_grads, slot_table, axis=0) * slot_gate[..., None]).astype(
        jnp.bfloat16
    )
    grad_arrived = lax.all_to_all(grad_expert_out, "wt", split_axis=0, concat_axis=0, tiled=True)
    grad_grouped = grad_arrived.reshape(shard_count, local_experts, capacity, model_width)
    owner_gate_up_grouped = owner_gate_up.reshape(shard_count, local_experts, capacity, 2 * F)
    owner_act_grouped = owner_act.reshape(shard_count, local_experts, capacity, F)
    owner_rows_grouped = owner_rows.reshape(shard_count, local_experts, capacity, model_width)
    grad_owner_act = jnp.einsum(
        "wecd,edf->wecf",
        grad_grouped,
        expert_weight[:, :, 2 * F :],
        preferred_element_type=jnp.float32,
    )
    grad_owner_gate_up = gate_up_grads(grad_owner_act, owner_gate_up_grouped, F)
    grad_owner_rows = jnp.einsum(
        "wecf,edf->wecd",
        grad_owner_gate_up,
        expert_weight[:, :, : 2 * F],
        preferred_element_type=jnp.float32,
    ).astype(jnp.bfloat16)
    front = jnp.einsum(
        "wecd,wecf->edf", owner_rows_grouped, grad_owner_gate_up, preferred_element_type=jnp.float32
    )
    back = jnp.einsum(
        "wecd,wecf->edf", grad_grouped, owner_act_grouped, preferred_element_type=jnp.float32
    )
    expert_grad = jnp.concatenate([front, back], axis=2)
    grad_rows = lax.all_to_all(
        grad_owner_rows.reshape(shard_count * local_experts, capacity, model_width),
        "wt",
        split_axis=0,
        concat_axis=0,
        tiled=True,
    )
    grad_normed_mid = (
        grad_normed_mid
        + jnp.zeros((token_rows + 1, model_width), jnp.float32)
        .at[slot_table]
        .add(grad_rows.astype(jnp.float32))[:token_rows]
    )
    grad_gain_mid_local = jnp.sum(grad_normed_mid * scaled_mid, axis=0)
    grad_middle = grad_final + norm_back(grad_normed_mid, scaled_mid, inverse_mid, gain_mid_float)
    grad_branch = grad_middle.astype(jnp.bfloat16)
    mixed_gradient = lax.dot_general(
        grad_branch, full_out, contract_last, preferred_element_type=jnp.float32
    ).astype(jnp.bfloat16)
    grad_out_local = lax.dot_general(
        mixed_rows, grad_branch, contract_first, preferred_element_type=jnp.float32
    )
    context_recomputed = lax.all_gather(context_local, "ctx", axis=0, tiled=True)
    backward_keys = context_recomputed[:, :key_value_width].reshape(
        number_of_blocks, key_row_count, KEY_VALUE_HEADS, HEAD_SIZE
    )
    backward_values = context_recomputed[:, key_value_width:].reshape(
        number_of_blocks, key_row_count, KEY_VALUE_HEADS, HEAD_SIZE
    )
    attention_output_gradient = mixed_gradient.reshape(
        token_rows, KEY_VALUE_HEADS, query_groups, HEAD_SIZE
    )
    grad_queries, grad_keys, grad_values = attend_backward(
        query_rows,
        backward_keys,
        backward_values,
        place_blocks,
        query_place,
        log_total,
        attention_output_gradient,
        attention_output,
        score_scale,
    )
    grad_context_all = jnp.concatenate(
        [
            grad_keys.reshape(seq_rows, key_value_width),
            grad_values.reshape(seq_rows, key_value_width),
        ],
        axis=1,
    )
    grad_context = lax.psum_scatter(
        grad_context_all.astype(jnp.bfloat16), "ctx", scatter_dimension=0, tiled=True
    ).astype(jnp.float32)
    grad_projected = jnp.concatenate(
        [grad_queries.reshape(token_rows, query_total_width), grad_context], axis=1
    ).astype(jnp.bfloat16)
    grad_normed_in = lax.dot_general(
        grad_projected, full_qkv, contract_last, preferred_element_type=jnp.float32
    )
    grad_qkv_local = lax.dot_general(
        normed_in, grad_projected, contract_first, preferred_element_type=jnp.float32
    )
    grad_gain_in_local = jnp.sum(grad_normed_in * scaled_in, axis=0)
    grad_inputs = grad_middle + norm_back(grad_normed_in, scaled_in, inverse_in, gain_in_float)
    weight_sums = (
        lax.psum_scatter(
            grad_gain_in_local.astype(jnp.bfloat16), "wt", scatter_dimension=0, tiled=True
        ).astype(jnp.float32),
        lax.psum_scatter(
            grad_qkv_local.astype(jnp.bfloat16), "wt", scatter_dimension=0, tiled=True
        ).astype(jnp.float32),
        lax.psum_scatter(
            grad_out_local.astype(jnp.bfloat16), "wt", scatter_dimension=0, tiled=True
        ).astype(jnp.float32),
        lax.psum_scatter(
            grad_gain_mid_local.astype(jnp.bfloat16), "wt", scatter_dimension=0, tiled=True
        ).astype(jnp.float32),
        lax.psum_scatter(
            grad_shared_full.astype(jnp.bfloat16), "wt", scatter_dimension=0, tiled=True
        ).astype(jnp.float32),
    )
    summed = (
        lax.psum(weight_sums[0].astype(jnp.bfloat16), "ctx").astype(jnp.float32),
        lax.psum(weight_sums[1].astype(jnp.bfloat16), "ctx").astype(jnp.float32),
        lax.psum(weight_sums[2].astype(jnp.bfloat16), "ctx").astype(jnp.float32),
        lax.psum(weight_sums[3].astype(jnp.bfloat16), "ctx").astype(jnp.float32),
        lax.psum(weight_sums[4].astype(jnp.bfloat16), "ctx").astype(jnp.float32),
        lax.psum(expert_grad.astype(jnp.bfloat16), "ctx").astype(jnp.float32),
    )
    return (
        final_state.astype(jnp.bfloat16)[None],
        loss_value,
        grad_inputs[None],
        summed[0],
        summed[1],
        summed[2],
        summed[3],
        summed[4],
        summed[5],
    )


PLANE = [[0, 2, 4, 6], [1, 3, 5, 7]]
COSTS = {
    "project": 0.3,
    "attend": 0.3,
    "leave": 0.3,
    "join_shared": 0.3,
    "experts": 0.3,
    "experts_back": 0.3,
    "enter_back": 0.3,
    "attend_back": 0.3,
    "finish": 0.3,
    "weight_grad": 0.3,
    "expert_grad": 0.3,
    "blend_split": 0.3,
    "blend_pair": 0.3,
    "blend_sum": 0.3,
    "blend_stack": 0.3,
    "place_sum": 0.3,
    "place_shared": 0.3,
    "place_heads": 0.3,
}


def flip(value, bit):
    return lax.ppermute(value, "ctx", [(index, index ^ bit) for index in range(8)])


def line_swap(value, offset):
    return lax.ppermute(value, "wt", [(index, index ^ offset) for index in range(4)])


def line_middle(value):
    return lax.ppermute(value, "wt", [(1, 2), (2, 1)])


def line_outward(value):
    return lax.ppermute(value, "wt", [(1, 0), (2, 3)])


def line_inward(value):
    return lax.ppermute(value, "wt", [(0, 1), (3, 2)])


def line_gather(value, at_end):
    near = line_swap(value, 1)
    middle = line_middle(value)
    middle_far = line_middle(near)
    outward = line_outward(middle)
    outward_far = line_outward(middle_far)
    return [
        value,
        near,
        jnp.where(at_end, outward, middle_far),
        jnp.where(at_end, outward_far, middle),
    ]


def line_reduce(parts):
    far = line_inward(parts[3])
    carried = parts[2] + far
    inward = line_inward(carried)
    crossed = line_middle(carried)
    near = line_swap(parts[1] + crossed, 1)
    middle = line_middle(parts[3] + inward)
    return (
        parts[0].astype(jnp.float32) + near.astype(jnp.float32) + middle.astype(jnp.float32)
    )


def chips_exchange(blocks):
    return lax.all_to_all(
        blocks,
        "ctx",
        split_axis=0,
        concat_axis=0,
        tiled=True,
        axis_index_groups=PLANE,
    )


def line_exchange(blocks):
    return lax.all_to_all(blocks, "wt", split_axis=0, concat_axis=0, tiled=True)


def chips_gather(value, x_last):
    along_x = flip(value, 2)
    along_y = flip(value, 4)
    corner = flip(along_y, 2) if x_last else flip(along_x, 4)
    return [value, along_x, along_y, corner]


def core_swap(values):
    return [flip(value, 1) for value in values]


def everywhere_sum(value):
    for bit in (1, 2, 4):
        value = value + flip(value, bit)
    for offset in (1, 2):
        value = value + line_swap(value, offset)
    return value


def pick(blocks, index):
    return lax.dynamic_index_in_dim(blocks, index, 0, keepdims=False)


def chips_reduce(keep, came):
    half = keep.shape[1] // 2
    upper = keep[:, :half] + came[:, :half]
    lower = keep[:, half:] + came[:, half:]
    upper_came = flip(upper[1::2], 2)
    lower_came = flip(lower[2:], 4)
    upper = upper[0::2] + upper_came
    lower = lower[:2] + lower_came
    upper_came = flip(upper[1], 4)
    lower_came = flip(lower[1], 2)
    return jnp.concatenate([upper[0] + upper_came, lower[0] + lower_came], axis=0)


def dot_plain(left, right):
    return lax.dot_general(
        left, right, (((1,), (0,)), ((), ())), preferred_element_type=jnp.float32
    )


def dot_last(left, right):
    return lax.dot_general(
        left, right, (((1,), (1,)), ((), ())), preferred_element_type=jnp.float32
    )


def dot_first(left, right):
    return lax.dot_general(
        left, right, (((0,), (0,)), ((), ())), preferred_element_type=jnp.float32
    )


def call(kernel, name, meta, arrays, grid, in_specs, out_specs, out_shape, scratch, flops, moved):
    return pl.pallas_call(
        kernel,
        grid_spec=pltpu.PrefetchScalarGridSpec(
            num_scalar_prefetch=1,
            grid=grid,
            in_specs=in_specs,
            out_specs=out_specs,
            scratch_shapes=scratch,
        ),
        out_shape=out_shape,
        compiler_params=pltpu.CompilerParams(vmem_limit_bytes=48 * 1024 * 1024),
        cost_estimate=pl.CostEstimate(
            flops=int(COSTS.get(name, 1.0) * 1e9), bytes_accessed=1000, transcendentals=0
        ),
        name=name,
    )(meta, *arrays)


def whole(array):
    rank = len(array.shape)
    return pl.BlockSpec(tuple(array.shape), lambda *_: (0,) * rank)


def shape_of(shape, dtype):
    return jax.ShapeDtypeStruct(shape, dtype)


def size_of(arrays):
    return sum(math.prod(a.shape) * a.dtype.itemsize for a in arrays)


def blend(meta, name, function, arrays, pieces=4):
    rows = arrays[0].shape[-2]
    tile = rows // pieces
    outs = jax.eval_shape(function, *[shape_of(a.shape, a.dtype) for a in arrays])
    many = isinstance(outs, (list, tuple))
    outs = list(outs) if many else [outs]

    def spec(a):
        rank = len(a.shape)
        lead = a.shape[:-2]
        return pl.BlockSpec(
            tuple(lead) + (tile, a.shape[-1]),
            lambda i, m: (0,) * (rank - 2) + (i, 0),
        )

    def kernel(meta_ref, *refs):
        result = function(*[ref[...] for ref in refs[: len(arrays)]])
        result = list(result) if many else [result]
        for ref, value in zip(refs[len(arrays) :], result):
            ref[...] = value

    result = call(
        kernel,
        name,
        meta,
        arrays,
        (pieces,),
        [spec(a) for a in arrays],
        [spec(a) for a in outs],
        outs,
        [],
        0,
        0,
    )
    return result if many else result[0]


def aligned(value, step):
    return pl.multiple_of(value * step, step)


def project_kernel(meta, blocks_ref, gain_ref, mine, other, *refs):
    normed_ref, query_ref, pair_ref, weight_ref = refs
    core = meta[0] & 1
    rows = mine.shape[1]

    @pl.when(pl.program_id(0) == 0)
    def _():
        for i in range(4):
            at = 2 * (meta[1] ^ i)
            weight_ref[pl.ds(aligned(at + core, rows), rows), :] = mine[i]
            weight_ref[pl.ds(aligned(at + 1 - core, rows), rows), :] = other[i]

    states = blocks_ref[0].astype(jnp.float32)
    inverse = lax.rsqrt(jnp.mean(states * states, axis=-1, keepdims=True) + norm_eps)
    normed = (states * inverse * gain_ref[...]).astype(jnp.bfloat16)
    normed_ref[0] = normed
    projected = dot_plain(normed, weight_ref[...]).astype(jnp.bfloat16)
    query_width = query_ref.shape[-1]
    query_ref[0] = projected[:, :query_width]
    pair_ref[0] = projected[:, query_width:]


def project(meta, blocks, gain, mine, other, query_width):
    _, token_rows, width = blocks.shape
    columns = mine.shape[2]
    arrays = [blocks, gain, mine, other]
    outs = [
        shape_of((4, token_rows, width), jnp.bfloat16),
        shape_of((4, token_rows, query_width), jnp.bfloat16),
        shape_of((4, token_rows, columns - query_width), jnp.bfloat16),
        shape_of((width, columns), jnp.bfloat16),
    ]
    return call(
        project_kernel,
        "project",
        meta,
        arrays,
        (4,),
        [pl.BlockSpec((1, token_rows, width), lambda r, m: (r, 0, 0))]
        + [whole(a) for a in arrays[1:]],
        [
            pl.BlockSpec((1, token_rows, width), lambda r, m: (r, 0, 0)),
            pl.BlockSpec((1, token_rows, query_width), lambda r, m: (r, 0, 0)),
            pl.BlockSpec((1, token_rows, columns - query_width), lambda r, m: (r, 0, 0)),
            whole(outs[3]),
        ],
        outs,
        [],
        2 * 4 * token_rows * width * columns,
        size_of(arrays) + size_of(outs),
    )


def sort_pairs(meta, mine_ref, other_ref, keys, values):
    half = mine_ref.shape[1] // 2
    for slot in range(16):
        block, part = (slot, 0) if slot < 8 else (15 - slot, 1)
        place = block >> 1
        rows = pl.ds(part * half, half)
        to = pl.ds(slot * half, half)

        @pl.when((meta[0] & 1) == (block & 1))
        def _():
            keys[to, :] = mine_ref[place, rows, :HEAD_SIZE]
            values[to, :] = mine_ref[place, rows, HEAD_SIZE:]

        @pl.when((meta[0] & 1) != (block & 1))
        def _():
            keys[to, :] = other_ref[place, rows, :HEAD_SIZE]
            values[to, :] = other_ref[place, rows, HEAD_SIZE:]


def stack_heads(rows):
    count = rows.shape[1] // HEAD_SIZE
    return jnp.concatenate(
        [rows[:, h * HEAD_SIZE : (h + 1) * HEAD_SIZE] for h in range(count)], axis=0
    )


def unstack_heads(rows, count):
    each = rows.shape[0] // count
    return jnp.concatenate([rows[h * each : (h + 1) * each] for h in range(count)], axis=1)


def step_slot(meta):
    step = pl.program_id(0)
    block = 2 * (step >> 1) + (meta[0] & 1)
    return jnp.where((step & 1) == 0, block, 15 - block)


def allowed_pairs(start, slot, shape, half):
    key_place = start + lax.broadcasted_iota(jnp.int32, shape, 0)
    query_place = slot * half + (lax.broadcasted_iota(jnp.int32, shape, 1) & (half - 1))
    return key_place <= query_place


def key_spans(step, half, span):
    pairs = (step // 2 if step % 2 == 0 else 7 - step // 2) + 1
    rows = pairs * 2 * half
    return [(at, min(span, rows - at)) for at in range(0, rows, span)]


def attend_kernel(scale, span, meta, query_ref, mine_ref, other_ref, *refs):
    out_ref, log_ref, keys, values, values_turned = refs
    half, group_width = query_ref.shape[1:]
    count = group_width // HEAD_SIZE

    @pl.when(pl.program_id(0) == 0)
    def _():
        sort_pairs(meta, mine_ref, other_ref, keys, values)
        values_turned[...] = values[...].T

    slot = step_slot(meta)
    query = stack_heads(query_ref[0])
    wide = count * half

    def run(spans):
        highest = jnp.full((1, wide), masked_score, jnp.float32)
        total = jnp.zeros((1, wide), jnp.float32)
        mixed = jnp.zeros((HEAD_SIZE, wide), jnp.float32)
        for start, size in spans:
            at = pl.ds(start, size)
            scores = dot_last(keys[at, :], query) * scale
            if start == spans[-1][0]:
                seen = allowed_pairs(start, slot, scores.shape, half)
                scores = jnp.where(seen, scores, masked_score)
            new = jnp.maximum(highest, jnp.max(scores, axis=0, keepdims=True))
            rescale = jnp.exp(highest - new)
            powers = jnp.exp(scores - new)
            total = total * rescale + jnp.sum(powers, axis=0, keepdims=True)
            mixed = mixed * rescale + dot_plain(
                values_turned[:, at], powers.astype(jnp.bfloat16)
            )
            highest = new
        log_ref[0] = highest + jnp.log(total)
        out_ref[0] = unstack_heads((mixed / total).T, count).astype(jnp.bfloat16)

    for step in range(8):

        @pl.when(pl.program_id(0) == step)
        def _():
            run(key_spans(step, half, span))


def attend(meta, query, mine, other, scale):
    token_rows, group_width = query.shape[1:]
    half = token_rows // 2
    count = group_width // HEAD_SIZE
    everything = 8 * token_rows
    span = 1024
    arrays = [query, mine, other]
    outs = [
        shape_of(query.shape, jnp.bfloat16),
        shape_of((8, 1, count * half), jnp.float32),
    ]
    return call(
        functools.partial(attend_kernel, scale, span),
        "attend",
        meta,
        arrays,
        (8,),
        [
            pl.BlockSpec((1, half, group_width), lambda i, m: (i // 2, i % 2, 0)),
            whole(mine),
            whole(other),
        ],
        [
            pl.BlockSpec((1, half, group_width), lambda i, m: (i // 2, i % 2, 0)),
            pl.BlockSpec((1, 1, count * half), lambda i, m: (i, 0, 0)),
        ],
        outs,
        [
            pltpu.VMEM((everything, HEAD_SIZE), jnp.bfloat16),
            pltpu.VMEM((everything, HEAD_SIZE), jnp.bfloat16),
            pltpu.VMEM((HEAD_SIZE, everything), jnp.bfloat16),
        ],
        2 * 2 * 4 * token_rows * everything * group_width,
        size_of(arrays) + size_of(outs),
    )


def attend_back_kernel(scale, span, meta, query_ref, mine_ref, other_ref, log_ref, *refs):
    mixed_ref, grad_ref, grad_query_ref, grad_mine_ref, grad_other_ref = refs[:5]
    keys, values, keys_turned, grad_keys, grad_values = refs[5:]
    step = pl.program_id(0)
    half, group_width = query_ref.shape[1:]
    count = group_width // HEAD_SIZE

    @pl.when(step == 0)
    def _():
        sort_pairs(meta, mine_ref, other_ref, keys, values)
        keys_turned[...] = keys[...].T
        grad_keys[...] = jnp.zeros_like(grad_keys)
        grad_values[...] = jnp.zeros_like(grad_values)

    slot = step_slot(meta)
    query = stack_heads(query_ref[0])
    mixed = stack_heads(mixed_ref[0]).astype(jnp.float32)
    grad = stack_heads(grad_ref[0])
    delta = jnp.sum((mixed * grad.astype(jnp.float32)).T, axis=0, keepdims=True)
    log_total = log_ref[0]

    def run(spans):
        grad_turned = jnp.zeros((HEAD_SIZE, count * half), jnp.float32)
        for start, size in spans:
            at = pl.ds(start, size)
            scores = dot_last(keys[at, :], query) * scale
            probs = jnp.exp(scores - log_total)
            if start == spans[-1][0]:
                probs = jnp.where(allowed_pairs(start, slot, probs.shape, half), probs, 0.0)
            grad_probs = dot_last(values[at, :], grad)
            grad_scores = (probs * (grad_probs - delta)).astype(jnp.bfloat16)
            grad_values[at, :] += dot_plain(probs.astype(jnp.bfloat16), grad)
            grad_keys[at, :] += dot_plain(grad_scores, query)
            grad_turned += dot_plain(keys_turned[:, at], grad_scores)
        grad_query_ref[0] = unstack_heads((grad_turned * scale).T, count).astype(jnp.bfloat16)

    for at_step in range(8):

        @pl.when(step == at_step)
        def _():
            run(key_spans(at_step, half, span))

    @pl.when(step == 7)
    def _():
        for slot_at in range(16):
            block, part = (slot_at, 0) if slot_at < 8 else (15 - slot_at, 1)
            place = block >> 1
            rows = pl.ds(part * half, half)
            here = pl.ds(slot_at * half, half)
            both = jnp.concatenate([grad_keys[here, :] * scale, grad_values[here, :]], axis=1)

            @pl.when((meta[0] & 1) == (block & 1))
            def _():
                grad_mine_ref[place, rows, :] = both

            @pl.when((meta[0] & 1) != (block & 1))
            def _():
                grad_other_ref[place, rows, :] = both.astype(jnp.bfloat16)


def attend_back(meta, query, mine, other, log_total, mixed, grad, scale):
    token_rows, group_width = query.shape[1:]
    half = token_rows // 2
    count = group_width // HEAD_SIZE
    everything = 8 * token_rows
    span = 512
    arrays = [query, mine, other, log_total, mixed, grad]
    outs = [
        shape_of(query.shape, jnp.bfloat16),
        shape_of(mine.shape, jnp.float32),
        shape_of(mine.shape, jnp.bfloat16),
    ]
    return call(
        functools.partial(attend_back_kernel, scale, span),
        "attend_back",
        meta,
        arrays,
        (8,),
        [
            pl.BlockSpec((1, half, group_width), lambda i, m: (i // 2, i % 2, 0)),
            whole(mine),
            whole(other),
            pl.BlockSpec((1, 1, count * half), lambda i, m: (i, 0, 0)),
            pl.BlockSpec((1, half, group_width), lambda i, m: (i // 2, i % 2, 0)),
            pl.BlockSpec((1, half, group_width), lambda i, m: (i // 2, i % 2, 0)),
        ],
        [
            pl.BlockSpec((1, half, group_width), lambda i, m: (i // 2, i % 2, 0)),
            whole(outs[1]),
            whole(outs[2]),
        ],
        outs,
        [
            pltpu.VMEM((everything, HEAD_SIZE), jnp.bfloat16),
            pltpu.VMEM((everything, HEAD_SIZE), jnp.bfloat16),
            pltpu.VMEM((HEAD_SIZE, everything), jnp.bfloat16),
            pltpu.VMEM((everything, HEAD_SIZE), jnp.float32),
            pltpu.VMEM((everything, HEAD_SIZE), jnp.float32),
        ],
        5 * 2 * 4 * token_rows * everything * group_width,
        size_of(arrays) + size_of(outs),
    )


def leave_kernel(meta, *refs):
    parts, mine, other, states_ref, gain_ref = refs[:4], *refs[4:8]
    weight_ref, middle_ref, normed_ref = refs[8:]
    core, chip = meta[0] & 1, meta[0] >> 1
    rows = mine.shape[1]
    for i in range(4):
        weight_ref[pl.ds(aligned(2 * i + core, rows), rows), :] = mine[i]
        weight_ref[pl.ds(aligned(2 * i + 1 - core, rows), rows), :] = other[i]
    middle = states_ref[...].astype(jnp.float32)
    for r in range(4):
        at = pl.ds(aligned(chip ^ r, 2 * rows), 2 * rows)
        middle += dot_plain(parts[r][...], weight_ref[at, :])
    middle_ref[...] = middle
    inverse = lax.rsqrt(jnp.mean(middle * middle, axis=-1, keepdims=True) + norm_eps)
    normed_ref[...] = (middle * inverse * gain_ref[...]).astype(jnp.bfloat16)


def leave(meta, parts, mine, other, states, gain):
    token_rows, width = states.shape
    arrays = list(parts) + [mine, other, states, gain]
    outs = [
        shape_of((8 * mine.shape[1], width), jnp.bfloat16),
        shape_of((token_rows, width), jnp.float32),
        shape_of((token_rows, width), jnp.bfloat16),
    ]
    return call(
        leave_kernel,
        "leave",
        meta,
        arrays,
        (1,),
        [whole(a) for a in arrays],
        [whole(a) for a in outs],
        outs,
        [],
        2 * token_rows * width * width,
        size_of(arrays) + size_of(outs),
    )


def norm_back_rows(grad_normed, states, gain):
    inverse = lax.rsqrt(jnp.mean(states * states, axis=-1, keepdims=True) + norm_eps)
    scaled = states * inverse
    gain_grad = jnp.sum(grad_normed * scaled, axis=0, keepdims=True)
    grad_scaled = grad_normed * gain
    shift = jnp.mean(grad_scaled * scaled, axis=-1, keepdims=True)
    return inverse * (grad_scaled - scaled * shift), gain_grad


def enter_back_kernel(meta, final_ref, normed_ref, middle_ref, gain_ref, weight_ref, *refs):
    grad_ref, branch_ref, gain_grad_ref, mixed_ref = refs
    grad, gain_grad = norm_back_rows(normed_ref[...], middle_ref[...], gain_ref[...])
    grad = grad + final_ref[...]
    grad_ref[...] = grad
    gain_grad_ref[...] = gain_grad
    branch = grad.astype(jnp.bfloat16)
    branch_ref[...] = branch
    rows = weight_ref.shape[0] // 4
    for r in range(4):
        mixed_ref[r] = dot_last(branch, weight_ref[rows * r : rows * (r + 1), :]).astype(
            jnp.bfloat16
        )


def enter_back(meta, grad_final, grad_normed, middle, gain, weight):
    token_rows, width = middle.shape
    arrays = [grad_final, grad_normed, middle, gain, weight]
    outs = [
        shape_of((token_rows, width), jnp.float32),
        shape_of((token_rows, width), jnp.bfloat16),
        shape_of((1, width), jnp.float32),
        shape_of((4, token_rows, weight.shape[0] // 4), jnp.bfloat16),
    ]
    return call(
        enter_back_kernel,
        "enter_back",
        meta,
        arrays,
        (1,),
        [whole(a) for a in arrays],
        [whole(a) for a in outs],
        outs,
        [],
        2 * token_rows * width * width,
        size_of(arrays) + size_of(outs),
    )


def finish_kernel(meta, *refs):
    parts, mine, other = refs[:3]
    states_ref, middle_ref, gain_ref, grad_ref, gain_grad_ref, total = refs[3:]
    core, chip = meta[0] & 1, meta[0] >> 1
    columns = mine.shape[1]
    for at, weights in ((core, mine), (1 - core, other)):
        total[:, pl.ds(aligned(at, columns), columns)] = sum(
            dot_last(parts[r], weights[chip ^ r]) for r in range(4)
        )
    grad, gain_grad = norm_back_rows(
        total[...], states_ref[...].astype(jnp.float32), gain_ref[...]
    )
    grad_ref[0] = grad + middle_ref[...]
    gain_grad_ref[...] = gain_grad


def finish(meta, parts, mine, other, states, grad_middle, gain):
    token_rows, width = states.shape
    arrays = [parts, mine, other, states, grad_middle, gain]
    outs = [
        shape_of((1, token_rows, width), jnp.float32),
        shape_of((1, width), jnp.float32),
    ]
    return call(
        finish_kernel,
        "finish",
        meta,
        arrays,
        (1,),
        [whole(a) for a in arrays],
        [whole(a) for a in outs],
        outs,
        [pltpu.VMEM((token_rows, width), jnp.float32)],
        2 * token_rows * width * 4 * parts.shape[2],
        size_of(arrays) + size_of(outs),
    )


def gated(gate_up, units):
    gate_part = gate_up[:, :units]
    sigma = 1.0 / (1.0 + jnp.exp(-gate_part))
    return gate_part * sigma * gate_up[:, units:]


def gated_back(grad_act, gate_up, units):
    gate_part = gate_up[:, :units].astype(jnp.float32)
    up_part = gate_up[:, units:].astype(jnp.float32)
    sigma = 1.0 / (1.0 + jnp.exp(-gate_part))
    linear = gate_part * sigma
    grad_gate = grad_act * up_part * (sigma * (1.0 + gate_part * (1.0 - sigma)))
    return grad_gate, grad_act * linear, linear * up_part


def experts_kernel(
    meta, rows_ref, gates_ref, expert_ref, shared_ref, gate_up_ref, shared_gate_up_ref, out_ref, total
):
    expert = pl.program_id(0)
    rows = rows_ref[...]

    @pl.when(expert == 0)
    def _():
        units = shared_ref.shape[1] // 3
        gate_up = dot_plain(rows, shared_ref[:, : 2 * units])
        shared_gate_up_ref[...] = gate_up.astype(jnp.bfloat16)
        act = gated(gate_up, units).astype(jnp.bfloat16)
        total[...] = dot_last(act, shared_ref[:, 2 * units :])

    gate_up = dot_plain(rows, expert_ref[0, :, : 2 * F])
    gate_up_ref[0] = gate_up.astype(jnp.bfloat16)
    act = (gated(gate_up, F) * gates_ref[0]).astype(jnp.bfloat16)
    total[...] += dot_last(act, expert_ref[0, :, 2 * F :])

    @pl.when(expert == pl.num_programs(0) - 1)
    def _():
        out_ref[...] = total[...].astype(jnp.bfloat16)


def experts(meta, rows, gates, expert_weight, shared_slice):
    local_experts, width, _ = expert_weight.shape
    token_rows = rows.shape[0]
    shared_units = shared_slice.shape[1] // 3
    arrays = [rows, gates, expert_weight, shared_slice]
    outs = [
        shape_of((local_experts, token_rows, 2 * F), jnp.bfloat16),
        shape_of((token_rows, 2 * shared_units), jnp.bfloat16),
        shape_of((token_rows, width), jnp.bfloat16),
    ]
    return call(
        experts_kernel,
        "experts",
        meta,
        arrays,
        (local_experts,),
        [
            whole(rows),
            pl.BlockSpec((1, token_rows, 1), lambda e, m: (e, 0, 0)),
            pl.BlockSpec((1, width, 3 * F), lambda e, m: (e, 0, 0)),
            whole(shared_slice),
        ],
        [
            pl.BlockSpec((1, token_rows, 2 * F), lambda e, m: (e, 0, 0)),
            whole(outs[1]),
            whole(outs[2]),
        ],
        outs,
        [pltpu.VMEM((token_rows, width), jnp.float32)],
        2 * token_rows * width * 3 * (F * local_experts + shared_units),
        size_of(arrays) + size_of(outs),
    )


def experts_back_kernel(
    meta,
    grad_ref,
    gates_ref,
    gate_up_ref,
    shared_gate_up_ref,
    expert_ref,
    shared_ref,
    grad_gate_up_ref,
    act_ref,
    shared_grad_ref,
    shared_act_ref,
    grad_rows_ref,
    total,
):
    expert = pl.program_id(0)
    grad = grad_ref[...]

    @pl.when(expert == 0)
    def _():
        units = shared_ref.shape[1] // 3
        grad_act = dot_plain(grad, shared_ref[:, 2 * units :])
        grad_gate, grad_up, act = gated_back(grad_act, shared_gate_up_ref[...], units)
        both = jnp.concatenate([grad_gate, grad_up], axis=1).astype(jnp.bfloat16)
        shared_grad_ref[0] = both
        shared_act_ref[0] = act.astype(jnp.bfloat16)
        total[...] = dot_last(both, shared_ref[:, : 2 * units])

    grad_act = dot_plain(grad, expert_ref[0, :, 2 * F :]) * gates_ref[0]
    grad_gate, grad_up, act = gated_back(grad_act, gate_up_ref[0], F)
    both = jnp.concatenate([grad_gate, grad_up], axis=1).astype(jnp.bfloat16)
    grad_gate_up_ref[0] = both
    act_ref[0] = (act * gates_ref[0]).astype(jnp.bfloat16)
    total[...] += dot_last(both, expert_ref[0, :, : 2 * F])

    @pl.when(expert == pl.num_programs(0) - 1)
    def _():
        grad_rows_ref[...] = total[...].astype(jnp.bfloat16)


def experts_back(meta, grad, gates, gate_up, shared_gate_up, expert_weight, shared_slice):
    local_experts, width, _ = expert_weight.shape
    token_rows = grad.shape[0]
    shared_units = shared_slice.shape[1] // 3
    arrays = [grad, gates, gate_up, shared_gate_up, expert_weight, shared_slice]
    outs = [
        shape_of((local_experts, token_rows, 2 * F), jnp.bfloat16),
        shape_of((local_experts, token_rows, F), jnp.bfloat16),
        shape_of((1, token_rows, 2 * shared_units), jnp.bfloat16),
        shape_of((1, token_rows, shared_units), jnp.bfloat16),
        shape_of((token_rows, width), jnp.bfloat16),
    ]
    return call(
        experts_back_kernel,
        "experts_back",
        meta,
        arrays,
        (local_experts,),
        [
            whole(grad),
            pl.BlockSpec((1, token_rows, 1), lambda e, m: (e, 0, 0)),
            pl.BlockSpec((1, token_rows, 2 * F), lambda e, m: (e, 0, 0)),
            whole(shared_gate_up),
            pl.BlockSpec((1, width, 3 * F), lambda e, m: (e, 0, 0)),
            whole(shared_slice),
        ],
        [
            pl.BlockSpec((1, token_rows, 2 * F), lambda e, m: (e, 0, 0)),
            pl.BlockSpec((1, token_rows, F), lambda e, m: (e, 0, 0)),
            whole(outs[2]),
            whole(outs[3]),
            whole(outs[4]),
        ],
        outs,
        [pltpu.VMEM((token_rows, width), jnp.float32)],
        2 * token_rows * width * 3 * (F * local_experts + shared_units),
        size_of(arrays) + size_of(outs),
    )


def weight_grad_kernel(pairs, core_at, meta, *refs):
    keep_ref, give_ref = refs[-2:]
    at = 0
    columns = 0
    parts = []
    for count in pairs:
        lefts, rights = refs[at : at + count], refs[at + count : at + 2 * count]
        at += 2 * count
        parts.append(
            sum(dot_first(a[...], b[0]) for a, b in zip(lefts, rights)).astype(jnp.bfloat16)
        )
    half = keep_ref.shape[1]

    for core, (first, second) in ((0, (keep_ref, give_ref)), (1, (give_ref, keep_ref))):

        @pl.when((meta[core_at] & 1) == core)
        def _():
            start = 0
            for part in parts:
                stop = start + part.shape[1]
                first[0, :, start:stop] = part[:half]
                second[0, :, start:stop] = part[half:]
                start = stop


def expert_grad_kernel(count, meta, *refs):
    rows, grads, front, acts = (refs[i * count : (i + 1) * count] for i in range(4))
    out_ref = refs[-1] if len(refs) == 4 * count + 1 else refs[-2]
    tile = rows[0].shape[1]
    both = 3 * F

    def pair(front_refs, act_refs):
        return [
            sum(dot_first(a[...], b[0]) for a, b in zip(left, right)).astype(jnp.bfloat16)
            for left, right in ((rows, front_refs), (grads, act_refs))
        ]

    left, right = pair(front, acts)
    out_ref[0, :tile, : left.shape[1]] = left
    out_ref[0, :tile, left.shape[1] : both] = right
    if len(refs) > 4 * count + 1:
        held = refs[-1]
        left, right = pair(refs[4 * count : 5 * count], refs[5 * count : 6 * count])
        split, columns = left.shape[1], left.shape[1] + right.shape[1]
        held[:, :split] = left
        held[:, split:] = right
        quarter = tile // 4
        first = 2 * meta[2]
        out_ref[0, tile:, :columns] = held[pl.ds(aligned(first, quarter), quarter), :]
        out_ref[0, tile:, columns:] = held[pl.ds(aligned(first + 1, quarter), quarter), :]


def expert_grad(meta, expert, half, rows, grads, front, acts, shared=None):
    count = len(rows)
    token_rows, width = rows[0].shape
    tile = width // 4
    arrays = list(rows) + list(grads) + list(front) + list(acts)
    column = pl.BlockSpec((token_rows, tile), lambda i, m: (0, i ^ m[0]))

    def of_expert(a):
        return pl.BlockSpec((1,) + a.shape[1:], lambda i, m: (m[1], 0, 0))

    in_specs = [column] * (2 * count) + [of_expert(a) for a in arrays[2 * count :]]
    below, scratch = 0, []
    if shared is not None:
        arrays += list(shared[0]) + list(shared[1])
        in_specs += [whole(a) for a in arrays[4 * count :]]
        below = tile // 4
        columns = shared[0][0].shape[-1] + shared[1][0].shape[-1]
        scratch = [pltpu.VMEM((tile, columns), jnp.bfloat16)]
    return call(
        functools.partial(expert_grad_kernel, count),
        "expert_grad",
        jnp.stack([meta[0] >> 1, expert, half]),
        arrays,
        (4,),
        in_specs,
        pl.BlockSpec((1, tile + below, 3 * F), lambda i, m: (i, 0, 0)),
        shape_of((4, tile + below, 3 * F), jnp.bfloat16),
        scratch,
        0,
        0,
    )


def weight_grad(meta, order, operands, index):
    token_rows, width = operands[0][0][0].shape
    tile = width // 4
    scalars = jnp.stack([order, meta[0]])
    arrays, in_specs, columns = [], [], 0
    for lefts, rights in operands:
        arrays += list(lefts) + list(rights)
        in_specs += [pl.BlockSpec((token_rows, tile), lambda i, m: (0, i ^ m[0]))] * len(lefts)
        units = rights[0].shape[-1]
        at = index if rights[0].shape[0] > 1 else 0
        in_specs += [
            pl.BlockSpec((1, token_rows, units), lambda i, m, at=at: (at, 0, 0))
        ] * len(rights)
        columns += units
    tokens = token_rows * len(operands[0][0])
    counts = [len(left) for left, _ in operands]
    outs = [shape_of((4, tile // 2, columns), jnp.bfloat16)] * 2
    return call(
        functools.partial(weight_grad_kernel, counts, 1),
        "weight_grad",
        scalars,
        arrays,
        (4,),
        in_specs,
        [pl.BlockSpec((1, tile // 2, columns), lambda i, m: (i, 0, 0))] * 2,
        outs,
        [],
        2 * tokens * width * columns,
        size_of(outs) + 4 * tokens * width + 2 * tokens * columns,
    )


def place_sum_kernel(meta, *refs):
    rows = refs[-1].shape[1]
    refs[-1][0] = refs[-2][0, :rows].astype(jnp.float32)


def place_sum(meta, total, index, of_other, shape, value, stride, offset):
    _, rows, columns = value.shape
    arrays = [value]
    in_specs = [pl.BlockSpec((1, rows, columns), lambda r, m: (r, 0, 0))]
    aliases = {}
    if total is not None:
        arrays = [total] + arrays
        in_specs = [pl.BlockSpec(memory_space=pl.ANY)] + in_specs
        aliases = {1: 0}
    return pl.pallas_call(
        place_sum_kernel,
        grid_spec=pltpu.PrefetchScalarGridSpec(
            num_scalar_prefetch=1,
            grid=(2,),
            in_specs=in_specs,
            out_specs=pl.BlockSpec(
                (1, shape[1] // 4, shape[2]),
                lambda r, m: (2 * ((m[0] & 1) ^ of_other) + index, (m[0] >> 1) ^ (stride * r + offset), 0),
            ),
        ),
        out_shape=shape_of(shape, jnp.float32),
        input_output_aliases=aliases,
        compiler_params=pltpu.CompilerParams(vmem_limit_bytes=48 * 1024 * 1024),
        cost_estimate=pl.CostEstimate(
            flops=int(COSTS.get("place_sum", 1.0) * 1e9), bytes_accessed=1000, transcendentals=0
        ),
        name="place_sum",
    )(meta, *arrays)


def place_shared_kernel(meta, mine_low, mine_high, other_low, other_high, out_ref):
    core = meta[0] & 1
    rows = mine_low.shape[1]
    for at, low, high in ((core, mine_low, mine_high), (1 - core, other_low, other_high)):
        out_ref[pl.ds(aligned(2 * at, rows), rows), :] = low[0].astype(jnp.float32)
        out_ref[pl.ds(aligned(2 * at + 1, rows), rows), :] = high[0].astype(jnp.float32)


def place_shared(meta, mine, other):
    _, rows, columns = mine.shape
    units = columns // 6
    low = pl.BlockSpec((1, rows, units), lambda i, j, m: (i, 0, j))
    high = pl.BlockSpec((1, rows, units), lambda i, j, m: (i, 0, 3 + j))
    outs = shape_of((4 * rows, 2 * columns), jnp.float32)
    return call(
        place_shared_kernel,
        "place_shared",
        meta,
        [mine, mine, other, other],
        (4, 3),
        [low, high, low, high],
        pl.BlockSpec((4 * rows, units), lambda i, j, m: (0, 4 * j + (m[1] ^ i))),
        outs,
        [],
        0,
        0,
    )


def place_heads_kernel(meta, *refs):
    mine, other, out_ref = refs[:4], refs[4], refs[5]
    core, chip = meta[0] & 1, meta[0] >> 1
    rows, columns = mine[0].shape
    group_width = columns - 2 * HEAD_SIZE
    for r in range(4):
        head = chip ^ r
        for at, pieces in ((core, [piece[...] for piece in mine]), (1 - core, other)):
            to = pl.ds(aligned(at, rows), rows)
            values = pieces[r].astype(jnp.float32)
            out_ref[to, pl.ds(aligned(head, group_width), group_width)] = values[:, :group_width]
            out_ref[to, pl.ds(aligned(4 * group_width // HEAD_SIZE + head, HEAD_SIZE), HEAD_SIZE)] = (
                values[:, group_width : group_width + HEAD_SIZE]
            )
            out_ref[
                to, pl.ds(aligned(4 * group_width // HEAD_SIZE + 4 + head, HEAD_SIZE), HEAD_SIZE)
            ] = values[:, group_width + HEAD_SIZE :]


def place_heads(meta, mine, other):
    rows, columns = mine[0].shape
    arrays = list(mine) + [other]
    outs = shape_of((2 * rows, 4 * columns), jnp.float32)
    return call(
        place_heads_kernel,
        "place_heads",
        meta,
        arrays,
        (1,),
        [whole(a) for a in arrays],
        whole(outs),
        outs,
        [],
        0,
        size_of(arrays + [outs]),
    )


def join_shared_kernel(meta, mine, other, out_ref):
    step = pl.program_id(0)
    rows = mine.shape[2]
    first = meta[0] ^ (2 * step)
    for i in range(4):
        at = 8 * (meta[1] ^ i)
        out_ref[pl.ds(aligned(at + first, rows), rows), :] = mine[0, i]
        out_ref[pl.ds(aligned(at + (first ^ 1), rows), rows), :] = other[0, i]


def join_shared(meta, mine, other):
    _, _, rows, columns = mine.shape
    block = pl.BlockSpec((1, 4, rows, columns), lambda r, m: (r, 0, 0, 0))
    outs = shape_of((32 * rows, columns), jnp.bfloat16)
    return call(
        join_shared_kernel,
        "join_shared",
        meta,
        [mine, other],
        (4,),
        [block, block],
        whole(outs),
        outs,
        [],
        0,
        size_of([mine, other, outs]),
    )


class Clock:
    def __init__(self):
        self.last = None

    def __call__(self, *values):
        if self.last is None:
            return values if len(values) > 1 else values[0]
        held = lax.optimization_barrier(tuple(values) + (self.last,))[:-1]
        return held if len(held) > 1 else held[0]

    def mark(self, value):
        self.last = value
        return value


EARLY = (
    "H", "W", "K", "S", "K", "W", "S", "W", "K", "S", "O", "S", "M", "M", "S", "O", "M", "S", "M", "R", "M", "K", "M", "K",
    "M", "K", "R", "M", "K", "M", "M", "M", "M", "R", "M", "M",
)
LATE = (
    "L", "0", "1", "0", "0", "L", "1", "1", "L", "L", "O", "0", "1", "L", "L", "1", "0", "O", "Q", "1", "O", "0", "L", "Q",
    "O", "L", "1", "Q", "1", "Q", "0", "O", "0", "Q", "L", "1", "0", "O", "Q", "S", "1", "0", "L", "O", "Q", "1", "S", "L",
    "0", "O", "Q", "L", "Q", "O", "S",
)


def fast_device(
    hidden,
    teacher,
    valid_mask,
    routes,
    route_gates,
    gain_in,
    query_key_value_weight,
    out_weight,
    gain_mid,
    shared_weight,
    expert_weight,
):
    token_rows, width = hidden.shape[1:]
    context_count, shard_count = 8, 4
    context_index = lax.axis_index("ctx").astype(jnp.int32)
    shard_index = lax.axis_index("wt").astype(jnp.int32)
    plain_meta = jnp.stack([context_index, shard_index])
    core = context_index & 1
    chip = context_index >> 1
    at_end = (shard_index == 0) | (shard_index == shard_count - 1)
    group_width = QUERY_HEADS // KEY_VALUE_HEADS * HEAD_SIZE
    query_width = QUERY_HEADS * HEAD_SIZE
    kv_width = KEY_VALUE_HEADS * HEAD_SIZE
    scale = 1.0 / math.sqrt(HEAD_SIZE)
    all_tokens = token_rows * context_count * shard_count
    shard_rows = query_key_value_weight.shape[0]
    half_rows = shard_rows // 2
    local_experts = expert_weight.shape[0]
    bf16, f32 = jnp.bfloat16, jnp.float32
    states = hidden[0]
    clock = Clock()
    have = {}

    def meta():
        return clock(plain_meta)

    def now(*values):
        return clock(*values)

    def ready(*values):
        values = clock(*values)
        clock.mark(values[0] if isinstance(values, tuple) or isinstance(values, list) else values)
        return values


    def hidden_chain():
        have["blocks"] = chips_exchange(jnp.broadcast_to(states, (4,) + states.shape))
        yield

    def qkv_chain():
        rows = lax.dynamic_slice_in_dim(query_key_value_weight, core * half_rows, half_rows, 0)
        half = jnp.concatenate(
            [
                lax.dynamic_slice_in_dim(rows, chip * group_width, group_width, 1),
                lax.dynamic_slice_in_dim(rows, query_width + chip * HEAD_SIZE, HEAD_SIZE, 1),
                lax.dynamic_slice_in_dim(
                    rows, query_width + kv_width + chip * HEAD_SIZE, HEAD_SIZE, 1
                ),
            ],
            axis=1,
        )
        came = line_swap(half, 1)
        yield
        pair = clock.mark(jnp.stack([half, now(came)]))
        came = line_swap(pair, 2)
        yield
        have["qkv_mine"] = clock.mark(jnp.concatenate([pair, now(came)]))
        have["qkv_other"] = flip(have["qkv_mine"], 1)
        yield

    def small_chain():
        expert_ids = jnp.arange(EXPERTS, dtype=jnp.int32)
        matrix = jnp.sum(
            jnp.where(
                routes[0][None, :, :] == expert_ids[:, None, None], route_gates[0][None, :, :], 0.0
            ),
            axis=-1,
        )
        have["valid"] = valid_mask[0].astype(f32)
        gains = jnp.concatenate([gain_in, gain_mid]).astype(f32).reshape(-1, token_rows)
        gain_rows = gains.shape[0]
        filled = EXPERTS + gain_rows
        pack = jnp.concatenate(
            [
                matrix,
                gains,
                jnp.full((32 - filled, token_rows), jnp.sum(have["valid"]), f32),
            ]
        )
        came = line_swap(pack, 1)
        yield
        pair = clock.mark(jnp.stack([pack, now(came)]))
        came = line_swap(pair, 2)
        yield
        all_packs = clock.mark(jnp.concatenate([pair, now(came)]))
        have["gates"] = [
            lax.dynamic_slice_in_dim(
                all_packs[i], shard_index * local_experts, local_experts, 0
            )[..., None]
            for i in range(4)
        ]
        gains = all_packs[:, EXPERTS:filled].reshape(4, 2, shard_rows)
        gains = jnp.stack([pick(gains, shard_index ^ i) for i in range(4)], axis=1)
        have["gains"] = gains.reshape(2, 1, width)
        total = jnp.broadcast_to(jnp.sum(all_packs[:, filled, 0]), (8, 128))
        yield
        total = now(total)
        for bit in (1, 2, 4):
            came = flip(total, bit)
            yield
            total = clock.mark(total + now(came))
        have["count"] = total[0, 0]
        yield

    def shared_chain():
        eighth = shard_rows // 8
        units = SF // shard_count
        piece = lax.dynamic_slice_in_dim(shared_weight, context_index * eighth, eighth, 0)
        piece = piece.reshape(eighth, 3, shard_count, units)

        piece = jnp.transpose(piece, (2, 0, 1, 3)).reshape(shard_count, eighth, 3 * units)
        parts = [pick(piece, shard_index ^ i) for i in range(4)]
        came = line_swap(now(jnp.stack([parts[1], parts[3]])), 1)
        yield
        came = now(came)
        mine = jnp.stack([parts[0], came[0]])
        came = line_swap(clock.mark(jnp.stack([parts[2], came[1]])), 2)
        yield
        pieces = clock.mark(jnp.concatenate([mine, now(came)]))
        came = flip(pieces, 2)
        yield
        pair = clock.mark(jnp.stack([pieces, now(came)]))
        came = flip(pair, 4)
        yield
        mine = clock.mark(jnp.concatenate([pair, now(came)]))
        other = flip(mine, 1)
        yield
        have["shared"] = join_shared(meta(), mine, other)
        clock.mark(have["shared"])
        yield

    def out_chain():
        half = lax.dynamic_slice_in_dim(now(out_weight), core * half_rows, half_rows, 0)
        came = line_exchange(jnp.broadcast_to(half, (4,) + half.shape))
        yield
        have["out_mine"] = clock.mark(now(came))
        have["out_other"] = flip(have["out_mine"], 1)
        yield

    def qkv_all_chain():
        half = lax.dynamic_slice_in_dim(
            now(have["qkv_slice"]), core * (width // 2), width // 2, 0
        )
        came = flip(half, 2)
        yield
        pair = clock.mark(jnp.stack([half, now(came)]))
        came = flip(pair, 4)
        yield
        have["rel_mine"] = clock.mark(jnp.concatenate([pair, now(came)]))
        have["rel_other"] = flip(have["rel_mine"], 1)
        yield

    def main_chain():
        gains = have["gains"]
        normed_in, query, pair, qkv_slice = project(
            meta(), have["blocks"], gains[0], have["qkv_mine"], have["qkv_other"], group_width
        )
        clock.mark(pair)
        have["normed_in"], have["qkv_slice"] = normed_in, qkv_slice
        pair_other = flip(pair, 1)
        yield
        mixed_heads, log_total = attend(meta(), query, pair, pair_other, scale)
        clock.mark(log_total)
        have["attend"] = (query, pair, pair_other, log_total, mixed_heads)
        parts = ready(*[pick(mixed_heads, chip ^ r) for r in range(4)])
        mixed = [parts[0]] + [flip(parts[r], 2 * r) for r in (1, 2, 3)]
        have["mixed"] = mixed
        yield
        out_full, middle, normed_mid = leave(
            meta(), mixed, have["out_mine"], have["out_other"], states, gains[1]
        )
        have["out_full"], have["middle"] = out_full, middle
        clock.mark(normed_mid)

        near, center = line_swap(normed_mid, 1), line_middle(normed_mid)
        yield
        gates, shared_slice = have["gates"], have["shared"]
        gate_ups, shared_gate_ups, outs = [], [], []

        def forward(rows, i):
            result = experts(meta(), rows, gates[i], expert_weight, shared_slice)
            clock.mark(result[2])
            gate_ups.append(result[0])
            shared_gate_ups.append(result[1])
            outs.append(result[2])

        forward(normed_mid, 0)
        yield
        near, center = now(near, center)
        far, outward = line_middle(near), line_outward(center)
        forward(near, 1)
        yield
        far, outward = now(far, outward)
        outward_far = line_outward(far)
        third = clock.mark(jnp.where(at_end, outward, far))
        forward(third, 2)
        yield
        outward_far = now(outward_far)
        fourth = clock.mark(jnp.where(at_end, outward_far, center))
        forward(fourth, 3)
        line_rows = [normed_mid, near, third, fourth]
        came = line_inward(outs[3])
        yield
        carried = clock.mark(outs[2] + now(came))
        inward, crossed = line_inward(carried), line_middle(carried)
        yield
        inward, crossed = now(inward, crossed)
        near_out, middle_out = ready(outs[1] + crossed, outs[3] + inward)
        near_out, middle_out = line_swap(near_out, 1), line_middle(middle_out)
        yield
        near_out, middle_out = now(near_out, middle_out)
        final_state = (
            middle + outs[0].astype(f32) + near_out.astype(f32) + middle_out.astype(f32)
        )
        valid = have["valid"]
        deviation = final_state - teacher[0].astype(f32)
        have["squared"] = jnp.sum(valid[:, None] * deviation * deviation)
        grad_final = all_tokens / have["count"] * valid[:, None] * deviation
        have["final"], have["grad_final"] = final_state.astype(bf16)[None], grad_final
        grad_low = clock.mark(grad_final.astype(bf16))
        near, center = line_swap(grad_low, 1), line_middle(grad_low)
        yield
        kept = []

        def backward(grads, i):
            kept.append(
                experts_back(
                    meta(),
                    grads,
                    gates[i],
                    gate_ups[i],
                    shared_gate_ups[i],
                    expert_weight,
                    shared_slice,
                )
            )
            clock.mark(kept[-1][4])

        backward(grad_low, 0)
        yield
        near, center = now(near, center)
        far, outward = line_middle(near), line_outward(center)
        backward(near, 1)
        yield
        far, outward = now(far, outward)
        outward_far = line_outward(far)
        third = clock.mark(jnp.where(at_end, outward, far))
        backward(third, 2)
        yield
        outward_far = now(outward_far)
        fourth = clock.mark(jnp.where(at_end, outward_far, center))
        backward(fourth, 3)
        have["line"] = (line_rows, [grad_low, near, third, fourth])
        have["experts"] = list(zip(*kept))
        yield


    def states_chain():
        outs = have["experts"][4]
        came = line_inward(outs[3])
        yield
        carried = clock.mark(outs[2] + now(came))
        inward, crossed = line_inward(carried), line_middle(carried)
        yield
        inward, crossed = now(inward, crossed)
        near_out, middle_out = ready(outs[1] + crossed, outs[3] + inward)
        near_out, middle_out = line_swap(near_out, 1), line_middle(middle_out)
        yield
        near_out, middle_out = now(near_out, middle_out)
        grad_normed = clock.mark(
            outs[0].astype(f32) + near_out.astype(f32) + middle_out.astype(f32)
        )
        grad_middle, grad_branch, grad_gain_mid, grad_mixed = enter_back(
            meta(),
            have["grad_final"],
            grad_normed,
            have["middle"],
            have["gains"][1],
            have["out_full"],
        )
        clock.mark(grad_branch)
        have["grad_branch"], have["grad_gain_mid"] = grad_branch, grad_gain_mid
        grad_mixed = chips_exchange(ready(grad_mixed))
        yield
        query, pair, pair_other, log_total, mixed_heads = have["attend"]
        grad_query, grad_pair, grad_other = attend_back(
            meta(), query, pair, pair_other, log_total, mixed_heads, grad_mixed, scale
        )
        clock.mark(grad_query)
        came = flip(grad_other, 1)
        yield
        grad_pair = grad_pair + now(came).astype(f32)
        projected = clock.mark(jnp.concatenate([grad_query, grad_pair.astype(bf16)], axis=-1))
        have["grad_projected"] = projected
        parts = chips_exchange(ready(projected))
        yield
        grad_hidden, grad_gain_in = finish(
            meta(),
            parts,
            have["rel_mine"],
            have["rel_other"],
            states,
            grad_middle,
            have["gains"][0],
        )
        clock.mark(grad_gain_in)
        have["grad_hidden"] = grad_hidden
        sums = jnp.concatenate(
            [grad_gain_in, have["grad_gain_mid"], jnp.full((6, width), have["squared"], f32)],
            axis=0,
        )
        for offset in (1, 2):
            came = line_swap(sums, offset)
            yield
            sums = clock.mark(sums + now(came))
        for bit in (1, 2, 4):
            came = flip(sums, bit)
            yield
            sums = clock.mark(sums + now(came))
        own = lax.dynamic_slice_in_dim(sums, shard_index * shard_rows, shard_rows, 1)
        have["sums"] = (own, 0.5 * sums[2, 0] / (have["count"] * width))
        yield

    def expert_chain(index):
        line_rows, line_grads = have["line"]
        grad_gate_ups, acts, shared_grads, shared_acts = have["experts"][:4]
        shared = (shared_grads, shared_acts) if index == 0 else None

        def grad_of(at):
            return clock.mark(
                expert_grad(
                    meta(),
                    2 * at + index,
                    at,
                    line_rows,
                    line_grads,
                    grad_gate_ups,
                    acts,
                    shared,
                )
            )

        came = flip(grad_of(1 - core), 1)
        yield
        keep = grad_of(core)
        yield
        x_first = index % 2 == 0
        first, second = (2, 4) if x_first else (4, 2)
        picked = ((1, 3), (0, 2)) if x_first else ((2, 3), (0, 1))
        pieces = keep.shape[1] // 96

        def split_sum(keep, came):
            return [
                jnp.stack([keep[i] + came[i] for i in places]) for places in picked
            ]

        give, keep = blend(meta(), "blend_split", split_sum, [keep, came], pieces)
        clock.mark(give)
        came = flip(give, first)
        yield
        give, keep = blend(
            meta(), "blend_pair", lambda k, c: [k[1] + c[1], k[0] + c[0]], [keep, came], pieces
        )
        clock.mark(give)
        came = flip(give, second)
        yield
        own = clock.mark(blend(meta(), "blend_sum", lambda k, c: k + c, [keep, came], pieces))
        came = flip(own, second)
        yield
        pair = clock.mark(
            blend(meta(), "blend_stack", lambda a, b: jnp.stack([a, b]), [own, came], pieces)
        )
        came = flip(pair, first)
        pair_other = flip(pair, 1)
        yield

        def place(of_other, value, far):
            stride, offset = (2, far) if x_first else (1, 2 * far)
            have["grad_experts"] = place_sum(
                meta(),
                have.get("grad_experts"),
                index,
                of_other,
                expert_weight.shape,
                value,
                stride,
                offset,
            )
            clock.mark(have["grad_experts"])

        place(0, pair, 0)
        yield
        place(1, pair_other, 0)
        yield
        came = now(came)
        came_other = flip(came, 1)
        if index == 0:
            have["shared_sum"] = jnp.stack([pair[0], came[0], pair[1], came[1]])[:, shard_rows:]
        yield
        place(0, came, 1)
        yield
        place(1, came_other, 1)
        yield

    def shared_grad_chain():
        total = now(have["shared_sum"])
        parts = ready(*[pick(total, chip ^ shard_index ^ i) for i in range(4)])
        came = [line_swap(parts[i], i) for i in (1, 2, 3)]
        yield
        mine = clock.mark(jnp.stack([parts[0]] + list(now(*came))))
        other = flip(mine, 1)
        yield
        have["grad_shared"] = clock.mark(place_shared(meta(), mine, other))
        yield

    def line_reduce_steps(keep, came):
        came = now(came)
        parts = [keep[i] + came[i] for i in range(4)]
        came = line_inward(clock.mark(parts[3]))
        yield
        carried = clock.mark(parts[2] + now(came))
        inward, crossed = line_inward(carried), line_middle(carried)
        yield
        inward, crossed = now(inward, crossed)
        near_out, middle_out = ready(parts[1] + crossed, parts[3] + inward)
        near_out, middle_out = line_swap(near_out, 1), line_middle(middle_out)
        yield
        near_out, middle_out = now(near_out, middle_out)
        have["line_sum"] = clock.mark(
            (parts[0].astype(f32) + near_out.astype(f32) + middle_out.astype(f32)).astype(bf16)
        )

    def out_grad_chain():
        mixed = jnp.concatenate(have["mixed"], axis=1)
        keep, give = weight_grad(
            meta(), chip ^ shard_index, [([mixed], [have["grad_branch"][None]])], 0
        )
        clock.mark(keep)
        came = flip(give, 1)
        yield
        yield from line_reduce_steps(keep, came)
        total = have["line_sum"]
        yield
        total = ready(total)
        came = flip(total, 2)
        yield
        total = clock.mark(total + now(came))
        came = flip(total, 4)
        yield
        mine = clock.mark(total + now(came))
        other = flip(mine, 1)
        yield
        mine, other = now(mine, other)
        have["grad_out"] = clock.mark(
            jnp.where(
                core == 0,
                jnp.concatenate([mine, other], axis=0),
                jnp.concatenate([other, mine], axis=0),
            ).astype(f32)
        )
        yield

    def qkv_grad_chain():
        normed_in = have["normed_in"].reshape(4 * token_rows, width)
        projected = have["grad_projected"].reshape(1, 4 * token_rows, -1)
        keep, give = weight_grad(meta(), shard_index, [([normed_in], [projected])], 0)
        clock.mark(keep)
        came = flip(give, 1)
        yield
        yield from line_reduce_steps(keep, came)
        own = have["line_sum"]
        yield
        own = ready(own)
        came = flip(own, 2)
        yield
        pair = clock.mark(jnp.stack([own, now(came)]))
        came = flip(pair, 4)
        yield
        mine = clock.mark(jnp.concatenate([pair, now(came)]))
        other = flip(mine, 1)
        yield
        have["grad_qkv"] = clock.mark(place_heads(meta(), [mine[r] for r in range(4)], other))
        yield

    early = {
        "H": hidden_chain(),
        "W": qkv_chain(),
        "S": shared_chain(),
        "O": out_chain(),
        "K": small_chain(),
        "R": qkv_all_chain(),
        "M": main_chain(),
    }
    late = {
        "L": states_chain(),
        "S": shared_grad_chain(),
        "O": out_grad_chain(),
        "Q": qkv_grad_chain(),
    }
    for index in range(local_experts // 2):
        late[str(index)] = expert_chain(index)
    for chains, order in ((early, EARLY), (late, LATE)):
        for name in order:
            next(chains[name], None)
        for name in chains:
            for _ in chains[name]:
                pass

    own, loss_value = have["sums"]
    return (
        have["final"],
        loss_value,
        have["grad_hidden"],
        own[0],
        have["grad_qkv"],
        have["grad_out"],
        own[1],
        have["grad_shared"],
        have["grad_experts"],
    )


def solution(mesh):
    in_specs = (
        P("wt", "ctx", None),
        P("wt", "ctx", None),
        P("wt", "ctx"),
        P("wt", "ctx", None),
        P("wt", "ctx", None),
        P("wt"),
        P("wt", None),
        P("wt", None),
        P("wt"),
        P("wt", None),
        P("wt", None, None),
    )
    out_specs = (
        P("wt", "ctx", None),
        P(),
        P("wt", "ctx", None),
        P("wt"),
        P("wt", None),
        P("wt", None),
        P("wt"),
        P("wt", None),
        P("wt", None, None),
    )
    plane_of_eight = dict(mesh.shape) == {"ctx": 8, "wt": 4}
    return jax.shard_map(
        fast_device if plane_of_eight else on_device, mesh=mesh, in_specs=in_specs, out_specs=out_specs, check_vma=False
    )
```

```python
import functools
import math

import jax
import jax.numpy as jnp
from jax import lax
from jax.experimental import pallas as pl
from jax.experimental.pallas import tpu as pltpu
from jax.sharding import PartitionSpec as P

QUERY_HEADS = 12
KEY_VALUE_HEADS = 4
HEAD_SIZE = 128
F = 512
SF = 1024
EXPERTS = 16
TOP = 6


norm_eps = 1e-05
masked_score = -1e30


def sigmoid_linear(values):
    return values * jax.nn.sigmoid(values)


def silu_slope(values):
    sigma_value = jax.nn.sigmoid(values)
    return sigma_value * (1.0 + values * (1.0 - sigma_value))


def normalize(values):
    inverse = lax.rsqrt(jnp.mean(values * values, axis=-1, keepdims=True) + norm_eps)
    return (values * inverse, inverse)


def norm_back(grad_normed, scaled, inverse, gain_vector):
    grad_scaled = grad_normed * gain_vector
    return inverse * (grad_scaled - scaled * jnp.mean(grad_scaled * scaled, axis=-1, keepdims=True))


def positions(row_ids, token_rows, context_count):
    piece_index = row_ids // token_rows
    within = row_ids % token_rows
    half_rows = token_rows // 2
    mirrored = jnp.where(within < half_rows, piece_index, 2 * context_count - 1 - piece_index)
    return mirrored * half_rows + within % half_rows


def route_tables(local_routes, local_gates, experts, capacity):
    token_rows = local_routes.shape[0]
    flat_routes = local_routes.reshape(-1)
    one_hot = (flat_routes[:, None] == jnp.arange(experts, dtype=jnp.int32)[None, :]).astype(
        jnp.int32
    )
    earlier = jnp.cumsum(one_hot, axis=0) - one_hot
    slot_index = jnp.sum(earlier * one_hot, axis=1)
    token_index = jnp.arange(flat_routes.shape[0], dtype=jnp.int32) // local_routes.shape[1]
    slot_table = (
        jnp.full((experts, capacity), token_rows, jnp.int32)
        .at[flat_routes, slot_index]
        .set(token_index)
    )
    slot_gate = (
        jnp.zeros((experts, capacity), jnp.float32)
        .at[flat_routes, slot_index]
        .set(local_gates.reshape(-1))
    )
    return (slot_table, slot_gate)


def block_scores(query_rows, key_block, key_position, query_place, score_scale):
    scores = (
        jnp.einsum("qhgd,khd->qhgk", query_rows, key_block, preferred_element_type=jnp.float32)
        * score_scale
    )
    allowed = key_position[None, None, None, :] <= query_place[:, None, None, None]
    return jnp.where(allowed, scores, masked_score)


def attend_forward(
    query_rows, blocked_keys, blocked_values, place_blocks, query_place, score_scale
):
    head_shape = query_rows.shape[:3]

    def online_step(running, block_args):
        running_max, running_sum, accumulated = running
        key_block, value_block, key_position = block_args
        scores = block_scores(query_rows, key_block, key_position, query_place, score_scale)
        new_max = jnp.maximum(running_max, jnp.max(scores, axis=-1))
        rescale = jnp.exp(running_max - new_max)
        powers = jnp.exp(scores - new_max[..., None])
        new_sum = running_sum * rescale + jnp.sum(powers, axis=-1)
        weighted = jnp.einsum(
            "qhgk,khd->qhgd",
            powers.astype(jnp.bfloat16),
            value_block,
            preferred_element_type=jnp.float32,
        )
        return ((new_max, new_sum, accumulated * rescale[..., None] + weighted), None)

    initial = (
        jnp.full(head_shape, masked_score, jnp.float32),
        jnp.zeros(head_shape, jnp.float32),
        jnp.zeros(query_rows.shape, jnp.float32),
    )
    row_max, row_sum, accumulated = lax.scan(
        online_step, initial, (blocked_keys, blocked_values, place_blocks)
    )[0]
    log_total = row_max + jnp.log(row_sum)
    return (accumulated / row_sum[..., None], log_total)


def attend_backward(
    query_rows,
    blocked_keys,
    blocked_values,
    place_blocks,
    query_place,
    log_total,
    attention_output_gradient,
    attention_output,
    score_scale,
):
    row_delta = jnp.sum(attention_output_gradient.astype(jnp.float32) * attention_output, axis=-1)

    def block_grads(grad_queries, block_args):
        key_block, value_block, key_position = block_args
        scores = block_scores(query_rows, key_block, key_position, query_place, score_scale)
        probabilities = jnp.exp(scores - log_total[..., None])
        grad_probs = jnp.einsum(
            "qhgd,khd->qhgk",
            attention_output_gradient,
            value_block,
            preferred_element_type=jnp.float32,
        )
        grad_scores = (probabilities * (grad_probs - row_delta[..., None])).astype(jnp.bfloat16)
        grad_queries = grad_queries + jnp.einsum(
            "qhgk,khd->qhgd", grad_scores, key_block, preferred_element_type=jnp.float32
        )
        grad_keys = (
            jnp.einsum(
                "qhgk,qhgd->khd", grad_scores, query_rows, preferred_element_type=jnp.float32
            )
            * score_scale
        )
        grad_values = jnp.einsum(
            "qhgk,qhgd->khd",
            probabilities.astype(jnp.bfloat16),
            attention_output_gradient,
            preferred_element_type=jnp.float32,
        )
        return (grad_queries, (grad_keys, grad_values))

    grad_queries, (grad_keys, grad_values) = lax.scan(
        block_grads,
        jnp.zeros(query_rows.shape, jnp.float32),
        (blocked_keys, blocked_values, place_blocks),
    )
    return (grad_queries * score_scale, grad_keys, grad_values)


def gate_up_grads(grad_act, gate_up, hidden_units):
    gate_part = gate_up[..., :hidden_units]
    up_part = gate_up[..., hidden_units:]
    return jnp.concatenate(
        [grad_act * up_part * silu_slope(gate_part), grad_act * sigmoid_linear(gate_part)], axis=-1
    ).astype(jnp.bfloat16)


def on_device(
    hidden,
    teacher,
    valid_mask,
    routes,
    route_gates,
    gain_in,
    query_key_value_weight,
    out_weight,
    gain_mid,
    shared_weight,
    expert_weight,
):
    token_rows = hidden.shape[1]
    model_width = hidden.shape[2]
    context_count = lax.axis_size("ctx")
    shard_count = lax.axis_size("wt")
    seq_rows = token_rows * context_count
    all_tokens = seq_rows * shard_count
    query_groups = QUERY_HEADS // KEY_VALUE_HEADS
    query_total_width = QUERY_HEADS * HEAD_SIZE
    key_value_width = KEY_VALUE_HEADS * HEAD_SIZE
    score_scale = 1.0 / math.sqrt(HEAD_SIZE)
    key_row_count = min(512, seq_rows)
    number_of_blocks = seq_rows // key_row_count
    capacity = token_rows * TOP // 12
    local_experts = expert_weight.shape[0]
    contract_last = (((1,), (1,)), ((), ()))
    contract_first = (((0,), (0,)), ((), ()))
    full_gain_in, full_qkv, full_out, full_gain_mid, full_shared = (
        lax.all_gather(gain_in, "wt", axis=0, tiled=True),
        lax.all_gather(query_key_value_weight, "wt", axis=0, tiled=True),
        lax.all_gather(out_weight, "wt", axis=0, tiled=True),
        lax.all_gather(gain_mid, "wt", axis=0, tiled=True),
        lax.all_gather(shared_weight, "wt", axis=0, tiled=True),
    )
    gain_in_float = full_gain_in.astype(jnp.float32)
    gain_mid_float = full_gain_mid.astype(jnp.float32)
    inputs = hidden[0].astype(jnp.float32)
    scaled_in, inverse_in = normalize(inputs)
    normed_in = (scaled_in * gain_in_float).astype(jnp.bfloat16)
    projected_rows = jnp.dot(normed_in, full_qkv, preferred_element_type=jnp.float32).astype(
        jnp.bfloat16
    )
    query_rows = projected_rows[:, :query_total_width].reshape(
        token_rows, KEY_VALUE_HEADS, query_groups, HEAD_SIZE
    )
    context_local = projected_rows[:, query_total_width:]
    context_gathered = lax.all_gather(context_local, "ctx", axis=0, tiled=True)
    context_index = lax.axis_index("ctx")
    query_place = positions(
        context_index * token_rows + jnp.arange(token_rows, dtype=jnp.int32),
        token_rows,
        context_count,
    )
    place_blocks = positions(
        jnp.arange(seq_rows, dtype=jnp.int32), token_rows, context_count
    ).reshape(number_of_blocks, key_row_count)
    blocked_keys = context_gathered[:, :key_value_width].reshape(
        number_of_blocks, key_row_count, KEY_VALUE_HEADS, HEAD_SIZE
    )
    blocked_values = context_gathered[:, key_value_width:].reshape(
        number_of_blocks, key_row_count, KEY_VALUE_HEADS, HEAD_SIZE
    )
    attention_output, log_total = attend_forward(
        query_rows, blocked_keys, blocked_values, place_blocks, query_place, score_scale
    )
    mixed_rows = attention_output.reshape(token_rows, query_total_width).astype(jnp.bfloat16)
    middle = inputs + jnp.dot(mixed_rows, full_out, preferred_element_type=jnp.float32)
    scaled_mid, inverse_mid = normalize(middle)
    normed_mid = (scaled_mid * gain_mid_float).astype(jnp.bfloat16)
    shared_gate_up = jnp.dot(
        normed_mid, full_shared[:, : 2 * SF], preferred_element_type=jnp.float32
    )
    shared_act = (sigmoid_linear(shared_gate_up[:, :SF]) * shared_gate_up[:, SF:]).astype(
        jnp.bfloat16
    )
    shared_out = lax.dot_general(
        shared_act, full_shared[:, 2 * SF :], contract_last, preferred_element_type=jnp.float32
    )
    slot_table, slot_gate = route_tables(routes[0], route_gates[0], EXPERTS, capacity)
    padded_rows = jnp.concatenate([normed_mid, jnp.zeros((1, model_width), jnp.bfloat16)], axis=0)
    expert_rows = jnp.take(padded_rows, slot_table, axis=0)
    arrived = lax.all_to_all(expert_rows, "wt", split_axis=0, concat_axis=0, tiled=True)
    slot_count = arrived.shape[1]
    grouped = arrived.reshape(shard_count, local_experts, slot_count, model_width)
    owner_gate_up = jnp.einsum(
        "wesd,edf->wesf", grouped, expert_weight[:, :, : 2 * F], preferred_element_type=jnp.float32
    )
    owner_act = (sigmoid_linear(owner_gate_up[..., :F]) * owner_gate_up[..., F:]).astype(
        jnp.bfloat16
    )
    owner_out = jnp.einsum(
        "wesf,edf->wesd",
        owner_act,
        expert_weight[:, :, 2 * F :],
        preferred_element_type=jnp.float32,
    ).astype(jnp.bfloat16)
    returned = lax.all_to_all(
        owner_out.reshape(shard_count * local_experts, slot_count, model_width),
        "wt",
        split_axis=0,
        concat_axis=0,
        tiled=True,
    )
    expert_out, owner_rows, owner_gate_up, owner_act = (
        returned,
        arrived,
        owner_gate_up.reshape(shard_count * local_experts, slot_count, 2 * F),
        owner_act.reshape(shard_count * local_experts, slot_count, F),
    )
    routed = (
        jnp.zeros((token_rows + 1, model_width), jnp.float32)
        .at[slot_table]
        .add(expert_out.astype(jnp.float32) * slot_gate[..., None])[:token_rows]
    )
    final_state = middle + shared_out + routed
    valid_float = valid_mask[0].astype(jnp.float32)
    deviation = final_state - teacher[0].astype(jnp.float32)
    squared_local = jnp.sum(valid_float[:, None] * deviation * deviation)
    count_local = jnp.sum(valid_float)
    squared_total, valid_count = lax.psum((squared_local, count_local), ("ctx", "wt"))
    loss_value = 0.5 * squared_total / (valid_count * model_width)
    grad_final = all_tokens / valid_count * valid_float[:, None] * deviation
    grad_shared_out = grad_final.astype(jnp.bfloat16)
    grad_shared_act = jnp.dot(
        grad_shared_out, full_shared[:, 2 * SF :], preferred_element_type=jnp.float32
    )
    grad_shared_down = lax.dot_general(
        grad_shared_out, shared_act, contract_first, preferred_element_type=jnp.float32
    )
    grad_shared_gate_up = gate_up_grads(grad_shared_act, shared_gate_up, SF)
    grad_normed_mid = lax.dot_general(
        grad_shared_gate_up,
        full_shared[:, : 2 * SF],
        contract_last,
        preferred_element_type=jnp.float32,
    )
    grad_shared_front = lax.dot_general(
        normed_mid, grad_shared_gate_up, contract_first, preferred_element_type=jnp.float32
    )
    grad_shared_full = jnp.concatenate([grad_shared_front, grad_shared_down], axis=1)
    padded_grads = jnp.concatenate([grad_final, jnp.zeros((1, model_width), jnp.float32)], axis=0)
    grad_expert_out = (jnp.take(padded_grads, slot_table, axis=0) * slot_gate[..., None]).astype(
        jnp.bfloat16
    )
    grad_arrived = lax.all_to_all(grad_expert_out, "wt", split_axis=0, concat_axis=0, tiled=True)
    grad_grouped = grad_arrived.reshape(shard_count, local_experts, capacity, model_width)
    owner_gate_up_grouped = owner_gate_up.reshape(shard_count, local_experts, capacity, 2 * F)
    owner_act_grouped = owner_act.reshape(shard_count, local_experts, capacity, F)
    owner_rows_grouped = owner_rows.reshape(shard_count, local_experts, capacity, model_width)
    grad_owner_act = jnp.einsum(
        "wecd,edf->wecf",
        grad_grouped,
        expert_weight[:, :, 2 * F :],
        preferred_element_type=jnp.float32,
    )
    grad_owner_gate_up = gate_up_grads(grad_owner_act, owner_gate_up_grouped, F)
    grad_owner_rows = jnp.einsum(
        "wecf,edf->wecd",
        grad_owner_gate_up,
        expert_weight[:, :, : 2 * F],
        preferred_element_type=jnp.float32,
    ).astype(jnp.bfloat16)
    front = jnp.einsum(
        "wecd,wecf->edf", owner_rows_grouped, grad_owner_gate_up, preferred_element_type=jnp.float32
    )
    back = jnp.einsum(
        "wecd,wecf->edf", grad_grouped, owner_act_grouped, preferred_element_type=jnp.float32
    )
    expert_grad = jnp.concatenate([front, back], axis=2)
    grad_rows = lax.all_to_all(
        grad_owner_rows.reshape(shard_count * local_experts, capacity, model_width),
        "wt",
        split_axis=0,
        concat_axis=0,
        tiled=True,
    )
    grad_normed_mid = (
        grad_normed_mid
        + jnp.zeros((token_rows + 1, model_width), jnp.float32)
        .at[slot_table]
        .add(grad_rows.astype(jnp.float32))[:token_rows]
    )
    grad_gain_mid_local = jnp.sum(grad_normed_mid * scaled_mid, axis=0)
    grad_middle = grad_final + norm_back(grad_normed_mid, scaled_mid, inverse_mid, gain_mid_float)
    grad_branch = grad_middle.astype(jnp.bfloat16)
    mixed_gradient = lax.dot_general(
        grad_branch, full_out, contract_last, preferred_element_type=jnp.float32
    ).astype(jnp.bfloat16)
    grad_out_local = lax.dot_general(
        mixed_rows, grad_branch, contract_first, preferred_element_type=jnp.float32
    )
    context_recomputed = lax.all_gather(context_local, "ctx", axis=0, tiled=True)
    backward_keys = context_recomputed[:, :key_value_width].reshape(
        number_of_blocks, key_row_count, KEY_VALUE_HEADS, HEAD_SIZE
    )
    backward_values = context_recomputed[:, key_value_width:].reshape(
        number_of_blocks, key_row_count, KEY_VALUE_HEADS, HEAD_SIZE
    )
    attention_output_gradient = mixed_gradient.reshape(
        token_rows, KEY_VALUE_HEADS, query_groups, HEAD_SIZE
    )
    grad_queries, grad_keys, grad_values = attend_backward(
        query_rows,
        backward_keys,
        backward_values,
        place_blocks,
        query_place,
        log_total,
        attention_output_gradient,
        attention_output,
        score_scale,
    )
    grad_context_all = jnp.concatenate(
        [
            grad_keys.reshape(seq_rows, key_value_width),
            grad_values.reshape(seq_rows, key_value_width),
        ],
        axis=1,
    )
    grad_context = lax.psum_scatter(
        grad_context_all.astype(jnp.bfloat16), "ctx", scatter_dimension=0, tiled=True
    ).astype(jnp.float32)
    grad_projected = jnp.concatenate(
        [grad_queries.reshape(token_rows, query_total_width), grad_context], axis=1
    ).astype(jnp.bfloat16)
    grad_normed_in = lax.dot_general(
        grad_projected, full_qkv, contract_last, preferred_element_type=jnp.float32
    )
    grad_qkv_local = lax.dot_general(
        normed_in, grad_projected, contract_first, preferred_element_type=jnp.float32
    )
    grad_gain_in_local = jnp.sum(grad_normed_in * scaled_in, axis=0)
    grad_inputs = grad_middle + norm_back(grad_normed_in, scaled_in, inverse_in, gain_in_float)
    weight_sums = (
        lax.psum_scatter(
            grad_gain_in_local.astype(jnp.bfloat16), "wt", scatter_dimension=0, tiled=True
        ).astype(jnp.float32),
        lax.psum_scatter(
            grad_qkv_local.astype(jnp.bfloat16), "wt", scatter_dimension=0, tiled=True
        ).astype(jnp.float32),
        lax.psum_scatter(
            grad_out_local.astype(jnp.bfloat16), "wt", scatter_dimension=0, tiled=True
        ).astype(jnp.float32),
        lax.psum_scatter(
            grad_gain_mid_local.astype(jnp.bfloat16), "wt", scatter_dimension=0, tiled=True
        ).astype(jnp.float32),
        lax.psum_scatter(
            grad_shared_full.astype(jnp.bfloat16), "wt", scatter_dimension=0, tiled=True
        ).astype(jnp.float32),
    )
    summed = (
        lax.psum(weight_sums[0].astype(jnp.bfloat16), "ctx").astype(jnp.float32),
        lax.psum(weight_sums[1].astype(jnp.bfloat16), "ctx").astype(jnp.float32),
        lax.psum(weight_sums[2].astype(jnp.bfloat16), "ctx").astype(jnp.float32),
        lax.psum(weight_sums[3].astype(jnp.bfloat16), "ctx").astype(jnp.float32),
        lax.psum(weight_sums[4].astype(jnp.bfloat16), "ctx").astype(jnp.float32),
        lax.psum(expert_grad.astype(jnp.bfloat16), "ctx").astype(jnp.float32),
    )
    return (
        final_state.astype(jnp.bfloat16)[None],
        loss_value,
        grad_inputs[None],
        summed[0],
        summed[1],
        summed[2],
        summed[3],
        summed[4],
        summed[5],
    )


PLANE = [[0, 2, 4, 6], [1, 3, 5, 7]]
COSTS = {
    "project": 0.3,
    "attend": 0.3,
    "leave": 0.3,
    "join_shared": 0.3,
    "experts": 0.3,
    "experts_back": 0.3,
    "enter_back": 0.3,
    "attend_back": 0.3,
    "finish": 0.3,
    "weight_grad": 0.3,
    "expert_grad": 0.3,
    "blend_split": 0.3,
    "blend_pair": 0.3,
    "blend_sum": 0.3,
    "blend_stack": 0.3,
    "place_sum": 0.3,
    "place_shared": 0.3,
    "place_heads": 0.3,
}


def flip(value, bit):
    return lax.ppermute(value, "ctx", [(index, index ^ bit) for index in range(8)])


def line_swap(value, offset):
    return lax.ppermute(value, "wt", [(index, index ^ offset) for index in range(4)])


def line_middle(value):
    return lax.ppermute(value, "wt", [(1, 2), (2, 1)])


def line_outward(value):
    return lax.ppermute(value, "wt", [(1, 0), (2, 3)])


def line_inward(value):
    return lax.ppermute(value, "wt", [(0, 1), (3, 2)])


def line_gather(value, at_end):
    near = line_swap(value, 1)
    middle = line_middle(value)
    middle_far = line_middle(near)
    outward = line_outward(middle)
    outward_far = line_outward(middle_far)
    return [
        value,
        near,
        jnp.where(at_end, outward, middle_far),
        jnp.where(at_end, outward_far, middle),
    ]


def line_reduce(parts):
    far = line_inward(parts[3])
    carried = parts[2] + far
    inward = line_inward(carried)
    crossed = line_middle(carried)
    near = line_swap(parts[1] + crossed, 1)
    middle = line_middle(parts[3] + inward)
    return (
        parts[0].astype(jnp.float32) + near.astype(jnp.float32) + middle.astype(jnp.float32)
    )


def chips_exchange(blocks):
    return lax.all_to_all(
        blocks,
        "ctx",
        split_axis=0,
        concat_axis=0,
        tiled=True,
        axis_index_groups=PLANE,
    )


def line_exchange(blocks):
    return lax.all_to_all(blocks, "wt", split_axis=0, concat_axis=0, tiled=True)


def chips_gather(value, x_last):
    along_x = flip(value, 2)
    along_y = flip(value, 4)
    corner = flip(along_y, 2) if x_last else flip(along_x, 4)
    return [value, along_x, along_y, corner]


def core_swap(values):
    return [flip(value, 1) for value in values]


def everywhere_sum(value):
    for bit in (1, 2, 4):
        value = value + flip(value, bit)
    for offset in (1, 2):
        value = value + line_swap(value, offset)
    return value


def pick(blocks, index):
    return lax.dynamic_index_in_dim(blocks, index, 0, keepdims=False)


def chips_reduce(keep, came):
    half = keep.shape[1] // 2
    upper = keep[:, :half] + came[:, :half]
    lower = keep[:, half:] + came[:, half:]
    upper_came = flip(upper[1::2], 2)
    lower_came = flip(lower[2:], 4)
    upper = upper[0::2] + upper_came
    lower = lower[:2] + lower_came
    upper_came = flip(upper[1], 4)
    lower_came = flip(lower[1], 2)
    return jnp.concatenate([upper[0] + upper_came, lower[0] + lower_came], axis=0)


def dot_plain(left, right):
    return lax.dot_general(
        left, right, (((1,), (0,)), ((), ())), preferred_element_type=jnp.float32
    )


def dot_last(left, right):
    return lax.dot_general(
        left, right, (((1,), (1,)), ((), ())), preferred_element_type=jnp.float32
    )


def dot_first(left, right):
    return lax.dot_general(
        left, right, (((0,), (0,)), ((), ())), preferred_element_type=jnp.float32
    )


def call(kernel, name, meta, arrays, grid, in_specs, out_specs, out_shape, scratch, flops, moved):
    return pl.pallas_call(
        kernel,
        grid_spec=pltpu.PrefetchScalarGridSpec(
            num_scalar_prefetch=1,
            grid=grid,
            in_specs=in_specs,
            out_specs=out_specs,
            scratch_shapes=scratch,
        ),
        out_shape=out_shape,
        compiler_params=pltpu.CompilerParams(vmem_limit_bytes=48 * 1024 * 1024),
        cost_estimate=pl.CostEstimate(
            flops=int(COSTS.get(name, 1.0) * 1e9), bytes_accessed=1000, transcendentals=0
        ),
        name=name,
    )(meta, *arrays)


def whole(array):
    rank = len(array.shape)
    return pl.BlockSpec(tuple(array.shape), lambda *_: (0,) * rank)


def shape_of(shape, dtype):
    return jax.ShapeDtypeStruct(shape, dtype)


def size_of(arrays):
    return sum(math.prod(a.shape) * a.dtype.itemsize for a in arrays)


def blend(meta, name, function, arrays, pieces=4):
    rows = arrays[0].shape[-2]
    tile = rows // pieces
    outs = jax.eval_shape(function, *[shape_of(a.shape, a.dtype) for a in arrays])
    many = isinstance(outs, (list, tuple))
    outs = list(outs) if many else [outs]

    def spec(a):
        rank = len(a.shape)
        lead = a.shape[:-2]
        return pl.BlockSpec(
            tuple(lead) + (tile, a.shape[-1]),
            lambda i, m: (0,) * (rank - 2) + (i, 0),
        )

    def kernel(meta_ref, *refs):
        result = function(*[ref[...] for ref in refs[: len(arrays)]])
        result = list(result) if many else [result]
        for ref, value in zip(refs[len(arrays) :], result):
            ref[...] = value

    result = call(
        kernel,
        name,
        meta,
        arrays,
        (pieces,),
        [spec(a) for a in arrays],
        [spec(a) for a in outs],
        outs,
        [],
        0,
        0,
    )
    return result if many else result[0]


def aligned(value, step):
    return pl.multiple_of(value * step, step)


def project_kernel(meta, blocks_ref, gain_ref, mine, other, *refs):
    normed_ref, query_ref, pair_ref, weight_ref = refs
    core = meta[0] & 1
    rows = mine.shape[1]

    @pl.when(pl.program_id(0) == 0)
    def _():
        for i in range(4):
            at = 2 * (meta[1] ^ i)
            weight_ref[pl.ds(aligned(at + core, rows), rows), :] = mine[i]
            weight_ref[pl.ds(aligned(at + 1 - core, rows), rows), :] = other[i]

    states = blocks_ref[0].astype(jnp.float32)
    inverse = lax.rsqrt(jnp.mean(states * states, axis=-1, keepdims=True) + norm_eps)
    normed = (states * inverse * gain_ref[...]).astype(jnp.bfloat16)
    normed_ref[0] = normed
    projected = dot_plain(normed, weight_ref[...]).astype(jnp.bfloat16)
    query_width = query_ref.shape[-1]
    query_ref[0] = projected[:, :query_width]
    pair_ref[0] = projected[:, query_width:]


def project(meta, blocks, gain, mine, other, query_width):
    _, token_rows, width = blocks.shape
    columns = mine.shape[2]
    arrays = [blocks, gain, mine, other]
    outs = [
        shape_of((4, token_rows, width), jnp.bfloat16),
        shape_of((4, token_rows, query_width), jnp.bfloat16),
        shape_of((4, token_rows, columns - query_width), jnp.bfloat16),
        shape_of((width, columns), jnp.bfloat16),
    ]
    return call(
        project_kernel,
        "project",
        meta,
        arrays,
        (4,),
        [pl.BlockSpec((1, token_rows, width), lambda r, m: (r, 0, 0))]
        + [whole(a) for a in arrays[1:]],
        [
            pl.BlockSpec((1, token_rows, width), lambda r, m: (r, 0, 0)),
            pl.BlockSpec((1, token_rows, query_width), lambda r, m: (r, 0, 0)),
            pl.BlockSpec((1, token_rows, columns - query_width), lambda r, m: (r, 0, 0)),
            whole(outs[3]),
        ],
        outs,
        [],
        2 * 4 * token_rows * width * columns,
        size_of(arrays) + size_of(outs),
    )


def sort_pairs(meta, mine_ref, other_ref, keys, values):
    half = mine_ref.shape[1] // 2
    for slot in range(16):
        block, part = (slot, 0) if slot < 8 else (15 - slot, 1)
        place = block >> 1
        rows = pl.ds(part * half, half)
        to = pl.ds(slot * half, half)

        @pl.when((meta[0] & 1) == (block & 1))
        def _():
            keys[to, :] = mine_ref[place, rows, :HEAD_SIZE]
            values[to, :] = mine_ref[place, rows, HEAD_SIZE:]

        @pl.when((meta[0] & 1) != (block & 1))
        def _():
            keys[to, :] = other_ref[place, rows, :HEAD_SIZE]
            values[to, :] = other_ref[place, rows, HEAD_SIZE:]


def stack_heads(rows):
    count = rows.shape[1] // HEAD_SIZE
    return jnp.concatenate(
        [rows[:, h * HEAD_SIZE : (h + 1) * HEAD_SIZE] for h in range(count)], axis=0
    )


def unstack_heads(rows, count):
    each = rows.shape[0] // count
    return jnp.concatenate([rows[h * each : (h + 1) * each] for h in range(count)], axis=1)


def step_slot(meta):
    step = pl.program_id(0)
    block = 2 * (step >> 1) + (meta[0] & 1)
    return jnp.where((step & 1) == 0, block, 15 - block)


def allowed_pairs(start, slot, shape, half):
    key_place = start + lax.broadcasted_iota(jnp.int32, shape, 0)
    query_place = slot * half + (lax.broadcasted_iota(jnp.int32, shape, 1) & (half - 1))
    return key_place <= query_place


def key_spans(step, half, span):
    pairs = (step // 2 if step % 2 == 0 else 7 - step // 2) + 1
    rows = pairs * 2 * half
    return [(at, min(span, rows - at)) for at in range(0, rows, span)]


def attend_kernel(scale, span, meta, query_ref, mine_ref, other_ref, *refs):
    out_ref, log_ref, keys, values, values_turned = refs
    half, group_width = query_ref.shape[1:]
    count = group_width // HEAD_SIZE

    @pl.when(pl.program_id(0) == 0)
    def _():
        sort_pairs(meta, mine_ref, other_ref, keys, values)
        values_turned[...] = values[...].T

    slot = step_slot(meta)
    query = stack_heads(query_ref[0])
    wide = count * half

    def run(spans):
        highest = jnp.full((1, wide), masked_score, jnp.float32)
        total = jnp.zeros((1, wide), jnp.float32)
        mixed = jnp.zeros((HEAD_SIZE, wide), jnp.float32)
        for start, size in spans:
            at = pl.ds(start, size)
            scores = dot_last(keys[at, :], query) * scale
            if start == spans[-1][0]:
                seen = allowed_pairs(start, slot, scores.shape, half)
                scores = jnp.where(seen, scores, masked_score)
            new = jnp.maximum(highest, jnp.max(scores, axis=0, keepdims=True))
            rescale = jnp.exp(highest - new)
            powers = jnp.exp(scores - new)
            total = total * rescale + jnp.sum(powers, axis=0, keepdims=True)
            mixed = mixed * rescale + dot_plain(
                values_turned[:, at], powers.astype(jnp.bfloat16)
            )
            highest = new
        log_ref[0] = highest + jnp.log(total)
        out_ref[0] = unstack_heads((mixed / total).T, count).astype(jnp.bfloat16)

    for step in range(8):

        @pl.when(pl.program_id(0) == step)
        def _():
            run(key_spans(step, half, span))


def attend(meta, query, mine, other, scale):
    token_rows, group_width = query.shape[1:]
    half = token_rows // 2
    count = group_width // HEAD_SIZE
    everything = 8 * token_rows
    span = 1024
    arrays = [query, mine, other]
    outs = [
        shape_of(query.shape, jnp.bfloat16),
        shape_of((8, 1, count * half), jnp.float32),
    ]
    return call(
        functools.partial(attend_kernel, scale, span),
        "attend",
        meta,
        arrays,
        (8,),
        [
            pl.BlockSpec((1, half, group_width), lambda i, m: (i // 2, i % 2, 0)),
            whole(mine),
            whole(other),
        ],
        [
            pl.BlockSpec((1, half, group_width), lambda i, m: (i // 2, i % 2, 0)),
            pl.BlockSpec((1, 1, count * half), lambda i, m: (i, 0, 0)),
        ],
        outs,
        [
            pltpu.VMEM((everything, HEAD_SIZE), jnp.bfloat16),
            pltpu.VMEM((everything, HEAD_SIZE), jnp.bfloat16),
            pltpu.VMEM((HEAD_SIZE, everything), jnp.bfloat16),
        ],
        2 * 2 * 4 * token_rows * everything * group_width,
        size_of(arrays) + size_of(outs),
    )


def attend_back_kernel(scale, span, meta, query_ref, mine_ref, other_ref, log_ref, *refs):
    mixed_ref, grad_ref, grad_query_ref, grad_mine_ref, grad_other_ref = refs[:5]
    keys, values, keys_turned, grad_keys, grad_values = refs[5:]
    step = pl.program_id(0)
    half, group_width = query_ref.shape[1:]
    count = group_width // HEAD_SIZE

    @pl.when(step == 0)
    def _():
        sort_pairs(meta, mine_ref, other_ref, keys, values)
        keys_turned[...] = keys[...].T
        grad_keys[...] = jnp.zeros_like(grad_keys)
        grad_values[...] = jnp.zeros_like(grad_values)

    slot = step_slot(meta)
    query = stack_heads(query_ref[0])
    mixed = stack_heads(mixed_ref[0]).astype(jnp.float32)
    grad = stack_heads(grad_ref[0])
    delta = jnp.sum((mixed * grad.astype(jnp.float32)).T, axis=0, keepdims=True)
    log_total = log_ref[0]

    def run(spans):
        grad_turned = jnp.zeros((HEAD_SIZE, count * half), jnp.float32)
        for start, size in spans:
            at = pl.ds(start, size)
            scores = dot_last(keys[at, :], query) * scale
            probs = jnp.exp(scores - log_total)
            if start == spans[-1][0]:
                probs = jnp.where(allowed_pairs(start, slot, probs.shape, half), probs, 0.0)
            grad_probs = dot_last(values[at, :], grad)
            grad_scores = (probs * (grad_probs - delta)).astype(jnp.bfloat16)
            grad_values[at, :] += dot_plain(probs.astype(jnp.bfloat16), grad)
            grad_keys[at, :] += dot_plain(grad_scores, query)
            grad_turned += dot_plain(keys_turned[:, at], grad_scores)
        grad_query_ref[0] = unstack_heads((grad_turned * scale).T, count).astype(jnp.bfloat16)

    for at_step in range(8):

        @pl.when(step == at_step)
        def _():
            run(key_spans(at_step, half, span))

    @pl.when(step == 7)
    def _():
        for slot_at in range(16):
            block, part = (slot_at, 0) if slot_at < 8 else (15 - slot_at, 1)
            place = block >> 1
            rows = pl.ds(part * half, half)
            here = pl.ds(slot_at * half, half)
            both = jnp.concatenate([grad_keys[here, :] * scale, grad_values[here, :]], axis=1)

            @pl.when((meta[0] & 1) == (block & 1))
            def _():
                grad_mine_ref[place, rows, :] = both

            @pl.when((meta[0] & 1) != (block & 1))
            def _():
                grad_other_ref[place, rows, :] = both.astype(jnp.bfloat16)


def attend_back(meta, query, mine, other, log_total, mixed, grad, scale):
    token_rows, group_width = query.shape[1:]
    half = token_rows // 2
    count = group_width // HEAD_SIZE
    everything = 8 * token_rows
    span = 512
    arrays = [query, mine, other, log_total, mixed, grad]
    outs = [
        shape_of(query.shape, jnp.bfloat16),
        shape_of(mine.shape, jnp.float32),
        shape_of(mine.shape, jnp.bfloat16),
    ]
    return call(
        functools.partial(attend_back_kernel, scale, span),
        "attend_back",
        meta,
        arrays,
        (8,),
        [
            pl.BlockSpec((1, half, group_width), lambda i, m: (i // 2, i % 2, 0)),
            whole(mine),
            whole(other),
            pl.BlockSpec((1, 1, count * half), lambda i, m: (i, 0, 0)),
            pl.BlockSpec((1, half, group_width), lambda i, m: (i // 2, i % 2, 0)),
            pl.BlockSpec((1, half, group_width), lambda i, m: (i // 2, i % 2, 0)),
        ],
        [
            pl.BlockSpec((1, half, group_width), lambda i, m: (i // 2, i % 2, 0)),
            whole(outs[1]),
            whole(outs[2]),
        ],
        outs,
        [
            pltpu.VMEM((everything, HEAD_SIZE), jnp.bfloat16),
            pltpu.VMEM((everything, HEAD_SIZE), jnp.bfloat16),
            pltpu.VMEM((HEAD_SIZE, everything), jnp.bfloat16),
            pltpu.VMEM((everything, HEAD_SIZE), jnp.float32),
            pltpu.VMEM((everything, HEAD_SIZE), jnp.float32),
        ],
        5 * 2 * 4 * token_rows * everything * group_width,
        size_of(arrays) + size_of(outs),
    )


def leave_kernel(meta, *refs):
    parts, mine, other, states_ref, gain_ref = refs[:4], *refs[4:8]
    weight_ref, middle_ref, normed_ref = refs[8:]
    core, chip = meta[0] & 1, meta[0] >> 1
    rows = mine.shape[1]
    for i in range(4):
        weight_ref[pl.ds(aligned(2 * i + core, rows), rows), :] = mine[i]
        weight_ref[pl.ds(aligned(2 * i + 1 - core, rows), rows), :] = other[i]
    middle = states_ref[...].astype(jnp.float32)
    for r in range(4):
        at = pl.ds(aligned(chip ^ r, 2 * rows), 2 * rows)
        middle += dot_plain(parts[r][...], weight_ref[at, :])
    middle_ref[...] = middle
    inverse = lax.rsqrt(jnp.mean(middle * middle, axis=-1, keepdims=True) + norm_eps)
    normed_ref[...] = (middle * inverse * gain_ref[...]).astype(jnp.bfloat16)


def leave(meta, parts, mine, other, states, gain):
    token_rows, width = states.shape
    arrays = list(parts) + [mine, other, states, gain]
    outs = [
        shape_of((8 * mine.shape[1], width), jnp.bfloat16),
        shape_of((token_rows, width), jnp.float32),
        shape_of((token_rows, width), jnp.bfloat16),
    ]
    return call(
        leave_kernel,
        "leave",
        meta,
        arrays,
        (1,),
        [whole(a) for a in arrays],
        [whole(a) for a in outs],
        outs,
        [],
        2 * token_rows * width * width,
        size_of(arrays) + size_of(outs),
    )


def norm_back_rows(grad_normed, states, gain):
    inverse = lax.rsqrt(jnp.mean(states * states, axis=-1, keepdims=True) + norm_eps)
    scaled = states * inverse
    gain_grad = jnp.sum(grad_normed * scaled, axis=0, keepdims=True)
    grad_scaled = grad_normed * gain
    shift = jnp.mean(grad_scaled * scaled, axis=-1, keepdims=True)
    return inverse * (grad_scaled - scaled * shift), gain_grad


def enter_back_kernel(meta, final_ref, normed_ref, middle_ref, gain_ref, weight_ref, *refs):
    grad_ref, branch_ref, gain_grad_ref, mixed_ref = refs
    grad, gain_grad = norm_back_rows(normed_ref[...], middle_ref[...], gain_ref[...])
    grad = grad + final_ref[...]
    grad_ref[...] = grad
    gain_grad_ref[...] = gain_grad
    branch = grad.astype(jnp.bfloat16)
    branch_ref[...] = branch
    rows = weight_ref.shape[0] // 4
    for r in range(4):
        mixed_ref[r] = dot_last(branch, weight_ref[rows * r : rows * (r + 1), :]).astype(
            jnp.bfloat16
        )


def enter_back(meta, grad_final, grad_normed, middle, gain, weight):
    token_rows, width = middle.shape
    arrays = [grad_final, grad_normed, middle, gain, weight]
    outs = [
        shape_of((token_rows, width), jnp.float32),
        shape_of((token_rows, width), jnp.bfloat16),
        shape_of((1, width), jnp.float32),
        shape_of((4, token_rows, weight.shape[0] // 4), jnp.bfloat16),
    ]
    return call(
        enter_back_kernel,
        "enter_back",
        meta,
        arrays,
        (1,),
        [whole(a) for a in arrays],
        [whole(a) for a in outs],
        outs,
        [],
        2 * token_rows * width * width,
        size_of(arrays) + size_of(outs),
    )


def finish_kernel(meta, *refs):
    parts, mine, other = refs[:3]
    states_ref, middle_ref, gain_ref, grad_ref, gain_grad_ref, total = refs[3:]
    core, chip = meta[0] & 1, meta[0] >> 1
    columns = mine.shape[1]
    for at, weights in ((core, mine), (1 - core, other)):
        total[:, pl.ds(aligned(at, columns), columns)] = sum(
            dot_last(parts[r], weights[chip ^ r]) for r in range(4)
        )
    grad, gain_grad = norm_back_rows(
        total[...], states_ref[...].astype(jnp.float32), gain_ref[...]
    )
    grad_ref[0] = grad + middle_ref[...]
    gain_grad_ref[...] = gain_grad


def finish(meta, parts, mine, other, states, grad_middle, gain):
    token_rows, width = states.shape
    arrays = [parts, mine, other, states, grad_middle, gain]
    outs = [
        shape_of((1, token_rows, width), jnp.float32),
        shape_of((1, width), jnp.float32),
    ]
    return call(
        finish_kernel,
        "finish",
        meta,
        arrays,
        (1,),
        [whole(a) for a in arrays],
        [whole(a) for a in outs],
        outs,
        [pltpu.VMEM((token_rows, width), jnp.float32)],
        2 * token_rows * width * 4 * parts.shape[2],
        size_of(arrays) + size_of(outs),
    )


def gated(gate_up, units):
    gate_part = gate_up[:, :units]
    sigma = 1.0 / (1.0 + jnp.exp(-gate_part))
    return gate_part * sigma * gate_up[:, units:]


def gated_back(grad_act, gate_up, units):
    gate_part = gate_up[:, :units].astype(jnp.float32)
    up_part = gate_up[:, units:].astype(jnp.float32)
    sigma = 1.0 / (1.0 + jnp.exp(-gate_part))
    linear = gate_part * sigma
    grad_gate = grad_act * up_part * (sigma * (1.0 + gate_part * (1.0 - sigma)))
    return grad_gate, grad_act * linear, linear * up_part


def experts_kernel(
    meta, rows_ref, gates_ref, expert_ref, shared_ref, gate_up_ref, shared_gate_up_ref, out_ref, total
):
    expert = pl.program_id(0)
    rows = rows_ref[...]

    @pl.when(expert == 0)
    def _():
        units = shared_ref.shape[1] // 3
        gate_up = dot_plain(rows, shared_ref[:, : 2 * units])
        shared_gate_up_ref[...] = gate_up.astype(jnp.bfloat16)
        act = gated(gate_up, units).astype(jnp.bfloat16)
        total[...] = dot_last(act, shared_ref[:, 2 * units :])

    gate_up = dot_plain(rows, expert_ref[0, :, : 2 * F])
    gate_up_ref[0] = gate_up.astype(jnp.bfloat16)
    act = (gated(gate_up, F) * gates_ref[0]).astype(jnp.bfloat16)
    total[...] += dot_last(act, expert_ref[0, :, 2 * F :])

    @pl.when(expert == pl.num_programs(0) - 1)
    def _():
        out_ref[...] = total[...].astype(jnp.bfloat16)


def experts(meta, rows, gates, expert_weight, shared_slice):
    local_experts, width, _ = expert_weight.shape
    token_rows = rows.shape[0]
    shared_units = shared_slice.shape[1] // 3
    arrays = [rows, gates, expert_weight, shared_slice]
    outs = [
        shape_of((local_experts, token_rows, 2 * F), jnp.bfloat16),
        shape_of((token_rows, 2 * shared_units), jnp.bfloat16),
        shape_of((token_rows, width), jnp.bfloat16),
    ]
    return call(
        experts_kernel,
        "experts",
        meta,
        arrays,
        (local_experts,),
        [
            whole(rows),
            pl.BlockSpec((1, token_rows, 1), lambda e, m: (e, 0, 0)),
            pl.BlockSpec((1, width, 3 * F), lambda e, m: (e, 0, 0)),
            whole(shared_slice),
        ],
        [
            pl.BlockSpec((1, token_rows, 2 * F), lambda e, m: (e, 0, 0)),
            whole(outs[1]),
            whole(outs[2]),
        ],
        outs,
        [pltpu.VMEM((token_rows, width), jnp.float32)],
        2 * token_rows * width * 3 * (F * local_experts + shared_units),
        size_of(arrays) + size_of(outs),
    )


def experts_back_kernel(
    meta,
    grad_ref,
    gates_ref,
    gate_up_ref,
    shared_gate_up_ref,
    expert_ref,
    shared_ref,
    grad_gate_up_ref,
    act_ref,
    shared_grad_ref,
    shared_act_ref,
    grad_rows_ref,
    total,
):
    expert = pl.program_id(0)
    grad = grad_ref[...]

    @pl.when(expert == 0)
    def _():
        units = shared_ref.shape[1] // 3
        grad_act = dot_plain(grad, shared_ref[:, 2 * units :])
        grad_gate, grad_up, act = gated_back(grad_act, shared_gate_up_ref[...], units)
        both = jnp.concatenate([grad_gate, grad_up], axis=1).astype(jnp.bfloat16)
        shared_grad_ref[0] = both
        shared_act_ref[0] = act.astype(jnp.bfloat16)
        total[...] = dot_last(both, shared_ref[:, : 2 * units])

    grad_act = dot_plain(grad, expert_ref[0, :, 2 * F :]) * gates_ref[0]
    grad_gate, grad_up, act = gated_back(grad_act, gate_up_ref[0], F)
    both = jnp.concatenate([grad_gate, grad_up], axis=1).astype(jnp.bfloat16)
    grad_gate_up_ref[0] = both
    act_ref[0] = (act * gates_ref[0]).astype(jnp.bfloat16)
    total[...] += dot_last(both, expert_ref[0, :, : 2 * F])

    @pl.when(expert == pl.num_programs(0) - 1)
    def _():
        grad_rows_ref[...] = total[...].astype(jnp.bfloat16)


def experts_back(meta, grad, gates, gate_up, shared_gate_up, expert_weight, shared_slice):
    local_experts, width, _ = expert_weight.shape
    token_rows = grad.shape[0]
    shared_units = shared_slice.shape[1] // 3
    arrays = [grad, gates, gate_up, shared_gate_up, expert_weight, shared_slice]
    outs = [
        shape_of((local_experts, token_rows, 2 * F), jnp.bfloat16),
        shape_of((local_experts, token_rows, F), jnp.bfloat16),
        shape_of((1, token_rows, 2 * shared_units), jnp.bfloat16),
        shape_of((1, token_rows, shared_units), jnp.bfloat16),
        shape_of((token_rows, width), jnp.bfloat16),
    ]
    return call(
        experts_back_kernel,
        "experts_back",
        meta,
        arrays,
        (local_experts,),
        [
            whole(grad),
            pl.BlockSpec((1, token_rows, 1), lambda e, m: (e, 0, 0)),
            pl.BlockSpec((1, token_rows, 2 * F), lambda e, m: (e, 0, 0)),
            whole(shared_gate_up),
            pl.BlockSpec((1, width, 3 * F), lambda e, m: (e, 0, 0)),
            whole(shared_slice),
        ],
        [
            pl.BlockSpec((1, token_rows, 2 * F), lambda e, m: (e, 0, 0)),
            pl.BlockSpec((1, token_rows, F), lambda e, m: (e, 0, 0)),
            whole(outs[2]),
            whole(outs[3]),
            whole(outs[4]),
        ],
        outs,
        [pltpu.VMEM((token_rows, width), jnp.float32)],
        2 * token_rows * width * 3 * (F * local_experts + shared_units),
        size_of(arrays) + size_of(outs),
    )


def weight_grad_kernel(pairs, core_at, meta, *refs):
    keep_ref, give_ref = refs[-2:]
    at = 0
    columns = 0
    parts = []
    for count in pairs:
        lefts, rights = refs[at : at + count], refs[at + count : at + 2 * count]
        at += 2 * count
        parts.append(
            sum(dot_first(a[...], b[0]) for a, b in zip(lefts, rights)).astype(jnp.bfloat16)
        )
    half = keep_ref.shape[1]

    for core, (first, second) in ((0, (keep_ref, give_ref)), (1, (give_ref, keep_ref))):

        @pl.when((meta[core_at] & 1) == core)
        def _():
            start = 0
            for part in parts:
                stop = start + part.shape[1]
                first[0, :, start:stop] = part[:half]
                second[0, :, start:stop] = part[half:]
                start = stop


def expert_grad_kernel(count, meta, *refs):
    rows, grads, front, acts = (refs[i * count : (i + 1) * count] for i in range(4))
    out_ref = refs[-1] if len(refs) == 4 * count + 1 else refs[-2]
    tile = rows[0].shape[1]
    both = 3 * F

    def pair(front_refs, act_refs):
        return [
            sum(dot_first(a[...], b[0]) for a, b in zip(left, right)).astype(jnp.bfloat16)
            for left, right in ((rows, front_refs), (grads, act_refs))
        ]

    left, right = pair(front, acts)
    out_ref[0, :tile, : left.shape[1]] = left
    out_ref[0, :tile, left.shape[1] : both] = right
    if len(refs) > 4 * count + 1:
        held = refs[-1]
        left, right = pair(refs[4 * count : 5 * count], refs[5 * count : 6 * count])
        split, columns = left.shape[1], left.shape[1] + right.shape[1]
        held[:, :split] = left
        held[:, split:] = right
        quarter = tile // 4
        first = 2 * meta[2]
        out_ref[0, tile:, :columns] = held[pl.ds(aligned(first, quarter), quarter), :]
        out_ref[0, tile:, columns:] = held[pl.ds(aligned(first + 1, quarter), quarter), :]


def expert_grad(meta, expert, half, rows, grads, front, acts, shared=None):
    count = len(rows)
    token_rows, width = rows[0].shape
    tile = width // 4
    arrays = list(rows) + list(grads) + list(front) + list(acts)
    column = pl.BlockSpec((token_rows, tile), lambda i, m: (0, i ^ m[0]))

    def of_expert(a):
        return pl.BlockSpec((1,) + a.shape[1:], lambda i, m: (m[1], 0, 0))

    in_specs = [column] * (2 * count) + [of_expert(a) for a in arrays[2 * count :]]
    below, scratch = 0, []
    if shared is not None:
        arrays += list(shared[0]) + list(shared[1])
        in_specs += [whole(a) for a in arrays[4 * count :]]
        below = tile // 4
        columns = shared[0][0].shape[-1] + shared[1][0].shape[-1]
        scratch = [pltpu.VMEM((tile, columns), jnp.bfloat16)]
    return call(
        functools.partial(expert_grad_kernel, count),
        "expert_grad",
        jnp.stack([meta[0] >> 1, expert, half]),
        arrays,
        (4,),
        in_specs,
        pl.BlockSpec((1, tile + below, 3 * F), lambda i, m: (i, 0, 0)),
        shape_of((4, tile + below, 3 * F), jnp.bfloat16),
        scratch,
        0,
        0,
    )


def weight_grad(meta, order, operands, index):
    token_rows, width = operands[0][0][0].shape
    tile = width // 4
    scalars = jnp.stack([order, meta[0]])
    arrays, in_specs, columns = [], [], 0
    for lefts, rights in operands:
        arrays += list(lefts) + list(rights)
        in_specs += [pl.BlockSpec((token_rows, tile), lambda i, m: (0, i ^ m[0]))] * len(lefts)
        units = rights[0].shape[-1]
        at = index if rights[0].shape[0] > 1 else 0
        in_specs += [
            pl.BlockSpec((1, token_rows, units), lambda i, m, at=at: (at, 0, 0))
        ] * len(rights)
        columns += units
    tokens = token_rows * len(operands[0][0])
    counts = [len(left) for left, _ in operands]
    outs = [shape_of((4, tile // 2, columns), jnp.bfloat16)] * 2
    return call(
        functools.partial(weight_grad_kernel, counts, 1),
        "weight_grad",
        scalars,
        arrays,
        (4,),
        in_specs,
        [pl.BlockSpec((1, tile // 2, columns), lambda i, m: (i, 0, 0))] * 2,
        outs,
        [],
        2 * tokens * width * columns,
        size_of(outs) + 4 * tokens * width + 2 * tokens * columns,
    )


def place_sum_kernel(meta, *refs):
    rows = refs[-1].shape[1]
    refs[-1][0] = refs[-2][0, :rows].astype(jnp.float32)


def place_sum(meta, total, index, of_other, shape, value, stride, offset):
    _, rows, columns = value.shape
    arrays = [value]
    in_specs = [pl.BlockSpec((1, rows, columns), lambda r, m: (r, 0, 0))]
    aliases = {}
    if total is not None:
        arrays = [total] + arrays
        in_specs = [pl.BlockSpec(memory_space=pl.ANY)] + in_specs
        aliases = {1: 0}
    return pl.pallas_call(
        place_sum_kernel,
        grid_spec=pltpu.PrefetchScalarGridSpec(
            num_scalar_prefetch=1,
            grid=(2,),
            in_specs=in_specs,
            out_specs=pl.BlockSpec(
                (1, shape[1] // 4, shape[2]),
                lambda r, m: (2 * ((m[0] & 1) ^ of_other) + index, (m[0] >> 1) ^ (stride * r + offset), 0),
            ),
        ),
        out_shape=shape_of(shape, jnp.float32),
        input_output_aliases=aliases,
        compiler_params=pltpu.CompilerParams(vmem_limit_bytes=48 * 1024 * 1024),
        cost_estimate=pl.CostEstimate(
            flops=int(COSTS.get("place_sum", 1.0) * 1e9), bytes_accessed=1000, transcendentals=0
        ),
        name="place_sum",
    )(meta, *arrays)


def place_shared_kernel(meta, mine_low, mine_high, other_low, other_high, out_ref):
    core = meta[0] & 1
    rows = mine_low.shape[1]
    for at, low, high in ((core, mine_low, mine_high), (1 - core, other_low, other_high)):
        out_ref[pl.ds(aligned(2 * at, rows), rows), :] = low[0].astype(jnp.float32)
        out_ref[pl.ds(aligned(2 * at + 1, rows), rows), :] = high[0].astype(jnp.float32)


def place_shared(meta, mine, other):
    _, rows, columns = mine.shape
    units = columns // 6
    low = pl.BlockSpec((1, rows, units), lambda i, j, m: (i, 0, j))
    high = pl.BlockSpec((1, rows, units), lambda i, j, m: (i, 0, 3 + j))
    outs = shape_of((4 * rows, 2 * columns), jnp.float32)
    return call(
        place_shared_kernel,
        "place_shared",
        meta,
        [mine, mine, other, other],
        (4, 3),
        [low, high, low, high],
        pl.BlockSpec((4 * rows, units), lambda i, j, m: (0, 4 * j + (m[1] ^ i))),
        outs,
        [],
        0,
        0,
    )


def place_heads_kernel(meta, *refs):
    mine, other, out_ref = refs[:4], refs[4], refs[5]
    core, chip = meta[0] & 1, meta[0] >> 1
    rows, columns = mine[0].shape
    group_width = columns - 2 * HEAD_SIZE
    for r in range(4):
        head = chip ^ r
        for at, pieces in ((core, [piece[...] for piece in mine]), (1 - core, other)):
            to = pl.ds(aligned(at, rows), rows)
            values = pieces[r].astype(jnp.float32)
            out_ref[to, pl.ds(aligned(head, group_width), group_width)] = values[:, :group_width]
            out_ref[to, pl.ds(aligned(4 * group_width // HEAD_SIZE + head, HEAD_SIZE), HEAD_SIZE)] = (
                values[:, group_width : group_width + HEAD_SIZE]
            )
            out_ref[
                to, pl.ds(aligned(4 * group_width // HEAD_SIZE + 4 + head, HEAD_SIZE), HEAD_SIZE)
            ] = values[:, group_width + HEAD_SIZE :]


def place_heads(meta, mine, other):
    rows, columns = mine[0].shape
    arrays = list(mine) + [other]
    outs = shape_of((2 * rows, 4 * columns), jnp.float32)
    return call(
        place_heads_kernel,
        "place_heads",
        meta,
        arrays,
        (1,),
        [whole(a) for a in arrays],
        whole(outs),
        outs,
        [],
        0,
        size_of(arrays + [outs]),
    )


def join_shared_kernel(meta, mine, other, out_ref):
    step = pl.program_id(0)
    rows = mine.shape[2]
    first = meta[0] ^ (2 * step)
    for i in range(4):
        at = 8 * (meta[1] ^ i)
        out_ref[pl.ds(aligned(at + first, rows), rows), :] = mine[0, i]
        out_ref[pl.ds(aligned(at + (first ^ 1), rows), rows), :] = other[0, i]


def join_shared(meta, mine, other):
    _, _, rows, columns = mine.shape
    block = pl.BlockSpec((1, 4, rows, columns), lambda r, m: (r, 0, 0, 0))
    outs = shape_of((32 * rows, columns), jnp.bfloat16)
    return call(
        join_shared_kernel,
        "join_shared",
        meta,
        [mine, other],
        (4,),
        [block, block],
        whole(outs),
        outs,
        [],
        0,
        size_of([mine, other, outs]),
    )


class Clock:
    def __init__(self):
        self.last = None

    def __call__(self, *values):
        if self.last is None:
            return values if len(values) > 1 else values[0]
        held = lax.optimization_barrier(tuple(values) + (self.last,))[:-1]
        return held if len(held) > 1 else held[0]

    def mark(self, value):
        self.last = value
        return value


EARLY = (
    "H", "W", "K", "S", "K", "W", "S", "W", "K", "S", "O", "S", "M", "M", "S", "O", "M", "S", "M", "R", "M", "K", "M", "K",
    "M", "K", "R", "M", "K", "M", "M", "M", "M", "R", "M", "M",
)
LATE = (
    "L", "0", "1", "0", "0", "L", "1", "1", "L", "L", "O", "0", "1", "L", "L", "1", "0", "O", "Q", "1", "O", "0", "L", "Q",
    "O", "L", "1", "Q", "0", "Q", "O", "O", "Q", "L", "1", "0", "1", "0", "O", "Q", "S", "1", "0", "L", "O", "Q", "1", "S",
    "L", "0", "O", "Q", "L", "Q", "O", "S",
)


def fast_device(
    hidden,
    teacher,
    valid_mask,
    routes,
    route_gates,
    gain_in,
    query_key_value_weight,
    out_weight,
    gain_mid,
    shared_weight,
    expert_weight,
):
    token_rows, width = hidden.shape[1:]
    context_count, shard_count = 8, 4
    context_index = lax.axis_index("ctx").astype(jnp.int32)
    shard_index = lax.axis_index("wt").astype(jnp.int32)
    plain_meta = jnp.stack([context_index, shard_index])
    core = context_index & 1
    chip = context_index >> 1
    at_end = (shard_index == 0) | (shard_index == shard_count - 1)
    group_width = QUERY_HEADS // KEY_VALUE_HEADS * HEAD_SIZE
    query_width = QUERY_HEADS * HEAD_SIZE
    kv_width = KEY_VALUE_HEADS * HEAD_SIZE
    scale = 1.0 / math.sqrt(HEAD_SIZE)
    all_tokens = token_rows * context_count * shard_count
    shard_rows = query_key_value_weight.shape[0]
    half_rows = shard_rows // 2
    local_experts = expert_weight.shape[0]
    bf16, f32 = jnp.bfloat16, jnp.float32
    states = hidden[0]
    clock = Clock()
    have = {}

    def meta():
        return clock(plain_meta)

    def now(*values):
        return clock(*values)

    def ready(*values):
        values = clock(*values)
        clock.mark(values[0] if isinstance(values, tuple) or isinstance(values, list) else values)
        return values


    def hidden_chain():
        have["blocks"] = chips_exchange(jnp.broadcast_to(states, (4,) + states.shape))
        yield

    def qkv_chain():
        rows = lax.dynamic_slice_in_dim(query_key_value_weight, core * half_rows, half_rows, 0)
        half = jnp.concatenate(
            [
                lax.dynamic_slice_in_dim(rows, chip * group_width, group_width, 1),
                lax.dynamic_slice_in_dim(rows, query_width + chip * HEAD_SIZE, HEAD_SIZE, 1),
                lax.dynamic_slice_in_dim(
                    rows, query_width + kv_width + chip * HEAD_SIZE, HEAD_SIZE, 1
                ),
            ],
            axis=1,
        )
        came = line_swap(half, 1)
        yield
        pair = clock.mark(jnp.stack([half, now(came)]))
        came = line_swap(pair, 2)
        yield
        have["qkv_mine"] = clock.mark(jnp.concatenate([pair, now(came)]))
        have["qkv_other"] = flip(have["qkv_mine"], 1)
        yield

    def small_chain():
        expert_ids = jnp.arange(EXPERTS, dtype=jnp.int32)
        matrix = jnp.sum(
            jnp.where(
                routes[0][None, :, :] == expert_ids[:, None, None], route_gates[0][None, :, :], 0.0
            ),
            axis=-1,
        )
        have["valid"] = valid_mask[0].astype(f32)
        gains = jnp.concatenate([gain_in, gain_mid]).astype(f32).reshape(-1, token_rows)
        gain_rows = gains.shape[0]
        filled = EXPERTS + gain_rows
        pack = jnp.concatenate(
            [
                matrix,
                gains,
                jnp.full((32 - filled, token_rows), jnp.sum(have["valid"]), f32),
            ]
        )
        came = line_swap(pack, 1)
        yield
        pair = clock.mark(jnp.stack([pack, now(came)]))
        came = line_swap(pair, 2)
        yield
        all_packs = clock.mark(jnp.concatenate([pair, now(came)]))
        have["gates"] = [
            lax.dynamic_slice_in_dim(
                all_packs[i], shard_index * local_experts, local_experts, 0
            )[..., None]
            for i in range(4)
        ]
        gains = all_packs[:, EXPERTS:filled].reshape(4, 2, shard_rows)
        gains = jnp.stack([pick(gains, shard_index ^ i) for i in range(4)], axis=1)
        have["gains"] = gains.reshape(2, 1, width)
        total = jnp.broadcast_to(jnp.sum(all_packs[:, filled, 0]), (8, 128))
        yield
        total = now(total)
        for bit in (1, 2, 4):
            came = flip(total, bit)
            yield
            total = clock.mark(total + now(came))
        have["count"] = total[0, 0]
        yield

    def shared_chain():
        eighth = shard_rows // 8
        units = SF // shard_count
        piece = lax.dynamic_slice_in_dim(shared_weight, context_index * eighth, eighth, 0)
        piece = piece.reshape(eighth, 3, shard_count, units)

        piece = jnp.transpose(piece, (2, 0, 1, 3)).reshape(shard_count, eighth, 3 * units)
        parts = [pick(piece, shard_index ^ i) for i in range(4)]
        came = line_swap(now(jnp.stack([parts[1], parts[3]])), 1)
        yield
        came = now(came)
        mine = jnp.stack([parts[0], came[0]])
        came = line_swap(clock.mark(jnp.stack([parts[2], came[1]])), 2)
        yield
        pieces = clock.mark(jnp.concatenate([mine, now(came)]))
        came = flip(pieces, 2)
        yield
        pair = clock.mark(jnp.stack([pieces, now(came)]))
        came = flip(pair, 4)
        yield
        mine = clock.mark(jnp.concatenate([pair, now(came)]))
        other = flip(mine, 1)
        yield
        have["shared"] = join_shared(meta(), mine, other)
        clock.mark(have["shared"])
        yield

    def out_chain():
        half = lax.dynamic_slice_in_dim(now(out_weight), core * half_rows, half_rows, 0)
        came = line_exchange(jnp.broadcast_to(half, (4,) + half.shape))
        yield
        have["out_mine"] = clock.mark(now(came))
        have["out_other"] = flip(have["out_mine"], 1)
        yield

    def qkv_all_chain():
        half = lax.dynamic_slice_in_dim(
            now(have["qkv_slice"]), core * (width // 2), width // 2, 0
        )
        came = flip(half, 2)
        yield
        pair = clock.mark(jnp.stack([half, now(came)]))
        came = flip(pair, 4)
        yield
        have["rel_mine"] = clock.mark(jnp.concatenate([pair, now(came)]))
        have["rel_other"] = flip(have["rel_mine"], 1)
        yield

    def main_chain():
        gains = have["gains"]
        normed_in, query, pair, qkv_slice = project(
            meta(), have["blocks"], gains[0], have["qkv_mine"], have["qkv_other"], group_width
        )
        clock.mark(pair)
        have["normed_in"], have["qkv_slice"] = normed_in, qkv_slice
        pair_other = flip(pair, 1)
        yield
        mixed_heads, log_total = attend(meta(), query, pair, pair_other, scale)
        clock.mark(log_total)
        have["attend"] = (query, pair, pair_other, log_total, mixed_heads)
        parts = ready(*[pick(mixed_heads, chip ^ r) for r in range(4)])
        mixed = [parts[0]] + [flip(parts[r], 2 * r) for r in (1, 2, 3)]
        have["mixed"] = mixed
        yield
        out_full, middle, normed_mid = leave(
            meta(), mixed, have["out_mine"], have["out_other"], states, gains[1]
        )
        have["out_full"], have["middle"] = out_full, middle
        clock.mark(normed_mid)

        near, center = line_swap(normed_mid, 1), line_middle(normed_mid)
        yield
        gates, shared_slice = have["gates"], have["shared"]
        gate_ups, shared_gate_ups, outs = [], [], []

        def forward(rows, i):
            result = experts(meta(), rows, gates[i], expert_weight, shared_slice)
            clock.mark(result[2])
            gate_ups.append(result[0])
            shared_gate_ups.append(result[1])
            outs.append(result[2])

        forward(normed_mid, 0)
        yield
        near, center = now(near, center)
        far, outward = line_middle(near), line_outward(center)
        forward(near, 1)
        yield
        far, outward = now(far, outward)
        outward_far = line_outward(far)
        third = clock.mark(jnp.where(at_end, outward, far))
        forward(third, 2)
        yield
        outward_far = now(outward_far)
        fourth = clock.mark(jnp.where(at_end, outward_far, center))
        forward(fourth, 3)
        line_rows = [normed_mid, near, third, fourth]
        came = line_inward(outs[3])
        yield
        carried = clock.mark(outs[2] + now(came))
        inward, crossed = line_inward(carried), line_middle(carried)
        yield
        inward, crossed = now(inward, crossed)
        near_out, middle_out = ready(outs[1] + crossed, outs[3] + inward)
        near_out, middle_out = line_swap(near_out, 1), line_middle(middle_out)
        yield
        near_out, middle_out = now(near_out, middle_out)
        final_state = (
            middle + outs[0].astype(f32) + near_out.astype(f32) + middle_out.astype(f32)
        )
        valid = have["valid"]
        deviation = final_state - teacher[0].astype(f32)
        have["squared"] = jnp.sum(valid[:, None] * deviation * deviation)
        grad_final = all_tokens / have["count"] * valid[:, None] * deviation
        have["final"], have["grad_final"] = final_state.astype(bf16)[None], grad_final
        grad_low = clock.mark(grad_final.astype(bf16))
        near, center = line_swap(grad_low, 1), line_middle(grad_low)
        yield
        kept = []

        def backward(grads, i):
            kept.append(
                experts_back(
                    meta(),
                    grads,
                    gates[i],
                    gate_ups[i],
                    shared_gate_ups[i],
                    expert_weight,
                    shared_slice,
                )
            )
            clock.mark(kept[-1][4])

        backward(grad_low, 0)
        yield
        near, center = now(near, center)
        far, outward = line_middle(near), line_outward(center)
        backward(near, 1)
        yield
        far, outward = now(far, outward)
        outward_far = line_outward(far)
        third = clock.mark(jnp.where(at_end, outward, far))
        backward(third, 2)
        yield
        outward_far = now(outward_far)
        fourth = clock.mark(jnp.where(at_end, outward_far, center))
        backward(fourth, 3)
        have["line"] = (line_rows, [grad_low, near, third, fourth])
        have["experts"] = list(zip(*kept))
        yield


    def states_chain():
        outs = have["experts"][4]
        came = line_inward(outs[3])
        yield
        carried = clock.mark(outs[2] + now(came))
        inward, crossed = line_inward(carried), line_middle(carried)
        yield
        inward, crossed = now(inward, crossed)
        near_out, middle_out = ready(outs[1] + crossed, outs[3] + inward)
        near_out, middle_out = line_swap(near_out, 1), line_middle(middle_out)
        yield
        near_out, middle_out = now(near_out, middle_out)
        grad_normed = clock.mark(
            outs[0].astype(f32) + near_out.astype(f32) + middle_out.astype(f32)
        )
        grad_middle, grad_branch, grad_gain_mid, grad_mixed = enter_back(
            meta(),
            have["grad_final"],
            grad_normed,
            have["middle"],
            have["gains"][1],
            have["out_full"],
        )
        clock.mark(grad_branch)
        have["grad_branch"], have["grad_gain_mid"] = grad_branch, grad_gain_mid
        grad_mixed = chips_exchange(ready(grad_mixed))
        yield
        query, pair, pair_other, log_total, mixed_heads = have["attend"]
        grad_query, grad_pair, grad_other = attend_back(
            meta(), query, pair, pair_other, log_total, mixed_heads, grad_mixed, scale
        )
        clock.mark(grad_query)
        came = flip(grad_other, 1)
        yield
        grad_pair = grad_pair + now(came).astype(f32)
        projected = clock.mark(jnp.concatenate([grad_query, grad_pair.astype(bf16)], axis=-1))
        have["grad_projected"] = projected
        parts = chips_exchange(ready(projected))
        yield
        grad_hidden, grad_gain_in = finish(
            meta(),
            parts,
            have["rel_mine"],
            have["rel_other"],
            states,
            grad_middle,
            have["gains"][0],
        )
        clock.mark(grad_gain_in)
        have["grad_hidden"] = grad_hidden
        sums = jnp.concatenate(
            [grad_gain_in, have["grad_gain_mid"], jnp.full((6, width), have["squared"], f32)],
            axis=0,
        )
        for offset in (1, 2):
            came = line_swap(sums, offset)
            yield
            sums = clock.mark(sums + now(came))
        for bit in (1, 2, 4):
            came = flip(sums, bit)
            yield
            sums = clock.mark(sums + now(came))
        own = lax.dynamic_slice_in_dim(sums, shard_index * shard_rows, shard_rows, 1)
        have["sums"] = (own, 0.5 * sums[2, 0] / (have["count"] * width))
        yield

    def expert_chain(index):
        line_rows, line_grads = have["line"]
        grad_gate_ups, acts, shared_grads, shared_acts = have["experts"][:4]
        shared = (shared_grads, shared_acts) if index == 0 else None

        def grad_of(at):
            return clock.mark(
                expert_grad(
                    meta(),
                    2 * at + index,
                    at,
                    line_rows,
                    line_grads,
                    grad_gate_ups,
                    acts,
                    shared,
                )
            )

        came = flip(grad_of(1 - core), 1)
        yield
        keep = grad_of(core)
        yield
        x_first = index % 2 == 0
        first, second = (2, 4) if x_first else (4, 2)
        picked = ((1, 3), (0, 2)) if x_first else ((2, 3), (0, 1))
        pieces = keep.shape[1] // 96

        def split_sum(keep, came):
            return [
                jnp.stack([keep[i] + came[i] for i in places]) for places in picked
            ]

        give, keep = blend(meta(), "blend_split", split_sum, [keep, came], pieces)
        clock.mark(give)
        came = flip(give, first)
        yield
        give, keep = blend(
            meta(), "blend_pair", lambda k, c: [k[1] + c[1], k[0] + c[0]], [keep, came], pieces
        )
        clock.mark(give)
        came = flip(give, second)
        yield
        own = clock.mark(blend(meta(), "blend_sum", lambda k, c: k + c, [keep, came], pieces))
        came = flip(own, second)
        yield
        pair = clock.mark(
            blend(meta(), "blend_stack", lambda a, b: jnp.stack([a, b]), [own, came], pieces)
        )
        came = flip(pair, first)
        yield

        def place(of_other, value, far):
            stride, offset = (2, far) if x_first else (1, 2 * far)
            have["grad_experts"] = place_sum(
                meta(),
                have.get("grad_experts"),
                index,
                of_other,
                expert_weight.shape,
                value,
                stride,
                offset,
            )
            clock.mark(have["grad_experts"])

        place(0, pair, 0)
        pair_other = flip(now(pair), 1)
        yield
        place(1, pair_other, 0)
        yield
        came = now(came)
        came_other = flip(came, 1)
        if index == 0:
            have["shared_sum"] = jnp.stack([pair[0], came[0], pair[1], came[1]])[:, shard_rows:]
        yield
        place(0, came, 1)
        yield
        place(1, came_other, 1)
        yield

    def shared_grad_chain():
        total = now(have["shared_sum"])
        parts = ready(*[pick(total, chip ^ shard_index ^ i) for i in range(4)])
        came = [line_swap(parts[i], i) for i in (1, 2, 3)]
        yield
        mine = clock.mark(jnp.stack([parts[0]] + list(now(*came))))
        other = flip(mine, 1)
        yield
        have["grad_shared"] = clock.mark(place_shared(meta(), mine, other))
        yield

    def line_reduce_steps(keep, came):
        came = now(came)
        parts = [keep[i] + came[i] for i in range(4)]
        came = line_inward(clock.mark(parts[3]))
        yield
        carried = clock.mark(parts[2] + now(came))
        inward, crossed = line_inward(carried), line_middle(carried)
        yield
        inward, crossed = now(inward, crossed)
        near_out, middle_out = ready(parts[1] + crossed, parts[3] + inward)
        near_out, middle_out = line_swap(near_out, 1), line_middle(middle_out)
        yield
        near_out, middle_out = now(near_out, middle_out)
        have["line_sum"] = clock.mark(
            (parts[0].astype(f32) + near_out.astype(f32) + middle_out.astype(f32)).astype(bf16)
        )

    def out_grad_chain():
        mixed = jnp.concatenate(have["mixed"], axis=1)
        keep, give = weight_grad(
            meta(), chip ^ shard_index, [([mixed], [have["grad_branch"][None]])], 0
        )
        clock.mark(keep)
        came = flip(give, 1)
        yield
        yield from line_reduce_steps(keep, came)
        total = have["line_sum"]
        yield
        total = ready(total)
        came = flip(total, 2)
        yield
        total = clock.mark(total + now(came))
        came = flip(total, 4)
        yield
        mine = clock.mark(total + now(came))
        other = flip(mine, 1)
        yield
        mine, other = now(mine, other)
        have["grad_out"] = clock.mark(
            jnp.where(
                core == 0,
                jnp.concatenate([mine, other], axis=0),
                jnp.concatenate([other, mine], axis=0),
            ).astype(f32)
        )
        yield

    def qkv_grad_chain():
        normed_in = have["normed_in"].reshape(4 * token_rows, width)
        projected = have["grad_projected"].reshape(1, 4 * token_rows, -1)
        keep, give = weight_grad(meta(), shard_index, [([normed_in], [projected])], 0)
        clock.mark(keep)
        came = flip(give, 1)
        yield
        yield from line_reduce_steps(keep, came)
        own = have["line_sum"]
        yield
        own = ready(own)
        came = flip(own, 2)
        yield
        pair = clock.mark(jnp.stack([own, now(came)]))
        came = flip(pair, 4)
        yield
        mine = clock.mark(jnp.concatenate([pair, now(came)]))
        other = flip(mine, 1)
        yield
        have["grad_qkv"] = clock.mark(place_heads(meta(), [mine[r] for r in range(4)], other))
        yield

    early = {
        "H": hidden_chain(),
        "W": qkv_chain(),
        "S": shared_chain(),
        "O": out_chain(),
        "K": small_chain(),
        "R": qkv_all_chain(),
        "M": main_chain(),
    }
    late = {
        "L": states_chain(),
        "S": shared_grad_chain(),
        "O": out_grad_chain(),
        "Q": qkv_grad_chain(),
    }
    for index in range(local_experts // 2):
        late[str(index)] = expert_chain(index)
    for chains, order in ((early, EARLY), (late, LATE)):
        for name in order:
            next(chains[name], None)
        for name in chains:
            for _ in chains[name]:
                pass

    own, loss_value = have["sums"]
    return (
        have["final"],
        loss_value,
        have["grad_hidden"],
        own[0],
        have["grad_qkv"],
        have["grad_out"],
        own[1],
        have["grad_shared"],
        have["grad_experts"],
    )


def solution(mesh):
    in_specs = (
        P("wt", "ctx", None),
        P("wt", "ctx", None),
        P("wt", "ctx"),
        P("wt", "ctx", None),
        P("wt", "ctx", None),
        P("wt"),
        P("wt", None),
        P("wt", None),
        P("wt"),
        P("wt", None),
        P("wt", None, None),
    )
    out_specs = (
        P("wt", "ctx", None),
        P(),
        P("wt", "ctx", None),
        P("wt"),
        P("wt", None),
        P("wt", None),
        P("wt"),
        P("wt", None),
        P("wt", None, None),
    )
    plane_of_eight = dict(mesh.shape) == {"ctx": 8, "wt": 4}
    return jax.shard_map(
        fast_device if plane_of_eight else on_device, mesh=mesh, in_specs=in_specs, out_specs=out_specs, check_vma=False
    )
```
